32 devices in a mesh: dp: 16 (over z, y, x), section: 2 (over core).
Axes of the slice: x: 2, y: 2, z: 4, core: 2. Of those that a mesh axis runs over, the one named last changes fastest.
Arguments:
- token_ids: int32 [2, 16, 512], P(None, 'dp'), may hold values from 0 to 119551
- lengths: int32 [2, 16], P(None, 'dp'), may hold values from 128 to 512, as said below
- positions: int32 [2, 16, 32], P(None, 'dp'), may hold values from 0 to 511, as said below
- targets: int32 [2, 16, 32], P(None, 'dp'), may hold values from 0 to 119551
- loss_weights: int32 [2, 16, 32], P(None, 'dp'), may hold values from 1 to 5
- embed_table: bfloat16 [119552, 768], P('dp')
- pos_table: bfloat16 [512, 768], replicated, may hold values from -3 to 3
- norm_params: float32 [2, 6, 768], P('section')
- base_qkv: bfloat16 [2, 768, 2304], P('section'), may hold values from -0.21875 to 0.21875
- base_out: bfloat16 [2, 768, 768], P('section'), may hold values from -2.5 to 2.5
- base_up: bfloat16 [2, 768, 3072], P('section'), may hold values from -0.21875 to 0.21875
- base_down: bfloat16 [2, 3072, 768], P('section'), may hold values from -0.109375 to 0.109375
- master: float32 [2, 320, 48, 48], P('section', 'dp'), may hold values from -0.3125 to 0.3125
- momentum: float32 [2, 320, 48, 48], P('section', 'dp'), may hold values from -0.00024414062 to 0.00024414062
- stat_left: float32 [2, 320, 48, 48], P('section', 'dp')
- stat_right: float32 [2, 320, 48, 48], P('section', 'dp')
- root_left: float32 [2, 320, 48, 48], P('section', 'dp')
- root_right: float32 [2, 320, 48, 48], P('section', 'dp')
- vectors: float32 [2, 1728], P('section', 'dp'), may hold values from -3 to 3
- vec_first: float32 [2, 1728], P('section', 'dp'), may hold values from -7.6293945e-05 to 7.6293945e-05
- vec_second: float32 [2, 1728], P('section', 'dp'), may hold values from 2.4414062e-12 to 9.765625e-12
Outputs:
- grad_blocks: float32 [2, 320, 48, 48], P('section', 'dp')
- momentum_new: float32 [2, 320, 48, 48], P('section', 'dp')
- left_new: float32 [2, 320, 48, 48], P('section', 'dp')
- right_new: float32 [2, 320, 48, 48], P('section', 'dp')
- master_new: float32 [2, 320, 48, 48], P('section', 'dp')
- master_low: bfloat16 [2, 320, 48, 48], P('section', 'dp')
- first_new: float32 [2, 1728], P('section', 'dp')
- second_new: float32 [2, 1728], P('section', 'dp')
- vectors_new: float32 [2, 1728], P('section', 'dp')
- grad_norm: float32 [], replicated
- loss_sum: float32 [], replicated
- weight_sum: float32 [], replicated
The draws below stay inside these ranges and needn't reach their ends.
Inputs may be any that keep to these rules, and one draw needn't show every extreme that they name: `lengths`: one row of each micro-batch has length 512. The 32 positions of a row are distinct, increasing and below its length.
All inputs are finite; a program needn't handle non-finite values.
Results may differ from the reference program's by a relative error of at most 0.0052.
The reference program's roundings to bfloat16 on the way count: a program that leaves them out, or rounds other values in their place, can miss the bound.
Values may be sent and summed in bfloat16 or wider, within the bound.
No kernel may reach another device: no remote copies, remote signals or barrier semaphores. Data moves between devices by JAX's collectives and lax.ppermute only.
A program may use at most 576 MiB of HBM per device.

```python
import math
import jax
import jax.numpy as jnp
import numpy as np
from jax import lax

D = 768
HEADS = 12
HEAD_DIM = 64
FF = 3072
BOT = 384
INV_H = 192
VOCAB = 119552
SEQ = 512
COUNT = 32
MICRO = 2
BLOCK = 48
STEP = 10
HALF = 384
ROWS = 16
NB = 320
VL = 1728


def grad_scale():
    return 0.02 * (4.0 * D * BOT + 4.0 * HALF * INV_H) ** (-0.5)


def row_lengths(key):
    draw_key, pick_key = jax.random.split(key)
    drawn = jax.random.randint(draw_key, (MICRO, ROWS), SEQ // 4, SEQ + 1)
    longest = jax.random.randint(pick_key, (MICRO, 1), 0, ROWS)
    return jnp.where(jnp.arange(ROWS)[None, :] == longest, SEQ, drawn).astype(jnp.int32)


def draw_lengths(key, part):
    return row_lengths(key)


def draw_positions(key, part):
    limits = row_lengths(key)
    key = jax.random.fold_in(key, 2)
    slots = jnp.arange(COUNT)[None, None, :]
    lower = slots * limits[..., None] // COUNT
    upper = (slots + 1) * limits[..., None] // COUNT
    offset = jax.random.randint(key, (MICRO, ROWS, COUNT), 0, 1 << 20)
    return (lower + offset % (upper - lower)).astype(jnp.int32)


def draw_loss_weights(key, part):
    key = jax.random.fold_in(key, 3)
    levels = 1 + 5 * jnp.arange(ROWS)[None, :, None] // ROWS
    drawn = jax.random.randint(key, (MICRO, ROWS, COUNT), 0, 1 << 20)
    result = 1 + drawn % levels
    return result.at[:, ROWS - 1, 0].set(5).astype(jnp.int32)


def draw_embed_table(key, part):
    key = jax.random.fold_in(key, 5)
    ramp = jnp.arange(VOCAB, dtype=jnp.float32)[:, None] / VOCAB
    values = jax.random.normal(key, (VOCAB, D), jnp.float32)
    scale = 1.0 + 2.0 * ramp
    return (values * scale * D ** (-0.5)).astype(jnp.bfloat16)


def draw_norm_params(key, part):
    key = jax.random.fold_in(key, 6)
    gain_key, shift_key = jax.random.split(key)
    ramp = 0.5 + jnp.arange(D, dtype=jnp.float32) / D
    gains = ramp * jax.random.uniform(gain_key, (2, 3, D), jnp.float32, 0.8, 1.2)
    shifts = 0.2 * jax.random.normal(shift_key, (2, 3, D), jnp.float32)
    return jnp.stack([gains, shifts], 2).reshape(2, 6, D)


def symmetric_blocks(key, level, lowest, highest, spread_factor):
    diagonal_key, spread_key = jax.random.split(key)
    diagonal = jax.random.uniform(diagonal_key, (2, NB, BLOCK), jnp.float32, lowest, highest) * level
    spread = jax.random.normal(spread_key, (2, NB, BLOCK, BLOCK), jnp.float32)
    spread = (spread + jnp.swapaxes(spread, -1, -2)) * (spread_factor * level * BLOCK ** (-0.5))
    identity = jnp.eye(BLOCK, dtype=jnp.float32)
    return identity * diagonal[..., None] + (1.0 - identity) * spread


def draw_stat_left(key, part):
    key = jax.random.fold_in(key, 7)
    return symmetric_blocks(key, 0.01 / 0.99 * BLOCK * grad_scale() ** 2, 1.0, 4.0, 0.05)


def draw_stat_right(key, part):
    key = jax.random.fold_in(key, 8)
    return symmetric_blocks(key, 0.01 / 0.99 * BLOCK * grad_scale() ** 2, 1.0, 4.0, 0.05)


def draw_root_left(key, part):
    key = jax.random.fold_in(key, 9)
    return symmetric_blocks(key, (BLOCK * grad_scale() ** 2) ** (-0.25), 1.0, 2.0, 0.27)


def draw_root_right(key, part):
    key = jax.random.fold_in(key, 10)
    return symmetric_blocks(key, (BLOCK * grad_scale() ** 2) ** (-0.25), 1.0, 2.0, 0.27)


def place_ends(array, own_key, smallest, largest):
    longest = array.shape.index(max(array.shape))
    spots = []
    for shift in (0, 1):
        where = [jax.random.randint(jax.random.fold_in(own_key, axis), (), 0, length) for axis, length in enumerate(array.shape)]
        where[longest] = (where[longest] + shift) % array.shape[longest]
        spots.append(tuple(where))
    return array.at[spots[0]].set(smallest).at[spots[1]].set(largest)


def shard_levels(key, shape, cuts, smallest, top_value):
    factor_of = 1.0
    for axis_at, parts in cuts:
        draws = jax.random.uniform(jax.random.fold_in(jax.random.fold_in(key, 6), axis_at), (parts,), jnp.float32, smallest / len(cuts), top_value / len(cuts))
        factor_of = factor_of * jnp.repeat(jnp.exp(draws), shape[axis_at] // parts).reshape((-1,) + (1,) * (len(shape) - 1 - axis_at))
    return factor_of


def skewed_wide(stream_key, dims, amount, lean):
    portions = [min(1 << octave, amount + 1 - (1 << octave)) * (1 << 20) // math.isqrt((1 << octave) ** lean) + 1 for octave in range((amount + 1).bit_length()) if 1 << octave <= amount]
    scale = 1 + sum(portions) // (1 << 30)
    table = np.cumsum(np.array([max(1, weight // scale) for weight in portions]))
    lot = jax.random.randint(jax.random.fold_in(stream_key, 1), dims, 0, int(table[len(portions) - 1]))
    start = jnp.left_shift(1, jnp.searchsorted(jnp.asarray(table, jnp.int32), lot, side="right").astype(jnp.int32))
    rank = start - 1 + jax.random.randint(jax.random.fold_in(stream_key, 4), dims, 0, 1 << 30) % jnp.minimum(start, amount + 1 - start)
    return jax.random.permutation(jax.random.fold_in(stream_key, 2), amount)[rank].astype(jnp.int32)


def gaussian(own_key, shape, deviation, reach, shards=(), kind=jnp.bfloat16):
    level = shard_levels(own_key, shape, shards, -0.22, 0.18) if shards else 1.0
    values = jax.random.normal(own_key, shape, jnp.float32) * deviation * level
    return jnp.minimum(jnp.maximum(values, -reach), reach).astype(kind)


def setup_inputs(seed: int = 0) -> dict:
    splits = jax.random.split(jax.random.key(seed), 22)
    return {
        "token_ids": place_ends(skewed_wide(splits[0], (MICRO, ROWS, SEQ), VOCAB, 2), jax.random.fold_in(splits[0], 3), 0, VOCAB - 1).astype(jnp.int32),
        "lengths": draw_lengths(jax.random.fold_in(splits[21], 71), 0),
        "positions": draw_positions(jax.random.fold_in(splits[21], 71), 0),
        "targets": place_ends(skewed_wide(splits[3], (MICRO, ROWS, COUNT), VOCAB, 2), jax.random.fold_in(splits[3], 3), 0, VOCAB - 1).astype(jnp.int32),
        "loss_weights": draw_loss_weights(jax.random.fold_in(splits[21], 71), 0),
        "embed_table": draw_embed_table(jax.random.fold_in(splits[21], 71), 0),
        "pos_table": gaussian(splits[6], (SEQ, D), 0.5, 3.0),
        "norm_params": draw_norm_params(jax.random.fold_in(splits[21], 71), 0),
        "base_qkv": gaussian(splits[8], (2, D, 3 * D), D ** -0.5, 0.21875, ((0, 2),)),
        "base_out": gaussian(splits[9], (2, D, D), (max(D * 4 // SEQ, 1)) ** -0.5, 2.5, ((0, 2),)),
        "base_up": gaussian(splits[10], (2, D, FF), D ** -0.5, 0.21875, ((0, 2),)),
        "base_down": gaussian(splits[11], (2, FF, D), FF ** -0.5, 0.109375, ((0, 2),)),
        "master": gaussian(splits[12], (2, NB, BLOCK, BLOCK), BOT ** -0.5, 0.3125, ((0, 2), (1, 16)), jnp.float32),
        "momentum": gaussian(splits[13], (2, NB, BLOCK, BLOCK), (0.02 * (4 * D * BOT + 4 * HALF * INV_H) ** -0.5), 0.00024414062, ((0, 2), (1, 16)), jnp.float32),
        "stat_left": draw_stat_left(jax.random.fold_in(splits[21], 71), 0),
        "stat_right": draw_stat_right(jax.random.fold_in(splits[21], 71), 0),
        "root_left": draw_root_left(jax.random.fold_in(splits[21], 71), 0),
        "root_right": draw_root_right(jax.random.fold_in(splits[21], 71), 0),
        "vectors": gaussian(splits[18], (2, VL), 0.3, 3.0, ((0, 2), (1, 16)), jnp.float32),
        "vec_first": gaussian(splits[19], (2, VL), (0.00667 * (4 * D * BOT + 4 * HALF * INV_H) ** -0.5), 7.62939453125e-05, ((0, 2), (1, 16)), jnp.float32),
        "vec_second": jnp.clip(jnp.exp(math.log(9.765624940649698e-12) - 1.3862944 * jax.random.uniform(splits[20], (2, VL), jnp.float32) ** shard_levels(splits[20], (2, VL), ((0, 2), (1, 16)), -0.2, 0.2)), 2.4414062351624244e-12, 9.765624940649698e-12),
    }


HIGHEST = lax.Precision.HIGHEST
NORM_EPS = 1e-12
CLIP_NORM = 0.02
FIRST_DECAY = 0.9
STAT_DECAY = 0.99
MAT_RATE = 0.1
MAT_DECAY = 0.01
VEC_RATE = 0.05
VEC_SECOND = 0.999
VEC_EPS = 1e-08
VEC_DECAY = 0.01

@jax.custom_vjp
def low(v):
    return lax.optimization_barrier(v.astype(jnp.bfloat16)).astype(jnp.float32)

@jax.custom_vjp
def low_back(v):
    return v

def low_keep(v):
    return (low(v), None)

def low_pass(kept, grad):
    return (grad,)

def back_keep(v):
    return (v, None)

def back_low(kept, grad):
    return (low(grad),)
low.defvjp(low_keep, low_pass)
low_back.defvjp(back_keep, back_low)

def product(left, right):
    return jnp.dot(left, right, precision=HIGHEST)

def layer_norm(values, gain, shift):
    centered = values - lax.optimization_barrier(jnp.mean(values, -1, keepdims=True))
    spread = lax.optimization_barrier(jnp.mean(centered * centered, -1, keepdims=True))
    return centered * lax.rsqrt(spread + NORM_EPS) * gain + shift

def gelu_exact(values):
    return jax.nn.gelu(values, approximate=False)

def branch(values, params):
    w_down, b_down, w_up, b_up = params
    hidden = low_back(product(low(values), w_down) + b_down)
    return low_back(product(low(gelu_exact(hidden)), w_up) + b_up)

def attend(projected, length):
    query_rows = projected[:, :D].reshape(SEQ, HEADS, HEAD_DIM)
    key_rows = projected[:, D:2 * D].reshape(SEQ, HEADS, HEAD_DIM)
    value_rows = projected[:, 2 * D:].reshape(SEQ, HEADS, HEAD_DIM)
    scores = jnp.einsum('qhd,khd->hqk', query_rows, key_rows, precision=HIGHEST) * HEAD_DIM ** (-0.5)
    scores = jnp.where((jnp.arange(SEQ) < length)[None, None, :], low_back(scores), -1e+30)
    softmax_low = low(jax.nn.softmax(scores, -1))
    mixed = jnp.einsum('hqk,khd->qhd', softmax_low, value_rows, precision=HIGHEST).reshape(SEQ, D)
    return low_back(low(mixed))

def layer(hidden, lengths, base, gains, adapter):
    w_qkv, w_out, w_up, w_down = base
    projected = low_back(low(product(low(hidden), w_qkv)))
    mixed = lax.map(jax.checkpoint(lambda row_pair: attend(row_pair[0], row_pair[1])), (projected, lengths))
    attended = layer_norm(hidden + low_back(product(mixed, w_out)), gains[0], gains[1])
    inner = low_back(product(low(attended), w_up))
    summed = low_back(product(low(gelu_exact(inner)), w_down)) + attended
    return layer_norm(summed + branch(summed, adapter), gains[2], gains[3])

def head_loss(normed, table_full, positions, targets, loss_weights):
    row_index = jnp.arange(normed.shape[0])[:, None]
    chosen = normed[row_index, positions].reshape(-1, D)
    logits = low_back(product(low(chosen), table_full.T))
    target_logit = jnp.take_along_axis(logits, targets.reshape(-1, 1), axis=1)[:, 0]
    return jnp.sum(loss_weights.reshape(-1).astype(jnp.float32) * (jax.nn.logsumexp(logits, -1) - target_logit))

def to_blocks(matrix):
    rows_in, cols_in = matrix.shape
    return matrix.reshape(rows_in // BLOCK, BLOCK, cols_in // BLOCK, BLOCK).transpose(0, 2, 1, 3).reshape(-1, BLOCK, BLOCK)

def from_blocks(blocks, rows_in, cols_in):
    return blocks.reshape(rows_in // BLOCK, cols_in // BLOCK, BLOCK, BLOCK).transpose(0, 2, 1, 3).reshape(rows_in, cols_in)

def split_params(blocks, vector):
    adapter_count = D * BOT // BLOCK ** 2
    coupling_count = HALF * INV_H // BLOCK ** 2
    second_end = 2 * adapter_count
    adapter = (from_blocks(blocks[:adapter_count], D, BOT), vector[:BOT], from_blocks(blocks[adapter_count:second_end], BOT, D), vector[BOT:BOT + D])
    coupling = (from_blocks(blocks[second_end:second_end + coupling_count], HALF, INV_H), vector[BOT + D:BOT + D + INV_H], from_blocks(blocks[second_end + coupling_count:], INV_H, HALF), vector[BOT + D + INV_H:])
    return (adapter, coupling)

def join_params(adapter, coupling):
    blocks = jnp.concatenate([to_blocks(adapter[0]), to_blocks(adapter[2]), to_blocks(coupling[0]), to_blocks(coupling[2])])
    vector = jnp.concatenate([adapter[1], adapter[3], coupling[1], coupling[3]])
    return (blocks, vector)

def reference(token_ids, lengths, positions, targets, loss_weights, embed_table, pos_table, norm_params, base_qkv, base_out, base_up, base_down, master, momentum, stat_left, stat_right, root_left, root_right, vectors, vec_first, vec_second):
    table_full = embed_table.astype(jnp.float32)
    embedded = table_full[token_ids] + pos_table.astype(jnp.float32)
    bases = [tuple((weight[section_index].astype(jnp.float32) for weight in (base_qkv, base_out, base_up, base_down))) for section_index in range(2)]
    rounded_blocks = master.astype(jnp.bfloat16).astype(jnp.float32)
    rounded_vectors = vectors.astype(jnp.bfloat16).astype(jnp.float32)
    params = tuple((split_params(rounded_blocks[section_index], rounded_vectors[section_index]) for section_index in range(2)))

    def total(params):
        coupling_one, coupling_two = (params[0][1], params[1][1])
        loss_total = jnp.zeros((), jnp.float32)
        for micro_batch in range(MICRO):
            started = layer_norm(embedded[micro_batch], norm_params[0, 0], norm_params[0, 1])
            left_half = started[..., :HALF] + branch(started[..., HALF:], coupling_one)
            right_half = started[..., HALF:] + branch(left_half, coupling_two)
            hidden = jnp.concatenate([left_half, right_half], -1)
            hidden = layer(hidden, lengths[micro_batch], bases[0], norm_params[0, 2:], params[0][0])
            hidden = low_back(low(hidden))
            hidden = layer(hidden, lengths[micro_batch], bases[1], norm_params[1, 2:], params[1][0])
            right_half = hidden[..., HALF:] - branch(hidden[..., :HALF], coupling_two)
            left_half = hidden[..., :HALF] - branch(right_half, coupling_one)
            normed = layer_norm(jnp.concatenate([left_half, right_half], -1), norm_params[1, 0], norm_params[1, 1])
            loss_total = loss_total + jax.checkpoint(head_loss)(normed, table_full, positions[micro_batch], targets[micro_batch], loss_weights[micro_batch])
        return loss_total
    loss_sum, pull_back = jax.vjp(total, params)
    weight_sum = jnp.sum(loss_weights.astype(jnp.float32))
    gradients = pull_back(jnp.ones_like(loss_sum) / weight_sum)[0]
    joined = [join_params(gradients[section_index][0], gradients[section_index][1]) for section_index in range(2)]
    grad_blocks = jnp.stack([joined_pair[0] for joined_pair in joined])
    grad_vectors = jnp.stack([joined_pair[1] for joined_pair in joined])
    grad_norm = jnp.sqrt(jnp.sum(grad_blocks * grad_blocks) + jnp.sum(grad_vectors * grad_vectors))
    factor = CLIP_NORM / jnp.maximum(grad_norm, CLIP_NORM)
    grad_blocks = grad_blocks * factor
    grad_vectors = grad_vectors * factor
    momentum_new = FIRST_DECAY * momentum + (1.0 - FIRST_DECAY) * grad_blocks
    left_new = STAT_DECAY * stat_left + (1.0 - STAT_DECAY) * jnp.einsum('snij,snkj->snik', grad_blocks, grad_blocks, precision=HIGHEST)
    right_new = STAT_DECAY * stat_right + (1.0 - STAT_DECAY) * jnp.einsum('snji,snjk->snik', grad_blocks, grad_blocks, precision=HIGHEST)
    direction = jnp.einsum('snij,snjk->snik', root_left, momentum_new, precision=HIGHEST)
    direction = jnp.einsum('snij,snjk->snik', direction, root_right, precision=HIGHEST)
    master_new = master - MAT_RATE * (direction + MAT_DECAY * master)
    first_new = FIRST_DECAY * vec_first + (1.0 - FIRST_DECAY) * grad_vectors
    second_new = VEC_SECOND * vec_second + (1.0 - VEC_SECOND) * grad_vectors * grad_vectors
    corrected_first = first_new / (1.0 - FIRST_DECAY ** STEP)
    corrected_second = second_new / (1.0 - VEC_SECOND ** STEP)
    vectors_new = vectors - VEC_RATE * (corrected_first / (jnp.sqrt(corrected_second) + VEC_EPS) + VEC_DECAY * vectors)
    return (grad_blocks, momentum_new, left_new, right_new, master_new, master_new.astype(jnp.bfloat16), first_new, second_new, vectors_new, grad_norm, loss_sum, weight_sum)
```

```python
import jax
import jax.numpy as jnp
import numpy as np
from jax import lax
from jax.sharding import PartitionSpec as P

D = 768
HEADS = 12
HEAD_DIM = 64
BOT = 384
INV_H = 192
SEQ = 512
COUNT = 32
MICRO = 2
BLOCK = 48
STEP = 10
HALF = 384
IDS = SEQ + COUNT

HIGHEST = lax.Precision.HIGHEST
NORM_EPS = 1e-12
CLIP_NORM = 0.02
FIRST_DECAY = 0.9
STAT_DECAY = 0.99
MAT_RATE = 0.1
MAT_DECAY = 0.01
VEC_RATE = 0.05
VEC_SECOND = 0.999
VEC_EPS = 1e-08
VEC_DECAY = 0.01
F32 = jnp.float32
BF16 = jnp.bfloat16

CDF_SCALE = 0.42 / 2.0**0.5
CDF_POLY = (
    0.2368242366796694,
    0.239585811361218,
    0.1947261443420679,
    0.2687426685879861,
    -0.13052645834187002,
    0.4406726942003943,
    -0.32025628294963193,
    0.07023101752398136,
)


def matmul(left, right):
    return jnp.dot(left, right, preferred_element_type=F32)


def matmul_t(left, right):
    return lax.dot_general(left, right, (((1,), (1,)), ((), ())), preferred_element_type=F32)


def inner_rows(left, right):
    return lax.dot_general(left, right, (((0,), (0,)), ((), ())), preferred_element_type=F32)


def low(values):
    return values.astype(BF16)


def gelu_both(values):
    ratio = 1.0 / (1.0 + CDF_SCALE * jnp.abs(values))
    poly = jnp.full_like(ratio, 0.5 * CDF_POLY[-1])
    for factor in CDF_POLY[-2::-1]:
        poly = poly * ratio + 0.5 * factor
    bell = jnp.exp(-0.5 * values * values)
    tail = bell * (poly * ratio)
    cdf = jnp.where(values < 0, tail, 1.0 - tail)
    return values * cdf, cdf + values * (bell * (2.0 * np.pi) ** -0.5)


def layer_norm(values, gain, shift):
    centered = values - jnp.mean(values, -1, keepdims=True)
    inverse = lax.rsqrt(jnp.mean(centered * centered, -1, keepdims=True) + NORM_EPS)
    normal = centered * inverse
    return normal * gain + shift, (normal, inverse)


def norm_back(incoming, kept, gain):
    normal, inverse = kept
    scaled = incoming * gain
    return inverse * (
        scaled
        - jnp.mean(scaled, -1, keepdims=True)
        - normal * jnp.mean(scaled * normal, -1, keepdims=True)
    )


def to_blocks(matrix):
    rows_in, cols_in = matrix.shape
    return (
        matrix.reshape(rows_in // BLOCK, BLOCK, cols_in // BLOCK, BLOCK)
        .transpose(0, 2, 1, 3)
        .reshape(-1, BLOCK, BLOCK)
    )


def from_blocks(blocks, rows_in, cols_in):
    return (
        blocks.reshape(rows_in // BLOCK, cols_in // BLOCK, BLOCK, BLOCK)
        .transpose(0, 2, 1, 3)
        .reshape(rows_in, cols_in)
    )


def split_params(blocks, vector):
    adapter_count = D * BOT // BLOCK**2
    half_count = HALF * INV_H // BLOCK**2
    split_at = 2 * adapter_count
    adapter = (
        from_blocks(blocks[:adapter_count], D, BOT),
        vector[:BOT],
        from_blocks(blocks[adapter_count:split_at], BOT, D),
        vector[BOT : BOT + D],
    )
    coupling = (
        from_blocks(blocks[split_at : split_at + half_count], HALF, INV_H),
        vector[BOT + D : BOT + D + INV_H],
        from_blocks(blocks[split_at + half_count :], INV_H, HALF),
        vector[BOT + D + INV_H :],
    )
    return adapter, coupling


def join_params(adapter, coupling):
    blocks = jnp.concatenate(
        [to_blocks(adapter[0]), to_blocks(adapter[2]), to_blocks(coupling[0]), to_blocks(coupling[2])]
    )
    return blocks, jnp.concatenate([adapter[1], adapter[3], coupling[1], coupling[3]])


def branch_fwd(values, params):
    w_down, b_down, w_up, b_up = params
    low_in = low(values)
    active, slope = gelu_both(matmul(low_in, w_down) + b_down.astype(F32))
    active = low(active)
    return matmul(active, w_up) + b_up.astype(F32), (low_in, active, slope)


def branch_back(incoming, kept, params, inward=True):
    w_down, b_down, w_up, b_up = params
    low_in, active, slope = kept
    grad_low = low(incoming)
    hidden_grad = low(matmul_t(grad_low, w_up) * slope)
    weight_grads = (
        inner_rows(low_in, hidden_grad),
        jnp.sum(hidden_grad.astype(F32), 0),
        inner_rows(active, grad_low),
        jnp.sum(grad_low.astype(F32), 0),
    )
    return matmul_t(hidden_grad, w_down) if inward else None, weight_grads


def heads_of(rows):
    return rows.reshape(rows.shape[0], -1, HEAD_DIM)


def attend_fwd(query, key, value, length):
    scores = jnp.einsum("qhd,khd->hqk", heads_of(query), heads_of(key), preferred_element_type=F32)
    scores = scores * HEAD_DIM**-0.5
    scores = jnp.where((jnp.arange(SEQ) < length)[None, None, :], scores, -1e30)
    exponent = jnp.exp(scores - jnp.max(scores, -1, keepdims=True))
    soft = exponent * (1.0 / jnp.sum(exponent, -1, keepdims=True))
    mixed = jnp.einsum("hqk,khd->qhd", low(soft), heads_of(value), preferred_element_type=F32)
    return low(mixed.reshape(query.shape)), soft


def attend_back(query, key, value, soft, mixed_grad):
    grad_heads = heads_of(mixed_grad)
    weight_grad = jnp.einsum("qhd,khd->hqk", grad_heads, heads_of(value), preferred_element_type=F32)
    score_grad = low(soft * (weight_grad - jnp.sum(weight_grad * soft, -1, keepdims=True)))
    scale = HEAD_DIM**-0.5
    query_grad = jnp.einsum("hqk,khd->qhd", score_grad, heads_of(key), preferred_element_type=F32) * scale
    key_grad = jnp.einsum("hqk,qhd->khd", score_grad, heads_of(query), preferred_element_type=F32) * scale
    value_grad = jnp.einsum("hqk,qhd->khd", low(soft), grad_heads, preferred_element_type=F32)
    return tuple(low(grad.reshape(-1, D)) for grad in (query_grad, key_grad, value_grad))


def rest_fwd(hidden, mixed, weights):
    w_out, w_up, w_down, gains, adapter = weights
    attended, kept_one = layer_norm(hidden + matmul(mixed, w_out), gains[0], gains[1])
    active, slope = gelu_both(matmul(low(attended), w_up))
    summed = matmul(low(active), w_down) + attended
    branch_out, kept_branch = branch_fwd(summed, adapter)
    result, kept_two = layer_norm(summed + branch_out, gains[2], gains[3])
    return result, (kept_one, low(slope), kept_branch, kept_two)


def rest_back(incoming, kept, weights):
    w_out, w_up, w_down, gains, adapter = weights
    kept_one, slope, kept_branch, kept_two = kept
    second_grad = norm_back(incoming, kept_two, gains[2])
    branch_grad, adapter_grads = branch_back(second_grad, kept_branch, adapter)
    summed_grad = second_grad + branch_grad
    inner_grad = low(matmul_t(low(summed_grad), w_down) * slope.astype(F32))
    attended_grad = summed_grad + matmul_t(inner_grad, w_up)
    start_grad = norm_back(attended_grad, kept_one, gains[0])
    return start_grad, low(matmul_t(low(start_grad), w_out)), adapter_grads


def swap_add(own, other):
    came = lax.ppermute(low(other), "section", [(0, 1), (1, 0)])
    return own + came.astype(F32)


def pick(first_section, both):
    return jnp.where(first_section, both[0], both[1])


def plan_requests(ids, vocab_rows, slots):
    earlier = jnp.arange(IDS)[None, :] < jnp.arange(IDS)[:, None]
    same_id = ids[:, :, None] == ids[:, None, :]
    first = jnp.logical_not(jnp.any(same_id & earlier, -1))
    owner = ids // vocab_rows
    same_owner = owner[:, :, None] == owner[:, None, :]
    rank = jnp.sum((same_owner & earlier & first[:, None, :]).astype(jnp.int32), -1)
    slot = jnp.sum(jnp.where(same_id & first[:, None, :], rank[:, None, :], 0), -1)
    rounds = jnp.max(rank) // slots + 1
    return owner, slot, first, rounds


def fetch_rows(table, ids, first_section, weight_part, slots):
    parts = lax.axis_size("dp")
    vocab_rows = table.shape[0]
    owner, slot, first, rounds = plan_requests(ids, vocab_rows, slots)
    ids, owner, slot, first = (pick(first_section, both) for both in (ids, owner, slot, first))
    local = ids - owner * vocab_rows

    def places(turn):
        here = slot - turn * slots
        spot = jnp.where((here >= 0) & (here < slots), owner * slots + here, -1)
        return spot[:, None] == jnp.arange(parts * slots)[None, :]

    def wanted(hits):
        return jnp.sum(jnp.where(hits & first[:, None], local[:, None], 0), 0).reshape(parts, slots)

    def answer(asked, hits):
        rows = table.at[asked.reshape(-1)].get(mode="promise_in_bounds").reshape(parts, slots, D)
        came = lax.all_to_all(rows, "dp", 0, 0).reshape(parts * slots, D)
        return matmul(hits.astype(BF16), came)

    hits = places(0)
    extra = jnp.broadcast_to(jnp.stack([rounds, weight_part])[None], (parts, 2))
    asked = lax.all_to_all(jnp.concatenate([wanted(hits), extra], 1), "dp", 0, 0)
    total_rounds = jnp.max(asked[:, slots])
    weight_sum = jnp.sum(asked[:, slots + 1])
    rows = answer(asked[:, :slots], hits)

    def more(state):
        return state[0] < total_rounds

    def another(state):
        turn, rows = state
        hits = places(turn)
        asked = lax.all_to_all(wanted(hits), "dp", 0, 0)
        return turn + 1, rows + answer(asked, hits)

    return lax.while_loop(more, another, (jnp.int32(1), rows))[1], weight_sum.astype(F32)


def three_low(values):
    high = low(values)
    rest = values - high.astype(F32)
    middle = low(rest)
    return [high, middle, low(rest - middle.astype(F32))]


def head_parts(rows, table):
    logits = matmul_t(rows, table)
    highest = jnp.max(logits, -1, keepdims=True)
    exponent = jnp.exp(logits - highest)
    return matmul(low(exponent), table), highest, jnp.sum(exponent, -1, keepdims=True)


def head(normed, target_rows, row_weights, weight_sum, table):
    parts = lax.axis_size("dp")
    mine = low(normed)
    rows = lax.all_to_all(
        jnp.broadcast_to(mine[None], (parts, COUNT, D)), "dp", 0, 0
    ).reshape(parts * COUNT, D)
    mixed, highest, exp_total = head_parts(rows, table)
    stats = jnp.concatenate(three_low(highest) + three_low(exp_total), -1)
    stats = jnp.pad(stats, ((0, 0), (0, 128 - stats.shape[1])))
    packed = jnp.concatenate([low(mixed), stats], -1).reshape(parts, COUNT, D + 128)
    came = lax.all_to_all(packed, "dp", 0, 0).astype(F32)
    highest = jnp.sum(came[:, :, D : D + 3], -1)
    exp_total = jnp.sum(came[:, :, D + 3 : D + 6], -1)
    top = jnp.max(highest, 0)
    factor = jnp.exp(highest - top)
    total = jnp.sum(exp_total * factor, 0)
    target_logit = jnp.sum(mine.astype(F32) * target_rows, -1)
    loss = jnp.sum(row_weights * (top + jnp.log(total) - target_logit))
    expected = jnp.sum(came[:, :, :D] * (factor / total)[:, :, None], 0)
    return loss, (row_weights / weight_sum)[:, None] * (expected - target_rows)


def shards(
    token_ids,
    lengths,
    positions,
    targets,
    loss_weights,
    embed_table,
    pos_table,
    norm_params,
    base_qkv,
    base_out,
    base_up,
    base_down,
    master,
    momentum,
    stat_left,
    stat_right,
    root_left,
    root_right,
    vectors,
    vec_first,
    vec_second,
):
    parts = lax.axis_size("dp")
    first_section = lax.axis_index("section") == 0
    slots = -(-IDS * 5 // (4 * parts * 16)) * 16

    ids = jnp.concatenate([token_ids[:, 0], targets[:, 0]], -1)
    weight_part = jnp.sum(loss_weights)
    fetched, weight_sum = fetch_rows(embed_table, ids, first_section, weight_part, slots)
    length = pick(first_section, lengths[:, 0])
    spots = pick(first_section, positions[:, 0])
    row_weights = pick(first_section, loss_weights[:, 0]).astype(F32)

    own_blocks = master.shape[1]
    own_vector = vectors.shape[1]
    flat = low(jnp.concatenate([master[0].reshape(-1), vectors[0]]))
    gathered = lax.all_gather(flat, ("section", "dp")).reshape(MICRO, parts, -1)
    all_blocks = gathered[:, :, : own_blocks * BLOCK**2].reshape(MICRO, parts * own_blocks, BLOCK, BLOCK)
    all_vectors = gathered[:, :, own_blocks * BLOCK**2 :].reshape(MICRO, parts * own_vector)
    params = [split_params(all_blocks[s], all_vectors[s]) for s in range(MICRO)]
    adapters = [pair[0] for pair in params]
    coupling_one, coupling_two = (pair[1] for pair in params)
    norms = lax.all_gather(norm_params, "section", axis=0, tiled=True)
    w_qkv, w_out, w_up, w_down = (
        lax.all_gather(weight, "section", axis=0, tiled=True)
        for weight in (base_qkv, base_out, base_up, base_down)
    )
    rests = [(w_out[s], w_up[s], w_down[s], norms[s, 2:], adapters[s]) for s in range(MICRO)]

    started, _ = layer_norm(fetched[:SEQ] + pos_table.astype(F32), norms[0, 0], norms[0, 1])
    one_out, kept_one = branch_fwd(started[:, HALF:], coupling_one)
    left_half = started[:, :HALF] + one_out
    two_out, kept_two = branch_fwd(left_half, coupling_two)
    hidden = jnp.concatenate([left_half, started[:, HALF:] + two_out], -1)
    projected = low(matmul(low(hidden), w_qkv[0]))
    query, key, value = projected[:, :D], projected[:, D : 2 * D], projected[:, 2 * D :]
    mixed, soft = attend_fwd(query, key, value, length)
    section_out, kept_rest = rest_fwd(hidden, mixed, rests[0])
    section_out = low(section_out)

    chosen = (spots[:, None] == jnp.arange(SEQ)[None, :]).astype(BF16)
    at_spots = matmul(chosen, section_out)
    query_1 = low(matmul(low(at_spots), w_qkv[1][:, :D]))
    key_value = low(matmul(section_out, w_qkv[1][:, D:]))
    key_1, value_1 = key_value[:, :D], key_value[:, D:]
    mixed_1, soft_1 = attend_fwd(query_1, key_1, value_1, length)
    out_1, kept_rest_1 = rest_fwd(at_spots, mixed_1, rests[1])
    two_last, kept_two_last = branch_fwd(out_1[:, :HALF], coupling_two)
    right_last = out_1[:, HALF:] - two_last
    one_last, kept_one_last = branch_fwd(right_last, coupling_one)
    normed, kept_head = layer_norm(
        jnp.concatenate([out_1[:, :HALF] - one_last, right_last], -1), norms[1, 0], norms[1, 1]
    )

    loss_part, normed_grad = head(normed, fetched[SEQ:], row_weights, weight_sum, embed_table)

    restored_grad = norm_back(normed_grad, kept_head, norms[1, 0])
    left_grad = restored_grad[:, :HALF]
    into_right, grads_one = branch_back(-left_grad, kept_one_last, coupling_one)
    right_grad = restored_grad[:, HALF:] + into_right
    into_left, grads_two = branch_back(-right_grad, kept_two_last, coupling_two)
    out_grad = jnp.concatenate([left_grad + into_left, right_grad], -1)
    start_grad, mixed_grad, adapter_grads_1 = rest_back(out_grad, kept_rest_1, rests[1])
    query_grad, key_grad, value_grad = attend_back(query_1, key_1, value_1, soft_1, mixed_grad)
    spot_grad = start_grad + matmul_t(query_grad, w_qkv[1][:, :D])
    section_grad = (
        lax.dot_general(chosen.astype(F32), spot_grad, (((0,), (0,)), ((), ())), precision=HIGHEST)
        + matmul_t(key_grad, w_qkv[1][:, D : 2 * D])
        + matmul_t(value_grad, w_qkv[1][:, 2 * D :])
    )
    section_grad = low(section_grad).astype(F32)

    start_grad, mixed_grad, adapter_grads_0 = rest_back(section_grad, kept_rest, rests[0])
    query_grad, key_grad, value_grad = attend_back(query, key, value, soft, mixed_grad)
    hidden_grad = start_grad + matmul_t(
        jnp.concatenate([query_grad, key_grad, value_grad], -1), w_qkv[0]
    )
    into_left, first_two = branch_back(hidden_grad[:, HALF:], kept_two, coupling_two)
    _, first_one = branch_back(hidden_grad[:, :HALF] + into_left, kept_one, coupling_one, False)
    grads_one = jax.tree.map(jnp.add, grads_one, first_one)
    grads_two = jax.tree.map(jnp.add, grads_two, first_two)

    joined = [join_params(adapter_grads_0, grads_one), join_params(adapter_grads_1, grads_two)]
    flat = [
        jnp.concatenate(
            [blocks.reshape(parts, own_blocks * BLOCK**2), vector.reshape(parts, own_vector)], 1
        )
        for blocks, vector in joined
    ]
    summed = swap_add(
        jnp.where(first_section, flat[0], flat[1]), jnp.where(first_section, flat[1], flat[0])
    )
    owned = jnp.sum(lax.all_to_all(low(summed), "dp", 0, 0).astype(F32), 0)
    grad_blocks = owned[: own_blocks * BLOCK**2].reshape(own_blocks, BLOCK, BLOCK)
    grad_vector = owned[own_blocks * BLOCK**2 :]

    squares = jnp.sum(owned * owned)
    pair = jnp.broadcast_to(jnp.stack([squares, loss_part])[None], (parts * MICRO, 2))
    totals = jnp.sum(lax.all_to_all(pair, ("dp", "section"), 0, 0), 0)
    grad_norm = jnp.sqrt(totals[0])
    loss_sum = totals[1]
    factor = CLIP_NORM / jnp.maximum(grad_norm, CLIP_NORM)
    clipped = grad_blocks * factor
    clipped_vector = grad_vector * factor
    momentum_new = FIRST_DECAY * momentum[0] + (1.0 - FIRST_DECAY) * clipped
    left_new = STAT_DECAY * stat_left[0] + (1.0 - STAT_DECAY) * jnp.einsum(
        "nij,nkj->nik", clipped, clipped, precision=HIGHEST
    )
    right_new = STAT_DECAY * stat_right[0] + (1.0 - STAT_DECAY) * jnp.einsum(
        "nji,njk->nik", clipped, clipped, precision=HIGHEST
    )
    direction = jnp.einsum("nij,njk->nik", root_left[0], momentum_new, precision=HIGHEST)
    direction = jnp.einsum("nij,njk->nik", direction, root_right[0], precision=HIGHEST)
    master_new = master[0] - MAT_RATE * (direction + MAT_DECAY * master[0])
    first_new = FIRST_DECAY * vec_first[0] + (1.0 - FIRST_DECAY) * clipped_vector
    second_new = VEC_SECOND * vec_second[0] + (1.0 - VEC_SECOND) * clipped_vector * clipped_vector
    corrected_first = first_new / (1.0 - FIRST_DECAY**STEP)
    corrected_second = second_new / (1.0 - VEC_SECOND**STEP)
    vectors_new = vectors[0] - VEC_RATE * (
        corrected_first / (jnp.sqrt(corrected_second) + VEC_EPS) + VEC_DECAY * vectors[0]
    )
    return (
        clipped[None],
        momentum_new[None],
        left_new[None],
        right_new[None],
        master_new[None],
        master_new.astype(BF16)[None],
        first_new[None],
        second_new[None],
        vectors_new[None],
        grad_norm,
        loss_sum,
        weight_sum,
    )


def solution(mesh):
    rows = P(None, "dp", None)
    section = P("section", None, None)
    blocks = P("section", "dp", None, None)
    biases = P("section", "dp")
    return jax.shard_map(
        shards,
        mesh=mesh,
        in_specs=(rows, P(None, "dp"), rows, rows, rows, P("dp", None), P())
        + (section,) * 5
        + (blocks,) * 6
        + (biases,) * 3,
        out_specs=(blocks,) * 6 + (biases,) * 3 + (P(),) * 3,
        check_vma=False,
    )
```

```python
import jax
import jax.numpy as jnp
import numpy as np
from jax import lax
from jax.experimental import pallas as pl
from jax.experimental.pallas import tpu as pltpu
from jax.sharding import PartitionSpec as P

D = 768
HEADS = 12
HEAD_DIM = 64
BOT = 384
INV_H = 192
SEQ = 512
COUNT = 32
MICRO = 2
BLOCK = 48
STEP = 10
HALF = 384
IDS = SEQ + COUNT

HIGHEST = lax.Precision.HIGHEST
NORM_EPS = 1e-12
CLIP_NORM = 0.02
FIRST_DECAY = 0.9
STAT_DECAY = 0.99
MAT_RATE = 0.1
MAT_DECAY = 0.01
VEC_RATE = 0.05
VEC_SECOND = 0.999
VEC_EPS = 1e-08
VEC_DECAY = 0.01
F32 = jnp.float32
BF16 = jnp.bfloat16

CDF_SCALE = 0.42 / 2.0**0.5
CDF_POLY = (
    0.2368242366796694,
    0.239585811361218,
    0.1947261443420679,
    0.2687426685879861,
    -0.13052645834187002,
    0.4406726942003943,
    -0.32025628294963193,
    0.07023101752398136,
)


def matmul(left, right):
    return jnp.dot(left, right, preferred_element_type=F32)


def matmul_t(left, right):
    return lax.dot_general(left, right, (((1,), (1,)), ((), ())), preferred_element_type=F32)


def inner_rows(left, right):
    return lax.dot_general(left, right, (((0,), (0,)), ((), ())), preferred_element_type=F32)


def low(values):
    return values.astype(BF16)


def gelu_both(values):
    ratio = 1.0 / (1.0 + CDF_SCALE * jnp.abs(values))
    poly = jnp.full_like(ratio, 0.5 * CDF_POLY[-1])
    for factor in CDF_POLY[-2::-1]:
        poly = poly * ratio + 0.5 * factor
    bell = jnp.exp(-0.5 * values * values)
    tail = bell * (poly * ratio)
    cdf = jnp.where(values < 0, tail, 1.0 - tail)
    return values * cdf, cdf + values * (bell * (2.0 * np.pi) ** -0.5)


def layer_norm(values, gain, shift):
    centered = values - jnp.mean(values, -1, keepdims=True)
    inverse = lax.rsqrt(jnp.mean(centered * centered, -1, keepdims=True) + NORM_EPS)
    normal = centered * inverse
    return normal * gain + shift, (normal, inverse)


def norm_back(incoming, kept, gain):
    normal, inverse = kept
    scaled = incoming * gain
    return inverse * (
        scaled
        - jnp.mean(scaled, -1, keepdims=True)
        - normal * jnp.mean(scaled * normal, -1, keepdims=True)
    )


def to_blocks(matrix):
    rows_in, cols_in = matrix.shape
    return (
        matrix.reshape(rows_in // BLOCK, BLOCK, cols_in // BLOCK, BLOCK)
        .transpose(0, 2, 1, 3)
        .reshape(-1, BLOCK, BLOCK)
    )


def from_blocks(blocks, rows_in, cols_in):
    return (
        blocks.reshape(rows_in // BLOCK, cols_in // BLOCK, BLOCK, BLOCK)
        .transpose(0, 2, 1, 3)
        .reshape(rows_in, cols_in)
    )


def split_params(blocks, vector):
    adapter_count = D * BOT // BLOCK**2
    half_count = HALF * INV_H // BLOCK**2
    split_at = 2 * adapter_count
    adapter = (
        from_blocks(blocks[:adapter_count], D, BOT),
        vector[:BOT],
        from_blocks(blocks[adapter_count:split_at], BOT, D),
        vector[BOT : BOT + D],
    )
    coupling = (
        from_blocks(blocks[split_at : split_at + half_count], HALF, INV_H),
        vector[BOT + D : BOT + D + INV_H],
        from_blocks(blocks[split_at + half_count :], INV_H, HALF),
        vector[BOT + D + INV_H :],
    )
    return adapter, coupling


def join_params(adapter, coupling):
    blocks = jnp.concatenate(
        [to_blocks(adapter[0]), to_blocks(adapter[2]), to_blocks(coupling[0]), to_blocks(coupling[2])]
    )
    return blocks, jnp.concatenate([adapter[1], adapter[3], coupling[1], coupling[3]])


def branch_fwd(values, params):
    w_down, b_down, w_up, b_up = params
    low_in = low(values)
    active, slope = gelu_both(matmul(low_in, w_down) + b_down.astype(F32))
    active = low(active)
    return matmul(active, w_up) + b_up.astype(F32), (low_in, active, slope)


def branch_back(incoming, kept, params, inward=True):
    w_down, b_down, w_up, b_up = params
    low_in, active, slope = kept
    grad_low = low(incoming)
    hidden_grad = low(matmul_t(grad_low, w_up) * slope)
    weight_grads = (
        inner_rows(low_in, hidden_grad),
        jnp.sum(hidden_grad.astype(F32), 0),
        inner_rows(active, grad_low),
        jnp.sum(grad_low.astype(F32), 0),
    )
    return matmul_t(hidden_grad, w_down) if inward else None, weight_grads


def heads_of(rows):
    return rows.reshape(rows.shape[0], -1, HEAD_DIM)


def attend_fwd(query, key, value, length):
    scores = jnp.einsum("qhd,khd->hqk", heads_of(query), heads_of(key), preferred_element_type=F32)
    scores = scores * HEAD_DIM**-0.5
    scores = jnp.where((jnp.arange(SEQ) < length)[None, None, :], scores, -1e30)
    exponent = jnp.exp(scores - jnp.max(scores, -1, keepdims=True))
    soft = exponent * (1.0 / jnp.sum(exponent, -1, keepdims=True))
    mixed = jnp.einsum("hqk,khd->qhd", low(soft), heads_of(value), preferred_element_type=F32)
    return low(mixed.reshape(query.shape)), soft


def attend_back(query, key, value, soft, mixed_grad):
    grad_heads = heads_of(mixed_grad)
    weight_grad = jnp.einsum("qhd,khd->hqk", grad_heads, heads_of(value), preferred_element_type=F32)
    score_grad = low(soft * (weight_grad - jnp.sum(weight_grad * soft, -1, keepdims=True)))
    scale = HEAD_DIM**-0.5
    query_grad = jnp.einsum("hqk,khd->qhd", score_grad, heads_of(key), preferred_element_type=F32) * scale
    key_grad = jnp.einsum("hqk,qhd->khd", score_grad, heads_of(query), preferred_element_type=F32) * scale
    value_grad = jnp.einsum("hqk,qhd->khd", low(soft), grad_heads, preferred_element_type=F32)
    return tuple(low(grad.reshape(-1, D)) for grad in (query_grad, key_grad, value_grad))


def rest_fwd(hidden, mixed, weights):
    w_out, w_up, w_down, gains, adapter = weights
    attended, kept_one = layer_norm(hidden + matmul(mixed, w_out), gains[0], gains[1])
    active, slope = gelu_both(matmul(low(attended), w_up))
    summed = matmul(low(active), w_down) + attended
    branch_out, kept_branch = branch_fwd(summed, adapter)
    result, kept_two = layer_norm(summed + branch_out, gains[2], gains[3])
    return result, (kept_one, low(slope), kept_branch, kept_two)


def rest_back(incoming, kept, weights):
    w_out, w_up, w_down, gains, adapter = weights
    kept_one, slope, kept_branch, kept_two = kept
    second_grad = norm_back(incoming, kept_two, gains[2])
    branch_grad, adapter_grads = branch_back(second_grad, kept_branch, adapter)
    summed_grad = second_grad + branch_grad
    inner_grad = low(matmul_t(low(summed_grad), w_down) * slope.astype(F32))
    attended_grad = summed_grad + matmul_t(inner_grad, w_up)
    start_grad = norm_back(attended_grad, kept_one, gains[0])
    return start_grad, low(matmul_t(low(start_grad), w_out)), adapter_grads


GROUP_ROWS = 72
LANES = 128


def whole(shape):
    return pl.BlockSpec(shape, lambda *_: (0,) * len(shape))


def section_of(shape, section):
    return pl.BlockSpec((None,) + shape, lambda *_: (section,) + (0,) * len(shape))


def params_for(mebibytes):
    return pltpu.CompilerParams(vmem_limit_bytes=mebibytes * 2**20)


def roll(values, shift):
    return pltpu.roll(values, shift, 1)


def lane_of(values):
    return lax.broadcasted_iota(jnp.int32, values.shape, 1)


def fold_half(values, upper):
    top, bottom = values[:24], values[24:]
    if upper:
        return jnp.where(lane_of(top) < 64, roll(top, 64), bottom)
    return jnp.where(lane_of(top) < 64, top, roll(bottom, 64))


def unfold_half(values, upper):
    turned = roll(values, 64)
    return jnp.concatenate([turned, values] if upper else [values, turned], 0)


def join_pair(main_0, rest_0, main_1, rest_1):
    left = lane_of(main_0) < 64
    turned = roll(main_1, 64)
    return (
        main_0,
        jnp.where(left, unfold_half(rest_0, False), turned),
        jnp.where(left, turned, unfold_half(rest_1, True)),
    )


def cut_pair(tile_0, tile_1, tile_2):
    left = lane_of(tile_0) < 64
    return (
        (tile_0, fold_half(tile_1, False)),
        (jnp.where(left, roll(tile_1, 64), roll(tile_2, 64)), fold_half(tile_2, True)),
    )


def chunk_rows(own_blocks):
    return own_blocks // 4 * GROUP_ROWS + 8


def pack_own(master, bias_rows):
    count = master.shape[0]

    def kernel(master_ref, bias_ref, out_ref):
        row = lax.broadcasted_iota(jnp.int32, (BLOCK, 256), 0)
        col = lax.broadcasted_iota(jnp.int32, (BLOCK, 256), 1)
        pieces = []
        for group in range(count // 4):
            wide = jnp.zeros((BLOCK, 256), F32)
            for j in range(4):
                wide += matmul(low(master_ref[4 * group + j]), (col == row + BLOCK * j).astype(BF16))
            pieces += [wide[:, :LANES], fold_half(wide[:, LANES:], False)]
        out_ref[...] = low(jnp.concatenate(pieces + [bias_ref[...]], 0))

    return pl.pallas_call(
        kernel,
        out_shape=jax.ShapeDtypeStruct((chunk_rows(count), LANES), BF16),
        name="pack_own",
    )(master, bias_rows)


MATRICES = ((D, BOT), (BOT, D), (HALF, INV_H), (INV_H, HALF))


def unpack_all(gathered):
    sections, parts, rows, _ = gathered.shape
    per_part = (rows - 8) // GROUP_ROWS

    def kernel(in_ref, *out_refs):
        cache = {}

        def group(index):
            part = index // per_part
            if part not in cache:
                cache.clear()
                cache[part] = in_ref[part].astype(F32)
            base = index % per_part * GROUP_ROWS
            chunk = cache[part]
            return chunk[base : base + BLOCK], chunk[base + BLOCK : base + GROUP_ROWS]

        index = 0
        for (height, width), out_ref in zip(MATRICES, out_refs):
            for top in range(0, height, BLOCK):
                if width == INV_H:
                    main, rest = group(index)
                    index += 1
                    out_ref[top : top + BLOCK, :LANES] = low(main)
                    out_ref[top : top + BLOCK, LANES:] = low(unfold_half(rest, False)[:, :64])
                    continue
                for left in range(0, width, HALF):
                    tiles = join_pair(*group(index), *group(index + 1))
                    index += 2
                    for j, tile in enumerate(tiles):
                        at = left + j * LANES
                        out_ref[top : top + BLOCK, at : at + LANES] = low(tile)

    return pl.pallas_call(
        kernel,
        grid=(sections,),
        in_specs=[pl.BlockSpec((None, parts, rows, LANES), lambda s: (s, 0, 0, 0))],
        out_specs=[pl.BlockSpec((None,) + shape, lambda s: (s, 0, 0)) for shape in MATRICES],
        out_shape=[jax.ShapeDtypeStruct((sections,) + shape, BF16) for shape in MATRICES],
        compiler_params=params_for(32),
        name="unpack_all",
    )(gathered)


def pack_grads(grads, bias_rows, own_index, parts):
    per_part = 80 // parts
    rows = per_part * GROUP_ROWS + 8

    def kernel(index_ref, *refs):
        bias_ref, own_ref, other_ref = refs[8:]
        own = index_ref[0]
        for section in range(MICRO):
            pieces = []
            for (height, width), ref in zip(MATRICES, refs[4 * section : 4 * section + 4]):
                for top in range(0, height, BLOCK):
                    band = slice(top, top + BLOCK)
                    if width == INV_H:
                        tail = ref[band, LANES:]
                        tail = jnp.concatenate([tail, tail], 1)
                        pieces.append((ref[band, :LANES], fold_half(tail, False)))
                        continue
                    for left in range(0, width, HALF):
                        tiles = [ref[band, left + j * LANES : left + (j + 1) * LANES] for j in range(3)]
                        pieces += cut_pair(*tiles)
                while len(pieces) >= per_part:
                    part = sum_done[section]
                    sum_done[section] += 1
                    chunk = [half for pair in pieces[:per_part] for half in pair]
                    del pieces[:per_part]
                    chunk = jnp.concatenate(chunk + [bias_ref[section, part]], 0)

                    @pl.when(own == section)
                    def _(part=part, chunk=chunk):
                        own_ref[part] = chunk

                    @pl.when(own != section)
                    def _(part=part, chunk=chunk):
                        other_ref[part] = low(chunk)

    sum_done = [0, 0]
    return pl.pallas_call(
        kernel,
        in_specs=[pl.BlockSpec(memory_space=pltpu.SMEM)] + [pl.BlockSpec(memory_space=pltpu.VMEM)] * 9,
        out_shape=[
            jax.ShapeDtypeStruct((parts, rows, LANES), F32),
            jax.ShapeDtypeStruct((parts, rows, LANES), BF16),
        ],
        compiler_params=params_for(40),
        name="pack_grads",
    )(own_index, *grads[0], *grads[1], bias_rows)


def sum_owned(came, loss_part, copies):
    parts, rows, _ = came.shape
    per_part = (rows - 8) // GROUP_ROWS

    def kernel(loss_ref, came_ref, blocks_ref, bias_ref, pair_ref):
        total = came_ref[0].astype(F32)
        for part in range(1, parts):
            total += came_ref[part].astype(F32)
        for group in range(per_part):
            base = group * GROUP_ROWS
            main = total[base : base + BLOCK]
            rest = unfold_half(total[base + BLOCK : base + GROUP_ROWS], False)
            lane = lane_of(main)
            parts_of = (
                main,
                roll(main, 80),
                jnp.where(lane < 32, roll(main, 32), roll(rest, 32)),
                roll(rest, 112),
            )
            for j, values in enumerate(parts_of):
                blocks_ref[4 * group + j] = values[:, :BLOCK]
        bias_ref[...] = total[rows - 8 :]
        squares = jnp.sum(jnp.sum(total * total, 0, keepdims=True), 1, keepdims=True)
        lane = lax.broadcasted_iota(jnp.int32, (1, LANES), 1)
        pair = jnp.where(lane == 0, squares, jnp.where(lane == 1, loss_ref[0], 0.0))
        pair_ref[...] = jnp.broadcast_to(pair[None], pair_ref.shape)

    return pl.pallas_call(
        kernel,
        in_specs=[pl.BlockSpec(memory_space=pltpu.SMEM), pl.BlockSpec(memory_space=pltpu.VMEM)],
        out_shape=[
            jax.ShapeDtypeStruct((4 * per_part, BLOCK, BLOCK), F32),
            jax.ShapeDtypeStruct((8, LANES), F32),
            jax.ShapeDtypeStruct((copies, 1, LANES), F32),
        ],
        compiler_params=params_for(32),
        name="sum_owned",
    )(loss_part, came)


def swap_add(own, other):
    came = lax.ppermute(low(other), "section", [(0, 1), (1, 0)])
    return own + came.astype(F32)


def pick(first_section, both):
    return jnp.where(first_section, both[0], both[1])


def plan_requests(ids, vocab_rows, slots):
    earlier = jnp.arange(IDS)[None, :] < jnp.arange(IDS)[:, None]
    same_id = ids[:, :, None] == ids[:, None, :]
    first = jnp.logical_not(jnp.any(same_id & earlier, -1))
    owner = ids // vocab_rows
    same_owner = owner[:, :, None] == owner[:, None, :]
    rank = jnp.sum((same_owner & earlier & first[:, None, :]).astype(jnp.int32), -1)
    slot = jnp.sum(jnp.where(same_id & first[:, None, :], rank[:, None, :], 0), -1)
    rounds = jnp.max(rank) // slots + 1
    return owner, slot, first, rounds


def fetch_rows(table, ids, first_section, weight_part, slots):
    parts = lax.axis_size("dp")
    vocab_rows = table.shape[0]
    owner, slot, first, rounds = plan_requests(ids, vocab_rows, slots)
    ids, owner, slot, first = (pick(first_section, both) for both in (ids, owner, slot, first))
    local = ids - owner * vocab_rows

    def places(turn):
        here = slot - turn * slots
        spot = jnp.where((here >= 0) & (here < slots), owner * slots + here, -1)
        return spot[:, None] == jnp.arange(parts * slots)[None, :]

    def wanted(hits):
        return jnp.sum(jnp.where(hits & first[:, None], local[:, None], 0), 0).reshape(parts, slots)

    def answer(asked, hits):
        rows = table.at[asked.reshape(-1)].get(mode="promise_in_bounds").reshape(parts, slots, D)
        came = lax.all_to_all(rows, "dp", 0, 0).reshape(parts * slots, D)
        return matmul(hits.astype(BF16), came)

    hits = places(0)
    extra = jnp.broadcast_to(jnp.stack([rounds, weight_part])[None], (parts, 2))
    asked = lax.all_to_all(jnp.concatenate([wanted(hits), extra], 1), "dp", 0, 0)
    total_rounds = jnp.max(asked[:, slots])
    weight_sum = jnp.sum(asked[:, slots + 1])
    rows = answer(asked[:, :slots], hits)

    def more(state):
        return state[0] < total_rounds

    def another(state):
        turn, rows = state
        hits = places(turn)
        asked = lax.all_to_all(wanted(hits), "dp", 0, 0)
        return turn + 1, rows + answer(asked, hits)

    return lax.while_loop(more, another, (jnp.int32(1), rows))[1], weight_sum.astype(F32)


def three_low(values):
    high = low(values)
    rest = values - high.astype(F32)
    middle = low(rest)
    return [high, middle, low(rest - middle.astype(F32))]


def head_parts(rows, table):
    logits = matmul_t(rows, table)
    highest = jnp.max(logits, -1, keepdims=True)
    exponent = jnp.exp(logits - highest)
    return matmul(low(exponent), table), highest, jnp.sum(exponent, -1, keepdims=True)


def head(normed, target_rows, row_weights, weight_sum, table):
    parts = lax.axis_size("dp")
    mine = low(normed)
    rows = lax.all_to_all(
        jnp.broadcast_to(mine[None], (parts, COUNT, D)), "dp", 0, 0
    ).reshape(parts * COUNT, D)
    mixed, highest, exp_total = head_parts(rows, table)
    stats = jnp.concatenate(three_low(highest) + three_low(exp_total), -1)
    stats = jnp.pad(stats, ((0, 0), (0, 128 - stats.shape[1])))
    packed = jnp.concatenate([low(mixed), stats], -1).reshape(parts, COUNT, D + 128)
    came = lax.all_to_all(packed, "dp", 0, 0).astype(F32)
    highest = jnp.sum(came[:, :, D : D + 3], -1)
    exp_total = jnp.sum(came[:, :, D + 3 : D + 6], -1)
    top = jnp.max(highest, 0)
    factor = jnp.exp(highest - top)
    total = jnp.sum(exp_total * factor, 0)
    target_logit = jnp.sum(mine.astype(F32) * target_rows, -1)
    loss = jnp.sum(row_weights * (top + jnp.log(total) - target_logit))
    expected = jnp.sum(came[:, :, :D] * (factor / total)[:, :, None], 0)
    return loss, (row_weights / weight_sum)[:, None] * (expected - target_rows)


def bias_chunks(vector, parts):
    rows = vector.reshape(-1, parts, 1, vector.shape[-1] // parts)
    return jnp.pad(rows, ((0, 0), (0, 0), (0, 7), (0, LANES - rows.shape[-1])))


def gather_params(master, vector):
    parts = lax.axis_size("dp")
    count, width = master.shape[0], vector.shape[0]
    if count % 4 == 0 and width <= LANES:
        packed = pack_own(master, bias_chunks(vector, 1)[0, 0])
        gathered = lax.all_gather(packed, ("section", "dp")).reshape(MICRO, parts, -1, LANES)
        vectors = gathered[:, :, -8, :width].reshape(MICRO, parts * width)
        matrices = unpack_all(gathered)
        params = []
        for s in range(MICRO):
            down, up, c_down, c_up = (matrix[s] for matrix in matrices)
            bias = vectors[s]
            adapter = (down, bias[:BOT], up, bias[BOT : BOT + D])
            coupling = (c_down, bias[BOT + D : BOT + D + INV_H], c_up, bias[BOT + D + INV_H :])
            params.append((adapter, coupling))
    else:
        flat = low(jnp.concatenate([master.reshape(-1), vector]))
        gathered = lax.all_gather(flat, ("section", "dp")).reshape(MICRO, parts, -1)
        size = count * BLOCK**2
        all_blocks = gathered[:, :, :size].reshape(MICRO, parts * count, BLOCK, BLOCK)
        all_vectors = gathered[:, :, size:].reshape(MICRO, parts * width)
        params = [split_params(all_blocks[s], all_vectors[s]) for s in range(MICRO)]
    return [pair[0] for pair in params], params[0][1], params[1][1]


def sum_at_owners(grads, loss_part, count):
    parts = lax.axis_size("dp")
    section = lax.axis_index("section")
    width = (BOT + D + INV_H + HALF) // parts
    if count % 4 == 0 and width <= LANES:
        matrices = [(a[0], a[2], c[0], c[2]) for a, c in grads]
        biases = jnp.stack([jnp.concatenate([a[1], a[3], c[1], c[3]]) for a, c in grads])
        own, other = pack_grads(
            matrices, bias_chunks(biases, parts), section.reshape(1).astype(jnp.int32), parts
        )
        came = lax.all_to_all(low(swap_add(own, other)), "dp", 0, 0)
        blocks, bias, pair = sum_owned(came, loss_part.reshape(1), parts * MICRO)
        return blocks, bias[0, :width], pair
    flat = []
    for adapter, coupling in grads:
        blocks, vector = join_params(adapter, coupling)
        flat.append(
            jnp.concatenate([blocks.reshape(parts, count * BLOCK**2), vector.reshape(parts, width)], 1)
        )
    first = section == 0
    summed = swap_add(jnp.where(first, flat[0], flat[1]), jnp.where(first, flat[1], flat[0]))
    owned = jnp.sum(lax.all_to_all(low(summed), "dp", 0, 0).astype(F32), 0)
    blocks = owned[: count * BLOCK**2].reshape(count, BLOCK, BLOCK)
    pair = jnp.stack([jnp.sum(owned * owned), loss_part])
    pair = jnp.broadcast_to(pair[None, None], (parts * MICRO, 1, 2))
    return blocks, owned[count * BLOCK**2 :], pair


def shards(
    token_ids,
    lengths,
    positions,
    targets,
    loss_weights,
    embed_table,
    pos_table,
    norm_params,
    base_qkv,
    base_out,
    base_up,
    base_down,
    master,
    momentum,
    stat_left,
    stat_right,
    root_left,
    root_right,
    vectors,
    vec_first,
    vec_second,
):
    parts = lax.axis_size("dp")
    first_section = lax.axis_index("section") == 0
    slots = -(-IDS * 5 // (4 * parts * 16)) * 16

    ids = jnp.concatenate([token_ids[:, 0], targets[:, 0]], -1)
    weight_part = jnp.sum(loss_weights)
    fetched, weight_sum = fetch_rows(embed_table, ids, first_section, weight_part, slots)
    length = pick(first_section, lengths[:, 0])
    spots = pick(first_section, positions[:, 0])
    row_weights = pick(first_section, loss_weights[:, 0]).astype(F32)

    adapters, coupling_one, coupling_two = gather_params(master[0], vectors[0])
    norms = lax.all_gather(norm_params, "section", axis=0, tiled=True)
    w_qkv, w_out, w_up, w_down = (
        lax.all_gather(weight, "section", axis=0, tiled=True)
        for weight in (base_qkv, base_out, base_up, base_down)
    )
    rests = [(w_out[s], w_up[s], w_down[s], norms[s, 2:], adapters[s]) for s in range(MICRO)]

    started, _ = layer_norm(fetched[:SEQ] + pos_table.astype(F32), norms[0, 0], norms[0, 1])
    one_out, kept_one = branch_fwd(started[:, HALF:], coupling_one)
    left_half = started[:, :HALF] + one_out
    two_out, kept_two = branch_fwd(left_half, coupling_two)
    hidden = jnp.concatenate([left_half, started[:, HALF:] + two_out], -1)
    projected = low(matmul(low(hidden), w_qkv[0]))
    query, key, value = projected[:, :D], projected[:, D : 2 * D], projected[:, 2 * D :]
    mixed, soft = attend_fwd(query, key, value, length)
    section_out, kept_rest = rest_fwd(hidden, mixed, rests[0])
    section_out = low(section_out)

    chosen = (spots[:, None] == jnp.arange(SEQ)[None, :]).astype(BF16)
    at_spots = matmul(chosen, section_out)
    query_1 = low(matmul(low(at_spots), w_qkv[1][:, :D]))
    key_value = low(matmul(section_out, w_qkv[1][:, D:]))
    key_1, value_1 = key_value[:, :D], key_value[:, D:]
    mixed_1, soft_1 = attend_fwd(query_1, key_1, value_1, length)
    out_1, kept_rest_1 = rest_fwd(at_spots, mixed_1, rests[1])
    two_last, kept_two_last = branch_fwd(out_1[:, :HALF], coupling_two)
    right_last = out_1[:, HALF:] - two_last
    one_last, kept_one_last = branch_fwd(right_last, coupling_one)
    normed, kept_head = layer_norm(
        jnp.concatenate([out_1[:, :HALF] - one_last, right_last], -1), norms[1, 0], norms[1, 1]
    )

    loss_part, normed_grad = head(normed, fetched[SEQ:], row_weights, weight_sum, embed_table)

    restored_grad = norm_back(normed_grad, kept_head, norms[1, 0])
    left_grad = restored_grad[:, :HALF]
    into_right, grads_one = branch_back(-left_grad, kept_one_last, coupling_one)
    right_grad = restored_grad[:, HALF:] + into_right
    into_left, grads_two = branch_back(-right_grad, kept_two_last, coupling_two)
    out_grad = jnp.concatenate([left_grad + into_left, right_grad], -1)
    start_grad, mixed_grad, adapter_grads_1 = rest_back(out_grad, kept_rest_1, rests[1])
    query_grad, key_grad, value_grad = attend_back(query_1, key_1, value_1, soft_1, mixed_grad)
    spot_grad = start_grad + matmul_t(query_grad, w_qkv[1][:, :D])
    section_grad = (
        lax.dot_general(chosen.astype(F32), spot_grad, (((0,), (0,)), ((), ())), precision=HIGHEST)
        + matmul_t(key_grad, w_qkv[1][:, D : 2 * D])
        + matmul_t(value_grad, w_qkv[1][:, 2 * D :])
    )
    section_grad = low(section_grad).astype(F32)

    start_grad, mixed_grad, adapter_grads_0 = rest_back(section_grad, kept_rest, rests[0])
    query_grad, key_grad, value_grad = attend_back(query, key, value, soft, mixed_grad)
    hidden_grad = start_grad + matmul_t(
        jnp.concatenate([query_grad, key_grad, value_grad], -1), w_qkv[0]
    )
    into_left, first_two = branch_back(hidden_grad[:, HALF:], kept_two, coupling_two)
    _, first_one = branch_back(hidden_grad[:, :HALF] + into_left, kept_one, coupling_one, False)
    grads_one = jax.tree.map(jnp.add, grads_one, first_one)
    grads_two = jax.tree.map(jnp.add, grads_two, first_two)

    grad_blocks, grad_vector, pair = sum_at_owners(
        ((adapter_grads_0, grads_one), (adapter_grads_1, grads_two)), loss_part, master.shape[1]
    )
    totals = jnp.sum(lax.all_to_all(pair, ("dp", "section"), 0, 0), (0, 1))
    grad_norm = jnp.sqrt(totals[0])
    loss_sum = totals[1]
    factor = CLIP_NORM / jnp.maximum(grad_norm, CLIP_NORM)
    clipped = grad_blocks * factor
    clipped_vector = grad_vector * factor
    momentum_new = FIRST_DECAY * momentum[0] + (1.0 - FIRST_DECAY) * clipped
    left_new = STAT_DECAY * stat_left[0] + (1.0 - STAT_DECAY) * jnp.einsum(
        "nij,nkj->nik", clipped, clipped, precision=HIGHEST
    )
    right_new = STAT_DECAY * stat_right[0] + (1.0 - STAT_DECAY) * jnp.einsum(
        "nji,njk->nik", clipped, clipped, precision=HIGHEST
    )
    direction = jnp.einsum("nij,njk->nik", root_left[0], momentum_new, precision=HIGHEST)
    direction = jnp.einsum("nij,njk->nik", direction, root_right[0], precision=HIGHEST)
    master_new = master[0] - MAT_RATE * (direction + MAT_DECAY * master[0])
    first_new = FIRST_DECAY * vec_first[0] + (1.0 - FIRST_DECAY) * clipped_vector
    second_new = VEC_SECOND * vec_second[0] + (1.0 - VEC_SECOND) * clipped_vector * clipped_vector
    corrected_first = first_new / (1.0 - FIRST_DECAY**STEP)
    corrected_second = second_new / (1.0 - VEC_SECOND**STEP)
    vectors_new = vectors[0] - VEC_RATE * (
        corrected_first / (jnp.sqrt(corrected_second) + VEC_EPS) + VEC_DECAY * vectors[0]
    )
    return (
        clipped[None],
        momentum_new[None],
        left_new[None],
        right_new[None],
        master_new[None],
        master_new.astype(BF16)[None],
        first_new[None],
        second_new[None],
        vectors_new[None],
        grad_norm,
        loss_sum,
        weight_sum,
    )


def solution(mesh):
    rows = P(None, "dp", None)
    section = P("section", None, None)
    blocks = P("section", "dp", None, None)
    biases = P("section", "dp")
    return jax.shard_map(
        shards,
        mesh=mesh,
        in_specs=(rows, P(None, "dp"), rows, rows, rows, P("dp", None), P())
        + (section,) * 5
        + (blocks,) * 6
        + (biases,) * 3,
        out_specs=(blocks,) * 6 + (biases,) * 3 + (P(),) * 3,
        check_vma=False,
    )
```

```python
import jax
import jax.numpy as jnp
import numpy as np
from jax import lax
from jax.experimental import pallas as pl
from jax.experimental.pallas import tpu as pltpu
from jax.sharding import PartitionSpec as P

D = 768
HEADS = 12
HEAD_DIM = 64
BOT = 384
INV_H = 192
SEQ = 512
COUNT = 32
MICRO = 2
BLOCK = 48
STEP = 10
HALF = 384
IDS = SEQ + COUNT

HIGHEST = lax.Precision.HIGHEST
NORM_EPS = 1e-12
CLIP_NORM = 0.02
FIRST_DECAY = 0.9
STAT_DECAY = 0.99
MAT_RATE = 0.1
MAT_DECAY = 0.01
VEC_RATE = 0.05
VEC_SECOND = 0.999
VEC_EPS = 1e-08
VEC_DECAY = 0.01
F32 = jnp.float32
BF16 = jnp.bfloat16

CDF_SCALE = 0.42 / 2.0**0.5
CDF_POLY = (
    0.2368242366796694,
    0.239585811361218,
    0.1947261443420679,
    0.2687426685879861,
    -0.13052645834187002,
    0.4406726942003943,
    -0.32025628294963193,
    0.07023101752398136,
)


def matmul(left, right):
    return jnp.dot(left, right, preferred_element_type=F32)


def matmul_t(left, right):
    return lax.dot_general(left, right, (((1,), (1,)), ((), ())), preferred_element_type=F32)


def inner_rows(left, right):
    return lax.dot_general(left, right, (((0,), (0,)), ((), ())), preferred_element_type=F32)


def low(values):
    return values.astype(BF16)


def gelu_both(values):
    ratio = 1.0 / (1.0 + CDF_SCALE * jnp.abs(values))
    poly = jnp.full_like(ratio, 0.5 * CDF_POLY[-1])
    for factor in CDF_POLY[-2::-1]:
        poly = poly * ratio + 0.5 * factor
    bell = jnp.exp(-0.5 * values * values)
    tail = bell * (poly * ratio)
    cdf = jnp.where(values < 0, tail, 1.0 - tail)
    return values * cdf, cdf + values * (bell * (2.0 * np.pi) ** -0.5)


def layer_norm(values, gain, shift):
    centered = values - jnp.mean(values, -1, keepdims=True)
    inverse = lax.rsqrt(jnp.mean(centered * centered, -1, keepdims=True) + NORM_EPS)
    normal = centered * inverse
    return normal * gain + shift, (normal, inverse)


def norm_back(incoming, kept, gain):
    normal, inverse = kept
    scaled = incoming * gain
    return inverse * (
        scaled
        - jnp.mean(scaled, -1, keepdims=True)
        - normal * jnp.mean(scaled * normal, -1, keepdims=True)
    )


def to_blocks(matrix):
    rows_in, cols_in = matrix.shape
    return (
        matrix.reshape(rows_in // BLOCK, BLOCK, cols_in // BLOCK, BLOCK)
        .transpose(0, 2, 1, 3)
        .reshape(-1, BLOCK, BLOCK)
    )


def from_blocks(blocks, rows_in, cols_in):
    return (
        blocks.reshape(rows_in // BLOCK, cols_in // BLOCK, BLOCK, BLOCK)
        .transpose(0, 2, 1, 3)
        .reshape(rows_in, cols_in)
    )


def split_params(blocks, vector):
    adapter_count = D * BOT // BLOCK**2
    half_count = HALF * INV_H // BLOCK**2
    split_at = 2 * adapter_count
    adapter = (
        from_blocks(blocks[:adapter_count], D, BOT),
        vector[:BOT],
        from_blocks(blocks[adapter_count:split_at], BOT, D),
        vector[BOT : BOT + D],
    )
    coupling = (
        from_blocks(blocks[split_at : split_at + half_count], HALF, INV_H),
        vector[BOT + D : BOT + D + INV_H],
        from_blocks(blocks[split_at + half_count :], INV_H, HALF),
        vector[BOT + D + INV_H :],
    )
    return adapter, coupling


def join_params(adapter, coupling):
    blocks = jnp.concatenate(
        [to_blocks(adapter[0]), to_blocks(adapter[2]), to_blocks(coupling[0]), to_blocks(coupling[2])]
    )
    return blocks, jnp.concatenate([adapter[1], adapter[3], coupling[1], coupling[3]], 1)[0]


GROUP_ROWS = 72
LANES = 128


def whole(shape):
    return pl.BlockSpec(shape, lambda *_: (0,) * len(shape))


def section_of(shape, section):
    return pl.BlockSpec((None,) + shape, lambda *_: (section,) + (0,) * len(shape))


def params_for(mebibytes):
    return pltpu.CompilerParams(vmem_limit_bytes=mebibytes * 2**20)


def roll(values, shift):
    return pltpu.roll(values, shift, 1)


def lane_of(values):
    return lax.broadcasted_iota(jnp.int32, values.shape, 1)


def fold_half(values, upper):
    top, bottom = values[:24], values[24:]
    if upper:
        return jnp.where(lane_of(top) < 64, roll(top, 64), bottom)
    return jnp.where(lane_of(top) < 64, top, roll(bottom, 64))


def unfold_half(values, upper):
    turned = roll(values, 64)
    return jnp.concatenate([turned, values] if upper else [values, turned], 0)


def join_pair(main_0, rest_0, main_1, rest_1):
    left = lane_of(main_0) < 64
    turned = roll(main_1, 64)
    return (
        main_0,
        jnp.where(left, unfold_half(rest_0, False), turned),
        jnp.where(left, turned, unfold_half(rest_1, True)),
    )


def cut_pair(tile_0, tile_1, tile_2):
    left = lane_of(tile_0) < 64
    return (
        (tile_0, fold_half(tile_1, False)),
        (jnp.where(left, roll(tile_1, 64), roll(tile_2, 64)), fold_half(tile_2, True)),
    )


def chunk_rows(own_blocks):
    return own_blocks // 4 * GROUP_ROWS + 8


def pack_own(master, bias_rows):
    count = master.shape[0]

    def kernel(master_ref, bias_ref, out_ref):
        row = lax.broadcasted_iota(jnp.int32, (BLOCK, 256), 0)
        col = lax.broadcasted_iota(jnp.int32, (BLOCK, 256), 1)
        pieces = []
        for group in range(count // 4):
            wide = jnp.zeros((BLOCK, 256), F32)
            for j in range(4):
                wide += matmul(low(master_ref[4 * group + j]), (col == row + BLOCK * j).astype(BF16))
            pieces += [wide[:, :LANES], fold_half(wide[:, LANES:], False)]
        out_ref[...] = low(jnp.concatenate(pieces + [bias_ref[...]], 0))

    return pl.pallas_call(
        kernel,
        out_shape=jax.ShapeDtypeStruct((chunk_rows(count), LANES), BF16),
        name="pack_own",
    )(master, bias_rows)


MATRICES = ((D, BOT), (BOT, D), (HALF, INV_H), (INV_H, HALF))


def unpack_all(gathered):
    sections, parts, rows, _ = gathered.shape
    per_part = (rows - 8) // GROUP_ROWS

    def kernel(in_ref, *out_refs):
        cache = {}

        def group(index):
            part = index // per_part
            if part not in cache:
                cache.clear()
                cache[part] = in_ref[part].astype(F32)
            base = index % per_part * GROUP_ROWS
            chunk = cache[part]
            return chunk[base : base + BLOCK], chunk[base + BLOCK : base + GROUP_ROWS]

        index = 0
        for (height, width), out_ref in zip(MATRICES, out_refs):
            for top in range(0, height, BLOCK):
                if width == INV_H:
                    main, rest = group(index)
                    index += 1
                    out_ref[top : top + BLOCK, :LANES] = low(main)
                    out_ref[top : top + BLOCK, LANES:] = low(unfold_half(rest, False)[:, :64])
                    continue
                for left in range(0, width, HALF):
                    tiles = join_pair(*group(index), *group(index + 1))
                    index += 2
                    for j, tile in enumerate(tiles):
                        at = left + j * LANES
                        out_ref[top : top + BLOCK, at : at + LANES] = low(tile)

    return pl.pallas_call(
        kernel,
        grid=(sections,),
        in_specs=[pl.BlockSpec((None, parts, rows, LANES), lambda s: (s, 0, 0, 0))],
        out_specs=[pl.BlockSpec((None,) + shape, lambda s: (s, 0, 0)) for shape in MATRICES],
        out_shape=[jax.ShapeDtypeStruct((sections,) + shape, BF16) for shape in MATRICES],
        compiler_params=params_for(32),
        name="unpack_all",
    )(gathered)


def pack_grads(grads, bias_rows, own_index, parts):
    per_part = 80 // parts
    rows = per_part * GROUP_ROWS + 8

    def kernel(index_ref, *refs):
        bias_ref, own_ref, other_ref = refs[8:]
        own = index_ref[0]
        for section in range(MICRO):
            pieces = []
            for (height, width), ref in zip(MATRICES, refs[4 * section : 4 * section + 4]):
                for top in range(0, height, BLOCK):
                    band = slice(top, top + BLOCK)
                    if width == INV_H:
                        tail = ref[band, LANES:]
                        tail = jnp.concatenate([tail, tail], 1)
                        pieces.append((ref[band, :LANES], fold_half(tail, False)))
                        continue
                    for left in range(0, width, HALF):
                        tiles = [ref[band, left + j * LANES : left + (j + 1) * LANES] for j in range(3)]
                        pieces += cut_pair(*tiles)
                while len(pieces) >= per_part:
                    part = sum_done[section]
                    sum_done[section] += 1
                    chunk = [half for pair in pieces[:per_part] for half in pair]
                    del pieces[:per_part]
                    chunk = jnp.concatenate(chunk + [bias_ref[section, part]], 0)

                    @pl.when(own == section)
                    def _(part=part, chunk=chunk):
                        own_ref[part] = chunk

                    @pl.when(own != section)
                    def _(part=part, chunk=chunk):
                        other_ref[part] = low(chunk)

    sum_done = [0, 0]
    return pl.pallas_call(
        kernel,
        in_specs=[pl.BlockSpec(memory_space=pltpu.SMEM)] + [pl.BlockSpec(memory_space=pltpu.VMEM)] * 9,
        out_shape=[
            jax.ShapeDtypeStruct((parts, rows, LANES), F32),
            jax.ShapeDtypeStruct((parts, rows, LANES), BF16),
        ],
        compiler_params=params_for(40),
        name="pack_grads",
    )(own_index, *grads[0], *grads[1], bias_rows)


def sum_owned(came, loss_part, copies):
    parts, rows, _ = came.shape
    per_part = (rows - 8) // GROUP_ROWS

    def kernel(loss_ref, came_ref, blocks_ref, bias_ref, pair_ref):
        total = came_ref[0].astype(F32)
        for part in range(1, parts):
            total += came_ref[part].astype(F32)
        for group in range(per_part):
            base = group * GROUP_ROWS
            main = total[base : base + BLOCK]
            rest = unfold_half(total[base + BLOCK : base + GROUP_ROWS], False)
            lane = lane_of(main)
            parts_of = (
                main,
                roll(main, 80),
                jnp.where(lane < 32, roll(main, 32), roll(rest, 32)),
                roll(rest, 112),
            )
            for j, values in enumerate(parts_of):
                blocks_ref[4 * group + j] = values[:, :BLOCK]
        bias_ref[...] = total[rows - 8 :]
        squares = jnp.sum(jnp.sum(total * total, 0, keepdims=True), 1, keepdims=True)
        lane = lax.broadcasted_iota(jnp.int32, (1, LANES), 1)
        pair = jnp.where(lane == 0, squares, jnp.where(lane == 1, loss_ref[0], 0.0))
        pair_ref[...] = jnp.broadcast_to(pair[None], pair_ref.shape)

    return pl.pallas_call(
        kernel,
        in_specs=[pl.BlockSpec(memory_space=pltpu.SMEM), pl.BlockSpec(memory_space=pltpu.VMEM)],
        out_shape=[
            jax.ShapeDtypeStruct((4 * per_part, BLOCK, BLOCK), F32),
            jax.ShapeDtypeStruct((8, LANES), F32),
            jax.ShapeDtypeStruct((copies, 1, LANES), F32),
        ],
        compiler_params=params_for(32),
        name="sum_owned",
    )(loss_part, came)


GROUP = 256
HEADS_IN = GROUP // HEAD_DIM
GROUPS = D // GROUP
FF = 3072
TILE = 512
TILES = FF // TILE


def rows_of(count, size):
    return [slice(at, at + min(size, count)) for at in range(0, count, size)]


def vmem(count):
    return [pl.BlockSpec(memory_space=pltpu.VMEM)] * count


def hbm(count):
    return [pl.BlockSpec(memory_space=pl.ANY)] * count


def shape_of(*dims, kind=F32):
    return jax.ShapeDtypeStruct(dims, kind)


def start_copy(pair, section, window, target, sem):
    own, came = pair
    here = lax.axis_index("section") == section

    @pl.when(here)
    def _():
        pltpu.make_async_copy(own.at[window], target, sem).start()

    @pl.when(jnp.logical_not(here))
    def _():
        pltpu.make_async_copy(came.at[window], target, sem).start()


def wait_copy(pair, window, target, sem):
    pltpu.make_async_copy(pair[0].at[window], target, sem).wait()


def qkv_window(group, part):
    return 0, slice(None), pl.ds(part * D + group * GROUP, GROUP)


def head_mask(values, head):
    lane = lax.broadcasted_iota(jnp.int32, values.shape, 1)
    return (lane >= head * HEAD_DIM) & (lane < (head + 1) * HEAD_DIM)


def only_head(values, head):
    return jnp.where(head_mask(values, head), values, jnp.zeros_like(values))


def scaled_query(query):
    return low(query.astype(F32) * HEAD_DIM**-0.5)


def key_bias(length, shape, axis):
    return jnp.where(lax.broadcasted_iota(jnp.int32, shape, axis) < length, 0.0, -1e30)


def softmax_rows(scores):
    highest = jnp.max(scores, 1, keepdims=True)
    exponent = jnp.exp(scores - highest)
    total = jnp.sum(exponent, 1, keepdims=True)
    return low(exponent * (1.0 / total)), highest + jnp.log(total)


def first_kernel(fetched, pos_table, norms, coupling, w_qkv, length):
    def kernel(length_ref, fetched_ref, pos_ref, norms_ref, *refs):
        c_refs, w_pair, refs = refs[:8], refs[8:10], refs[10:]
        hidden_ref, q_ref, k_ref, v_ref, mixed_ref, lse_ref = refs[:6]
        kept_refs, (x_low, w_buf, s_buf, p_buf, lse_buf, sems) = refs[6:12], refs[12:]
        group = pl.program_id(0)

        @pl.when(group == 0)
        def _():
            for g in range(GROUPS):
                for part in range(3):
                    start_copy(w_pair, 0, qkv_window(g, part), w_buf.at[g, part], sems.at[g, part])
            for rows in rows_of(SEQ, 256):
                started, _ = layer_norm(
                    fetched_ref[rows] + pos_ref[rows].astype(F32), norms_ref[0, 0:1], norms_ref[0, 1:2]
                )
                left, right = started[:, :HALF], started[:, HALF:]
                low_one = low(right)
                active, slope = gelu_both(matmul(low_one, c_refs[0][...]) + c_refs[1][...])
                active = low(active)
                left = left + matmul(active, c_refs[2][...]) + c_refs[3][...]
                for ref, value in zip(kept_refs[:3], (low_one, active, low(slope))):
                    ref[rows] = value
                low_two = low(left)
                active, slope = gelu_both(matmul(low_two, c_refs[4][...]) + c_refs[5][...])
                active = low(active)
                right = right + matmul(active, c_refs[6][...]) + c_refs[7][...]
                for ref, value in zip(kept_refs[3:], (low_two, active, low(slope))):
                    ref[rows] = value
                hidden_ref[rows, :HALF] = left
                hidden_ref[rows, HALF:] = right
                x_low[rows, :HALF] = low_two
                x_low[rows, HALF:] = low(right)

        for part, ref in enumerate((q_ref, k_ref, v_ref)):
            wait_copy(w_pair, qkv_window(group, part), w_buf.at[group, part], sems.at[group, part])
            ref[...] = low(matmul(x_low[...], w_buf[group, part]))
        query = scaled_query(q_ref[...])
        key, value = k_ref[...], v_ref[...]
        bias = key_bias(length_ref[0], (1, SEQ), 1)
        lane = lax.broadcasted_iota(jnp.int32, (SEQ, LANES), 1)
        mixed = jnp.zeros((SEQ, GROUP), F32)
        lse_buf[...] = jnp.zeros((SEQ, LANES), F32)
        for head in range(HEADS_IN):
            s_ref, p_ref = s_buf.at[head % 2], p_buf.at[head % 2]
            s_ref[...] = matmul_t(only_head(query, head), key)
            for rows in rows_of(SEQ, 64):
                soft, lse = softmax_rows(s_ref[rows] + bias)
                p_ref[rows] = soft
                lse_buf[rows] = jnp.where(lane[rows] == head, lse, lse_buf[rows])
            mixed = jnp.where(head_mask(mixed, head), matmul(p_ref[...], value), mixed)
        mixed_ref[...] = low(mixed)
        lse_ref[...] = jnp.transpose(lse_buf[...])[:8]

    column = pl.BlockSpec((SEQ, GROUP), lambda g: (0, g))
    low_wide = shape_of(SEQ, D, kind=BF16)
    kept = [(SEQ, HALF), (SEQ, INV_H), (SEQ, INV_H)] * 2
    return pl.pallas_call(
        kernel,
        grid=(GROUPS,),
        in_specs=[pl.BlockSpec(memory_space=pltpu.SMEM)]
        + [whole((SEQ, D)), whole((SEQ, D)), whole((MICRO, 6, D))]
        + [whole(value.shape) for value in coupling]
        + hbm(2),
        out_specs=[whole((SEQ, D))]
        + [column] * 4
        + [pl.BlockSpec((None, 8, SEQ), lambda g: (g, 0, 0))]
        + [whole(dims) for dims in kept],
        out_shape=[shape_of(SEQ, D)]
        + [low_wide] * 4
        + [shape_of(GROUPS, 8, SEQ)]
        + [shape_of(*dims, kind=BF16) for dims in kept],
        scratch_shapes=[
            pltpu.VMEM((SEQ, D), BF16),
            pltpu.VMEM((GROUPS, 3, D, GROUP), BF16),
            pltpu.VMEM((2, SEQ, SEQ), F32),
            pltpu.VMEM((2, SEQ, SEQ), BF16),
            pltpu.VMEM((SEQ, LANES), F32),
            pltpu.SemaphoreType.DMA((GROUPS, 3)),
        ],
        compiler_params=params_for(48),
        name="first_layer_attention",
    )(length, fetched, pos_table, norms, *coupling, *w_qkv)


def spots_kernel(section_out, chosen, w_qkv, length):
    def kernel(length_ref, x_ref, chosen_ref, own_ref, came_ref, *refs):
        at_ref, q_ref, k_ref, v_ref, mixed_ref, lse_ref, at_low, w_buf, sems = refs
        w_pair = own_ref, came_ref
        group = pl.program_id(0)

        @pl.when(group == 0)
        def _():
            for g in range(GROUPS):
                for part in range(3):
                    start_copy(w_pair, 1, qkv_window(g, part), w_buf.at[g, part], sems.at[g, part])
            at_ref[...] = matmul(chosen_ref[...], x_ref[...])
            at_low[...] = low(at_ref[...])

        for part, ref in enumerate((q_ref, k_ref, v_ref)):
            wait_copy(w_pair, qkv_window(group, part), w_buf.at[group, part], sems.at[group, part])
            ref[...] = low(matmul(at_low[...] if part == 0 else x_ref[...], w_buf[group, part]))
        query = scaled_query(q_ref[...])
        query = jnp.concatenate([only_head(query, head) for head in range(HEADS_IN)], 0)
        bias = key_bias(length_ref[0], (1, SEQ), 1)
        soft, lse = softmax_rows(matmul_t(query, k_ref[...]) + bias)
        lse_ref[...] = lse
        every = matmul(soft, v_ref[...])
        mixed = every[:COUNT]
        for head in range(1, HEADS_IN):
            mixed = jnp.where(head_mask(mixed, head), every[head * COUNT : (head + 1) * COUNT], mixed)
        mixed_ref[...] = low(mixed)

    narrow = pl.BlockSpec((COUNT, GROUP), lambda g: (0, g))
    column = pl.BlockSpec((SEQ, GROUP), lambda g: (0, g))
    return pl.pallas_call(
        kernel,
        grid=(GROUPS,),
        in_specs=[pl.BlockSpec(memory_space=pltpu.SMEM), whole((SEQ, D)), whole((COUNT, SEQ))] + hbm(2),
        out_specs=[whole((COUNT, D)), narrow, column, column, narrow]
        + [pl.BlockSpec((None, HEADS_IN * COUNT, 1), lambda g: (g, 0, 0))],
        out_shape=[
            shape_of(COUNT, D),
            shape_of(COUNT, D, kind=BF16),
            shape_of(SEQ, D, kind=BF16),
            shape_of(SEQ, D, kind=BF16),
            shape_of(COUNT, D, kind=BF16),
            shape_of(GROUPS, HEADS_IN * COUNT, 1),
        ],
        scratch_shapes=[
            pltpu.VMEM((COUNT, D), BF16),
            pltpu.VMEM((GROUPS, 3, D, GROUP), BF16),
            pltpu.SemaphoreType.DMA((GROUPS, 3)),
        ],
        compiler_params=params_for(32),
        name="second_layer_attention",
    )(length, section_out, chosen, *w_qkv)


UP_WINDOWS = [(0, slice(None), slice(j * TILE, (j + 1) * TILE)) for j in range(TILES)]
DOWN_WINDOWS = [(0, slice(j * TILE, (j + 1) * TILE), slice(None)) for j in range(TILES)]
OUT_WINDOW = (0, slice(None), slice(None))


def rest_buffers():
    return [
        pltpu.VMEM((D, D), BF16),
        pltpu.VMEM((TILES, D, TILE), BF16),
        pltpu.VMEM((TILES, TILE, D), BF16),
        pltpu.SemaphoreType.DMA((2 * TILES + 1,)),
    ]


def start_rest(pairs, section, buffers):
    out_buf, up_buf, down_buf, sems = buffers
    start_copy(pairs[0], section, OUT_WINDOW, out_buf, sems.at[2 * TILES])
    for j in range(TILES):
        start_copy(pairs[1], section, UP_WINDOWS[j], up_buf.at[j], sems.at[j])
        start_copy(pairs[2], section, DOWN_WINDOWS[j], down_buf.at[j], sems.at[TILES + j])


def wait_out(pairs, buffers):
    wait_copy(pairs[0], OUT_WINDOW, buffers[0], buffers[3].at[2 * TILES])


def wait_tile(pairs, buffers, tile):
    _, up_buf, down_buf, sems = buffers
    wait_copy(pairs[1], UP_WINDOWS[0], up_buf.at[tile], sems.at[tile])
    wait_copy(pairs[2], DOWN_WINDOWS[0], down_buf.at[tile], sems.at[TILES + tile])


def rest_forward(section, hidden, mixed, norms, adapter, w_rest, coupling=None):
    rows = hidden.shape[0]
    step = min(rows, 256)
    last = coupling is not None
    extra_in = coupling if last else ()

    def kernel(hidden_ref, mixed_ref, norms_ref, *refs):
        a_refs, refs = refs[:4], refs[4:]
        c_refs, refs = refs[: len(extra_in)], refs[len(extra_in) :]
        w_flat, refs = refs[:6], refs[6:]
        pairs = [w_flat[2 * i : 2 * i + 2] for i in range(3)]
        outs, refs = refs[:n_outs], refs[n_outs:]
        result_ref, n1_ref, i1_ref, slope_ref, lin_ref, act_ref, bslope_ref, n2_ref, i2_ref = outs[:9]
        att, att_low, acc, u_buf, g_buf = refs[:5]
        buffers = refs[5:]
        tile = pl.program_id(0)
        gain = lambda i: norms_ref[section, i : i + 1]

        @pl.when(tile == 0)
        def _():
            start_rest(pairs, section, buffers)
            wait_out(pairs, buffers)
            for part in rows_of(rows, step):
                first = hidden_ref[part] + matmul(mixed_ref[part], buffers[0][...])
                values, (normal, inverse) = layer_norm(first, gain(2), gain(3))
                att[part] = values
                att_low[part] = low(values)
                n1_ref[part] = normal
                i1_ref[part] = inverse

        wait_tile(pairs, buffers, tile)
        for i, part in enumerate(rows_of(rows, step)):
            u_buf[i] = matmul(att_low[part], buffers[1][tile])
            for small in rows_of(step, 32):
                active, slope = gelu_both(u_buf[i, small])
                g_buf[i, small] = low(active)
                slope_ref[part.start + small.start : part.start + small.stop] = low(slope)
            product = matmul(g_buf[i], buffers[2][tile])

            @pl.when(tile == 0)
            def _(part=part, product=product):
                acc[part] = product

            @pl.when(tile > 0)
            def _(part=part, product=product):
                acc[part] += product

        @pl.when(tile == TILES - 1)
        def _():
            for part in rows_of(rows, step):
                summed = acc[part] + att[part]
                low_in = low(summed)
                active, slope = gelu_both(matmul(low_in, a_refs[0][...]) + a_refs[1][...])
                active = low(active)
                lin_ref[part], act_ref[part], bslope_ref[part] = low_in, active, low(slope)
                second = summed + (matmul(active, a_refs[2][...]) + a_refs[3][...])
                values, (normal, inverse) = layer_norm(second, gain(4), gain(5))
                n2_ref[part], i2_ref[part] = normal, inverse
                if not last:
                    result_ref[part] = low(values)
            if last:
                left, right = values[:, :HALF], values[:, HALF:]
                low_two = low(left)
                active_two, slope_two = gelu_both(matmul(low_two, c_refs[4][...]) + c_refs[5][...])
                active_two = low(active_two)
                right = right - (matmul(active_two, c_refs[6][...]) + c_refs[7][...])
                low_one = low(right)
                active_one, slope_one = gelu_both(matmul(low_one, c_refs[0][...]) + c_refs[1][...])
                active_one = low(active_one)
                left = left - (matmul(active_one, c_refs[2][...]) + c_refs[3][...])
                normed, (normal, inverse) = layer_norm(
                    jnp.concatenate([left, right], 1), gain(0), gain(1)
                )
                result_ref[...] = low(normed)
                kept = (normal, inverse, low_one, active_one, low(slope_one))
                kept += (low_two, active_two, low(slope_two))
                for ref, value in zip(outs[9:], kept):
                    ref[...] = value

    wide, thin = shape_of(rows, D), shape_of(rows, 1)
    out_shape = [shape_of(rows, D, kind=BF16), wide, thin, shape_of(rows, FF, kind=BF16)]
    out_shape += [shape_of(rows, D, kind=BF16), shape_of(rows, BOT, kind=BF16)]
    out_shape += [shape_of(rows, BOT, kind=BF16), wide, thin]
    if last:
        out_shape += [wide, thin]
        out_shape += [shape_of(rows, n, kind=BF16) for n in (HALF, INV_H, INV_H)] * 2
    n_outs = len(out_shape)
    out_specs = [whole(out.shape) for out in out_shape]
    out_specs[3] = pl.BlockSpec((rows, TILE), lambda j: (0, j))
    return pl.pallas_call(
        kernel,
        grid=(TILES,),
        in_specs=[whole((rows, D)), whole((rows, D)), whole((MICRO, 6, D))]
        + [whole(value.shape) for value in (*adapter, *extra_in)]
        + hbm(6),
        out_specs=out_specs,
        out_shape=out_shape,
        scratch_shapes=[
            pltpu.VMEM((rows, D), F32),
            pltpu.VMEM((rows, D), BF16),
            pltpu.VMEM((rows, D), F32),
            pltpu.VMEM((rows // step, step, TILE), F32),
            pltpu.VMEM((rows // step, step, TILE), BF16),
        ]
        + rest_buffers(),
        compiler_params=params_for(52),
        name="last_rows_forward" if last else "first_layer_rest",
    )(hidden, mixed, norms, *adapter, *extra_in, *[w for pair in w_rest for w in pair])


def column_sum(values):
    return jnp.sum(values.astype(F32), 0, keepdims=True)


def branch_grads(grad_low, kept, weights, out_refs):
    low_in, active, slope = kept
    hidden_grad = low(matmul_t(grad_low, weights[2]) * slope.astype(F32))
    out_refs[0][...] = inner_rows(low_in, hidden_grad)
    out_refs[1][...] = column_sum(hidden_grad)
    out_refs[2][...] = inner_rows(active, grad_low)
    out_refs[3][...] = column_sum(grad_low)
    return hidden_grad


ADAPTER_GRADS = ((D, BOT), (1, BOT), (BOT, D), (1, D))
COUPLING_GRADS = ((HALF, INV_H), (1, INV_H), (INV_H, HALF), (1, HALF))


def rest_backward(section, incoming, kept, norms, adapter, w_rest, head=None):
    n1, i1, slope, lin, act, bslope, n2, i2 = kept
    rows = n1.shape[0]
    step = min(rows, 256)
    last = head is not None
    if last:
        head_kept, coupling, normed, target_rows, row_weights, weight_sum = head
        extra_in = (*head_kept, *coupling, normed, target_rows, row_weights, weight_sum)
    else:
        extra_in = ()

    def kernel(incoming_ref, n1_ref, i1_ref, slope_ref, lin_ref, act_ref, bslope_ref, n2_ref, i2_ref, *refs):
        norms_ref, a_refs, refs = refs[0], refs[1:5], refs[5:]
        e_refs, refs = refs[: len(extra_in)], refs[len(extra_in) :]
        w_flat, refs = refs[:6], refs[6:]
        pairs = [w_flat[2 * i : 2 * i + 2] for i in range(3)]
        outs, refs = refs[:n_outs], refs[n_outs:]
        start_ref, mixed_ref, grad_refs = outs[0], outs[1], outs[2:6]
        summed, summed_low, acc, second_low, hidden_low = refs[:5]
        buffers = refs[5:]
        tile = pl.program_id(0)
        gain = lambda i: norms_ref[section, i : i + 1]

        def from_head():
            nh_ref, ih_ref = e_refs[:2]
            kept_one, kept_two = ([ref[...] for ref in e_refs[at : at + 3]] for at in (2, 5))
            c_one, c_two = ([ref[...] for ref in e_refs[at : at + 4]] for at in (8, 12))
            normed_ref, target_ref, weight_ref, total_ref = e_refs[16:]
            loss_ref, one_refs, two_refs = outs[6], outs[7:11], outs[11:15]
            parts = incoming_ref.shape[0]
            stats = incoming_ref[:, :, D:].astype(F32)
            highest = jnp.sum(stats[:, :, :3], 2, keepdims=True)
            totals = jnp.sum(stats[:, :, 3:6], 2, keepdims=True)
            top = jnp.max(highest, 0)
            factor = jnp.exp(highest - top[None])
            total = jnp.sum(totals * factor, 0)
            expected = jnp.zeros((rows, D), F32)
            for part in range(parts):
                expected += incoming_ref[part, :, :D].astype(F32) * (factor[part] / total)
            target = target_ref[...]
            target_logit = jnp.sum(normed_ref[...].astype(F32) * target, 1, keepdims=True)
            row_losses = weight_ref[...] * (top + jnp.log(total) - target_logit)
            loss_ref[...] = jnp.sum(row_losses, 0, keepdims=True)
            normed_grad = weight_ref[...] / total_ref[...] * (expected - target)
            restored = norm_back(normed_grad, (nh_ref[...], ih_ref[...]), gain(0))
            left, right = restored[:, :HALF], restored[:, HALF:]
            hidden = branch_grads(low(-left), kept_one, c_one, one_refs)
            right = right + matmul_t(hidden, c_one[0])
            hidden = branch_grads(low(-right), kept_two, c_two, two_refs)
            left = left + matmul_t(hidden, c_two[0])
            return jnp.concatenate([left, right], 1)

        @pl.when(tile == 0)
        def _():
            start_rest(pairs, section, buffers)
            for part in rows_of(rows, step):
                arrived = from_head() if last else incoming_ref[part].astype(F32)
                second = norm_back(arrived, (n2_ref[part], i2_ref[part]), gain(4))
                summed[part] = second
                second_low[part] = low(second)
            hidden_low[...] = branch_grads(
                second_low[...],
                (lin_ref[...], act_ref[...], bslope_ref[...]),
                [ref[...] for ref in a_refs],
                grad_refs,
            )
            for part in rows_of(rows, step):
                total = summed[part] + matmul_t(hidden_low[part], a_refs[0][...])
                summed[part] = total
                summed_low[part] = low(total)
                acc[part] = total

        wait_tile(pairs, buffers, tile)
        for part in rows_of(rows, step):
            inner = matmul_t(summed_low[part], buffers[2][tile])
            inner = low(inner * slope_ref[part].astype(F32))
            acc[part] += matmul_t(inner, buffers[1][tile])

        @pl.when(tile == TILES - 1)
        def _():
            wait_out(pairs, buffers)
            for part in rows_of(rows, step):
                start = norm_back(acc[part], (n1_ref[part], i1_ref[part]), gain(2))
                start_ref[part] = start
                mixed_ref[part] = low(matmul_t(low(start), buffers[0][...]))

    out_shape = [shape_of(rows, D), shape_of(rows, D, kind=BF16)]
    out_shape += [shape_of(*dims) for dims in ADAPTER_GRADS]
    if last:
        out_shape += [shape_of(1, 1)] + [shape_of(*dims) for dims in COUPLING_GRADS] * 2
    n_outs = len(out_shape)
    in_specs = [whole(value.shape) for value in (incoming, *kept, norms, *adapter, *extra_in)]
    in_specs[3] = pl.BlockSpec((rows, TILE), lambda j: (0, j))
    return pl.pallas_call(
        kernel,
        grid=(TILES,),
        in_specs=in_specs + hbm(6),
        out_specs=[whole(out.shape) for out in out_shape],
        out_shape=out_shape,
        scratch_shapes=[
            pltpu.VMEM((rows, D), F32),
            pltpu.VMEM((rows, D), BF16),
            pltpu.VMEM((rows, D), F32),
            pltpu.VMEM((rows, D), BF16),
            pltpu.VMEM((rows, BOT), BF16),
        ]
        + rest_buffers(),
        compiler_params=params_for(56),
        name="last_rows_backward" if last else "first_layer_rest_backward",
    )(incoming, *kept, norms, *adapter, *extra_in, *[w for pair in w_rest for w in pair])


def spots_backward(kept, mixed_grad, start_grad, chosen_t, w_qkv, length):
    query, key, value, lse = kept

    def kernel(length_ref, q_ref, k_ref, v_ref, lse_ref, mixed_ref, start_ref, chosen_ref, *refs):
        w_pair = refs[:2]
        out_ref, acc, spot, w_buf, sems = refs[2:]
        group = pl.program_id(0)

        @pl.when(group == 0)
        def _():
            for g in range(GROUPS):
                for part in range(3):
                    start_copy(w_pair, 1, qkv_window(g, part), w_buf.at[g, part], sems.at[g, part])
            spot[...] = start_ref[...]
            acc[...] = jnp.zeros_like(acc)

        stack = lambda values: jnp.concatenate([only_head(values, h) for h in range(HEADS_IN)], 0)
        query = stack(scaled_query(q_ref[...]))
        mixed = stack(mixed_ref[...])
        key, value = k_ref[...], v_ref[...]
        scores = matmul_t(query, key) + key_bias(length_ref[0], (1, SEQ), 1)
        soft = jnp.exp(scores - lse_ref[...])
        soft_grad = matmul_t(mixed, value)
        delta = jnp.sum(soft_grad * soft, 1, keepdims=True)
        score_grad = low(soft * (soft_grad - delta))
        every = matmul(score_grad, key)
        query_grad = every[:COUNT]
        for head in range(1, HEADS_IN):
            query_grad = jnp.where(
                head_mask(query_grad, head), every[head * COUNT : (head + 1) * COUNT], query_grad
            )
        query_grad = low(query_grad * HEAD_DIM**-0.5)
        key_grad = low(inner_rows(score_grad, query))
        value_grad = low(inner_rows(low(soft), mixed))
        for part in range(3):
            wait_copy(w_pair, qkv_window(group, part), w_buf.at[group, part], sems.at[group, part])
        spot[...] += matmul_t(query_grad, w_buf[group, 0])
        acc[...] += matmul_t(key_grad, w_buf[group, 1]) + matmul_t(value_grad, w_buf[group, 2])

        @pl.when(group == GROUPS - 1)
        def _():
            placed = jnp.dot(
                chosen_ref[...], spot[...], precision=HIGHEST, preferred_element_type=F32
            )
            out_ref[...] = low(acc[...] + placed)

    narrow = pl.BlockSpec((COUNT, GROUP), lambda g: (0, g))
    column = pl.BlockSpec((SEQ, GROUP), lambda g: (0, g))
    return pl.pallas_call(
        kernel,
        grid=(GROUPS,),
        in_specs=[pl.BlockSpec(memory_space=pltpu.SMEM), narrow, column, column]
        + [pl.BlockSpec((None, HEADS_IN * COUNT, 1), lambda g: (g, 0, 0)), narrow]
        + [whole((COUNT, D)), whole((SEQ, COUNT))]
        + hbm(2),
        out_specs=whole((SEQ, D)),
        out_shape=shape_of(SEQ, D, kind=BF16),
        scratch_shapes=[
            pltpu.VMEM((SEQ, D), F32),
            pltpu.VMEM((COUNT, D), F32),
            pltpu.VMEM((GROUPS, 3, D, GROUP), BF16),
            pltpu.SemaphoreType.DMA((GROUPS, 3)),
        ],
        compiler_params=params_for(40),
        name="second_layer_attention_backward",
    )(length, query, key, value, lse, mixed_grad, start_grad, chosen_t, *w_qkv)


def first_backward(kept, mixed_grad, start_grad, kept_coupling, coupling, head_grads, w_qkv, length):
    query, key, value, lse = kept

    def kernel(length_ref, q_ref, k_ref, v_ref, lse_ref, mixed_ref, start_ref, *refs):
        kept_refs, c_refs, h_refs = refs[:6], refs[6:14], refs[14:22]
        w_pair, out_refs = refs[22:24], refs[24:32]
        acc, s_buf, d_buf, p_low, ds_low, w_buf, sems = refs[32:]
        group = pl.program_id(0)

        @pl.when(group == 0)
        def _():
            for g in range(GROUPS):
                for part in range(3):
                    start_copy(w_pair, 0, qkv_window(g, part), w_buf.at[g, part], sems.at[g, part])
            acc[...] = start_ref[...]

        query = scaled_query(q_ref[...])
        key, value, mixed = k_ref[...], v_ref[...], mixed_ref[...]
        key_t = jnp.transpose(key)
        key_grad = jnp.zeros((SEQ, GROUP), F32)
        value_grad = jnp.zeros((SEQ, GROUP), F32)
        query_parts = []
        for head in range(HEADS_IN):
            slot = head % 2
            s_buf[slot] = matmul_t(only_head(key, head), query)
            d_buf[slot] = matmul_t(only_head(value, head), mixed)
            lse_row = lse_ref[head : head + 1]
            delta = jnp.zeros((8, SEQ), F32)
            for rows in rows_of(SEQ, 32):
                valid = lax.broadcasted_iota(jnp.int32, (32, 1), 0) + rows.start < length_ref[0]
                bias = jnp.where(valid, 0.0, -1e30)
                soft = jnp.exp(s_buf[slot, rows] + bias - lse_row)
                s_buf[slot, rows] = soft
                p_low[slot, rows] = low(soft)
                product = soft * d_buf[slot, rows]
                for at in range(0, 32, 8):
                    delta = delta + product[at : at + 8]
            delta = jnp.sum(delta, 0, keepdims=True)
            for rows in rows_of(SEQ, 32):
                ds_low[slot, rows] = low(s_buf[slot, rows] * (d_buf[slot, rows] - delta))
            value_grad += matmul(p_low[slot], only_head(mixed, head))
            key_grad += matmul(ds_low[slot], only_head(query, head))
            query_parts.append(matmul(key_t[head * HEAD_DIM : (head + 1) * HEAD_DIM], ds_low[slot]))
        query_grad = jnp.transpose(jnp.concatenate(query_parts, 0)) * HEAD_DIM**-0.5
        for part, grad in enumerate((query_grad, key_grad, value_grad)):
            wait_copy(w_pair, qkv_window(group, part), w_buf.at[group, part], sems.at[group, part])
            acc[...] += matmul_t(low(grad), w_buf[group, part])

        @pl.when(group == GROUPS - 1)
        def _():
            c_one, c_two = ([ref[...] for ref in c_refs[at : at + 4]] for at in (0, 4))
            kept_one, kept_two = ([ref[...] for ref in kept_refs[at : at + 3]] for at in (0, 3))
            hidden = branch_grads(low(acc[:, HALF:]), kept_two, c_two, out_refs[4:])
            left = acc[:, :HALF] + matmul_t(hidden, c_two[0])
            branch_grads(low(left), kept_one, c_one, out_refs[:4])
            for out_ref, ref in zip(out_refs, h_refs):
                out_ref[...] += ref[...]

    column = pl.BlockSpec((SEQ, GROUP), lambda g: (0, g))
    out_shape = [shape_of(*dims) for dims in COUPLING_GRADS] * 2
    return pl.pallas_call(
        kernel,
        grid=(GROUPS,),
        in_specs=[pl.BlockSpec(memory_space=pltpu.SMEM), column, column, column]
        + [pl.BlockSpec((None, 8, SEQ), lambda g: (g, 0, 0)), column, whole((SEQ, D))]
        + [whole(value.shape) for value in (*kept_coupling, *coupling, *head_grads)]
        + hbm(2),
        out_specs=[whole(out.shape) for out in out_shape],
        out_shape=out_shape,
        scratch_shapes=[
            pltpu.VMEM((SEQ, D), F32),
            pltpu.VMEM((2, SEQ, SEQ), F32),
            pltpu.VMEM((2, SEQ, SEQ), F32),
            pltpu.VMEM((2, SEQ, SEQ), BF16),
            pltpu.VMEM((2, SEQ, SEQ), BF16),
            pltpu.VMEM((GROUPS, 3, D, GROUP), BF16),
            pltpu.SemaphoreType.DMA((GROUPS, 3)),
        ],
        compiler_params=params_for(56),
        name="first_layer_attention_backward",
    )(length, query, key, value, lse, mixed_grad, start_grad, *kept_coupling, *coupling, *head_grads, *w_qkv)


VOCAB_TILE = 1280


def head_kernel(rows, table):
    count, vocab = rows.shape[0], table.shape[0]
    steps = pl.cdiv(vocab, VOCAB_TILE)
    half = count // 2

    def kernel(x_ref, table_ref, out_ref, acc, top, total, l_buf, p_buf):
        tile = pl.program_id(0)

        @pl.when(tile == 0)
        def _():
            acc[...] = jnp.zeros_like(acc)
            top[...] = jnp.full_like(top, -1e30)
            total[...] = jnp.zeros_like(total)

        left = vocab - tile * VOCAB_TILE
        row = lax.broadcasted_iota(jnp.int32, (VOCAB_TILE, 1), 0)
        entries = jnp.where(row < left, table_ref[...], jnp.zeros_like(table_ref))
        bias = key_bias(left, (1, VOCAB_TILE), 1)
        for i in range(2):
            part = slice(i * half, (i + 1) * half)
            l_buf[i] = matmul_t(x_ref[part], entries)
            for small in rows_of(half, 32):
                at = slice(part.start + small.start, part.start + small.stop)
                logits = l_buf[i, small] + bias
                earlier = top[at]
                highest = jnp.maximum(earlier, jnp.max(logits, 1, keepdims=True))
                exponent = jnp.exp(logits - highest)
                factor = jnp.exp(earlier - highest)
                top[at] = highest
                total[at] = total[at] * factor + jnp.sum(exponent, 1, keepdims=True)
                p_buf[i, small] = low(exponent)
                acc[at] = acc[at] * factor
            acc[part] += matmul(p_buf[i], entries)

        @pl.when(tile == steps - 1)
        def _():
            lane = lax.broadcasted_iota(jnp.int32, (count, LANES), 1)
            stats = jnp.zeros((count, LANES), F32)
            pieces = three_low(top[...]) + three_low(total[...])
            for j, piece in enumerate(pieces):
                stats = jnp.where(lane == j, piece.astype(F32), stats)
            out_ref[:, :D] = low(acc[...])
            out_ref[:, D:] = low(stats)

    return pl.pallas_call(
        kernel,
        grid=(steps,),
        in_specs=[whole((count, D)), pl.BlockSpec((VOCAB_TILE, D), lambda j: (j, 0))],
        out_specs=whole((count, D + LANES)),
        out_shape=shape_of(count, D + LANES, kind=BF16),
        scratch_shapes=[
            pltpu.VMEM((count, D), F32),
            pltpu.VMEM((count, 1), F32),
            pltpu.VMEM((count, 1), F32),
            pltpu.VMEM((2, half, VOCAB_TILE), F32),
            pltpu.VMEM((2, half, VOCAB_TILE), BF16),
        ],
        compiler_params=params_for(48),
        name="vocabulary_head",
    )(rows, table)


def swap_add(own, other):
    came = lax.ppermute(low(other), "section", [(0, 1), (1, 0)])
    return own + came.astype(F32)


def pick(first_section, both):
    return jnp.where(first_section, both[0], both[1])


def plan_requests(ids, vocab_rows, slots):
    earlier = jnp.arange(IDS)[None, :] < jnp.arange(IDS)[:, None]
    same_id = ids[:, :, None] == ids[:, None, :]
    first = jnp.logical_not(jnp.any(same_id & earlier, -1))
    owner = ids // vocab_rows
    same_owner = owner[:, :, None] == owner[:, None, :]
    rank = jnp.sum((same_owner & earlier & first[:, None, :]).astype(jnp.int32), -1)
    slot = jnp.sum(jnp.where(same_id & first[:, None, :], rank[:, None, :], 0), -1)
    rounds = jnp.max(rank) // slots + 1
    return owner, slot, first, rounds


def fetch_rows(table, ids, first_section, weight_part, slots):
    parts = lax.axis_size("dp")
    vocab_rows = table.shape[0]
    owner, slot, first, rounds = plan_requests(ids, vocab_rows, slots)
    ids, owner, slot, first = (pick(first_section, both) for both in (ids, owner, slot, first))
    local = ids - owner * vocab_rows

    def places(turn):
        here = slot - turn * slots
        spot = jnp.where((here >= 0) & (here < slots), owner * slots + here, -1)
        return spot[:, None] == jnp.arange(parts * slots)[None, :]

    def wanted(hits):
        return jnp.sum(jnp.where(hits & first[:, None], local[:, None], 0), 0).reshape(parts, slots)

    def answer(asked, hits):
        rows = table.at[asked.reshape(-1)].get(mode="promise_in_bounds").reshape(parts, slots, D)
        came = lax.all_to_all(rows, "dp", 0, 0).reshape(parts * slots, D)
        return matmul(hits.astype(BF16), came)

    hits = places(0)
    extra = jnp.broadcast_to(jnp.stack([rounds, weight_part])[None], (parts, 2))
    asked = lax.all_to_all(jnp.concatenate([wanted(hits), extra], 1), "dp", 0, 0)
    total_rounds = jnp.max(asked[:, slots])
    weight_sum = jnp.sum(asked[:, slots + 1])
    rows = answer(asked[:, :slots], hits)

    def more(state):
        return state[0] < total_rounds

    def another(state):
        turn, rows = state
        hits = places(turn)
        asked = lax.all_to_all(wanted(hits), "dp", 0, 0)
        return turn + 1, rows + answer(asked, hits)

    return lax.while_loop(more, another, (jnp.int32(1), rows))[1], weight_sum.astype(F32)


def three_low(values):
    high = low(values)
    rest = values - high.astype(F32)
    middle = low(rest)
    return [high, middle, low(rest - middle.astype(F32))]


def bias_chunks(vector, parts):
    rows = vector.reshape(-1, parts, 1, vector.shape[-1] // parts)
    return jnp.pad(rows, ((0, 0), (0, 0), (0, 7), (0, LANES - rows.shape[-1])))


def gather_params(master, vector):
    parts = lax.axis_size("dp")
    count, width = master.shape[0], vector.shape[0]
    if count % 4 == 0 and width <= LANES:
        packed = pack_own(master, bias_chunks(vector, 1)[0, 0])
        gathered = lax.all_gather(packed, ("section", "dp")).reshape(MICRO, parts, -1, LANES)
        vectors = gathered[:, :, -8, :width].reshape(MICRO, parts * width)
        matrices = unpack_all(gathered)
        params = []
        for s in range(MICRO):
            down, up, c_down, c_up = (matrix[s] for matrix in matrices)
            bias = vectors[s]
            adapter = (down, bias[:BOT], up, bias[BOT : BOT + D])
            coupling = (c_down, bias[BOT + D : BOT + D + INV_H], c_up, bias[BOT + D + INV_H :])
            params.append((adapter, coupling))
    else:
        flat = low(jnp.concatenate([master.reshape(-1), vector]))
        gathered = lax.all_gather(flat, ("section", "dp")).reshape(MICRO, parts, -1)
        size = count * BLOCK**2
        all_blocks = gathered[:, :, :size].reshape(MICRO, parts * count, BLOCK, BLOCK)
        all_vectors = gathered[:, :, size:].reshape(MICRO, parts * width)
        params = [split_params(all_blocks[s], all_vectors[s]) for s in range(MICRO)]
    as_rows = lambda p: (p[0], p[1].astype(F32)[None], p[2], p[3].astype(F32)[None])
    return [as_rows(pair[0]) for pair in params], as_rows(params[0][1]), as_rows(params[1][1])


def sum_at_owners(grads, loss_part, count):
    parts = lax.axis_size("dp")
    section = lax.axis_index("section")
    width = (BOT + D + INV_H + HALF) // parts
    if count % 4 == 0 and width <= LANES:
        matrices = [(a[0], a[2], c[0], c[2]) for a, c in grads]
        biases = jnp.concatenate([jnp.concatenate([a[1], a[3], c[1], c[3]], 1) for a, c in grads])
        own, other = pack_grads(
            matrices, bias_chunks(biases, parts), section.reshape(1).astype(jnp.int32), parts
        )
        came = lax.all_to_all(low(swap_add(own, other)), "dp", 0, 0)
        blocks, bias, pair = sum_owned(came, loss_part.reshape(1), parts * MICRO)
        return blocks, bias[0, :width], pair
    flat = []
    for adapter, coupling in grads:
        blocks, vector = join_params(adapter, coupling)
        flat.append(
            jnp.concatenate([blocks.reshape(parts, count * BLOCK**2), vector.reshape(parts, width)], 1)
        )
    first = section == 0
    summed = swap_add(jnp.where(first, flat[0], flat[1]), jnp.where(first, flat[1], flat[0]))
    owned = jnp.sum(lax.all_to_all(low(summed), "dp", 0, 0).astype(F32), 0)
    blocks = owned[: count * BLOCK**2].reshape(count, BLOCK, BLOCK)
    pair = jnp.stack([jnp.sum(owned * owned), loss_part[0, 0]])
    pair = jnp.broadcast_to(pair[None, None], (parts * MICRO, 1, 2))
    return blocks, owned[count * BLOCK**2 :], pair


def shards(
    token_ids,
    lengths,
    positions,
    targets,
    loss_weights,
    embed_table,
    pos_table,
    norm_params,
    base_qkv,
    base_out,
    base_up,
    base_down,
    master,
    momentum,
    stat_left,
    stat_right,
    root_left,
    root_right,
    vectors,
    vec_first,
    vec_second,
):
    parts = lax.axis_size("dp")
    first_section = lax.axis_index("section") == 0
    slots = -(-IDS * 5 // (4 * parts * 16)) * 16

    adapters, coupling_one, coupling_two = gather_params(master[0], vectors[0])
    coupling = (*coupling_one, *coupling_two)
    swapped = [lax.ppermute(w, "section", [(0, 1), (1, 0)]) for w in (base_qkv, base_out, base_up, base_down)]
    pairs = list(zip((base_qkv, base_out, base_up, base_down), swapped))
    w_qkv, w_rest = pairs[0], pairs[1:]
    came = lax.ppermute(norm_params, "section", [(0, 1), (1, 0)])
    norms = jnp.concatenate([pick(first_section, (norm_params, came)), pick(first_section, (came, norm_params))])

    ids = jnp.concatenate([token_ids[:, 0], targets[:, 0]], -1)
    weight_part = jnp.sum(loss_weights)
    fetched, weight_sum = fetch_rows(embed_table, ids, first_section, weight_part, slots)
    length = pick(first_section, lengths)
    spots = pick(first_section, positions[:, 0])
    row_weights = pick(first_section, loss_weights[:, 0]).astype(F32)[:, None]
    chosen = (spots[:, None] == jnp.arange(SEQ)[None, :]).astype(BF16)
    chosen_t = (spots[None, :] == jnp.arange(SEQ)[:, None]).astype(F32)

    hidden, query, key, value, mixed, lse, *kept_coupling = first_kernel(
        fetched, pos_table, norms, coupling, w_qkv, length
    )
    section_out, *kept = rest_forward(0, hidden, mixed, norms, adapters[0], w_rest)
    at_spots, query_1, key_1, value_1, mixed_1, lse_1 = spots_kernel(section_out, chosen, w_qkv, length)
    normed, *kept_1 = rest_forward(1, at_spots, mixed_1, norms, adapters[1], w_rest, coupling)

    rows = jnp.broadcast_to(normed[None], (parts, COUNT, D))
    rows = lax.all_to_all(rows, "dp", 0, 0).reshape(parts * COUNT, D)
    merged = head_kernel(rows, embed_table).reshape(parts, COUNT, D + LANES)
    merged = lax.all_to_all(merged, "dp", 0, 0)

    head = (kept_1[8:], coupling, normed, fetched[SEQ:], row_weights, weight_sum.reshape(1, 1))
    start_grad, mixed_grad, *grads = rest_backward(1, merged, kept_1[:8], norms, adapters[1], w_rest, head)
    adapter_grads_1, loss_part, head_grads = grads[:4], grads[4], grads[5:]
    section_grad = spots_backward(
        (query_1, key_1, value_1, lse_1), mixed_grad, start_grad, chosen_t, w_qkv, length
    )
    start_grad, mixed_grad, *adapter_grads_0 = rest_backward(0, section_grad, kept, norms, adapters[0], w_rest)
    grads = first_backward(
        (query, key, value, lse), mixed_grad, start_grad, kept_coupling, coupling, head_grads, w_qkv, length
    )
    grads_one, grads_two = grads[:4], grads[4:]

    grad_blocks, grad_vector, pair = sum_at_owners(
        ((adapter_grads_0, grads_one), (adapter_grads_1, grads_two)), loss_part, master.shape[1]
    )
    totals = jnp.sum(lax.all_to_all(pair, ("dp", "section"), 0, 0), (0, 1))
    grad_norm = jnp.sqrt(totals[0])
    loss_sum = totals[1]
    factor = CLIP_NORM / jnp.maximum(grad_norm, CLIP_NORM)
    clipped = grad_blocks * factor
    clipped_vector = grad_vector * factor
    momentum_new = FIRST_DECAY * momentum[0] + (1.0 - FIRST_DECAY) * clipped
    left_new = STAT_DECAY * stat_left[0] + (1.0 - STAT_DECAY) * jnp.einsum(
        "nij,nkj->nik", clipped, clipped, precision=HIGHEST
    )
    right_new = STAT_DECAY * stat_right[0] + (1.0 - STAT_DECAY) * jnp.einsum(
        "nji,njk->nik", clipped, clipped, precision=HIGHEST
    )
    direction = jnp.einsum("nij,njk->nik", root_left[0], momentum_new, precision=HIGHEST)
    direction = jnp.einsum("nij,njk->nik", direction, root_right[0], precision=HIGHEST)
    master_new = master[0] - MAT_RATE * (direction + MAT_DECAY * master[0])
    first_new = FIRST_DECAY * vec_first[0] + (1.0 - FIRST_DECAY) * clipped_vector
    second_new = VEC_SECOND * vec_second[0] + (1.0 - VEC_SECOND) * clipped_vector * clipped_vector
    corrected_first = first_new / (1.0 - FIRST_DECAY**STEP)
    corrected_second = second_new / (1.0 - VEC_SECOND**STEP)
    vectors_new = vectors[0] - VEC_RATE * (
        corrected_first / (jnp.sqrt(corrected_second) + VEC_EPS) + VEC_DECAY * vectors[0]
    )
    return (
        clipped[None],
        momentum_new[None],
        left_new[None],
        right_new[None],
        master_new[None],
        master_new.astype(BF16)[None],
        first_new[None],
        second_new[None],
        vectors_new[None],
        grad_norm,
        loss_sum,
        weight_sum,
    )


def solution(mesh):
    rows = P(None, "dp", None)
    section = P("section", None, None)
    blocks = P("section", "dp", None, None)
    biases = P("section", "dp")
    return jax.shard_map(
        shards,
        mesh=mesh,
        in_specs=(rows, P(None, "dp"), rows, rows, rows, P("dp", None), P())
        + (section,) * 5
        + (blocks,) * 6
        + (biases,) * 3,
        out_specs=(blocks,) * 6 + (biases,) * 3 + (P(),) * 3,
        check_vma=False,
    )
```

```python
import functools

import jax
import jax.numpy as jnp
import numpy as np
from jax import lax
from jax.experimental import pallas as pl
from jax.experimental.pallas import tpu as pltpu
from jax.sharding import PartitionSpec as P

D = 768
HEADS = 12
HEAD_DIM = 64
BOT = 384
INV_H = 192
SEQ = 512
COUNT = 32
MICRO = 2
BLOCK = 48
STEP = 10
HALF = 384
IDS = SEQ + COUNT

HIGHEST = lax.Precision.HIGHEST
NORM_EPS = 1e-12
CLIP_NORM = 0.02
FIRST_DECAY = 0.9
STAT_DECAY = 0.99
MAT_RATE = 0.1
MAT_DECAY = 0.01
VEC_RATE = 0.05
VEC_SECOND = 0.999
VEC_EPS = 1e-08
VEC_DECAY = 0.01
F32 = jnp.float32
BF16 = jnp.bfloat16

CDF_SCALE = 0.42 / 2.0**0.5
CDF_POLY = (
    0.2368242366796694,
    0.239585811361218,
    0.1947261443420679,
    0.2687426685879861,
    -0.13052645834187002,
    0.4406726942003943,
    -0.32025628294963193,
    0.07023101752398136,
)


def matmul(left, right):
    return jnp.dot(left, right, preferred_element_type=F32)


def matmul_t(left, right):
    return lax.dot_general(left, right, (((1,), (1,)), ((), ())), preferred_element_type=F32)


def inner_rows(left, right):
    return lax.dot_general(left, right, (((0,), (0,)), ((), ())), preferred_element_type=F32)


def low(values):
    return values.astype(BF16)


def gelu_both(values):
    ratio = 1.0 / (1.0 + CDF_SCALE * jnp.abs(values))
    poly = jnp.full_like(ratio, 0.5 * CDF_POLY[-1])
    for factor in CDF_POLY[-2::-1]:
        poly = poly * ratio + 0.5 * factor
    bell = jnp.exp(-0.5 * values * values)
    tail = bell * (poly * ratio)
    cdf = jnp.where(values < 0, tail, 1.0 - tail)
    return values * cdf, cdf + values * (bell * (2.0 * np.pi) ** -0.5)


def layer_norm(values, gain, shift):
    centered = values - jnp.mean(values, -1, keepdims=True)
    inverse = lax.rsqrt(jnp.mean(centered * centered, -1, keepdims=True) + NORM_EPS)
    normal = centered * inverse
    return normal * gain + shift, (normal, inverse)


def norm_back(incoming, kept, gain):
    normal, inverse = kept
    scaled = incoming * gain
    return inverse * (
        scaled
        - jnp.mean(scaled, -1, keepdims=True)
        - normal * jnp.mean(scaled * normal, -1, keepdims=True)
    )


def to_blocks(matrix):
    rows_in, cols_in = matrix.shape
    return (
        matrix.reshape(rows_in // BLOCK, BLOCK, cols_in // BLOCK, BLOCK)
        .transpose(0, 2, 1, 3)
        .reshape(-1, BLOCK, BLOCK)
    )


def from_blocks(blocks, rows_in, cols_in):
    return (
        blocks.reshape(rows_in // BLOCK, cols_in // BLOCK, BLOCK, BLOCK)
        .transpose(0, 2, 1, 3)
        .reshape(rows_in, cols_in)
    )


def split_params(blocks, vector):
    adapter_count = D * BOT // BLOCK**2
    half_count = HALF * INV_H // BLOCK**2
    split_at = 2 * adapter_count
    adapter = (
        from_blocks(blocks[:adapter_count], D, BOT),
        vector[:BOT],
        from_blocks(blocks[adapter_count:split_at], BOT, D),
        vector[BOT : BOT + D],
    )
    coupling = (
        from_blocks(blocks[split_at : split_at + half_count], HALF, INV_H),
        vector[BOT + D : BOT + D + INV_H],
        from_blocks(blocks[split_at + half_count :], INV_H, HALF),
        vector[BOT + D + INV_H :],
    )
    return adapter, coupling


def join_params(adapter, coupling):
    blocks = jnp.concatenate(
        [to_blocks(adapter[0]), to_blocks(adapter[2]), to_blocks(coupling[0]), to_blocks(coupling[2])]
    )
    return blocks, jnp.concatenate([adapter[1], adapter[3], coupling[1], coupling[3]], 1)[0]


GROUP_ROWS = 72
LANES = 128


def whole(shape):
    return pl.BlockSpec(shape, lambda *_: (0,) * len(shape))


def section_of(shape, section):
    return pl.BlockSpec((None,) + shape, lambda *_: (section,) + (0,) * len(shape))


def params_for(mebibytes):
    return pltpu.CompilerParams(vmem_limit_bytes=mebibytes * 2**20)


def roll(values, shift):
    return pltpu.roll(values, shift, 1)


def lane_of(values):
    return lax.broadcasted_iota(jnp.int32, values.shape, 1)


def fold_half(values, upper):
    top, bottom = values[:24], values[24:]
    if upper:
        return jnp.where(lane_of(top) < 64, roll(top, 64), bottom)
    return jnp.where(lane_of(top) < 64, top, roll(bottom, 64))


def unfold_half(values, upper):
    turned = roll(values, 64)
    return jnp.concatenate([turned, values] if upper else [values, turned], 0)


def join_pair(main_0, rest_0, main_1, rest_1):
    left = lane_of(main_0) < 64
    turned = roll(main_1, 64)
    return (
        main_0,
        jnp.where(left, unfold_half(rest_0, False), turned),
        jnp.where(left, turned, unfold_half(rest_1, True)),
    )


def cut_pair(tile_0, tile_1, tile_2):
    left = lane_of(tile_0) < 64
    return (
        (tile_0, fold_half(tile_1, False)),
        (jnp.where(left, roll(tile_1, 64), roll(tile_2, 64)), fold_half(tile_2, True)),
    )


def chunk_rows(own_blocks):
    return own_blocks // 4 * GROUP_ROWS + 8


def bias_row(tiles, part, width):
    at, shift = divmod(part * width, LANES)
    lane = lane_of(tiles[0])
    row = tiles[at]
    if shift:
        row = jnp.where(lane < LANES - shift, roll(row, LANES - shift), roll(tiles[at + 1], LANES - shift))
    return jnp.where(lane < width, row, 0.0)


def bias_tiles(first, second, third, fourth):
    cut = lambda values: [values[:, at : at + LANES] for at in range(0, values.shape[1], LANES)]
    zero = jnp.zeros((1, LANES), F32)
    left = lane_of(zero) < 64
    third_tail = jnp.concatenate([third[:, LANES:]] * 2, 1)
    turned = [roll(tile, 64) for tile in cut(fourth)]
    joints = [jnp.where(left, one, two) for one, two in zip([third_tail] + turned, turned + [zero])]
    return cut(first) + cut(second) + [third[:, :LANES]] + joints + [zero]


def tiles_of_rows(rows, width):
    tiles = []
    for tile in range(-(-len(rows) * width // LANES)):
        value = jnp.zeros((8, LANES), F32)
        lane = lane_of(value)
        for part, row in enumerate(rows):
            shift = part * width - tile * LANES
            if shift >= LANES or shift + width <= 0:
                continue
            turned = roll(row, shift % LANES) if shift % LANES else row
            value = jnp.where((lane >= shift) & (lane < shift + width), turned, value)
        tiles.append(value)
    return tiles


def pack_own(master, vector):
    count, width = master.shape[0], vector.shape[1]

    def kernel(master_ref, bias_ref, out_ref):
        row = lax.broadcasted_iota(jnp.int32, (BLOCK, 256), 0)
        col = lax.broadcasted_iota(jnp.int32, (BLOCK, 256), 1)
        pieces = []
        for group in range(count // 4):
            wide = jnp.zeros((BLOCK, 256), F32)
            for j in range(4):
                wide += matmul(low(master_ref[4 * group + j]), (col == row + BLOCK * j).astype(BF16))
            pieces += [wide[:, :LANES], fold_half(wide[:, LANES:], False)]
        bias = jnp.concatenate([bias_ref[...], jnp.zeros((1, LANES - width), F32)], 1)
        pieces.append(jnp.concatenate([bias, jnp.zeros((7, LANES), F32)], 0))
        out_ref[...] = low(jnp.concatenate(pieces, 0))

    return pl.pallas_call(
        kernel,
        out_shape=jax.ShapeDtypeStruct((chunk_rows(count), LANES), BF16),
        name="pack_own",
    )(master, vector)


MATRICES = ((D, BOT), (BOT, D), (HALF, INV_H), (INV_H, HALF))
BIASES = (BOT, D, INV_H, HALF)


def unpack_all(gathered, width):
    sections, parts, rows, _ = gathered.shape
    per_part = (rows - 8) // GROUP_ROWS

    def kernel(in_ref, *out_refs):
        cache = {}

        def group(index):
            part = index // per_part
            if part not in cache:
                cache.clear()
                cache[part] = in_ref[part].astype(F32)
            base = index % per_part * GROUP_ROWS
            chunk = cache[part]
            return chunk[base : base + BLOCK], chunk[base + BLOCK : base + GROUP_ROWS]

        index = 0
        for (height, columns), out_ref in zip(MATRICES, out_refs):
            for top in range(0, height, BLOCK):
                if columns == INV_H:
                    main, rest = group(index)
                    index += 1
                    out_ref[top : top + BLOCK, :LANES] = low(main)
                    out_ref[top : top + BLOCK, LANES:] = low(unfold_half(rest, False)[:, :64])
                    continue
                for left in range(0, columns, HALF):
                    tiles = join_pair(*group(index), *group(index + 1))
                    index += 2
                    for j, tile in enumerate(tiles):
                        at = left + j * LANES
                        out_ref[top : top + BLOCK, at : at + LANES] = low(tile)
        tiles = tiles_of_rows([in_ref[part, rows - 16 :].astype(F32)[8:] for part in range(parts)], width)
        first, second, third, fourth = out_refs[4:]
        first[...] = jnp.concatenate(tiles[:3], 1)[:1]
        second[...] = jnp.concatenate(tiles[3:9], 1)[:1]
        third[...] = jnp.concatenate([tiles[9], tiles[10][:, :64]], 1)[:1]
        left = lane_of(tiles[0]) < 64
        turned = [roll(tile, 64) for tile in tiles[10:14]]
        fourth[...] = jnp.concatenate(
            [jnp.where(left, one, two) for one, two in zip(turned, turned[1:])], 1
        )[:1]

    return pl.pallas_call(
        kernel,
        grid=(sections,),
        in_specs=[pl.BlockSpec((None, parts, rows, LANES), lambda s: (s, 0, 0, 0))],
        out_specs=[pl.BlockSpec((None,) + shape, lambda s: (s, 0, 0)) for shape in MATRICES]
        + [pl.BlockSpec((None, 1, size), lambda s: (s, 0, 0)) for size in BIASES],
        out_shape=[jax.ShapeDtypeStruct((sections,) + shape, BF16) for shape in MATRICES]
        + [jax.ShapeDtypeStruct((sections, 1, size), F32) for size in BIASES],
        compiler_params=params_for(32),
        name="unpack_all",
    )(gathered)


ADAPTER_GROUPS = 2 * D * BOT // BLOCK**2 // 4
COUPLING_GROUPS = 2 * HALF * INV_H // BLOCK**2 // 4
PART_GROUPS = (ADAPTER_GROUPS + COUPLING_GROUPS) // COUPLING_GROUPS
PART_ROWS = PART_GROUPS * GROUP_ROWS


def groups_of(refs, shapes):
    groups = []
    for ref, (height, width) in zip(refs, shapes):
        for top in range(0, height, BLOCK):
            band = slice(top, top + BLOCK)
            if width == INV_H:
                tail = ref[band, LANES:]
                groups.append((ref[band, :LANES], fold_half(jnp.concatenate([tail, tail], 1), False)))
                continue
            for left in range(0, width, HALF):
                groups += cut_pair(*[ref[band, left + j * LANES : left + (j + 1) * LANES] for j in range(3)])
    return [jnp.concatenate(group, 0) for group in groups]


def pack_adapter(refs, store):
    groups = groups_of(refs, MATRICES[:2])
    empty = jnp.zeros((GROUP_ROWS, LANES), F32)
    for part in range(COUPLING_GROUPS):
        chunk = groups[part * PART_GROUPS : (part + 1) * PART_GROUPS]
        chunk += [empty] * (PART_GROUPS - len(chunk))
        store(part, low(jnp.concatenate(chunk, 0)))


def pack_coupling(refs, tiles, width, store):
    for part, group in enumerate(groups_of(refs, MATRICES[2:])):
        bias = jnp.concatenate([bias_row(tiles, part, width), jnp.zeros((7, LANES), F32)], 0)
        store(part, jnp.concatenate([group, bias], 0))


def sum_parts(came_ref):
    total = came_ref[0].astype(F32)
    for part in range(1, came_ref.shape[0]):
        total += came_ref[part].astype(F32)
    return total


def square_sum(values):
    return jnp.sum(jnp.sum(values * values, 0, keepdims=True), 1, keepdims=True)


def sum_adapter(came):
    def kernel(came_ref, total_ref, square_ref):
        total = sum_parts(came_ref)
        total_ref[...] = total
        square_ref[...] = square_sum(total)

    return pl.pallas_call(
        kernel,
        out_shape=[jax.ShapeDtypeStruct((PART_ROWS, LANES), F32), jax.ShapeDtypeStruct((1, 1), F32)],
        compiler_params=params_for(32),
        name="sum_adapter",
    )(came)


def sum_coupling(came, squares, loss_part, copies):
    def kernel(came_ref, square_ref, loss_ref, group_ref, bias_ref, pair_ref):
        total = sum_parts(came_ref)
        group_ref[...] = total[:GROUP_ROWS]
        bias_ref[...] = total[GROUP_ROWS:]
        squares = square_ref[...] + square_sum(total)
        lane = lax.broadcasted_iota(jnp.int32, (1, LANES), 1)
        pair = jnp.where(lane == 0, squares, jnp.where(lane == 1, loss_ref[...], 0.0))
        pair_ref[...] = jnp.broadcast_to(pair[None], pair_ref.shape)

    return pl.pallas_call(
        kernel,
        out_shape=[
            jax.ShapeDtypeStruct((GROUP_ROWS, LANES), F32),
            jax.ShapeDtypeStruct((8, LANES), F32),
            jax.ShapeDtypeStruct((copies, 1, LANES), F32),
        ],
        name="sum_coupling",
    )(came, squares, loss_part)


def own_blocks_of(adapter_total, coupling_groups):
    def kernel(total_ref, *refs):
        group_refs, blocks_ref = refs[:-1], refs[-1]
        for group in range(PART_GROUPS):
            total = total_ref[group * GROUP_ROWS : (group + 1) * GROUP_ROWS] + group_refs[group][...]
            main, rest = total[:BLOCK], unfold_half(total[BLOCK:], False)
            lane = lane_of(main)
            pieces = (
                main,
                roll(main, 80),
                jnp.where(lane < 32, roll(main, 32), roll(rest, 32)),
                roll(rest, 112),
            )
            for j, values in enumerate(pieces):
                blocks_ref[4 * group + j] = values[:, :BLOCK]

    return pl.pallas_call(
        kernel,
        out_shape=jax.ShapeDtypeStruct((4 * PART_GROUPS, BLOCK, BLOCK), F32),
        name="own_blocks",
    )(adapter_total, *coupling_groups)


GROUP = 256
HEADS_IN = GROUP // HEAD_DIM
GROUPS = D // GROUP
FF = 3072
TILE = 512
TILES = FF // TILE


def rows_of(count, size):
    return [slice(at, at + min(size, count)) for at in range(0, count, size)]


def vmem(count):
    return [pl.BlockSpec(memory_space=pltpu.VMEM)] * count


def hbm(count):
    return [pl.BlockSpec(memory_space=pl.ANY)] * count


def shape_of(*dims, kind=F32):
    return jax.ShapeDtypeStruct(dims, kind)


def start_copy(pair, section, window, target, sem):
    own, came = pair
    here = lax.axis_index("section") == section

    @pl.when(here)
    def _():
        pltpu.make_async_copy(own.at[window], target, sem).start()

    @pl.when(jnp.logical_not(here))
    def _():
        pltpu.make_async_copy(came.at[window], target, sem).start()


def wait_copy(pair, window, target, sem):
    pltpu.make_async_copy(pair[0].at[window], target, sem).wait()


def qkv_window(group, part):
    return 0, slice(None), pl.ds(part * D + group * GROUP, GROUP)


def across(values):
    return jnp.broadcast_to(values, (values.shape[0], LANES))


def head_mask(values, head):
    lane = lax.broadcasted_iota(jnp.int32, values.shape, 1)
    return (lane >= head * HEAD_DIM) & (lane < (head + 1) * HEAD_DIM)


def only_head(values, head):
    return jnp.where(head_mask(values, head), values, jnp.zeros_like(values))


def scaled_query(query):
    return low(query.astype(F32) * HEAD_DIM**-0.5)


def key_bias(length, shape, axis):
    return jnp.where(lax.broadcasted_iota(jnp.int32, shape, axis) < length, 0.0, -1e30)


def softmax_rows(scores):
    highest = jnp.max(scores, 1, keepdims=True)
    exponent = jnp.exp(scores - highest)
    total = jnp.sum(exponent, 1, keepdims=True)
    return low(exponent * (1.0 / total)), highest + jnp.log(total)


def first_kernel(fetched, pos_table, norms, coupling, w_qkv, length):
    def kernel(length_ref, fetched_ref, pos_ref, norms_ref, *refs):
        c_refs, w_pair, refs = refs[:8], refs[8:10], refs[10:]
        hidden_ref, q_ref, k_ref, v_ref, mixed_ref, lse_ref = refs[:6]
        kept_refs, (x_low, w_buf, s_buf, p_buf, lse_buf, sems) = refs[6:12], refs[12:]
        group = pl.program_id(0)

        @pl.when(group == 0)
        def _():
            for g in range(GROUPS):
                for part in range(3):
                    start_copy(w_pair, 0, qkv_window(g, part), w_buf.at[g, part], sems.at[g, part])
            for rows in rows_of(SEQ, 256):
                started, _ = layer_norm(
                    fetched_ref[rows] + pos_ref[rows].astype(F32), norms_ref[0, 0:1], norms_ref[0, 1:2]
                )
                left, right = started[:, :HALF], started[:, HALF:]
                low_one = low(right)
                active, slope = gelu_both(matmul(low_one, c_refs[0][...]) + c_refs[1][...])
                active = low(active)
                left = left + matmul(active, c_refs[2][...]) + c_refs[3][...]
                for ref, value in zip(kept_refs[:3], (low_one, active, low(slope))):
                    ref[rows] = value
                low_two = low(left)
                active, slope = gelu_both(matmul(low_two, c_refs[4][...]) + c_refs[5][...])
                active = low(active)
                right = right + matmul(active, c_refs[6][...]) + c_refs[7][...]
                for ref, value in zip(kept_refs[3:], (low_two, active, low(slope))):
                    ref[rows] = value
                hidden_ref[rows, :HALF] = left
                hidden_ref[rows, HALF:] = right
                x_low[rows, :HALF] = low_two
                x_low[rows, HALF:] = low(right)

        for part, ref in enumerate((q_ref, k_ref, v_ref)):
            wait_copy(w_pair, qkv_window(group, part), w_buf.at[group, part], sems.at[group, part])
            ref[...] = low(matmul(x_low[...], w_buf[group, part]))
        query = scaled_query(q_ref[...])
        key, value = k_ref[...], v_ref[...]
        bias = key_bias(length_ref[0], (1, SEQ), 1)
        lane = lax.broadcasted_iota(jnp.int32, (SEQ, LANES), 1)
        mixed = jnp.zeros((SEQ, GROUP), F32)
        lse_buf[...] = jnp.zeros((SEQ, LANES), F32)
        for head in range(HEADS_IN):
            s_ref, p_ref = s_buf.at[head % 2], p_buf.at[head % 2]
            s_ref[...] = matmul_t(only_head(query, head), key)
            for rows in rows_of(SEQ, 64):
                soft, lse = softmax_rows(s_ref[rows] + bias)
                p_ref[rows] = soft
                lse_buf[rows] = jnp.where(lane[rows] == head, lse, lse_buf[rows])
            mixed = jnp.where(head_mask(mixed, head), matmul(p_ref[...], value), mixed)
        mixed_ref[...] = low(mixed)
        lse_ref[...] = jnp.transpose(lse_buf[...])[:8]

    column = pl.BlockSpec((SEQ, GROUP), lambda g: (0, g))
    low_wide = shape_of(SEQ, D, kind=BF16)
    kept = [(SEQ, HALF), (SEQ, INV_H), (SEQ, INV_H)] * 2
    return pl.pallas_call(
        kernel,
        grid=(GROUPS,),
        in_specs=[pl.BlockSpec(memory_space=pltpu.SMEM)]
        + [whole((SEQ, D)), whole((SEQ, D)), whole((MICRO, 6, D))]
        + [whole(value.shape) for value in coupling]
        + hbm(2),
        out_specs=[whole((SEQ, D))]
        + [column] * 4
        + [pl.BlockSpec((None, 8, SEQ), lambda g: (g, 0, 0))]
        + [whole(dims) for dims in kept],
        out_shape=[shape_of(SEQ, D)]
        + [low_wide] * 4
        + [shape_of(GROUPS, 8, SEQ)]
        + [shape_of(*dims, kind=BF16) for dims in kept],
        scratch_shapes=[
            pltpu.VMEM((SEQ, D), BF16),
            pltpu.VMEM((GROUPS, 3, D, GROUP), BF16),
            pltpu.VMEM((2, SEQ, SEQ), F32),
            pltpu.VMEM((2, SEQ, SEQ), BF16),
            pltpu.VMEM((SEQ, LANES), F32),
            pltpu.SemaphoreType.DMA((GROUPS, 3)),
        ],
        compiler_params=params_for(48),
        name="first_layer_attention",
    )(length, fetched, pos_table, norms, *coupling, *w_qkv)


def spots_kernel(section_out, chosen, w_qkv, length):
    def kernel(length_ref, x_ref, chosen_ref, own_ref, came_ref, *refs):
        at_ref, q_ref, k_ref, v_ref, mixed_ref, lse_ref, at_low, w_buf, sems = refs
        w_pair = own_ref, came_ref
        group = pl.program_id(0)

        @pl.when(group == 0)
        def _():
            for g in range(GROUPS):
                for part in range(3):
                    start_copy(w_pair, 1, qkv_window(g, part), w_buf.at[g, part], sems.at[g, part])
            at_ref[...] = matmul(chosen_ref[...], x_ref[...])
            at_low[...] = low(at_ref[...])

        for part, ref in enumerate((q_ref, k_ref, v_ref)):
            wait_copy(w_pair, qkv_window(group, part), w_buf.at[group, part], sems.at[group, part])
            ref[...] = low(matmul(at_low[...] if part == 0 else x_ref[...], w_buf[group, part]))
        query = scaled_query(q_ref[...])
        query = jnp.concatenate([only_head(query, head) for head in range(HEADS_IN)], 0)
        bias = key_bias(length_ref[0], (1, SEQ), 1)
        soft, lse = softmax_rows(matmul_t(query, k_ref[...]) + bias)
        lse_ref[...] = across(lse)
        every = matmul(soft, v_ref[...])
        mixed = every[:COUNT]
        for head in range(1, HEADS_IN):
            mixed = jnp.where(head_mask(mixed, head), every[head * COUNT : (head + 1) * COUNT], mixed)
        mixed_ref[...] = low(mixed)

    narrow = pl.BlockSpec((COUNT, GROUP), lambda g: (0, g))
    column = pl.BlockSpec((SEQ, GROUP), lambda g: (0, g))
    return pl.pallas_call(
        kernel,
        grid=(GROUPS,),
        in_specs=[pl.BlockSpec(memory_space=pltpu.SMEM), whole((SEQ, D)), whole((COUNT, SEQ))] + hbm(2),
        out_specs=[whole((COUNT, D)), narrow, column, column, narrow]
        + [pl.BlockSpec((None, HEADS_IN * COUNT, LANES), lambda g: (g, 0, 0))],
        out_shape=[
            shape_of(COUNT, D),
            shape_of(COUNT, D, kind=BF16),
            shape_of(SEQ, D, kind=BF16),
            shape_of(SEQ, D, kind=BF16),
            shape_of(COUNT, D, kind=BF16),
            shape_of(GROUPS, HEADS_IN * COUNT, LANES),
        ],
        scratch_shapes=[
            pltpu.VMEM((COUNT, D), BF16),
            pltpu.VMEM((GROUPS, 3, D, GROUP), BF16),
            pltpu.SemaphoreType.DMA((GROUPS, 3)),
        ],
        compiler_params=params_for(32),
        name="second_layer_attention",
    )(length, section_out, chosen, *w_qkv)


UP_WINDOWS = [(0, slice(None), slice(j * TILE, (j + 1) * TILE)) for j in range(TILES)]
DOWN_WINDOWS = [(0, slice(j * TILE, (j + 1) * TILE), slice(None)) for j in range(TILES)]
OUT_WINDOW = (0, slice(None), slice(None))


def rest_buffers():
    return [
        pltpu.VMEM((D, D), BF16),
        pltpu.VMEM((TILES, D, TILE), BF16),
        pltpu.VMEM((TILES, TILE, D), BF16),
        pltpu.SemaphoreType.DMA((2 * TILES + 1,)),
    ]


def start_rest(pairs, section, buffers):
    out_buf, up_buf, down_buf, sems = buffers
    start_copy(pairs[0], section, OUT_WINDOW, out_buf, sems.at[2 * TILES])
    for j in range(TILES):
        start_copy(pairs[1], section, UP_WINDOWS[j], up_buf.at[j], sems.at[j])
        start_copy(pairs[2], section, DOWN_WINDOWS[j], down_buf.at[j], sems.at[TILES + j])


def wait_out(pairs, buffers):
    wait_copy(pairs[0], OUT_WINDOW, buffers[0], buffers[3].at[2 * TILES])


def wait_tile(pairs, buffers, tile):
    _, up_buf, down_buf, sems = buffers
    wait_copy(pairs[1], UP_WINDOWS[0], up_buf.at[tile], sems.at[tile])
    wait_copy(pairs[2], DOWN_WINDOWS[0], down_buf.at[tile], sems.at[TILES + tile])


def rest_forward(section, hidden, mixed, norms, adapter, w_rest, coupling=None):
    rows = hidden.shape[0]
    step = min(rows, 256)
    last = coupling is not None
    extra_in = coupling if last else ()

    def kernel(hidden_ref, mixed_ref, norms_ref, *refs):
        a_refs, refs = refs[:4], refs[4:]
        c_refs, refs = refs[: len(extra_in)], refs[len(extra_in) :]
        w_flat, refs = refs[:6], refs[6:]
        pairs = [w_flat[2 * i : 2 * i + 2] for i in range(3)]
        outs, refs = refs[:n_outs], refs[n_outs:]
        result_ref, n1_ref, i1_ref, slope_ref, lin_ref, act_ref, bslope_ref, n2_ref, i2_ref = outs[:9]
        att, att_low, acc, u_buf, g_buf = refs[:5]
        buffers = refs[5:]
        tile = pl.program_id(0)
        gain = lambda i: norms_ref[section, i : i + 1]

        @pl.when(tile == 0)
        def _():
            start_rest(pairs, section, buffers)
            wait_out(pairs, buffers)
            for part in rows_of(rows, step):
                first = hidden_ref[part] + matmul(mixed_ref[part], buffers[0][...])
                values, (normal, inverse) = layer_norm(first, gain(2), gain(3))
                att[part] = values
                att_low[part] = low(values)
                n1_ref[part] = normal
                i1_ref[part] = across(inverse)

        wait_tile(pairs, buffers, tile)
        for i, part in enumerate(rows_of(rows, step)):
            u_buf[i] = matmul(att_low[part], buffers[1][tile])
            for small in rows_of(step, 32):
                active, slope = gelu_both(u_buf[i, small])
                g_buf[i, small] = low(active)
                slope_ref[part.start + small.start : part.start + small.stop] = low(slope)
            product = matmul(g_buf[i], buffers[2][tile])

            @pl.when(tile == 0)
            def _(part=part, product=product):
                acc[part] = product

            @pl.when(tile > 0)
            def _(part=part, product=product):
                acc[part] += product

        @pl.when(tile == TILES - 1)
        def _():
            for part in rows_of(rows, step):
                summed = acc[part] + att[part]
                low_in = low(summed)
                active, slope = gelu_both(matmul(low_in, a_refs[0][...]) + a_refs[1][...])
                active = low(active)
                lin_ref[part], act_ref[part], bslope_ref[part] = low_in, active, low(slope)
                second = summed + (matmul(active, a_refs[2][...]) + a_refs[3][...])
                values, (normal, inverse) = layer_norm(second, gain(4), gain(5))
                n2_ref[part], i2_ref[part] = normal, across(inverse)
                if not last:
                    result_ref[part] = low(values)
            if last:
                left, right = values[:, :HALF], values[:, HALF:]
                low_two = low(left)
                active_two, slope_two = gelu_both(matmul(low_two, c_refs[4][...]) + c_refs[5][...])
                active_two = low(active_two)
                right = right - (matmul(active_two, c_refs[6][...]) + c_refs[7][...])
                low_one = low(right)
                active_one, slope_one = gelu_both(matmul(low_one, c_refs[0][...]) + c_refs[1][...])
                active_one = low(active_one)
                left = left - (matmul(active_one, c_refs[2][...]) + c_refs[3][...])
                normed, (normal, inverse) = layer_norm(
                    jnp.concatenate([left, right], 1), gain(0), gain(1)
                )
                result_ref[...] = low(normed)
                kept = (normal, across(inverse), low_one, active_one, low(slope_one))
                kept += (low_two, active_two, low(slope_two))
                for ref, value in zip(outs[9:], kept):
                    ref[...] = value

    wide, thin = shape_of(rows, D), shape_of(rows, LANES)
    out_shape = [shape_of(rows, D, kind=BF16), wide, thin, shape_of(rows, FF, kind=BF16)]
    out_shape += [shape_of(rows, D, kind=BF16), shape_of(rows, BOT, kind=BF16)]
    out_shape += [shape_of(rows, BOT, kind=BF16), wide, thin]
    if last:
        out_shape += [wide, thin]
        out_shape += [shape_of(rows, n, kind=BF16) for n in (HALF, INV_H, INV_H)] * 2
    n_outs = len(out_shape)
    out_specs = [whole(out.shape) for out in out_shape]
    out_specs[3] = pl.BlockSpec((rows, TILE), lambda j: (0, j))
    return pl.pallas_call(
        kernel,
        grid=(TILES,),
        in_specs=[whole((rows, D)), whole((rows, D)), whole((MICRO, 6, D))]
        + [whole(value.shape) for value in (*adapter, *extra_in)]
        + hbm(6),
        out_specs=out_specs,
        out_shape=out_shape,
        scratch_shapes=[
            pltpu.VMEM((rows, D), F32),
            pltpu.VMEM((rows, D), BF16),
            pltpu.VMEM((rows, D), F32),
            pltpu.VMEM((rows // step, step, TILE), F32),
            pltpu.VMEM((rows // step, step, TILE), BF16),
        ]
        + rest_buffers(),
        compiler_params=params_for(52),
        name="last_rows_forward" if last else "first_layer_rest",
    )(hidden, mixed, norms, *adapter, *extra_in, *[w for pair in w_rest for w in pair])


def column_sum(values):
    return jnp.sum(values.astype(F32), 0, keepdims=True)


def branch_grads(grad_low, kept, weights, out_refs):
    low_in, active, slope = kept
    hidden_grad = low(matmul_t(grad_low, weights[2]) * slope.astype(F32))
    out_refs[0][...] = inner_rows(low_in, hidden_grad)
    out_refs[1][...] = column_sum(hidden_grad)
    out_refs[2][...] = inner_rows(active, grad_low)
    out_refs[3][...] = column_sum(grad_low)
    return hidden_grad


ADAPTER_GRADS = ((D, BOT), (1, BOT), (BOT, D), (1, D))
COUPLING_GRADS = ((HALF, INV_H), (1, INV_H), (INV_H, HALF), (1, HALF))


def rest_backward(section, incoming, kept, norms, adapter, w_rest, head=None, packed=False, other_packed=None):
    n1, i1, slope, lin, act, bslope, n2, i2 = kept
    rows = n1.shape[0]
    step = min(rows, 256)
    last = head is not None
    if last:
        head_kept, coupling, normed, target_rows, row_weights, weight_sum = head
        extra_in = (*head_kept, *coupling, normed, target_rows, row_weights, weight_sum)
    else:
        extra_in = () if other_packed is None else (other_packed,)

    def kernel(incoming_ref, n1_ref, i1_ref, slope_ref, lin_ref, act_ref, bslope_ref, n2_ref, i2_ref, *refs):
        norms_ref, a_refs, refs = refs[0], refs[1:5], refs[5:]
        e_refs, refs = refs[: len(extra_in)], refs[len(extra_in) :]
        w_flat, refs = refs[:6], refs[6:]
        pairs = [w_flat[2 * i : 2 * i + 2] for i in range(3)]
        outs, refs = refs[:n_outs], refs[n_outs:]
        start_ref, mixed_ref, grad_refs, outs = outs[0], outs[1], outs[2:6], outs[2:]
        summed, summed_low, acc, second_low, hidden_low = refs[:5]
        buffers, refs = refs[5:9], refs[9:]
        if packed:
            grad_refs = (refs[0], outs[0], refs[1], outs[1])
        tile = pl.program_id(0)
        gain = lambda i: norms_ref[section, i : i + 1]

        def pack():
            if last:
                def store(part, chunk):
                    outs[2][part] = chunk
            else:
                here = lax.axis_index("section") == section

                def store(part, chunk):
                    arrived = e_refs[0][part]
                    outs[2][part] = jnp.where(here, chunk, arrived)
                    outs[3][part] = jnp.where(here, arrived, chunk)

            pack_adapter((grad_refs[0], grad_refs[2]), store)

        def from_head():
            nh_ref, ih_ref = e_refs[:2]
            kept_one, kept_two = ([ref[...] for ref in e_refs[at : at + 3]] for at in (2, 5))
            c_one, c_two = ([ref[...] for ref in e_refs[at : at + 4]] for at in (8, 12))
            normed_ref, target_ref, weight_ref, total_ref = e_refs[16:]
            loss_ref, one_refs, two_refs = outs[-9], outs[-8:-4], outs[-4:]
            parts = incoming_ref.shape[0]
            stats = incoming_ref[:, :, D:].astype(F32)
            highest = jnp.sum(stats[:, :, :3], 2, keepdims=True)
            totals = jnp.sum(stats[:, :, 3:6], 2, keepdims=True)
            top = jnp.max(highest, 0)
            factor = jnp.exp(highest - top[None])
            total = jnp.sum(totals * factor, 0)
            expected = jnp.zeros((rows, D), F32)
            for part in range(parts):
                expected += incoming_ref[part, :, :D].astype(F32) * (factor[part] / total)
            target = target_ref[...]
            target_logit = jnp.sum(normed_ref[...].astype(F32) * target, 1, keepdims=True)
            row_losses = weight_ref[...] * (top + jnp.log(total) - target_logit)
            loss_ref[...] = jnp.sum(row_losses, 0, keepdims=True)
            normed_grad = weight_ref[...] / total_ref[...] * (expected - target)
            restored = norm_back(normed_grad, (nh_ref[...], ih_ref[:, :1]), gain(0))
            left, right = restored[:, :HALF], restored[:, HALF:]
            hidden = branch_grads(low(-left), kept_one, c_one, one_refs)
            right = right + matmul_t(hidden, c_one[0])
            hidden = branch_grads(low(-right), kept_two, c_two, two_refs)
            left = left + matmul_t(hidden, c_two[0])
            return jnp.concatenate([left, right], 1)

        @pl.when(tile == 0)
        def _():
            start_rest(pairs, section, buffers)
            for part in rows_of(rows, step):
                arrived = from_head() if last else incoming_ref[part].astype(F32)
                second = norm_back(arrived, (n2_ref[part], i2_ref[part, :1]), gain(4))
                summed[part] = second
                second_low[part] = low(second)
            hidden_low[...] = branch_grads(
                second_low[...],
                (lin_ref[...], act_ref[...], bslope_ref[...]),
                [ref[...] for ref in a_refs],
                grad_refs,
            )
            for part in rows_of(rows, step):
                total = summed[part] + matmul_t(hidden_low[part], a_refs[0][...])
                summed[part] = total
                summed_low[part] = low(total)
                acc[part] = total
            if packed:
                pack()

        wait_tile(pairs, buffers, tile)
        for part in rows_of(rows, step):
            inner = matmul_t(summed_low[part], buffers[2][tile])
            inner = low(inner * slope_ref[part].astype(F32))
            acc[part] += matmul_t(inner, buffers[1][tile])

        @pl.when(tile == TILES - 1)
        def _():
            wait_out(pairs, buffers)
            for part in rows_of(rows, step):
                start = norm_back(acc[part], (n1_ref[part], i1_ref[part, :1]), gain(2))
                start_ref[part] = start
                mixed_ref[part] = low(matmul_t(low(start), buffers[0][...]))

    out_shape = [shape_of(rows, D), shape_of(rows, D, kind=BF16)]
    if packed:
        chunks = shape_of(COUPLING_GROUPS, PART_ROWS, LANES, kind=BF16)
        out_shape += [shape_of(1, BOT), shape_of(1, D)] + [chunks] * (1 if last else 2)
    else:
        out_shape += [shape_of(*dims) for dims in ADAPTER_GRADS]
    if last:
        out_shape += [shape_of(1, 1)] + [shape_of(*dims) for dims in COUPLING_GRADS] * 2
    n_outs = len(out_shape)
    in_specs = [whole(value.shape) for value in (incoming, *kept, norms, *adapter, *extra_in)]
    in_specs[3] = pl.BlockSpec((rows, TILE), lambda j: (0, j))
    return pl.pallas_call(
        kernel,
        grid=(TILES,),
        in_specs=in_specs + hbm(6),
        out_specs=[whole(out.shape) for out in out_shape],
        out_shape=out_shape,
        scratch_shapes=[
            pltpu.VMEM((rows, D), F32),
            pltpu.VMEM((rows, D), BF16),
            pltpu.VMEM((rows, D), F32),
            pltpu.VMEM((rows, D), BF16),
            pltpu.VMEM((rows, BOT), BF16),
        ]
        + rest_buffers()
        + ([pltpu.VMEM((D, BOT), F32), pltpu.VMEM((BOT, D), F32)] if packed else []),
        compiler_params=params_for(58),
        name="last_rows_backward" if last else "first_layer_rest_backward",
    )(incoming, *kept, norms, *adapter, *extra_in, *[w for pair in w_rest for w in pair])


def spots_backward(kept, mixed_grad, start_grad, chosen_t, w_qkv, length):
    query, key, value, lse = kept

    def kernel(length_ref, q_ref, k_ref, v_ref, lse_ref, mixed_ref, start_ref, chosen_ref, *refs):
        w_pair = refs[:2]
        out_ref, acc, spot, w_buf, sems = refs[2:]
        group = pl.program_id(0)

        @pl.when(group == 0)
        def _():
            for g in range(GROUPS):
                for part in range(3):
                    start_copy(w_pair, 1, qkv_window(g, part), w_buf.at[g, part], sems.at[g, part])
            spot[...] = start_ref[...]
            acc[...] = jnp.zeros_like(acc)

        stack = lambda values: jnp.concatenate([only_head(values, h) for h in range(HEADS_IN)], 0)
        query = stack(scaled_query(q_ref[...]))
        mixed = stack(mixed_ref[...])
        key, value = k_ref[...], v_ref[...]
        scores = matmul_t(query, key) + key_bias(length_ref[0], (1, SEQ), 1)
        soft = jnp.exp(scores - lse_ref[:, :1])
        soft_grad = matmul_t(mixed, value)
        delta = jnp.sum(soft_grad * soft, 1, keepdims=True)
        score_grad = low(soft * (soft_grad - delta))
        every = matmul(score_grad, key)
        query_grad = every[:COUNT]
        for head in range(1, HEADS_IN):
            query_grad = jnp.where(
                head_mask(query_grad, head), every[head * COUNT : (head + 1) * COUNT], query_grad
            )
        query_grad = low(query_grad * HEAD_DIM**-0.5)
        key_grad = low(inner_rows(score_grad, query))
        value_grad = low(inner_rows(low(soft), mixed))
        for part in range(3):
            wait_copy(w_pair, qkv_window(group, part), w_buf.at[group, part], sems.at[group, part])
        spot[...] += matmul_t(query_grad, w_buf[group, 0])
        acc[...] += matmul_t(key_grad, w_buf[group, 1]) + matmul_t(value_grad, w_buf[group, 2])

        @pl.when(group == GROUPS - 1)
        def _():
            placed = jnp.dot(
                chosen_ref[...], spot[...], precision=HIGHEST, preferred_element_type=F32
            )
            out_ref[...] = low(acc[...] + placed)

    narrow = pl.BlockSpec((COUNT, GROUP), lambda g: (0, g))
    column = pl.BlockSpec((SEQ, GROUP), lambda g: (0, g))
    return pl.pallas_call(
        kernel,
        grid=(GROUPS,),
        in_specs=[pl.BlockSpec(memory_space=pltpu.SMEM), narrow, column, column]
        + [pl.BlockSpec((None, HEADS_IN * COUNT, LANES), lambda g: (g, 0, 0)), narrow]
        + [whole((COUNT, D)), whole((SEQ, COUNT))]
        + hbm(2),
        out_specs=whole((SEQ, D)),
        out_shape=shape_of(SEQ, D, kind=BF16),
        scratch_shapes=[
            pltpu.VMEM((SEQ, D), F32),
            pltpu.VMEM((COUNT, D), F32),
            pltpu.VMEM((GROUPS, 3, D, GROUP), BF16),
            pltpu.SemaphoreType.DMA((GROUPS, 3)),
        ],
        compiler_params=params_for(40),
        name="second_layer_attention_backward",
    )(length, query, key, value, lse, mixed_grad, start_grad, chosen_t, *w_qkv)


def first_backward(kept, mixed_grad, start_grad, kept_coupling, coupling, head_grads, w_qkv, length, biases=()):
    query, key, value, lse = kept

    def kernel(length_ref, q_ref, k_ref, v_ref, lse_ref, mixed_ref, start_ref, *refs):
        kept_refs, c_refs, h_refs, refs = refs[:6], refs[6:14], refs[14:22], refs[22:]
        b_refs, w_pair, refs = refs[: len(biases)], refs[len(biases) : len(biases) + 2], refs[len(biases) + 2 :]
        out_refs, refs = refs[: len(out_shape)], refs[len(out_shape) :]
        acc, s_buf, d_buf, p_low, ds_low, w_buf, sems = refs[:7]
        if biases:
            chunk_refs, out_refs = out_refs, refs[7:]
        group = pl.program_id(0)

        @pl.when(group == 0)
        def _():
            for g in range(GROUPS):
                for part in range(3):
                    start_copy(w_pair, 0, qkv_window(g, part), w_buf.at[g, part], sems.at[g, part])
            acc[...] = start_ref[...]

        query = scaled_query(q_ref[...])
        key, value, mixed = k_ref[...], v_ref[...], mixed_ref[...]
        key_t = jnp.transpose(key)
        key_grad = jnp.zeros((SEQ, GROUP), F32)
        value_grad = jnp.zeros((SEQ, GROUP), F32)
        query_parts = []
        for head in range(HEADS_IN):
            slot = head % 2
            s_buf[slot] = matmul_t(only_head(key, head), query)
            d_buf[slot] = matmul_t(only_head(value, head), mixed)
            lse_row = lse_ref[head : head + 1]
            delta = jnp.zeros((8, SEQ), F32)
            for rows in rows_of(SEQ, 32):
                valid = lax.broadcasted_iota(jnp.int32, (32, 1), 0) + rows.start < length_ref[0]
                bias = jnp.where(valid, 0.0, -1e30)
                soft = jnp.exp(s_buf[slot, rows] + bias - lse_row)
                s_buf[slot, rows] = soft
                p_low[slot, rows] = low(soft)
                product = soft * d_buf[slot, rows]
                for at in range(0, 32, 8):
                    delta = delta + product[at : at + 8]
            delta = jnp.sum(delta, 0, keepdims=True)
            for rows in rows_of(SEQ, 32):
                ds_low[slot, rows] = low(s_buf[slot, rows] * (d_buf[slot, rows] - delta))
            value_grad += matmul(p_low[slot], only_head(mixed, head))
            key_grad += matmul(ds_low[slot], only_head(query, head))
            query_parts.append(matmul(key_t[head * HEAD_DIM : (head + 1) * HEAD_DIM], ds_low[slot]))
        query_grad = jnp.transpose(jnp.concatenate(query_parts, 0)) * HEAD_DIM**-0.5
        for part, grad in enumerate((query_grad, key_grad, value_grad)):
            wait_copy(w_pair, qkv_window(group, part), w_buf.at[group, part], sems.at[group, part])
            acc[...] += matmul_t(low(grad), w_buf[group, part])

        @pl.when(group == GROUPS - 1)
        def _():
            c_one, c_two = ([ref[...] for ref in c_refs[at : at + 4]] for at in (0, 4))
            kept_one, kept_two = ([ref[...] for ref in kept_refs[at : at + 3]] for at in (0, 3))
            hidden = branch_grads(low(acc[:, HALF:]), kept_two, c_two, out_refs[4:])
            left = acc[:, :HALF] + matmul_t(hidden, c_two[0])
            branch_grads(low(left), kept_one, c_one, out_refs[:4])
            for out_ref, ref in zip(out_refs, h_refs):
                out_ref[...] += ref[...]
            if not biases:
                return
            here = lax.axis_index("section")
            for s in range(MICRO):
                one = out_refs[4 * s : 4 * s + 4]
                tiles = bias_tiles(b_refs[2 * s][...], b_refs[2 * s + 1][...], one[1][...], one[3][...])

                def store(part, chunk, s=s):
                    @pl.when(here == s)
                    def _():
                        chunk_refs[0][part] = chunk

                    @pl.when(here != s)
                    def _():
                        chunk_refs[1][part] = low(chunk)

                pack_coupling((one[0], one[2]), tiles, sum(BIASES) // COUPLING_GROUPS, store)

    column = pl.BlockSpec((SEQ, GROUP), lambda g: (0, g))
    out_shape = [shape_of(*dims) for dims in COUPLING_GRADS] * 2
    grad_buffers = []
    if biases:
        grad_buffers = [pltpu.VMEM(dims, F32) for dims in COUPLING_GRADS] * 2
        dims = (COUPLING_GROUPS, GROUP_ROWS + 8, LANES)
        out_shape = [shape_of(*dims), shape_of(*dims, kind=BF16)]
    return pl.pallas_call(
        kernel,
        grid=(GROUPS,),
        in_specs=[pl.BlockSpec(memory_space=pltpu.SMEM), column, column, column]
        + [pl.BlockSpec((None, 8, SEQ), lambda g: (g, 0, 0)), column, whole((SEQ, D))]
        + [whole(value.shape) for value in (*kept_coupling, *coupling, *head_grads, *biases)]
        + hbm(2),
        out_specs=[whole(out.shape) for out in out_shape],
        out_shape=out_shape,
        scratch_shapes=[
            pltpu.VMEM((SEQ, D), F32),
            pltpu.VMEM((2, SEQ, SEQ), F32),
            pltpu.VMEM((2, SEQ, SEQ), F32),
            pltpu.VMEM((2, SEQ, SEQ), BF16),
            pltpu.VMEM((2, SEQ, SEQ), BF16),
            pltpu.VMEM((GROUPS, 3, D, GROUP), BF16),
            pltpu.SemaphoreType.DMA((GROUPS, 3)),
        ]
        + grad_buffers,
        compiler_params=params_for(56),
        name="first_layer_attention_backward",
    )(length, query, key, value, lse, mixed_grad, start_grad, *kept_coupling, *coupling, *head_grads, *biases, *w_qkv)


VOCAB_TILE = 1280


def head_kernel(rows, table):
    count, vocab = rows.shape[0], table.shape[0]
    steps = pl.cdiv(vocab, VOCAB_TILE)
    half = count // 2

    def kernel(x_ref, table_ref, out_ref, acc, top, total, l_buf, p_buf):
        tile = pl.program_id(0)

        @pl.when(tile == 0)
        def _():
            acc[...] = jnp.zeros_like(acc)
            top[...] = jnp.full_like(top, -1e30)
            total[...] = jnp.zeros_like(total)

        left = vocab - tile * VOCAB_TILE
        row = lax.broadcasted_iota(jnp.int32, (VOCAB_TILE, 1), 0)
        entries = jnp.where(row < left, table_ref[...], jnp.zeros_like(table_ref))
        bias = key_bias(left, (1, VOCAB_TILE), 1)
        for i in range(2):
            part = slice(i * half, (i + 1) * half)
            l_buf[i] = matmul_t(x_ref[part], entries)
            for small in rows_of(half, 32):
                at = slice(part.start + small.start, part.start + small.stop)
                logits = l_buf[i, small] + bias
                earlier = top[at]
                highest = jnp.maximum(earlier, jnp.max(logits, 1, keepdims=True))
                exponent = jnp.exp(logits - highest)
                factor = jnp.exp(earlier - highest)
                top[at] = highest
                total[at] = total[at] * factor + jnp.sum(exponent, 1, keepdims=True)
                p_buf[i, small] = low(exponent)
                acc[at] = acc[at] * factor
            acc[part] += matmul(p_buf[i], entries)

        @pl.when(tile == steps - 1)
        def _():
            lane = lax.broadcasted_iota(jnp.int32, (count, LANES), 1)
            stats = jnp.zeros((count, LANES), F32)
            pieces = three_low(top[...]) + three_low(total[...])
            for j, piece in enumerate(pieces):
                stats = jnp.where(lane == j, piece.astype(F32), stats)
            out_ref[:, :D] = low(acc[...])
            out_ref[:, D:] = low(stats)

    return pl.pallas_call(
        kernel,
        grid=(steps,),
        in_specs=[whole((count, D)), pl.BlockSpec((VOCAB_TILE, D), lambda j: (j, 0))],
        out_specs=whole((count, D + LANES)),
        out_shape=shape_of(count, D + LANES, kind=BF16),
        scratch_shapes=[
            pltpu.VMEM((count, D), F32),
            pltpu.VMEM((count, 1), F32),
            pltpu.VMEM((count, 1), F32),
            pltpu.VMEM((2, half, VOCAB_TILE), F32),
            pltpu.VMEM((2, half, VOCAB_TILE), BF16),
        ],
        compiler_params=params_for(48),
        name="vocabulary_head",
    )(rows, table)


def swap_add(own, other):
    came = lax.ppermute(low(other), "section", [(0, 1), (1, 0)])
    return own + came.astype(F32)


def pick(first_section, both):
    return jnp.where(first_section, both[0], both[1])


def plan_requests(ids, vocab_rows, slots):
    earlier = jnp.arange(IDS)[None, :] < jnp.arange(IDS)[:, None]
    same_id = ids[:, :, None] == ids[:, None, :]
    first = jnp.logical_not(jnp.any(same_id & earlier, -1))
    owner = ids // vocab_rows
    same_owner = owner[:, :, None] == owner[:, None, :]
    rank = jnp.sum((same_owner & earlier & first[:, None, :]).astype(jnp.int32), -1)
    slot = jnp.sum(jnp.where(same_id & first[:, None, :], rank[:, None, :], 0), -1)
    rounds = jnp.max(rank) // slots + 1
    return owner, slot, first, rounds


def fetch_rows(table, ids, first_section, weight_part, slots):
    parts = lax.axis_size("dp")
    vocab_rows = table.shape[0]
    owner, slot, first, rounds = plan_requests(ids, vocab_rows, slots)
    ids, owner, slot, first = (pick(first_section, both) for both in (ids, owner, slot, first))
    local = ids - owner * vocab_rows

    def places(turn):
        here = slot - turn * slots
        spot = jnp.where((here >= 0) & (here < slots), owner * slots + here, -1)
        return spot[:, None] == jnp.arange(parts * slots)[None, :]

    def wanted(hits):
        return jnp.sum(jnp.where(hits & first[:, None], local[:, None], 0), 0).reshape(parts, slots)

    def answer(asked, hits):
        rows = table.at[asked.reshape(-1)].get(mode="promise_in_bounds").reshape(parts, slots, D)
        came = lax.all_to_all(rows, "dp", 0, 0).reshape(parts * slots, D)
        return matmul(hits.astype(BF16), came)

    hits = places(0)
    extra = jnp.broadcast_to(jnp.stack([rounds, weight_part])[None], (parts, 2))
    asked = lax.all_to_all(jnp.concatenate([wanted(hits), extra], 1), "dp", 0, 0)
    total_rounds = jnp.max(asked[:, slots])
    weight_sum = jnp.sum(asked[:, slots + 1])
    rows = answer(asked[:, :slots], hits)

    def more(state):
        return state[0] < total_rounds

    def another(state):
        turn, rows = state
        hits = places(turn)
        asked = lax.all_to_all(wanted(hits), "dp", 0, 0)
        return turn + 1, rows + answer(asked, hits)

    return lax.while_loop(more, another, (jnp.int32(1), rows))[1], weight_sum.astype(F32)


def three_low(values):
    high = low(values)
    rest = values - high.astype(F32)
    middle = low(rest)
    return [high, middle, low(rest - middle.astype(F32))]


def in_groups(count):
    return lax.axis_size("dp") == COUPLING_GROUPS and count == 4 * PART_GROUPS


def gather_params(master, vector):
    parts = lax.axis_size("dp")
    count, width = master.shape[0], vector.shape[0]
    if in_groups(count):
        packed = pack_own(master, vector[None])
        gathered = lax.all_gather(packed, ("section", "dp")).reshape(MICRO, parts, -1, LANES)
        arrays = unpack_all(gathered, width)
        params = []
        for s in range(MICRO):
            down, up, c_down, c_up, first, second, third, fourth = (array[s] for array in arrays)
            params.append(((down, first, up, second), (c_down, third, c_up, fourth)))
        return [pair[0] for pair in params], params[0][1], params[1][1]
    flat = low(jnp.concatenate([master.reshape(-1), vector]))
    gathered = lax.all_gather(flat, ("section", "dp")).reshape(MICRO, parts, -1)
    size = count * BLOCK**2
    all_blocks = gathered[:, :, :size].reshape(MICRO, parts * count, BLOCK, BLOCK)
    all_vectors = gathered[:, :, size:].reshape(MICRO, parts * width)
    params = [split_params(all_blocks[s], all_vectors[s]) for s in range(MICRO)]
    as_rows = lambda p: (p[0], p[1].astype(F32)[None], p[2], p[3].astype(F32)[None])
    return [as_rows(pair[0]) for pair in params], as_rows(params[0][1]), as_rows(params[1][1])


def sum_at_owners(grads, loss_part, count):
    parts = lax.axis_size("dp")
    width = sum(BIASES) // parts
    flat = []
    for adapter, coupling in grads:
        blocks, vector = join_params(adapter, coupling)
        flat.append(
            jnp.concatenate([blocks.reshape(parts, count * BLOCK**2), vector.reshape(parts, width)], 1)
        )
    first = lax.axis_index("section") == 0
    summed = swap_add(jnp.where(first, flat[0], flat[1]), jnp.where(first, flat[1], flat[0]))
    owned = jnp.sum(lax.all_to_all(low(summed), "dp", 0, 0).astype(F32), 0)
    blocks = owned[: count * BLOCK**2].reshape(count, BLOCK, BLOCK)
    pair = jnp.stack([jnp.sum(owned * owned), loss_part[0, 0]])
    pair = jnp.pad(pair, (0, LANES - 2))[None, None]
    return blocks, owned[count * BLOCK**2 :], jnp.broadcast_to(pair, (parts * MICRO, 1, LANES))


def to_coupling_owners(group):
    arrived = []
    for place in range(PART_GROUPS):
        route = []
        for part in range(COUPLING_GROUPS):
            owner, at = divmod(ADAPTER_GROUPS + part, PART_GROUPS)
            if at == place:
                route.append((part, owner))
        arrived.append(lax.ppermute(group, "dp", route))
    return arrived


def exact(spec, left, right):
    return jnp.einsum(spec, left, right, precision=HIGHEST)


def update(pair, grad, grad_vector, state):
    master, momentum, stat_left, stat_right, root_left, root_right, vectors, vec_first, vec_second = state
    left_square = exact("nij,nkj->nik", grad, grad)
    right_square = exact("nji,njk->nik", grad, grad)
    turned = exact("nij,njk->nik", exact("nij,njk->nik", root_left, grad), root_right)
    turned_old = exact("nij,njk->nik", exact("nij,njk->nik", root_left, momentum), root_right)

    def kernel(pair_ref, grad_ref, left_ref, right_ref, turned_ref, old_ref, vector_ref, *refs):
        master_ref, momentum_ref, stat_left_ref, stat_right_ref, vectors_ref, first_ref, second_ref = refs[:7]
        outs = refs[7:]
        totals = jnp.sum(pair_ref[...], 0)
        norm = jnp.sqrt(totals[:, :1])
        factor = CLIP_NORM / jnp.maximum(norm, CLIP_NORM)
        outs[9][...] = norm
        outs[10][...] = totals[:, 1:2]
        for n in range(grad_ref.shape[0]):
            clipped = grad_ref[n] * factor
            outs[0][0, n] = clipped
            outs[1][0, n] = FIRST_DECAY * momentum_ref[n] + (1.0 - FIRST_DECAY) * clipped
            square = (1.0 - STAT_DECAY) * factor * factor
            outs[2][0, n] = STAT_DECAY * stat_left_ref[n] + square * left_ref[n]
            outs[3][0, n] = STAT_DECAY * stat_right_ref[n] + square * right_ref[n]
            direction = FIRST_DECAY * old_ref[n] + (1.0 - FIRST_DECAY) * factor * turned_ref[n]
            master_new = master_ref[n] - MAT_RATE * (direction + MAT_DECAY * master_ref[n])
            outs[4][0, n] = master_new
            outs[5][0, n] = low(master_new)
        clipped = vector_ref[...] * factor
        first_new = FIRST_DECAY * first_ref[...] + (1.0 - FIRST_DECAY) * clipped
        second_new = VEC_SECOND * second_ref[...] + (1.0 - VEC_SECOND) * clipped * clipped
        outs[6][...] = first_new
        outs[7][...] = second_new
        corrected_first = first_new / (1.0 - FIRST_DECAY**STEP)
        corrected_second = second_new / (1.0 - VEC_SECOND**STEP)
        outs[8][...] = vectors_ref[...] - VEC_RATE * (
            corrected_first / (jnp.sqrt(corrected_second) + VEC_EPS) + VEC_DECAY * vectors_ref[...]
        )

    blocks = (1,) + grad.shape
    width = vectors.shape
    shapes = [shape_of(*blocks)] * 5 + [shape_of(*blocks, kind=BF16)] + [shape_of(*width)] * 3
    return pl.pallas_call(
        kernel,
        out_shape=shapes + [shape_of(1, 1)] * 2,
        compiler_params=params_for(40),
        name="update",
    )(
        pair, grad, left_square, right_square, turned, turned_old, grad_vector,
        master, momentum, stat_left, stat_right, vectors, vec_first, vec_second,
    )


def shards(
    token_ids,
    lengths,
    positions,
    targets,
    loss_weights,
    embed_table,
    pos_table,
    norm_params,
    base_qkv,
    base_out,
    base_up,
    base_down,
    master,
    momentum,
    stat_left,
    stat_right,
    root_left,
    root_right,
    vectors,
    vec_first,
    vec_second,
):
    parts = lax.axis_size("dp")
    first_section = lax.axis_index("section") == 0
    slots = -(-IDS * 5 // (4 * parts * 16)) * 16

    adapters, coupling_one, coupling_two = gather_params(master[0], vectors[0])
    coupling = (*coupling_one, *coupling_two)
    swapped = [lax.ppermute(w, "section", [(0, 1), (1, 0)]) for w in (base_qkv, base_out, base_up, base_down)]
    pairs = list(zip((base_qkv, base_out, base_up, base_down), swapped))
    w_qkv, w_rest = pairs[0], pairs[1:]
    came = lax.ppermute(norm_params, "section", [(0, 1), (1, 0)])
    norms = jnp.concatenate([pick(first_section, (norm_params, came)), pick(first_section, (came, norm_params))])

    ids = jnp.concatenate([token_ids[:, 0], targets[:, 0]], -1)
    weight_part = jnp.sum(loss_weights)
    fetched, weight_sum = fetch_rows(embed_table, ids, first_section, weight_part, slots)
    length = pick(first_section, lengths)
    spots = pick(first_section, positions[:, 0])
    row_weights = pick(first_section, loss_weights[:, 0]).astype(F32)[:, None]
    chosen = (spots[:, None] == jnp.arange(SEQ)[None, :]).astype(BF16)
    chosen_t = (spots[None, :] == jnp.arange(SEQ)[:, None]).astype(F32)

    hidden, query, key, value, mixed, lse, *kept_coupling = first_kernel(
        fetched, pos_table, norms, coupling, w_qkv, length
    )
    section_out, *kept = rest_forward(0, hidden, mixed, norms, adapters[0], w_rest)
    at_spots, query_1, key_1, value_1, mixed_1, lse_1 = spots_kernel(section_out, chosen, w_qkv, length)
    normed, *kept_1 = rest_forward(1, at_spots, mixed_1, norms, adapters[1], w_rest, coupling)

    rows = jnp.broadcast_to(normed[None], (parts, COUNT, D))
    rows = lax.all_to_all(rows, "dp", 0, 0).reshape(parts * COUNT, D)
    merged = head_kernel(rows, embed_table).reshape(parts, COUNT, D + LANES)
    merged = lax.all_to_all(merged, "dp", 0, 0)

    head = (kept_1[8:], coupling, normed, fetched[SEQ:], row_weights, weight_sum.reshape(1, 1))
    packed = in_groups(master.shape[1])
    start_grad, mixed_grad, *grads = rest_backward(
        1, merged, kept_1[:8], norms, adapters[1], w_rest, head, packed
    )
    adapter_grads_1, loss_part, head_grads = grads[:-9], grads[-9], grads[-8:]
    section_grad = spots_backward(
        (query_1, key_1, value_1, lse_1), mixed_grad, start_grad, chosen_t, w_qkv, length
    )
    start_grad, mixed_grad, *adapter_grads_0 = rest_backward(
        0, section_grad, kept, norms, adapters[0], w_rest, None, packed, adapter_grads_1[2] if packed else None
    )
    last = functools.partial(
        first_backward,
        (query, key, value, lse), mixed_grad, start_grad, kept_coupling, coupling, head_grads, w_qkv, length,
    )
    if packed:
        own, other = adapter_grads_0[2:]
        adapter_came = lax.all_to_all(low(swap_add(own.astype(F32), other)), "dp", 0, 0)
        own, other = last((*adapter_grads_0[:2], *adapter_grads_1[:2]))
        adapter_total, squares = sum_adapter(adapter_came)
        came = lax.all_to_all(low(swap_add(own, other)), "dp", 0, 0)
        group, bias, pair = sum_coupling(came, squares, loss_part, parts * MICRO)
        grad = own_blocks_of(adapter_total, to_coupling_owners(group))
        grad_vector = bias[:1, : vectors.shape[1]]
    else:
        grads = last()
        grad, grad_vector, pair = sum_at_owners(
            ((adapter_grads_0, grads[:4]), (adapter_grads_1, grads[4:])), loss_part, master.shape[1]
        )
        grad_vector = grad_vector[None]
    pair = lax.all_to_all(pair, ("dp", "section"), 0, 0)
    state = (master, momentum, stat_left, stat_right, root_left, root_right)
    *outs, grad_norm, loss_sum = update(
        pair, grad, grad_vector, [value[0] for value in state] + [vectors, vec_first, vec_second]
    )
    return (*outs, grad_norm[0, 0], loss_sum[0, 0], weight_sum)


def solution(mesh):
    rows = P(None, "dp", None)
    section = P("section", None, None)
    blocks = P("section", "dp", None, None)
    biases = P("section", "dp")
    return jax.shard_map(
        shards,
        mesh=mesh,
        in_specs=(rows, P(None, "dp"), rows, rows, rows, P("dp", None), P())
        + (section,) * 5
        + (blocks,) * 6
        + (biases,) * 3,
        out_specs=(blocks,) * 6 + (biases,) * 3 + (P(),) * 3,
        check_vma=False,
    )
```

```python
import functools

import jax
import jax.numpy as jnp
import numpy as np
from jax import lax
from jax.experimental import pallas as pl
from jax.experimental.pallas import tpu as pltpu
from jax.sharding import PartitionSpec as P

D = 768
HEADS = 12
HEAD_DIM = 64
BOT = 384
INV_H = 192
SEQ = 512
COUNT = 32
MICRO = 2
BLOCK = 48
STEP = 10
HALF = 384
IDS = SEQ + COUNT

HIGHEST = lax.Precision.HIGHEST
NORM_EPS = 1e-12
CLIP_NORM = 0.02
FIRST_DECAY = 0.9
STAT_DECAY = 0.99
MAT_RATE = 0.1
MAT_DECAY = 0.01
VEC_RATE = 0.05
VEC_SECOND = 0.999
VEC_EPS = 1e-08
VEC_DECAY = 0.01
F32 = jnp.float32
BF16 = jnp.bfloat16

CDF_SCALE = 0.42 / 2.0**0.5
CDF_POLY = (
    0.2368242366796694,
    0.239585811361218,
    0.1947261443420679,
    0.2687426685879861,
    -0.13052645834187002,
    0.4406726942003943,
    -0.32025628294963193,
    0.07023101752398136,
)


def matmul(left, right):
    return jnp.dot(left, right, preferred_element_type=F32)


def matmul_t(left, right):
    return lax.dot_general(left, right, (((1,), (1,)), ((), ())), preferred_element_type=F32)


def inner_rows(left, right):
    return lax.dot_general(left, right, (((0,), (0,)), ((), ())), preferred_element_type=F32)


def low(values):
    return values.astype(BF16)


def gelu_both(values):
    below = 1.0 + CDF_SCALE * jnp.abs(values)
    ratio = pl.reciprocal(below, approx=True)
    ratio = ratio * (2.0 - below * ratio)
    poly = jnp.full_like(ratio, 0.5 * CDF_POLY[-1])
    for factor in CDF_POLY[-2::-1]:
        poly = poly * ratio + 0.5 * factor
    bell = jnp.exp(-0.5 * values * values)
    tail = bell * (poly * ratio)
    cdf = jnp.where(values < 0, tail, 1.0 - tail)
    return values * cdf, cdf + values * (bell * (2.0 * np.pi) ** -0.5)


def layer_norm(values, gain, shift):
    centered = values - jnp.mean(values, -1, keepdims=True)
    inverse = lax.rsqrt(jnp.mean(centered * centered, -1, keepdims=True) + NORM_EPS)
    normal = centered * inverse
    return normal * gain + shift, (normal, inverse)


def norm_back(incoming, kept, gain):
    normal, inverse = kept
    scaled = incoming * gain
    return inverse * (
        scaled
        - jnp.mean(scaled, -1, keepdims=True)
        - normal * jnp.mean(scaled * normal, -1, keepdims=True)
    )


def to_blocks(matrix):
    rows_in, cols_in = matrix.shape
    return (
        matrix.reshape(rows_in // BLOCK, BLOCK, cols_in // BLOCK, BLOCK)
        .transpose(0, 2, 1, 3)
        .reshape(-1, BLOCK, BLOCK)
    )


def from_blocks(blocks, rows_in, cols_in):
    return (
        blocks.reshape(rows_in // BLOCK, cols_in // BLOCK, BLOCK, BLOCK)
        .transpose(0, 2, 1, 3)
        .reshape(rows_in, cols_in)
    )


def split_params(blocks, vector):
    adapter_count = D * BOT // BLOCK**2
    half_count = HALF * INV_H // BLOCK**2
    split_at = 2 * adapter_count
    adapter = (
        from_blocks(blocks[:adapter_count], D, BOT),
        vector[:BOT],
        from_blocks(blocks[adapter_count:split_at], BOT, D),
        vector[BOT : BOT + D],
    )
    coupling = (
        from_blocks(blocks[split_at : split_at + half_count], HALF, INV_H),
        vector[BOT + D : BOT + D + INV_H],
        from_blocks(blocks[split_at + half_count :], INV_H, HALF),
        vector[BOT + D + INV_H :],
    )
    return adapter, coupling


def join_params(adapter, coupling):
    blocks = jnp.concatenate(
        [to_blocks(adapter[0]), to_blocks(adapter[2]), to_blocks(coupling[0]), to_blocks(coupling[2])]
    )
    return blocks, jnp.concatenate([adapter[1], adapter[3], coupling[1], coupling[3]], 1)[0]


GROUP_ROWS = 72
LANES = 128


def whole(*_):
    return pl.BlockSpec(memory_space=pltpu.VMEM)


def params_for(mebibytes):
    return pltpu.CompilerParams(vmem_limit_bytes=mebibytes * 2**20)


def roll(values, shift):
    return pltpu.roll(values, shift, 1)


def lane_of(values):
    return lax.broadcasted_iota(jnp.int32, values.shape, 1)


def fold_half(values, upper):
    top, bottom = values[:24], values[24:]
    if upper:
        return jnp.where(lane_of(top) < 64, roll(top, 64), bottom)
    return jnp.where(lane_of(top) < 64, top, roll(bottom, 64))


def unfold_half(values, upper):
    turned = roll(values, 64)
    return jnp.concatenate([turned, values] if upper else [values, turned], 0)


def join_pair(main_0, rest_0, main_1, rest_1):
    left = lane_of(main_0) < 64
    turned = roll(main_1, 64)
    return (
        main_0,
        jnp.where(left, unfold_half(rest_0, False), turned),
        jnp.where(left, turned, unfold_half(rest_1, True)),
    )


def cut_pair(tile_0, tile_1, tile_2):
    left = lane_of(tile_0) < 64
    return (
        (tile_0, fold_half(tile_1, False)),
        (jnp.where(left, roll(tile_1, 64), roll(tile_2, 64)), fold_half(tile_2, True)),
    )


def chunk_rows(own_blocks):
    return own_blocks // 4 * GROUP_ROWS + 8


def bias_row(tiles, part, width):
    at, shift = divmod(part * width, LANES)
    lane = lane_of(tiles[0])
    row = tiles[at]
    if shift:
        row = jnp.where(lane < LANES - shift, roll(row, LANES - shift), roll(tiles[at + 1], LANES - shift))
    return jnp.where(lane < width, row, 0.0)


def bias_tiles(first, second, third, fourth):
    cut = lambda values: [values[:, at : at + LANES] for at in range(0, values.shape[1], LANES)]
    zero = jnp.zeros((1, LANES), F32)
    left = lane_of(zero) < 64
    third_tail = jnp.concatenate([third[:, LANES:]] * 2, 1)
    turned = [roll(tile, 64) for tile in cut(fourth)]
    joints = [jnp.where(left, one, two) for one, two in zip([third_tail] + turned, turned + [zero])]
    return cut(first) + cut(second) + [third[:, :LANES]] + joints + [zero]


def tiles_of_rows(rows, width):
    tiles = []
    for tile in range(-(-len(rows) * width // LANES)):
        value = jnp.zeros((8, LANES), F32)
        lane = lane_of(value)
        for part, row in enumerate(rows):
            shift = part * width - tile * LANES
            if shift >= LANES or shift + width <= 0:
                continue
            turned = roll(row, shift % LANES) if shift % LANES else row
            value = jnp.where((lane >= shift) & (lane < shift + width), turned, value)
        tiles.append(value)
    return tiles


def pack_own(master, vector):
    count, width = master.shape[0], vector.shape[1]

    def kernel(master_ref, bias_ref, out_ref):
        row = lax.broadcasted_iota(jnp.int32, (BLOCK, 256), 0)
        col = lax.broadcasted_iota(jnp.int32, (BLOCK, 256), 1)
        pieces = []
        for group in range(count // 4):
            wide = jnp.zeros((BLOCK, 256), F32)
            for j in range(4):
                wide += matmul(low(master_ref[4 * group + j]), (col == row + BLOCK * j).astype(BF16))
            pieces += [wide[:, :LANES], fold_half(wide[:, LANES:], False)]
        bias = jnp.concatenate([bias_ref[...], jnp.zeros((1, LANES - width), F32)], 1)
        pieces.append(jnp.concatenate([bias, jnp.zeros((7, LANES), F32)], 0))
        out_ref[...] = low(jnp.concatenate(pieces, 0))

    return pl.pallas_call(
        kernel,
        out_shape=jax.ShapeDtypeStruct((chunk_rows(count), LANES), BF16),
        name="pack_own",
    )(master, vector)


MATRICES = ((D, BOT), (BOT, D), (HALF, INV_H), (INV_H, HALF))
BIASES = (BOT, D, INV_H, HALF)


def unpack_all(gathered, width):
    sections, parts, rows, _ = gathered.shape
    per_part = (rows - 8) // GROUP_ROWS

    def kernel(in_ref, *out_refs):
        cache = {}

        def group(index):
            part = index // per_part
            if part not in cache:
                cache.clear()
                cache[part] = in_ref[part].astype(F32)
            base = index % per_part * GROUP_ROWS
            chunk = cache[part]
            return chunk[base : base + BLOCK], chunk[base + BLOCK : base + GROUP_ROWS]

        index = 0
        for (height, columns), out_ref in zip(MATRICES, out_refs):
            for top in range(0, height, BLOCK):
                if columns == INV_H:
                    main, rest = group(index)
                    index += 1
                    out_ref[top : top + BLOCK, :LANES] = low(main)
                    out_ref[top : top + BLOCK, LANES:] = low(unfold_half(rest, False)[:, :64])
                    continue
                for left in range(0, columns, HALF):
                    tiles = join_pair(*group(index), *group(index + 1))
                    index += 2
                    for j, tile in enumerate(tiles):
                        at = left + j * LANES
                        out_ref[top : top + BLOCK, at : at + LANES] = low(tile)
        tiles = tiles_of_rows([in_ref[part, rows - 16 :].astype(F32)[8:] for part in range(parts)], width)
        first, second, third, fourth = out_refs[4:]
        first[...] = jnp.concatenate(tiles[:3], 1)[:1]
        second[...] = jnp.concatenate(tiles[3:9], 1)[:1]
        third[...] = jnp.concatenate([tiles[9], tiles[10][:, :64]], 1)[:1]
        left = lane_of(tiles[0]) < 64
        turned = [roll(tile, 64) for tile in tiles[10:14]]
        fourth[...] = jnp.concatenate(
            [jnp.where(left, one, two) for one, two in zip(turned, turned[1:])], 1
        )[:1]

    return pl.pallas_call(
        kernel,
        grid=(sections,),
        in_specs=[pl.BlockSpec((None, parts, rows, LANES), lambda s: (s, 0, 0, 0))],
        out_specs=[pl.BlockSpec((None,) + shape, lambda s: (s, 0, 0)) for shape in MATRICES]
        + [pl.BlockSpec((None, 1, size), lambda s: (s, 0, 0)) for size in BIASES],
        out_shape=[jax.ShapeDtypeStruct((sections,) + shape, BF16) for shape in MATRICES]
        + [jax.ShapeDtypeStruct((sections, 1, size), F32) for size in BIASES],
        compiler_params=params_for(32),
        name="unpack_all",
    )(gathered)


ADAPTER_GROUPS = 2 * D * BOT // BLOCK**2 // 4
COUPLING_GROUPS = 2 * HALF * INV_H // BLOCK**2 // 4
PART_GROUPS = (ADAPTER_GROUPS + COUPLING_GROUPS) // COUPLING_GROUPS
PART_ROWS = PART_GROUPS * GROUP_ROWS


def groups_of(refs, shapes):
    groups = []
    for ref, (height, width) in zip(refs, shapes):
        for top in range(0, height, BLOCK):
            band = slice(top, top + BLOCK)
            if width == INV_H:
                tail = ref[band, LANES:]
                groups.append((ref[band, :LANES], fold_half(jnp.concatenate([tail, tail], 1), False)))
                continue
            for left in range(0, width, HALF):
                groups += cut_pair(*[ref[band, left + j * LANES : left + (j + 1) * LANES] for j in range(3)])
    return [jnp.concatenate(group, 0) for group in groups]


def pack_adapter(refs, store):
    groups = groups_of(refs, MATRICES[:2])
    empty = jnp.zeros((GROUP_ROWS, LANES), F32)
    for part in range(COUPLING_GROUPS):
        chunk = groups[part * PART_GROUPS : (part + 1) * PART_GROUPS]
        chunk += [empty] * (PART_GROUPS - len(chunk))
        store(part, low(jnp.concatenate(chunk, 0)))


def pack_coupling(refs, tiles, width, store):
    for part, group in enumerate(groups_of(refs, MATRICES[2:])):
        bias = jnp.concatenate([bias_row(tiles, part, width), jnp.zeros((7, LANES), F32)], 0)
        store(part, jnp.concatenate([group, bias], 0))


def sum_parts(came_ref):
    total = came_ref[0].astype(F32)
    for part in range(1, came_ref.shape[0]):
        total += came_ref[part].astype(F32)
    return total


def square_sum(values):
    return jnp.sum(jnp.sum(values * values, 0, keepdims=True), 1, keepdims=True)


def sum_adapter(came):
    def kernel(came_ref, total_ref, square_ref):
        total = sum_parts(came_ref)
        total_ref[...] = total
        square_ref[...] = square_sum(total)

    return pl.pallas_call(
        kernel,
        out_shape=[jax.ShapeDtypeStruct((PART_ROWS, LANES), F32), jax.ShapeDtypeStruct((1, 1), F32)],
        compiler_params=params_for(32),
        name="sum_adapter",
    )(came)


def sum_coupling(came, squares, loss_part, copies):
    def kernel(came_ref, square_ref, loss_ref, group_ref, bias_ref, pair_ref):
        total = sum_parts(came_ref)
        group_ref[...] = total[:GROUP_ROWS]
        bias_ref[...] = total[GROUP_ROWS:]
        squares = square_ref[...] + square_sum(total)
        lane = lax.broadcasted_iota(jnp.int32, (1, LANES), 1)
        pair = jnp.where(lane == 0, squares, jnp.where(lane == 1, loss_ref[...], 0.0))
        pair_ref[...] = jnp.broadcast_to(pair[None], pair_ref.shape)

    return pl.pallas_call(
        kernel,
        out_shape=[
            jax.ShapeDtypeStruct((GROUP_ROWS, LANES), F32),
            jax.ShapeDtypeStruct((8, LANES), F32),
            jax.ShapeDtypeStruct((copies, 1, LANES), F32),
        ],
        name="sum_coupling",
    )(came, squares, loss_part)


def own_blocks_of(adapter_total, coupling_groups):
    def kernel(total_ref, *refs):
        group_refs, blocks_ref = refs[:-1], refs[-1]
        for group in range(PART_GROUPS):
            total = total_ref[group * GROUP_ROWS : (group + 1) * GROUP_ROWS] + group_refs[group][...]
            main, rest = total[:BLOCK], unfold_half(total[BLOCK:], False)
            lane = lane_of(main)
            pieces = (
                main,
                roll(main, 80),
                jnp.where(lane < 32, roll(main, 32), roll(rest, 32)),
                roll(rest, 112),
            )
            for j, values in enumerate(pieces):
                blocks_ref[4 * group + j] = values[:, :BLOCK]

    return pl.pallas_call(
        kernel,
        out_shape=jax.ShapeDtypeStruct((4 * PART_GROUPS, BLOCK, BLOCK), F32),
        name="own_blocks",
    )(adapter_total, *coupling_groups)


GROUP = 256
HEADS_IN = GROUP // HEAD_DIM
GROUPS = D // GROUP
FF = 3072
TILE = 512
TILES = FF // TILE


def rows_of(count, size):
    return [slice(at, at + min(size, count)) for at in range(0, count, size)]


def hbm(count):
    return [pl.BlockSpec(memory_space=pltpu.HBM)] * count


def shape_of(*dims, kind=F32):
    return jax.ShapeDtypeStruct(dims, kind)


def start_copy(pair, section, window, target, sem):
    own, came = pair
    here = lax.axis_index("section") == section

    @pl.when(here)
    def _():
        pltpu.make_async_copy(own.at[window], target, sem).start()

    @pl.when(jnp.logical_not(here))
    def _():
        pltpu.make_async_copy(came.at[window], target, sem).start()


def wait_copy(pair, window, target, sem):
    pltpu.make_async_copy(pair[0].at[window], target, sem).wait()


def qkv_window(group, part):
    return 0, slice(None), pl.ds(part * D + group * GROUP, GROUP)


def across(values):
    return jnp.broadcast_to(values, (values.shape[0], LANES))


def group_columns(group):
    return pl.ds(pl.multiple_of(group * GROUP, GROUP), GROUP)


def tile_columns(tile):
    return pl.ds(pl.multiple_of(tile * TILE, TILE), TILE)


def head_mask(values, head):
    lane = lax.broadcasted_iota(jnp.int32, values.shape, 1)
    return (lane >= head * HEAD_DIM) & (lane < (head + 1) * HEAD_DIM)


def only_head(values, head):
    return jnp.where(head_mask(values, head), values, jnp.zeros_like(values))


def scaled_query(query):
    return low(query.astype(F32) * HEAD_DIM**-0.5)


def key_bias(length, shape, axis):
    return jnp.where(lax.broadcasted_iota(jnp.int32, shape, axis) < length, 0.0, -1e30)


def softmax_rows(scores):
    highest = jnp.max(scores, 1, keepdims=True)
    exponent = jnp.exp(scores - highest)
    total = jnp.sum(exponent, 1, keepdims=True)
    return low(exponent * (1.0 / total)), highest + jnp.log(total)


def first_kernel(fetched, pos_table, norms, coupling, w_qkv, length):
    def kernel(length_ref, fetched_ref, pos_ref, norms_ref, *refs):
        c_refs, w_pair, refs = refs[:8], refs[8:10], refs[10:]
        hidden_ref, q_ref, k_ref, v_ref, mixed_ref, lse_ref = refs[:6]
        kept_refs, (x_low, w_buf, s_buf, p_buf, lse_buf, sems) = refs[6:12], refs[12:]
        group = pl.program_id(0)
        columns = group_columns(group)

        @pl.when(group == 0)
        def _():
            for g in range(GROUPS):
                for part in range(3):
                    start_copy(w_pair, 0, qkv_window(g, part), w_buf.at[g, part], sems.at[g, part])
            for rows in rows_of(SEQ, 256):
                started, _ = layer_norm(
                    fetched_ref[rows] + pos_ref[rows].astype(F32), norms_ref[0, 0:1], norms_ref[0, 1:2]
                )
                left, right = started[:, :HALF], started[:, HALF:]
                low_one = low(right)
                active, slope = gelu_both(matmul(low_one, c_refs[0][...]) + c_refs[1][...])
                active = low(active)
                left = left + matmul(active, c_refs[2][...]) + c_refs[3][...]
                for ref, value in zip(kept_refs[:3], (low_one, active, low(slope))):
                    ref[rows] = value
                low_two = low(left)
                active, slope = gelu_both(matmul(low_two, c_refs[4][...]) + c_refs[5][...])
                active = low(active)
                right = right + matmul(active, c_refs[6][...]) + c_refs[7][...]
                for ref, value in zip(kept_refs[3:], (low_two, active, low(slope))):
                    ref[rows] = value
                hidden_ref[rows, :HALF] = left
                hidden_ref[rows, HALF:] = right
                x_low[rows, :HALF] = low_two
                x_low[rows, HALF:] = low(right)

        for part, ref in enumerate((q_ref, k_ref, v_ref)):
            wait_copy(w_pair, qkv_window(group, part), w_buf.at[group, part], sems.at[group, part])
            ref[:, columns] = low(matmul(x_low[...], w_buf[group, part]))
        query = scaled_query(q_ref[:, columns])
        key, value = k_ref[:, columns], v_ref[:, columns]
        bias = key_bias(length_ref[0], (1, SEQ), 1)
        lane = lax.broadcasted_iota(jnp.int32, (SEQ, LANES), 1)
        mixed = jnp.zeros((SEQ, GROUP), F32)
        lse_buf[...] = jnp.zeros((SEQ, LANES), F32)
        for head in range(HEADS_IN):
            s_ref, p_ref = s_buf.at[head % 2], p_buf.at[head % 2]
            s_ref[...] = matmul_t(only_head(query, head), key)
            for rows in rows_of(SEQ, 64):
                soft, lse = softmax_rows(s_ref[rows] + bias)
                p_ref[rows] = soft
                lse_buf[rows] = jnp.where(lane[rows] == head, lse, lse_buf[rows])
            mixed = jnp.where(head_mask(mixed, head), matmul(p_ref[...], value), mixed)
        mixed_ref[:, columns] = low(mixed)
        lse_ref[group] = jnp.transpose(lse_buf[...])[:8]

    low_wide = shape_of(SEQ, D, kind=BF16)
    kept = [(SEQ, HALF), (SEQ, INV_H), (SEQ, INV_H)] * 2
    return pl.pallas_call(
        kernel,
        grid=(GROUPS,),
        in_specs=[pl.BlockSpec(memory_space=pltpu.SMEM)]
        + [whole((SEQ, D)), whole((SEQ, D)), whole((MICRO, 6, D))]
        + [whole(value.shape) for value in coupling]
        + hbm(2),
        out_specs=[whole((SEQ, D))]
        + [whole()] * 5
        + [whole(dims) for dims in kept],
        out_shape=[shape_of(SEQ, D)]
        + [low_wide] * 4
        + [shape_of(GROUPS, 8, SEQ)]
        + [shape_of(*dims, kind=BF16) for dims in kept],
        scratch_shapes=[
            pltpu.VMEM((SEQ, D), BF16),
            pltpu.VMEM((GROUPS, 3, D, GROUP), BF16),
            pltpu.VMEM((2, SEQ, SEQ), F32),
            pltpu.VMEM((2, SEQ, SEQ), BF16),
            pltpu.VMEM((SEQ, LANES), F32),
            pltpu.SemaphoreType.DMA((GROUPS, 3)),
        ],
        compiler_params=params_for(24),
        name="first_layer_attention",
    )(length, fetched, pos_table, norms, *coupling, *w_qkv)


def spots_kernel(section_out, chosen, w_qkv, length):
    def kernel(length_ref, x_ref, chosen_ref, own_ref, came_ref, *refs):
        at_ref, q_ref, k_ref, v_ref, mixed_ref, lse_ref, at_low, w_buf, sems = refs
        w_pair = own_ref, came_ref
        group = pl.program_id(0)
        columns = group_columns(group)

        @pl.when(group == 0)
        def _():
            for g in range(GROUPS):
                for part in range(3):
                    start_copy(w_pair, 1, qkv_window(g, part), w_buf.at[g, part], sems.at[g, part])
            at_ref[...] = matmul(chosen_ref[...], x_ref[...])
            at_low[...] = low(at_ref[...])

        for part, ref in enumerate((q_ref, k_ref, v_ref)):
            wait_copy(w_pair, qkv_window(group, part), w_buf.at[group, part], sems.at[group, part])
            ref[:, columns] = low(matmul(at_low[...] if part == 0 else x_ref[...], w_buf[group, part]))
        query = scaled_query(q_ref[:, columns])
        query = jnp.concatenate([only_head(query, head) for head in range(HEADS_IN)], 0)
        bias = key_bias(length_ref[0], (1, SEQ), 1)
        soft, lse = softmax_rows(matmul_t(query, k_ref[:, columns]) + bias)
        lse_ref[group] = across(lse)
        every = matmul(soft, v_ref[:, columns])
        mixed = every[:COUNT]
        for head in range(1, HEADS_IN):
            mixed = jnp.where(head_mask(mixed, head), every[head * COUNT : (head + 1) * COUNT], mixed)
        mixed_ref[:, columns] = low(mixed)

    return pl.pallas_call(
        kernel,
        grid=(GROUPS,),
        in_specs=[pl.BlockSpec(memory_space=pltpu.SMEM), whole((SEQ, D)), whole((COUNT, SEQ))] + hbm(2),
        out_specs=[whole()] * 6,
        out_shape=[
            shape_of(COUNT, D),
            shape_of(COUNT, D, kind=BF16),
            shape_of(SEQ, D, kind=BF16),
            shape_of(SEQ, D, kind=BF16),
            shape_of(COUNT, D, kind=BF16),
            shape_of(GROUPS, HEADS_IN * COUNT, LANES),
        ],
        scratch_shapes=[
            pltpu.VMEM((COUNT, D), BF16),
            pltpu.VMEM((GROUPS, 3, D, GROUP), BF16),
            pltpu.SemaphoreType.DMA((GROUPS, 3)),
        ],
        compiler_params=params_for(20),
        name="second_layer_attention",
    )(length, section_out, chosen, *w_qkv)


UP_WINDOWS = [(0, slice(None), slice(j * TILE, (j + 1) * TILE)) for j in range(TILES)]
DOWN_WINDOWS = [(0, slice(j * TILE, (j + 1) * TILE), slice(None)) for j in range(TILES)]
OUT_WINDOW = (0, slice(None), slice(None))


def rest_buffers():
    return [
        pltpu.VMEM((D, D), BF16),
        pltpu.VMEM((TILES, D, TILE), BF16),
        pltpu.VMEM((TILES, TILE, D), BF16),
        pltpu.SemaphoreType.DMA((2 * TILES + 1,)),
    ]


def start_rest(pairs, section, buffers):
    out_buf, up_buf, down_buf, sems = buffers
    start_copy(pairs[0], section, OUT_WINDOW, out_buf, sems.at[2 * TILES])
    for j in range(TILES):
        start_copy(pairs[1], section, UP_WINDOWS[j], up_buf.at[j], sems.at[j])
        start_copy(pairs[2], section, DOWN_WINDOWS[j], down_buf.at[j], sems.at[TILES + j])


def wait_out(pairs, buffers):
    wait_copy(pairs[0], OUT_WINDOW, buffers[0], buffers[3].at[2 * TILES])


def wait_up(pairs, buffers, tile):
    wait_copy(pairs[1], UP_WINDOWS[0], buffers[1].at[tile], buffers[3].at[tile])


def wait_down(pairs, buffers, tile):
    wait_copy(pairs[2], DOWN_WINDOWS[0], buffers[2].at[tile], buffers[3].at[TILES + tile])


def rest_forward(section, hidden, mixed, norms, adapter, w_rest, coupling=None):
    rows = hidden.shape[0]
    step = min(rows, 256)
    last = coupling is not None
    extra_in = coupling if last else ()

    def kernel(hidden_ref, mixed_ref, norms_ref, *refs):
        a_refs, refs = refs[:4], refs[4:]
        c_refs, refs = refs[: len(extra_in)], refs[len(extra_in) :]
        w_flat, refs = refs[:6], refs[6:]
        pairs = [w_flat[2 * i : 2 * i + 2] for i in range(3)]
        outs, refs = refs[:n_outs], refs[n_outs:]
        result_ref, n1_ref, i1_ref, slope_ref, lin_ref, act_ref, bslope_ref, n2_ref, i2_ref = outs[:9]
        att_low, acc, u_even, u_odd, g_even, g_odd = refs[:6]
        buffers = refs[6:]
        turn = pl.program_id(0)
        gain = lambda i: norms_ref[section, i : i + 1]

        @pl.when(turn == 0)
        def _():
            start_rest(pairs, section, buffers)
            wait_out(pairs, buffers)
            for part in rows_of(rows, step):
                first = hidden_ref[part] + matmul(mixed_ref[part], buffers[0][...])
                values, (normal, inverse) = layer_norm(first, gain(2), gain(3))
                acc[part] = values
                att_low[part] = low(values)
                n1_ref[part] = normal
                i1_ref[part] = across(inverse)
            wait_up(pairs, buffers, 0)
            for part in rows_of(rows, step):
                u_even[part] = matmul(att_low[part], buffers[1][0])

        even, odd = 2 * turn, 2 * turn + 1
        after = jnp.minimum(even + 2, TILES - 1)
        wait_down(pairs, buffers, even)
        wait_up(pairs, buffers, odd)
        wait_down(pairs, buffers, odd)

        @pl.when(even + 2 < TILES)
        def _():
            wait_up(pairs, buffers, even + 2)

        for now, u_now, g_now, later, u_later in (
            (even, u_even, g_even, odd, u_odd),
            (odd, u_odd, g_odd, after, u_even),
        ):
            for part in rows_of(rows, step):
                for small in rows_of(step, 32):
                    at = slice(part.start + small.start, part.start + small.stop)
                    active, slope = gelu_both(u_now[at])
                    g_now[at] = low(active)
                    slope_ref[at, tile_columns(now)] = low(slope)
                u_later[part] = matmul(att_low[part], buffers[1][later])
                acc[part] += matmul(g_now[part], buffers[2][now])

        @pl.when(turn == TILES // 2 - 1)
        def _():
            for part in rows_of(rows, step):
                summed = acc[part]
                low_in = low(summed)
                active, slope = gelu_both(matmul(low_in, a_refs[0][...]) + a_refs[1][...])
                active = low(active)
                lin_ref[part], act_ref[part], bslope_ref[part] = low_in, active, low(slope)
                second = summed + (matmul(active, a_refs[2][...]) + a_refs[3][...])
                values, (normal, inverse) = layer_norm(second, gain(4), gain(5))
                n2_ref[part], i2_ref[part] = normal, across(inverse)
                if not last:
                    result_ref[part] = low(values)
            if last:
                left, right = values[:, :HALF], values[:, HALF:]
                low_two = low(left)
                active_two, slope_two = gelu_both(matmul(low_two, c_refs[4][...]) + c_refs[5][...])
                active_two = low(active_two)
                right = right - (matmul(active_two, c_refs[6][...]) + c_refs[7][...])
                low_one = low(right)
                active_one, slope_one = gelu_both(matmul(low_one, c_refs[0][...]) + c_refs[1][...])
                active_one = low(active_one)
                left = left - (matmul(active_one, c_refs[2][...]) + c_refs[3][...])
                normed, (normal, inverse) = layer_norm(
                    jnp.concatenate([left, right], 1), gain(0), gain(1)
                )
                result_ref[...] = low(normed)
                kept = (normal, across(inverse), low_one, active_one, low(slope_one))
                kept += (low_two, active_two, low(slope_two))
                for ref, value in zip(outs[9:], kept):
                    ref[...] = value

    wide, thin = shape_of(rows, D), shape_of(rows, LANES)
    out_shape = [shape_of(rows, D, kind=BF16), wide, thin, shape_of(rows, FF, kind=BF16)]
    out_shape += [shape_of(rows, D, kind=BF16), shape_of(rows, BOT, kind=BF16)]
    out_shape += [shape_of(rows, BOT, kind=BF16), wide, thin]
    if last:
        out_shape += [wide, thin]
        out_shape += [shape_of(rows, n, kind=BF16) for n in (HALF, INV_H, INV_H)] * 2
    n_outs = len(out_shape)
    out_specs = [whole(out.shape) for out in out_shape]
    return pl.pallas_call(
        kernel,
        grid=(TILES // 2,),
        in_specs=[whole((rows, D)), whole((rows, D)), whole((MICRO, 6, D))]
        + [whole(value.shape) for value in (*adapter, *extra_in)]
        + hbm(6),
        out_specs=out_specs,
        out_shape=out_shape,
        scratch_shapes=[
            pltpu.VMEM((rows, D), BF16),
            pltpu.VMEM((rows, D), F32),
            pltpu.VMEM((rows, TILE), F32),
            pltpu.VMEM((rows, TILE), F32),
            pltpu.VMEM((rows, TILE), BF16),
            pltpu.VMEM((rows, TILE), BF16),
        ]
        + rest_buffers(),
        compiler_params=params_for(28),
        name="last_rows_forward" if last else "first_layer_rest",
    )(hidden, mixed, norms, *adapter, *extra_in, *[w for pair in w_rest for w in pair])


def column_sum(values):
    return jnp.sum(values.astype(F32), 0, keepdims=True)


def branch_grads(grad_low, kept, weights, out_refs):
    low_in, active, slope = kept
    hidden_grad = low(matmul_t(grad_low, weights[2]) * slope.astype(F32))
    out_refs[0][...] = inner_rows(low_in, hidden_grad)
    out_refs[1][...] = column_sum(hidden_grad)
    out_refs[2][...] = inner_rows(active, grad_low)
    out_refs[3][...] = column_sum(grad_low)
    return hidden_grad


ADAPTER_GRADS = ((D, BOT), (1, BOT), (BOT, D), (1, D))
COUPLING_GRADS = ((HALF, INV_H), (1, INV_H), (INV_H, HALF), (1, HALF))


def rest_backward(section, incoming, kept, norms, adapter, w_rest, head=None, packed=False, other_packed=None):
    n1, i1, slope, lin, act, bslope, n2, i2 = kept
    rows = n1.shape[0]
    step = min(rows, 256)
    last = head is not None
    if last:
        head_kept, coupling, normed, target_rows, row_weights, weight_sum = head
        extra_in = (*head_kept, *coupling, normed, target_rows, row_weights, weight_sum)
    else:
        extra_in = () if other_packed is None else (other_packed,)

    def kernel(incoming_ref, n1_ref, i1_ref, slope_ref, lin_ref, act_ref, bslope_ref, n2_ref, i2_ref, *refs):
        norms_ref, a_refs, refs = refs[0], refs[1:5], refs[5:]
        e_refs, refs = refs[: len(extra_in)], refs[len(extra_in) :]
        w_flat, refs = refs[:6], refs[6:]
        pairs = [w_flat[2 * i : 2 * i + 2] for i in range(3)]
        outs, refs = refs[:n_outs], refs[n_outs:]
        start_ref, mixed_ref, grad_refs, outs = outs[0], outs[1], outs[2:6], outs[2:]
        summed, summed_low, acc, second_low, hidden_low = refs[:5]
        buffers, refs = refs[5:9], refs[9:]
        if packed:
            grad_refs = (refs[0], outs[0], refs[1], outs[1])
        tile = pl.program_id(0)
        gain = lambda i: norms_ref[section, i : i + 1]

        def pack():
            if last:
                def store(part, chunk):
                    outs[2][part] = chunk
            else:
                here = lax.axis_index("section") == section

                def store(part, chunk):
                    arrived = e_refs[0][part]
                    outs[2][part] = jnp.where(here, chunk, arrived)
                    outs[3][part] = jnp.where(here, arrived, chunk)

            pack_adapter((grad_refs[0], grad_refs[2]), store)

        def from_head():
            nh_ref, ih_ref = e_refs[:2]
            kept_one, kept_two = ([ref[...] for ref in e_refs[at : at + 3]] for at in (2, 5))
            c_one, c_two = ([ref[...] for ref in e_refs[at : at + 4]] for at in (8, 12))
            normed_ref, target_ref, weight_ref, total_ref = e_refs[16:]
            loss_ref, one_refs, two_refs = outs[-9], outs[-8:-4], outs[-4:]
            parts = incoming_ref.shape[0]
            stats = incoming_ref[:, :, D:].astype(F32)
            highest = jnp.sum(stats[:, :, :3], 2, keepdims=True)
            totals = jnp.sum(stats[:, :, 3:6], 2, keepdims=True)
            top = jnp.max(highest, 0)
            factor = jnp.exp(highest - top[None])
            total = jnp.sum(totals * factor, 0)
            expected = jnp.zeros((rows, D), F32)
            for part in range(parts):
                expected += incoming_ref[part, :, :D].astype(F32) * (factor[part] / total)
            target = target_ref[...]
            target_logit = jnp.sum(normed_ref[...].astype(F32) * target, 1, keepdims=True)
            row_losses = weight_ref[...] * (top + jnp.log(total) - target_logit)
            loss_ref[...] = jnp.sum(row_losses, 0, keepdims=True)
            normed_grad = weight_ref[...] / total_ref[...] * (expected - target)
            restored = norm_back(normed_grad, (nh_ref[...], ih_ref[:, :1]), gain(0))
            left, right = restored[:, :HALF], restored[:, HALF:]
            hidden = branch_grads(low(-left), kept_one, c_one, one_refs)
            right = right + matmul_t(hidden, c_one[0])
            hidden = branch_grads(low(-right), kept_two, c_two, two_refs)
            left = left + matmul_t(hidden, c_two[0])
            return jnp.concatenate([left, right], 1)

        @pl.when(tile == 0)
        def _():
            start_rest(pairs, section, buffers)
            for part in rows_of(rows, step):
                arrived = from_head() if last else incoming_ref[part].astype(F32)
                second = norm_back(arrived, (n2_ref[part], i2_ref[part, :1]), gain(4))
                summed[part] = second
                second_low[part] = low(second)
            hidden_low[...] = branch_grads(
                second_low[...],
                (lin_ref[...], act_ref[...], bslope_ref[...]),
                [ref[...] for ref in a_refs],
                grad_refs,
            )
            for part in rows_of(rows, step):
                total = summed[part] + matmul_t(hidden_low[part], a_refs[0][...])
                summed[part] = total
                summed_low[part] = low(total)
                acc[part] = total
            if packed:
                pack()

        for now in (2 * tile, 2 * tile + 1):
            wait_up(pairs, buffers, now)
            wait_down(pairs, buffers, now)
        for now in (2 * tile, 2 * tile + 1):
            for part in rows_of(rows, step):
                inner = matmul_t(summed_low[part], buffers[2][now])
                inner = low(inner * slope_ref[part, tile_columns(now)].astype(F32))
                acc[part] += matmul_t(inner, buffers[1][now])

        @pl.when(tile == TILES // 2 - 1)
        def _():
            wait_out(pairs, buffers)
            for part in rows_of(rows, step):
                start = norm_back(acc[part], (n1_ref[part], i1_ref[part, :1]), gain(2))
                start_ref[part] = start
                mixed_ref[part] = low(matmul_t(low(start), buffers[0][...]))

    out_shape = [shape_of(rows, D), shape_of(rows, D, kind=BF16)]
    if packed:
        chunks = shape_of(COUPLING_GROUPS, PART_ROWS, LANES, kind=BF16)
        out_shape += [shape_of(1, BOT), shape_of(1, D)] + [chunks] * (1 if last else 2)
    else:
        out_shape += [shape_of(*dims) for dims in ADAPTER_GRADS]
    if last:
        out_shape += [shape_of(1, 1)] + [shape_of(*dims) for dims in COUPLING_GRADS] * 2
    n_outs = len(out_shape)
    in_specs = [whole(value.shape) for value in (incoming, *kept, norms, *adapter, *extra_in)]
    return pl.pallas_call(
        kernel,
        grid=(TILES // 2,),
        in_specs=in_specs + hbm(6),
        out_specs=[whole(out.shape) for out in out_shape],
        out_shape=out_shape,
        scratch_shapes=[
            pltpu.VMEM((rows, D), F32),
            pltpu.VMEM((rows, D), BF16),
            pltpu.VMEM((rows, D), F32),
            pltpu.VMEM((rows, D), BF16),
            pltpu.VMEM((rows, BOT), BF16),
        ]
        + rest_buffers()
        + ([pltpu.VMEM((D, BOT), F32), pltpu.VMEM((BOT, D), F32)] if packed else []),
        compiler_params=params_for(34),
        name="last_rows_backward" if last else "first_layer_rest_backward",
    )(incoming, *kept, norms, *adapter, *extra_in, *[w for pair in w_rest for w in pair])


def spots_backward(kept, mixed_grad, start_grad, chosen_t, w_qkv, length):
    query, key, value, lse = kept

    def kernel(length_ref, q_ref, k_ref, v_ref, lse_ref, mixed_ref, start_ref, chosen_ref, *refs):
        w_pair = refs[:2]
        out_ref, acc, spot, w_buf, sems = refs[2:]
        group = pl.program_id(0)
        columns = group_columns(group)

        @pl.when(group == 0)
        def _():
            for g in range(GROUPS):
                for part in range(3):
                    start_copy(w_pair, 1, qkv_window(g, part), w_buf.at[g, part], sems.at[g, part])
            spot[...] = start_ref[...]
            acc[...] = jnp.zeros_like(acc)

        stack = lambda values: jnp.concatenate([only_head(values, h) for h in range(HEADS_IN)], 0)
        query = stack(scaled_query(q_ref[:, columns]))
        mixed = stack(mixed_ref[:, columns])
        key, value = k_ref[:, columns], v_ref[:, columns]
        scores = matmul_t(query, key) + key_bias(length_ref[0], (1, SEQ), 1)
        soft = jnp.exp(scores - lse_ref[group][:, :1])
        soft_grad = matmul_t(mixed, value)
        delta = jnp.sum(soft_grad * soft, 1, keepdims=True)
        score_grad = low(soft * (soft_grad - delta))
        every = matmul(score_grad, key)
        query_grad = every[:COUNT]
        for head in range(1, HEADS_IN):
            query_grad = jnp.where(
                head_mask(query_grad, head), every[head * COUNT : (head + 1) * COUNT], query_grad
            )
        query_grad = low(query_grad * HEAD_DIM**-0.5)
        key_grad = low(inner_rows(score_grad, query))
        value_grad = low(inner_rows(low(soft), mixed))
        for part in range(3):
            wait_copy(w_pair, qkv_window(group, part), w_buf.at[group, part], sems.at[group, part])
        spot[...] += matmul_t(query_grad, w_buf[group, 0])
        acc[...] += matmul_t(key_grad, w_buf[group, 1]) + matmul_t(value_grad, w_buf[group, 2])

        @pl.when(group == GROUPS - 1)
        def _():
            placed = jnp.dot(
                chosen_ref[...], spot[...], precision=HIGHEST, preferred_element_type=F32
            )
            out_ref[...] = low(acc[...] + placed)

    return pl.pallas_call(
        kernel,
        grid=(GROUPS,),
        in_specs=[pl.BlockSpec(memory_space=pltpu.SMEM)]
        + [whole()] * 7
        + hbm(2),
        out_specs=whole((SEQ, D)),
        out_shape=shape_of(SEQ, D, kind=BF16),
        scratch_shapes=[
            pltpu.VMEM((SEQ, D), F32),
            pltpu.VMEM((COUNT, D), F32),
            pltpu.VMEM((GROUPS, 3, D, GROUP), BF16),
            pltpu.SemaphoreType.DMA((GROUPS, 3)),
        ],
        compiler_params=params_for(20),
        name="second_layer_attention_backward",
    )(length, query, key, value, lse, mixed_grad, start_grad, chosen_t, *w_qkv)


def first_backward(kept, mixed_grad, start_grad, kept_coupling, coupling, head_grads, w_qkv, length, biases=()):
    query, key, value, lse = kept

    def kernel(length_ref, q_ref, k_ref, v_ref, lse_ref, mixed_ref, start_ref, *refs):
        kept_refs, c_refs, h_refs, refs = refs[:6], refs[6:14], refs[14:22], refs[22:]
        b_refs, w_pair, refs = refs[: len(biases)], refs[len(biases) : len(biases) + 2], refs[len(biases) + 2 :]
        out_refs, refs = refs[: len(out_shape)], refs[len(out_shape) :]
        acc, s_buf, d_buf, p_low, ds_low, w_buf, sems = refs[:7]
        if biases:
            chunk_refs, out_refs = out_refs, refs[7:]
        group = pl.program_id(0)
        columns = group_columns(group)

        @pl.when(group == 0)
        def _():
            for g in range(GROUPS):
                for part in range(3):
                    start_copy(w_pair, 0, qkv_window(g, part), w_buf.at[g, part], sems.at[g, part])
            acc[...] = start_ref[...]

        query = scaled_query(q_ref[:, columns])
        key, value, mixed = k_ref[:, columns], v_ref[:, columns], mixed_ref[:, columns]
        lse_rows = lse_ref[group]
        key_t = jnp.transpose(key)
        key_grad = jnp.zeros((SEQ, GROUP), F32)
        value_grad = jnp.zeros((SEQ, GROUP), F32)
        query_parts = []
        for head in range(HEADS_IN):
            slot = head % 2
            s_buf[slot] = matmul_t(only_head(key, head), query)
            d_buf[slot] = matmul_t(only_head(value, head), mixed)
            lse_row = lse_rows[head : head + 1]
            delta = jnp.zeros((8, SEQ), F32)
            for rows in rows_of(SEQ, 32):
                valid = lax.broadcasted_iota(jnp.int32, (32, 1), 0) + rows.start < length_ref[0]
                bias = jnp.where(valid, 0.0, -1e30)
                soft = jnp.exp(s_buf[slot, rows] + bias - lse_row)
                s_buf[slot, rows] = soft
                p_low[slot, rows] = low(soft)
                product = soft * d_buf[slot, rows]
                for at in range(0, 32, 8):
                    delta = delta + product[at : at + 8]
            delta = jnp.sum(delta, 0, keepdims=True)
            for rows in rows_of(SEQ, 32):
                ds_low[slot, rows] = low(s_buf[slot, rows] * (d_buf[slot, rows] - delta))
            value_grad += matmul(p_low[slot], only_head(mixed, head))
            key_grad += matmul(ds_low[slot], only_head(query, head))
            query_parts.append(matmul(key_t[head * HEAD_DIM : (head + 1) * HEAD_DIM], ds_low[slot]))
        query_grad = jnp.transpose(jnp.concatenate(query_parts, 0)) * HEAD_DIM**-0.5
        for part, grad in enumerate((query_grad, key_grad, value_grad)):
            wait_copy(w_pair, qkv_window(group, part), w_buf.at[group, part], sems.at[group, part])
            acc[...] += matmul_t(low(grad), w_buf[group, part])

        @pl.when(group == GROUPS - 1)
        def _():
            c_one, c_two = ([ref[...] for ref in c_refs[at : at + 4]] for at in (0, 4))
            kept_one, kept_two = ([ref[...] for ref in kept_refs[at : at + 3]] for at in (0, 3))
            hidden = branch_grads(low(acc[:, HALF:]), kept_two, c_two, out_refs[4:])
            left = acc[:, :HALF] + matmul_t(hidden, c_two[0])
            branch_grads(low(left), kept_one, c_one, out_refs[:4])
            for out_ref, ref in zip(out_refs, h_refs):
                out_ref[...] += ref[...]
            if not biases:
                return
            here = lax.axis_index("section")
            for s in range(MICRO):
                one = out_refs[4 * s : 4 * s + 4]
                tiles = bias_tiles(b_refs[2 * s][...], b_refs[2 * s + 1][...], one[1][...], one[3][...])

                def store(part, chunk, s=s):
                    @pl.when(here == s)
                    def _():
                        chunk_refs[0][part] = chunk

                    @pl.when(here != s)
                    def _():
                        chunk_refs[1][part] = low(chunk)

                pack_coupling((one[0], one[2]), tiles, sum(BIASES) // COUPLING_GROUPS, store)

    out_shape = [shape_of(*dims) for dims in COUPLING_GRADS] * 2
    grad_buffers = []
    if biases:
        grad_buffers = [pltpu.VMEM(dims, F32) for dims in COUPLING_GRADS] * 2
        dims = (COUPLING_GROUPS, GROUP_ROWS + 8, LANES)
        out_shape = [shape_of(*dims), shape_of(*dims, kind=BF16)]
    return pl.pallas_call(
        kernel,
        grid=(GROUPS,),
        in_specs=[pl.BlockSpec(memory_space=pltpu.SMEM)]
        + [whole()] * 6
        + [whole(value.shape) for value in (*kept_coupling, *coupling, *head_grads, *biases)]
        + hbm(2),
        out_specs=[whole(out.shape) for out in out_shape],
        out_shape=out_shape,
        scratch_shapes=[
            pltpu.VMEM((SEQ, D), F32),
            pltpu.VMEM((2, SEQ, SEQ), F32),
            pltpu.VMEM((2, SEQ, SEQ), F32),
            pltpu.VMEM((2, SEQ, SEQ), BF16),
            pltpu.VMEM((2, SEQ, SEQ), BF16),
            pltpu.VMEM((GROUPS, 3, D, GROUP), BF16),
            pltpu.SemaphoreType.DMA((GROUPS, 3)),
        ]
        + grad_buffers,
        compiler_params=params_for(28),
        name="first_layer_attention_backward",
    )(length, query, key, value, lse, mixed_grad, start_grad, *kept_coupling, *coupling, *head_grads, *biases, *w_qkv)


VOCAB_TILE = 1280


def head_kernel(rows, table):
    count, vocab = rows.shape[0], table.shape[0]
    last = pl.cdiv(vocab, VOCAB_TILE) - 1
    turns = last // 2 + 1
    parts = rows_of(count, 256)

    def kernel(x_ref, even_ref, odd_ref, after_ref, out_ref, acc, top, total, l_even, l_odd, p_even, p_odd):
        turn = pl.program_id(0)

        def entries_of(ref, tile):
            row = lax.broadcasted_iota(jnp.int32, (VOCAB_TILE, 1), 0)
            return jnp.where(row < vocab - tile * VOCAB_TILE, ref[...], jnp.zeros_like(ref))

        @pl.when(turn == 0)
        def _():
            acc[...] = jnp.zeros_like(acc)
            top[...] = jnp.full_like(top, -1e30)
            total[...] = jnp.zeros_like(total)
            entries = entries_of(even_ref, 0)
            for part in parts:
                l_even[part] = matmul_t(x_ref[part], entries)

        even = entries_of(even_ref, 2 * turn)
        odd = entries_of(odd_ref, 2 * turn + 1)
        after = entries_of(after_ref, 2 * turn + 2)
        for tile, l_now, p_now, now, l_later, later in (
            (2 * turn, l_even, p_even, even, l_odd, odd),
            (2 * turn + 1, l_odd, p_odd, odd, l_even, after),
        ):
            bias = key_bias(vocab - tile * VOCAB_TILE, (1, VOCAB_TILE), 1)
            for part in parts:
                for small in rows_of(256, 32):
                    at = slice(part.start + small.start, part.start + small.stop)
                    logits = l_now[at] + bias
                    earlier = top[at]
                    highest = jnp.maximum(earlier, jnp.max(logits, 1, keepdims=True))
                    exponent = jnp.exp(logits - highest)
                    factor = jnp.exp(earlier - highest)
                    top[at] = highest
                    total[at] = total[at] * factor + jnp.sum(exponent, 1, keepdims=True)
                    p_now[at] = low(exponent)
                    acc[at] = acc[at] * factor
                l_later[part] = matmul_t(x_ref[part], later)
                acc[part] += matmul(p_now[part], now)

        @pl.when(turn == turns - 1)
        def _():
            lane = lax.broadcasted_iota(jnp.int32, (count, LANES), 1)
            stats = jnp.zeros((count, LANES), F32)
            pieces = three_low(top[...]) + three_low(total[...])
            for j, piece in enumerate(pieces):
                stats = jnp.where(lane == j, piece.astype(F32), stats)
            out_ref[:, :D] = low(acc[...])
            out_ref[:, D:] = low(stats)

    def tile_at(shift):
        return pl.BlockSpec((VOCAB_TILE, D), lambda j: (jnp.minimum(2 * j + shift, last), 0))

    return pl.pallas_call(
        kernel,
        grid=(turns,),
        in_specs=[whole()] + [tile_at(shift) for shift in range(3)],
        out_specs=whole(),
        out_shape=shape_of(count, D + LANES, kind=BF16),
        scratch_shapes=[
            pltpu.VMEM((count, D), F32),
            pltpu.VMEM((count, 1), F32),
            pltpu.VMEM((count, 1), F32),
            pltpu.VMEM((count, VOCAB_TILE), F32),
            pltpu.VMEM((count, VOCAB_TILE), F32),
            pltpu.VMEM((count, VOCAB_TILE), BF16),
            pltpu.VMEM((count, VOCAB_TILE), BF16),
        ],
        compiler_params=params_for(44),
        name="vocabulary_head",
    )(rows, table, table, table)


def swap_add(own, other):
    came = lax.ppermute(low(other), "section", [(0, 1), (1, 0)])
    return own + came.astype(F32)


def pick(first_section, both):
    return jnp.where(first_section, both[0], both[1])


def plan_requests(ids, vocab_rows, slots):
    earlier = jnp.arange(IDS)[None, :] < jnp.arange(IDS)[:, None]
    same_id = ids[:, :, None] == ids[:, None, :]
    first = jnp.logical_not(jnp.any(same_id & earlier, -1))
    owner = ids // vocab_rows
    same_owner = owner[:, :, None] == owner[:, None, :]
    rank = jnp.sum((same_owner & earlier & first[:, None, :]).astype(jnp.int32), -1)
    slot = jnp.sum(jnp.where(same_id & first[:, None, :], rank[:, None, :], 0), -1)
    rounds = jnp.max(rank) // slots + 1
    return owner, slot, first, rounds


def fetch_rows(table, ids, first_section, weight_part, slots):
    parts = lax.axis_size("dp")
    vocab_rows = table.shape[0]
    owner, slot, first, rounds = plan_requests(ids, vocab_rows, slots)
    ids, owner, slot, first = (pick(first_section, both) for both in (ids, owner, slot, first))
    local = ids - owner * vocab_rows

    def places(turn):
        here = slot - turn * slots
        spot = jnp.where((here >= 0) & (here < slots), owner * slots + here, -1)
        return spot[:, None] == jnp.arange(parts * slots)[None, :]

    def wanted(hits):
        return jnp.sum(jnp.where(hits & first[:, None], local[:, None], 0), 0).reshape(parts, slots)

    def answer(asked, hits):
        rows = table.at[asked.reshape(-1)].get(mode="promise_in_bounds").reshape(parts, slots, D)
        came = lax.all_to_all(rows, "dp", 0, 0).reshape(parts * slots, D)
        return matmul(hits.astype(BF16), came)

    hits = places(0)
    extra = jnp.broadcast_to(jnp.stack([rounds, weight_part])[None], (parts, 2))
    asked = lax.all_to_all(jnp.concatenate([wanted(hits), extra], 1), "dp", 0, 0)
    total_rounds = jnp.max(asked[:, slots])
    weight_sum = jnp.sum(asked[:, slots + 1])
    rows = answer(asked[:, :slots], hits)

    def more(state):
        return state[0] < total_rounds

    def another(state):
        turn, rows = state
        hits = places(turn)
        asked = lax.all_to_all(wanted(hits), "dp", 0, 0)
        return turn + 1, rows + answer(asked, hits)

    return lax.while_loop(more, another, (jnp.int32(1), rows))[1], weight_sum.astype(F32)


def three_low(values):
    high = low(values)
    rest = values - high.astype(F32)
    middle = low(rest)
    return [high, middle, low(rest - middle.astype(F32))]


def in_groups(count):
    return lax.axis_size("dp") == COUPLING_GROUPS and count == 4 * PART_GROUPS


def gather_params(master, vector):
    parts = lax.axis_size("dp")
    count, width = master.shape[0], vector.shape[0]
    if in_groups(count):
        packed = pack_own(master, vector[None])
        gathered = lax.all_gather(packed, ("section", "dp")).reshape(MICRO, parts, -1, LANES)
        arrays = unpack_all(gathered, width)
        params = []
        for s in range(MICRO):
            down, up, c_down, c_up, first, second, third, fourth = (array[s] for array in arrays)
            params.append(((down, first, up, second), (c_down, third, c_up, fourth)))
        return [pair[0] for pair in params], params[0][1], params[1][1]
    flat = low(jnp.concatenate([master.reshape(-1), vector]))
    gathered = lax.all_gather(flat, ("section", "dp")).reshape(MICRO, parts, -1)
    size = count * BLOCK**2
    all_blocks = gathered[:, :, :size].reshape(MICRO, parts * count, BLOCK, BLOCK)
    all_vectors = gathered[:, :, size:].reshape(MICRO, parts * width)
    params = [split_params(all_blocks[s], all_vectors[s]) for s in range(MICRO)]
    as_rows = lambda p: (p[0], p[1].astype(F32)[None], p[2], p[3].astype(F32)[None])
    return [as_rows(pair[0]) for pair in params], as_rows(params[0][1]), as_rows(params[1][1])


def sum_at_owners(grads, loss_part, count):
    parts = lax.axis_size("dp")
    width = sum(BIASES) // parts
    flat = []
    for adapter, coupling in grads:
        blocks, vector = join_params(adapter, coupling)
        flat.append(
            jnp.concatenate([blocks.reshape(parts, count * BLOCK**2), vector.reshape(parts, width)], 1)
        )
    first = lax.axis_index("section") == 0
    summed = swap_add(jnp.where(first, flat[0], flat[1]), jnp.where(first, flat[1], flat[0]))
    owned = jnp.sum(lax.all_to_all(low(summed), "dp", 0, 0).astype(F32), 0)
    blocks = owned[: count * BLOCK**2].reshape(count, BLOCK, BLOCK)
    pair = jnp.stack([jnp.sum(owned * owned), loss_part[0, 0]])
    pair = jnp.pad(pair, (0, LANES - 2))[None, None]
    return blocks, owned[count * BLOCK**2 :], jnp.broadcast_to(pair, (parts * MICRO, 1, LANES))


def to_coupling_owners(group):
    arrived = []
    for place in range(PART_GROUPS):
        route = []
        for part in range(COUPLING_GROUPS):
            owner, at = divmod(ADAPTER_GROUPS + part, PART_GROUPS)
            if at == place:
                route.append((part, owner))
        arrived.append(lax.ppermute(group, "dp", route))
    return arrived


def exact(spec, left, right):
    return jnp.einsum(spec, left, right, precision=HIGHEST)


def update(pair, grad, grad_vector, state):
    master, momentum, stat_left, stat_right, root_left, root_right, vectors, vec_first, vec_second = state
    left_square = exact("nij,nkj->nik", grad, grad)
    right_square = exact("nji,njk->nik", grad, grad)
    turned = exact("nij,njk->nik", exact("nij,njk->nik", root_left, grad), root_right)
    turned_old = exact("nij,njk->nik", exact("nij,njk->nik", root_left, momentum), root_right)

    def kernel(pair_ref, grad_ref, left_ref, right_ref, turned_ref, old_ref, vector_ref, *refs):
        master_ref, momentum_ref, stat_left_ref, stat_right_ref, vectors_ref, first_ref, second_ref = refs[:7]
        outs = refs[7:]
        totals = jnp.sum(pair_ref[...], 0)
        norm = jnp.sqrt(totals[:, :1])
        factor = CLIP_NORM / jnp.maximum(norm, CLIP_NORM)
        outs[9][...] = norm
        outs[10][...] = totals[:, 1:2]
        for n in range(grad_ref.shape[0]):
            clipped = grad_ref[n] * factor
            outs[0][0, n] = clipped
            outs[1][0, n] = FIRST_DECAY * momentum_ref[n] + (1.0 - FIRST_DECAY) * clipped
            square = (1.0 - STAT_DECAY) * factor * factor
            outs[2][0, n] = STAT_DECAY * stat_left_ref[n] + square * left_ref[n]
            outs[3][0, n] = STAT_DECAY * stat_right_ref[n] + square * right_ref[n]
            direction = FIRST_DECAY * old_ref[n] + (1.0 - FIRST_DECAY) * factor * turned_ref[n]
            master_new = master_ref[n] - MAT_RATE * (direction + MAT_DECAY * master_ref[n])
            outs[4][0, n] = master_new
            outs[5][0, n] = low(master_new)
        clipped = vector_ref[...] * factor
        first_new = FIRST_DECAY * first_ref[...] + (1.0 - FIRST_DECAY) * clipped
        second_new = VEC_SECOND * second_ref[...] + (1.0 - VEC_SECOND) * clipped * clipped
        outs[6][...] = first_new
        outs[7][...] = second_new
        corrected_first = first_new / (1.0 - FIRST_DECAY**STEP)
        corrected_second = second_new / (1.0 - VEC_SECOND**STEP)
        outs[8][...] = vectors_ref[...] - VEC_RATE * (
            corrected_first / (jnp.sqrt(corrected_second) + VEC_EPS) + VEC_DECAY * vectors_ref[...]
        )

    blocks = (1,) + grad.shape
    width = vectors.shape
    shapes = [shape_of(*blocks)] * 5 + [shape_of(*blocks, kind=BF16)] + [shape_of(*width)] * 3
    return pl.pallas_call(
        kernel,
        out_shape=shapes + [shape_of(1, 1)] * 2,
        compiler_params=params_for(40),
        name="update",
    )(
        pair, grad, left_square, right_square, turned, turned_old, grad_vector,
        master, momentum, stat_left, stat_right, vectors, vec_first, vec_second,
    )


def shards(
    token_ids,
    lengths,
    positions,
    targets,
    loss_weights,
    embed_table,
    pos_table,
    norm_params,
    base_qkv,
    base_out,
    base_up,
    base_down,
    master,
    momentum,
    stat_left,
    stat_right,
    root_left,
    root_right,
    vectors,
    vec_first,
    vec_second,
):
    parts = lax.axis_size("dp")
    first_section = lax.axis_index("section") == 0
    slots = -(-IDS * 5 // (4 * parts * 16)) * 16

    adapters, coupling_one, coupling_two = gather_params(master[0], vectors[0])
    coupling = (*coupling_one, *coupling_two)
    swapped = [lax.ppermute(w, "section", [(0, 1), (1, 0)]) for w in (base_qkv, base_out, base_up, base_down)]
    pairs = list(zip((base_qkv, base_out, base_up, base_down), swapped))
    w_qkv, w_rest = pairs[0], pairs[1:]
    came = lax.ppermute(norm_params, "section", [(0, 1), (1, 0)])
    norms = jnp.concatenate([pick(first_section, (norm_params, came)), pick(first_section, (came, norm_params))])

    ids = jnp.concatenate([token_ids[:, 0], targets[:, 0]], -1)
    weight_part = jnp.sum(loss_weights)
    fetched, weight_sum = fetch_rows(embed_table, ids, first_section, weight_part, slots)
    length = pick(first_section, lengths)
    spots = pick(first_section, positions[:, 0])
    row_weights = pick(first_section, loss_weights[:, 0]).astype(F32)[:, None]
    chosen = (spots[:, None] == jnp.arange(SEQ)[None, :]).astype(BF16)
    chosen_t = (spots[None, :] == jnp.arange(SEQ)[:, None]).astype(F32)

    hidden, query, key, value, mixed, lse, *kept_coupling = first_kernel(
        fetched, pos_table, norms, coupling, w_qkv, length
    )
    section_out, *kept = rest_forward(0, hidden, mixed, norms, adapters[0], w_rest)
    at_spots, query_1, key_1, value_1, mixed_1, lse_1 = spots_kernel(section_out, chosen, w_qkv, length)
    normed, *kept_1 = rest_forward(1, at_spots, mixed_1, norms, adapters[1], w_rest, coupling)

    rows = jnp.broadcast_to(normed[None], (parts, COUNT, D))
    rows = lax.all_to_all(rows, "dp", 0, 0).reshape(parts * COUNT, D)
    merged = head_kernel(rows, embed_table).reshape(parts, COUNT, D + LANES)
    merged = lax.all_to_all(merged, "dp", 0, 0)

    head = (kept_1[8:], coupling, normed, fetched[SEQ:], row_weights, weight_sum.reshape(1, 1))
    packed = in_groups(master.shape[1])
    start_grad, mixed_grad, *grads = rest_backward(
        1, merged, kept_1[:8], norms, adapters[1], w_rest, head, packed
    )
    adapter_grads_1, loss_part, head_grads = grads[:-9], grads[-9], grads[-8:]
    section_grad = spots_backward(
        (query_1, key_1, value_1, lse_1), mixed_grad, start_grad, chosen_t, w_qkv, length
    )
    start_grad, mixed_grad, *adapter_grads_0 = rest_backward(
        0, section_grad, kept, norms, adapters[0], w_rest, None, packed, adapter_grads_1[2] if packed else None
    )
    last = functools.partial(
        first_backward,
        (query, key, value, lse), mixed_grad, start_grad, kept_coupling, coupling, head_grads, w_qkv, length,
    )
    if packed:
        own, other = adapter_grads_0[2:]
        adapter_came = lax.all_to_all(low(swap_add(own.astype(F32), other)), "dp", 0, 0)
        own, other = last((*adapter_grads_0[:2], *adapter_grads_1[:2]))
        adapter_total, squares = sum_adapter(adapter_came)
        came = lax.all_to_all(low(swap_add(own, other)), "dp", 0, 0)
        group, bias, pair = sum_coupling(came, squares, loss_part, parts * MICRO)
        grad = own_blocks_of(adapter_total, to_coupling_owners(group))
        grad_vector = bias[:1, : vectors.shape[1]]
    else:
        grads = last()
        grad, grad_vector, pair = sum_at_owners(
            ((adapter_grads_0, grads[:4]), (adapter_grads_1, grads[4:])), loss_part, master.shape[1]
        )
        grad_vector = grad_vector[None]
    pair = lax.all_to_all(pair, ("dp", "section"), 0, 0)
    state = (master, momentum, stat_left, stat_right, root_left, root_right)
    *outs, grad_norm, loss_sum = update(
        pair, grad, grad_vector, [value[0] for value in state] + [vectors, vec_first, vec_second]
    )
    return (*outs, grad_norm[0, 0], loss_sum[0, 0], weight_sum)


def solution(mesh):
    rows = P(None, "dp", None)
    section = P("section", None, None)
    blocks = P("section", "dp", None, None)
    biases = P("section", "dp")
    return jax.shard_map(
        shards,
        mesh=mesh,
        in_specs=(rows, P(None, "dp"), rows, rows, rows, P("dp", None), P())
        + (section,) * 5
        + (blocks,) * 6
        + (biases,) * 3,
        out_specs=(blocks,) * 6 + (biases,) * 3 + (P(),) * 3,
        check_vma=False,
    )
```

```python
import functools

import jax
import jax.numpy as jnp
import numpy as np
from jax import lax
from jax.experimental import pallas as pl
from jax.experimental.pallas import tpu as pltpu
from jax.sharding import PartitionSpec as P

D = 768
HEADS = 12
HEAD_DIM = 64
BOT = 384
INV_H = 192
SEQ = 512
COUNT = 32
MICRO = 2
BLOCK = 48
STEP = 10
HALF = 384
IDS = SEQ + COUNT

HIGHEST = lax.Precision.HIGHEST
NORM_EPS = 1e-12
CLIP_NORM = 0.02
FIRST_DECAY = 0.9
STAT_DECAY = 0.99
MAT_RATE = 0.1
MAT_DECAY = 0.01
VEC_RATE = 0.05
VEC_SECOND = 0.999
VEC_EPS = 1e-08
VEC_DECAY = 0.01
F32 = jnp.float32
BF16 = jnp.bfloat16

CDF_SCALE = 0.42 / 2.0**0.5
CDF_POLY = (
    0.2368242366796694,
    0.239585811361218,
    0.1947261443420679,
    0.2687426685879861,
    -0.13052645834187002,
    0.4406726942003943,
    -0.32025628294963193,
    0.07023101752398136,
)


def matmul(left, right):
    return jnp.dot(left, right, preferred_element_type=F32)


def matmul_t(left, right):
    return lax.dot_general(left, right, (((1,), (1,)), ((), ())), preferred_element_type=F32)


def inner_rows(left, right):
    return lax.dot_general(left, right, (((0,), (0,)), ((), ())), preferred_element_type=F32)


def low(values):
    return values.astype(BF16)


def gelu_both(values):
    below = 1.0 + CDF_SCALE * jnp.abs(values)
    ratio = pl.reciprocal(below, approx=True)
    ratio = ratio * (2.0 - below * ratio)
    poly = jnp.full_like(ratio, 0.5 * CDF_POLY[-1])
    for factor in CDF_POLY[-2::-1]:
        poly = poly * ratio + 0.5 * factor
    bell = jnp.exp(-0.5 * values * values)
    tail = bell * (poly * ratio)
    cdf = jnp.where(values < 0, tail, 1.0 - tail)
    return values * cdf, cdf + values * (bell * (2.0 * np.pi) ** -0.5)


def layer_norm(values, gain, shift):
    centered = values - jnp.mean(values, -1, keepdims=True)
    inverse = lax.rsqrt(jnp.mean(centered * centered, -1, keepdims=True) + NORM_EPS)
    normal = centered * inverse
    return normal * gain + shift, (normal, inverse)


def norm_back(incoming, kept, gain):
    normal, inverse = kept
    scaled = incoming * gain
    return inverse * (
        scaled
        - jnp.mean(scaled, -1, keepdims=True)
        - normal * jnp.mean(scaled * normal, -1, keepdims=True)
    )


def to_blocks(matrix):
    rows_in, cols_in = matrix.shape
    return (
        matrix.reshape(rows_in // BLOCK, BLOCK, cols_in // BLOCK, BLOCK)
        .transpose(0, 2, 1, 3)
        .reshape(-1, BLOCK, BLOCK)
    )


def from_blocks(blocks, rows_in, cols_in):
    return (
        blocks.reshape(rows_in // BLOCK, cols_in // BLOCK, BLOCK, BLOCK)
        .transpose(0, 2, 1, 3)
        .reshape(rows_in, cols_in)
    )


def split_params(blocks, vector):
    adapter_count = D * BOT // BLOCK**2
    half_count = HALF * INV_H // BLOCK**2
    split_at = 2 * adapter_count
    adapter = (
        from_blocks(blocks[:adapter_count], D, BOT),
        vector[:BOT],
        from_blocks(blocks[adapter_count:split_at], BOT, D),
        vector[BOT : BOT + D],
    )
    coupling = (
        from_blocks(blocks[split_at : split_at + half_count], HALF, INV_H),
        vector[BOT + D : BOT + D + INV_H],
        from_blocks(blocks[split_at + half_count :], INV_H, HALF),
        vector[BOT + D + INV_H :],
    )
    return adapter, coupling


def join_params(adapter, coupling):
    blocks = jnp.concatenate(
        [to_blocks(adapter[0]), to_blocks(adapter[2]), to_blocks(coupling[0]), to_blocks(coupling[2])]
    )
    return blocks, jnp.concatenate([adapter[1], adapter[3], coupling[1], coupling[3]], 1)[0]


GROUP_ROWS = 72
LANES = 128


def params_for(mebibytes):
    return pltpu.CompilerParams(vmem_limit_bytes=mebibytes * 2**20)


def roll(values, shift):
    return pltpu.roll(values, shift, 1)


def lane_of(values):
    return lax.broadcasted_iota(jnp.int32, values.shape, 1)


def fold_half(values, upper):
    top, bottom = values[:24], values[24:]
    if upper:
        return jnp.where(lane_of(top) < 64, roll(top, 64), bottom)
    return jnp.where(lane_of(top) < 64, top, roll(bottom, 64))


def unfold_half(values, upper):
    turned = roll(values, 64)
    return jnp.concatenate([turned, values] if upper else [values, turned], 0)


def join_pair(main_0, rest_0, main_1, rest_1):
    left = lane_of(main_0) < 64
    turned = roll(main_1, 64)
    return (
        main_0,
        jnp.where(left, unfold_half(rest_0, False), turned),
        jnp.where(left, turned, unfold_half(rest_1, True)),
    )


def cut_pair(tile_0, tile_1, tile_2):
    left = lane_of(tile_0) < 64
    return (
        (tile_0, fold_half(tile_1, False)),
        (jnp.where(left, roll(tile_1, 64), roll(tile_2, 64)), fold_half(tile_2, True)),
    )


def chunk_rows(own_blocks):
    return own_blocks // 4 * GROUP_ROWS + 8


def bias_row(tiles, part, width):
    at, shift = divmod(part * width, LANES)
    lane = lane_of(tiles[0])
    row = tiles[at]
    if shift:
        row = jnp.where(lane < LANES - shift, roll(row, LANES - shift), roll(tiles[at + 1], LANES - shift))
    return jnp.where(lane < width, row, 0.0)


def bias_tiles(first, second, third, fourth):
    cut = lambda values: [values[:, at : at + LANES] for at in range(0, values.shape[1], LANES)]
    zero = jnp.zeros((1, LANES), F32)
    left = lane_of(zero) < 64
    third_tail = jnp.concatenate([third[:, LANES:]] * 2, 1)
    turned = [roll(tile, 64) for tile in cut(fourth)]
    joints = [jnp.where(left, one, two) for one, two in zip([third_tail] + turned, turned + [zero])]
    return cut(first) + cut(second) + [third[:, :LANES]] + joints + [zero]


def tiles_of_rows(rows, width):
    tiles = []
    for tile in range(-(-len(rows) * width // LANES)):
        value = jnp.zeros((8, LANES), F32)
        lane = lane_of(value)
        for part, row in enumerate(rows):
            shift = part * width - tile * LANES
            if shift >= LANES or shift + width <= 0:
                continue
            turned = roll(row, shift % LANES) if shift % LANES else row
            value = jnp.where((lane >= shift) & (lane < shift + width), turned, value)
        tiles.append(value)
    return tiles


def pack_own(master, vector):
    count, width = master.shape[0], vector.shape[1]

    def kernel(master_ref, bias_ref, out_ref):
        row = lax.broadcasted_iota(jnp.int32, (BLOCK, 256), 0)
        col = lax.broadcasted_iota(jnp.int32, (BLOCK, 256), 1)
        pieces = []
        for group in range(count // 4):
            wide = jnp.zeros((BLOCK, 256), F32)
            for j in range(4):
                wide += matmul(low(master_ref[4 * group + j]), (col == row + BLOCK * j).astype(BF16))
            pieces += [wide[:, :LANES], fold_half(wide[:, LANES:], False)]
        bias = jnp.concatenate([bias_ref[...], jnp.zeros((1, LANES - width), F32)], 1)
        pieces.append(jnp.concatenate([bias, jnp.zeros((7, LANES), F32)], 0))
        out_ref[...] = low(jnp.concatenate(pieces, 0))

    return pl.pallas_call(
        kernel,
        out_shape=jax.ShapeDtypeStruct((chunk_rows(count), LANES), BF16),
        name="pack_own",
    )(master, vector)


MATRICES = ((D, BOT), (BOT, D), (HALF, INV_H), (INV_H, HALF))
BIASES = (BOT, D, INV_H, HALF)


def unpack_all(own, came, width):
    parts, rows, _ = own.shape
    per_part = (rows - 8) // GROUP_ROWS
    names = [prefix + name for prefix in ("a_", "c_") for name in ("down", "up")]
    names += [prefix + name for prefix in ("a_", "c_") for name in ("bias_down", "bias_up")]

    def kernel(own_hbm, came_hbm, *refs):
        out_hbm, in_bufs, out_refs, in_sems, out_sems = refs[:8], refs[8], refs[9:17], refs[17], refs[18]
        here = lax.axis_index("section")
        copies = [
            pltpu.make_async_copy(ref, in_bufs.at[at], in_sems.at[i])
            for i, (ref, at) in enumerate(((own_hbm, here), (came_hbm, 1 - here)))
        ]
        for copy in copies:
            copy.start()
        for copy in copies:
            copy.wait()

        def unpack(s, carry):
            cache = {}

            def group(index):
                part = index // per_part
                if part not in cache:
                    cache.clear()
                    cache[part] = in_bufs[s, part].astype(F32)
                base = index % per_part * GROUP_ROWS
                chunk = cache[part]
                return chunk[base : base + BLOCK], chunk[base + BLOCK : base + GROUP_ROWS]

            index = 0
            for (height, columns), out_ref in zip(MATRICES, out_refs):
                for top in range(0, height, BLOCK):
                    if columns == INV_H:
                        main, rest = group(index)
                        index += 1
                        out_ref[s, top : top + BLOCK, :LANES] = low(main)
                        out_ref[s, top : top + BLOCK, LANES:] = low(unfold_half(rest, False)[:, :64])
                        continue
                    for left in range(0, columns, HALF):
                        tiles = join_pair(*group(index), *group(index + 1))
                        index += 2
                        for j, tile in enumerate(tiles):
                            at = left + j * LANES
                            out_ref[s, top : top + BLOCK, at : at + LANES] = low(tile)
            tiles = tiles_of_rows(
                [in_bufs[s, part, rows - 16 :].astype(F32)[8:] for part in range(parts)], width
            )
            first, second, third, fourth = out_refs[4:]
            first[s] = jnp.concatenate(tiles[:3], 1)[:1]
            second[s] = jnp.concatenate(tiles[3:9], 1)[:1]
            third[s] = jnp.concatenate([tiles[9], tiles[10][:, :64]], 1)[:1]
            left = lane_of(tiles[0]) < 64
            turned = [roll(tile, 64) for tile in tiles[10:14]]
            fourth[s] = jnp.concatenate(
                [jnp.where(left, one, two) for one, two in zip(turned, turned[1:])], 1
            )[:1]
            return carry

        lax.fori_loop(0, MICRO, unpack, 0)
        copies = [
            pltpu.make_async_copy(buf, ref, out_sems.at[i]) for i, (buf, ref) in enumerate(zip(out_refs, out_hbm))
        ]
        for copy in copies:
            copy.start()
        for copy in copies:
            copy.wait()

    shapes = [((MICRO,) + shape, BF16) for shape in MATRICES] + [((MICRO, 1, size), F32) for size in BIASES]
    hbm = pl.BlockSpec(memory_space=pltpu.HBM)
    arrays = pl.pallas_call(
        kernel,
        in_specs=[hbm] * 2,
        out_specs=[hbm] * 8,
        out_shape=[jax.ShapeDtypeStruct(*shape) for shape in shapes],
        scratch_shapes=[pltpu.VMEM((MICRO, parts, rows, LANES), BF16)]
        + [pltpu.VMEM(*shape) for shape in shapes]
        + [pltpu.SemaphoreType.DMA((2,)), pltpu.SemaphoreType.DMA((8,))],
        compiler_params=params_for(24),
        name="unpack_all",
    )(own, came)
    return dict(zip(names, arrays))


ADAPTER_GROUPS = 2 * D * BOT // BLOCK**2 // 4
COUPLING_GROUPS = 2 * HALF * INV_H // BLOCK**2 // 4
PART_GROUPS = (ADAPTER_GROUPS + COUPLING_GROUPS) // COUPLING_GROUPS
PART_ROWS = PART_GROUPS * GROUP_ROWS


def groups_of(refs, shapes):
    groups = []
    for ref, (height, width) in zip(refs, shapes):
        for top in range(0, height, BLOCK):
            band = slice(top, top + BLOCK)
            if width == INV_H:
                tail = ref[band, LANES:]
                groups.append((ref[band, :LANES], fold_half(jnp.concatenate([tail, tail], 1), False)))
                continue
            for left in range(0, width, HALF):
                groups += cut_pair(*[ref[band, left + j * LANES : left + (j + 1) * LANES] for j in range(3)])
    return [jnp.concatenate(group, 0) for group in groups]


def pack_adapter(refs, store):
    groups = groups_of(refs, MATRICES[:2])
    empty = jnp.zeros((GROUP_ROWS, LANES), F32)
    for part in range(COUPLING_GROUPS):
        chunk = groups[part * PART_GROUPS : (part + 1) * PART_GROUPS]
        chunk += [empty] * (PART_GROUPS - len(chunk))
        store(part, low(jnp.concatenate(chunk, 0)))


def pack_coupling(refs, tiles, width, store):
    for part, group in enumerate(groups_of(refs, MATRICES[2:])):
        bias = jnp.concatenate([bias_row(tiles, part, width), jnp.zeros((7, LANES), F32)], 0)
        store(part, jnp.concatenate([group, bias], 0))


def sum_parts(came_ref):
    total = came_ref[0].astype(F32)
    for part in range(1, came_ref.shape[0]):
        total += came_ref[part].astype(F32)
    return total


def square_sum(values):
    return jnp.sum(jnp.sum(values * values, 0, keepdims=True), 1, keepdims=True)


def sum_adapter(came):
    def kernel(came_ref, total_ref, square_ref):
        total = sum_parts(came_ref)
        total_ref[...] = total
        square_ref[...] = square_sum(total)

    return pl.pallas_call(
        kernel,
        out_shape=[jax.ShapeDtypeStruct((PART_ROWS, LANES), F32), jax.ShapeDtypeStruct((1, 1), F32)],
        compiler_params=params_for(32),
        name="sum_adapter",
    )(came)


def sum_coupling(came, squares, loss_part, copies):
    def kernel(came_ref, square_ref, loss_ref, group_ref, bias_ref, pair_ref):
        total = sum_parts(came_ref)
        group_ref[...] = total[:GROUP_ROWS]
        bias_ref[...] = total[GROUP_ROWS:]
        squares = square_ref[...] + square_sum(total)
        lane = lax.broadcasted_iota(jnp.int32, (1, LANES), 1)
        pair = jnp.where(lane == 0, squares, jnp.where(lane == 1, loss_ref[...], 0.0))
        pair_ref[...] = jnp.broadcast_to(pair[None], pair_ref.shape)

    return pl.pallas_call(
        kernel,
        out_shape=[
            jax.ShapeDtypeStruct((GROUP_ROWS, LANES), F32),
            jax.ShapeDtypeStruct((8, LANES), F32),
            jax.ShapeDtypeStruct((copies, 1, LANES), F32),
        ],
        name="sum_coupling",
    )(came, squares, loss_part)


def own_blocks_of(adapter_total, coupling_groups):
    def kernel(total_ref, *refs):
        group_refs, blocks_ref = refs[:-1], refs[-1]
        for group in range(PART_GROUPS):
            total = total_ref[group * GROUP_ROWS : (group + 1) * GROUP_ROWS] + group_refs[group][...]
            main, rest = total[:BLOCK], unfold_half(total[BLOCK:], False)
            lane = lane_of(main)
            pieces = (
                main,
                roll(main, 80),
                jnp.where(lane < 32, roll(main, 32), roll(rest, 32)),
                roll(rest, 112),
            )
            for j, values in enumerate(pieces):
                blocks_ref[4 * group + j] = values[:, :BLOCK]

    return pl.pallas_call(
        kernel,
        out_shape=jax.ShapeDtypeStruct((4 * PART_GROUPS, BLOCK, BLOCK), F32),
        name="own_blocks",
    )(adapter_total, *coupling_groups)


GROUP = 256
HEADS_IN = GROUP // HEAD_DIM
GROUPS = D // GROUP
FF = 3072
TILE = 512
TILES = FF // TILE
STEP_ROWS = 256
SMALL_ROWS = 32


def rows_of(count, size):
    return [slice(at, at + min(size, count)) for at in range(0, count, size)]


def shape_of(*dims, kind=F32):
    return jax.ShapeDtypeStruct(dims, kind)


class Mover:
    def __init__(self, ins, in_bufs, in_sems, outs, out_bufs, out_sems):
        self.ins = {
            name: pltpu.make_async_copy(ref, in_bufs[name], in_sems.at[i])
            for i, (name, ref) in enumerate(ins.items())
        }
        self.outs = {
            name: pltpu.make_async_copy(out_bufs[name], ref, out_sems.at[i])
            for i, (name, ref) in enumerate(outs.items())
        }
        self.in_bufs, self.out = in_bufs, out_bufs
        self.started, self.waited, self.sent = [], [], []

    def start(self, *names):
        for name in names or [n for n in self.ins if n not in self.started]:
            self.ins[name].start()
            self.started.append(name)

    def get(self, name):
        if name not in self.waited:
            self.ins[name].wait()
            self.waited.append(name)
        return self.in_bufs[name]

    def send(self, *names):
        for name in names:
            self.outs[name].start()
            self.sent.append(name)

    def finish(self):
        self.send(*[name for name in self.outs if name not in self.sent])
        for name in self.ins:
            self.get(name)
        for name in self.sent:
            self.outs[name].wait()


def moved_call(body, scalars, ins, outs, pairs, scratch, mebibytes, name, raw_outs=()):
    in_names, out_names = list(ins), list(outs)

    def kernel(*refs):
        refs = list(refs)

        def take(count):
            taken, refs[:] = refs[:count], refs[count:]
            return taken

        scalar_refs = take(len(scalars))
        in_hbm = dict(zip(in_names, take(len(ins))))
        pair_refs = [tuple(take(2)) for _ in pairs]
        out_hbm = dict(zip(out_names, take(len(outs))))
        raw_refs = take(len(raw_outs))
        in_bufs = dict(zip(in_names, take(len(ins))))
        out_bufs = dict(zip(out_names, take(len(outs))))
        in_sems, out_sems = take(2)
        move = Mover(in_hbm, in_bufs, in_sems, out_hbm, out_bufs, out_sems)
        body(move, scalar_refs, pair_refs, raw_refs, refs)
        move.finish()

    hbm = pl.BlockSpec(memory_space=pltpu.HBM)
    buffers = [pltpu.VMEM(value.shape, value.dtype) for value in (*ins.values(), *outs.values())]
    results = pl.pallas_call(
        kernel,
        in_specs=[pl.BlockSpec(memory_space=pltpu.SMEM)] * len(scalars) + [hbm] * (len(ins) + 2 * len(pairs)),
        out_specs=[hbm] * (len(outs) + len(raw_outs)),
        out_shape=[*outs.values(), *raw_outs],
        scratch_shapes=buffers
        + [pltpu.SemaphoreType.DMA((len(ins),)), pltpu.SemaphoreType.DMA((max(len(outs), 1),))]
        + list(scratch),
        compiler_params=params_for(mebibytes),
        name=name,
    )(*scalars, *ins.values(), *[w for pair in pairs for w in pair])
    return dict(zip(out_names, results)), results[len(out_names) :]


def start_copy(pair, section, window, target, sem):
    own, came = pair
    here = lax.axis_index("section") == section

    @pl.when(here)
    def _():
        pltpu.make_async_copy(own.at[window], target, sem).start()

    @pl.when(jnp.logical_not(here))
    def _():
        pltpu.make_async_copy(came.at[window], target, sem).start()


def wait_copy(pair, window, target, sem):
    pltpu.make_async_copy(pair[0].at[window], target, sem).wait()


def qkv_window(group, part):
    return 0, slice(None), pl.ds(part * D + group * GROUP, GROUP)


def qkv_buffers():
    return [pltpu.VMEM((GROUPS, 3, D, GROUP), BF16), pltpu.SemaphoreType.DMA((GROUPS, 3))]


def start_qkv(pair, section, buffers):
    for group in range(GROUPS):
        for part in range(3):
            start_copy(pair, section, qkv_window(group, part), buffers[0].at[group, part], buffers[1].at[group, part])


def wait_qkv(pair, buffers, group, part):
    wait_copy(pair, qkv_window(0, 0), buffers[0].at[group, part], buffers[1].at[group, part])


UP_WINDOWS = [(0, slice(None), slice(j * TILE, (j + 1) * TILE)) for j in range(TILES)]
DOWN_WINDOWS = [(0, slice(j * TILE, (j + 1) * TILE), slice(None)) for j in range(TILES)]
OUT_WINDOW = (0, slice(None), slice(None))


def rest_buffers():
    return [
        pltpu.VMEM((D, D), BF16),
        pltpu.VMEM((TILES, D, TILE), BF16),
        pltpu.VMEM((TILES, TILE, D), BF16),
        pltpu.SemaphoreType.DMA((2 * TILES + 1,)),
    ]


def start_out(pairs, section, buffers):
    start_copy(pairs[0], section, OUT_WINDOW, buffers[0], buffers[3].at[2 * TILES])


def start_tiles(pairs, section, buffers):
    for j in range(TILES):
        start_copy(pairs[1], section, UP_WINDOWS[j], buffers[1].at[j], buffers[3].at[j])
        start_copy(pairs[2], section, DOWN_WINDOWS[j], buffers[2].at[j], buffers[3].at[TILES + j])


def wait_out(pairs, buffers):
    wait_copy(pairs[0], OUT_WINDOW, buffers[0], buffers[3].at[2 * TILES])


def wait_up(pairs, buffers, tile):
    wait_copy(pairs[1], UP_WINDOWS[0], buffers[1].at[tile], buffers[3].at[tile])


def wait_down(pairs, buffers, tile):
    wait_copy(pairs[2], DOWN_WINDOWS[0], buffers[2].at[tile], buffers[3].at[TILES + tile])


def across(values):
    return jnp.broadcast_to(values, (values.shape[0], LANES))


def group_columns(group):
    return pl.ds(pl.multiple_of(group * GROUP, GROUP), GROUP)


def tile_columns(tile):
    return pl.ds(pl.multiple_of(tile * TILE, TILE), TILE)


def head_mask(values, head):
    lane = lax.broadcasted_iota(jnp.int32, values.shape, 1)
    return (lane >= head * HEAD_DIM) & (lane < (head + 1) * HEAD_DIM)


def only_head(values, head):
    return jnp.where(head_mask(values, head), values, jnp.zeros_like(values))


def scaled_query(query):
    return low(query.astype(F32) * HEAD_DIM**-0.5)


def key_bias(length, shape, axis):
    return jnp.where(lax.broadcasted_iota(jnp.int32, shape, axis) < length, 0.0, -1e30)


def softmax_rows(scores):
    highest = jnp.max(scores, 1, keepdims=True)
    exponent = jnp.exp(scores - highest)
    total = jnp.sum(exponent, 1, keepdims=True)
    return low(exponent * (1.0 / total)), highest + jnp.log(total)


def branch_rows(low_in, weights):
    active, slope = gelu_both(matmul(low_in, weights[0]) + weights[1])
    active = low(active)
    return matmul(active, weights[2]) + weights[3], active, low(slope)


PARAMS = ("down", "bias_down", "up", "bias_up")


def adapter_of(move, section):
    return [move.get("a_" + name)[section] for name in PARAMS]


def coupling_of(move, section):
    return [move.get("c_" + name)[section] for name in PARAMS]


def rest_rows(move, tag, rows, section, hidden, mixed, finish, scratch, pairs, buffers, after_loop=None):
    att_low, acc, u_even, u_odd, g_even, g_odd = scratch
    gain = lambda i: move.get("norms")[section, i : i + 1]
    keep = lambda name: move.out[tag + name]
    parts = rows_of(rows, STEP_ROWS)
    wait_out(pairs, buffers)
    for part in parts:
        first = hidden[part] + matmul(mixed[part], buffers[0][...])
        values, (normal, inverse) = layer_norm(first, gain(2), gain(3))
        acc[part] = values
        att_low[part] = low(values)
        keep("n1")[part] = normal
        keep("i1")[part] = across(inverse)
    move.send(tag + "n1", tag + "i1")
    wait_up(pairs, buffers, 0)
    for part in parts:
        u_even[part] = matmul(att_low[part], buffers[1][0])

    def turn(j, carry):
        even, odd = 2 * j, 2 * j + 1
        after = jnp.minimum(even + 2, TILES - 1)
        wait_down(pairs, buffers, even)
        wait_up(pairs, buffers, odd)
        wait_down(pairs, buffers, odd)

        @pl.when(even + 2 < TILES)
        def _():
            wait_up(pairs, buffers, even + 2)

        for now, u_now, g_now, later, u_later in (
            (even, u_even, g_even, odd, u_odd),
            (odd, u_odd, g_odd, after, u_even),
        ):
            for part in parts:
                for small in rows_of(part.stop - part.start, SMALL_ROWS):
                    at = slice(part.start + small.start, part.start + small.stop)
                    active, slope = gelu_both(u_now[at])
                    g_now[at] = low(active)
                    keep("slope")[at, tile_columns(now)] = low(slope)
                u_later[part] = matmul(att_low[part], buffers[1][later])
                acc[part] += matmul(g_now[part], buffers[2][now])
        return carry

    lax.fori_loop(0, TILES // 2, turn, 0)
    if after_loop is not None:
        after_loop()
    move.send(tag + "slope")
    adapter = adapter_of(move, section)
    for part in parts:
        summed = acc[part]
        low_in = low(summed)
        out, active, slope = branch_rows(low_in, adapter)
        keep("lin")[part], keep("act")[part], keep("bslope")[part] = low_in, active, slope
        values, (normal, inverse) = layer_norm(summed + out, gain(4), gain(5))
        keep("n2")[part], keep("i2")[part] = normal, across(inverse)
        finish(part, values)
    move.send(*[tag + name for name in ("lin", "act", "bslope", "n2", "i2")])


def kept_shapes(tag, rows):
    wide, thin = shape_of(rows, D), shape_of(rows, LANES)
    kept = {"n1": wide, "i1": thin, "slope": shape_of(rows, FF, kind=BF16)}
    kept |= {"lin": shape_of(rows, D, kind=BF16), "act": shape_of(rows, BOT, kind=BF16)}
    kept |= {"bslope": shape_of(rows, BOT, kind=BF16), "n2": wide, "i2": thin}
    return {tag + name: shape for name, shape in kept.items()}


def branch_shapes(tag, rows):
    sizes = {"lin": HALF, "act": INV_H, "bslope": INV_H}
    return {tag + name: shape_of(rows, size, kind=BF16) for name, size in sizes.items()}


def forward_kernel(ins, scalars, pairs, parts, slots):
    some_low = lambda *dims: shape_of(*dims, kind=BF16)
    outs = {"target_rows": shape_of(COUNT, D)}
    outs |= branch_shapes("f_", SEQ) | branch_shapes("g_", SEQ)
    outs |= {"q0": some_low(SEQ, D), "k0": some_low(SEQ, D), "v0": some_low(SEQ, D)}
    outs |= {"lse0": shape_of(GROUPS, 8, SEQ)}
    outs |= kept_shapes("x_", SEQ)
    outs |= {"q1": some_low(COUNT, D), "k1": some_low(SEQ, D), "v1": some_low(SEQ, D)}
    outs |= {"lse1": shape_of(GROUPS, HEADS_IN * COUNT, LANES)}
    outs |= kept_shapes("y_", COUNT)
    outs |= branch_shapes("p_", COUNT) | branch_shapes("r_", COUNT)
    outs |= {"nh": shape_of(COUNT, D), "ih": shape_of(COUNT, LANES), "normed": some_low(COUNT, D)}

    def body(move, scalar_refs, pair_refs, raw_refs, scratch):
        length = scalar_refs[0][0]
        hidden, x_low, s_even, s_odd, p_even, p_odd, lse_buf, mixed, section_out = scratch[:9]
        at_spots, at_low, mixed_1 = scratch[9:12]
        rest_scratch, qkv_0, qkv_1, rest_w = scratch[12:18], scratch[18:20], scratch[20:22], scratch[22:26]
        row_sems = scratch[26]
        qkv_pair, rest_pairs = pair_refs[0], pair_refs[1:]
        out = move.out
        norm = lambda s, i: move.get("norms")[s, i : i + 1]

        move.start("came", "spot", "extra", "pos", "norms")
        move.start(*["c_" + name for name in PARAMS])
        start_qkv(qkv_pair, 0, qkv_0)
        start_out(rest_pairs, 0, rest_w)
        move.start(*["a_" + name for name in PARAMS], "chosen")
        start_tiles(rest_pairs, 0, rest_w)
        start_qkv(qkv_pair, 1, qkv_1)

        came, spot, extra = move.get("came"), move.get("spot"), move.get("extra")

        def rows_at(part):
            lane = lax.broadcasted_iota(jnp.int32, (part.stop - part.start, parts * slots), 1)
            hits = (spot[part][:, :1] == lane).astype(BF16)
            return matmul(hits, came[...]) + extra[part]

        out["target_rows"][...] = rows_at(slice(SEQ, SEQ + COUNT))
        move.send("target_rows")
        one, two = coupling_of(move, 0), coupling_of(move, 1)
        for part in rows_of(SEQ, STEP_ROWS):
            started, _ = layer_norm(rows_at(part) + move.get("pos")[part].astype(F32), norm(0, 0), norm(0, 1))
            left, right = started[:, :HALF], started[:, HALF:]
            low_one = low(right)
            added, active, slope = branch_rows(low_one, one)
            out["f_lin"][part], out["f_act"][part], out["f_bslope"][part] = low_one, active, slope
            left = left + added
            low_two = low(left)
            added, active, slope = branch_rows(low_two, two)
            out["g_lin"][part], out["g_act"][part], out["g_bslope"][part] = low_two, active, slope
            right = right + added
            hidden[part, :HALF] = left
            hidden[part, HALF:] = right
            x_low[part, :HALF] = low_two
            x_low[part, HALF:] = low(right)
        move.send(*[tag + name for tag in ("f_", "g_") for name in ("lin", "act", "bslope")])

        lse_buf[...] = jnp.zeros((SEQ, LANES), F32)

        def attend(group, carry):
            columns = group_columns(group)
            for part, name in enumerate(("q0", "k0", "v0")):
                wait_qkv(qkv_pair, qkv_0, group, part)
                out[name][:, columns] = low(matmul(x_low[...], qkv_0[0][group, part]))
            query = scaled_query(out["q0"][:, columns])
            key, value = out["k0"][:, columns], out["v0"][:, columns]
            bias = key_bias(length, (1, SEQ), 1)
            lane = lax.broadcasted_iota(jnp.int32, (SMALL_ROWS * 2, LANES), 1)
            joined = jnp.zeros((SEQ, GROUP), F32)
            for head in range(HEADS_IN):
                scores, soft_buf = ((s_even, p_even), (s_odd, p_odd))[head % 2]
                scores[...] = matmul_t(only_head(query, head), key)
                for rows in rows_of(SEQ, SMALL_ROWS * 2):
                    soft, lse = softmax_rows(scores[rows] + bias)
                    soft_buf[rows] = soft
                    lse_buf[rows] = jnp.where(lane == head, lse, lse_buf[rows])
                joined = jnp.where(head_mask(joined, head), matmul(soft_buf[...], value), joined)
            mixed[:, columns] = low(joined)
            out["lse0"][group] = jnp.transpose(lse_buf[...])[:8]
            return carry

        lax.fori_loop(0, GROUPS, attend, 0)
        move.send("q0", "k0", "v0", "lse0")

        def to_section_out(part, values):
            section_out[part] = low(values)

        def next_weights():
            start_out(rest_pairs, 1, rest_w)
            start_tiles(rest_pairs, 1, rest_w)

        rest_rows(
            move, "x_", SEQ, 0, hidden, mixed, to_section_out, rest_scratch, rest_pairs, rest_w, next_weights
        )

        at_spots[...] = matmul(move.get("chosen")[...], section_out[...])
        at_low[...] = low(at_spots[...])

        def attend_spots(group, carry):
            columns = group_columns(group)
            for part, name in enumerate(("q1", "k1", "v1")):
                wait_qkv(qkv_pair, qkv_1, group, part)
                source = at_low if part == 0 else section_out
                out[name][:, columns] = low(matmul(source[...], qkv_1[0][group, part]))
            query = scaled_query(out["q1"][:, columns])
            query = jnp.concatenate([only_head(query, head) for head in range(HEADS_IN)], 0)
            bias = key_bias(length, (1, SEQ), 1)
            soft, lse = softmax_rows(matmul_t(query, out["k1"][:, columns]) + bias)
            out["lse1"][group] = across(lse)
            every = matmul(soft, out["v1"][:, columns])
            joined = every[:COUNT]
            for head in range(1, HEADS_IN):
                joined = jnp.where(head_mask(joined, head), every[head * COUNT : (head + 1) * COUNT], joined)
            mixed_1[:, columns] = low(joined)
            return carry

        lax.fori_loop(0, GROUPS, attend_spots, 0)
        move.send("q1", "k1", "v1", "lse1")

        def to_normed(part, values):
            left, right = values[:, :HALF], values[:, HALF:]
            low_two = low(left)
            taken, active, slope = branch_rows(low_two, two)
            out["r_lin"][...], out["r_act"][...], out["r_bslope"][...] = low_two, active, slope
            right = right - taken
            low_one = low(right)
            taken, active, slope = branch_rows(low_one, one)
            out["p_lin"][...], out["p_act"][...], out["p_bslope"][...] = low_one, active, slope
            left = left - taken
            values, (normal, inverse) = layer_norm(jnp.concatenate([left, right], 1), norm(1, 0), norm(1, 1))
            out["nh"][...], out["ih"][...], out["normed"][...] = normal, across(inverse), low(values)

        rest_rows(move, "y_", COUNT, 1, at_spots, mixed_1, to_normed, rest_scratch, rest_pairs, rest_w)
        copies = [
            pltpu.make_async_copy(out["normed"], raw_refs[0].at[part], row_sems.at[part]) for part in range(parts)
        ]
        for copy in copies:
            copy.start()
        for copy in copies:
            copy.wait()

    buffer = lambda *dims: pltpu.VMEM(dims, F32)
    buffer_low = lambda *dims: pltpu.VMEM(dims, BF16)
    scratch = [buffer(SEQ, D), buffer_low(SEQ, D), buffer(SEQ, SEQ), buffer(SEQ, SEQ)]
    scratch += [buffer_low(SEQ, SEQ), buffer_low(SEQ, SEQ), buffer(SEQ, LANES)]
    scratch += [buffer_low(SEQ, D), buffer_low(SEQ, D)]
    scratch += [buffer(COUNT, D), buffer_low(COUNT, D), buffer_low(COUNT, D)]
    scratch += [buffer_low(SEQ, D), buffer(SEQ, D), buffer(SEQ, TILE), buffer(SEQ, TILE)]
    scratch += [buffer_low(SEQ, TILE), buffer_low(SEQ, TILE)]
    scratch += qkv_buffers() + qkv_buffers() + rest_buffers()
    scratch += [pltpu.SemaphoreType.DMA((parts,))]
    raw = [shape_of(parts, COUNT, D, kind=BF16)]
    kept, (rows,) = moved_call(body, scalars, ins, outs, pairs, scratch, 58, "forward", raw)
    return kept, rows


def column_sum(values):
    return jnp.sum(values.astype(F32), 0, keepdims=True)


def branch_grads(grad_low, kept, weights, out_refs):
    low_in, active, slope = kept
    hidden_grad = low(matmul_t(grad_low, weights[2]) * slope.astype(F32))
    out_refs[0][...] = inner_rows(low_in, hidden_grad)
    out_refs[1][...] = column_sum(hidden_grad)
    out_refs[2][...] = inner_rows(active, grad_low)
    out_refs[3][...] = column_sum(grad_low)
    return hidden_grad


ADAPTER_GRADS = ((D, BOT), (1, BOT), (BOT, D), (1, D))
COUPLING_GRADS = ((HALF, INV_H), (1, INV_H), (INV_H, HALF), (1, HALF))


def branch_kept(move, tag):
    return [move.get(tag + name)[...] for name in ("lin", "act", "bslope")]


def rest_back_rows(move, tag, rows, section, incoming, scratch, pairs, buffers, grad_refs, results, packing=None):
    summed_low, acc, second_low = scratch
    start_ref, mixed_ref = results
    gain = lambda i: move.get("norms")[section, i : i + 1]
    kept = lambda name: move.get(tag + name)
    parts = rows_of(rows, STEP_ROWS)
    adapter = [move.get("a_" + name)[section] for name in PARAMS[::2]]
    adapter = [adapter[0], None, adapter[1]]
    for part in parts:
        second = norm_back(incoming(part), (kept("n2")[part], kept("i2")[part, :1]), gain(4))
        acc[part] = second
        second_low[part] = low(second)
    hidden_grad = branch_grads(second_low[:rows], branch_kept(move, tag), adapter, grad_refs)
    for part in parts:
        total = acc[part] + matmul_t(hidden_grad[part], adapter[0])
        acc[part] = total
        summed_low[part] = low(total)
    if packing is not None:
        packing()
    slope = kept("slope")

    def turn(j, carry):
        for now in (2 * j, 2 * j + 1):
            wait_up(pairs, buffers, now)
            wait_down(pairs, buffers, now)
        for now in (2 * j, 2 * j + 1):
            for part in parts:
                inner = matmul_t(summed_low[part], buffers[2][now])
                inner = low(inner * slope[part, tile_columns(now)].astype(F32))
                acc[part] += matmul_t(inner, buffers[1][now])
        return carry

    lax.fori_loop(0, TILES // 2, turn, 0)
    wait_out(pairs, buffers)
    for part in parts:
        start = norm_back(acc[part], (kept("n1")[part], kept("i1")[part, :1]), gain(2))
        start_ref[part] = start
        mixed_ref[part] = low(matmul_t(low(start), buffers[0][...]))


def backward_kernel(ins, scalars, pairs, packed):
    parts = ins["merged"].shape[0]
    outs = {"loss": shape_of(1, LANES)}
    outs |= {f"head{i}": shape_of(*dims) for i, dims in enumerate(COUPLING_GRADS * 2)}
    outs |= {f"bias{s}{i}": shape_of(1, size) for s in range(MICRO) for i, size in enumerate((BOT, D))}
    if packed:
        chunks = shape_of(COUPLING_GROUPS, PART_ROWS, LANES, kind=BF16)
        outs |= {"own": chunks, "other": chunks}
    else:
        outs |= {f"matrix{s}{i}": shape_of(*MATRICES[i]) for s in range(MICRO) for i in range(2)}
    outs |= {"start": shape_of(SEQ, D), "mixed": shape_of(SEQ, D, kind=BF16)}

    def body(move, scalar_refs, pair_refs, raw_refs, scratch):
        length = scalar_refs[0][0]
        rest_scratch, spot, mixed_1, acc_1, section_grad = scratch[:3], *scratch[3:7]
        qkv_w, rest_w, refs = scratch[7:9], scratch[9:13], scratch[13:]
        qkv_pair, rest_pairs = pair_refs[0], pair_refs[1:]
        out = move.out
        norm = lambda s, i: move.get("norms")[s, i : i + 1]

        move.start("merged", "normed", "target_rows", "row_weights", "weight_sum", "nh", "ih", "norms")
        move.start(*["c_" + name for name in PARAMS[::2]])
        move.start(*[tag + name for tag in ("p_", "r_") for name in ("lin", "act", "bslope")])
        move.start(*["a_" + name for name in PARAMS[::2]])
        move.start(*[name for name in move.ins if name.startswith("y_")])
        start_tiles(rest_pairs, 1, rest_w)
        start_out(rest_pairs, 1, rest_w)
        start_qkv(qkv_pair, 1, qkv_w)
        move.start()

        def from_head(part):
            merged = move.get("merged")
            stats = merged[:, :, D:].astype(F32)
            highest = jnp.sum(stats[:, :, :3], 2, keepdims=True)
            totals = jnp.sum(stats[:, :, 3:6], 2, keepdims=True)
            top = jnp.max(highest, 0)
            factor = jnp.exp(highest - top[None])
            total = jnp.sum(totals * factor, 0)
            expected = jnp.zeros((COUNT, D), F32)
            for i in range(parts):
                expected += merged[i, :, :D].astype(F32) * (factor[i] / total)
            target = move.get("target_rows")[...]
            target_logit = jnp.sum(move.get("normed")[...].astype(F32) * target, 1, keepdims=True)
            weight = move.get("row_weights")[...]
            row_losses = weight[:, :1] * (top + jnp.log(total) - target_logit)
            out["loss"][...] = across(jnp.sum(row_losses, 0, keepdims=True))
            normed_grad = (weight / move.get("weight_sum")[...])[:, :1] * (expected - target)
            kept = (move.get("nh")[...], move.get("ih")[:, :1])
            restored = norm_back(normed_grad, kept, norm(1, 0))
            left, right = restored[:, :HALF], restored[:, HALF:]
            one, two = (
                [move.get("c_down")[s], None, move.get("c_up")[s]] for s in range(MICRO)
            )
            grads = [out[f"head{i}"] for i in range(8)]
            hidden = branch_grads(low(-left), branch_kept(move, "p_"), one, grads[:4])
            right = right + matmul_t(hidden, one[0])
            hidden = branch_grads(low(-right), branch_kept(move, "r_"), two, grads[4:])
            left = left + matmul_t(hidden, two[0])
            return jnp.concatenate([left, right], 1)

        def grads_of(section):
            if packed:
                return (refs[0], out[f"bias{section}0"], refs[1], out[f"bias{section}1"])
            return (
                out[f"matrix{section}0"], out[f"bias{section}0"], out[f"matrix{section}1"], out[f"bias{section}1"],
            )

        def pack_second():
            def store(part, chunk):
                refs[2][part] = chunk

            pack_adapter((refs[0], refs[1]), store)

        def pack_both():
            here = lax.axis_index("section") == 0

            def store(part, chunk):
                arrived = refs[2][part]
                out["own"][part] = jnp.where(here, chunk, arrived)
                out["other"][part] = jnp.where(here, arrived, chunk)

            pack_adapter((refs[0], refs[1]), store)
            move.send("own", "other")

        rest_back_rows(
            move, "y_", COUNT, 1, from_head, rest_scratch, rest_pairs, rest_w, grads_of(1), (spot, mixed_1),
            pack_second if packed else None,
        )
        start_tiles(rest_pairs, 0, rest_w)
        start_out(rest_pairs, 0, rest_w)

        acc_1[...] = jnp.zeros_like(acc_1)
        q_ref, k_ref, v_ref, lse_ref = (move.get(name) for name in ("q1", "k1", "v1", "lse1"))

        def attend_back(group, carry):
            columns = group_columns(group)
            stack = lambda values: jnp.concatenate([only_head(values, h) for h in range(HEADS_IN)], 0)
            query = stack(scaled_query(q_ref[:, columns]))
            mixed = stack(mixed_1[:, columns])
            key, value = k_ref[:, columns], v_ref[:, columns]
            scores = matmul_t(query, key) + key_bias(length, (1, SEQ), 1)
            soft = jnp.exp(scores - lse_ref[group][:, :1])
            soft_grad = matmul_t(mixed, value)
            delta = jnp.sum(soft_grad * soft, 1, keepdims=True)
            score_grad = low(soft * (soft_grad - delta))
            every = matmul(score_grad, key)
            query_grad = every[:COUNT]
            for head in range(1, HEADS_IN):
                query_grad = jnp.where(
                    head_mask(query_grad, head), every[head * COUNT : (head + 1) * COUNT], query_grad
                )
            query_grad = low(query_grad * HEAD_DIM**-0.5)
            key_grad = low(inner_rows(score_grad, query))
            value_grad = low(inner_rows(low(soft), mixed))
            for part in range(3):
                wait_qkv(qkv_pair, qkv_w, group, part)
            spot[...] += matmul_t(query_grad, qkv_w[0][group, 0])
            acc_1[...] += matmul_t(key_grad, qkv_w[0][group, 1]) + matmul_t(value_grad, qkv_w[0][group, 2])
            return carry

        lax.fori_loop(0, GROUPS, attend_back, 0)
        placed = jnp.dot(
            move.get("chosen_t")[...], spot[...], precision=HIGHEST, preferred_element_type=F32
        )
        section_grad[...] = low(acc_1[...] + placed)

        rest_back_rows(
            move, "x_", SEQ, 0, lambda part: section_grad[part].astype(F32), rest_scratch, rest_pairs, rest_w,
            grads_of(0), (out["start"], out["mixed"]), pack_both if packed else None,
        )

    scratch = [pltpu.VMEM((SEQ, D), BF16), pltpu.VMEM((SEQ, D), F32), pltpu.VMEM((SEQ, D), BF16)]
    scratch += [pltpu.VMEM((COUNT, D), F32), pltpu.VMEM((COUNT, D), BF16), pltpu.VMEM((SEQ, D), F32)]
    scratch += [pltpu.VMEM((SEQ, D), BF16)] + qkv_buffers() + rest_buffers()
    if packed:
        scratch += [pltpu.VMEM((D, BOT), F32), pltpu.VMEM((BOT, D), F32)]
        scratch += [pltpu.VMEM((COUPLING_GROUPS, PART_ROWS, LANES), BF16)]
    return moved_call(body, scalars, ins, outs, pairs, scratch, 58, "backward")[0]


def first_backward(ins, scalars, pairs, packed):
    if packed:
        dims = (COUPLING_GROUPS, GROUP_ROWS + 8, LANES)
        outs = {"own": shape_of(*dims), "other": shape_of(*dims, kind=BF16)}
    else:
        outs = {f"grad{i}": shape_of(*dims) for i, dims in enumerate(COUPLING_GRADS * 2)}

    def body(move, scalar_refs, pair_refs, raw_refs, scratch):
        length = scalar_refs[0][0]
        acc = move.in_bufs["start"]
        s_even, s_odd, d_even, d_odd, p_even, p_odd, ds_even, ds_odd = scratch[:8]
        qkv_w, refs = scratch[8:10], scratch[10:]
        out = move.out
        move.start("q0", "k0", "v0", "lse0", "mixed")
        start_qkv(pair_refs[0], 0, qkv_w)
        move.start()
        q_ref, k_ref, v_ref, lse_ref, mixed_ref = (
            move.get(name) for name in ("q0", "k0", "v0", "lse0", "mixed")
        )
        move.get("start")

        def attend_back(group, carry):
            columns = group_columns(group)
            query = scaled_query(q_ref[:, columns])
            key, value, mixed = k_ref[:, columns], v_ref[:, columns], mixed_ref[:, columns]
            lse_rows = lse_ref[group]
            key_t = jnp.transpose(key)
            key_grad = jnp.zeros((SEQ, GROUP), F32)
            value_grad = jnp.zeros((SEQ, GROUP), F32)
            query_parts = []
            for head in range(HEADS_IN):
                s_buf, d_buf, p_low, ds_low = (
                    (s_even, d_even, p_even, ds_even),
                    (s_odd, d_odd, p_odd, ds_odd),
                )[head % 2]
                s_buf[...] = matmul_t(only_head(key, head), query)
                d_buf[...] = matmul_t(only_head(value, head), mixed)
                lse_row = lse_rows[head : head + 1]
                delta = jnp.zeros((8, SEQ), F32)
                for rows in rows_of(SEQ, SMALL_ROWS):
                    valid = lax.broadcasted_iota(jnp.int32, (SMALL_ROWS, 1), 0) + rows.start < length
                    bias = jnp.where(valid, 0.0, -1e30)
                    soft = jnp.exp(s_buf[rows] + bias - lse_row)
                    s_buf[rows] = soft
                    p_low[rows] = low(soft)
                    product = soft * d_buf[rows]
                    for at in range(0, SMALL_ROWS, 8):
                        delta = delta + product[at : at + 8]
                delta = jnp.sum(delta, 0, keepdims=True)
                for rows in rows_of(SEQ, SMALL_ROWS):
                    ds_low[rows] = low(s_buf[rows] * (d_buf[rows] - delta))
                value_grad += matmul(p_low[...], only_head(mixed, head))
                key_grad += matmul(ds_low[...], only_head(query, head))
                query_parts.append(matmul(key_t[head * HEAD_DIM : (head + 1) * HEAD_DIM], ds_low[...]))
            query_grad = jnp.transpose(jnp.concatenate(query_parts, 0)) * HEAD_DIM**-0.5
            for part, grad in enumerate((query_grad, key_grad, value_grad)):
                wait_qkv(pair_refs[0], qkv_w, group, part)
                acc[...] += matmul_t(low(grad), qkv_w[0][group, part])
            return carry

        lax.fori_loop(0, GROUPS, attend_back, 0)
        one, two = ([move.get("c_down")[s], None, move.get("c_up")[s]] for s in range(MICRO))
        grads = refs if packed else [out[f"grad{i}"] for i in range(8)]
        hidden = branch_grads(low(acc[:, HALF:]), branch_kept(move, "g_"), two, grads[4:])
        left = acc[:, :HALF] + matmul_t(hidden, two[0])
        branch_grads(low(left), branch_kept(move, "f_"), one, grads[:4])
        for i, ref in enumerate(grads):
            ref[...] += move.get(f"head{i}")[...]
        if not packed:
            return
        here = lax.axis_index("section")
        for s in range(MICRO):
            some = grads[4 * s : 4 * s + 4]
            biases = [move.get(f"bias{s}{i}")[...] for i in range(2)]
            tiles = bias_tiles(*biases, some[1][...], some[3][...])

            def store(part, chunk, s=s):
                @pl.when(here == s)
                def _():
                    out["own"][part] = chunk

                @pl.when(here != s)
                def _():
                    out["other"][part] = low(chunk)

            pack_coupling((some[0], some[2]), tiles, sum(BIASES) // COUPLING_GROUPS, store)

    scratch = [pltpu.VMEM((SEQ, SEQ), F32)] * 4 + [pltpu.VMEM((SEQ, SEQ), BF16)] * 4 + qkv_buffers()
    if packed:
        scratch += [pltpu.VMEM(dims, F32) for dims in COUPLING_GRADS * 2]
    return moved_call(body, scalars, ins, outs, pairs[:1], scratch, 40, "first_backward")[0]


VOCAB_TILE = 1280


def head_kernel(rows, table):
    parts_in, each, _ = rows.shape
    count, vocab = parts_in * each, table.shape[0]
    last = pl.cdiv(vocab, VOCAB_TILE) - 1
    turns = last // 2 + 1
    parts = rows_of(count, STEP_ROWS)

    def kernel(x_hbm, even_ref, odd_ref, after_ref, out_hbm, *refs):
        x_ref, out_ref, acc, top, total, l_even, l_odd, p_even, p_odd, sems = refs
        turn = pl.program_id(0)

        def entries_of(ref, tile):
            row = lax.broadcasted_iota(jnp.int32, (VOCAB_TILE, 1), 0)
            return jnp.where(row < vocab - tile * VOCAB_TILE, ref[...], jnp.zeros_like(ref))

        @pl.when(turn == 0)
        def _():
            copy = pltpu.make_async_copy(x_hbm, x_ref, sems.at[0])
            copy.start()
            acc[...] = jnp.zeros_like(acc)
            top[...] = jnp.full_like(top, -1e30)
            total[...] = jnp.zeros_like(total)
            entries = entries_of(even_ref, 0)
            copy.wait()
            for part in parts:
                l_even[part] = matmul_t(x_ref[part], entries)

        even = entries_of(even_ref, 2 * turn)
        odd = entries_of(odd_ref, 2 * turn + 1)
        after = entries_of(after_ref, 2 * turn + 2)
        for tile, l_now, p_now, now, l_later, later in (
            (2 * turn, l_even, p_even, even, l_odd, odd),
            (2 * turn + 1, l_odd, p_odd, odd, l_even, after),
        ):
            bias = key_bias(vocab - tile * VOCAB_TILE, (1, VOCAB_TILE), 1)
            for part in parts:
                for small in rows_of(STEP_ROWS, SMALL_ROWS):
                    at = slice(part.start + small.start, part.start + small.stop)
                    logits = l_now[at] + bias
                    earlier = top[at]
                    highest = jnp.maximum(earlier, jnp.max(logits, 1, keepdims=True))
                    exponent = jnp.exp(logits - highest)
                    factor = jnp.exp(earlier - highest)
                    top[at] = highest
                    total[at] = total[at] * factor + jnp.sum(exponent, 1, keepdims=True)
                    p_now[at] = low(exponent)
                    acc[at] = acc[at] * factor
                l_later[part] = matmul_t(x_ref[part], later)
                acc[part] += matmul(p_now[part], now)

        @pl.when(turn == turns - 1)
        def _():
            lane = lax.broadcasted_iota(jnp.int32, (count, LANES), 1)
            stats = jnp.zeros((count, LANES), F32)
            pieces = three_low(top[...]) + three_low(total[...])
            for j, piece in enumerate(pieces):
                stats = jnp.where(lane == j, piece.astype(F32), stats)
            out_ref[:, :D] = low(acc[...])
            out_ref[:, D:] = low(stats)
            copy = pltpu.make_async_copy(out_ref, out_hbm, sems.at[1])
            copy.start()
            copy.wait()

    def tile_at(shift):
        return pl.BlockSpec((VOCAB_TILE, D), lambda j: (jnp.minimum(2 * j + shift, last), 0))

    hbm = pl.BlockSpec(memory_space=pltpu.HBM)
    return pl.pallas_call(
        kernel,
        grid=(turns,),
        in_specs=[hbm] + [tile_at(shift) for shift in range(3)],
        out_specs=hbm,
        out_shape=shape_of(count, D + LANES, kind=BF16),
        scratch_shapes=[
            pltpu.VMEM((count, D), BF16),
            pltpu.VMEM((count, D + LANES), BF16),
            pltpu.VMEM((count, D), F32),
            pltpu.VMEM((count, 1), F32),
            pltpu.VMEM((count, 1), F32),
            pltpu.VMEM((count, VOCAB_TILE), F32),
            pltpu.VMEM((count, VOCAB_TILE), F32),
            pltpu.VMEM((count, VOCAB_TILE), BF16),
            pltpu.VMEM((count, VOCAB_TILE), BF16),
            pltpu.SemaphoreType.DMA((2,)),
        ],
        compiler_params=params_for(58),
        name="vocabulary_head",
    )(rows.reshape(count, D), table, table, table).reshape(parts_in, each, D + LANES)


def swap_add(own, other):
    came = lax.ppermute(low(other), "section", [(0, 1), (1, 0)])
    return own + came.astype(F32)


def pick(first_section, both):
    return jnp.where(first_section, both[0], both[1])


def plan_requests(ids, weights, vocab_rows, slots, parts):
    turned = jnp.transpose(ids)

    def kernel(ids_ref, turned_ref, weights_ref, asked_ref, code_ref, spot_ref):
        here = lax.axis_index("section")
        i_index = lax.broadcasted_iota(jnp.int32, (IDS, IDS), 0)
        j_index = lax.broadcasted_iota(jnp.int32, (IDS, IDS), 1)
        earlier, later = j_index < i_index, i_index < j_index

        def owner_of(values):
            return jnp.floor((values.astype(F32) + 0.5) * (1.0 / vocab_rows)).astype(jnp.int32)

        def count(hits, axis):
            return jnp.sum(hits.astype(F32), axis, keepdims=True)

        most = jnp.zeros((1, 1), F32)
        for m in range(MICRO):
            row, col = ids_ref[m : m + 1], turned_ref[:, m : m + 1]
            same_id = row == col
            first_col = count(same_id & earlier, 1) == 0
            first_row = count(same_id & later, 0) == 0
            owner_row, owner_col = owner_of(row), owner_of(col)
            same_owner = owner_row == owner_col
            rank_row = count(same_owner & later & first_col, 0)
            rank_col = count(same_owner & earlier & first_row, 1)
            most = jnp.maximum(most, jnp.max(rank_row, 1, keepdims=True))

            @pl.when(here == m)
            def _():
                slot_row = jnp.sum(jnp.where(same_id & first_col, rank_col, 0.0), 0, keepdims=True)
                slot_col = jnp.sum(jnp.where(same_id & first_row, rank_row, 0.0), 1, keepdims=True)
                slot_row, slot_col = slot_row.astype(jnp.int32), slot_col.astype(jnp.int32)
                code_ref[...] = (owner_row + parts * first_row.astype(jnp.int32)) * 1024 + slot_row
                spot = jnp.where(slot_col < slots, owner_col * slots + slot_col, -1)
                spot_ref[...] = jnp.broadcast_to(spot, (IDS, LANES))
                lane = lax.broadcasted_iota(jnp.int32, (IDS, LANES), 1)
                local = (col - owner_col * vocab_rows).astype(F32)
                wanted = first_col & (slot_col < slots) & (slot_col == lane)
                wanted = jnp.where(wanted, local, 0.0)
                for part in range(parts):
                    asked = jnp.sum(jnp.where(owner_col == part, wanted, 0.0), 0, keepdims=True)
                    asked_ref[part] = asked.astype(jnp.int32)

        rounds = jnp.floor((most + 0.5) * (1.0 / slots)).astype(jnp.int32) + 1
        total = jnp.sum(jnp.sum(weights_ref[...], 0, keepdims=True), 1, keepdims=True)
        lane = lax.broadcasted_iota(jnp.int32, (1, LANES), 1)
        for part in range(parts):
            row = asked_ref[part]
            asked_ref[part] = jnp.where(lane == slots, rounds, jnp.where(lane == slots + 1, total, row))

    return pl.pallas_call(
        kernel,
        out_shape=[
            jax.ShapeDtypeStruct((parts, 1, LANES), jnp.int32),
            jax.ShapeDtypeStruct((1, IDS), jnp.int32),
            jax.ShapeDtypeStruct((IDS, LANES), jnp.int32),
        ],
        compiler_params=params_for(24),
        name="plan_requests",
    )(ids, turned, weights)


def fetch_rows(table, ids, first_section, weights, slots):
    parts = lax.axis_size("dp")
    vocab_rows = table.shape[0]
    asked, code, spot = plan_requests(ids, weights, vocab_rows, slots, parts)
    asked = lax.all_to_all(asked, "dp", 0, 0)[:, 0]
    total_rounds = jnp.max(asked[:, slots])
    weight_sum = jnp.sum(asked[:, slots + 1])

    def answer(asked):
        rows = table.at[asked.reshape(-1)].get(mode="promise_in_bounds").reshape(parts, slots, D)
        return lax.all_to_all(rows, "dp", 0, 0).reshape(parts * slots, D)

    came = answer(asked[:, :slots])

    def more(state):
        return state[0] < total_rounds

    def another(state):
        turn, extra = state
        place, slot = code[0] // 1024, code[0] % 1024
        owner, first = place % parts, place >= parts
        local = pick(first_section, ids) - owner * vocab_rows
        here = slot - turn * slots
        at = jnp.where((here >= 0) & (here < slots), owner * slots + here, -1)
        hits = at[:, None] == jnp.arange(parts * slots)[None, :]
        wanted = jnp.sum(jnp.where(hits & first[:, None], local[:, None], 0), 0).reshape(parts, slots)
        rows = answer(lax.all_to_all(wanted, "dp", 0, 0))
        return turn + 1, extra + matmul(hits.astype(BF16), rows)

    extra = lax.while_loop(more, another, (jnp.int32(1), jnp.zeros((IDS, D), F32)))[1]
    return came, spot, extra, weight_sum.astype(F32)


def three_low(values):
    high = low(values)
    rest = values - high.astype(F32)
    middle = low(rest)
    return [high, middle, low(rest - middle.astype(F32))]


def in_groups(count):
    return lax.axis_size("dp") == COUPLING_GROUPS and count == 4 * PART_GROUPS


def gather_params(master, vector):
    parts = lax.axis_size("dp")
    count, width = master.shape[0], vector.shape[0]
    if in_groups(count):
        own = lax.all_gather(pack_own(master, vector[None]), "dp")
        return unpack_all(own, lax.ppermute(own, "section", [(0, 1), (1, 0)]), width)
    flat = low(jnp.concatenate([master.reshape(-1), vector]))
    gathered = lax.all_gather(flat, ("section", "dp")).reshape(MICRO, parts, -1)
    size = count * BLOCK**2
    all_blocks = gathered[:, :, :size].reshape(MICRO, parts * count, BLOCK, BLOCK)
    all_vectors = gathered[:, :, size:].reshape(MICRO, parts * width)
    arrays = {}
    both = [split_params(all_blocks[s], all_vectors[s]) for s in range(MICRO)]
    for prefix, which in (("a_", 0), ("c_", 1)):
        for i, name in enumerate(PARAMS):
            values = jnp.stack([pair[which][i] for pair in both])
            arrays[prefix + name] = values if i % 2 == 0 else values.astype(F32)[:, None]
    return arrays


def sum_at_owners(grads, loss_part, count):
    parts = lax.axis_size("dp")
    width = sum(BIASES) // parts
    flat = []
    for adapter, coupling in grads:
        blocks, vector = join_params(adapter, coupling)
        flat.append(
            jnp.concatenate([blocks.reshape(parts, count * BLOCK**2), vector.reshape(parts, width)], 1)
        )
    first = lax.axis_index("section") == 0
    summed = swap_add(jnp.where(first, flat[0], flat[1]), jnp.where(first, flat[1], flat[0]))
    owned = jnp.sum(lax.all_to_all(low(summed), "dp", 0, 0).astype(F32), 0)
    blocks = owned[: count * BLOCK**2].reshape(count, BLOCK, BLOCK)
    pair = jnp.stack([jnp.sum(owned * owned), loss_part[0, 0]])
    pair = jnp.pad(pair, (0, LANES - 2))[None, None]
    return blocks, owned[count * BLOCK**2 :], jnp.broadcast_to(pair, (parts * MICRO, 1, LANES))


def to_coupling_owners(group):
    arrived = []
    for place in range(PART_GROUPS):
        route = []
        for part in range(COUPLING_GROUPS):
            owner, at = divmod(ADAPTER_GROUPS + part, PART_GROUPS)
            if at == place:
                route.append((part, owner))
        arrived.append(lax.ppermute(group, "dp", route))
    return arrived


def exact(spec, left, right):
    return jnp.einsum(spec, left, right, precision=HIGHEST)


def update(pair, grad, grad_vector, state):
    master, momentum, stat_left, stat_right, root_left, root_right, vectors, vec_first, vec_second = state
    left_square = exact("nij,nkj->nik", grad, grad)
    right_square = exact("nji,njk->nik", grad, grad)
    turned = exact("nij,njk->nik", exact("nij,njk->nik", root_left, grad), root_right)
    turned_old = exact("nij,njk->nik", exact("nij,njk->nik", root_left, momentum), root_right)

    def kernel(pair_ref, grad_ref, left_ref, right_ref, turned_ref, old_ref, vector_ref, *refs):
        master_ref, momentum_ref, stat_left_ref, stat_right_ref, vectors_ref, first_ref, second_ref = refs[:7]
        outs = refs[7:]
        totals = jnp.sum(pair_ref[...], 0)
        norm = jnp.sqrt(totals[:, :1])
        factor = CLIP_NORM / jnp.maximum(norm, CLIP_NORM)
        outs[9][...] = norm
        outs[10][...] = totals[:, 1:2]
        for n in range(grad_ref.shape[0]):
            clipped = grad_ref[n] * factor
            outs[0][0, n] = clipped
            outs[1][0, n] = FIRST_DECAY * momentum_ref[n] + (1.0 - FIRST_DECAY) * clipped
            square = (1.0 - STAT_DECAY) * factor * factor
            outs[2][0, n] = STAT_DECAY * stat_left_ref[n] + square * left_ref[n]
            outs[3][0, n] = STAT_DECAY * stat_right_ref[n] + square * right_ref[n]
            direction = FIRST_DECAY * old_ref[n] + (1.0 - FIRST_DECAY) * factor * turned_ref[n]
            master_new = master_ref[n] - MAT_RATE * (direction + MAT_DECAY * master_ref[n])
            outs[4][0, n] = master_new
            outs[5][0, n] = low(master_new)
        clipped = vector_ref[...] * factor
        first_new = FIRST_DECAY * first_ref[...] + (1.0 - FIRST_DECAY) * clipped
        second_new = VEC_SECOND * second_ref[...] + (1.0 - VEC_SECOND) * clipped * clipped
        outs[6][...] = first_new
        outs[7][...] = second_new
        corrected_first = first_new / (1.0 - FIRST_DECAY**STEP)
        corrected_second = second_new / (1.0 - VEC_SECOND**STEP)
        outs[8][...] = vectors_ref[...] - VEC_RATE * (
            corrected_first / (jnp.sqrt(corrected_second) + VEC_EPS) + VEC_DECAY * vectors_ref[...]
        )

    blocks = (1,) + grad.shape
    width = vectors.shape
    shapes = [shape_of(*blocks)] * 5 + [shape_of(*blocks, kind=BF16)] + [shape_of(*width)] * 3
    return pl.pallas_call(
        kernel,
        out_shape=shapes + [shape_of(1, 1)] * 2,
        compiler_params=params_for(40),
        name="update",
    )(
        pair, grad, left_square, right_square, turned, turned_old, grad_vector,
        master, momentum, stat_left, stat_right, vectors, vec_first, vec_second,
    )


def shards(
    token_ids,
    lengths,
    positions,
    targets,
    loss_weights,
    embed_table,
    pos_table,
    norm_params,
    base_qkv,
    base_out,
    base_up,
    base_down,
    master,
    momentum,
    stat_left,
    stat_right,
    root_left,
    root_right,
    vectors,
    vec_first,
    vec_second,
):
    parts = lax.axis_size("dp")
    first_section = lax.axis_index("section") == 0
    slots = -(-IDS * 5 // (4 * parts * 16)) * 16

    params = gather_params(master[0], vectors[0])
    swap = [(0, 1), (1, 0)]
    pairs = [(w, lax.ppermute(w, "section", swap)) for w in (base_qkv, base_out, base_up, base_down)]
    came = lax.ppermute(norm_params, "section", swap)
    norms = jnp.concatenate([pick(first_section, (norm_params, came)), pick(first_section, (came, norm_params))])

    ids = jnp.concatenate([token_ids[:, 0], targets[:, 0]], -1)
    came, spot, extra, weight_sum = fetch_rows(embed_table, ids, first_section, loss_weights[:, 0], slots)
    length = pick(first_section, lengths)
    spots = pick(first_section, positions[:, 0])
    row_weights = pick(first_section, loss_weights[:, 0]).astype(F32)
    chosen = (spots[:, None] == jnp.arange(SEQ)[None, :]).astype(BF16)
    chosen_t = (spots[None, :] == jnp.arange(SEQ)[:, None]).astype(F32)

    ins = {"came": came, "spot": spot, "extra": extra, "pos": pos_table, "norms": norms, "chosen": chosen}
    kept, rows = forward_kernel(ins | params, (length,), pairs, parts, slots)

    rows = lax.all_to_all(rows, "dp", 0, 0)
    merged = lax.all_to_all(head_kernel(rows, embed_table), "dp", 0, 0)

    packed = in_groups(master.shape[1])
    matrices = {name: params[name] for name in ("a_down", "a_up", "c_down", "c_up")}
    first_part = ("q0", "k0", "v0", "lse0") + tuple(
        tag + name for tag in ("f_", "g_") for name in ("lin", "act", "bslope")
    )
    ins = {name: value for name, value in kept.items() if name not in first_part}
    ins |= {"merged": merged, "norms": norms, "chosen_t": chosen_t}
    ins |= {
        "row_weights": jnp.broadcast_to(row_weights[:, None], (COUNT, LANES)),
        "weight_sum": jnp.broadcast_to(weight_sum, (1, LANES)),
    }
    back = backward_kernel(ins | matrices, (length,), pairs, packed)
    loss_part = back["loss"][:, :1]
    ins = {name: kept[name] for name in first_part}
    ins |= {name: back[name] for name in ("start", "mixed")}
    ins |= {f"head{i}": back[f"head{i}"] for i in range(8)}
    ins |= {name: matrices[name] for name in ("c_down", "c_up")}
    if packed:
        ins |= {name: back[name] for name in ("bias00", "bias01", "bias10", "bias11")}
        summed = low(swap_add(back["own"].astype(F32), back["other"]))
        summed, ins["mixed"] = lax.optimization_barrier((summed, ins["mixed"]))
        adapter_came = lax.all_to_all(summed, "dp", 0, 0)
        grads = first_backward(ins, (length,), pairs, packed)
        adapter_total, squares = sum_adapter(adapter_came)
        came = lax.all_to_all(low(swap_add(grads["own"], grads["other"])), "dp", 0, 0)
        group, bias, pair = sum_coupling(came, squares, loss_part, parts * MICRO)
        grad = own_blocks_of(adapter_total, to_coupling_owners(group))
        grad_vector = bias[:1, : vectors.shape[1]]
    else:
        grads = first_backward(ins, (length,), pairs, packed)
        both = []
        for s in range(MICRO):
            adapter = [back[f"{kind}{s}{i}"] for i in range(2) for kind in ("matrix", "bias")]
            both.append((adapter, [grads[f"grad{4 * s + i}"] for i in range(4)]))
        grad, grad_vector, pair = sum_at_owners(both, loss_part, master.shape[1])
        grad_vector = grad_vector[None]
    pair = lax.all_to_all(pair, ("dp", "section"), 0, 0)
    state = (master, momentum, stat_left, stat_right, root_left, root_right)
    *outs, grad_norm, loss_sum = update(
        pair, grad, grad_vector, [value[0] for value in state] + [vectors, vec_first, vec_second]
    )
    return (*outs, grad_norm[0, 0], loss_sum[0, 0], weight_sum)


def solution(mesh):
    rows = P(None, "dp", None)
    section = P("section", None, None)
    blocks = P("section", "dp", None, None)
    biases = P("section", "dp")
    return jax.shard_map(
        shards,
        mesh=mesh,
        in_specs=(rows, P(None, "dp"), rows, rows, rows, P("dp", None), P())
        + (section,) * 5
        + (blocks,) * 6
        + (biases,) * 3,
        out_specs=(blocks,) * 6 + (biases,) * 3 + (P(),) * 3,
        check_vma=False,
    )
```

```python
from typing import Any, NamedTuple

import jax
import jax.numpy as jnp
import numpy as np
from jax import lax
from jax.experimental import pallas as pl
from jax.experimental.pallas import tpu as pltpu
from jax.sharding import PartitionSpec as P

D = 768
HEADS = 12
HEAD_DIM = 64
BOT = 384
INV_H = 192
SEQ = 512
COUNT = 32
MICRO = 2
BLOCK = 48
STEP = 10
HALF = 384
IDS = SEQ + COUNT

HIGHEST = lax.Precision.HIGHEST
NORM_EPS = 1e-12
CLIP_NORM = 0.02
FIRST_DECAY = 0.9
STAT_DECAY = 0.99
MAT_RATE = 0.1
MAT_DECAY = 0.01
VEC_RATE = 0.05
VEC_SECOND = 0.999
VEC_EPS = 1e-08
VEC_DECAY = 0.01
F32 = jnp.float32
BF16 = jnp.bfloat16

CDF_SCALE = 0.42 / 2.0**0.5
CDF_POLY = (
    0.2368242366796694,
    0.239585811361218,
    0.1947261443420679,
    0.2687426685879861,
    -0.13052645834187002,
    0.4406726942003943,
    -0.32025628294963193,
    0.07023101752398136,
)


def matmul(left, right):
    return jnp.dot(left, right, preferred_element_type=F32)


def matmul_t(left, right):
    return lax.dot_general(left, right, (((1,), (1,)), ((), ())), preferred_element_type=F32)


def inner_rows(left, right):
    return lax.dot_general(left, right, (((0,), (0,)), ((), ())), preferred_element_type=F32)


def low(values):
    return values.astype(BF16)


def gelu_both(values):
    below = 1.0 + CDF_SCALE * jnp.abs(values)
    ratio = pl.reciprocal(below, approx=True)
    ratio = ratio * (2.0 - below * ratio)
    poly = jnp.full_like(ratio, 0.5 * CDF_POLY[-1])
    for factor in CDF_POLY[-2::-1]:
        poly = poly * ratio + 0.5 * factor
    bell = jnp.exp(-0.5 * values * values)
    tail = bell * (poly * ratio)
    cdf = jnp.where(values < 0, tail, 1.0 - tail)
    return values * cdf, cdf + values * (bell * (2.0 * np.pi) ** -0.5)


def layer_norm(values, gain, shift):
    centered = values - jnp.mean(values, -1, keepdims=True)
    inverse = lax.rsqrt(jnp.mean(centered * centered, -1, keepdims=True) + NORM_EPS)
    normal = centered * inverse
    return normal * gain + shift, (normal, inverse)


def norm_back(incoming, kept, gain):
    normal, inverse = kept
    scaled = incoming * gain
    return inverse * (
        scaled
        - jnp.mean(scaled, -1, keepdims=True)
        - normal * jnp.mean(scaled * normal, -1, keepdims=True)
    )


def to_blocks(matrix):
    rows_in, cols_in = matrix.shape
    return (
        matrix.reshape(rows_in // BLOCK, BLOCK, cols_in // BLOCK, BLOCK)
        .transpose(0, 2, 1, 3)
        .reshape(-1, BLOCK, BLOCK)
    )


def from_blocks(blocks, rows_in, cols_in):
    return (
        blocks.reshape(rows_in // BLOCK, cols_in // BLOCK, BLOCK, BLOCK)
        .transpose(0, 2, 1, 3)
        .reshape(rows_in, cols_in)
    )


def split_params(blocks, vector):
    adapter_count = D * BOT // BLOCK**2
    half_count = HALF * INV_H // BLOCK**2
    split_at = 2 * adapter_count
    adapter = (
        from_blocks(blocks[:adapter_count], D, BOT),
        vector[:BOT],
        from_blocks(blocks[adapter_count:split_at], BOT, D),
        vector[BOT : BOT + D],
    )
    coupling = (
        from_blocks(blocks[split_at : split_at + half_count], HALF, INV_H),
        vector[BOT + D : BOT + D + INV_H],
        from_blocks(blocks[split_at + half_count :], INV_H, HALF),
        vector[BOT + D + INV_H :],
    )
    return adapter, coupling


def join_params(adapter, coupling):
    blocks = jnp.concatenate(
        [to_blocks(adapter[0]), to_blocks(adapter[2]), to_blocks(coupling[0]), to_blocks(coupling[2])]
    )
    return blocks, jnp.concatenate([adapter[1], adapter[3], coupling[1], coupling[3]], 1)[0]


GROUP_ROWS = 72
LANES = 128


def params_for(mebibytes):
    return pltpu.CompilerParams(vmem_limit_bytes=mebibytes * 2**20)


def roll(values, shift):
    return pltpu.roll(values, shift, 1)


def lane_of(values):
    return lax.broadcasted_iota(jnp.int32, values.shape, 1)


def fold_half(values, upper):
    top, bottom = values[:24], values[24:]
    if upper:
        return jnp.where(lane_of(top) < 64, roll(top, 64), bottom)
    return jnp.where(lane_of(top) < 64, top, roll(bottom, 64))


def unfold_half(values, upper):
    turned = roll(values, 64)
    return jnp.concatenate([turned, values] if upper else [values, turned], 0)


def join_pair(main_0, rest_0, main_1, rest_1):
    left = lane_of(main_0) < 64
    turned = roll(main_1, 64)
    return (
        main_0,
        jnp.where(left, unfold_half(rest_0, False), turned),
        jnp.where(left, turned, unfold_half(rest_1, True)),
    )


def cut_pair(tile_0, tile_1, tile_2):
    left = lane_of(tile_0) < 64
    return (
        (tile_0, fold_half(tile_1, False)),
        (jnp.where(left, roll(tile_1, 64), roll(tile_2, 64)), fold_half(tile_2, True)),
    )


def chunk_rows(own_blocks):
    return own_blocks // 4 * GROUP_ROWS + 8


def bias_row(tiles, part, width):
    at, shift = divmod(part * width, LANES)
    lane = lane_of(tiles[0])
    row = tiles[at]
    if shift:
        row = jnp.where(lane < LANES - shift, roll(row, LANES - shift), roll(tiles[at + 1], LANES - shift))
    return jnp.where(lane < width, row, 0.0)


def bias_tiles(first, second, third, fourth):
    cut = lambda values: [values[:, at : at + LANES] for at in range(0, values.shape[1], LANES)]
    zero = jnp.zeros((1, LANES), F32)
    left = lane_of(zero) < 64
    third_tail = jnp.concatenate([third[:, LANES:]] * 2, 1)
    turned = [roll(tile, 64) for tile in cut(fourth)]
    joints = [jnp.where(left, one, two) for one, two in zip([third_tail] + turned, turned + [zero])]
    return cut(first) + cut(second) + [third[:, :LANES]] + joints + [zero]


def tiles_of_rows(rows, width):
    tiles = []
    for tile in range(-(-len(rows) * width // LANES)):
        value = jnp.zeros((8, LANES), F32)
        lane = lane_of(value)
        for part, row in enumerate(rows):
            shift = part * width - tile * LANES
            if shift >= LANES or shift + width <= 0:
                continue
            turned = roll(row, shift % LANES) if shift % LANES else row
            value = jnp.where((lane >= shift) & (lane < shift + width), turned, value)
        tiles.append(value)
    return tiles


def pack_own(master, vector):
    count, width = master.shape[0], vector.shape[1]

    def kernel(master_ref, bias_ref, out_ref):
        row = lax.broadcasted_iota(jnp.int32, (BLOCK, 256), 0)
        col = lax.broadcasted_iota(jnp.int32, (BLOCK, 256), 1)
        pieces = []
        for group in range(count // 4):
            wide = jnp.zeros((BLOCK, 256), F32)
            for j in range(4):
                wide += matmul(low(master_ref[4 * group + j]), (col == row + BLOCK * j).astype(BF16))
            pieces += [wide[:, :LANES], fold_half(wide[:, LANES:], False)]
        bias = jnp.concatenate([bias_ref[...], jnp.zeros((1, LANES - width), F32)], 1)
        pieces.append(jnp.concatenate([bias, jnp.zeros((7, LANES), F32)], 0))
        out_ref[...] = low(jnp.concatenate(pieces, 0))

    return pl.pallas_call(
        kernel,
        out_shape=jax.ShapeDtypeStruct((chunk_rows(count), LANES), BF16),
        name="pack_own",
    )(master, vector)


MATRICES = ((D, BOT), (BOT, D), (HALF, INV_H), (INV_H, HALF))
BIASES = (BOT, D, INV_H, HALF)


def unpack_all(own, came, width):
    lines, planes, rows, _ = own.shape
    parts = lines * planes
    per_part = (rows - 8) // GROUP_ROWS

    def kernel(own_hbm, came_hbm, *refs):
        out_hbm, in_bufs, out_refs, in_sems, out_sems = refs[:8], refs[8], refs[9:17], refs[17], refs[18]
        here = lax.axis_index("section")
        copies = [
            pltpu.make_async_copy(ref, in_bufs.at[at], in_sems.at[i])
            for i, (ref, at) in enumerate(((own_hbm, here), (came_hbm, 1 - here)))
        ]
        for copy in copies:
            copy.start()
        for copy in copies:
            copy.wait()

        def unpack(s, carry):
            cache = {}

            def group(index):
                part = index // per_part
                if part not in cache:
                    cache.clear()
                    cache[part] = in_bufs[s, part % lines, part // lines].astype(F32)
                base = index % per_part * GROUP_ROWS
                chunk = cache[part]
                return chunk[base : base + BLOCK], chunk[base + BLOCK : base + GROUP_ROWS]

            index = 0
            for (height, columns), out_ref in zip(MATRICES, out_refs):
                for top in range(0, height, BLOCK):
                    if columns == INV_H:
                        main, rest = group(index)
                        index += 1
                        out_ref[s, top : top + BLOCK, :LANES] = low(main)
                        out_ref[s, top : top + BLOCK, LANES:] = low(unfold_half(rest, False)[:, :64])
                        continue
                    for left in range(0, columns, HALF):
                        tiles = join_pair(*group(index), *group(index + 1))
                        index += 2
                        for j, tile in enumerate(tiles):
                            at = left + j * LANES
                            out_ref[s, top : top + BLOCK, at : at + LANES] = low(tile)
            tiles = tiles_of_rows(
                [in_bufs[s, part % lines, part // lines, rows - 16 :].astype(F32)[8:] for part in range(parts)], width
            )
            first, second, third, fourth = out_refs[4:]
            first[s] = jnp.concatenate(tiles[:3], 1)[:1]
            second[s] = jnp.concatenate(tiles[3:9], 1)[:1]
            third[s] = jnp.concatenate([tiles[9], tiles[10][:, :64]], 1)[:1]
            left = lane_of(tiles[0]) < 64
            turned = [roll(tile, 64) for tile in tiles[10:14]]
            fourth[s] = jnp.concatenate(
                [jnp.where(left, one, two) for one, two in zip(turned, turned[1:])], 1
            )[:1]
            return carry

        lax.fori_loop(0, MICRO, unpack, 0)
        copies = [
            pltpu.make_async_copy(buf, ref, out_sems.at[i]) for i, (buf, ref) in enumerate(zip(out_refs, out_hbm))
        ]
        for copy in copies:
            copy.start()
        for copy in copies:
            copy.wait()

    shapes = [((MICRO,) + shape, BF16) for shape in MATRICES] + [((MICRO, 1, size), F32) for size in BIASES]
    hbm = pl.BlockSpec(memory_space=pltpu.HBM)
    arrays = pl.pallas_call(
        kernel,
        in_specs=[hbm] * 2,
        out_specs=[hbm] * 8,
        out_shape=[jax.ShapeDtypeStruct(*shape) for shape in shapes],
        scratch_shapes=[pltpu.VMEM((MICRO, lines, planes, rows, LANES), BF16)]
        + [pltpu.VMEM(*shape) for shape in shapes]
        + [pltpu.SemaphoreType.DMA((2,)), pltpu.SemaphoreType.DMA((8,))],
        compiler_params=params_for(MOST_VMEM),
        name="unpack_all",
    )(own, came)
    down, up, c_down, c_up, bias_down, bias_up, c_bias_down, c_bias_up = arrays
    return Params(down, bias_down, up, bias_up), Params(c_down, c_bias_down, c_up, c_bias_up)


ADAPTER_GROUPS = 2 * D * BOT // BLOCK**2 // 4
COUPLING_GROUPS = 2 * HALF * INV_H // BLOCK**2 // 4
PART_GROUPS = (ADAPTER_GROUPS + COUPLING_GROUPS) // COUPLING_GROUPS
PART_ROWS = PART_GROUPS * GROUP_ROWS


def groups_of(refs, shapes):
    groups = []
    for ref, (height, width) in zip(refs, shapes):
        for top in range(0, height, BLOCK):
            band = slice(top, top + BLOCK)
            if width == INV_H:
                tail = ref[band, LANES:]
                groups.append((ref[band, :LANES], fold_half(jnp.concatenate([tail, tail], 1), False)))
                continue
            for left in range(0, width, HALF):
                groups += cut_pair(*[ref[band, left + j * LANES : left + (j + 1) * LANES] for j in range(3)])
    return [jnp.concatenate(group, 0) for group in groups]


def pack_adapter(refs, store):
    groups = groups_of(refs, MATRICES[:2])
    empty = jnp.zeros((GROUP_ROWS, LANES), F32)
    for part in range(COUPLING_GROUPS):
        chunk = groups[part * PART_GROUPS : (part + 1) * PART_GROUPS]
        chunk += [empty] * (PART_GROUPS - len(chunk))
        store(part, low(jnp.concatenate(chunk, 0)))


def pack_coupling(refs, tiles, width, store):
    for part, group in enumerate(groups_of(refs, MATRICES[2:])):
        bias = jnp.concatenate([bias_row(tiles, part, width), jnp.zeros((7, LANES), F32)], 0)
        store(part, jnp.concatenate([group, bias], 0))


def sum_parts(came_ref):
    total = came_ref[0].astype(F32)
    for part in range(1, came_ref.shape[0]):
        total += came_ref[part].astype(F32)
    return total


def square_sum(values):
    return jnp.sum(jnp.sum(values * values, 0, keepdims=True), 1, keepdims=True)


def sum_adapter(came):
    def kernel(came_ref, total_ref, square_ref):
        total = sum_parts(came_ref)
        total_ref[...] = total
        square_ref[...] = square_sum(total)

    return pl.pallas_call(
        kernel,
        out_shape=[jax.ShapeDtypeStruct((PART_ROWS, LANES), F32), jax.ShapeDtypeStruct((1, 1), F32)],
        compiler_params=params_for(32),
        name="sum_adapter",
    )(came)


def sum_coupling(came, squares, loss_part, copies):
    def kernel(came_ref, square_ref, loss_ref, group_ref, bias_ref, pair_ref):
        total = sum_parts(came_ref)
        group_ref[...] = total[:GROUP_ROWS]
        bias_ref[...] = total[GROUP_ROWS:]
        squares = square_ref[...] + square_sum(total)
        lane = lax.broadcasted_iota(jnp.int32, (1, LANES), 1)
        pair = jnp.where(lane == 0, squares, jnp.where(lane == 1, loss_ref[...], 0.0))
        pair_ref[...] = jnp.broadcast_to(pair[None], pair_ref.shape)

    return pl.pallas_call(
        kernel,
        out_shape=[
            jax.ShapeDtypeStruct((GROUP_ROWS, LANES), F32),
            jax.ShapeDtypeStruct((8, LANES), F32),
            jax.ShapeDtypeStruct((copies, 1, LANES), F32),
        ],
        name="sum_coupling",
    )(came, squares, loss_part)


def grad_products(adapter_total, coupling_groups, root_left, root_right):
    count = 4 * PART_GROUPS

    def exact_dot(left, right, dims):
        return lax.dot_general(left, right, (dims, ((), ())), precision=HIGHEST, preferred_element_type=F32)

    def kernel(total_ref, left_ref, right_ref, *refs):
        group_refs, (grad_ref, left_square_ref, right_square_ref, turned_ref) = refs[:-4], refs[-4:]
        for group in range(PART_GROUPS):
            total = total_ref[group * GROUP_ROWS : (group + 1) * GROUP_ROWS] + group_refs[group][...]
            main, rest = total[:BLOCK], unfold_half(total[BLOCK:], False)
            lane = lane_of(main)
            pieces = (
                main,
                roll(main, 80),
                jnp.where(lane < 32, roll(main, 32), roll(rest, 32)),
                roll(rest, 112),
            )
            for j, values in enumerate(pieces):
                grad_ref[4 * group + j] = values[:, :BLOCK]
        for n in range(count):
            grad = grad_ref[n]
            left_square_ref[n] = exact_dot(grad, grad, ((1,), (1,)))
            right_square_ref[n] = exact_dot(grad, grad, ((0,), (0,)))
            turned_ref[n] = exact_dot(
                exact_dot(left_ref[n], grad, ((1,), (0,))), right_ref[n], ((1,), (0,))
            )

    return pl.pallas_call(
        kernel,
        out_shape=[jax.ShapeDtypeStruct((count, BLOCK, BLOCK), F32)] * 4,
        compiler_params=params_for(24),
        name="grad_products",
    )(adapter_total, root_left, root_right, *coupling_groups)


MOST_VMEM = 64
GROUP = 256
HEADS_IN = GROUP // HEAD_DIM
GROUPS = D // GROUP
FF = 3072
TILE = 512
TILES = FF // TILE
STEP_ROWS = 256
SMALL_ROWS = 32


def rows_of(count, size):
    return [slice(at, at + min(size, count)) for at in range(0, count, size)]


def shape_of(*dims, kind=F32):
    return jax.ShapeDtypeStruct(dims, kind)


class Params(NamedTuple):
    down: Any
    bias_down: Any
    up: Any
    bias_up: Any


class Branch(NamedTuple):
    lin: Any
    act: Any
    slope: Any


class Attention(NamedTuple):
    query: Any
    key: Any
    value: Any
    lse: Any


class Rest(NamedTuple):
    normal_1: Any
    inverse_1: Any
    slope: Any
    branch: Any
    normal_2: Any
    inverse_2: Any


class Last(NamedTuple):
    one: Any
    two: Any
    normal: Any
    inverse: Any
    normed: Any


class ForwardIn(NamedTuple):
    came: Any
    spot: Any
    extra: Any
    pos: Any
    norms: Any
    chosen: Any
    adapter: Any
    coupling: Any


class Forward(NamedTuple):
    target_rows: Any
    one: Any
    two: Any
    attention_0: Any
    rest_0: Any
    attention_1: Any
    rest_1: Any
    last: Any


class BackIn(NamedTuple):
    merged: Any
    row_weights: Any
    weight_sum: Any
    norms: Any
    chosen_t: Any
    adapter: Any
    coupling: Any
    target_rows: Any
    rest_0: Any
    attention_1: Any
    rest_1: Any
    last: Any


class Back(NamedTuple):
    loss: Any
    one: Any
    two: Any
    adapters: Any
    start: Any
    mixed: Any


class FirstIn(NamedTuple):
    attention: Any
    mixed: Any
    start: Any
    coupling: Any
    one: Any
    two: Any
    grads_one: Any
    grads_two: Any
    biases: Any


class Operand:
    def __init__(self, ref, buffer, sem):
        self.buffer, self.copy = buffer, pltpu.make_async_copy(ref, buffer, sem)
        self.started = self.waited = False

    def start(self):
        if not self.started:
            self.copy.start()
        self.started = True

    def get(self):
        self.start()
        if not self.waited:
            self.copy.wait()
        self.waited = True
        return self.buffer


class Result:
    def __init__(self, ref, buffer, sem):
        self.buffer, self.copy = buffer, pltpu.make_async_copy(buffer, ref, sem)
        self.sent = False

    def send(self):
        if not self.sent:
            self.copy.start()
        self.sent = True


def start(*operands):
    for operand in jax.tree.leaves(operands):
        operand.start()


def send(*results):
    for result in jax.tree.leaves(results):
        result.send()


def moved_call(body, scalars, ins, outs, pairs, scratch, name, raw_outs=()):
    in_leaves, in_tree = jax.tree.flatten(ins)
    out_leaves, out_tree = jax.tree.flatten(outs)

    def kernel(*refs):
        refs = list(refs)

        def take(count):
            taken, refs[:] = refs[:count], refs[count:]
            return taken

        scalar_refs, in_refs = take(len(scalars)), take(len(in_leaves))
        pair_refs = [tuple(take(2)) for _ in pairs]
        out_refs, raw_refs = take(len(out_leaves)), take(len(raw_outs))
        in_buffers, out_buffers, (in_sems, out_sems) = take(len(in_leaves)), take(len(out_leaves)), take(2)
        operands = [Operand(*two, in_sems.at[i]) for i, two in enumerate(zip(in_refs, in_buffers))]
        results = [Result(*two, out_sems.at[i]) for i, two in enumerate(zip(out_refs, out_buffers))]
        body(in_tree.unflatten(operands), out_tree.unflatten(results), scalar_refs, pair_refs, raw_refs, refs)
        send(results)
        for operand in operands:
            operand.get()
        for result in results:
            result.copy.wait()

    hbm = pl.BlockSpec(memory_space=pltpu.HBM)
    buffers = [pltpu.VMEM(value.shape, value.dtype) for value in (*in_leaves, *out_leaves)]
    results = pl.pallas_call(
        kernel,
        in_specs=[pl.BlockSpec(memory_space=pltpu.SMEM)] * len(scalars) + [hbm] * (len(in_leaves) + 2 * len(pairs)),
        out_specs=[hbm] * (len(out_leaves) + len(raw_outs)),
        out_shape=[*out_leaves, *raw_outs],
        scratch_shapes=buffers
        + [pltpu.SemaphoreType.DMA((len(in_leaves),)), pltpu.SemaphoreType.DMA((len(out_leaves),))]
        + list(scratch),
        compiler_params=params_for(MOST_VMEM),
        name=name,
    )(*scalars, *in_leaves, *[w for pair in pairs for w in pair])
    return out_tree.unflatten(results[: len(out_leaves)]), results[len(out_leaves) :]


def start_copy(pair, section, window, target, sem):
    own, came = pair
    here = lax.axis_index("section") == section

    @pl.when(here)
    def _():
        pltpu.make_async_copy(own.at[window], target, sem).start()

    @pl.when(jnp.logical_not(here))
    def _():
        pltpu.make_async_copy(came.at[window], target, sem).start()


def wait_copy(pair, window, target, sem):
    pltpu.make_async_copy(pair[0].at[window], target, sem).wait()


def qkv_window(group, part):
    return 0, slice(None), pl.ds(part * D + group * GROUP, GROUP)


def qkv_buffers():
    return [pltpu.VMEM((GROUPS, 3, D, GROUP), BF16), pltpu.SemaphoreType.DMA((GROUPS, 3))]


def start_qkv(pair, section, buffers):
    for group in range(GROUPS):
        for part in range(3):
            start_copy(pair, section, qkv_window(group, part), buffers[0].at[group, part], buffers[1].at[group, part])


def wait_qkv(pair, buffers, group, part):
    wait_copy(pair, qkv_window(0, 0), buffers[0].at[group, part], buffers[1].at[group, part])


UP_WINDOWS = [(0, slice(None), slice(j * TILE, (j + 1) * TILE)) for j in range(TILES)]
DOWN_WINDOWS = [(0, slice(j * TILE, (j + 1) * TILE), slice(None)) for j in range(TILES)]
OUT_WINDOW = (0, slice(None), slice(None))


def rest_buffers():
    return [
        pltpu.VMEM((D, D), BF16),
        pltpu.VMEM((TILES, D, TILE), BF16),
        pltpu.VMEM((TILES, TILE, D), BF16),
        pltpu.SemaphoreType.DMA((2 * TILES + 1,)),
    ]


def start_out(pairs, section, buffers):
    start_copy(pairs[0], section, OUT_WINDOW, buffers[0], buffers[3].at[2 * TILES])


def start_tiles(pairs, section, buffers):
    for j in range(TILES):
        start_copy(pairs[1], section, UP_WINDOWS[j], buffers[1].at[j], buffers[3].at[j])
        start_copy(pairs[2], section, DOWN_WINDOWS[j], buffers[2].at[j], buffers[3].at[TILES + j])


def wait_out(pairs, buffers):
    wait_copy(pairs[0], OUT_WINDOW, buffers[0], buffers[3].at[2 * TILES])


def wait_up(pairs, buffers, tile):
    wait_copy(pairs[1], UP_WINDOWS[0], buffers[1].at[tile], buffers[3].at[tile])


def wait_down(pairs, buffers, tile):
    wait_copy(pairs[2], DOWN_WINDOWS[0], buffers[2].at[tile], buffers[3].at[TILES + tile])


def across(values):
    return jnp.broadcast_to(values, (values.shape[0], LANES))


def group_columns(group):
    return pl.ds(pl.multiple_of(group * GROUP, GROUP), GROUP)


def tile_columns(tile):
    return pl.ds(pl.multiple_of(tile * TILE, TILE), TILE)


def head_mask(values, head):
    lane = lax.broadcasted_iota(jnp.int32, values.shape, 1)
    return (lane >= head * HEAD_DIM) & (lane < (head + 1) * HEAD_DIM)


def only_head(values, head):
    return jnp.where(head_mask(values, head), values, jnp.zeros_like(values))


def scaled_query(query):
    return low(query.astype(F32) * HEAD_DIM**-0.5)


def key_bias(length, shape, axis):
    return jnp.where(lax.broadcasted_iota(jnp.int32, shape, axis) < length, 0.0, -1e30)


def softmax_rows(scores):
    highest = jnp.max(scores, 1, keepdims=True)
    exponent = jnp.exp(scores - highest)
    total = jnp.sum(exponent, 1, keepdims=True)
    return low(exponent * (1.0 / total)), highest + jnp.log(total)


def branch_rows(low_in, weights):
    active, slope = gelu_both(matmul(low_in, weights[0]) + weights[1])
    active = low(active)
    return matmul(active, weights[2]) + weights[3], active, low(slope)


def section_params(params, section):
    return [operand.get()[section] for operand in params]


def rest_rows(out, rows, section, norms, adapter, hidden, mixed, finish, scratch, pairs, buffers, after_loop=None):
    att_low, acc, u_even, u_odd, g_even, g_odd = scratch
    gain = lambda i: norms[section, i : i + 1]
    parts = rows_of(rows, STEP_ROWS)
    every = slice(0, rows)
    wait_out(pairs, buffers)
    for part in parts:
        first = hidden[part] + matmul(mixed[part], buffers[0][...])
        values, (normal, inverse) = layer_norm(first, gain(2), gain(3))
        acc[part] = values
        att_low[part] = low(values)
        out.normal_1.buffer[part] = normal
        out.inverse_1.buffer[part] = across(inverse)
    send(out.normal_1, out.inverse_1)
    wait_up(pairs, buffers, 0)
    u_even[every] = matmul(att_low[every], buffers[1][0])

    def turn(j, carry):
        even, odd = 2 * j, 2 * j + 1
        after = jnp.minimum(even + 2, TILES - 1)
        wait_down(pairs, buffers, even)
        wait_up(pairs, buffers, odd)
        wait_down(pairs, buffers, odd)

        @pl.when(even + 2 < TILES)
        def _():
            wait_up(pairs, buffers, even + 2)

        for now, u_now, g_now, later, u_later in (
            (even, u_even, g_even, odd, u_odd),
            (odd, u_odd, g_odd, after, u_even),
        ):
            for at in rows_of(rows, SMALL_ROWS):
                active, slope = gelu_both(u_now[at])
                g_now[at] = low(active)
                out.slope.buffer[at, tile_columns(now)] = low(slope)
            u_later[every] = matmul(att_low[every], buffers[1][later])
            acc[every] += matmul(g_now[every], buffers[2][now])
        return carry

    lax.fori_loop(0, TILES // 2, turn, 0)
    if after_loop is not None:
        after_loop()
    send(out.slope)
    weights = section_params(adapter, section)
    for part in parts:
        summed = acc[part]
        low_in = low(summed)
        added, *kept = branch_rows(low_in, weights)
        for result, value in zip(out.branch, (low_in, *kept)):
            result.buffer[part] = value
        values, (normal, inverse) = layer_norm(summed + added, gain(4), gain(5))
        out.normal_2.buffer[part], out.inverse_2.buffer[part] = normal, across(inverse)
        finish(part, values)
    send(out.branch, out.normal_2, out.inverse_2)


def low_shape(*dims):
    return shape_of(*dims, kind=BF16)


def branch_shapes(rows, wide, narrow):
    return Branch(low_shape(rows, wide), low_shape(rows, narrow), low_shape(rows, narrow))


def rest_shapes(rows):
    wide, thin = shape_of(rows, D), shape_of(rows, LANES)
    return Rest(wide, thin, low_shape(rows, FF), branch_shapes(rows, D, BOT), wide, thin)


def forward_kernel(ins, scalars, pairs, parts, slots):
    coupling_shapes = lambda rows: branch_shapes(rows, HALF, INV_H)
    outs = Forward(
        target_rows=shape_of(COUNT, D),
        one=coupling_shapes(SEQ),
        two=coupling_shapes(SEQ),
        attention_0=Attention(*[low_shape(SEQ, D)] * 3, shape_of(GROUPS, 8, SEQ)),
        rest_0=rest_shapes(SEQ),
        attention_1=Attention(
            low_shape(COUNT, D), *[low_shape(SEQ, D)] * 2, shape_of(GROUPS, HEADS_IN * COUNT, LANES)
        ),
        rest_1=rest_shapes(COUNT),
        last=Last(
            coupling_shapes(COUNT), coupling_shapes(COUNT),
            shape_of(COUNT, D), shape_of(COUNT, LANES), low_shape(COUNT, D),
        ),
    )

    def body(ins, out, scalar_refs, pair_refs, raw_refs, scratch):
        length = scalar_refs[0][0]
        hidden, x_low, s_even, s_odd, p_even, p_odd, lse_buf, mixed, section_out = scratch[:9]
        at_spots, at_low, mixed_1 = scratch[9:12]
        rest_scratch, qkv_0, qkv_1, rest_w = scratch[12:18], scratch[18:20], scratch[20:22], scratch[22:26]
        row_sems = scratch[26]
        qkv_pair, rest_pairs = pair_refs[0], pair_refs[1:]

        start(ins.came, ins.spot, ins.extra, ins.pos, ins.norms, ins.coupling)
        start_qkv(qkv_pair, 0, qkv_0)
        start_out(rest_pairs, 0, rest_w)
        start(ins.adapter, ins.chosen)
        start_tiles(rest_pairs, 0, rest_w)
        start_qkv(qkv_pair, 1, qkv_1)
        norms = ins.norms.get()
        norm = lambda s, i: norms[s, i : i + 1]

        came, spot, extra = ins.came.get(), ins.spot.get(), ins.extra.get()

        def rows_at(part):
            lane = lax.broadcasted_iota(jnp.int32, (part.stop - part.start, parts * slots), 1)
            hits = (spot[part][:, :1] == lane).astype(BF16)
            return matmul(hits, came[...]) + extra[part]

        out.target_rows.buffer[...] = rows_at(slice(SEQ, SEQ + COUNT))
        send(out.target_rows)
        one, two = section_params(ins.coupling, 0), section_params(ins.coupling, 1)

        def put(results, part, *values):
            for result, value in zip(results, values):
                result.buffer[part] = value

        for part in rows_of(SEQ, STEP_ROWS):
            started, _ = layer_norm(rows_at(part) + ins.pos.get()[part].astype(F32), norm(0, 0), norm(0, 1))
            left, right = started[:, :HALF], started[:, HALF:]
            low_one = low(right)
            added, active, slope = branch_rows(low_one, one)
            put(out.one, part, low_one, active, slope)
            left = left + added
            low_two = low(left)
            added, active, slope = branch_rows(low_two, two)
            put(out.two, part, low_two, active, slope)
            right = right + added
            hidden[part, :HALF] = left
            hidden[part, HALF:] = right
            x_low[part, :HALF] = low_two
            x_low[part, HALF:] = low(right)
        send(out.one, out.two)

        lse_buf[...] = jnp.zeros((SEQ, LANES), F32)
        q_ref, k_ref, v_ref, lse_ref = (result.buffer for result in out.attention_0)

        def attend(group, carry):
            columns = group_columns(group)
            for part, ref in enumerate((q_ref, k_ref, v_ref)):
                wait_qkv(qkv_pair, qkv_0, group, part)
                ref[:, columns] = low(matmul(x_low[...], qkv_0[0][group, part]))
            query = scaled_query(q_ref[:, columns])
            key, value = k_ref[:, columns], v_ref[:, columns]
            bias = key_bias(length, (1, SEQ), 1)
            lane = lax.broadcasted_iota(jnp.int32, (SMALL_ROWS * 2, LANES), 1)
            joined = jnp.zeros((SEQ, GROUP), F32)
            for head in range(HEADS_IN):
                scores, soft_buf = ((s_even, p_even), (s_odd, p_odd))[head % 2]
                scores[...] = matmul_t(only_head(query, head), key)
                for rows in rows_of(SEQ, SMALL_ROWS * 2):
                    soft, lse = softmax_rows(scores[rows] + bias)
                    soft_buf[rows] = soft
                    lse_buf[rows] = jnp.where(lane == head, lse, lse_buf[rows])
                joined = jnp.where(head_mask(joined, head), matmul(soft_buf[...], value), joined)
            mixed[:, columns] = low(joined)
            lse_ref[group] = jnp.transpose(lse_buf[...])[:8]
            return carry

        lax.fori_loop(0, GROUPS, attend, 0)
        send(out.attention_0)

        def to_section_out(part, values):
            section_out[part] = low(values)

        def next_weights():
            start_out(rest_pairs, 1, rest_w)
            start_tiles(rest_pairs, 1, rest_w)

        rest_rows(
            out.rest_0, SEQ, 0, norms, ins.adapter, hidden, mixed, to_section_out,
            rest_scratch, rest_pairs, rest_w, next_weights,
        )

        at_spots[...] = matmul(ins.chosen.get()[...], section_out[...])
        at_low[...] = low(at_spots[...])
        q_1, k_1, v_1, lse_1 = (result.buffer for result in out.attention_1)

        def attend_spots(group, carry):
            columns = group_columns(group)
            for part, ref in enumerate((q_1, k_1, v_1)):
                wait_qkv(qkv_pair, qkv_1, group, part)
                source = at_low if part == 0 else section_out
                ref[:, columns] = low(matmul(source[...], qkv_1[0][group, part]))
            query = scaled_query(q_1[:, columns])
            query = jnp.concatenate([only_head(query, head) for head in range(HEADS_IN)], 0)
            bias = key_bias(length, (1, SEQ), 1)
            soft, lse = softmax_rows(matmul_t(query, k_1[:, columns]) + bias)
            lse_1[group] = across(lse)
            every = matmul(soft, v_1[:, columns])
            joined = every[:COUNT]
            for head in range(1, HEADS_IN):
                joined = jnp.where(head_mask(joined, head), every[head * COUNT : (head + 1) * COUNT], joined)
            mixed_1[:, columns] = low(joined)
            return carry

        lax.fori_loop(0, GROUPS, attend_spots, 0)
        send(out.attention_1)

        def to_normed(part, values):
            left, right = values[:, :HALF], values[:, HALF:]
            low_two = low(left)
            taken, active, slope = branch_rows(low_two, two)
            put(out.last.two, part, low_two, active, slope)
            right = right - taken
            low_one = low(right)
            taken, active, slope = branch_rows(low_one, one)
            put(out.last.one, part, low_one, active, slope)
            left = left - taken
            values, (normal, inverse) = layer_norm(jnp.concatenate([left, right], 1), norm(1, 0), norm(1, 1))
            put(out.last[2:], part, normal, across(inverse), low(values))

        rest_rows(
            out.rest_1, COUNT, 1, norms, ins.adapter, at_spots, mixed_1, to_normed,
            rest_scratch, rest_pairs, rest_w,
        )
        copies = [
            pltpu.make_async_copy(out.last.normed.buffer, raw_refs[0].at[part], row_sems.at[part]) for part in range(parts)
        ]
        for copy in copies:
            copy.start()
        for copy in copies:
            copy.wait()

    buffer = lambda *dims: pltpu.VMEM(dims, F32)
    buffer_low = lambda *dims: pltpu.VMEM(dims, BF16)
    scratch = [buffer(SEQ, D), buffer_low(SEQ, D), buffer(SEQ, SEQ), buffer(SEQ, SEQ)]
    scratch += [buffer_low(SEQ, SEQ), buffer_low(SEQ, SEQ), buffer(SEQ, LANES)]
    scratch += [buffer_low(SEQ, D), buffer_low(SEQ, D)]
    scratch += [buffer(COUNT, D), buffer_low(COUNT, D), buffer_low(COUNT, D)]
    scratch += [buffer_low(SEQ, D), buffer(SEQ, D), buffer(SEQ, TILE), buffer(SEQ, TILE)]
    scratch += [buffer_low(SEQ, TILE), buffer_low(SEQ, TILE)]
    scratch += qkv_buffers() + qkv_buffers() + rest_buffers()
    scratch += [pltpu.SemaphoreType.DMA((parts,))]
    raw = [low_shape(parts, COUNT, D)]
    kept, (rows,) = moved_call(body, scalars, ins, outs, pairs, scratch, "forward", raw)
    return kept, rows


def column_sum(values):
    return jnp.sum(values.astype(F32), 0, keepdims=True)


def branch_grads(grad_low, kept, weights, out_refs):
    low_in, active, slope = kept
    hidden_grad = low(matmul_t(grad_low, weights[2]) * slope.astype(F32))
    out_refs[0][...] = inner_rows(low_in, hidden_grad)
    out_refs[1][...] = column_sum(hidden_grad)
    out_refs[2][...] = inner_rows(active, grad_low)
    out_refs[3][...] = column_sum(grad_low)
    return hidden_grad


ADAPTER_GRADS = ((D, BOT), (1, BOT), (BOT, D), (1, D))
COUPLING_GRADS = ((HALF, INV_H), (1, INV_H), (INV_H, HALF), (1, HALF))


def branch_kept(branch):
    return [operand.get()[...] for operand in branch]


def grad_weights(pair, section):
    return [pair[0].get()[section], None, pair[1].get()[section]]


def rest_back_rows(kept, rows, section, norms, adapter, incoming, scratch, pairs, buffers, grad_refs, results, packing=None):
    summed_low, acc, second_low = scratch
    start_ref, mixed_ref = results
    gain = lambda i: norms[section, i : i + 1]
    parts = rows_of(rows, STEP_ROWS)
    weights = grad_weights(adapter, section)
    for part in parts:
        norm_kept = kept.normal_2.get()[part], kept.inverse_2.get()[part, :1]
        second = norm_back(incoming(part), norm_kept, gain(4))
        acc[part] = second
        second_low[part] = low(second)
    hidden_grad = branch_grads(second_low[:rows], branch_kept(kept.branch), weights, grad_refs)
    for part in parts:
        total = acc[part] + matmul_t(hidden_grad[part], weights[0])
        acc[part] = total
        summed_low[part] = low(total)
    if packing is not None:
        packing()
    slope = kept.slope.get()

    def turn(j, carry):
        for now in (2 * j, 2 * j + 1):
            wait_up(pairs, buffers, now)
            wait_down(pairs, buffers, now)
        for now in (2 * j, 2 * j + 1):
            for part in parts:
                inner = matmul_t(summed_low[part], buffers[2][now])
                inner = low(inner * slope[part, tile_columns(now)].astype(F32))
                acc[part] += matmul_t(inner, buffers[1][now])
        return carry

    lax.fori_loop(0, TILES // 2, turn, 0)
    wait_out(pairs, buffers)
    for part in parts:
        norm_kept = kept.normal_1.get()[part], kept.inverse_1.get()[part, :1]
        back = norm_back(acc[part], norm_kept, gain(2))
        start_ref[part] = back
        mixed_ref[part] = low(matmul_t(low(back), buffers[0][...]))


def backward_kernel(ins, scalars, pairs, packed):
    parts = ins.merged.shape[0]
    grads = [shape_of(*dims) for dims in COUPLING_GRADS]
    if packed:
        chunks = low_shape(COUPLING_GROUPS, PART_ROWS, LANES)
        adapters = [[shape_of(1, BOT), shape_of(1, D)] for _ in range(MICRO)] + [chunks, chunks]
    else:
        adapters = [[shape_of(*dims) for dims in ADAPTER_GRADS] for _ in range(MICRO)]
    outs = Back(shape_of(1, LANES), grads, grads, adapters, shape_of(SEQ, D), low_shape(SEQ, D))

    def body(ins, out, scalar_refs, pair_refs, raw_refs, scratch):
        length = scalar_refs[0][0]
        rest_scratch, spot, mixed_1, acc_1, section_grad = scratch[:3], *scratch[3:7]
        qkv_w, rest_w, refs = scratch[7:9], scratch[9:13], scratch[13:]
        qkv_pair, rest_pairs = pair_refs[0], pair_refs[1:]

        start(ins.merged, ins.row_weights, ins.weight_sum, ins.target_rows, ins.last, ins.norms)
        start(ins.coupling, ins.adapter, ins.rest_1)
        start_tiles(rest_pairs, 1, rest_w)
        start_out(rest_pairs, 1, rest_w)
        start_qkv(qkv_pair, 1, qkv_w)
        start(ins)
        norms = ins.norms.get()

        def from_head(part):
            merged = ins.merged.get()
            stats = merged[:, :, D:].astype(F32)
            highest = jnp.sum(stats[:, :, :3], 2, keepdims=True)
            totals = jnp.sum(stats[:, :, 3:6], 2, keepdims=True)
            top = jnp.max(highest, 0)
            factor = jnp.exp(highest - top[None])
            total = jnp.sum(totals * factor, 0)
            expected = jnp.zeros((COUNT, D), F32)
            for i in range(parts):
                expected += merged[i, :, :D].astype(F32) * (factor[i] / total)
            target = ins.target_rows.get()[...]
            target_logit = jnp.sum(ins.last.normed.get()[...].astype(F32) * target, 1, keepdims=True)
            weight = ins.row_weights.get()[...]
            row_losses = weight[:, :1] * (top + jnp.log(total) - target_logit)
            out.loss.buffer[...] = across(jnp.sum(row_losses, 0, keepdims=True))
            normed_grad = (weight / ins.weight_sum.get()[...])[:, :1] * (expected - target)
            kept = (ins.last.normal.get()[...], ins.last.inverse.get()[:, :1])
            restored = norm_back(normed_grad, kept, norms[1, 0:1])
            left, right = restored[:, :HALF], restored[:, HALF:]
            one, two = (grad_weights(ins.coupling, s) for s in range(MICRO))
            refs_of = lambda results: [result.buffer for result in results]
            hidden = branch_grads(low(-left), branch_kept(ins.last.one), one, refs_of(out.one))
            right = right + matmul_t(hidden, one[0])
            hidden = branch_grads(low(-right), branch_kept(ins.last.two), two, refs_of(out.two))
            left = left + matmul_t(hidden, two[0])
            return jnp.concatenate([left, right], 1)

        def grads_of(section):
            buffers = [result.buffer for result in out.adapters[section]]
            return (refs[0], buffers[0], refs[1], buffers[1]) if packed else buffers

        def pack_second():
            def store(part, chunk):
                refs[2][part] = chunk

            pack_adapter((refs[0], refs[1]), store)

        def pack_both():
            here = lax.axis_index("section") == 0
            own, other = out.adapters[2:]

            def store(part, chunk):
                arrived = refs[2][part]
                own.buffer[part] = jnp.where(here, chunk, arrived)
                other.buffer[part] = jnp.where(here, arrived, chunk)

            pack_adapter((refs[0], refs[1]), store)
            send(own, other)

        rest_back_rows(
            ins.rest_1, COUNT, 1, norms, ins.adapter, from_head, rest_scratch, rest_pairs, rest_w,
            grads_of(1), (spot, mixed_1), pack_second if packed else None,
        )
        start_tiles(rest_pairs, 0, rest_w)
        start_out(rest_pairs, 0, rest_w)

        acc_1[...] = jnp.zeros_like(acc_1)
        q_ref, k_ref, v_ref, lse_ref = (operand.get() for operand in ins.attention_1)

        def attend_back(group, carry):
            columns = group_columns(group)
            stack = lambda values: jnp.concatenate([only_head(values, h) for h in range(HEADS_IN)], 0)
            query = stack(scaled_query(q_ref[:, columns]))
            mixed = stack(mixed_1[:, columns])
            key, value = k_ref[:, columns], v_ref[:, columns]
            scores = matmul_t(query, key) + key_bias(length, (1, SEQ), 1)
            soft = jnp.exp(scores - lse_ref[group][:, :1])
            soft_grad = matmul_t(mixed, value)
            delta = jnp.sum(soft_grad * soft, 1, keepdims=True)
            score_grad = low(soft * (soft_grad - delta))
            every = matmul(score_grad, key)
            query_grad = every[:COUNT]
            for head in range(1, HEADS_IN):
                query_grad = jnp.where(
                    head_mask(query_grad, head), every[head * COUNT : (head + 1) * COUNT], query_grad
                )
            query_grad = low(query_grad * HEAD_DIM**-0.5)
            key_grad = low(inner_rows(score_grad, query))
            value_grad = low(inner_rows(low(soft), mixed))
            for part in range(3):
                wait_qkv(qkv_pair, qkv_w, group, part)
            spot[...] += matmul_t(query_grad, qkv_w[0][group, 0])
            acc_1[...] += matmul_t(key_grad, qkv_w[0][group, 1]) + matmul_t(value_grad, qkv_w[0][group, 2])
            return carry

        lax.fori_loop(0, GROUPS, attend_back, 0)
        placed = jnp.dot(ins.chosen_t.get()[...], spot[...], precision=HIGHEST, preferred_element_type=F32)
        section_grad[...] = low(acc_1[...] + placed)

        rest_back_rows(
            ins.rest_0, SEQ, 0, norms, ins.adapter, lambda part: section_grad[part].astype(F32),
            rest_scratch, rest_pairs, rest_w, grads_of(0), (out.start.buffer, out.mixed.buffer),
            pack_both if packed else None,
        )

    scratch = [pltpu.VMEM((SEQ, D), BF16), pltpu.VMEM((SEQ, D), F32), pltpu.VMEM((SEQ, D), BF16)]
    scratch += [pltpu.VMEM((COUNT, D), F32), pltpu.VMEM((COUNT, D), BF16), pltpu.VMEM((SEQ, D), F32)]
    scratch += [pltpu.VMEM((SEQ, D), BF16)] + qkv_buffers() + rest_buffers()
    if packed:
        scratch += [pltpu.VMEM((D, BOT), F32), pltpu.VMEM((BOT, D), F32)]
        scratch += [pltpu.VMEM((COUPLING_GROUPS, PART_ROWS, LANES), BF16)]
    return moved_call(body, scalars, ins, outs, pairs, scratch, "backward")[0]


def first_backward(ins, scalars, pairs, packed):
    if packed:
        dims = (COUPLING_GROUPS, GROUP_ROWS + 8, LANES)
        outs = (shape_of(*dims), low_shape(*dims))
    else:
        outs = [shape_of(*dims) for dims in COUPLING_GRADS * 2]

    def body(ins, out, scalar_refs, pair_refs, raw_refs, scratch):
        length = scalar_refs[0][0]
        s_even, s_odd, d_even, d_odd, p_even, p_odd, ds_even, ds_odd = scratch[:8]
        qkv_w, refs = scratch[8:10], scratch[10:]
        start(ins.attention, ins.mixed)
        start_qkv(pair_refs[0], 0, qkv_w)
        start(ins)
        q_ref, k_ref, v_ref, lse_ref = (operand.get() for operand in ins.attention)
        mixed_ref, acc = ins.mixed.get(), ins.start.get()

        def attend_back(group, carry):
            columns = group_columns(group)
            query = scaled_query(q_ref[:, columns])
            key, value, mixed = k_ref[:, columns], v_ref[:, columns], mixed_ref[:, columns]
            lse_rows = lse_ref[group]
            key_t = jnp.transpose(key)
            key_grad = jnp.zeros((SEQ, GROUP), F32)
            value_grad = jnp.zeros((SEQ, GROUP), F32)
            query_parts = []
            for head in range(HEADS_IN):
                s_buf, d_buf, p_low, ds_low = (
                    (s_even, d_even, p_even, ds_even),
                    (s_odd, d_odd, p_odd, ds_odd),
                )[head % 2]
                s_buf[...] = matmul_t(only_head(key, head), query)
                d_buf[...] = matmul_t(only_head(value, head), mixed)
                lse_row = lse_rows[head : head + 1]
                delta = jnp.zeros((8, SEQ), F32)
                for rows in rows_of(SEQ, SMALL_ROWS):
                    valid = lax.broadcasted_iota(jnp.int32, (SMALL_ROWS, 1), 0) + rows.start < length
                    bias = jnp.where(valid, 0.0, -1e30)
                    soft = jnp.exp(s_buf[rows] + bias - lse_row)
                    s_buf[rows] = soft
                    p_low[rows] = low(soft)
                    product = soft * d_buf[rows]
                    for at in range(0, SMALL_ROWS, 8):
                        delta = delta + product[at : at + 8]
                delta = jnp.sum(delta, 0, keepdims=True)
                for rows in rows_of(SEQ, SMALL_ROWS):
                    ds_low[rows] = low(s_buf[rows] * (d_buf[rows] - delta))
                value_grad += matmul(p_low[...], only_head(mixed, head))
                key_grad += matmul(ds_low[...], only_head(query, head))
                query_parts.append(matmul(key_t[head * HEAD_DIM : (head + 1) * HEAD_DIM], ds_low[...]))
            query_grad = jnp.transpose(jnp.concatenate(query_parts, 0)) * HEAD_DIM**-0.5
            for part, grad in enumerate((query_grad, key_grad, value_grad)):
                wait_qkv(pair_refs[0], qkv_w, group, part)
                acc[...] += matmul_t(low(grad), qkv_w[0][group, part])
            return carry

        lax.fori_loop(0, GROUPS, attend_back, 0)
        one, two = (grad_weights(ins.coupling, s) for s in range(MICRO))
        grads = refs if packed else [result.buffer for result in out]
        hidden = branch_grads(low(acc[:, HALF:]), branch_kept(ins.two), two, grads[4:])
        left = acc[:, :HALF] + matmul_t(hidden, two[0])
        branch_grads(low(left), branch_kept(ins.one), one, grads[:4])
        for ref, operand in zip(grads, (*ins.grads_one, *ins.grads_two)):
            ref[...] += operand.get()[...]
        if not packed:
            return
        here = lax.axis_index("section")
        for s in range(MICRO):
            some = grads[4 * s : 4 * s + 4]
            biases = [operand.get()[...] for operand in ins.biases[s]]
            tiles = bias_tiles(*biases, some[1][...], some[3][...])

            def store(part, chunk, s=s):
                @pl.when(here == s)
                def _():
                    out[0].buffer[part] = chunk

                @pl.when(here != s)
                def _():
                    out[1].buffer[part] = low(chunk)

            pack_coupling((some[0], some[2]), tiles, sum(BIASES) // COUPLING_GROUPS, store)

    scratch = [pltpu.VMEM((SEQ, SEQ), F32)] * 4 + [pltpu.VMEM((SEQ, SEQ), BF16)] * 4 + qkv_buffers()
    if packed:
        scratch += [pltpu.VMEM(dims, F32) for dims in COUPLING_GRADS * 2]
    return moved_call(body, scalars, ins, outs, pairs[:1], scratch, "first_backward")[0]


VOCAB_TILE = 1280


def head_kernel(rows, table):
    parts_in, each, _ = rows.shape
    count, vocab = parts_in * each, table.shape[0]
    last = pl.cdiv(vocab, VOCAB_TILE) - 1
    turns = last // 2 + 1

    def kernel(x_hbm, even_ref, odd_ref, after_ref, out_hbm, *refs):
        x_ref, out_ref, acc, top, total, l_even, l_odd, p_even, p_odd, sems = refs
        turn = pl.program_id(0)

        def entries_of(ref, tile):
            row = lax.broadcasted_iota(jnp.int32, (VOCAB_TILE, 1), 0)
            return jnp.where(row < vocab - tile * VOCAB_TILE, ref[...], jnp.zeros_like(ref))

        @pl.when(turn == 0)
        def _():
            copy = pltpu.make_async_copy(x_hbm, x_ref, sems.at[0])
            copy.start()
            acc[...] = jnp.zeros_like(acc)
            top[...] = jnp.full_like(top, -1e30)
            total[...] = jnp.zeros_like(total)
            entries = entries_of(even_ref, 0)
            copy.wait()
            l_even[...] = matmul_t(x_ref[...], entries)

        even = entries_of(even_ref, 2 * turn)
        odd = entries_of(odd_ref, 2 * turn + 1)
        after = entries_of(after_ref, 2 * turn + 2)
        for tile, l_now, p_now, now, l_later, later in (
            (2 * turn, l_even, p_even, even, l_odd, odd),
            (2 * turn + 1, l_odd, p_odd, odd, l_even, after),
        ):
            bias = key_bias(vocab - tile * VOCAB_TILE, (1, VOCAB_TILE), 1)
            for at in rows_of(count, SMALL_ROWS):
                logits = l_now[at] + bias
                earlier = top[at]
                highest = jnp.maximum(earlier, jnp.max(logits, 1, keepdims=True))
                exponent = jnp.exp(logits - highest)
                factor = jnp.exp(earlier - highest)
                top[at] = highest
                total[at] = total[at] * factor + jnp.sum(exponent, 1, keepdims=True)
                p_now[at] = low(exponent)
                acc[at] = acc[at] * factor
            l_later[...] = matmul_t(x_ref[...], later)
            acc[...] += matmul(p_now[...], now)

        @pl.when(turn == turns - 1)
        def _():
            lane = lax.broadcasted_iota(jnp.int32, (count, LANES), 1)
            stats = jnp.zeros((count, LANES), F32)
            pieces = three_low(top[...]) + three_low(total[...])
            for j, piece in enumerate(pieces):
                stats = jnp.where(lane == j, piece.astype(F32), stats)
            out_ref[:, :D] = low(acc[...])
            out_ref[:, D:] = low(stats)
            copy = pltpu.make_async_copy(out_ref, out_hbm, sems.at[1])
            copy.start()
            copy.wait()

    def tile_at(shift):
        return pl.BlockSpec((VOCAB_TILE, D), lambda j: (jnp.minimum(2 * j + shift, last), 0))

    hbm = pl.BlockSpec(memory_space=pltpu.HBM)
    return pl.pallas_call(
        kernel,
        grid=(turns,),
        in_specs=[hbm] + [tile_at(shift) for shift in range(3)],
        out_specs=hbm,
        out_shape=shape_of(count, D + LANES, kind=BF16),
        scratch_shapes=[
            pltpu.VMEM((count, D), BF16),
            pltpu.VMEM((count, D + LANES), BF16),
            pltpu.VMEM((count, D), F32),
            pltpu.VMEM((count, 1), F32),
            pltpu.VMEM((count, 1), F32),
            pltpu.VMEM((count, VOCAB_TILE), F32),
            pltpu.VMEM((count, VOCAB_TILE), F32),
            pltpu.VMEM((count, VOCAB_TILE), BF16),
            pltpu.VMEM((count, VOCAB_TILE), BF16),
            pltpu.SemaphoreType.DMA((2,)),
        ],
        compiler_params=params_for(MOST_VMEM),
        name="vocabulary_head",
    )(rows.reshape(count, D), table, table, table).reshape(parts_in, each, D + LANES)


def swap_add(own, other):
    came = lax.ppermute(low(other), "section", [(0, 1), (1, 0)])
    return own + came.astype(F32)


def pick(first_section, both):
    return jnp.where(first_section, both[0], both[1])


def plan_requests(ids, weights, vocab_rows, slots, parts):
    turned = jnp.transpose(ids)

    def kernel(ids_ref, turned_ref, weights_ref, asked_ref, code_ref, spot_ref):
        here = lax.axis_index("section")
        i_index = lax.broadcasted_iota(jnp.int32, (IDS, IDS), 0)
        j_index = lax.broadcasted_iota(jnp.int32, (IDS, IDS), 1)
        earlier, later = j_index < i_index, i_index < j_index

        def owner_of(values):
            return jnp.floor((values.astype(F32) + 0.5) * (1.0 / vocab_rows)).astype(jnp.int32)

        def count(hits, axis):
            return jnp.sum(hits.astype(F32), axis, keepdims=True)

        most = jnp.zeros((1, 1), F32)
        for m in range(MICRO):
            row, col = ids_ref[m : m + 1], turned_ref[:, m : m + 1]
            same_id = row == col
            first_col = count(same_id & earlier, 1) == 0
            first_row = count(same_id & later, 0) == 0
            owner_row, owner_col = owner_of(row), owner_of(col)
            same_owner = owner_row == owner_col
            rank_row = count(same_owner & later & first_col, 0)
            rank_col = count(same_owner & earlier & first_row, 1)
            most = jnp.maximum(most, jnp.max(rank_row, 1, keepdims=True))

            @pl.when(here == m)
            def _():
                slot_row = jnp.sum(jnp.where(same_id & first_col, rank_col, 0.0), 0, keepdims=True)
                slot_col = jnp.sum(jnp.where(same_id & first_row, rank_row, 0.0), 1, keepdims=True)
                slot_row, slot_col = slot_row.astype(jnp.int32), slot_col.astype(jnp.int32)
                code_ref[...] = (owner_row + parts * first_row.astype(jnp.int32)) * 1024 + slot_row
                spot = jnp.where(slot_col < slots, owner_col * slots + slot_col, -1)
                spot_ref[...] = jnp.broadcast_to(spot, (IDS, LANES))
                lane = lax.broadcasted_iota(jnp.int32, (IDS, LANES), 1)
                local = (col - owner_col * vocab_rows).astype(F32)
                wanted = first_col & (slot_col < slots) & (slot_col == lane)
                wanted = jnp.where(wanted, local, 0.0)
                for part in range(parts):
                    asked = jnp.sum(jnp.where(owner_col == part, wanted, 0.0), 0, keepdims=True)
                    asked_ref[part] = asked.astype(jnp.int32)

        rounds = jnp.floor((most + 0.5) * (1.0 / slots)).astype(jnp.int32) + 1
        total = jnp.sum(jnp.sum(weights_ref[...], 0, keepdims=True), 1, keepdims=True)
        lane = lax.broadcasted_iota(jnp.int32, (1, LANES), 1)
        for part in range(parts):
            row = asked_ref[part]
            asked_ref[part] = jnp.where(lane == slots, rounds, jnp.where(lane == slots + 1, total, row))

    return pl.pallas_call(
        kernel,
        out_shape=[
            jax.ShapeDtypeStruct((parts, 1, LANES), jnp.int32),
            jax.ShapeDtypeStruct((1, IDS), jnp.int32),
            jax.ShapeDtypeStruct((IDS, LANES), jnp.int32),
        ],
        compiler_params=params_for(24),
        name="plan_requests",
    )(ids, turned, weights)


def fetch_rows(table, ids, first_section, weights, slots):
    parts = lax.axis_size("dp")
    vocab_rows = table.shape[0]
    asked, code, spot = plan_requests(ids, weights, vocab_rows, slots, parts)
    asked = lax.all_to_all(asked, "dp", 0, 0)[:, 0]
    total_rounds = jnp.max(asked[:, slots])
    weight_sum = jnp.sum(asked[:, slots + 1])

    def answer(asked):
        rows = table.at[asked.reshape(-1)].get(mode="promise_in_bounds").reshape(parts, slots, D)
        return lax.all_to_all(rows, "dp", 0, 0).reshape(parts * slots, D)

    came = answer(asked[:, :slots])

    def more(state):
        return state[0] < total_rounds

    def another(state):
        turn, extra = state
        place, slot = code[0] // 1024, code[0] % 1024
        owner, first = place % parts, place >= parts
        local = pick(first_section, ids) - owner * vocab_rows
        here = slot - turn * slots
        at = jnp.where((here >= 0) & (here < slots), owner * slots + here, -1)
        hits = at[:, None] == jnp.arange(parts * slots)[None, :]
        wanted = jnp.sum(jnp.where(hits & first[:, None], local[:, None], 0), 0).reshape(parts, slots)
        rows = answer(lax.all_to_all(wanted, "dp", 0, 0))
        return turn + 1, extra + matmul(hits.astype(BF16), rows)

    extra = lax.while_loop(more, another, (jnp.int32(1), jnp.zeros((IDS, D), F32)))[1]
    return came, spot, extra, weight_sum.astype(F32)


def three_low(values):
    high = low(values)
    rest = values - high.astype(F32)
    middle = low(rest)
    return [high, middle, low(rest - middle.astype(F32))]


def in_groups(count):
    return lax.axis_size("dp") == COUPLING_GROUPS and count == 4 * PART_GROUPS


def gather_params(master, vector):
    parts = lax.axis_size("dp")
    count, width = master.shape[0], vector.shape[0]
    if in_groups(count):
        lines = 4
        planes = parts // lines
        across_planes = [[plane * lines + line for plane in range(planes)] for line in range(lines)]
        in_plane = [[plane * lines + line for line in range(lines)] for plane in range(planes)]
        some = lax.all_gather(pack_own(master, vector[None]), "dp", axis_index_groups=across_planes)
        own = lax.all_gather(some, "dp", axis_index_groups=in_plane)
        return unpack_all(own, lax.ppermute(own, "section", [(0, 1), (1, 0)]), width)
    flat = low(jnp.concatenate([master.reshape(-1), vector]))
    gathered = lax.all_gather(flat, ("section", "dp")).reshape(MICRO, parts, -1)
    size = count * BLOCK**2
    all_blocks = gathered[:, :, :size].reshape(MICRO, parts * count, BLOCK, BLOCK)
    all_vectors = gathered[:, :, size:].reshape(MICRO, parts * width)
    both = [split_params(all_blocks[s], all_vectors[s]) for s in range(MICRO)]

    def stacked(which):
        down, bias_down, up, bias_up = (jnp.stack([pair[which][i] for pair in both]) for i in range(4))
        return Params(down, bias_down.astype(F32)[:, None], up, bias_up.astype(F32)[:, None])

    return stacked(0), stacked(1)


def sum_at_owners(grads, loss_part, count):
    parts = lax.axis_size("dp")
    width = sum(BIASES) // parts
    flat = []
    for adapter, coupling in grads:
        blocks, vector = join_params(adapter, coupling)
        flat.append(
            jnp.concatenate([blocks.reshape(parts, count * BLOCK**2), vector.reshape(parts, width)], 1)
        )
    first = lax.axis_index("section") == 0
    summed = swap_add(jnp.where(first, flat[0], flat[1]), jnp.where(first, flat[1], flat[0]))
    owned = jnp.sum(lax.all_to_all(low(summed), "dp", 0, 0).astype(F32), 0)
    blocks = owned[: count * BLOCK**2].reshape(count, BLOCK, BLOCK)
    pair = jnp.stack([jnp.sum(owned * owned), loss_part[0, 0]])
    pair = jnp.pad(pair, (0, LANES - 2))[None, None]
    return blocks, owned[count * BLOCK**2 :], jnp.broadcast_to(pair, (parts * MICRO, 1, LANES))


def to_coupling_owners(group):
    arrived = []
    for place in range(PART_GROUPS):
        route = []
        for part in range(COUPLING_GROUPS):
            owner, at = divmod(ADAPTER_GROUPS + part, PART_GROUPS)
            if at == place:
                route.append((part, owner))
        arrived.append(lax.ppermute(group, "dp", route))
    return arrived


def exact(spec, left, right):
    return jnp.einsum(spec, left, right, precision=HIGHEST)


def update(pair, products, grad_vector, state):
    master, momentum, stat_left, stat_right, root_left, root_right, vectors, vec_first, vec_second = state
    grad, left_square, right_square, turned = products
    turned_old = exact("nij,njk->nik", exact("nij,njk->nik", root_left, momentum), root_right)

    def kernel(pair_ref, grad_ref, left_ref, right_ref, turned_ref, old_ref, vector_ref, *refs):
        master_ref, momentum_ref, stat_left_ref, stat_right_ref, vectors_ref, first_ref, second_ref = refs[:7]
        outs = refs[7:]
        totals = jnp.sum(pair_ref[...], 0)
        norm = jnp.sqrt(totals[:, :1])
        factor = CLIP_NORM / jnp.maximum(norm, CLIP_NORM)
        outs[9][...] = norm
        outs[10][...] = totals[:, 1:2]
        for n in range(grad_ref.shape[0]):
            clipped = grad_ref[n] * factor
            outs[0][0, n] = clipped
            outs[1][0, n] = FIRST_DECAY * momentum_ref[n] + (1.0 - FIRST_DECAY) * clipped
            square = (1.0 - STAT_DECAY) * factor * factor
            outs[2][0, n] = STAT_DECAY * stat_left_ref[n] + square * left_ref[n]
            outs[3][0, n] = STAT_DECAY * stat_right_ref[n] + square * right_ref[n]
            direction = FIRST_DECAY * old_ref[n] + (1.0 - FIRST_DECAY) * factor * turned_ref[n]
            master_new = master_ref[n] - MAT_RATE * (direction + MAT_DECAY * master_ref[n])
            outs[4][0, n] = master_new
            outs[5][0, n] = low(master_new)
        clipped = vector_ref[...] * factor
        first_new = FIRST_DECAY * first_ref[...] + (1.0 - FIRST_DECAY) * clipped
        second_new = VEC_SECOND * second_ref[...] + (1.0 - VEC_SECOND) * clipped * clipped
        outs[6][...] = first_new
        outs[7][...] = second_new
        corrected_first = first_new / (1.0 - FIRST_DECAY**STEP)
        corrected_second = second_new / (1.0 - VEC_SECOND**STEP)
        outs[8][...] = vectors_ref[...] - VEC_RATE * (
            corrected_first / (jnp.sqrt(corrected_second) + VEC_EPS) + VEC_DECAY * vectors_ref[...]
        )

    blocks = (1,) + grad.shape
    width = vectors.shape
    shapes = [shape_of(*blocks)] * 5 + [shape_of(*blocks, kind=BF16)] + [shape_of(*width)] * 3
    return pl.pallas_call(
        kernel,
        out_shape=shapes + [shape_of(1, 1)] * 2,
        compiler_params=params_for(40),
        name="update",
    )(
        pair, grad, left_square, right_square, turned, turned_old, grad_vector,
        master, momentum, stat_left, stat_right, vectors, vec_first, vec_second,
    )


def shards(
    token_ids,
    lengths,
    positions,
    targets,
    loss_weights,
    embed_table,
    pos_table,
    norm_params,
    base_qkv,
    base_out,
    base_up,
    base_down,
    master,
    momentum,
    stat_left,
    stat_right,
    root_left,
    root_right,
    vectors,
    vec_first,
    vec_second,
):
    parts = lax.axis_size("dp")
    first_section = lax.axis_index("section") == 0
    slots = -(-IDS * 5 // (4 * parts * 16)) * 16

    adapter, coupling = gather_params(master[0], vectors[0])
    swap = [(0, 1), (1, 0)]
    pairs = [(w, lax.ppermute(w, "section", swap)) for w in (base_qkv, base_out, base_up, base_down)]
    came = lax.ppermute(norm_params, "section", swap)
    norms = jnp.concatenate([pick(first_section, (norm_params, came)), pick(first_section, (came, norm_params))])

    ids = jnp.concatenate([token_ids[:, 0], targets[:, 0]], -1)
    came, spot, extra, weight_sum = fetch_rows(embed_table, ids, first_section, loss_weights[:, 0], slots)
    length = pick(first_section, lengths)
    spots = pick(first_section, positions[:, 0])
    row_weights = pick(first_section, loss_weights[:, 0]).astype(F32)
    chosen = (spots[:, None] == jnp.arange(SEQ)[None, :]).astype(BF16)
    chosen_t = (spots[None, :] == jnp.arange(SEQ)[:, None]).astype(F32)

    ins = ForwardIn(came, spot, extra, pos_table, norms, chosen, adapter, coupling)
    kept, rows = forward_kernel(ins, (length,), pairs, parts, slots)

    rows = lax.all_to_all(rows, "dp", 0, 0)
    merged = lax.all_to_all(head_kernel(rows, embed_table), "dp", 0, 0)

    packed = in_groups(master.shape[1])
    row_weights = jnp.broadcast_to(row_weights[:, None], (COUNT, LANES))
    weight_row = jnp.broadcast_to(weight_sum, (1, LANES))
    adapter, coupling = adapter[::2], coupling[::2]
    ins = BackIn(
        merged, row_weights, weight_row, norms, chosen_t, adapter, coupling,
        kept.target_rows, kept.rest_0, kept.attention_1, kept.rest_1, kept.last,
    )
    back = backward_kernel(ins, (length,), pairs, packed)
    loss_part, mixed_grad = back.loss[:, :1], back.mixed
    if packed:
        own, other = back.adapters[MICRO:]
        summed = low(swap_add(own.astype(F32), other))
        summed, mixed_grad = lax.optimization_barrier((summed, mixed_grad))
        adapter_came = lax.all_to_all(summed, "dp", 0, 0)
    ins = FirstIn(
        kept.attention_0, mixed_grad, back.start, coupling, kept.one, kept.two, back.one, back.two,
        back.adapters[:MICRO] if packed else (),
    )
    grads = first_backward(ins, (length,), pairs, packed)
    if packed:
        adapter_total, squares = sum_adapter(adapter_came)
        came = lax.all_to_all(low(swap_add(*grads)), "dp", 0, 0)
        group, bias, pair = sum_coupling(came, squares, loss_part, parts * MICRO)
        products = grad_products(adapter_total, to_coupling_owners(group), root_left[0], root_right[0])
        grad_vector = bias[:1, : vectors.shape[1]]
    else:
        both = [(back.adapters[s], grads[4 * s : 4 * s + 4]) for s in range(MICRO)]
        grad, grad_vector, pair = sum_at_owners(both, loss_part, master.shape[1])
        turned = exact("nij,njk->nik", exact("nij,njk->nik", root_left[0], grad), root_right[0])
        products = grad, exact("nij,nkj->nik", grad, grad), exact("nji,njk->nik", grad, grad), turned
        grad_vector = grad_vector[None]
    pair = lax.all_to_all(pair, ("dp", "section"), 0, 0)
    state = (master, momentum, stat_left, stat_right, root_left, root_right)
    *outs, grad_norm, loss_sum = update(
        pair, products, grad_vector, [value[0] for value in state] + [vectors, vec_first, vec_second]
    )
    return (*outs, grad_norm[0, 0], loss_sum[0, 0], weight_sum)


def solution(mesh):
    rows = P(None, "dp", None)
    section = P("section", None, None)
    blocks = P("section", "dp", None, None)
    biases = P("section", "dp")
    return jax.shard_map(
        shards,
        mesh=mesh,
        in_specs=(rows, P(None, "dp"), rows, rows, rows, P("dp", None), P())
        + (section,) * 5
        + (blocks,) * 6
        + (biases,) * 3,
        out_specs=(blocks,) * 6 + (biases,) * 3 + (P(),) * 3,
        check_vma=False,
    )
```

```python
import functools
from typing import Any, NamedTuple

import jax
import jax.numpy as jnp
import numpy as np
from jax import lax
from jax.experimental import pallas as pl
from jax.experimental.pallas import tpu as pltpu
from jax.sharding import PartitionSpec as P

D = 768
HEADS = 12
HEAD_DIM = 64
BOT = 384
INV_H = 192
SEQ = 512
COUNT = 32
MICRO = 2
BLOCK = 48
STEP = 10
HALF = 384
IDS = SEQ + COUNT

HIGHEST = lax.Precision.HIGHEST
NORM_EPS = 1e-12
CLIP_NORM = 0.02
FIRST_DECAY = 0.9
STAT_DECAY = 0.99
MAT_RATE = 0.1
MAT_DECAY = 0.01
VEC_RATE = 0.05
VEC_SECOND = 0.999
VEC_EPS = 1e-08
VEC_DECAY = 0.01
F32 = jnp.float32
BF16 = jnp.bfloat16

CDF_SCALE = 0.42 / 2.0**0.5
CDF_POLY = (
    0.2368242366796694,
    0.239585811361218,
    0.1947261443420679,
    0.2687426685879861,
    -0.13052645834187002,
    0.4406726942003943,
    -0.32025628294963193,
    0.07023101752398136,
)


def matmul(left, right):
    return jnp.dot(left, right, preferred_element_type=F32)


def matmul_t(left, right):
    return lax.dot_general(left, right, (((1,), (1,)), ((), ())), preferred_element_type=F32)


def inner_rows(left, right):
    return lax.dot_general(left, right, (((0,), (0,)), ((), ())), preferred_element_type=F32)


def low(values):
    return values.astype(BF16)


def gelu_both(values):
    below = 1.0 + CDF_SCALE * jnp.abs(values)
    ratio = pl.reciprocal(below, approx=True)
    ratio = ratio * (2.0 - below * ratio)
    poly = jnp.full_like(ratio, 0.5 * CDF_POLY[-1])
    for factor in CDF_POLY[-2::-1]:
        poly = poly * ratio + 0.5 * factor
    bell = jnp.exp(-0.5 * values * values)
    tail = bell * (poly * ratio)
    cdf = jnp.where(values < 0, tail, 1.0 - tail)
    return values * cdf, cdf + values * (bell * (2.0 * np.pi) ** -0.5)


def layer_norm(values, gain, shift):
    centered = values - jnp.mean(values, -1, keepdims=True)
    inverse = lax.rsqrt(jnp.mean(centered * centered, -1, keepdims=True) + NORM_EPS)
    normal = centered * inverse
    return normal * gain + shift, (normal, inverse)


def norm_back(incoming, kept, gain):
    normal, inverse = kept
    scaled = incoming * gain
    return inverse * (
        scaled
        - jnp.mean(scaled, -1, keepdims=True)
        - normal * jnp.mean(scaled * normal, -1, keepdims=True)
    )


def to_blocks(matrix):
    rows_in, cols_in = matrix.shape
    return (
        matrix.reshape(rows_in // BLOCK, BLOCK, cols_in // BLOCK, BLOCK)
        .transpose(0, 2, 1, 3)
        .reshape(-1, BLOCK, BLOCK)
    )


def from_blocks(blocks, rows_in, cols_in):
    return (
        blocks.reshape(rows_in // BLOCK, cols_in // BLOCK, BLOCK, BLOCK)
        .transpose(0, 2, 1, 3)
        .reshape(rows_in, cols_in)
    )


def split_params(blocks, vector):
    adapter_count = D * BOT // BLOCK**2
    half_count = HALF * INV_H // BLOCK**2
    split_at = 2 * adapter_count
    adapter = (
        from_blocks(blocks[:adapter_count], D, BOT),
        vector[:BOT],
        from_blocks(blocks[adapter_count:split_at], BOT, D),
        vector[BOT : BOT + D],
    )
    coupling = (
        from_blocks(blocks[split_at : split_at + half_count], HALF, INV_H),
        vector[BOT + D : BOT + D + INV_H],
        from_blocks(blocks[split_at + half_count :], INV_H, HALF),
        vector[BOT + D + INV_H :],
    )
    return adapter, coupling


def join_params(adapter, coupling):
    blocks = jnp.concatenate(
        [to_blocks(adapter[0]), to_blocks(adapter[2]), to_blocks(coupling[0]), to_blocks(coupling[2])]
    )
    return blocks, jnp.concatenate([adapter[1], adapter[3], coupling[1], coupling[3]], 1)[0]


GROUP_ROWS = 72
LANES = 128


def params_for(mebibytes):
    return pltpu.CompilerParams(vmem_limit_bytes=mebibytes * 2**20)


def roll(values, shift):
    return pltpu.roll(values, shift, 1)


def lane_of(values):
    return lax.broadcasted_iota(jnp.int32, values.shape, 1)


def fold_half(values, upper):
    top, bottom = values[:24], values[24:]
    if upper:
        return jnp.where(lane_of(top) < 64, roll(top, 64), bottom)
    return jnp.where(lane_of(top) < 64, top, roll(bottom, 64))


def unfold_half(values, upper):
    turned = roll(values, 64)
    return jnp.concatenate([turned, values] if upper else [values, turned], 0)


def join_pair(main_0, rest_0, main_1, rest_1):
    left = lane_of(main_0) < 64
    turned = roll(main_1, 64)
    return (
        main_0,
        jnp.where(left, unfold_half(rest_0, False), turned),
        jnp.where(left, turned, unfold_half(rest_1, True)),
    )


def cut_pair(tile_0, tile_1, tile_2):
    left = lane_of(tile_0) < 64
    return (
        (tile_0, fold_half(tile_1, False)),
        (jnp.where(left, roll(tile_1, 64), roll(tile_2, 64)), fold_half(tile_2, True)),
    )


def chunk_rows(own_blocks):
    return own_blocks // 4 * GROUP_ROWS + 8


def bias_row(tiles, part, width):
    at, shift = divmod(part * width, LANES)
    lane = lane_of(tiles[0])
    row = tiles[at]
    if shift:
        row = jnp.where(lane < LANES - shift, roll(row, LANES - shift), roll(tiles[at + 1], LANES - shift))
    return jnp.where(lane < width, row, 0.0)


def bias_tiles(first, second, third, fourth):
    cut = lambda values: [values[:, at : at + LANES] for at in range(0, values.shape[1], LANES)]
    zero = jnp.zeros((1, LANES), F32)
    left = lane_of(zero) < 64
    third_tail = jnp.concatenate([third[:, LANES:]] * 2, 1)
    turned = [roll(tile, 64) for tile in cut(fourth)]
    joints = [jnp.where(left, one, two) for one, two in zip([third_tail] + turned, turned + [zero])]
    return cut(first) + cut(second) + [third[:, :LANES]] + joints + [zero]


def tiles_of_rows(rows, width):
    tiles = []
    for tile in range(-(-len(rows) * width // LANES)):
        value = jnp.zeros((8, LANES), F32)
        lane = lane_of(value)
        for part, row in enumerate(rows):
            shift = part * width - tile * LANES
            if shift >= LANES or shift + width <= 0:
                continue
            turned = roll(row, shift % LANES) if shift % LANES else row
            value = jnp.where((lane >= shift) & (lane < shift + width), turned, value)
        tiles.append(value)
    return tiles


def pack_own(master, vector, copies):
    count, width = master.shape[0], vector.shape[1]

    def kernel(master_ref, bias_ref, out_ref):
        row = lax.broadcasted_iota(jnp.int32, (BLOCK, 256), 0)
        col = lax.broadcasted_iota(jnp.int32, (BLOCK, 256), 1)
        pieces = []
        for group in range(count // 4):
            wide = jnp.zeros((BLOCK, 256), F32)
            for j in range(4):
                wide += matmul(low(master_ref[4 * group + j]), (col == row + BLOCK * j).astype(BF16))
            pieces += [wide[:, :LANES], fold_half(wide[:, LANES:], False)]
        bias = jnp.concatenate([bias_ref[...], jnp.zeros((1, LANES - width), F32)], 1)
        pieces.append(jnp.concatenate([bias, jnp.zeros((7, LANES), F32)], 0))
        packed = low(jnp.concatenate(pieces, 0))
        for copy in range(copies):
            out_ref[copy] = packed

    return pl.pallas_call(
        kernel,
        out_shape=jax.ShapeDtypeStruct((copies, chunk_rows(count), LANES), BF16),
        name="pack_own",
    )(master, vector)


MATRICES = ((D, BOT), (BOT, D), (HALF, INV_H), (INV_H, HALF))
BIASES = (BOT, D, INV_H, HALF)


def unpack_all(own, came, width):
    lines, planes, rows, _ = own.shape
    parts = lines * planes
    per_part = (rows - 8) // GROUP_ROWS

    def kernel(own_hbm, came_hbm, *refs):
        out_hbm, in_bufs, out_refs, in_sems, out_sems = refs[:8], refs[8], refs[9:17], refs[17], refs[18]
        here = lax.axis_index("section")
        copies = [
            pltpu.make_async_copy(ref, in_bufs.at[at], in_sems.at[i])
            for i, (ref, at) in enumerate(((own_hbm, here), (came_hbm, 1 - here)))
        ]
        for copy in copies:
            copy.start()
        for copy in copies:
            copy.wait()

        def unpack(s, carry):
            cache = {}

            def group(index):
                part = index // per_part
                if part not in cache:
                    cache.clear()
                    cache[part] = in_bufs[s, part % lines, part // lines].astype(F32)
                base = index % per_part * GROUP_ROWS
                chunk = cache[part]
                return chunk[base : base + BLOCK], chunk[base + BLOCK : base + GROUP_ROWS]

            index = 0
            for (height, columns), out_ref in zip(MATRICES, out_refs):
                for top in range(0, height, BLOCK):
                    if columns == INV_H:
                        main, rest = group(index)
                        index += 1
                        out_ref[s, top : top + BLOCK, :LANES] = low(main)
                        out_ref[s, top : top + BLOCK, LANES:] = low(unfold_half(rest, False)[:, :64])
                        continue
                    for left in range(0, columns, HALF):
                        tiles = join_pair(*group(index), *group(index + 1))
                        index += 2
                        for j, tile in enumerate(tiles):
                            at = left + j * LANES
                            out_ref[s, top : top + BLOCK, at : at + LANES] = low(tile)
            tiles = tiles_of_rows(
                [in_bufs[s, part % lines, part // lines, rows - 16 :].astype(F32)[8:] for part in range(parts)], width
            )
            first, second, third, fourth = out_refs[4:]
            first[s] = jnp.concatenate(tiles[:3], 1)[:1]
            second[s] = jnp.concatenate(tiles[3:9], 1)[:1]
            third[s] = jnp.concatenate([tiles[9], tiles[10][:, :64]], 1)[:1]
            left = lane_of(tiles[0]) < 64
            turned = [roll(tile, 64) for tile in tiles[10:14]]
            fourth[s] = jnp.concatenate(
                [jnp.where(left, one, two) for one, two in zip(turned, turned[1:])], 1
            )[:1]
            return carry

        lax.fori_loop(0, MICRO, unpack, 0)
        copies = [
            pltpu.make_async_copy(buf, ref, out_sems.at[i]) for i, (buf, ref) in enumerate(zip(out_refs, out_hbm))
        ]
        for copy in copies:
            copy.start()
        for copy in copies:
            copy.wait()

    shapes = [((MICRO,) + shape, BF16) for shape in MATRICES] + [((MICRO, 1, size), F32) for size in BIASES]
    hbm = pl.BlockSpec(memory_space=pltpu.HBM)
    arrays = pl.pallas_call(
        kernel,
        in_specs=[hbm] * 2,
        out_specs=[hbm] * 8,
        out_shape=[jax.ShapeDtypeStruct(*shape) for shape in shapes],
        scratch_shapes=[pltpu.VMEM((MICRO, lines, planes, rows, LANES), BF16)]
        + [pltpu.VMEM(*shape) for shape in shapes]
        + [pltpu.SemaphoreType.DMA((2,)), pltpu.SemaphoreType.DMA((8,))],
        compiler_params=params_for(MOST_VMEM),
        name="unpack_all",
    )(own, came)
    down, up, c_down, c_up, bias_down, bias_up, c_bias_down, c_bias_up = arrays
    return Params(down, bias_down, up, bias_up), Params(c_down, c_bias_down, c_up, c_bias_up)


ADAPTER_GROUPS = 2 * D * BOT // BLOCK**2 // 4
COUPLING_GROUPS = 2 * HALF * INV_H // BLOCK**2 // 4
PART_GROUPS = (ADAPTER_GROUPS + COUPLING_GROUPS) // COUPLING_GROUPS
PART_ROWS = PART_GROUPS * GROUP_ROWS


def groups_of(refs, shapes):
    groups = []
    for ref, (height, width) in zip(refs, shapes):
        for top in range(0, height, BLOCK):
            band = slice(top, top + BLOCK)
            if width == INV_H:
                tail = ref[band, LANES:]
                groups.append((ref[band, :LANES], fold_half(jnp.concatenate([tail, tail], 1), False)))
                continue
            for left in range(0, width, HALF):
                groups += cut_pair(*[ref[band, left + j * LANES : left + (j + 1) * LANES] for j in range(3)])
    return [jnp.concatenate(group, 0) for group in groups]


def pack_adapter(refs, store):
    groups = groups_of(refs, MATRICES[:2])
    empty = jnp.zeros((GROUP_ROWS, LANES), F32)
    for part in range(COUPLING_GROUPS):
        chunk = groups[part * PART_GROUPS : (part + 1) * PART_GROUPS]
        chunk += [empty] * (PART_GROUPS - len(chunk))
        store(part, low(jnp.concatenate(chunk, 0)))


def pack_coupling(refs, tiles, width, store):
    for part, group in enumerate(groups_of(refs, MATRICES[2:])):
        bias = jnp.concatenate([bias_row(tiles, part, width), jnp.zeros((7, LANES), F32)], 0)
        store(part, jnp.concatenate([group, bias], 0))


def sum_parts(came_ref):
    total = came_ref[0].astype(F32)
    for part in range(1, came_ref.shape[0]):
        total += came_ref[part].astype(F32)
    return total


def square_sum(values):
    return jnp.sum(jnp.sum(values * values, 0, keepdims=True), 1, keepdims=True)


def sum_adapter(came):
    def kernel(came_ref, total_ref, square_ref):
        total = sum_parts(came_ref)
        total_ref[...] = total
        square_ref[...] = square_sum(total)

    return pl.pallas_call(
        kernel,
        out_shape=[jax.ShapeDtypeStruct((PART_ROWS, LANES), F32), jax.ShapeDtypeStruct((1, 1), F32)],
        compiler_params=params_for(32),
        name="sum_adapter",
    )(came)


def sum_coupling(came, squares, loss_part, copies):
    def kernel(came_ref, square_ref, loss_ref, group_ref, bias_ref, pair_ref):
        total = sum_parts(came_ref)
        group_ref[...] = total[:GROUP_ROWS]
        bias_ref[...] = total[GROUP_ROWS:]
        squares = square_ref[...] + square_sum(total)
        lane = lax.broadcasted_iota(jnp.int32, (8, LANES), 1)
        pair = jnp.where(lane == 0, squares, jnp.where(lane == 1, loss_ref[:, :1], 0.0))
        for copy in range(copies):
            pair_ref[copy] = pair

    return pl.pallas_call(
        kernel,
        out_shape=[
            jax.ShapeDtypeStruct((GROUP_ROWS, LANES), F32),
            jax.ShapeDtypeStruct((8, LANES), F32),
            jax.ShapeDtypeStruct((copies, 8, LANES), F32),
        ],
        name="sum_coupling",
    )(came, squares, loss_part)


def grad_products(adapter_total, coupling_groups, root_left, root_right):
    count = 4 * PART_GROUPS

    def exact_dot(left, right, dims):
        return lax.dot_general(left, right, (dims, ((), ())), precision=HIGHEST, preferred_element_type=F32)

    def kernel(total_ref, left_ref, right_ref, *refs):
        group_refs, (grad_ref, left_square_ref, right_square_ref, turned_ref) = refs[:-4], refs[-4:]
        for group in range(PART_GROUPS):
            total = total_ref[group * GROUP_ROWS : (group + 1) * GROUP_ROWS] + group_refs[group][...]
            main, rest = total[:BLOCK], unfold_half(total[BLOCK:], False)
            lane = lane_of(main)
            pieces = (
                main,
                roll(main, 80),
                jnp.where(lane < 32, roll(main, 32), roll(rest, 32)),
                roll(rest, 112),
            )
            for j, values in enumerate(pieces):
                grad_ref[4 * group + j] = values[:, :BLOCK]
        for n in range(count):
            grad = grad_ref[n]
            left_square_ref[n] = exact_dot(grad, grad, ((1,), (1,)))
            right_square_ref[n] = exact_dot(grad, grad, ((0,), (0,)))
            turned_ref[n] = exact_dot(
                exact_dot(left_ref[n], grad, ((1,), (0,))), right_ref[n], ((1,), (0,))
            )

    return pl.pallas_call(
        kernel,
        out_shape=[jax.ShapeDtypeStruct((count, BLOCK, BLOCK), F32)] * 4,
        compiler_params=params_for(24),
        name="grad_products",
    )(adapter_total, root_left, root_right, *coupling_groups)


MOST_VMEM = 64
GROUP = 256
HEADS_IN = GROUP // HEAD_DIM
GROUPS = D // GROUP
FF = 3072
TILE = 512
TILES = FF // TILE
STEP_ROWS = 256
SMALL_ROWS = 32


def rows_of(count, size):
    return [slice(at, at + min(size, count)) for at in range(0, count, size)]


def shape_of(*dims, kind=F32):
    return jax.ShapeDtypeStruct(dims, kind)


class Params(NamedTuple):
    down: Any
    bias_down: Any
    up: Any
    bias_up: Any


class Branch(NamedTuple):
    lin: Any
    act: Any
    slope: Any


class Attention(NamedTuple):
    query: Any
    key: Any
    value: Any
    lse: Any


class Rest(NamedTuple):
    normal_1: Any
    inverse_1: Any
    slope: Any
    branch: Any
    normal_2: Any
    inverse_2: Any


class Last(NamedTuple):
    one: Any
    two: Any
    normal: Any
    inverse: Any
    normed: Any


class ForwardIn(NamedTuple):
    came: Any
    spot: Any
    extra: Any
    pos: Any
    norms: Any
    chosen: Any
    adapter: Any
    coupling: Any


class Forward(NamedTuple):
    target_rows: Any
    one: Any
    two: Any
    attention_0: Any
    rest_0: Any
    attention_1: Any
    rest_1: Any
    last: Any


class BackIn(NamedTuple):
    merged: Any
    row_weights: Any
    weight_sum: Any
    norms: Any
    chosen_t: Any
    adapter: Any
    coupling: Any
    target_rows: Any
    rest_0: Any
    attention_1: Any
    rest_1: Any
    last: Any


class Back(NamedTuple):
    loss: Any
    one: Any
    two: Any
    adapters: Any
    start: Any
    mixed: Any


class FirstIn(NamedTuple):
    attention: Any
    mixed: Any
    start: Any
    coupling: Any
    one: Any
    two: Any
    grads_one: Any
    grads_two: Any
    biases: Any


class Operand:
    def __init__(self, ref, buffer, sem):
        self.buffer, self.copy = buffer, pltpu.make_async_copy(ref, buffer, sem)
        self.started = self.waited = False

    def start(self):
        if not self.started:
            self.copy.start()
        self.started = True

    def get(self):
        self.start()
        if not self.waited:
            self.copy.wait()
        self.waited = True
        return self.buffer


class Result:
    def __init__(self, ref, buffer, sem):
        self.buffer, self.copy = buffer, pltpu.make_async_copy(buffer, ref, sem)
        self.sent = False

    def send(self):
        if not self.sent:
            self.copy.start()
        self.sent = True


def start(*operands):
    for operand in jax.tree.leaves(operands):
        operand.start()


def send(*results):
    for result in jax.tree.leaves(results):
        result.send()


def moved_call(body, scalars, ins, outs, pairs, scratch, name, raw_outs=()):
    in_leaves, in_tree = jax.tree.flatten(ins)
    out_leaves, out_tree = jax.tree.flatten(outs)

    def kernel(*refs):
        refs = list(refs)

        def take(count):
            taken, refs[:] = refs[:count], refs[count:]
            return taken

        scalar_refs, in_refs = take(len(scalars)), take(len(in_leaves))
        pair_refs = [tuple(take(2)) for _ in pairs]
        out_refs, raw_refs = take(len(out_leaves)), take(len(raw_outs))
        in_buffers, out_buffers, (in_sems, out_sems) = take(len(in_leaves)), take(len(out_leaves)), take(2)
        operands = [Operand(*two, in_sems.at[i]) for i, two in enumerate(zip(in_refs, in_buffers))]
        results = [Result(*two, out_sems.at[i]) for i, two in enumerate(zip(out_refs, out_buffers))]
        body(in_tree.unflatten(operands), out_tree.unflatten(results), scalar_refs, pair_refs, raw_refs, refs)
        send(results)
        for operand in operands:
            operand.get()
        for result in results:
            result.copy.wait()

    hbm = pl.BlockSpec(memory_space=pltpu.HBM)
    buffers = [pltpu.VMEM(value.shape, value.dtype) for value in (*in_leaves, *out_leaves)]
    results = pl.pallas_call(
        kernel,
        in_specs=[pl.BlockSpec(memory_space=pltpu.SMEM)] * len(scalars) + [hbm] * (len(in_leaves) + 2 * len(pairs)),
        out_specs=[hbm] * (len(out_leaves) + len(raw_outs)),
        out_shape=[*out_leaves, *raw_outs],
        scratch_shapes=buffers
        + [pltpu.SemaphoreType.DMA((len(in_leaves),)), pltpu.SemaphoreType.DMA((len(out_leaves),))]
        + list(scratch),
        compiler_params=params_for(MOST_VMEM),
        name=name,
    )(*scalars, *in_leaves, *[w for pair in pairs for w in pair])
    return out_tree.unflatten(results[: len(out_leaves)]), results[len(out_leaves) :]


def start_copy(pair, section, window, target, sem):
    own, came = pair
    here = lax.axis_index("section") == section

    @pl.when(here)
    def _():
        pltpu.make_async_copy(own.at[window], target, sem).start()

    @pl.when(jnp.logical_not(here))
    def _():
        pltpu.make_async_copy(came.at[window], target, sem).start()


def wait_copy(pair, window, target, sem):
    pltpu.make_async_copy(pair[0].at[window], target, sem).wait()


def qkv_window(group, part):
    return 0, slice(None), pl.ds(part * D + group * GROUP, GROUP)


def qkv_buffers():
    return [pltpu.VMEM((GROUPS, 3, D, GROUP), BF16), pltpu.SemaphoreType.DMA((GROUPS, 3))]


def start_qkv(pair, section, buffers):
    for group in range(GROUPS):
        for part in range(3):
            start_copy(pair, section, qkv_window(group, part), buffers[0].at[group, part], buffers[1].at[group, part])


def wait_qkv(pair, buffers, group, part):
    wait_copy(pair, qkv_window(0, 0), buffers[0].at[group, part], buffers[1].at[group, part])


UP_WINDOWS = [(0, slice(None), slice(j * TILE, (j + 1) * TILE)) for j in range(TILES)]
DOWN_WINDOWS = [(0, slice(j * TILE, (j + 1) * TILE), slice(None)) for j in range(TILES)]
OUT_WINDOW = (0, slice(None), slice(None))


def rest_buffers():
    return [
        pltpu.VMEM((D, D), BF16),
        pltpu.VMEM((TILES, D, TILE), BF16),
        pltpu.VMEM((TILES, TILE, D), BF16),
        pltpu.SemaphoreType.DMA((2 * TILES + 1,)),
    ]


def start_out(pairs, section, buffers):
    start_copy(pairs[0], section, OUT_WINDOW, buffers[0], buffers[3].at[2 * TILES])


def start_tiles(pairs, section, buffers):
    for j in range(TILES):
        start_copy(pairs[1], section, UP_WINDOWS[j], buffers[1].at[j], buffers[3].at[j])
        start_copy(pairs[2], section, DOWN_WINDOWS[j], buffers[2].at[j], buffers[3].at[TILES + j])


def wait_out(pairs, buffers):
    wait_copy(pairs[0], OUT_WINDOW, buffers[0], buffers[3].at[2 * TILES])


def wait_up(pairs, buffers, tile):
    wait_copy(pairs[1], UP_WINDOWS[0], buffers[1].at[tile], buffers[3].at[tile])


def wait_down(pairs, buffers, tile):
    wait_copy(pairs[2], DOWN_WINDOWS[0], buffers[2].at[tile], buffers[3].at[TILES + tile])


def across(values):
    return jnp.broadcast_to(values, (values.shape[0], LANES))


def group_columns(group):
    return pl.ds(pl.multiple_of(group * GROUP, GROUP), GROUP)


def tile_columns(tile):
    return pl.ds(pl.multiple_of(tile * TILE, TILE), TILE)


def head_mask(values, head):
    lane = lax.broadcasted_iota(jnp.int32, values.shape, 1)
    return (lane >= head * HEAD_DIM) & (lane < (head + 1) * HEAD_DIM)


def only_head(values, head):
    return jnp.where(head_mask(values, head), values, jnp.zeros_like(values))


def scaled_query(query):
    return low(query.astype(F32) * HEAD_DIM**-0.5)


def key_bias(length, shape, axis):
    return jnp.where(lax.broadcasted_iota(jnp.int32, shape, axis) < length, 0.0, -1e30)


def softmax_rows(scores):
    highest = jnp.max(scores, 1, keepdims=True)
    exponent = jnp.exp(scores - highest)
    total = jnp.sum(exponent, 1, keepdims=True)
    return low(exponent * (1.0 / total)), highest + jnp.log(total)


def branch_rows(low_in, weights):
    active, slope = gelu_both(matmul(low_in, weights[0]) + weights[1])
    active = low(active)
    return matmul(active, weights[2]) + weights[3], active, low(slope)


def alternate(*lists):
    steps = [((i + 0.5) / len(steps), k, step) for k, steps in enumerate(lists) for i, step in enumerate(steps)]
    for _, _, step in sorted(steps, key=lambda entry: entry[:2]):
        step()


def section_params(params, section):
    return [operand.get()[section] for operand in params]


def rest_rows(out, rows, section, norms, adapter, hidden, mixed, finish, scratch, pairs, buffers, after_loop=None):
    att_low, acc, u_even, u_odd, g_even, g_odd = scratch
    gain = lambda i: norms[section, i : i + 1]
    parts = rows_of(rows, STEP_ROWS)
    every = slice(0, rows)
    wait_out(pairs, buffers)
    for part in parts:
        first = hidden[part] + matmul(mixed[part], buffers[0][...])
        values, (normal, inverse) = layer_norm(first, gain(2), gain(3))
        acc[part] = values
        att_low[part] = low(values)
        out.normal_1.buffer[part] = normal
        out.inverse_1.buffer[part] = across(inverse)
    send(out.normal_1, out.inverse_1)
    wait_up(pairs, buffers, 0)
    g_odd[every] = jnp.zeros_like(g_odd[every])

    def gelu_steps(u_ref, g_ref, tile):
        def step(at):
            active, slope = gelu_both(u_ref[at])
            g_ref[at] = low(active)
            out.slope.buffer[at, tile_columns(tile)] = low(slope)

        return [functools.partial(step, at) for at in rows_of(rows, SMALL_ROWS)]

    def up_steps(u_ref, tile):
        def step(columns):
            u_ref[every, columns] = matmul(att_low[every], buffers[1][tile, :, columns])

        return [functools.partial(step, columns) for columns in rows_of(TILE, GROUP)]

    def down_steps(g_ref, tile):
        def step(columns):
            acc[every, columns] += matmul(g_ref[every], buffers[2][tile, :, columns])

        return [functools.partial(step, columns) for columns in rows_of(D, GROUP)]

    alternate(up_steps(u_even, 0))

    def turn(j, carry):
        even, odd = 2 * j, 2 * j + 1
        before, after = jnp.maximum(even - 1, 0), jnp.minimum(even + 2, TILES - 1)
        wait_down(pairs, buffers, even)
        wait_up(pairs, buffers, odd)
        wait_down(pairs, buffers, odd)

        @pl.when(even + 2 < TILES)
        def _():
            wait_up(pairs, buffers, even + 2)

        alternate(gelu_steps(u_even, g_even, even), down_steps(g_odd, before) + up_steps(u_odd, odd))
        alternate(gelu_steps(u_odd, g_odd, odd), down_steps(g_even, even) + up_steps(u_even, after))
        return carry

    lax.fori_loop(0, TILES // 2, turn, 0)
    alternate(down_steps(g_odd, TILES - 1))
    if after_loop is not None:
        after_loop()
    send(out.slope)
    weights = section_params(adapter, section)
    for part in parts:
        summed = acc[part]
        low_in = low(summed)
        added, *kept = branch_rows(low_in, weights)
        for result, value in zip(out.branch, (low_in, *kept)):
            result.buffer[part] = value
        values, (normal, inverse) = layer_norm(summed + added, gain(4), gain(5))
        out.normal_2.buffer[part], out.inverse_2.buffer[part] = normal, across(inverse)
        finish(part, values)
    send(out.branch, out.normal_2, out.inverse_2)


def low_shape(*dims):
    return shape_of(*dims, kind=BF16)


def branch_shapes(rows, wide, narrow):
    return Branch(low_shape(rows, wide), low_shape(rows, narrow), low_shape(rows, narrow))


def rest_shapes(rows):
    wide, thin = shape_of(rows, D), shape_of(rows, LANES)
    return Rest(wide, thin, low_shape(rows, FF), branch_shapes(rows, D, BOT), wide, thin)


def forward_kernel(ins, scalars, pairs, parts, slots):
    coupling_shapes = lambda rows: branch_shapes(rows, HALF, INV_H)
    outs = Forward(
        target_rows=shape_of(COUNT, D),
        one=coupling_shapes(SEQ),
        two=coupling_shapes(SEQ),
        attention_0=Attention(*[low_shape(SEQ, D)] * 3, shape_of(GROUPS, 8, SEQ)),
        rest_0=rest_shapes(SEQ),
        attention_1=Attention(
            low_shape(COUNT, D), *[low_shape(SEQ, D)] * 2, shape_of(GROUPS, HEADS_IN * COUNT, LANES)
        ),
        rest_1=rest_shapes(COUNT),
        last=Last(
            coupling_shapes(COUNT), coupling_shapes(COUNT),
            shape_of(COUNT, D), shape_of(COUNT, LANES), low_shape(COUNT, D),
        ),
    )

    def body(ins, out, scalar_refs, pair_refs, raw_refs, scratch):
        length = scalar_refs[0][0]
        hidden, x_low, s_even, s_odd, p_even, p_odd, lse_buf, mixed, section_out = scratch[:9]
        at_spots, at_low, mixed_1 = scratch[9:12]
        rest_scratch, qkv_0, qkv_1, rest_w = scratch[12:18], scratch[18:20], scratch[20:22], scratch[22:26]
        row_sems, joined = scratch[26:28]
        qkv_pair, rest_pairs = pair_refs[0], pair_refs[1:]

        start(ins.came, ins.spot, ins.extra, ins.pos, ins.norms, ins.coupling)
        start_qkv(qkv_pair, 0, qkv_0)
        start_out(rest_pairs, 0, rest_w)
        start(ins.adapter, ins.chosen)
        start_tiles(rest_pairs, 0, rest_w)
        start_qkv(qkv_pair, 1, qkv_1)
        norms = ins.norms.get()
        norm = lambda s, i: norms[s, i : i + 1]

        came, spot, extra = ins.came.get(), ins.spot.get(), ins.extra.get()

        def rows_at(part):
            lane = lax.broadcasted_iota(jnp.int32, (part.stop - part.start, parts * slots), 1)
            hits = (spot[part][:, :1] == lane).astype(BF16)
            return matmul(hits, came[...]) + extra[part]

        out.target_rows.buffer[...] = rows_at(slice(SEQ, SEQ + COUNT))
        send(out.target_rows)
        one, two = section_params(ins.coupling, 0), section_params(ins.coupling, 1)

        def put(results, part, *values):
            for result, value in zip(results, values):
                result.buffer[part] = value

        for part in rows_of(SEQ, STEP_ROWS):
            started, _ = layer_norm(rows_at(part) + ins.pos.get()[part].astype(F32), norm(0, 0), norm(0, 1))
            left, right = started[:, :HALF], started[:, HALF:]
            low_one = low(right)
            added, active, slope = branch_rows(low_one, one)
            put(out.one, part, low_one, active, slope)
            left = left + added
            low_two = low(left)
            added, active, slope = branch_rows(low_two, two)
            put(out.two, part, low_two, active, slope)
            right = right + added
            hidden[part, :HALF] = left
            hidden[part, HALF:] = right
            x_low[part, :HALF] = low_two
            x_low[part, HALF:] = low(right)
        send(out.one, out.two)

        lse_buf[...] = jnp.zeros((SEQ, LANES), F32)
        q_ref, k_ref, v_ref, lse_ref = (result.buffer for result in out.attention_0)

        def attend(group, carry):
            columns = group_columns(group)
            for part, ref in enumerate((q_ref, k_ref, v_ref)):
                wait_qkv(qkv_pair, qkv_0, group, part)
                ref[:, columns] = low(matmul(x_low[...], qkv_0[0][group, part]))
            query = scaled_query(q_ref[:, columns])
            key, value = k_ref[:, columns], v_ref[:, columns]
            bias = key_bias(length, (1, SEQ), 1)
            lane = lax.broadcasted_iota(jnp.int32, (SMALL_ROWS * 2, LANES), 1)
            buffers = ((s_even, p_even), (s_odd, p_odd)) * 2

            def score_steps(head):
                def step():
                    buffers[head][0][...] = matmul_t(only_head(query, head), key)

                return [step] if head < HEADS_IN else []

            def soft_steps(head):
                def step(rows):
                    soft, lse = softmax_rows(buffers[head][0][rows] + bias)
                    buffers[head][1][rows] = soft
                    lse_buf[rows] = jnp.where(lane == head, lse, lse_buf[rows])

                return [functools.partial(step, rows) for rows in rows_of(SEQ, SMALL_ROWS * 2)]

            def mix_steps(head):
                def step():
                    mixed_head = matmul(buffers[head][1][...], value)
                    if head == 0:
                        joined[...] = mixed_head
                    else:
                        joined[...] = jnp.where(head_mask(mixed_head, head), mixed_head, joined[...])

                return [step] if head >= 0 else []

            alternate(score_steps(0))
            for head in range(HEADS_IN):
                alternate(soft_steps(head), score_steps(head + 1) + mix_steps(head - 1))
            alternate(mix_steps(HEADS_IN - 1))
            mixed[:, columns] = low(joined[...])
            lse_ref[group] = jnp.transpose(lse_buf[...])[:8]
            return carry

        lax.fori_loop(0, GROUPS, attend, 0)
        send(out.attention_0)

        def to_section_out(part, values):
            section_out[part] = low(values)

        def next_weights():
            start_out(rest_pairs, 1, rest_w)
            start_tiles(rest_pairs, 1, rest_w)

        rest_rows(
            out.rest_0, SEQ, 0, norms, ins.adapter, hidden, mixed, to_section_out,
            rest_scratch, rest_pairs, rest_w, next_weights,
        )

        at_spots[...] = matmul(ins.chosen.get()[...], section_out[...])
        at_low[...] = low(at_spots[...])
        q_1, k_1, v_1, lse_1 = (result.buffer for result in out.attention_1)

        def attend_spots(group, carry):
            columns = group_columns(group)
            for part, ref in enumerate((q_1, k_1, v_1)):
                wait_qkv(qkv_pair, qkv_1, group, part)
                source = at_low if part == 0 else section_out
                ref[:, columns] = low(matmul(source[...], qkv_1[0][group, part]))
            query = scaled_query(q_1[:, columns])
            query = jnp.concatenate([only_head(query, head) for head in range(HEADS_IN)], 0)
            bias = key_bias(length, (1, SEQ), 1)
            soft, lse = softmax_rows(matmul_t(query, k_1[:, columns]) + bias)
            lse_1[group] = across(lse)
            every = matmul(soft, v_1[:, columns])
            joined = every[:COUNT]
            for head in range(1, HEADS_IN):
                joined = jnp.where(head_mask(joined, head), every[head * COUNT : (head + 1) * COUNT], joined)
            mixed_1[:, columns] = low(joined)
            return carry

        lax.fori_loop(0, GROUPS, attend_spots, 0)
        send(out.attention_1)

        def to_normed(part, values):
            left, right = values[:, :HALF], values[:, HALF:]
            low_two = low(left)
            taken, active, slope = branch_rows(low_two, two)
            put(out.last.two, part, low_two, active, slope)
            right = right - taken
            low_one = low(right)
            taken, active, slope = branch_rows(low_one, one)
            put(out.last.one, part, low_one, active, slope)
            left = left - taken
            values, (normal, inverse) = layer_norm(jnp.concatenate([left, right], 1), norm(1, 0), norm(1, 1))
            put(out.last[2:], part, normal, across(inverse), low(values))

        rest_rows(
            out.rest_1, COUNT, 1, norms, ins.adapter, at_spots, mixed_1, to_normed,
            rest_scratch, rest_pairs, rest_w,
        )
        copies = [
            pltpu.make_async_copy(out.last.normed.buffer, raw_refs[0].at[part], row_sems.at[part]) for part in range(parts)
        ]
        for copy in copies:
            copy.start()
        for copy in copies:
            copy.wait()

    buffer = lambda *dims: pltpu.VMEM(dims, F32)
    buffer_low = lambda *dims: pltpu.VMEM(dims, BF16)
    scratch = [buffer(SEQ, D), buffer_low(SEQ, D), buffer(SEQ, SEQ), buffer(SEQ, SEQ)]
    scratch += [buffer_low(SEQ, SEQ), buffer_low(SEQ, SEQ), buffer(SEQ, LANES)]
    scratch += [buffer_low(SEQ, D), buffer_low(SEQ, D)]
    scratch += [buffer(COUNT, D), buffer_low(COUNT, D), buffer_low(COUNT, D)]
    scratch += [buffer_low(SEQ, D), buffer(SEQ, D), buffer(SEQ, TILE), buffer(SEQ, TILE)]
    scratch += [buffer_low(SEQ, TILE), buffer_low(SEQ, TILE)]
    scratch += qkv_buffers() + qkv_buffers() + rest_buffers()
    scratch += [pltpu.SemaphoreType.DMA((parts,)), buffer(SEQ, GROUP)]
    raw = [low_shape(parts, COUNT, D)]
    kept, (rows,) = moved_call(body, scalars, ins, outs, pairs, scratch, "forward", raw)
    return kept, rows


def column_sum(values):
    return jnp.sum(values.astype(F32), 0, keepdims=True)


def branch_grads(grad_low, kept, weights, out_refs):
    low_in, active, slope = kept
    hidden_grad = low(matmul_t(grad_low, weights[2]) * slope.astype(F32))
    out_refs[0][...] = inner_rows(low_in, hidden_grad)
    out_refs[1][...] = column_sum(hidden_grad)
    out_refs[2][...] = inner_rows(active, grad_low)
    out_refs[3][...] = column_sum(grad_low)
    return hidden_grad


ADAPTER_GRADS = ((D, BOT), (1, BOT), (BOT, D), (1, D))
COUPLING_GRADS = ((HALF, INV_H), (1, INV_H), (INV_H, HALF), (1, HALF))


def branch_kept(branch):
    return [operand.get()[...] for operand in branch]


def grad_weights(pair, section):
    return [pair[0].get()[section], None, pair[1].get()[section]]


def rest_back_rows(kept, rows, section, norms, adapter, incoming, scratch, pairs, buffers, grad_refs, results, packing=None):
    summed_low, acc, second_low = scratch
    start_ref, mixed_ref = results
    gain = lambda i: norms[section, i : i + 1]
    parts = rows_of(rows, STEP_ROWS)
    weights = grad_weights(adapter, section)
    for part in parts:
        norm_kept = kept.normal_2.get()[part], kept.inverse_2.get()[part, :1]
        second = norm_back(incoming(part), norm_kept, gain(4))
        acc[part] = second
        second_low[part] = low(second)
    hidden_grad = branch_grads(second_low[:rows], branch_kept(kept.branch), weights, grad_refs)
    for part in parts:
        total = acc[part] + matmul_t(hidden_grad[part], weights[0])
        acc[part] = total
        summed_low[part] = low(total)
    if packing is not None:
        packing()
    slope = kept.slope.get()

    def turn(j, carry):
        for now in (2 * j, 2 * j + 1):
            wait_up(pairs, buffers, now)
            wait_down(pairs, buffers, now)
        for now in (2 * j, 2 * j + 1):
            for part in parts:
                inner = matmul_t(summed_low[part], buffers[2][now])
                inner = low(inner * slope[part, tile_columns(now)].astype(F32))
                acc[part] += matmul_t(inner, buffers[1][now])
        return carry

    lax.fori_loop(0, TILES // 2, turn, 0)
    wait_out(pairs, buffers)
    for part in parts:
        norm_kept = kept.normal_1.get()[part], kept.inverse_1.get()[part, :1]
        back = norm_back(acc[part], norm_kept, gain(2))
        start_ref[part] = back
        mixed_ref[part] = low(matmul_t(low(back), buffers[0][...]))


def backward_kernel(ins, scalars, pairs, packed):
    parts = ins.merged.shape[0]
    grads = [shape_of(*dims) for dims in COUPLING_GRADS]
    if packed:
        chunks = low_shape(COUPLING_GROUPS, PART_ROWS, LANES)
        adapters = [[shape_of(1, BOT), shape_of(1, D)] for _ in range(MICRO)] + [chunks, chunks]
    else:
        adapters = [[shape_of(*dims) for dims in ADAPTER_GRADS] for _ in range(MICRO)]
    outs = Back(shape_of(1, LANES), grads, grads, adapters, shape_of(SEQ, D), low_shape(SEQ, D))

    def body(ins, out, scalar_refs, pair_refs, raw_refs, scratch):
        length = scalar_refs[0][0]
        rest_scratch, spot, mixed_1, acc_1, section_grad = scratch[:3], *scratch[3:7]
        qkv_w, rest_w, refs = scratch[7:9], scratch[9:13], scratch[13:]
        qkv_pair, rest_pairs = pair_refs[0], pair_refs[1:]

        start(ins.merged, ins.row_weights, ins.weight_sum, ins.target_rows, ins.last, ins.norms)
        start(ins.coupling, ins.adapter, ins.rest_1)
        start_tiles(rest_pairs, 1, rest_w)
        start_out(rest_pairs, 1, rest_w)
        start_qkv(qkv_pair, 1, qkv_w)
        start(ins)
        norms = ins.norms.get()

        def from_head(part):
            merged = ins.merged.get()
            stats = merged[:, :, D:].astype(F32)
            highest = jnp.sum(stats[:, :, :3], 2, keepdims=True)
            totals = jnp.sum(stats[:, :, 3:6], 2, keepdims=True)
            top = jnp.max(highest, 0)
            factor = jnp.exp(highest - top[None])
            total = jnp.sum(totals * factor, 0)
            expected = jnp.zeros((COUNT, D), F32)
            for i in range(parts):
                expected += merged[i, :, :D].astype(F32) * (factor[i] / total)
            target = ins.target_rows.get()[...]
            target_logit = jnp.sum(ins.last.normed.get()[...].astype(F32) * target, 1, keepdims=True)
            weight = ins.row_weights.get()[...]
            row_losses = weight[:, :1] * (top + jnp.log(total) - target_logit)
            out.loss.buffer[...] = across(jnp.sum(row_losses, 0, keepdims=True))
            normed_grad = (weight / ins.weight_sum.get()[...])[:, :1] * (expected - target)
            kept = (ins.last.normal.get()[...], ins.last.inverse.get()[:, :1])
            restored = norm_back(normed_grad, kept, norms[1, 0:1])
            left, right = restored[:, :HALF], restored[:, HALF:]
            one, two = (grad_weights(ins.coupling, s) for s in range(MICRO))
            refs_of = lambda results: [result.buffer for result in results]
            hidden = branch_grads(low(-left), branch_kept(ins.last.one), one, refs_of(out.one))
            right = right + matmul_t(hidden, one[0])
            hidden = branch_grads(low(-right), branch_kept(ins.last.two), two, refs_of(out.two))
            left = left + matmul_t(hidden, two[0])
            return jnp.concatenate([left, right], 1)

        def grads_of(section):
            buffers = [result.buffer for result in out.adapters[section]]
            return (refs[0], buffers[0], refs[1], buffers[1]) if packed else buffers

        def pack_second():
            def store(part, chunk):
                refs[2][part] = chunk

            pack_adapter((refs[0], refs[1]), store)

        def pack_both():
            here = lax.axis_index("section") == 0
            own, other = out.adapters[2:]

            def store(part, chunk):
                arrived = refs[2][part]
                own.buffer[part] = jnp.where(here, chunk, arrived)
                other.buffer[part] = jnp.where(here, arrived, chunk)

            pack_adapter((refs[0], refs[1]), store)
            send(own, other)

        rest_back_rows(
            ins.rest_1, COUNT, 1, norms, ins.adapter, from_head, rest_scratch, rest_pairs, rest_w,
            grads_of(1), (spot, mixed_1), pack_second if packed else None,
        )
        start_tiles(rest_pairs, 0, rest_w)
        start_out(rest_pairs, 0, rest_w)

        acc_1[...] = jnp.zeros_like(acc_1)
        q_ref, k_ref, v_ref, lse_ref = (operand.get() for operand in ins.attention_1)

        def attend_back(group, carry):
            columns = group_columns(group)
            stack = lambda values: jnp.concatenate([only_head(values, h) for h in range(HEADS_IN)], 0)
            query = stack(scaled_query(q_ref[:, columns]))
            mixed = stack(mixed_1[:, columns])
            key, value = k_ref[:, columns], v_ref[:, columns]
            scores = matmul_t(query, key) + key_bias(length, (1, SEQ), 1)
            soft = jnp.exp(scores - lse_ref[group][:, :1])
            soft_grad = matmul_t(mixed, value)
            delta = jnp.sum(soft_grad * soft, 1, keepdims=True)
            score_grad = low(soft * (soft_grad - delta))
            every = matmul(score_grad, key)
            query_grad = every[:COUNT]
            for head in range(1, HEADS_IN):
                query_grad = jnp.where(
                    head_mask(query_grad, head), every[head * COUNT : (head + 1) * COUNT], query_grad
                )
            query_grad = low(query_grad * HEAD_DIM**-0.5)
            key_grad = low(inner_rows(score_grad, query))
            value_grad = low(inner_rows(low(soft), mixed))
            for part in range(3):
                wait_qkv(qkv_pair, qkv_w, group, part)
            spot[...] += matmul_t(query_grad, qkv_w[0][group, 0])
            acc_1[...] += matmul_t(key_grad, qkv_w[0][group, 1]) + matmul_t(value_grad, qkv_w[0][group, 2])
            return carry

        lax.fori_loop(0, GROUPS, attend_back, 0)
        placed = jnp.dot(ins.chosen_t.get()[...], spot[...], precision=HIGHEST, preferred_element_type=F32)
        section_grad[...] = low(acc_1[...] + placed)

        rest_back_rows(
            ins.rest_0, SEQ, 0, norms, ins.adapter, lambda part: section_grad[part].astype(F32),
            rest_scratch, rest_pairs, rest_w, grads_of(0), (out.start.buffer, out.mixed.buffer),
            pack_both if packed else None,
        )

    scratch = [pltpu.VMEM((SEQ, D), BF16), pltpu.VMEM((SEQ, D), F32), pltpu.VMEM((SEQ, D), BF16)]
    scratch += [pltpu.VMEM((COUNT, D), F32), pltpu.VMEM((COUNT, D), BF16), pltpu.VMEM((SEQ, D), F32)]
    scratch += [pltpu.VMEM((SEQ, D), BF16)] + qkv_buffers() + rest_buffers()
    if packed:
        scratch += [pltpu.VMEM((D, BOT), F32), pltpu.VMEM((BOT, D), F32)]
        scratch += [pltpu.VMEM((COUPLING_GROUPS, PART_ROWS, LANES), BF16)]
    return moved_call(body, scalars, ins, outs, pairs, scratch, "backward")[0]


def first_backward(ins, scalars, pairs, packed):
    if packed:
        dims = (COUPLING_GROUPS, GROUP_ROWS + 8, LANES)
        outs = (shape_of(*dims), low_shape(*dims))
    else:
        outs = [shape_of(*dims) for dims in COUPLING_GRADS * 2]

    def body(ins, out, scalar_refs, pair_refs, raw_refs, scratch):
        length = scalar_refs[0][0]
        s_even, s_odd, d_even, d_odd, p_even, p_odd, ds_even, ds_odd = scratch[:8]
        qkv_w, (key_grad, value_grad, query_grad_t), refs = scratch[8:10], scratch[10:13], scratch[13:]
        start(ins.attention, ins.mixed)
        start_qkv(pair_refs[0], 0, qkv_w)
        start(ins)
        q_ref, k_ref, v_ref, lse_ref = (operand.get() for operand in ins.attention)
        mixed_ref, acc = ins.mixed.get(), ins.start.get()

        def attend_back(group, carry):
            columns = group_columns(group)
            query = scaled_query(q_ref[:, columns])
            key, value, mixed = k_ref[:, columns], v_ref[:, columns], mixed_ref[:, columns]
            lse_rows = lse_ref[group]
            key_t = jnp.transpose(key)
            buffers = ((s_even, d_even, p_even, ds_even), (s_odd, d_odd, p_odd, ds_odd)) * 2

            def product_steps(head):
                def scores():
                    buffers[head][0][...] = matmul_t(only_head(key, head), query)

                def soft_grads():
                    buffers[head][1][...] = matmul_t(only_head(value, head), mixed)

                return [scores, soft_grads] if head < HEADS_IN else []

            def soft_steps(head):
                s_buf, d_buf, p_low, ds_low = buffers[head]
                delta = [jnp.zeros((8, SEQ), F32)]

                def soft_step(rows):
                    valid = lax.broadcasted_iota(jnp.int32, (SMALL_ROWS, 1), 0) + rows.start < length
                    bias = jnp.where(valid, 0.0, -1e30)
                    soft = jnp.exp(s_buf[rows] + bias - lse_rows[head : head + 1])
                    s_buf[rows] = soft
                    p_low[rows] = low(soft)
                    product = soft * d_buf[rows]
                    for at in range(0, SMALL_ROWS, 8):
                        delta[0] = delta[0] + product[at : at + 8]

                def sum_step():
                    delta[0] = jnp.sum(delta[0], 0, keepdims=True)

                def grad_step(rows):
                    ds_low[rows] = low(s_buf[rows] * (d_buf[rows] - delta[0]))

                parts = rows_of(SEQ, SMALL_ROWS)
                steps = [functools.partial(soft_step, rows) for rows in parts] + [sum_step]
                return steps + [functools.partial(grad_step, rows) for rows in parts]

            def grad_steps(head):
                _, _, p_low, ds_low = buffers[max(head, 0)]

                def add(ref, grad):
                    ref[...] = grad if head == 0 else ref[...] + grad

                def value_step():
                    add(value_grad, matmul(p_low[...], only_head(mixed, head)))

                def key_step():
                    add(key_grad, matmul(ds_low[...], only_head(query, head)))

                def query_step():
                    rows = slice(head * HEAD_DIM, (head + 1) * HEAD_DIM)
                    query_grad_t[rows] = matmul(key_t[rows], ds_low[...])

                return [value_step, key_step, query_step] if head >= 0 else []

            alternate(product_steps(0))
            for head in range(HEADS_IN):
                alternate(soft_steps(head), product_steps(head + 1) + grad_steps(head - 1))
            alternate(grad_steps(HEADS_IN - 1))
            query_grad = jnp.transpose(query_grad_t[...]) * HEAD_DIM**-0.5
            for part, grad in enumerate((query_grad, key_grad[...], value_grad[...])):
                wait_qkv(pair_refs[0], qkv_w, group, part)
                acc[...] += matmul_t(low(grad), qkv_w[0][group, part])
            return carry

        lax.fori_loop(0, GROUPS, attend_back, 0)
        one, two = (grad_weights(ins.coupling, s) for s in range(MICRO))
        grads = refs if packed else [result.buffer for result in out]
        hidden = branch_grads(low(acc[:, HALF:]), branch_kept(ins.two), two, grads[4:])
        left = acc[:, :HALF] + matmul_t(hidden, two[0])
        branch_grads(low(left), branch_kept(ins.one), one, grads[:4])
        for ref, operand in zip(grads, (*ins.grads_one, *ins.grads_two)):
            ref[...] += operand.get()[...]
        if not packed:
            return
        here = lax.axis_index("section")
        for s in range(MICRO):
            some = grads[4 * s : 4 * s + 4]
            biases = [operand.get()[...] for operand in ins.biases[s]]
            tiles = bias_tiles(*biases, some[1][...], some[3][...])

            def store(part, chunk, s=s):
                @pl.when(here == s)
                def _():
                    out[0].buffer[part] = chunk

                @pl.when(here != s)
                def _():
                    out[1].buffer[part] = low(chunk)

            pack_coupling((some[0], some[2]), tiles, sum(BIASES) // COUPLING_GROUPS, store)

    scratch = [pltpu.VMEM((SEQ, SEQ), F32)] * 4 + [pltpu.VMEM((SEQ, SEQ), BF16)] * 4 + qkv_buffers()
    scratch += [pltpu.VMEM((SEQ, GROUP), F32)] * 2 + [pltpu.VMEM((GROUP, SEQ), F32)]
    if packed:
        scratch += [pltpu.VMEM(dims, F32) for dims in COUPLING_GRADS * 2]
    return moved_call(body, scalars, ins, outs, pairs[:1], scratch, "first_backward")[0]


VOCAB_TILE = 1280


def head_stats(top, total):
    lane = lax.broadcasted_iota(jnp.int32, (top.shape[0], LANES), 1)
    stats = jnp.zeros(lane.shape, F32)
    for j, piece in enumerate(three_low(top) + three_low(total)):
        stats = jnp.where(lane == j, piece.astype(F32), stats)
    return low(stats)


def head_kernel(rows, table):
    parts, each, _ = rows.shape
    count, vocab = parts * each, table.shape[0]
    tiles = pl.cdiv(vocab, VOCAB_TILE)
    if vocab < VOCAB_TILE or (vocab - VOCAB_TILE) % 16 or tiles % 2:
        return blocked_head_kernel(rows, table)
    starts = [min(tile * VOCAB_TILE, vocab - VOCAB_TILE) for tile in range(tiles)]

    def kernel(x_hbm, table_hbm, out_hbm, *refs):
        x_ref, out_ref, entries, acc, top, total, factor_even, factor_odd = refs[:8]
        l_even, l_odd, p_even, p_odd, sems = refs[8:]
        fetch = pltpu.make_async_copy(x_hbm, x_ref, sems.at[tiles])
        fetch.start()
        for tile, at in enumerate(starts):
            copy = pltpu.make_async_copy(table_hbm.at[pl.ds(at, VOCAB_TILE)], entries.at[tile], sems.at[tile])
            copy.start()

        def wait_tile(tile):
            window = table_hbm.at[pl.ds(0, VOCAB_TILE)]
            pltpu.make_async_copy(window, entries.at[tile], sems.at[tile]).wait()

        def logit_steps(l_ref, tile):
            def step(columns):
                l_ref[:, columns] = matmul_t(x_ref[...], entries[tile, columns])

            return [functools.partial(step, columns) for columns in rows_of(VOCAB_TILE, GROUP)]

        def soft_steps(l_ref, p_ref, factor_ref, tile):
            start = jnp.minimum(tile * VOCAB_TILE, vocab - VOCAB_TILE)
            lane = lax.broadcasted_iota(jnp.int32, (1, VOCAB_TILE), 1)
            bias = jnp.where(lane + start >= tile * VOCAB_TILE, 0.0, -1e30)

            def step(at):
                logits = l_ref[at] + bias
                earlier = top[at]
                highest = jnp.maximum(earlier, jnp.max(logits, 1, keepdims=True))
                exponent = jnp.exp(logits - highest)
                factor = jnp.exp(earlier - highest)
                top[at] = highest
                total[at] = total[at] * factor + jnp.sum(exponent, 1, keepdims=True)
                p_ref[at] = low(exponent)
                factor_ref[at] = across(factor)

            return [functools.partial(step, at) for at in rows_of(count, SMALL_ROWS)]

        def sum_steps(p_ref, factor_ref, tile):
            def step(columns):
                factor = factor_ref[...]
                factor = jnp.concatenate([factor, factor], 1)
                acc[:, columns] = acc[:, columns] * factor + matmul(p_ref[...], entries[tile, :, columns])

            return [functools.partial(step, columns) for columns in rows_of(D, GROUP)]

        acc[...] = jnp.zeros_like(acc)
        top[...] = jnp.full_like(top, -1e30)
        total[...] = jnp.zeros_like(total)
        p_odd[...] = jnp.zeros_like(p_odd)
        factor_odd[...] = jnp.ones_like(factor_odd)
        fetch.wait()
        wait_tile(0)
        alternate(logit_steps(l_even, 0))

        def turn(j, carry):
            even, odd = 2 * j, 2 * j + 1
            before, after = jnp.maximum(even - 1, 0), jnp.minimum(even + 2, tiles - 1)
            wait_tile(odd)

            @pl.when(even + 2 < tiles)
            def _():
                wait_tile(even + 2)

            alternate(
                soft_steps(l_even, p_even, factor_even, even),
                sum_steps(p_odd, factor_odd, before) + logit_steps(l_odd, odd),
            )
            alternate(
                soft_steps(l_odd, p_odd, factor_odd, odd),
                sum_steps(p_even, factor_even, even) + logit_steps(l_even, after),
            )
            return carry

        lax.fori_loop(0, tiles // 2, turn, 0)
        alternate(sum_steps(p_odd, factor_odd, tiles - 1))
        out_ref[:, :D] = low(acc[...])
        out_ref[:, D:] = head_stats(top[...], total[...])
        copy = pltpu.make_async_copy(out_ref, out_hbm, sems.at[tiles])
        copy.start()
        copy.wait()

    hbm = pl.BlockSpec(memory_space=pltpu.HBM)
    return pl.pallas_call(
        kernel,
        in_specs=[hbm, hbm],
        out_specs=hbm,
        out_shape=low_shape(count, D + LANES),
        scratch_shapes=[
            pltpu.VMEM((count, D), BF16),
            pltpu.VMEM((count, D + LANES), BF16),
            pltpu.VMEM((tiles, VOCAB_TILE, D), BF16),
            pltpu.VMEM((count, D), F32),
            pltpu.VMEM((count, 1), F32),
            pltpu.VMEM((count, 1), F32),
        ]
        + [pltpu.VMEM((count, LANES), F32)] * 2
        + [pltpu.VMEM((count, VOCAB_TILE), F32)] * 2
        + [pltpu.VMEM((count, VOCAB_TILE), BF16)] * 2
        + [pltpu.SemaphoreType.DMA((tiles + 1,))],
        compiler_params=params_for(MOST_VMEM),
        name="vocabulary_head",
    )(rows.reshape(count, D), table).reshape(parts, each, D + LANES)


def blocked_head_kernel(rows, table):
    parts_in, each, _ = rows.shape
    count, vocab = parts_in * each, table.shape[0]
    last = pl.cdiv(vocab, VOCAB_TILE) - 1
    turns = last // 2 + 1

    def kernel(x_hbm, even_ref, odd_ref, after_ref, out_hbm, *refs):
        x_ref, out_ref, acc, top, total, l_even, l_odd, p_even, p_odd, sems = refs
        turn = pl.program_id(0)

        def entries_of(ref, tile):
            row = lax.broadcasted_iota(jnp.int32, (VOCAB_TILE, 1), 0)
            return jnp.where(row < vocab - tile * VOCAB_TILE, ref[...], jnp.zeros_like(ref))

        @pl.when(turn == 0)
        def _():
            copy = pltpu.make_async_copy(x_hbm, x_ref, sems.at[0])
            copy.start()
            acc[...] = jnp.zeros_like(acc)
            top[...] = jnp.full_like(top, -1e30)
            total[...] = jnp.zeros_like(total)
            entries = entries_of(even_ref, 0)
            copy.wait()
            l_even[...] = matmul_t(x_ref[...], entries)

        even = entries_of(even_ref, 2 * turn)
        odd = entries_of(odd_ref, 2 * turn + 1)
        after = entries_of(after_ref, 2 * turn + 2)
        for tile, l_now, p_now, now, l_later, later in (
            (2 * turn, l_even, p_even, even, l_odd, odd),
            (2 * turn + 1, l_odd, p_odd, odd, l_even, after),
        ):
            bias = key_bias(vocab - tile * VOCAB_TILE, (1, VOCAB_TILE), 1)
            for at in rows_of(count, SMALL_ROWS):
                logits = l_now[at] + bias
                earlier = top[at]
                highest = jnp.maximum(earlier, jnp.max(logits, 1, keepdims=True))
                exponent = jnp.exp(logits - highest)
                factor = jnp.exp(earlier - highest)
                top[at] = highest
                total[at] = total[at] * factor + jnp.sum(exponent, 1, keepdims=True)
                p_now[at] = low(exponent)
                acc[at] = acc[at] * factor
            l_later[...] = matmul_t(x_ref[...], later)
            acc[...] += matmul(p_now[...], now)

        @pl.when(turn == turns - 1)
        def _():
            out_ref[:, :D] = low(acc[...])
            out_ref[:, D:] = head_stats(top[...], total[...])
            copy = pltpu.make_async_copy(out_ref, out_hbm, sems.at[1])
            copy.start()
            copy.wait()

    def tile_at(shift):
        return pl.BlockSpec((VOCAB_TILE, D), lambda j: (jnp.minimum(2 * j + shift, last), 0))

    hbm = pl.BlockSpec(memory_space=pltpu.HBM)
    return pl.pallas_call(
        kernel,
        grid=(turns,),
        in_specs=[hbm] + [tile_at(shift) for shift in range(3)],
        out_specs=hbm,
        out_shape=shape_of(count, D + LANES, kind=BF16),
        scratch_shapes=[
            pltpu.VMEM((count, D), BF16),
            pltpu.VMEM((count, D + LANES), BF16),
            pltpu.VMEM((count, D), F32),
            pltpu.VMEM((count, 1), F32),
            pltpu.VMEM((count, 1), F32),
            pltpu.VMEM((count, VOCAB_TILE), F32),
            pltpu.VMEM((count, VOCAB_TILE), F32),
            pltpu.VMEM((count, VOCAB_TILE), BF16),
            pltpu.VMEM((count, VOCAB_TILE), BF16),
            pltpu.SemaphoreType.DMA((2,)),
        ],
        compiler_params=params_for(MOST_VMEM),
        name="vocabulary_head",
    )(rows.reshape(count, D), table, table, table).reshape(parts_in, each, D + LANES)


def swap_add(own, other):
    came = lax.ppermute(low(other), "section", [(0, 1), (1, 0)])
    return own + came.astype(F32)


def pick(first_section, both):
    return jnp.where(first_section, both[0], both[1])


def plan_requests(ids, weights, vocab_rows, slots, parts):
    turned = jnp.transpose(ids)

    def kernel(ids_ref, turned_ref, weights_ref, asked_ref, code_ref, spot_ref):
        here = lax.axis_index("section")
        i_index = lax.broadcasted_iota(jnp.int32, (IDS, IDS), 0)
        j_index = lax.broadcasted_iota(jnp.int32, (IDS, IDS), 1)
        earlier, later = j_index < i_index, i_index < j_index

        def owner_of(values):
            return jnp.floor((values.astype(F32) + 0.5) * (1.0 / vocab_rows)).astype(jnp.int32)

        def count(hits, axis):
            return jnp.sum(hits.astype(F32), axis, keepdims=True)

        most = jnp.zeros((1, 1), F32)
        for m in range(MICRO):
            row, col = ids_ref[m : m + 1], turned_ref[:, m : m + 1]
            same_id = row == col
            first_col = count(same_id & earlier, 1) == 0
            first_row = count(same_id & later, 0) == 0
            owner_row, owner_col = owner_of(row), owner_of(col)
            same_owner = owner_row == owner_col
            rank_row = count(same_owner & later & first_col, 0)
            rank_col = count(same_owner & earlier & first_row, 1)
            most = jnp.maximum(most, jnp.max(rank_row, 1, keepdims=True))

            @pl.when(here == m)
            def _():
                slot_row = jnp.sum(jnp.where(same_id & first_col, rank_col, 0.0), 0, keepdims=True)
                slot_col = jnp.sum(jnp.where(same_id & first_row, rank_row, 0.0), 1, keepdims=True)
                slot_row, slot_col = slot_row.astype(jnp.int32), slot_col.astype(jnp.int32)
                code_ref[...] = (owner_row + parts * first_row.astype(jnp.int32)) * 1024 + slot_row
                spot = jnp.where(slot_col < slots, owner_col * slots + slot_col, -1)
                spot_ref[...] = jnp.broadcast_to(spot, (IDS, LANES))
                lane = lax.broadcasted_iota(jnp.int32, (IDS, LANES), 1)
                local = (col - owner_col * vocab_rows).astype(F32)
                wanted = first_col & (slot_col < slots) & (slot_col == lane)
                wanted = jnp.where(wanted, local, 0.0)
                for part in range(parts):
                    asked = jnp.sum(jnp.where(owner_col == part, wanted, 0.0), 0, keepdims=True)
                    asked_ref[part] = asked.astype(jnp.int32)

        rounds = jnp.floor((most + 0.5) * (1.0 / slots)).astype(jnp.int32) + 1
        total = jnp.sum(jnp.sum(weights_ref[...], 0, keepdims=True), 1, keepdims=True)
        lane = lax.broadcasted_iota(jnp.int32, (1, LANES), 1)
        for part in range(parts):
            row = asked_ref[part]
            asked_ref[part] = jnp.where(lane == slots, rounds, jnp.where(lane == slots + 1, total, row))

    return pl.pallas_call(
        kernel,
        out_shape=[
            jax.ShapeDtypeStruct((parts, 1, LANES), jnp.int32),
            jax.ShapeDtypeStruct((1, IDS), jnp.int32),
            jax.ShapeDtypeStruct((IDS, LANES), jnp.int32),
        ],
        compiler_params=params_for(24),
        name="plan_requests",
    )(ids, turned, weights)


def fetch_rows(table, ids, first_section, plan, slots):
    parts = lax.axis_size("dp")
    vocab_rows = table.shape[0]
    asked, code, spot = plan
    asked = lax.all_to_all(asked, "dp", 0, 0)[:, 0]
    total_rounds = jnp.max(asked[:, slots])
    weight_sum = jnp.sum(asked[:, slots + 1])

    def answer(asked):
        rows = table.at[asked.reshape(-1)].get(mode="promise_in_bounds").reshape(parts, slots, D)
        return lax.all_to_all(rows, "dp", 0, 0).reshape(parts * slots, D)

    came = answer(asked[:, :slots])

    def more(state):
        return state[0] < total_rounds

    def another(state):
        turn, extra = state
        place, slot = code[0] // 1024, code[0] % 1024
        owner, first = place % parts, place >= parts
        local = pick(first_section, ids) - owner * vocab_rows
        here = slot - turn * slots
        at = jnp.where((here >= 0) & (here < slots), owner * slots + here, -1)
        hits = at[:, None] == jnp.arange(parts * slots)[None, :]
        wanted = jnp.sum(jnp.where(hits & first[:, None], local[:, None], 0), 0).reshape(parts, slots)
        rows = answer(lax.all_to_all(wanted, "dp", 0, 0))
        return turn + 1, extra + matmul(hits.astype(BF16), rows)

    extra = lax.while_loop(more, another, (jnp.int32(1), jnp.zeros((IDS, D), F32)))[1]
    return came, spot, extra, weight_sum.astype(F32)


def three_low(values):
    high = low(values)
    rest = values - high.astype(F32)
    middle = low(rest)
    return [high, middle, low(rest - middle.astype(F32))]


def in_groups(count):
    return lax.axis_size("dp") == COUPLING_GROUPS and count == 4 * PART_GROUPS


def gather_params(master, vector):
    parts = lax.axis_size("dp")
    count, width = master.shape[0], vector.shape[0]
    if in_groups(count):
        lines = 4
        planes = parts // lines
        across_planes = [[plane * lines + line for plane in range(planes)] for line in range(lines)]
        in_plane = [[plane * lines + line for line in range(lines)] for plane in range(planes)]
        some = pack_own(master, vector[None], planes)
        some = lax.all_to_all(some, "dp", 0, 0, axis_index_groups=across_planes)
        own = lax.all_gather(some, "dp", axis_index_groups=in_plane)
        return unpack_all(own, lax.ppermute(own, "section", [(0, 1), (1, 0)]), width)
    flat = low(jnp.concatenate([master.reshape(-1), vector]))
    gathered = lax.all_gather(flat, ("section", "dp")).reshape(MICRO, parts, -1)
    size = count * BLOCK**2
    all_blocks = gathered[:, :, :size].reshape(MICRO, parts * count, BLOCK, BLOCK)
    all_vectors = gathered[:, :, size:].reshape(MICRO, parts * width)
    both = [split_params(all_blocks[s], all_vectors[s]) for s in range(MICRO)]

    def stacked(which):
        down, bias_down, up, bias_up = (jnp.stack([pair[which][i] for pair in both]) for i in range(4))
        return Params(down, bias_down.astype(F32)[:, None], up, bias_up.astype(F32)[:, None])

    return stacked(0), stacked(1)


def sum_at_owners(grads, loss_part, count):
    parts = lax.axis_size("dp")
    width = sum(BIASES) // parts
    flat = []
    for adapter, coupling in grads:
        blocks, vector = join_params(adapter, coupling)
        flat.append(
            jnp.concatenate([blocks.reshape(parts, count * BLOCK**2), vector.reshape(parts, width)], 1)
        )
    first = lax.axis_index("section") == 0
    summed = swap_add(jnp.where(first, flat[0], flat[1]), jnp.where(first, flat[1], flat[0]))
    owned = jnp.sum(lax.all_to_all(low(summed), "dp", 0, 0).astype(F32), 0)
    blocks = owned[: count * BLOCK**2].reshape(count, BLOCK, BLOCK)
    pair = jnp.stack([jnp.sum(owned * owned), loss_part[0, 0]])
    pair = jnp.pad(pair, (0, LANES - 2))[None, None]
    return blocks, owned[count * BLOCK**2 :], jnp.broadcast_to(pair, (parts * MICRO, 8, LANES))


def to_coupling_owners(group):
    arrived = []
    for place in range(PART_GROUPS):
        route = []
        for part in range(COUPLING_GROUPS):
            owner, at = divmod(ADAPTER_GROUPS + part, PART_GROUPS)
            if at == place:
                route.append((part, owner))
        arrived.append(lax.ppermute(group, "dp", route))
    return arrived


def exact(spec, left, right):
    return jnp.einsum(spec, left, right, precision=HIGHEST)


def update(pair, products, grad_vector, state):
    master, momentum, stat_left, stat_right, root_left, root_right, vectors, vec_first, vec_second = state
    grad, left_square, right_square, turned = products
    turned_old = exact("nij,njk->nik", exact("nij,njk->nik", root_left, momentum), root_right)

    blocks = (1,) + grad.shape
    outs = [shape_of(*blocks)] * 5 + [low_shape(*blocks)] + [shape_of(*vectors.shape)] * 3 + [shape_of(1, 1)] * 2

    def body(ins, out, scalar_refs, pair_refs, raw_refs, scratch):
        start(ins)
        (pair_ref, grad_ref, left_ref, right_ref, turned_ref, vector_ref, old_ref), ins = (
            [operand.get() for operand in ins[:7]],
            [operand.get() for operand in ins[7:]],
        )
        master_ref, momentum_ref, stat_left_ref, stat_right_ref, vectors_ref, first_ref, second_ref = ins
        outs = [result.buffer for result in out]
        totals = jnp.sum(pair_ref[...], 0)[:1]
        norm = jnp.sqrt(totals[:, :1])
        factor = CLIP_NORM / jnp.maximum(norm, CLIP_NORM)
        outs[9][...] = norm
        outs[10][...] = totals[:, 1:2]
        square = (1.0 - STAT_DECAY) * factor * factor
        for n in range(grad_ref.shape[0]):
            clipped = grad_ref[n] * factor
            outs[0][0, n] = clipped
            outs[1][0, n] = FIRST_DECAY * momentum_ref[n] + (1.0 - FIRST_DECAY) * clipped
            outs[2][0, n] = STAT_DECAY * stat_left_ref[n] + square * left_ref[n]
            outs[3][0, n] = STAT_DECAY * stat_right_ref[n] + square * right_ref[n]
            direction = FIRST_DECAY * old_ref[n] + (1.0 - FIRST_DECAY) * factor * turned_ref[n]
            master_new = master_ref[n] - MAT_RATE * (direction + MAT_DECAY * master_ref[n])
            outs[4][0, n] = master_new
            outs[5][0, n] = low(master_new)
        clipped = vector_ref[...] * factor
        first_new = FIRST_DECAY * first_ref[...] + (1.0 - FIRST_DECAY) * clipped
        second_new = VEC_SECOND * second_ref[...] + (1.0 - VEC_SECOND) * clipped * clipped
        outs[6][...] = first_new
        outs[7][...] = second_new
        corrected_first = first_new / (1.0 - FIRST_DECAY**STEP)
        corrected_second = second_new / (1.0 - VEC_SECOND**STEP)
        outs[8][...] = vectors_ref[...] - VEC_RATE * (
            corrected_first / (jnp.sqrt(corrected_second) + VEC_EPS) + VEC_DECAY * vectors_ref[...]
        )

    ins = [pair, grad, left_square, right_square, turned, grad_vector, turned_old]
    ins += [master, momentum, stat_left, stat_right, vectors, vec_first, vec_second]
    return moved_call(body, (), ins, outs, (), [], "update")[0]


def shards(
    token_ids,
    lengths,
    positions,
    targets,
    loss_weights,
    embed_table,
    pos_table,
    norm_params,
    base_qkv,
    base_out,
    base_up,
    base_down,
    master,
    momentum,
    stat_left,
    stat_right,
    root_left,
    root_right,
    vectors,
    vec_first,
    vec_second,
):
    parts = lax.axis_size("dp")
    first_section = lax.axis_index("section") == 0
    slots = -(-IDS * 5 // (4 * parts * 16)) * 16

    ids = jnp.concatenate([token_ids[:, 0], targets[:, 0]], -1)
    asked, *plan = plan_requests(ids, loss_weights[:, 0], embed_table.shape[0], slots, parts)
    asked, own_master = lax.optimization_barrier((asked, master[0]))
    adapter, coupling = gather_params(own_master, vectors[0])
    swap = [(0, 1), (1, 0)]
    pairs = [(w, lax.ppermute(w, "section", swap)) for w in (base_qkv, base_out, base_up, base_down)]
    came = lax.ppermute(norm_params, "section", swap)
    norms = jnp.concatenate([pick(first_section, (norm_params, came)), pick(first_section, (came, norm_params))])

    came, spot, extra, weight_sum = fetch_rows(embed_table, ids, first_section, (asked, *plan), slots)
    length = pick(first_section, lengths)
    spots = pick(first_section, positions[:, 0])
    row_weights = pick(first_section, loss_weights[:, 0]).astype(F32)
    chosen = (spots[:, None] == jnp.arange(SEQ)[None, :]).astype(BF16)
    chosen_t = (spots[None, :] == jnp.arange(SEQ)[:, None]).astype(F32)

    ins = ForwardIn(came, spot, extra, pos_table, norms, chosen, adapter, coupling)
    kept, rows = forward_kernel(ins, (length,), pairs, parts, slots)

    rows = lax.all_to_all(rows, "dp", 0, 0)
    merged = lax.all_to_all(head_kernel(rows, embed_table), "dp", 0, 0)

    packed = in_groups(master.shape[1])
    row_weights = jnp.broadcast_to(row_weights[:, None], (COUNT, LANES))
    weight_row = jnp.broadcast_to(weight_sum, (1, LANES))
    adapter, coupling = adapter[::2], coupling[::2]
    ins = BackIn(
        merged, row_weights, weight_row, norms, chosen_t, adapter, coupling,
        kept.target_rows, kept.rest_0, kept.attention_1, kept.rest_1, kept.last,
    )
    back = backward_kernel(ins, (length,), pairs, packed)
    loss_part, mixed_grad = back.loss, back.mixed
    if packed:
        own, other = back.adapters[MICRO:]
        summed = low(swap_add(own.astype(F32), other))
        summed, mixed_grad = lax.optimization_barrier((summed, mixed_grad))
        adapter_came = lax.all_to_all(summed, "dp", 0, 0)
    ins = FirstIn(
        kept.attention_0, mixed_grad, back.start, coupling, kept.one, kept.two, back.one, back.two,
        back.adapters[:MICRO] if packed else (),
    )
    grads = first_backward(ins, (length,), pairs, packed)
    if packed:
        adapter_total, squares = sum_adapter(adapter_came)
        came = lax.all_to_all(low(swap_add(*grads)), "dp", 0, 0)
        group, bias, pair = sum_coupling(came, squares, loss_part, parts * MICRO)
        products = grad_products(adapter_total, to_coupling_owners(group), root_left[0], root_right[0])
        grad_vector = bias[:1, : vectors.shape[1]]
    else:
        both = [(back.adapters[s], grads[4 * s : 4 * s + 4]) for s in range(MICRO)]
        grad, grad_vector, pair = sum_at_owners(both, loss_part, master.shape[1])
        turned = exact("nij,njk->nik", exact("nij,njk->nik", root_left[0], grad), root_right[0])
        products = grad, exact("nij,nkj->nik", grad, grad), exact("nji,njk->nik", grad, grad), turned
        grad_vector = grad_vector[None]
    pair = lax.all_to_all(pair, ("dp", "section"), 0, 0)
    state = (master, momentum, stat_left, stat_right, root_left, root_right)
    *outs, grad_norm, loss_sum = update(
        pair, products, grad_vector, [value[0] for value in state] + [vectors, vec_first, vec_second]
    )
    return (*outs, grad_norm[0, 0], loss_sum[0, 0], weight_sum)


def solution(mesh):
    rows = P(None, "dp", None)
    section = P("section", None, None)
    blocks = P("section", "dp", None, None)
    biases = P("section", "dp")
    return jax.shard_map(
        shards,
        mesh=mesh,
        in_specs=(rows, P(None, "dp"), rows, rows, rows, P("dp", None), P())
        + (section,) * 5
        + (blocks,) * 6
        + (biases,) * 3,
        out_specs=(blocks,) * 6 + (biases,) * 3 + (P(),) * 3,
        check_vma=False,
    )
```

```python
import functools
from typing import Any, NamedTuple

import jax
import jax.numpy as jnp
import numpy as np
from jax import lax
from jax.experimental import pallas as pl
from jax.experimental.pallas import tpu as pltpu
from jax.sharding import PartitionSpec as P

D = 768
HEADS = 12
HEAD_DIM = 64
BOT = 384
INV_H = 192
SEQ = 512
COUNT = 32
MICRO = 2
BLOCK = 48
STEP = 10
HALF = 384
IDS = SEQ + COUNT

HIGHEST = lax.Precision.HIGHEST
NORM_EPS = 1e-12
CLIP_NORM = 0.02
FIRST_DECAY = 0.9
STAT_DECAY = 0.99
MAT_RATE = 0.1
MAT_DECAY = 0.01
VEC_RATE = 0.05
VEC_SECOND = 0.999
VEC_EPS = 1e-08
VEC_DECAY = 0.01
F32 = jnp.float32
BF16 = jnp.bfloat16

CDF_SCALE = 0.42 / 2.0**0.5
CDF_POLY = (
    0.2368242366796694,
    0.239585811361218,
    0.1947261443420679,
    0.2687426685879861,
    -0.13052645834187002,
    0.4406726942003943,
    -0.32025628294963193,
    0.07023101752398136,
)


def matmul(left, right):
    return jnp.dot(left, right, preferred_element_type=F32)


def matmul_t(left, right):
    return lax.dot_general(left, right, (((1,), (1,)), ((), ())), preferred_element_type=F32)


def inner_rows(left, right):
    return lax.dot_general(left, right, (((0,), (0,)), ((), ())), preferred_element_type=F32)


def low(values):
    return values.astype(BF16)


def gelu_both(values):
    below = 1.0 + CDF_SCALE * jnp.abs(values)
    ratio = pl.reciprocal(below, approx=True)
    ratio = ratio * (2.0 - below * ratio)
    poly = jnp.full_like(ratio, 0.5 * CDF_POLY[-1])
    for factor in CDF_POLY[-2::-1]:
        poly = poly * ratio + 0.5 * factor
    bell = jnp.exp(-0.5 * values * values)
    tail = bell * (poly * ratio)
    cdf = jnp.where(values < 0, tail, 1.0 - tail)
    return values * cdf, cdf + values * (bell * (2.0 * np.pi) ** -0.5)


def layer_norm(values, gain, shift):
    centered = values - jnp.mean(values, -1, keepdims=True)
    inverse = lax.rsqrt(jnp.mean(centered * centered, -1, keepdims=True) + NORM_EPS)
    normal = centered * inverse
    return normal * gain + shift, (normal, inverse)


def norm_back(incoming, kept, gain):
    normal, inverse = kept
    scaled = incoming * gain
    return inverse * (
        scaled
        - jnp.mean(scaled, -1, keepdims=True)
        - normal * jnp.mean(scaled * normal, -1, keepdims=True)
    )


def to_blocks(matrix):
    rows_in, cols_in = matrix.shape
    return (
        matrix.reshape(rows_in // BLOCK, BLOCK, cols_in // BLOCK, BLOCK)
        .transpose(0, 2, 1, 3)
        .reshape(-1, BLOCK, BLOCK)
    )


def from_blocks(blocks, rows_in, cols_in):
    return (
        blocks.reshape(rows_in // BLOCK, cols_in // BLOCK, BLOCK, BLOCK)
        .transpose(0, 2, 1, 3)
        .reshape(rows_in, cols_in)
    )


def split_params(blocks, vector):
    adapter_count = D * BOT // BLOCK**2
    half_count = HALF * INV_H // BLOCK**2
    split_at = 2 * adapter_count
    adapter = (
        from_blocks(blocks[:adapter_count], D, BOT),
        vector[:BOT],
        from_blocks(blocks[adapter_count:split_at], BOT, D),
        vector[BOT : BOT + D],
    )
    coupling = (
        from_blocks(blocks[split_at : split_at + half_count], HALF, INV_H),
        vector[BOT + D : BOT + D + INV_H],
        from_blocks(blocks[split_at + half_count :], INV_H, HALF),
        vector[BOT + D + INV_H :],
    )
    return adapter, coupling


def join_params(adapter, coupling):
    blocks = jnp.concatenate(
        [to_blocks(adapter[0]), to_blocks(adapter[2]), to_blocks(coupling[0]), to_blocks(coupling[2])]
    )
    return blocks, jnp.concatenate([adapter[1], adapter[3], coupling[1], coupling[3]], 1)[0]


GROUP_ROWS = 72
LANES = 128


def params_for(mebibytes):
    return pltpu.CompilerParams(vmem_limit_bytes=mebibytes * 2**20)


def roll(values, shift):
    return pltpu.roll(values, shift, 1)


def lane_of(values):
    return lax.broadcasted_iota(jnp.int32, values.shape, 1)


def fold_half(values, upper):
    top, bottom = values[:24], values[24:]
    if upper:
        return jnp.where(lane_of(top) < 64, roll(top, 64), bottom)
    return jnp.where(lane_of(top) < 64, top, roll(bottom, 64))


def unfold_half(values, upper):
    turned = roll(values, 64)
    return jnp.concatenate([turned, values] if upper else [values, turned], 0)


def join_pair(main_0, rest_0, main_1, rest_1):
    left = lane_of(main_0) < 64
    turned = roll(main_1, 64)
    return (
        main_0,
        jnp.where(left, unfold_half(rest_0, False), turned),
        jnp.where(left, turned, unfold_half(rest_1, True)),
    )


def cut_pair(tile_0, tile_1, tile_2):
    left = lane_of(tile_0) < 64
    return (
        (tile_0, fold_half(tile_1, False)),
        (jnp.where(left, roll(tile_1, 64), roll(tile_2, 64)), fold_half(tile_2, True)),
    )


def chunk_rows(own_blocks):
    return own_blocks // 4 * GROUP_ROWS + 8


def bias_row(tiles, part, width):
    at, shift = divmod(part * width, LANES)
    lane = lane_of(tiles[0])
    row = tiles[at]
    if shift:
        row = jnp.where(lane < LANES - shift, roll(row, LANES - shift), roll(tiles[at + 1], LANES - shift))
    return jnp.where(lane < width, row, 0.0)


def bias_tiles(first, second, third, fourth):
    cut = lambda values: [values[:, at : at + LANES] for at in range(0, values.shape[1], LANES)]
    zero = jnp.zeros((1, LANES), F32)
    left = lane_of(zero) < 64
    third_tail = jnp.concatenate([third[:, LANES:]] * 2, 1)
    turned = [roll(tile, 64) for tile in cut(fourth)]
    joints = [jnp.where(left, one, two) for one, two in zip([third_tail] + turned, turned + [zero])]
    return cut(first) + cut(second) + [third[:, :LANES]] + joints + [zero]


def tiles_of_rows(rows, width):
    tiles = []
    for tile in range(-(-len(rows) * width // LANES)):
        value = jnp.zeros((8, LANES), F32)
        lane = lane_of(value)
        for part, row in enumerate(rows):
            shift = part * width - tile * LANES
            if shift >= LANES or shift + width <= 0:
                continue
            turned = roll(row, shift % LANES) if shift % LANES else row
            value = jnp.where((lane >= shift) & (lane < shift + width), turned, value)
        tiles.append(value)
    return tiles


def pack_own(master, vector, copies):
    count, width = master.shape[0], vector.shape[1]

    def kernel(master_ref, bias_ref, out_ref):
        row = lax.broadcasted_iota(jnp.int32, (BLOCK, 256), 0)
        col = lax.broadcasted_iota(jnp.int32, (BLOCK, 256), 1)
        pieces = []
        for group in range(count // 4):
            wide = jnp.zeros((BLOCK, 256), F32)
            for j in range(4):
                wide += matmul(low(master_ref[4 * group + j]), (col == row + BLOCK * j).astype(BF16))
            pieces += [wide[:, :LANES], fold_half(wide[:, LANES:], False)]
        bias = jnp.concatenate([bias_ref[...], jnp.zeros((1, LANES - width), F32)], 1)
        pieces.append(jnp.concatenate([bias, jnp.zeros((7, LANES), F32)], 0))
        packed = low(jnp.concatenate(pieces, 0))
        for copy in range(copies):
            out_ref[copy] = packed

    return pl.pallas_call(
        kernel,
        out_shape=jax.ShapeDtypeStruct((copies, chunk_rows(count), LANES), BF16),
        name="pack_own",
    )(master, vector)


MATRICES = ((D, BOT), (BOT, D), (HALF, INV_H), (INV_H, HALF))
BIASES = (BOT, D, INV_H, HALF)


def unpack_all(own, came, width):
    lines, planes, rows, _ = own.shape
    parts = lines * planes
    per_part = (rows - 8) // GROUP_ROWS

    def kernel(own_hbm, came_hbm, *refs):
        out_hbm, in_bufs, out_refs, in_sems, out_sems = refs[:8], refs[8], refs[9:17], refs[17], refs[18]
        here = lax.axis_index("section")
        copies = [
            pltpu.make_async_copy(ref, in_bufs.at[at], in_sems.at[i])
            for i, (ref, at) in enumerate(((own_hbm, here), (came_hbm, 1 - here)))
        ]
        for copy in copies:
            copy.start()
        for copy in copies:
            copy.wait()

        def unpack(s, carry):
            cache = {}

            def group(index):
                part = index // per_part
                if part not in cache:
                    cache.clear()
                    cache[part] = in_bufs[s, part % lines, part // lines].astype(F32)
                base = index % per_part * GROUP_ROWS
                chunk = cache[part]
                return chunk[base : base + BLOCK], chunk[base + BLOCK : base + GROUP_ROWS]

            index = 0
            for (height, columns), out_ref in zip(MATRICES, out_refs):
                for top in range(0, height, BLOCK):
                    if columns == INV_H:
                        main, rest = group(index)
                        index += 1
                        out_ref[s, top : top + BLOCK, :LANES] = low(main)
                        out_ref[s, top : top + BLOCK, LANES:] = low(unfold_half(rest, False)[:, :64])
                        continue
                    for left in range(0, columns, HALF):
                        tiles = join_pair(*group(index), *group(index + 1))
                        index += 2
                        for j, tile in enumerate(tiles):
                            at = left + j * LANES
                            out_ref[s, top : top + BLOCK, at : at + LANES] = low(tile)
            tiles = tiles_of_rows(
                [in_bufs[s, part % lines, part // lines, rows - 16 :].astype(F32)[8:] for part in range(parts)], width
            )
            first, second, third, fourth = out_refs[4:]
            first[s] = jnp.concatenate(tiles[:3], 1)[:1]
            second[s] = jnp.concatenate(tiles[3:9], 1)[:1]
            third[s] = jnp.concatenate([tiles[9], tiles[10][:, :64]], 1)[:1]
            left = lane_of(tiles[0]) < 64
            turned = [roll(tile, 64) for tile in tiles[10:14]]
            fourth[s] = jnp.concatenate(
                [jnp.where(left, one, two) for one, two in zip(turned, turned[1:])], 1
            )[:1]
            return carry

        lax.fori_loop(0, MICRO, unpack, 0)
        copies = [
            pltpu.make_async_copy(buf, ref, out_sems.at[i]) for i, (buf, ref) in enumerate(zip(out_refs, out_hbm))
        ]
        for copy in copies:
            copy.start()
        for copy in copies:
            copy.wait()

    shapes = [((MICRO,) + shape, BF16) for shape in MATRICES] + [((MICRO, 1, size), F32) for size in BIASES]
    hbm = pl.BlockSpec(memory_space=pltpu.HBM)
    arrays = pl.pallas_call(
        kernel,
        in_specs=[hbm] * 2,
        out_specs=[hbm] * 8,
        out_shape=[jax.ShapeDtypeStruct(*shape) for shape in shapes],
        scratch_shapes=[pltpu.VMEM((MICRO, lines, planes, rows, LANES), BF16)]
        + [pltpu.VMEM(*shape) for shape in shapes]
        + [pltpu.SemaphoreType.DMA((2,)), pltpu.SemaphoreType.DMA((8,))],
        compiler_params=params_for(MOST_VMEM),
        name="unpack_all",
    )(own, came)
    down, up, c_down, c_up, bias_down, bias_up, c_bias_down, c_bias_up = arrays
    return Params(down, bias_down, up, bias_up), Params(c_down, c_bias_down, c_up, c_bias_up)


ADAPTER_GROUPS = 2 * D * BOT // BLOCK**2 // 4
COUPLING_GROUPS = 2 * HALF * INV_H // BLOCK**2 // 4
PART_GROUPS = (ADAPTER_GROUPS + COUPLING_GROUPS) // COUPLING_GROUPS
PART_ROWS = PART_GROUPS * GROUP_ROWS


def groups_of(refs, shapes):
    groups = []
    for ref, (height, width) in zip(refs, shapes):
        for top in range(0, height, BLOCK):
            band = slice(top, top + BLOCK)
            if width == INV_H:
                tail = ref[band, LANES:]
                groups.append((ref[band, :LANES], fold_half(jnp.concatenate([tail, tail], 1), False)))
                continue
            for left in range(0, width, HALF):
                groups += cut_pair(*[ref[band, left + j * LANES : left + (j + 1) * LANES] for j in range(3)])
    return [jnp.concatenate(group, 0) for group in groups]


def pack_adapter(refs, store):
    groups = groups_of(refs, MATRICES[:2])
    empty = jnp.zeros((GROUP_ROWS, LANES), F32)
    for part in range(COUPLING_GROUPS):
        chunk = groups[part * PART_GROUPS : (part + 1) * PART_GROUPS]
        chunk += [empty] * (PART_GROUPS - len(chunk))
        store(part, low(jnp.concatenate(chunk, 0)))


def pack_coupling(refs, tiles, width, store):
    for part, group in enumerate(groups_of(refs, MATRICES[2:])):
        bias = jnp.concatenate([bias_row(tiles, part, width), jnp.zeros((7, LANES), F32)], 0)
        store(part, jnp.concatenate([group, bias], 0))


def sum_parts(came_ref):
    total = came_ref[0].astype(F32)
    for part in range(1, came_ref.shape[0]):
        total += came_ref[part].astype(F32)
    return total


def square_sum(values):
    return jnp.sum(jnp.sum(values * values, 0, keepdims=True), 1, keepdims=True)


def sum_adapter(came):
    def kernel(came_ref, total_ref, square_ref):
        total = sum_parts(came_ref)
        total_ref[...] = total
        square_ref[...] = square_sum(total)

    return pl.pallas_call(
        kernel,
        out_shape=[jax.ShapeDtypeStruct((PART_ROWS, LANES), F32), jax.ShapeDtypeStruct((1, 1), F32)],
        compiler_params=params_for(32),
        name="sum_adapter",
    )(came)


def sum_coupling(came, squares, loss_part, copies):
    def kernel(came_ref, square_ref, loss_ref, group_ref, bias_ref, pair_ref):
        total = sum_parts(came_ref)
        group_ref[...] = total[:GROUP_ROWS]
        bias_ref[...] = total[GROUP_ROWS:]
        squares = square_ref[...] + square_sum(total)
        lane = lax.broadcasted_iota(jnp.int32, (8, LANES), 1)
        pair = jnp.where(lane == 0, squares, jnp.where(lane == 1, loss_ref[:, :1], 0.0))
        for copy in range(copies):
            pair_ref[copy] = pair

    return pl.pallas_call(
        kernel,
        out_shape=[
            jax.ShapeDtypeStruct((GROUP_ROWS, LANES), F32),
            jax.ShapeDtypeStruct((8, LANES), F32),
            jax.ShapeDtypeStruct((copies, 8, LANES), F32),
        ],
        name="sum_coupling",
    )(came, squares, loss_part)


def grad_products(adapter_total, coupling_groups, root_left, root_right):
    count = 4 * PART_GROUPS

    def exact_dot(left, right, dims):
        return lax.dot_general(left, right, (dims, ((), ())), precision=HIGHEST, preferred_element_type=F32)

    def body(ins, out, scalar_refs, pair_refs, raw_refs, scratch):
        start(ins)
        total_ref, left_ref, right_ref, *group_refs = (operand.get() for operand in ins)
        grad_ref, left_square_ref, right_square_ref, turned_ref = (result.buffer for result in out)
        for group in range(PART_GROUPS):
            total = total_ref[group * GROUP_ROWS : (group + 1) * GROUP_ROWS] + group_refs[group][...]
            main, rest = total[:BLOCK], unfold_half(total[BLOCK:], False)
            lane = lane_of(main)
            pieces = (
                main,
                roll(main, 80),
                jnp.where(lane < 32, roll(main, 32), roll(rest, 32)),
                roll(rest, 112),
            )
            for j, values in enumerate(pieces):
                grad_ref[4 * group + j] = values[:, :BLOCK]
        for n in range(count):
            grad = grad_ref[n]
            left_square_ref[n] = exact_dot(grad, grad, ((1,), (1,)))
            right_square_ref[n] = exact_dot(grad, grad, ((0,), (0,)))
            turned_ref[n] = exact_dot(
                exact_dot(left_ref[n], grad, ((1,), (0,))), right_ref[n], ((1,), (0,))
            )

    ins = [adapter_total, root_left, root_right, *coupling_groups]
    outs = [jax.ShapeDtypeStruct((count, BLOCK, BLOCK), F32)] * 4
    return moved_call(body, (), ins, outs, (), [], "grad_products")[0]


MOST_VMEM = 64
GROUP = 256
HEADS_IN = GROUP // HEAD_DIM
GROUPS = D // GROUP
FF = 3072
TILE = 512
TILES = FF // TILE
STEP_ROWS = 256
SMALL_ROWS = 32


def rows_of(count, size):
    return [slice(at, at + min(size, count)) for at in range(0, count, size)]


def shape_of(*dims, kind=F32):
    return jax.ShapeDtypeStruct(dims, kind)


class Params(NamedTuple):
    down: Any
    bias_down: Any
    up: Any
    bias_up: Any


class Branch(NamedTuple):
    lin: Any
    act: Any
    slope: Any


class Attention(NamedTuple):
    query: Any
    key: Any
    value: Any
    lse: Any


class Rest(NamedTuple):
    normal_1: Any
    inverse_1: Any
    slope: Any
    branch: Any
    normal_2: Any
    inverse_2: Any


class Last(NamedTuple):
    one: Any
    two: Any
    normal: Any
    inverse: Any
    normed: Any


class ForwardIn(NamedTuple):
    came: Any
    spot: Any
    extra: Any
    pos: Any
    norms: Any
    chosen: Any
    adapter: Any
    coupling: Any


class Forward(NamedTuple):
    target_rows: Any
    one: Any
    two: Any
    attention_0: Any
    rest_0: Any
    attention_1: Any
    rest_1: Any
    last: Any


class BackIn(NamedTuple):
    merged: Any
    row_weights: Any
    weight_sum: Any
    norms: Any
    chosen_t: Any
    adapter: Any
    coupling: Any
    target_rows: Any
    rest_0: Any
    attention_1: Any
    rest_1: Any
    last: Any


class Back(NamedTuple):
    loss: Any
    one: Any
    two: Any
    adapters: Any
    start: Any
    mixed: Any


class FirstIn(NamedTuple):
    attention: Any
    mixed: Any
    start: Any
    coupling: Any
    one: Any
    two: Any
    grads_one: Any
    grads_two: Any
    biases: Any


class Operand:
    def __init__(self, ref, buffer, sem):
        self.buffer, self.copy = buffer, pltpu.make_async_copy(ref, buffer, sem)
        self.started = self.waited = False

    def start(self):
        if not self.started:
            self.copy.start()
        self.started = True

    def get(self):
        self.start()
        if not self.waited:
            self.copy.wait()
        self.waited = True
        return self.buffer


class Result:
    def __init__(self, ref, buffer, sem):
        self.buffer, self.copy = buffer, pltpu.make_async_copy(buffer, ref, sem)
        self.sent = False

    def send(self):
        if not self.sent:
            self.copy.start()
        self.sent = True


def start(*operands):
    for operand in jax.tree.leaves(operands):
        operand.start()


def send(*results):
    for result in jax.tree.leaves(results):
        result.send()


def moved_call(body, scalars, ins, outs, pairs, scratch, name, raw_outs=()):
    in_leaves, in_tree = jax.tree.flatten(ins)
    out_leaves, out_tree = jax.tree.flatten(outs)

    def kernel(*refs):
        refs = list(refs)

        def take(count):
            taken, refs[:] = refs[:count], refs[count:]
            return taken

        scalar_refs, in_refs = take(len(scalars)), take(len(in_leaves))
        pair_refs = [tuple(take(2)) for _ in pairs]
        out_refs, raw_refs = take(len(out_leaves)), take(len(raw_outs))
        in_buffers, out_buffers, (in_sems, out_sems) = take(len(in_leaves)), take(len(out_leaves)), take(2)
        operands = [Operand(*two, in_sems.at[i]) for i, two in enumerate(zip(in_refs, in_buffers))]
        results = [Result(*two, out_sems.at[i]) for i, two in enumerate(zip(out_refs, out_buffers))]
        body(in_tree.unflatten(operands), out_tree.unflatten(results), scalar_refs, pair_refs, raw_refs, refs)
        send(results)
        for operand in operands:
            operand.get()
        for result in results:
            result.copy.wait()

    hbm = pl.BlockSpec(memory_space=pltpu.HBM)
    buffers = [pltpu.VMEM(value.shape, value.dtype) for value in (*in_leaves, *out_leaves)]
    results = pl.pallas_call(
        kernel,
        in_specs=[pl.BlockSpec(memory_space=pltpu.SMEM)] * len(scalars) + [hbm] * (len(in_leaves) + 2 * len(pairs)),
        out_specs=[hbm] * (len(out_leaves) + len(raw_outs)),
        out_shape=[*out_leaves, *raw_outs],
        scratch_shapes=buffers
        + [pltpu.SemaphoreType.DMA((len(in_leaves),)), pltpu.SemaphoreType.DMA((len(out_leaves),))]
        + list(scratch),
        compiler_params=params_for(MOST_VMEM),
        name=name,
    )(*scalars, *in_leaves, *[w for pair in pairs for w in pair])
    return out_tree.unflatten(results[: len(out_leaves)]), results[len(out_leaves) :]


def start_copy(pair, section, window, target, sem):
    own, came = pair
    here = lax.axis_index("section") == section

    @pl.when(here)
    def _():
        pltpu.make_async_copy(own.at[window], target, sem).start()

    @pl.when(jnp.logical_not(here))
    def _():
        pltpu.make_async_copy(came.at[window], target, sem).start()


def wait_copy(pair, window, target, sem):
    pltpu.make_async_copy(pair[0].at[window], target, sem).wait()


def qkv_window(group, part):
    return 0, slice(None), pl.ds(part * D + group * GROUP, GROUP)


def qkv_buffers():
    return [pltpu.VMEM((GROUPS, 3, D, GROUP), BF16), pltpu.SemaphoreType.DMA((GROUPS, 3))]


def start_qkv(pair, section, buffers):
    for group in range(GROUPS):
        for part in range(3):
            start_copy(pair, section, qkv_window(group, part), buffers[0].at[group, part], buffers[1].at[group, part])


def wait_qkv(pair, buffers, group, part):
    wait_copy(pair, qkv_window(0, 0), buffers[0].at[group, part], buffers[1].at[group, part])


UP_WINDOWS = [(0, slice(None), slice(j * TILE, (j + 1) * TILE)) for j in range(TILES)]
DOWN_WINDOWS = [(0, slice(j * TILE, (j + 1) * TILE), slice(None)) for j in range(TILES)]
OUT_WINDOW = (0, slice(None), slice(None))


def rest_buffers():
    return [
        pltpu.VMEM((D, D), BF16),
        pltpu.VMEM((TILES, D, TILE), BF16),
        pltpu.VMEM((TILES, TILE, D), BF16),
        pltpu.SemaphoreType.DMA((2 * TILES + 1,)),
    ]


def start_out(pairs, section, buffers):
    start_copy(pairs[0], section, OUT_WINDOW, buffers[0], buffers[3].at[2 * TILES])


def start_tiles(pairs, section, buffers):
    for j in range(TILES):
        start_copy(pairs[1], section, UP_WINDOWS[j], buffers[1].at[j], buffers[3].at[j])
        start_copy(pairs[2], section, DOWN_WINDOWS[j], buffers[2].at[j], buffers[3].at[TILES + j])


def wait_out(pairs, buffers):
    wait_copy(pairs[0], OUT_WINDOW, buffers[0], buffers[3].at[2 * TILES])


def wait_up(pairs, buffers, tile):
    wait_copy(pairs[1], UP_WINDOWS[0], buffers[1].at[tile], buffers[3].at[tile])


def wait_down(pairs, buffers, tile):
    wait_copy(pairs[2], DOWN_WINDOWS[0], buffers[2].at[tile], buffers[3].at[TILES + tile])


def across(values):
    return jnp.broadcast_to(values, (values.shape[0], LANES))


def group_columns(group):
    return pl.ds(pl.multiple_of(group * GROUP, GROUP), GROUP)


def tile_columns(tile):
    return pl.ds(pl.multiple_of(tile * TILE, TILE), TILE)


def head_mask(values, head):
    lane = lax.broadcasted_iota(jnp.int32, values.shape, 1)
    return (lane >= head * HEAD_DIM) & (lane < (head + 1) * HEAD_DIM)


def only_head(values, head):
    return jnp.where(head_mask(values, head), values, jnp.zeros_like(values))


def scaled_query(query):
    return low(query.astype(F32) * HEAD_DIM**-0.5)


def key_bias(length, shape, axis):
    return jnp.where(lax.broadcasted_iota(jnp.int32, shape, axis) < length, 0.0, -1e30)


def softmax_rows(scores):
    highest = jnp.max(scores, 1, keepdims=True)
    exponent = jnp.exp(scores - highest)
    total = jnp.sum(exponent, 1, keepdims=True)
    return low(exponent * (1.0 / total)), highest + jnp.log(total)


def branch_rows(low_in, weights):
    active, slope = gelu_both(matmul(low_in, weights[0]) + weights[1])
    active = low(active)
    return matmul(active, weights[2]) + weights[3], active, low(slope)


def alternate(*lists):
    steps = [((i + 0.5) / len(steps), k, step) for k, steps in enumerate(lists) for i, step in enumerate(steps)]
    for _, _, step in sorted(steps, key=lambda entry: entry[:2]):
        step()


def section_params(params, section):
    return [operand.get()[section] for operand in params]


def rest_rows(out, rows, section, norms, adapter, hidden, mixed, finish, scratch, pairs, buffers, after_loop=None):
    att_low, acc, u_even, u_odd, g_even, g_odd = scratch
    gain = lambda i: norms[section, i : i + 1]
    parts = rows_of(rows, STEP_ROWS)
    every = slice(0, rows)
    wait_out(pairs, buffers)
    for part in parts:
        first = hidden[part] + matmul(mixed[part], buffers[0][...])
        values, (normal, inverse) = layer_norm(first, gain(2), gain(3))
        acc[part] = values
        att_low[part] = low(values)
        out.normal_1.buffer[part] = normal
        out.inverse_1.buffer[part] = across(inverse)
    send(out.normal_1, out.inverse_1)
    wait_up(pairs, buffers, 0)
    g_odd[every] = jnp.zeros_like(g_odd[every])

    def gelu_steps(u_ref, g_ref, tile):
        def step(at):
            active, slope = gelu_both(u_ref[at])
            g_ref[at] = low(active)
            out.slope.buffer[at, tile_columns(tile)] = low(slope)

        return [functools.partial(step, at) for at in rows_of(rows, SMALL_ROWS)]

    def up_steps(u_ref, tile):
        def step(columns):
            u_ref[every, columns] = matmul(att_low[every], buffers[1][tile, :, columns])

        return [functools.partial(step, columns) for columns in rows_of(TILE, GROUP)]

    def down_steps(g_ref, tile):
        def step(columns):
            acc[every, columns] += matmul(g_ref[every], buffers[2][tile, :, columns])

        return [functools.partial(step, columns) for columns in rows_of(D, GROUP)]

    alternate(up_steps(u_even, 0))

    def turn(j, carry):
        even, odd = 2 * j, 2 * j + 1
        before, after = jnp.maximum(even - 1, 0), jnp.minimum(even + 2, TILES - 1)
        wait_down(pairs, buffers, even)
        wait_up(pairs, buffers, odd)
        wait_down(pairs, buffers, odd)

        @pl.when(even + 2 < TILES)
        def _():
            wait_up(pairs, buffers, even + 2)

        alternate(gelu_steps(u_even, g_even, even), down_steps(g_odd, before) + up_steps(u_odd, odd))
        alternate(gelu_steps(u_odd, g_odd, odd), down_steps(g_even, even) + up_steps(u_even, after))
        return carry

    lax.fori_loop(0, TILES // 2, turn, 0)
    alternate(down_steps(g_odd, TILES - 1))
    if after_loop is not None:
        after_loop()
    send(out.slope)
    weights = section_params(adapter, section)
    for part in parts:
        summed = acc[part]
        low_in = low(summed)
        added, *kept = branch_rows(low_in, weights)
        for result, value in zip(out.branch, (low_in, *kept)):
            result.buffer[part] = value
        values, (normal, inverse) = layer_norm(summed + added, gain(4), gain(5))
        out.normal_2.buffer[part], out.inverse_2.buffer[part] = normal, across(inverse)
        finish(part, values)
    send(out.branch, out.normal_2, out.inverse_2)


def low_shape(*dims):
    return shape_of(*dims, kind=BF16)


def branch_shapes(rows, wide, narrow):
    return Branch(low_shape(rows, wide), low_shape(rows, narrow), low_shape(rows, narrow))


def rest_shapes(rows):
    wide, thin = shape_of(rows, D), shape_of(rows, LANES)
    return Rest(wide, thin, low_shape(rows, FF), branch_shapes(rows, D, BOT), wide, thin)


def forward_kernel(ins, scalars, pairs, parts, slots):
    coupling_shapes = lambda rows: branch_shapes(rows, HALF, INV_H)
    outs = Forward(
        target_rows=shape_of(COUNT, D),
        one=coupling_shapes(SEQ),
        two=coupling_shapes(SEQ),
        attention_0=Attention(*[low_shape(SEQ, D)] * 3, shape_of(GROUPS, 8, SEQ)),
        rest_0=rest_shapes(SEQ),
        attention_1=Attention(
            low_shape(COUNT, D), *[low_shape(SEQ, D)] * 2, shape_of(GROUPS, HEADS_IN * COUNT, LANES)
        ),
        rest_1=rest_shapes(COUNT),
        last=Last(
            coupling_shapes(COUNT), coupling_shapes(COUNT),
            shape_of(COUNT, D), shape_of(COUNT, LANES), low_shape(COUNT, D),
        ),
    )

    def body(ins, out, scalar_refs, pair_refs, raw_refs, scratch):
        length = scalar_refs[0][0]
        hidden, x_low, s_even, s_odd, p_even, p_odd, lse_buf, mixed, section_out = scratch[:9]
        at_spots, at_low, mixed_1 = scratch[9:12]
        rest_scratch, qkv_0, qkv_1, rest_w = scratch[12:18], scratch[18:20], scratch[20:22], scratch[22:26]
        row_sems, joined = scratch[26:28]
        qkv_pair, rest_pairs = pair_refs[0], pair_refs[1:]

        start(ins.came, ins.spot, ins.pos, ins.norms, ins.coupling)
        norms = ins.norms.get()
        norm = lambda s, i: norms[s, i : i + 1]

        came, spot = ins.came.get(), ins.spot.get()
        start_qkv(qkv_pair, 0, qkv_0)
        start_out(rest_pairs, 0, rest_w)

        def rows_at(part):
            lane = lax.broadcasted_iota(jnp.int32, (part.stop - part.start, parts * slots), 1)
            hits = (spot[part][:, :1] == lane).astype(BF16)
            return matmul(hits, came[...])

        targets = slice(SEQ, SEQ + COUNT)
        out.target_rows.buffer[...] = rows_at(targets)
        for part in rows_of(SEQ, STEP_ROWS):
            hidden[part] = rows_at(part)

        @pl.when(scalar_refs[1][0] > 1)
        def _():
            ins.extra.copy.start()
            ins.extra.copy.wait()
            out.target_rows.buffer[...] += ins.extra.buffer[targets]
            hidden[...] += ins.extra.buffer[:SEQ]

        ins.extra.started = ins.extra.waited = True
        send(out.target_rows)
        start(ins.adapter, ins.chosen)
        start_tiles(rest_pairs, 0, rest_w)
        one, two = section_params(ins.coupling, 0), section_params(ins.coupling, 1)

        def put(results, part, *values):
            for result, value in zip(results, values):
                result.buffer[part] = value

        for part in rows_of(SEQ, STEP_ROWS):
            started, _ = layer_norm(hidden[part] + ins.pos.get()[part].astype(F32), norm(0, 0), norm(0, 1))
            left, right = started[:, :HALF], started[:, HALF:]
            low_one = low(right)
            added, active, slope = branch_rows(low_one, one)
            put(out.one, part, low_one, active, slope)
            left = left + added
            low_two = low(left)
            added, active, slope = branch_rows(low_two, two)
            put(out.two, part, low_two, active, slope)
            right = right + added
            hidden[part, :HALF] = left
            hidden[part, HALF:] = right
            x_low[part, :HALF] = low_two
            x_low[part, HALF:] = low(right)
        send(out.one, out.two)

        start_qkv(qkv_pair, 1, qkv_1)
        lse_buf[...] = jnp.zeros((SEQ, LANES), F32)
        q_ref, k_ref, v_ref, lse_ref = (result.buffer for result in out.attention_0)

        def attend(group, carry):
            columns = group_columns(group)
            for part, ref in enumerate((q_ref, k_ref, v_ref)):
                wait_qkv(qkv_pair, qkv_0, group, part)
                ref[:, columns] = low(matmul(x_low[...], qkv_0[0][group, part]))
            query = scaled_query(q_ref[:, columns])
            key, value = k_ref[:, columns], v_ref[:, columns]
            bias = key_bias(length, (1, SEQ), 1)
            lane = lax.broadcasted_iota(jnp.int32, (SMALL_ROWS * 2, LANES), 1)
            buffers = ((s_even, p_even), (s_odd, p_odd)) * 2

            def score_steps(head):
                def step():
                    buffers[head][0][...] = matmul_t(only_head(query, head), key)

                return [step] if head < HEADS_IN else []

            def soft_steps(head):
                def step(rows):
                    soft, lse = softmax_rows(buffers[head][0][rows] + bias)
                    buffers[head][1][rows] = soft
                    lse_buf[rows] = jnp.where(lane == head, lse, lse_buf[rows])

                return [functools.partial(step, rows) for rows in rows_of(SEQ, SMALL_ROWS * 2)]

            def mix_steps(head):
                def step():
                    mixed_head = matmul(buffers[head][1][...], value)
                    if head == 0:
                        joined[...] = mixed_head
                    else:
                        joined[...] = jnp.where(head_mask(mixed_head, head), mixed_head, joined[...])

                return [step] if head >= 0 else []

            alternate(score_steps(0))
            for head in range(HEADS_IN):
                alternate(soft_steps(head), score_steps(head + 1) + mix_steps(head - 1))
            alternate(mix_steps(HEADS_IN - 1))
            mixed[:, columns] = low(joined[...])
            lse_ref[group] = jnp.transpose(lse_buf[...])[:8]
            return carry

        lax.fori_loop(0, GROUPS, attend, 0)
        send(out.attention_0)

        def to_section_out(part, values):
            section_out[part] = low(values)

        def next_weights():
            start_out(rest_pairs, 1, rest_w)
            start_tiles(rest_pairs, 1, rest_w)

        rest_rows(
            out.rest_0, SEQ, 0, norms, ins.adapter, hidden, mixed, to_section_out,
            rest_scratch, rest_pairs, rest_w, next_weights,
        )

        at_spots[...] = matmul(ins.chosen.get()[...], section_out[...])
        at_low[...] = low(at_spots[...])
        q_1, k_1, v_1, lse_1 = (result.buffer for result in out.attention_1)

        def attend_spots(group, carry):
            columns = group_columns(group)
            for part, ref in enumerate((q_1, k_1, v_1)):
                wait_qkv(qkv_pair, qkv_1, group, part)
                source = at_low if part == 0 else section_out
                ref[:, columns] = low(matmul(source[...], qkv_1[0][group, part]))
            query = scaled_query(q_1[:, columns])
            query = jnp.concatenate([only_head(query, head) for head in range(HEADS_IN)], 0)
            bias = key_bias(length, (1, SEQ), 1)
            soft, lse = softmax_rows(matmul_t(query, k_1[:, columns]) + bias)
            lse_1[group] = across(lse)
            every = matmul(soft, v_1[:, columns])
            joined = every[:COUNT]
            for head in range(1, HEADS_IN):
                joined = jnp.where(head_mask(joined, head), every[head * COUNT : (head + 1) * COUNT], joined)
            mixed_1[:, columns] = low(joined)
            return carry

        lax.fori_loop(0, GROUPS, attend_spots, 0)
        send(out.attention_1)

        def to_normed(part, values):
            left, right = values[:, :HALF], values[:, HALF:]
            low_two = low(left)
            taken, active, slope = branch_rows(low_two, two)
            put(out.last.two, part, low_two, active, slope)
            right = right - taken
            low_one = low(right)
            taken, active, slope = branch_rows(low_one, one)
            put(out.last.one, part, low_one, active, slope)
            left = left - taken
            values, (normal, inverse) = layer_norm(jnp.concatenate([left, right], 1), norm(1, 0), norm(1, 1))
            put(out.last[2:], part, normal, across(inverse), low(values))

        rest_rows(
            out.rest_1, COUNT, 1, norms, ins.adapter, at_spots, mixed_1, to_normed,
            rest_scratch, rest_pairs, rest_w,
        )
        copies = [
            pltpu.make_async_copy(out.last.normed.buffer, raw_refs[0].at[part], row_sems.at[part]) for part in range(parts)
        ]
        for copy in copies:
            copy.start()
        for copy in copies:
            copy.wait()

    buffer = lambda *dims: pltpu.VMEM(dims, F32)
    buffer_low = lambda *dims: pltpu.VMEM(dims, BF16)
    scratch = [buffer(SEQ, D), buffer_low(SEQ, D), buffer(SEQ, SEQ), buffer(SEQ, SEQ)]
    scratch += [buffer_low(SEQ, SEQ), buffer_low(SEQ, SEQ), buffer(SEQ, LANES)]
    scratch += [buffer_low(SEQ, D), buffer_low(SEQ, D)]
    scratch += [buffer(COUNT, D), buffer_low(COUNT, D), buffer_low(COUNT, D)]
    scratch += [buffer_low(SEQ, D), buffer(SEQ, D), buffer(SEQ, TILE), buffer(SEQ, TILE)]
    scratch += [buffer_low(SEQ, TILE), buffer_low(SEQ, TILE)]
    scratch += qkv_buffers() + qkv_buffers() + rest_buffers()
    scratch += [pltpu.SemaphoreType.DMA((parts,)), buffer(SEQ, GROUP)]
    raw = [low_shape(parts, COUNT, D)]
    kept, (rows,) = moved_call(body, scalars, ins, outs, pairs, scratch, "forward", raw)
    return kept, rows


def column_sum(values):
    return jnp.sum(values.astype(F32), 0, keepdims=True)


def branch_grads(grad_low, kept, weights, out_refs):
    low_in, active, slope = kept
    hidden_grad = low(matmul_t(grad_low, weights[2]) * slope.astype(F32))
    out_refs[0][...] = inner_rows(low_in, hidden_grad)
    out_refs[1][...] = column_sum(hidden_grad)
    out_refs[2][...] = inner_rows(active, grad_low)
    out_refs[3][...] = column_sum(grad_low)
    return hidden_grad


ADAPTER_GRADS = ((D, BOT), (1, BOT), (BOT, D), (1, D))
COUPLING_GRADS = ((HALF, INV_H), (1, INV_H), (INV_H, HALF), (1, HALF))


def branch_kept(branch):
    return [operand.get()[...] for operand in branch]


def grad_weights(pair, section):
    return [pair[0].get()[section], None, pair[1].get()[section]]


def rest_back_rows(kept, rows, section, norms, adapter, incoming, scratch, pairs, buffers, grad_refs, results, packing=None):
    summed_low, acc, second_low = scratch
    start_ref, mixed_ref = results
    gain = lambda i: norms[section, i : i + 1]
    parts = rows_of(rows, STEP_ROWS)
    weights = grad_weights(adapter, section)
    for part in parts:
        norm_kept = kept.normal_2.get()[part], kept.inverse_2.get()[part, :1]
        second = norm_back(incoming(part), norm_kept, gain(4))
        acc[part] = second
        second_low[part] = low(second)
    hidden_grad = branch_grads(second_low[:rows], branch_kept(kept.branch), weights, grad_refs)
    for part in parts:
        total = acc[part] + matmul_t(hidden_grad[part], weights[0])
        acc[part] = total
        summed_low[part] = low(total)
    if packing is not None:
        packing()
    slope = kept.slope.get()

    def turn(j, carry):
        for now in (2 * j, 2 * j + 1):
            wait_up(pairs, buffers, now)
            wait_down(pairs, buffers, now)
        for now in (2 * j, 2 * j + 1):
            for part in parts:
                inner = matmul_t(summed_low[part], buffers[2][now])
                inner = low(inner * slope[part, tile_columns(now)].astype(F32))
                acc[part] += matmul_t(inner, buffers[1][now])
        return carry

    lax.fori_loop(0, TILES // 2, turn, 0)
    wait_out(pairs, buffers)
    for part in parts:
        norm_kept = kept.normal_1.get()[part], kept.inverse_1.get()[part, :1]
        back = norm_back(acc[part], norm_kept, gain(2))
        start_ref[part] = back
        mixed_ref[part] = low(matmul_t(low(back), buffers[0][...]))


def backward_kernel(ins, scalars, pairs, packed):
    parts = ins.merged.shape[0]
    grads = [shape_of(*dims) for dims in COUPLING_GRADS]
    if packed:
        chunks = low_shape(COUPLING_GROUPS, PART_ROWS, LANES)
        adapters = [[shape_of(1, BOT), shape_of(1, D)] for _ in range(MICRO)] + [chunks, chunks]
    else:
        adapters = [[shape_of(*dims) for dims in ADAPTER_GRADS] for _ in range(MICRO)]
    outs = Back(shape_of(1, LANES), grads, grads, adapters, shape_of(SEQ, D), low_shape(SEQ, D))

    def body(ins, out, scalar_refs, pair_refs, raw_refs, scratch):
        length = scalar_refs[0][0]
        rest_scratch, spot, mixed_1, acc_1, section_grad = scratch[:3], *scratch[3:7]
        qkv_w, rest_w, refs = scratch[7:9], scratch[9:13], scratch[13:]
        qkv_pair, rest_pairs = pair_refs[0], pair_refs[1:]

        start(ins.merged, ins.row_weights, ins.weight_sum, ins.target_rows, ins.last, ins.norms)
        start(ins.coupling, ins.rest_1, ins.adapter)
        start_tiles(rest_pairs, 1, rest_w)
        start_out(rest_pairs, 1, rest_w)
        norms = ins.norms.get()

        def from_head(part):
            merged = ins.merged.get()
            start_qkv(qkv_pair, 1, qkv_w)
            start(ins.attention_1, ins.chosen_t)
            stats = merged[:, :, D:].astype(F32)
            highest = jnp.sum(stats[:, :, :3], 2, keepdims=True)
            totals = jnp.sum(stats[:, :, 3:6], 2, keepdims=True)
            top = jnp.max(highest, 0)
            factor = jnp.exp(highest - top[None])
            total = jnp.sum(totals * factor, 0)
            expected = jnp.zeros((COUNT, D), F32)
            for i in range(parts):
                expected += merged[i, :, :D].astype(F32) * (factor[i] / total)
            target = ins.target_rows.get()[...]
            target_logit = jnp.sum(ins.last.normed.get()[...].astype(F32) * target, 1, keepdims=True)
            weight = ins.row_weights.get()[...]
            row_losses = weight[:, :1] * (top + jnp.log(total) - target_logit)
            out.loss.buffer[...] = across(jnp.sum(row_losses, 0, keepdims=True))
            normed_grad = (weight / ins.weight_sum.get()[...])[:, :1] * (expected - target)
            kept = (ins.last.normal.get()[...], ins.last.inverse.get()[:, :1])
            restored = norm_back(normed_grad, kept, norms[1, 0:1])
            left, right = restored[:, :HALF], restored[:, HALF:]
            one, two = (grad_weights(ins.coupling, s) for s in range(MICRO))
            refs_of = lambda results: [result.buffer for result in results]
            hidden = branch_grads(low(-left), branch_kept(ins.last.one), one, refs_of(out.one))
            right = right + matmul_t(hidden, one[0])
            hidden = branch_grads(low(-right), branch_kept(ins.last.two), two, refs_of(out.two))
            left = left + matmul_t(hidden, two[0])
            return jnp.concatenate([left, right], 1)

        def grads_of(section):
            buffers = [result.buffer for result in out.adapters[section]]
            return (refs[0], buffers[0], refs[1], buffers[1]) if packed else buffers

        def pack_second():
            def store(part, chunk):
                refs[2][part] = chunk

            pack_adapter((refs[0], refs[1]), store)

        def pack_both():
            here = lax.axis_index("section") == 0
            own, other = out.adapters[2:]

            def store(part, chunk):
                arrived = refs[2][part]
                own.buffer[part] = jnp.where(here, chunk, arrived)
                other.buffer[part] = jnp.where(here, arrived, chunk)

            pack_adapter((refs[0], refs[1]), store)
            send(own, other)

        rest_back_rows(
            ins.rest_1, COUNT, 1, norms, ins.adapter, from_head, rest_scratch, rest_pairs, rest_w,
            grads_of(1), (spot, mixed_1), pack_second if packed else None,
        )
        start(ins.rest_0)
        start_tiles(rest_pairs, 0, rest_w)
        start_out(rest_pairs, 0, rest_w)

        acc_1[...] = jnp.zeros_like(acc_1)
        q_ref, k_ref, v_ref, lse_ref = (operand.get() for operand in ins.attention_1)

        def attend_back(group, carry):
            columns = group_columns(group)
            stack = lambda values: jnp.concatenate([only_head(values, h) for h in range(HEADS_IN)], 0)
            query = stack(scaled_query(q_ref[:, columns]))
            mixed = stack(mixed_1[:, columns])
            key, value = k_ref[:, columns], v_ref[:, columns]
            scores = matmul_t(query, key) + key_bias(length, (1, SEQ), 1)
            soft = jnp.exp(scores - lse_ref[group][:, :1])
            soft_grad = matmul_t(mixed, value)
            delta = jnp.sum(soft_grad * soft, 1, keepdims=True)
            score_grad = low(soft * (soft_grad - delta))
            every = matmul(score_grad, key)
            query_grad = every[:COUNT]
            for head in range(1, HEADS_IN):
                query_grad = jnp.where(
                    head_mask(query_grad, head), every[head * COUNT : (head + 1) * COUNT], query_grad
                )
            query_grad = low(query_grad * HEAD_DIM**-0.5)
            key_grad = low(inner_rows(score_grad, query))
            value_grad = low(inner_rows(low(soft), mixed))
            for part in range(3):
                wait_qkv(qkv_pair, qkv_w, group, part)
            spot[...] += matmul_t(query_grad, qkv_w[0][group, 0])
            acc_1[...] += matmul_t(key_grad, qkv_w[0][group, 1]) + matmul_t(value_grad, qkv_w[0][group, 2])
            return carry

        lax.fori_loop(0, GROUPS, attend_back, 0)
        placed = jnp.dot(ins.chosen_t.get()[...], spot[...], precision=HIGHEST, preferred_element_type=F32)
        section_grad[...] = low(acc_1[...] + placed)

        rest_back_rows(
            ins.rest_0, SEQ, 0, norms, ins.adapter, lambda part: section_grad[part].astype(F32),
            rest_scratch, rest_pairs, rest_w, grads_of(0), (out.start.buffer, out.mixed.buffer),
            pack_both if packed else None,
        )

    scratch = [pltpu.VMEM((SEQ, D), BF16), pltpu.VMEM((SEQ, D), F32), pltpu.VMEM((SEQ, D), BF16)]
    scratch += [pltpu.VMEM((COUNT, D), F32), pltpu.VMEM((COUNT, D), BF16), pltpu.VMEM((SEQ, D), F32)]
    scratch += [pltpu.VMEM((SEQ, D), BF16)] + qkv_buffers() + rest_buffers()
    if packed:
        scratch += [pltpu.VMEM((D, BOT), F32), pltpu.VMEM((BOT, D), F32)]
        scratch += [pltpu.VMEM((COUPLING_GROUPS, PART_ROWS, LANES), BF16)]
    return moved_call(body, scalars, ins, outs, pairs, scratch, "backward")[0]


def first_backward(ins, scalars, pairs, packed):
    if packed:
        dims = (COUPLING_GROUPS, GROUP_ROWS + 8, LANES)
        outs = (shape_of(*dims), low_shape(*dims))
    else:
        outs = [shape_of(*dims) for dims in COUPLING_GRADS * 2]

    def body(ins, out, scalar_refs, pair_refs, raw_refs, scratch):
        length = scalar_refs[0][0]
        s_even, s_odd, d_even, d_odd, p_even, p_odd, ds_even, ds_odd = scratch[:8]
        qkv_w, (key_grad, value_grad, query_grad_t), refs = scratch[8:10], scratch[10:13], scratch[13:]
        start(ins.attention, ins.mixed)
        q_ref, k_ref, v_ref, lse_ref = (operand.get() for operand in ins.attention)
        mixed_ref = ins.mixed.get()
        start(ins.start)
        start_qkv(pair_refs[0], 0, qkv_w)
        start(ins)
        acc = ins.start.get()

        def attend_back(group, carry):
            columns = group_columns(group)
            query = scaled_query(q_ref[:, columns])
            key, value, mixed = k_ref[:, columns], v_ref[:, columns], mixed_ref[:, columns]
            lse_rows = lse_ref[group]
            key_t = jnp.transpose(key)
            buffers = ((s_even, d_even, p_even, ds_even), (s_odd, d_odd, p_odd, ds_odd)) * 2

            def product_steps(head):
                def scores():
                    buffers[head][0][...] = matmul_t(only_head(key, head), query)

                def soft_grads():
                    buffers[head][1][...] = matmul_t(only_head(value, head), mixed)

                return [scores, soft_grads] if head < HEADS_IN else []

            def soft_steps(head):
                s_buf, d_buf, p_low, ds_low = buffers[head]
                delta = [jnp.zeros((8, SEQ), F32)]

                def soft_step(rows):
                    valid = lax.broadcasted_iota(jnp.int32, (SMALL_ROWS, 1), 0) + rows.start < length
                    bias = jnp.where(valid, 0.0, -1e30)
                    soft = jnp.exp(s_buf[rows] + bias - lse_rows[head : head + 1])
                    s_buf[rows] = soft
                    p_low[rows] = low(soft)
                    product = soft * d_buf[rows]
                    for at in range(0, SMALL_ROWS, 8):
                        delta[0] = delta[0] + product[at : at + 8]

                def sum_step():
                    delta[0] = jnp.sum(delta[0], 0, keepdims=True)

                def grad_step(rows):
                    ds_low[rows] = low(s_buf[rows] * (d_buf[rows] - delta[0]))

                parts = rows_of(SEQ, SMALL_ROWS)
                steps = [functools.partial(soft_step, rows) for rows in parts] + [sum_step]
                return steps + [functools.partial(grad_step, rows) for rows in parts]

            def grad_steps(head):
                _, _, p_low, ds_low = buffers[max(head, 0)]

                def add(ref, grad):
                    ref[...] = grad if head == 0 else ref[...] + grad

                def value_step():
                    add(value_grad, matmul(p_low[...], only_head(mixed, head)))

                def key_step():
                    add(key_grad, matmul(ds_low[...], only_head(query, head)))

                def query_step():
                    rows = slice(head * HEAD_DIM, (head + 1) * HEAD_DIM)
                    query_grad_t[rows] = matmul(key_t[rows], ds_low[...])

                return [value_step, key_step, query_step] if head >= 0 else []

            alternate(product_steps(0))
            for head in range(HEADS_IN):
                alternate(soft_steps(head), product_steps(head + 1) + grad_steps(head - 1))
            alternate(grad_steps(HEADS_IN - 1))
            query_grad = jnp.transpose(query_grad_t[...]) * HEAD_DIM**-0.5
            for part, grad in enumerate((query_grad, key_grad[...], value_grad[...])):
                wait_qkv(pair_refs[0], qkv_w, group, part)
                acc[...] += matmul_t(low(grad), qkv_w[0][group, part])
            return carry

        lax.fori_loop(0, GROUPS, attend_back, 0)
        one, two = (grad_weights(ins.coupling, s) for s in range(MICRO))
        grads = refs if packed else [result.buffer for result in out]
        hidden = branch_grads(low(acc[:, HALF:]), branch_kept(ins.two), two, grads[4:])
        left = acc[:, :HALF] + matmul_t(hidden, two[0])
        branch_grads(low(left), branch_kept(ins.one), one, grads[:4])
        for ref, operand in zip(grads, (*ins.grads_one, *ins.grads_two)):
            ref[...] += operand.get()[...]
        if not packed:
            return
        here = lax.axis_index("section")
        for s in range(MICRO):
            some = grads[4 * s : 4 * s + 4]
            biases = [operand.get()[...] for operand in ins.biases[s]]
            tiles = bias_tiles(*biases, some[1][...], some[3][...])

            def store(part, chunk, s=s):
                @pl.when(here == s)
                def _():
                    out[0].buffer[part] = chunk

                @pl.when(here != s)
                def _():
                    out[1].buffer[part] = low(chunk)

            pack_coupling((some[0], some[2]), tiles, sum(BIASES) // COUPLING_GROUPS, store)

    scratch = [pltpu.VMEM((SEQ, SEQ), F32)] * 4 + [pltpu.VMEM((SEQ, SEQ), BF16)] * 4 + qkv_buffers()
    scratch += [pltpu.VMEM((SEQ, GROUP), F32)] * 2 + [pltpu.VMEM((GROUP, SEQ), F32)]
    if packed:
        scratch += [pltpu.VMEM(dims, F32) for dims in COUPLING_GRADS * 2]
    return moved_call(body, scalars, ins, outs, pairs[:1], scratch, "first_backward")[0]


VOCAB_TILE = 1280


def head_stats(top, total):
    lane = lax.broadcasted_iota(jnp.int32, (top.shape[0], LANES), 1)
    stats = jnp.zeros(lane.shape, F32)
    for j, piece in enumerate(three_low(top) + three_low(total)):
        stats = jnp.where(lane == j, piece.astype(F32), stats)
    return low(stats)


def head_kernel(rows, table):
    parts, each, _ = rows.shape
    count, vocab = parts * each, table.shape[0]
    tiles = pl.cdiv(vocab, VOCAB_TILE)
    if vocab < VOCAB_TILE or (vocab - VOCAB_TILE) % 16 or tiles % 2:
        return blocked_head_kernel(rows, table)
    starts = [min(tile * VOCAB_TILE, vocab - VOCAB_TILE) for tile in range(tiles)]

    def kernel(x_hbm, table_hbm, out_hbm, *refs):
        x_ref, out_ref, entries, acc, top, total, factor_even, factor_odd = refs[:8]
        l_even, l_odd, p_even, p_odd, sems = refs[8:]
        fetch = pltpu.make_async_copy(x_hbm, x_ref, sems.at[tiles])
        fetch.start()

        def start_tiles_from(first, count):
            for tile in range(first, first + count):
                window = table_hbm.at[pl.ds(starts[tile], VOCAB_TILE)]
                pltpu.make_async_copy(window, entries.at[tile], sems.at[tile]).start()

        start_tiles_from(0, 1)

        def wait_tile(tile):
            window = table_hbm.at[pl.ds(0, VOCAB_TILE)]
            pltpu.make_async_copy(window, entries.at[tile], sems.at[tile]).wait()

        def logit_steps(l_ref, tile):
            def step(columns):
                l_ref[:, columns] = matmul_t(x_ref[...], entries[tile, columns])

            return [functools.partial(step, columns) for columns in rows_of(VOCAB_TILE, GROUP)]

        def soft_steps(l_ref, p_ref, factor_ref, tile):
            start = jnp.minimum(tile * VOCAB_TILE, vocab - VOCAB_TILE)
            lane = lax.broadcasted_iota(jnp.int32, (1, VOCAB_TILE), 1)
            bias = jnp.where(lane + start >= tile * VOCAB_TILE, 0.0, -1e30)

            def step(at):
                logits = l_ref[at] + bias
                earlier = top[at]
                highest = jnp.maximum(earlier, jnp.max(logits, 1, keepdims=True))
                exponent = jnp.exp(logits - highest)
                factor = jnp.exp(earlier - highest)
                top[at] = highest
                total[at] = total[at] * factor + jnp.sum(exponent, 1, keepdims=True)
                p_ref[at] = low(exponent)
                factor_ref[at] = across(factor)

            return [functools.partial(step, at) for at in rows_of(count, SMALL_ROWS)]

        def sum_steps(p_ref, factor_ref, tile):
            def step(columns):
                factor = factor_ref[...]
                factor = jnp.concatenate([factor, factor], 1)
                acc[:, columns] = acc[:, columns] * factor + matmul(p_ref[...], entries[tile, :, columns])

            return [functools.partial(step, columns) for columns in rows_of(D, GROUP)]

        acc[...] = jnp.zeros_like(acc)
        top[...] = jnp.full_like(top, -1e30)
        total[...] = jnp.zeros_like(total)
        p_odd[...] = jnp.zeros_like(p_odd)
        factor_odd[...] = jnp.ones_like(factor_odd)
        fetch.wait()
        wait_tile(0)
        start_tiles_from(1, tiles - 1)
        alternate(logit_steps(l_even, 0))

        def turn(j, carry):
            even, odd = 2 * j, 2 * j + 1
            before, after = jnp.maximum(even - 1, 0), jnp.minimum(even + 2, tiles - 1)
            wait_tile(odd)

            @pl.when(even + 2 < tiles)
            def _():
                wait_tile(even + 2)

            alternate(
                soft_steps(l_even, p_even, factor_even, even),
                sum_steps(p_odd, factor_odd, before) + logit_steps(l_odd, odd),
            )
            alternate(
                soft_steps(l_odd, p_odd, factor_odd, odd),
                sum_steps(p_even, factor_even, even) + logit_steps(l_even, after),
            )
            return carry

        lax.fori_loop(0, tiles // 2, turn, 0)
        alternate(sum_steps(p_odd, factor_odd, tiles - 1))
        out_ref[:, :D] = low(acc[...])
        out_ref[:, D:] = head_stats(top[...], total[...])
        copy = pltpu.make_async_copy(out_ref, out_hbm, sems.at[tiles])
        copy.start()
        copy.wait()

    hbm = pl.BlockSpec(memory_space=pltpu.HBM)
    return pl.pallas_call(
        kernel,
        in_specs=[hbm, hbm],
        out_specs=hbm,
        out_shape=low_shape(count, D + LANES),
        scratch_shapes=[
            pltpu.VMEM((count, D), BF16),
            pltpu.VMEM((count, D + LANES), BF16),
            pltpu.VMEM((tiles, VOCAB_TILE, D), BF16),
            pltpu.VMEM((count, D), F32),
            pltpu.VMEM((count, 1), F32),
            pltpu.VMEM((count, 1), F32),
        ]
        + [pltpu.VMEM((count, LANES), F32)] * 2
        + [pltpu.VMEM((count, VOCAB_TILE), F32)] * 2
        + [pltpu.VMEM((count, VOCAB_TILE), BF16)] * 2
        + [pltpu.SemaphoreType.DMA((tiles + 1,))],
        compiler_params=params_for(MOST_VMEM),
        name="vocabulary_head",
    )(rows.reshape(count, D), table).reshape(parts, each, D + LANES)


def blocked_head_kernel(rows, table):
    parts_in, each, _ = rows.shape
    count, vocab = parts_in * each, table.shape[0]
    last = pl.cdiv(vocab, VOCAB_TILE) - 1
    turns = last // 2 + 1

    def kernel(x_hbm, even_ref, odd_ref, after_ref, out_hbm, *refs):
        x_ref, out_ref, acc, top, total, l_even, l_odd, p_even, p_odd, sems = refs
        turn = pl.program_id(0)

        def entries_of(ref, tile):
            row = lax.broadcasted_iota(jnp.int32, (VOCAB_TILE, 1), 0)
            return jnp.where(row < vocab - tile * VOCAB_TILE, ref[...], jnp.zeros_like(ref))

        @pl.when(turn == 0)
        def _():
            copy = pltpu.make_async_copy(x_hbm, x_ref, sems.at[0])
            copy.start()
            acc[...] = jnp.zeros_like(acc)
            top[...] = jnp.full_like(top, -1e30)
            total[...] = jnp.zeros_like(total)
            entries = entries_of(even_ref, 0)
            copy.wait()
            l_even[...] = matmul_t(x_ref[...], entries)

        even = entries_of(even_ref, 2 * turn)
        odd = entries_of(odd_ref, 2 * turn + 1)
        after = entries_of(after_ref, 2 * turn + 2)
        for tile, l_now, p_now, now, l_later, later in (
            (2 * turn, l_even, p_even, even, l_odd, odd),
            (2 * turn + 1, l_odd, p_odd, odd, l_even, after),
        ):
            bias = key_bias(vocab - tile * VOCAB_TILE, (1, VOCAB_TILE), 1)
            for at in rows_of(count, SMALL_ROWS):
                logits = l_now[at] + bias
                earlier = top[at]
                highest = jnp.maximum(earlier, jnp.max(logits, 1, keepdims=True))
                exponent = jnp.exp(logits - highest)
                factor = jnp.exp(earlier - highest)
                top[at] = highest
                total[at] = total[at] * factor + jnp.sum(exponent, 1, keepdims=True)
                p_now[at] = low(exponent)
                acc[at] = acc[at] * factor
            l_later[...] = matmul_t(x_ref[...], later)
            acc[...] += matmul(p_now[...], now)

        @pl.when(turn == turns - 1)
        def _():
            out_ref[:, :D] = low(acc[...])
            out_ref[:, D:] = head_stats(top[...], total[...])
            copy = pltpu.make_async_copy(out_ref, out_hbm, sems.at[1])
            copy.start()
            copy.wait()

    def tile_at(shift):
        return pl.BlockSpec((VOCAB_TILE, D), lambda j: (jnp.minimum(2 * j + shift, last), 0))

    hbm = pl.BlockSpec(memory_space=pltpu.HBM)
    return pl.pallas_call(
        kernel,
        grid=(turns,),
        in_specs=[hbm] + [tile_at(shift) for shift in range(3)],
        out_specs=hbm,
        out_shape=shape_of(count, D + LANES, kind=BF16),
        scratch_shapes=[
            pltpu.VMEM((count, D), BF16),
            pltpu.VMEM((count, D + LANES), BF16),
            pltpu.VMEM((count, D), F32),
            pltpu.VMEM((count, 1), F32),
            pltpu.VMEM((count, 1), F32),
            pltpu.VMEM((count, VOCAB_TILE), F32),
            pltpu.VMEM((count, VOCAB_TILE), F32),
            pltpu.VMEM((count, VOCAB_TILE), BF16),
            pltpu.VMEM((count, VOCAB_TILE), BF16),
            pltpu.SemaphoreType.DMA((2,)),
        ],
        compiler_params=params_for(MOST_VMEM),
        name="vocabulary_head",
    )(rows.reshape(count, D), table, table, table).reshape(parts_in, each, D + LANES)


def swap_add(own, other):
    came = lax.ppermute(low(other), "section", [(0, 1), (1, 0)])
    return own + came.astype(F32)


def pick(first_section, both):
    return jnp.where(first_section, both[0], both[1])


def plan_requests(ids, weights, vocab_rows, slots, parts):
    turned = jnp.transpose(ids)

    def kernel(ids_ref, turned_ref, weights_ref, asked_ref, code_ref, spot_ref):
        here = lax.axis_index("section")
        i_index = lax.broadcasted_iota(jnp.int32, (IDS, IDS), 0)
        j_index = lax.broadcasted_iota(jnp.int32, (IDS, IDS), 1)
        earlier, later = j_index < i_index, i_index < j_index

        def owner_of(values):
            return jnp.floor((values.astype(F32) + 0.5) * (1.0 / vocab_rows)).astype(jnp.int32)

        def count(hits, axis):
            return jnp.sum(hits.astype(F32), axis, keepdims=True)

        most = jnp.zeros((1, 1), F32)
        for m in range(MICRO):
            row, col = ids_ref[m : m + 1], turned_ref[:, m : m + 1]
            same_id = row == col
            first_col = count(same_id & earlier, 1) == 0
            first_row = count(same_id & later, 0) == 0
            owner_row, owner_col = owner_of(row), owner_of(col)
            same_owner = owner_row == owner_col
            rank_row = count(same_owner & later & first_col, 0)
            rank_col = count(same_owner & earlier & first_row, 1)
            most = jnp.maximum(most, jnp.max(rank_row, 1, keepdims=True))

            @pl.when(here == m)
            def _():
                slot_row = jnp.sum(jnp.where(same_id & first_col, rank_col, 0.0), 0, keepdims=True)
                slot_col = jnp.sum(jnp.where(same_id & first_row, rank_row, 0.0), 1, keepdims=True)
                slot_row, slot_col = slot_row.astype(jnp.int32), slot_col.astype(jnp.int32)
                code_ref[...] = (owner_row + parts * first_row.astype(jnp.int32)) * 1024 + slot_row
                spot = jnp.where(slot_col < slots, owner_col * slots + slot_col, -1)
                spot_ref[...] = jnp.broadcast_to(spot, (IDS, LANES))
                lane = lax.broadcasted_iota(jnp.int32, (IDS, LANES), 1)
                local = (col - owner_col * vocab_rows).astype(F32)
                wanted = first_col & (slot_col < slots) & (slot_col == lane)
                wanted = jnp.where(wanted, local, 0.0)
                for part in range(parts):
                    asked = jnp.sum(jnp.where(owner_col == part, wanted, 0.0), 0, keepdims=True)
                    asked_ref[part] = asked.astype(jnp.int32)

        rounds = jnp.floor((most + 0.5) * (1.0 / slots)).astype(jnp.int32) + 1
        total = jnp.sum(jnp.sum(weights_ref[...], 0, keepdims=True), 1, keepdims=True)
        lane = lax.broadcasted_iota(jnp.int32, (1, LANES), 1)
        for part in range(parts):
            row = asked_ref[part]
            asked_ref[part] = jnp.where(lane == slots, rounds, jnp.where(lane == slots + 1, total, row))

    return pl.pallas_call(
        kernel,
        out_shape=[
            jax.ShapeDtypeStruct((parts, 1, LANES), jnp.int32),
            jax.ShapeDtypeStruct((1, IDS), jnp.int32),
            jax.ShapeDtypeStruct((IDS, LANES), jnp.int32),
        ],
        compiler_params=params_for(24),
        name="plan_requests",
    )(ids, turned, weights)


def fetch_rows(table, ids, first_section, plan, slots):
    parts = lax.axis_size("dp")
    vocab_rows = table.shape[0]
    asked, code, spot = plan
    asked = lax.all_to_all(asked, "dp", 0, 0)[:, 0]
    total_rounds = jnp.max(asked[:, slots])
    weight_sum = jnp.sum(asked[:, slots + 1])

    def answer(asked):
        rows = table.at[asked.reshape(-1)].get(mode="promise_in_bounds").reshape(parts, slots, D)
        return lax.all_to_all(rows, "dp", 0, 0).reshape(parts * slots, D)

    came = answer(asked[:, :slots])

    def more(state):
        return state[0] < total_rounds

    def another(state):
        turn, extra = state
        place, slot = code[0] // 1024, code[0] % 1024
        owner, first = place % parts, place >= parts
        local = pick(first_section, ids) - owner * vocab_rows
        here = slot - turn * slots
        at = jnp.where((here >= 0) & (here < slots), owner * slots + here, -1)
        hits = at[:, None] == jnp.arange(parts * slots)[None, :]
        wanted = jnp.sum(jnp.where(hits & first[:, None], local[:, None], 0), 0).reshape(parts, slots)
        rows = answer(lax.all_to_all(wanted, "dp", 0, 0))
        return turn + 1, extra + matmul(hits.astype(BF16), rows)

    extra = lax.while_loop(more, another, (jnp.int32(1), jnp.zeros((IDS, D), F32)))[1]
    return came, spot, extra, total_rounds, weight_sum.astype(F32)


def three_low(values):
    high = low(values)
    rest = values - high.astype(F32)
    middle = low(rest)
    return [high, middle, low(rest - middle.astype(F32))]


def in_groups(count):
    return lax.axis_size("dp") == COUPLING_GROUPS and count == 4 * PART_GROUPS


def gather_params(master, vector):
    parts = lax.axis_size("dp")
    count, width = master.shape[0], vector.shape[0]
    if in_groups(count):
        lines = 4
        planes = parts // lines
        across_planes = [[plane * lines + line for plane in range(planes)] for line in range(lines)]
        in_plane = [[plane * lines + line for line in range(lines)] for plane in range(planes)]
        some = pack_own(master, vector[None], planes)
        some = lax.all_to_all(some, "dp", 0, 0, axis_index_groups=across_planes)
        own = lax.all_gather(some, "dp", axis_index_groups=in_plane)
        return unpack_all(own, lax.ppermute(own, "section", [(0, 1), (1, 0)]), width)
    flat = low(jnp.concatenate([master.reshape(-1), vector]))
    gathered = lax.all_gather(flat, ("section", "dp")).reshape(MICRO, parts, -1)
    size = count * BLOCK**2
    all_blocks = gathered[:, :, :size].reshape(MICRO, parts * count, BLOCK, BLOCK)
    all_vectors = gathered[:, :, size:].reshape(MICRO, parts * width)
    both = [split_params(all_blocks[s], all_vectors[s]) for s in range(MICRO)]

    def stacked(which):
        down, bias_down, up, bias_up = (jnp.stack([pair[which][i] for pair in both]) for i in range(4))
        return Params(down, bias_down.astype(F32)[:, None], up, bias_up.astype(F32)[:, None])

    return stacked(0), stacked(1)


def sum_at_owners(grads, loss_part, count):
    parts = lax.axis_size("dp")
    width = sum(BIASES) // parts
    flat = []
    for adapter, coupling in grads:
        blocks, vector = join_params(adapter, coupling)
        flat.append(
            jnp.concatenate([blocks.reshape(parts, count * BLOCK**2), vector.reshape(parts, width)], 1)
        )
    first = lax.axis_index("section") == 0
    summed = swap_add(jnp.where(first, flat[0], flat[1]), jnp.where(first, flat[1], flat[0]))
    owned = jnp.sum(lax.all_to_all(low(summed), "dp", 0, 0).astype(F32), 0)
    blocks = owned[: count * BLOCK**2].reshape(count, BLOCK, BLOCK)
    pair = jnp.stack([jnp.sum(owned * owned), loss_part[0, 0]])
    pair = jnp.pad(pair, (0, LANES - 2))[None, None]
    return blocks, owned[count * BLOCK**2 :], jnp.broadcast_to(pair, (parts * MICRO, 8, LANES))


def to_coupling_owners(group):
    arrived = []
    for place in range(PART_GROUPS):
        route = []
        for part in range(COUPLING_GROUPS):
            owner, at = divmod(ADAPTER_GROUPS + part, PART_GROUPS)
            if at == place:
                route.append((part, owner))
        arrived.append(lax.ppermute(group, "dp", route))
    return arrived


def exact(spec, left, right):
    return jnp.einsum(spec, left, right, precision=HIGHEST)


def update(pair, products, turned_old, grad_vector, state):
    master, momentum, stat_left, stat_right, vectors, vec_first, vec_second = state
    grad, left_square, right_square, turned = products

    blocks = (1,) + grad.shape
    outs = [shape_of(*blocks)] * 5 + [low_shape(*blocks)] + [shape_of(*vectors.shape)] * 3 + [shape_of(1, 1)] * 2

    def body(ins, out, scalar_refs, pair_refs, raw_refs, scratch):
        start(ins)
        (pair_ref, grad_ref, left_ref, right_ref, turned_ref, vector_ref, old_ref), ins = (
            [operand.get() for operand in ins[:7]],
            [operand.get() for operand in ins[7:]],
        )
        master_ref, momentum_ref, stat_left_ref, stat_right_ref, vectors_ref, first_ref, second_ref = ins
        outs = [result.buffer for result in out]
        totals = jnp.sum(pair_ref[...], 0)[:1]
        norm = jnp.sqrt(totals[:, :1])
        factor = CLIP_NORM / jnp.maximum(norm, CLIP_NORM)
        outs[9][...] = norm
        outs[10][...] = totals[:, 1:2]
        square = (1.0 - STAT_DECAY) * factor * factor
        for n in range(grad_ref.shape[0]):
            clipped = grad_ref[n] * factor
            outs[0][0, n] = clipped
            outs[1][0, n] = FIRST_DECAY * momentum_ref[n] + (1.0 - FIRST_DECAY) * clipped
            outs[2][0, n] = STAT_DECAY * stat_left_ref[n] + square * left_ref[n]
            outs[3][0, n] = STAT_DECAY * stat_right_ref[n] + square * right_ref[n]
            direction = FIRST_DECAY * old_ref[n] + (1.0 - FIRST_DECAY) * factor * turned_ref[n]
            master_new = master_ref[n] - MAT_RATE * (direction + MAT_DECAY * master_ref[n])
            outs[4][0, n] = master_new
            outs[5][0, n] = low(master_new)
        clipped = vector_ref[...] * factor
        first_new = FIRST_DECAY * first_ref[...] + (1.0 - FIRST_DECAY) * clipped
        second_new = VEC_SECOND * second_ref[...] + (1.0 - VEC_SECOND) * clipped * clipped
        outs[6][...] = first_new
        outs[7][...] = second_new
        corrected_first = first_new / (1.0 - FIRST_DECAY**STEP)
        corrected_second = second_new / (1.0 - VEC_SECOND**STEP)
        outs[8][...] = vectors_ref[...] - VEC_RATE * (
            corrected_first / (jnp.sqrt(corrected_second) + VEC_EPS) + VEC_DECAY * vectors_ref[...]
        )

    ins = [pair, grad, left_square, right_square, turned, grad_vector, turned_old]
    ins += [master, momentum, stat_left, stat_right, vectors, vec_first, vec_second]
    return moved_call(body, (), ins, outs, (), [], "update")[0]


def shards(
    token_ids,
    lengths,
    positions,
    targets,
    loss_weights,
    embed_table,
    pos_table,
    norm_params,
    base_qkv,
    base_out,
    base_up,
    base_down,
    master,
    momentum,
    stat_left,
    stat_right,
    root_left,
    root_right,
    vectors,
    vec_first,
    vec_second,
):
    parts = lax.axis_size("dp")
    first_section = lax.axis_index("section") == 0
    slots = -(-IDS * 5 // (4 * parts * 16)) * 16

    ids = jnp.concatenate([token_ids[:, 0], targets[:, 0]], -1)
    plan = plan_requests(ids, loss_weights[:, 0], embed_table.shape[0], slots, parts)
    adapter, coupling = gather_params(master[0], vectors[0])
    swap = [(0, 1), (1, 0)]
    pairs = [(w, lax.ppermute(w, "section", swap)) for w in (base_qkv, base_out, base_up, base_down)]
    came = lax.ppermute(norm_params, "section", swap)
    norms = jnp.concatenate([pick(first_section, (norm_params, came)), pick(first_section, (came, norm_params))])

    came, spot, extra, rounds, weight_sum = fetch_rows(embed_table, ids, first_section, plan, slots)
    turned_old = exact("nij,njk->nik", exact("nij,njk->nik", root_left[0], momentum[0]), root_right[0])
    spot, turned_old = lax.optimization_barrier((spot, turned_old))
    length = pick(first_section, lengths)
    spots = pick(first_section, positions[:, 0])
    row_weights = pick(first_section, loss_weights[:, 0]).astype(F32)
    chosen = (spots[:, None] == jnp.arange(SEQ)[None, :]).astype(BF16)
    chosen_t = (spots[None, :] == jnp.arange(SEQ)[:, None]).astype(F32)

    ins = ForwardIn(came, spot, extra, pos_table, norms, chosen, adapter, coupling)
    kept, rows = forward_kernel(ins, (length, rounds.reshape(1)), pairs, parts, slots)

    rows = lax.all_to_all(rows, "dp", 0, 0)
    merged = lax.all_to_all(head_kernel(rows, embed_table), "dp", 0, 0)

    packed = in_groups(master.shape[1])
    row_weights = jnp.broadcast_to(row_weights[:, None], (COUNT, LANES))
    weight_row = jnp.broadcast_to(weight_sum, (1, LANES))
    adapter, coupling = adapter[::2], coupling[::2]
    ins = BackIn(
        merged, row_weights, weight_row, norms, chosen_t, adapter, coupling,
        kept.target_rows, kept.rest_0, kept.attention_1, kept.rest_1, kept.last,
    )
    back = backward_kernel(ins, (length,), pairs, packed)
    loss_part, mixed_grad = back.loss, back.mixed
    if packed:
        own, other = back.adapters[MICRO:]
        summed = low(swap_add(own.astype(F32), other))
        summed, mixed_grad = lax.optimization_barrier((summed, mixed_grad))
        adapter_came = lax.all_to_all(summed, "dp", 0, 0)
    ins = FirstIn(
        kept.attention_0, mixed_grad, back.start, coupling, kept.one, kept.two, back.one, back.two,
        back.adapters[:MICRO] if packed else (),
    )
    grads = first_backward(ins, (length,), pairs, packed)
    if packed:
        adapter_total, squares = sum_adapter(adapter_came)
        came = lax.all_to_all(low(swap_add(*grads)), "dp", 0, 0)
        group, bias, pair = sum_coupling(came, squares, loss_part, parts * MICRO)
        products = grad_products(adapter_total, to_coupling_owners(group), root_left[0], root_right[0])
        grad_vector = bias[:1, : vectors.shape[1]]
    else:
        both = [(back.adapters[s], grads[4 * s : 4 * s + 4]) for s in range(MICRO)]
        grad, grad_vector, pair = sum_at_owners(both, loss_part, master.shape[1])
        turned = exact("nij,njk->nik", exact("nij,njk->nik", root_left[0], grad), root_right[0])
        products = grad, exact("nij,nkj->nik", grad, grad), exact("nji,njk->nik", grad, grad), turned
        grad_vector = grad_vector[None]
    pair = lax.all_to_all(pair, ("dp", "section"), 0, 0)
    state = (master, momentum, stat_left, stat_right)
    *outs, grad_norm, loss_sum = update(
        pair, products, turned_old, grad_vector, [value[0] for value in state] + [vectors, vec_first, vec_second]
    )
    return (*outs, grad_norm[0, 0], loss_sum[0, 0], weight_sum)


def solution(mesh):
    rows = P(None, "dp", None)
    section = P("section", None, None)
    blocks = P("section", "dp", None, None)
    biases = P("section", "dp")
    return jax.shard_map(
        shards,
        mesh=mesh,
        in_specs=(rows, P(None, "dp"), rows, rows, rows, P("dp", None), P())
        + (section,) * 5
        + (blocks,) * 6
        + (biases,) * 3,
        out_specs=(blocks,) * 6 + (biases,) * 3 + (P(),) * 3,
        check_vma=False,
    )
```

```python
import functools
from typing import Any, NamedTuple

import jax
import jax.numpy as jnp
import numpy as np
from jax import lax
from jax.experimental import pallas as pl
from jax.experimental.pallas import tpu as pltpu
from jax.sharding import PartitionSpec as P

D = 768
HEADS = 12
HEAD_DIM = 64
BOT = 384
INV_H = 192
SEQ = 512
COUNT = 32
MICRO = 2
BLOCK = 48
STEP = 10
HALF = 384
IDS = SEQ + COUNT

HIGHEST = lax.Precision.HIGHEST
NORM_EPS = 1e-12
CLIP_NORM = 0.02
FIRST_DECAY = 0.9
STAT_DECAY = 0.99
MAT_RATE = 0.1
MAT_DECAY = 0.01
VEC_RATE = 0.05
VEC_SECOND = 0.999
VEC_EPS = 1e-08
VEC_DECAY = 0.01
F32 = jnp.float32
BF16 = jnp.bfloat16

CDF_SCALE = 0.42 / 2.0**0.5
CDF_POLY = (
    0.2368242366796694,
    0.239585811361218,
    0.1947261443420679,
    0.2687426685879861,
    -0.13052645834187002,
    0.4406726942003943,
    -0.32025628294963193,
    0.07023101752398136,
)


def matmul(left, right):
    return jnp.dot(left, right, preferred_element_type=F32)


def matmul_t(left, right):
    return lax.dot_general(left, right, (((1,), (1,)), ((), ())), preferred_element_type=F32)


def inner_rows(left, right):
    return lax.dot_general(left, right, (((0,), (0,)), ((), ())), preferred_element_type=F32)


def low(values):
    return values.astype(BF16)


def gelu_both(values):
    below = 1.0 + CDF_SCALE * jnp.abs(values)
    ratio = pl.reciprocal(below, approx=True)
    ratio = ratio * (2.0 - below * ratio)
    poly = jnp.full_like(ratio, 0.5 * CDF_POLY[-1])
    for factor in CDF_POLY[-2::-1]:
        poly = poly * ratio + 0.5 * factor
    bell = jnp.exp(-0.5 * values * values)
    tail = bell * (poly * ratio)
    cdf = jnp.where(values < 0, tail, 1.0 - tail)
    return values * cdf, cdf + values * (bell * (2.0 * np.pi) ** -0.5)


def layer_norm(values, gain, shift):
    centered = values - jnp.mean(values, -1, keepdims=True)
    inverse = lax.rsqrt(jnp.mean(centered * centered, -1, keepdims=True) + NORM_EPS)
    normal = centered * inverse
    return normal * gain + shift, (normal, inverse)


def norm_back(incoming, kept, gain):
    normal, inverse = kept
    scaled = incoming * gain
    return inverse * (
        scaled
        - jnp.mean(scaled, -1, keepdims=True)
        - normal * jnp.mean(scaled * normal, -1, keepdims=True)
    )


def to_blocks(matrix):
    rows_in, cols_in = matrix.shape
    return (
        matrix.reshape(rows_in // BLOCK, BLOCK, cols_in // BLOCK, BLOCK)
        .transpose(0, 2, 1, 3)
        .reshape(-1, BLOCK, BLOCK)
    )


def from_blocks(blocks, rows_in, cols_in):
    return (
        blocks.reshape(rows_in // BLOCK, cols_in // BLOCK, BLOCK, BLOCK)
        .transpose(0, 2, 1, 3)
        .reshape(rows_in, cols_in)
    )


def split_params(blocks, vector):
    adapter_count = D * BOT // BLOCK**2
    half_count = HALF * INV_H // BLOCK**2
    split_at = 2 * adapter_count
    adapter = (
        from_blocks(blocks[:adapter_count], D, BOT),
        vector[:BOT],
        from_blocks(blocks[adapter_count:split_at], BOT, D),
        vector[BOT : BOT + D],
    )
    coupling = (
        from_blocks(blocks[split_at : split_at + half_count], HALF, INV_H),
        vector[BOT + D : BOT + D + INV_H],
        from_blocks(blocks[split_at + half_count :], INV_H, HALF),
        vector[BOT + D + INV_H :],
    )
    return adapter, coupling


def join_params(adapter, coupling):
    blocks = jnp.concatenate(
        [to_blocks(adapter[0]), to_blocks(adapter[2]), to_blocks(coupling[0]), to_blocks(coupling[2])]
    )
    return blocks, jnp.concatenate([adapter[1], adapter[3], coupling[1], coupling[3]], 1)[0]


GROUP_ROWS = 72
LANES = 128


def params_for(mebibytes):
    return pltpu.CompilerParams(vmem_limit_bytes=mebibytes * 2**20)


def roll(values, shift):
    return pltpu.roll(values, shift, 1)


def lane_of(values):
    return lax.broadcasted_iota(jnp.int32, values.shape, 1)


def fold_half(values, upper):
    top, bottom = values[:24], values[24:]
    if upper:
        return jnp.where(lane_of(top) < 64, roll(top, 64), bottom)
    return jnp.where(lane_of(top) < 64, top, roll(bottom, 64))


def unfold_half(values, upper):
    turned = roll(values, 64)
    return jnp.concatenate([turned, values] if upper else [values, turned], 0)


def join_pair(main_0, rest_0, main_1, rest_1):
    left = lane_of(main_0) < 64
    turned = roll(main_1, 64)
    return (
        main_0,
        jnp.where(left, unfold_half(rest_0, False), turned),
        jnp.where(left, turned, unfold_half(rest_1, True)),
    )


def cut_pair(tile_0, tile_1, tile_2):
    left = lane_of(tile_0) < 64
    return (
        (tile_0, fold_half(tile_1, False)),
        (jnp.where(left, roll(tile_1, 64), roll(tile_2, 64)), fold_half(tile_2, True)),
    )


def chunk_rows(own_blocks):
    return own_blocks // 4 * GROUP_ROWS + 8


def bias_row(tiles, part, width):
    at, shift = divmod(part * width, LANES)
    lane = lane_of(tiles[0])
    row = tiles[at]
    if shift:
        row = jnp.where(lane < LANES - shift, roll(row, LANES - shift), roll(tiles[at + 1], LANES - shift))
    return jnp.where(lane < width, row, 0.0)


def bias_tiles(first, second, third, fourth):
    cut = lambda values: [values[:, at : at + LANES] for at in range(0, values.shape[1], LANES)]
    zero = jnp.zeros((1, LANES), F32)
    left = lane_of(zero) < 64
    third_tail = jnp.concatenate([third[:, LANES:]] * 2, 1)
    turned = [roll(tile, 64) for tile in cut(fourth)]
    joints = [jnp.where(left, one, two) for one, two in zip([third_tail] + turned, turned + [zero])]
    return cut(first) + cut(second) + [third[:, :LANES]] + joints + [zero]


def tiles_of_rows(rows, width):
    tiles = []
    for tile in range(-(-len(rows) * width // LANES)):
        value = jnp.zeros((8, LANES), F32)
        lane = lane_of(value)
        for part, row in enumerate(rows):
            shift = part * width - tile * LANES
            if shift >= LANES or shift + width <= 0:
                continue
            turned = roll(row, shift % LANES) if shift % LANES else row
            value = jnp.where((lane >= shift) & (lane < shift + width), turned, value)
        tiles.append(value)
    return tiles


def pack_own(master, vector, copies):
    count, width = master.shape[0], vector.shape[1]

    def kernel(master_ref, bias_ref, out_ref):
        row = lax.broadcasted_iota(jnp.int32, (BLOCK, 256), 0)
        col = lax.broadcasted_iota(jnp.int32, (BLOCK, 256), 1)
        pieces = []
        for group in range(count // 4):
            wide = jnp.zeros((BLOCK, 256), F32)
            for j in range(4):
                wide += matmul(low(master_ref[4 * group + j]), (col == row + BLOCK * j).astype(BF16))
            pieces += [wide[:, :LANES], fold_half(wide[:, LANES:], False)]
        bias = jnp.concatenate([bias_ref[...], jnp.zeros((1, LANES - width), F32)], 1)
        pieces.append(jnp.concatenate([bias, jnp.zeros((7, LANES), F32)], 0))
        packed = low(jnp.concatenate(pieces, 0))
        for copy in range(copies):
            out_ref[copy] = packed

    return pl.pallas_call(
        kernel,
        out_shape=jax.ShapeDtypeStruct((copies, chunk_rows(count), LANES), BF16),
        name="pack_own",
    )(master, vector)


MATRICES = ((D, BOT), (BOT, D), (HALF, INV_H), (INV_H, HALF))
BIASES = (BOT, D, INV_H, HALF)


def unpack_all(own, came, width):
    lines, planes, rows, _ = own.shape
    parts = lines * planes
    per_part = (rows - 8) // GROUP_ROWS

    def kernel(own_hbm, came_hbm, *refs):
        out_hbm, in_bufs, out_refs, in_sems, out_sems = refs[:8], refs[8], refs[9:17], refs[17], refs[18]
        here = lax.axis_index("section")
        copies = [
            pltpu.make_async_copy(ref, in_bufs.at[at], in_sems.at[i])
            for i, (ref, at) in enumerate(((own_hbm, here), (came_hbm, 1 - here)))
        ]
        for copy in copies:
            copy.start()
        for copy in copies:
            copy.wait()

        def unpack(s, carry):
            cache = {}

            def group(index):
                part = index // per_part
                if part not in cache:
                    cache.clear()
                    cache[part] = in_bufs[s, part % lines, part // lines].astype(F32)
                base = index % per_part * GROUP_ROWS
                chunk = cache[part]
                return chunk[base : base + BLOCK], chunk[base + BLOCK : base + GROUP_ROWS]

            index = 0
            for (height, columns), out_ref in zip(MATRICES, out_refs):
                for top in range(0, height, BLOCK):
                    if columns == INV_H:
                        main, rest = group(index)
                        index += 1
                        out_ref[s, top : top + BLOCK, :LANES] = low(main)
                        out_ref[s, top : top + BLOCK, LANES:] = low(unfold_half(rest, False)[:, :64])
                        continue
                    for left in range(0, columns, HALF):
                        tiles = join_pair(*group(index), *group(index + 1))
                        index += 2
                        for j, tile in enumerate(tiles):
                            at = left + j * LANES
                            out_ref[s, top : top + BLOCK, at : at + LANES] = low(tile)
            tiles = tiles_of_rows(
                [in_bufs[s, part % lines, part // lines, rows - 16 :].astype(F32)[8:] for part in range(parts)], width
            )
            first, second, third, fourth = out_refs[4:]
            first[s] = jnp.concatenate(tiles[:3], 1)[:1]
            second[s] = jnp.concatenate(tiles[3:9], 1)[:1]
            third[s] = jnp.concatenate([tiles[9], tiles[10][:, :64]], 1)[:1]
            left = lane_of(tiles[0]) < 64
            turned = [roll(tile, 64) for tile in tiles[10:14]]
            fourth[s] = jnp.concatenate(
                [jnp.where(left, one, two) for one, two in zip(turned, turned[1:])], 1
            )[:1]
            return carry

        lax.fori_loop(0, MICRO, unpack, 0)
        copies = [
            pltpu.make_async_copy(buf, ref, out_sems.at[i]) for i, (buf, ref) in enumerate(zip(out_refs, out_hbm))
        ]
        for copy in copies:
            copy.start()
        for copy in copies:
            copy.wait()

    shapes = [((MICRO,) + shape, BF16) for shape in MATRICES] + [((MICRO, 1, size), F32) for size in BIASES]
    hbm = pl.BlockSpec(memory_space=pltpu.HBM)
    arrays = pl.pallas_call(
        kernel,
        in_specs=[hbm] * 2,
        out_specs=[hbm] * 8,
        out_shape=[jax.ShapeDtypeStruct(*shape) for shape in shapes],
        scratch_shapes=[pltpu.VMEM((MICRO, lines, planes, rows, LANES), BF16)]
        + [pltpu.VMEM(*shape) for shape in shapes]
        + [pltpu.SemaphoreType.DMA((2,)), pltpu.SemaphoreType.DMA((8,))],
        compiler_params=params_for(MOST_VMEM),
        name="unpack_all",
    )(own, came)
    down, up, c_down, c_up, bias_down, bias_up, c_bias_down, c_bias_up = arrays
    return Params(down, bias_down, up, bias_up), Params(c_down, c_bias_down, c_up, c_bias_up)


ADAPTER_GROUPS = 2 * D * BOT // BLOCK**2 // 4
COUPLING_GROUPS = 2 * HALF * INV_H // BLOCK**2 // 4
PART_GROUPS = (ADAPTER_GROUPS + COUPLING_GROUPS) // COUPLING_GROUPS
PART_ROWS = PART_GROUPS * GROUP_ROWS


def groups_of(refs, shapes):
    groups = []
    for ref, (height, width) in zip(refs, shapes):
        for top in range(0, height, BLOCK):
            band = slice(top, top + BLOCK)
            if width == INV_H:
                tail = ref[band, LANES:]
                groups.append((ref[band, :LANES], fold_half(jnp.concatenate([tail, tail], 1), False)))
                continue
            for left in range(0, width, HALF):
                groups += cut_pair(*[ref[band, left + j * LANES : left + (j + 1) * LANES] for j in range(3)])
    return [jnp.concatenate(group, 0) for group in groups]


def pack_adapter(refs, store):
    groups = groups_of(refs, MATRICES[:2])
    empty = jnp.zeros((GROUP_ROWS, LANES), F32)
    for part in range(COUPLING_GROUPS):
        chunk = groups[part * PART_GROUPS : (part + 1) * PART_GROUPS]
        chunk += [empty] * (PART_GROUPS - len(chunk))
        store(part, low(jnp.concatenate(chunk, 0)))


def pack_coupling(refs, tiles, width, store):
    for part, group in enumerate(groups_of(refs, MATRICES[2:])):
        bias = jnp.concatenate([bias_row(tiles, part, width), jnp.zeros((7, LANES), F32)], 0)
        store(part, jnp.concatenate([group, bias], 0))


def sum_parts(came_ref):
    total = came_ref[0].astype(F32)
    for part in range(1, came_ref.shape[0]):
        total += came_ref[part].astype(F32)
    return total


def square_sum(values):
    return jnp.sum(jnp.sum(values * values, 0, keepdims=True), 1, keepdims=True)


def sum_adapter(came):
    def kernel(came_ref, total_ref, square_ref):
        total = sum_parts(came_ref)
        total_ref[...] = total
        square_ref[...] = square_sum(total)

    return pl.pallas_call(
        kernel,
        out_shape=[jax.ShapeDtypeStruct((PART_ROWS, LANES), F32), jax.ShapeDtypeStruct((1, 1), F32)],
        compiler_params=params_for(32),
        name="sum_adapter",
    )(came)


def sum_coupling(came, squares, loss_part, copies):
    def kernel(came_ref, square_ref, loss_ref, group_ref, bias_ref, pair_ref):
        total = sum_parts(came_ref)
        group_ref[...] = total[:GROUP_ROWS]
        bias_ref[...] = total[GROUP_ROWS:]
        squares = square_ref[...] + square_sum(total)
        lane = lax.broadcasted_iota(jnp.int32, (8, LANES), 1)
        pair = jnp.where(lane == 0, squares, jnp.where(lane == 1, loss_ref[:, :1], 0.0))
        for copy in range(copies):
            pair_ref[copy] = pair

    return pl.pallas_call(
        kernel,
        out_shape=[
            jax.ShapeDtypeStruct((GROUP_ROWS, LANES), F32),
            jax.ShapeDtypeStruct((8, LANES), F32),
            jax.ShapeDtypeStruct((copies, 8, LANES), F32),
        ],
        name="sum_coupling",
    )(came, squares, loss_part)


def grad_products(adapter_total, coupling_groups, root_left, root_right):
    count = 4 * PART_GROUPS

    def exact_dot(left, right, dims):
        return lax.dot_general(left, right, (dims, ((), ())), precision=HIGHEST, preferred_element_type=F32)

    def body(ins, out, scalar_refs, pair_refs, raw_refs, scratch):
        start(ins)
        total_ref, left_ref, right_ref, *group_refs = (operand.get() for operand in ins)
        grad_ref, left_square_ref, right_square_ref, turned_ref = (result.buffer for result in out)
        for group in range(PART_GROUPS):
            total = total_ref[group * GROUP_ROWS : (group + 1) * GROUP_ROWS] + group_refs[group][...]
            main, rest = total[:BLOCK], unfold_half(total[BLOCK:], False)
            lane = lane_of(main)
            pieces = (
                main,
                roll(main, 80),
                jnp.where(lane < 32, roll(main, 32), roll(rest, 32)),
                roll(rest, 112),
            )
            for j, values in enumerate(pieces):
                grad_ref[4 * group + j] = values[:, :BLOCK]
        for n in range(count):
            grad = grad_ref[n]
            left_square_ref[n] = exact_dot(grad, grad, ((1,), (1,)))
            right_square_ref[n] = exact_dot(grad, grad, ((0,), (0,)))
            turned_ref[n] = exact_dot(
                exact_dot(left_ref[n], grad, ((1,), (0,))), right_ref[n], ((1,), (0,))
            )

    ins = [adapter_total, root_left, root_right, *coupling_groups]
    outs = [jax.ShapeDtypeStruct((count, BLOCK, BLOCK), F32)] * 4
    return moved_call(body, (), ins, outs, (), [], "grad_products")[0]


MOST_VMEM = 64
GROUP = 256
HEADS_IN = GROUP // HEAD_DIM
GROUPS = D // GROUP
FF = 3072
TILE = 512
TILES = FF // TILE
STEP_ROWS = 256
SMALL_ROWS = 32


def rows_of(count, size):
    return [slice(at, at + min(size, count)) for at in range(0, count, size)]


def shape_of(*dims, kind=F32):
    return jax.ShapeDtypeStruct(dims, kind)


class Params(NamedTuple):
    down: Any
    bias_down: Any
    up: Any
    bias_up: Any


class Branch(NamedTuple):
    lin: Any
    act: Any
    slope: Any


class Attention(NamedTuple):
    query: Any
    key: Any
    value: Any
    lse: Any


class Rest(NamedTuple):
    normal_1: Any
    inverse_1: Any
    slope: Any
    branch: Any
    normal_2: Any
    inverse_2: Any


class Last(NamedTuple):
    one: Any
    two: Any
    normal: Any
    inverse: Any
    normed: Any


class ForwardIn(NamedTuple):
    came: Any
    spot: Any
    extra: Any
    pos: Any
    norms: Any
    chosen: Any
    adapter: Any
    coupling: Any


class Forward(NamedTuple):
    target_rows: Any
    one: Any
    two: Any
    attention_0: Any
    rest_0: Any
    attention_1: Any
    rest_1: Any
    last: Any


class BackIn(NamedTuple):
    merged: Any
    row_weights: Any
    weight_sum: Any
    norms: Any
    chosen_t: Any
    adapter: Any
    coupling: Any
    target_rows: Any
    rest_0: Any
    attention_1: Any
    rest_1: Any
    last: Any


class Back(NamedTuple):
    loss: Any
    one: Any
    two: Any
    adapters: Any
    start: Any
    mixed: Any


class FirstIn(NamedTuple):
    attention: Any
    mixed: Any
    start: Any
    coupling: Any
    one: Any
    two: Any
    grads_one: Any
    grads_two: Any
    biases: Any


class Operand:
    def __init__(self, ref, buffer, sem):
        self.buffer, self.copy = buffer, pltpu.make_async_copy(ref, buffer, sem)
        self.started = self.waited = False

    def start(self):
        if not self.started:
            self.copy.start()
        self.started = True

    def get(self):
        self.start()
        if not self.waited:
            self.copy.wait()
        self.waited = True
        return self.buffer


class Result:
    def __init__(self, ref, buffer, sem):
        self.buffer, self.copy = buffer, pltpu.make_async_copy(buffer, ref, sem)
        self.sent = False

    def send(self):
        if not self.sent:
            self.copy.start()
        self.sent = True


def start(*operands):
    for operand in jax.tree.leaves(operands):
        operand.start()


def send(*results):
    for result in jax.tree.leaves(results):
        result.send()


def moved_call(body, scalars, ins, outs, pairs, scratch, name, raw_outs=()):
    in_leaves, in_tree = jax.tree.flatten(ins)
    out_leaves, out_tree = jax.tree.flatten(outs)

    def kernel(*refs):
        refs = list(refs)

        def take(count):
            taken, refs[:] = refs[:count], refs[count:]
            return taken

        scalar_refs, in_refs = take(len(scalars)), take(len(in_leaves))
        pair_refs = [tuple(take(2)) for _ in pairs]
        out_refs, raw_refs = take(len(out_leaves)), take(len(raw_outs))
        in_buffers, out_buffers, (in_sems, out_sems) = take(len(in_leaves)), take(len(out_leaves)), take(2)
        operands = [Operand(*two, in_sems.at[i]) for i, two in enumerate(zip(in_refs, in_buffers))]
        results = [Result(*two, out_sems.at[i]) for i, two in enumerate(zip(out_refs, out_buffers))]
        body(in_tree.unflatten(operands), out_tree.unflatten(results), scalar_refs, pair_refs, raw_refs, refs)
        send(results)
        for operand in operands:
            operand.get()
        for result in results:
            result.copy.wait()

    hbm = pl.BlockSpec(memory_space=pltpu.HBM)
    buffers = [pltpu.VMEM(value.shape, value.dtype) for value in (*in_leaves, *out_leaves)]
    results = pl.pallas_call(
        kernel,
        in_specs=[pl.BlockSpec(memory_space=pltpu.SMEM)] * len(scalars) + [hbm] * (len(in_leaves) + 2 * len(pairs)),
        out_specs=[hbm] * (len(out_leaves) + len(raw_outs)),
        out_shape=[*out_leaves, *raw_outs],
        scratch_shapes=buffers
        + [pltpu.SemaphoreType.DMA((len(in_leaves),)), pltpu.SemaphoreType.DMA((len(out_leaves),))]
        + list(scratch),
        compiler_params=params_for(MOST_VMEM),
        name=name,
    )(*scalars, *in_leaves, *[w for pair in pairs for w in pair])
    return out_tree.unflatten(results[: len(out_leaves)]), results[len(out_leaves) :]


def start_copy(pair, section, window, target, sem):
    own, came = pair
    here = lax.axis_index("section") == section

    @pl.when(here)
    def _():
        pltpu.make_async_copy(own.at[window], target, sem).start()

    @pl.when(jnp.logical_not(here))
    def _():
        pltpu.make_async_copy(came.at[window], target, sem).start()


def wait_copy(pair, window, target, sem):
    pltpu.make_async_copy(pair[0].at[window], target, sem).wait()


def qkv_window(group, part):
    return 0, slice(None), pl.ds(part * D + group * GROUP, GROUP)


def qkv_buffers():
    return [pltpu.VMEM((GROUPS, 3, D, GROUP), BF16), pltpu.SemaphoreType.DMA((GROUPS, 3))]


def start_qkv(pair, section, buffers):
    for group in range(GROUPS):
        for part in range(3):
            start_copy(pair, section, qkv_window(group, part), buffers[0].at[group, part], buffers[1].at[group, part])


def wait_qkv(pair, buffers, group, part):
    wait_copy(pair, qkv_window(0, 0), buffers[0].at[group, part], buffers[1].at[group, part])


UP_WINDOWS = [(0, slice(None), slice(j * TILE, (j + 1) * TILE)) for j in range(TILES)]
DOWN_WINDOWS = [(0, slice(j * TILE, (j + 1) * TILE), slice(None)) for j in range(TILES)]
OUT_WINDOW = (0, slice(None), slice(None))


def rest_buffers():
    return [
        pltpu.VMEM((D, D), BF16),
        pltpu.VMEM((TILES, D, TILE), BF16),
        pltpu.VMEM((TILES, TILE, D), BF16),
        pltpu.SemaphoreType.DMA((2 * TILES + 1,)),
    ]


def start_out(pairs, section, buffers):
    start_copy(pairs[0], section, OUT_WINDOW, buffers[0], buffers[3].at[2 * TILES])


def start_tiles(pairs, section, buffers):
    for j in range(TILES):
        start_copy(pairs[1], section, UP_WINDOWS[j], buffers[1].at[j], buffers[3].at[j])
        start_copy(pairs[2], section, DOWN_WINDOWS[j], buffers[2].at[j], buffers[3].at[TILES + j])


def wait_out(pairs, buffers):
    wait_copy(pairs[0], OUT_WINDOW, buffers[0], buffers[3].at[2 * TILES])


def wait_up(pairs, buffers, tile):
    wait_copy(pairs[1], UP_WINDOWS[0], buffers[1].at[tile], buffers[3].at[tile])


def wait_down(pairs, buffers, tile):
    wait_copy(pairs[2], DOWN_WINDOWS[0], buffers[2].at[tile], buffers[3].at[TILES + tile])


def across(values):
    return jnp.broadcast_to(values, (values.shape[0], LANES))


def group_columns(group):
    return pl.ds(pl.multiple_of(group * GROUP, GROUP), GROUP)


def tile_columns(tile):
    return pl.ds(pl.multiple_of(tile * TILE, TILE), TILE)


def head_mask(values, head):
    lane = lax.broadcasted_iota(jnp.int32, values.shape, 1)
    return (lane >= head * HEAD_DIM) & (lane < (head + 1) * HEAD_DIM)


def only_head(values, head):
    return jnp.where(head_mask(values, head), values, jnp.zeros_like(values))


def scaled_query(query):
    return low(query.astype(F32) * HEAD_DIM**-0.5)


def key_bias(length, shape, axis):
    return jnp.where(lax.broadcasted_iota(jnp.int32, shape, axis) < length, 0.0, -1e30)


def softmax_rows(scores):
    highest = jnp.max(scores, 1, keepdims=True)
    exponent = jnp.exp(scores - highest)
    total = jnp.sum(exponent, 1, keepdims=True)
    return low(exponent * (1.0 / total)), highest + jnp.log(total)


def branch_rows(low_in, weights):
    active, slope = gelu_both(matmul(low_in, weights[0]) + weights[1])
    active = low(active)
    return matmul(active, weights[2]) + weights[3], active, low(slope)


def alternate(*lists):
    steps = [((i + 0.5) / len(steps), k, step) for k, steps in enumerate(lists) for i, step in enumerate(steps)]
    for _, _, step in sorted(steps, key=lambda entry: entry[:2]):
        step()


def section_params(params, section):
    return [operand.get()[section] for operand in params]


def rest_rows(out, rows, section, norms, adapter, hidden, mixed, finish, scratch, pairs, buffers, after_loop=None):
    att_low, acc, u_even, u_odd, g_even, g_odd = scratch
    gain = lambda i: norms[section, i : i + 1]
    parts = rows_of(rows, STEP_ROWS)
    every = slice(0, rows)
    wait_out(pairs, buffers)
    for part in parts:
        first = hidden[part] + matmul(mixed[part], buffers[0][...])
        values, (normal, inverse) = layer_norm(first, gain(2), gain(3))
        acc[part] = values
        att_low[part] = low(values)
        out.normal_1.buffer[part] = normal
        out.inverse_1.buffer[part] = across(inverse)
    send(out.normal_1, out.inverse_1)
    wait_up(pairs, buffers, 0)
    g_odd[every] = jnp.zeros_like(g_odd[every])

    def gelu_steps(u_ref, g_ref, tile):
        def step(at):
            active, slope = gelu_both(u_ref[at])
            g_ref[at] = low(active)
            out.slope.buffer[at, tile_columns(tile)] = low(slope)

        return [functools.partial(step, at) for at in rows_of(rows, SMALL_ROWS)]

    def up_steps(u_ref, tile):
        def step(columns):
            u_ref[every, columns] = matmul(att_low[every], buffers[1][tile, :, columns])

        return [functools.partial(step, columns) for columns in rows_of(TILE, GROUP)]

    def down_steps(g_ref, tile):
        def step(columns):
            acc[every, columns] += matmul(g_ref[every], buffers[2][tile, :, columns])

        return [functools.partial(step, columns) for columns in rows_of(D, GROUP)]

    alternate(up_steps(u_even, 0))

    def turn(j, carry):
        even, odd = 2 * j, 2 * j + 1
        before, after = jnp.maximum(even - 1, 0), jnp.minimum(even + 2, TILES - 1)
        wait_down(pairs, buffers, even)
        wait_up(pairs, buffers, odd)
        wait_down(pairs, buffers, odd)

        @pl.when(even + 2 < TILES)
        def _():
            wait_up(pairs, buffers, even + 2)

        alternate(gelu_steps(u_even, g_even, even), down_steps(g_odd, before) + up_steps(u_odd, odd))
        alternate(gelu_steps(u_odd, g_odd, odd), down_steps(g_even, even) + up_steps(u_even, after))
        return carry

    lax.fori_loop(0, TILES // 2, turn, 0)
    alternate(down_steps(g_odd, TILES - 1))
    if after_loop is not None:
        after_loop()
    send(out.slope)
    weights = section_params(adapter, section)
    for part in parts:
        summed = acc[part]
        low_in = low(summed)
        added, *kept = branch_rows(low_in, weights)
        for result, value in zip(out.branch, (low_in, *kept)):
            result.buffer[part] = value
        values, (normal, inverse) = layer_norm(summed + added, gain(4), gain(5))
        out.normal_2.buffer[part], out.inverse_2.buffer[part] = normal, across(inverse)
        finish(part, values)
    send(out.branch, out.normal_2, out.inverse_2)


def low_shape(*dims):
    return shape_of(*dims, kind=BF16)


def branch_shapes(rows, wide, narrow):
    return Branch(low_shape(rows, wide), low_shape(rows, narrow), low_shape(rows, narrow))


def rest_shapes(rows):
    wide, thin = shape_of(rows, D), shape_of(rows, LANES)
    return Rest(wide, thin, low_shape(rows, FF), branch_shapes(rows, D, BOT), wide, thin)


def forward_kernel(ins, scalars, pairs, parts, slots):
    coupling_shapes = lambda rows: branch_shapes(rows, HALF, INV_H)
    outs = Forward(
        target_rows=shape_of(COUNT, D),
        one=coupling_shapes(SEQ),
        two=coupling_shapes(SEQ),
        attention_0=Attention(*[low_shape(SEQ, D)] * 3, shape_of(GROUPS, 8, SEQ)),
        rest_0=rest_shapes(SEQ),
        attention_1=Attention(
            low_shape(COUNT, D), *[low_shape(SEQ, D)] * 2, shape_of(GROUPS, HEADS_IN * COUNT, LANES)
        ),
        rest_1=rest_shapes(COUNT),
        last=Last(
            coupling_shapes(COUNT), coupling_shapes(COUNT),
            shape_of(COUNT, D), shape_of(COUNT, LANES), low_shape(COUNT, D),
        ),
    )

    def body(ins, out, scalar_refs, pair_refs, raw_refs, scratch):
        length = scalar_refs[0][0]
        hidden, x_low, s_even, s_odd, p_even, p_odd, lse_buf, mixed, section_out = scratch[:9]
        at_spots, at_low, mixed_1 = scratch[9:12]
        rest_scratch, qkv_0, qkv_1, rest_w = scratch[12:18], scratch[18:20], scratch[20:22], scratch[22:26]
        row_sems, joined = scratch[26:28]
        qkv_pair, rest_pairs = pair_refs[0], pair_refs[1:]

        start(ins.came, ins.spot, ins.pos, ins.norms, ins.coupling)
        norms = ins.norms.get()
        norm = lambda s, i: norms[s, i : i + 1]

        came, spot = ins.came.get(), ins.spot.get()
        start_qkv(qkv_pair, 0, qkv_0)
        start_out(rest_pairs, 0, rest_w)

        def rows_at(part):
            lane = lax.broadcasted_iota(jnp.int32, (part.stop - part.start, parts * slots), 1)
            hits = (spot[part][:, :1] == lane).astype(BF16)
            return matmul(hits, came[...])

        targets = slice(SEQ, SEQ + COUNT)
        out.target_rows.buffer[...] = rows_at(targets)
        for part in rows_of(SEQ, STEP_ROWS):
            hidden[part] = rows_at(part)

        @pl.when(scalar_refs[1][0] > 1)
        def _():
            ins.extra.copy.start()
            ins.extra.copy.wait()
            out.target_rows.buffer[...] += ins.extra.buffer[targets]
            hidden[...] += ins.extra.buffer[:SEQ]

        ins.extra.started = ins.extra.waited = True
        send(out.target_rows)
        start(ins.adapter, ins.chosen)
        start_tiles(rest_pairs, 0, rest_w)
        one, two = section_params(ins.coupling, 0), section_params(ins.coupling, 1)

        def put(results, part, *values):
            for result, value in zip(results, values):
                result.buffer[part] = value

        for part in rows_of(SEQ, STEP_ROWS):
            started, _ = layer_norm(hidden[part] + ins.pos.get()[part].astype(F32), norm(0, 0), norm(0, 1))
            left, right = started[:, :HALF], started[:, HALF:]
            low_one = low(right)
            added, active, slope = branch_rows(low_one, one)
            put(out.one, part, low_one, active, slope)
            left = left + added
            low_two = low(left)
            added, active, slope = branch_rows(low_two, two)
            put(out.two, part, low_two, active, slope)
            right = right + added
            hidden[part, :HALF] = left
            hidden[part, HALF:] = right
            x_low[part, :HALF] = low_two
            x_low[part, HALF:] = low(right)
        send(out.one, out.two)

        start_qkv(qkv_pair, 1, qkv_1)
        lse_buf[...] = jnp.zeros((SEQ, LANES), F32)
        q_ref, k_ref, v_ref, lse_ref = (result.buffer for result in out.attention_0)

        def attend(group, carry):
            columns = group_columns(group)
            for part, ref in enumerate((q_ref, k_ref, v_ref)):
                wait_qkv(qkv_pair, qkv_0, group, part)
                ref[:, columns] = low(matmul(x_low[...], qkv_0[0][group, part]))
            query = scaled_query(q_ref[:, columns])
            key, value = k_ref[:, columns], v_ref[:, columns]
            bias = key_bias(length, (1, SEQ), 1)
            lane = lax.broadcasted_iota(jnp.int32, (SMALL_ROWS * 2, LANES), 1)
            buffers = ((s_even, p_even), (s_odd, p_odd)) * 2

            def score_steps(head):
                def step():
                    buffers[head][0][...] = matmul_t(only_head(query, head), key)

                return [step] if head < HEADS_IN else []

            def soft_steps(head):
                def step(rows):
                    soft, lse = softmax_rows(buffers[head][0][rows] + bias)
                    buffers[head][1][rows] = soft
                    lse_buf[rows] = jnp.where(lane == head, lse, lse_buf[rows])

                return [functools.partial(step, rows) for rows in rows_of(SEQ, SMALL_ROWS * 2)]

            def mix_steps(head):
                def step():
                    mixed_head = matmul(buffers[head][1][...], value)
                    if head == 0:
                        joined[...] = mixed_head
                    else:
                        joined[...] = jnp.where(head_mask(mixed_head, head), mixed_head, joined[...])

                return [step] if head >= 0 else []

            alternate(score_steps(0))
            for head in range(HEADS_IN):
                alternate(soft_steps(head), score_steps(head + 1) + mix_steps(head - 1))
            alternate(mix_steps(HEADS_IN - 1))
            mixed[:, columns] = low(joined[...])
            lse_ref[group] = jnp.transpose(lse_buf[...])[:8]
            return carry

        lax.fori_loop(0, GROUPS, attend, 0)
        send(out.attention_0)

        def to_section_out(part, values):
            section_out[part] = low(values)

        def next_weights():
            start_out(rest_pairs, 1, rest_w)
            start_tiles(rest_pairs, 1, rest_w)

        rest_rows(
            out.rest_0, SEQ, 0, norms, ins.adapter, hidden, mixed, to_section_out,
            rest_scratch, rest_pairs, rest_w, next_weights,
        )

        at_spots[...] = matmul(ins.chosen.get()[...], section_out[...])
        at_low[...] = low(at_spots[...])
        q_1, k_1, v_1, lse_1 = (result.buffer for result in out.attention_1)

        groups = rows_of(D, GROUP)
        for group, columns in enumerate(groups):
            for part, ref in enumerate((q_1, k_1, v_1)):
                wait_qkv(qkv_pair, qkv_1, group, part)
                source = at_low if part == 0 else section_out
                ref[:, columns] = low(matmul(source[...], qkv_1[0][group, part]))
        bias = key_bias(length, (1, SEQ), 1)
        for group, columns in enumerate(groups):
            query = scaled_query(q_1[:, columns])
            query = jnp.concatenate([only_head(query, head) for head in range(HEADS_IN)], 0)
            soft, lse = softmax_rows(matmul_t(query, k_1[:, columns]) + bias)
            lse_1[group] = across(lse)
            every = matmul(soft, v_1[:, columns])
            mixed_group = every[:COUNT]
            for head in range(1, HEADS_IN):
                rows = slice(head * COUNT, (head + 1) * COUNT)
                mixed_group = jnp.where(head_mask(mixed_group, head), every[rows], mixed_group)
            mixed_1[:, columns] = low(mixed_group)
        send(out.attention_1)

        def to_normed(part, values):
            left, right = values[:, :HALF], values[:, HALF:]
            low_two = low(left)
            taken, active, slope = branch_rows(low_two, two)
            put(out.last.two, part, low_two, active, slope)
            right = right - taken
            low_one = low(right)
            taken, active, slope = branch_rows(low_one, one)
            put(out.last.one, part, low_one, active, slope)
            left = left - taken
            values, (normal, inverse) = layer_norm(jnp.concatenate([left, right], 1), norm(1, 0), norm(1, 1))
            put(out.last[2:], part, normal, across(inverse), low(values))

        rest_rows(
            out.rest_1, COUNT, 1, norms, ins.adapter, at_spots, mixed_1, to_normed,
            rest_scratch, rest_pairs, rest_w,
        )
        copies = [
            pltpu.make_async_copy(out.last.normed.buffer, raw_refs[0].at[i], row_sems.at[i])
            for i in range(raw[0].shape[0])
        ]
        for copy in copies:
            copy.start()
        for copy in copies:
            copy.wait()

    buffer = lambda *dims: pltpu.VMEM(dims, F32)
    buffer_low = lambda *dims: pltpu.VMEM(dims, BF16)
    scratch = [buffer(SEQ, D), buffer_low(SEQ, D), buffer(SEQ, SEQ), buffer(SEQ, SEQ)]
    scratch += [buffer_low(SEQ, SEQ), buffer_low(SEQ, SEQ), buffer(SEQ, LANES)]
    scratch += [buffer_low(SEQ, D), buffer_low(SEQ, D)]
    scratch += [buffer(COUNT, D), buffer_low(COUNT, D), buffer_low(COUNT, D)]
    scratch += [buffer_low(SEQ, D), buffer(SEQ, D), buffer(SEQ, TILE), buffer(SEQ, TILE)]
    scratch += [buffer_low(SEQ, TILE), buffer_low(SEQ, TILE)]
    scratch += qkv_buffers() + qkv_buffers() + rest_buffers()
    scratch += [pltpu.SemaphoreType.DMA((parts,)), buffer(SEQ, GROUP)]
    raw = [low_shape(parts // LINES if parts == COUPLING_GROUPS else parts, COUNT, D)]
    kept, (rows,) = moved_call(body, scalars, ins, outs, pairs, scratch, "forward", raw)
    return kept, rows


def column_sum(values):
    return jnp.sum(values.astype(F32), 0, keepdims=True)


def branch_grads(grad_low, kept, weights, out_refs):
    low_in, active, slope = kept
    hidden_grad = low(matmul_t(grad_low, weights[2]) * slope.astype(F32))
    out_refs[0][...] = inner_rows(low_in, hidden_grad)
    out_refs[1][...] = column_sum(hidden_grad)
    out_refs[2][...] = inner_rows(active, grad_low)
    out_refs[3][...] = column_sum(grad_low)
    return hidden_grad


ADAPTER_GRADS = ((D, BOT), (1, BOT), (BOT, D), (1, D))
COUPLING_GRADS = ((HALF, INV_H), (1, INV_H), (INV_H, HALF), (1, HALF))


def branch_kept(branch):
    return [operand.get()[...] for operand in branch]


def grad_weights(pair, section):
    return [pair[0].get()[section], None, pair[1].get()[section]]


def rest_back_rows(kept, rows, section, norms, adapter, incoming, scratch, pairs, buffers, grad_refs, results, packing=None):
    summed_low, acc, second_low = scratch
    start_ref, mixed_ref = results
    gain = lambda i: norms[section, i : i + 1]
    parts = rows_of(rows, STEP_ROWS)
    weights = grad_weights(adapter, section)
    for part in parts:
        norm_kept = kept.normal_2.get()[part], kept.inverse_2.get()[part, :1]
        second = norm_back(incoming(part), norm_kept, gain(4))
        acc[part] = second
        second_low[part] = low(second)
    hidden_grad = branch_grads(second_low[:rows], branch_kept(kept.branch), weights, grad_refs)
    for part in parts:
        total = acc[part] + matmul_t(hidden_grad[part], weights[0])
        acc[part] = total
        summed_low[part] = low(total)
    if packing is not None:
        packing()
    slope = kept.slope.get()

    def turn(j, carry):
        for now in (2 * j, 2 * j + 1):
            wait_up(pairs, buffers, now)
            wait_down(pairs, buffers, now)
        for now in (2 * j, 2 * j + 1):
            for part in parts:
                inner = matmul_t(summed_low[part], buffers[2][now])
                inner = low(inner * slope[part, tile_columns(now)].astype(F32))
                acc[part] += matmul_t(inner, buffers[1][now])
        return carry

    lax.fori_loop(0, TILES // 2, turn, 0)
    wait_out(pairs, buffers)
    for part in parts:
        norm_kept = kept.normal_1.get()[part], kept.inverse_1.get()[part, :1]
        back = norm_back(acc[part], norm_kept, gain(2))
        start_ref[part] = back
        mixed_ref[part] = low(matmul_t(low(back), buffers[0][...]))


def backward_kernel(ins, scalars, pairs, packed):
    parts = ins.merged.shape[0]
    grads = [shape_of(*dims) for dims in COUPLING_GRADS]
    if packed:
        chunks = low_shape(COUPLING_GROUPS, PART_ROWS, LANES)
        adapters = [[shape_of(1, BOT), shape_of(1, D)] for _ in range(MICRO)] + [chunks, chunks]
    else:
        adapters = [[shape_of(*dims) for dims in ADAPTER_GRADS] for _ in range(MICRO)]
    outs = Back(shape_of(1, LANES), grads, grads, adapters, shape_of(SEQ, D), low_shape(SEQ, D))

    def body(ins, out, scalar_refs, pair_refs, raw_refs, scratch):
        length = scalar_refs[0][0]
        rest_scratch, spot, mixed_1, acc_1, section_grad = scratch[:3], *scratch[3:7]
        qkv_w, rest_w, refs = scratch[7:9], scratch[9:13], scratch[13:]
        qkv_pair, rest_pairs = pair_refs[0], pair_refs[1:]

        start(ins.merged, ins.row_weights, ins.weight_sum, ins.target_rows, ins.last, ins.norms)
        start(ins.coupling, ins.adapter, ins.rest_1)
        start_tiles(rest_pairs, 1, rest_w)
        start_out(rest_pairs, 1, rest_w)
        start_qkv(qkv_pair, 1, qkv_w)
        start(ins)
        norms = ins.norms.get()

        def from_head(part):
            merged = ins.merged.get()
            stats = merged[:, :, D:].astype(F32)
            highest = jnp.sum(stats[:, :, :3], 2, keepdims=True)
            totals = jnp.sum(stats[:, :, 3:6], 2, keepdims=True)
            top = jnp.max(highest, 0)
            factor = jnp.exp(highest - top[None])
            total = jnp.sum(totals * factor, 0)
            expected = jnp.zeros((COUNT, D), F32)
            for i in range(parts):
                expected += merged[i, :, :D].astype(F32) * (factor[i] / total)
            target = ins.target_rows.get()[...]
            target_logit = jnp.sum(ins.last.normed.get()[...].astype(F32) * target, 1, keepdims=True)
            weight = ins.row_weights.get()[...]
            row_losses = weight[:, :1] * (top + jnp.log(total) - target_logit)
            out.loss.buffer[...] = across(jnp.sum(row_losses, 0, keepdims=True))
            normed_grad = (weight / ins.weight_sum.get()[...])[:, :1] * (expected - target)
            kept = (ins.last.normal.get()[...], ins.last.inverse.get()[:, :1])
            restored = norm_back(normed_grad, kept, norms[1, 0:1])
            left, right = restored[:, :HALF], restored[:, HALF:]
            one, two = (grad_weights(ins.coupling, s) for s in range(MICRO))
            refs_of = lambda results: [result.buffer for result in results]
            hidden = branch_grads(low(-left), branch_kept(ins.last.one), one, refs_of(out.one))
            right = right + matmul_t(hidden, one[0])
            hidden = branch_grads(low(-right), branch_kept(ins.last.two), two, refs_of(out.two))
            left = left + matmul_t(hidden, two[0])
            return jnp.concatenate([left, right], 1)

        def grads_of(section):
            buffers = [result.buffer for result in out.adapters[section]]
            return (refs[0], buffers[0], refs[1], buffers[1]) if packed else buffers

        def pack_second():
            def store(part, chunk):
                refs[2][part] = chunk

            pack_adapter((refs[0], refs[1]), store)

        def pack_both():
            here = lax.axis_index("section") == 0
            own, other = out.adapters[2:]

            def store(part, chunk):
                arrived = refs[2][part]
                own.buffer[part] = jnp.where(here, chunk, arrived)
                other.buffer[part] = jnp.where(here, arrived, chunk)

            pack_adapter((refs[0], refs[1]), store)
            send(own, other)

        rest_back_rows(
            ins.rest_1, COUNT, 1, norms, ins.adapter, from_head, rest_scratch, rest_pairs, rest_w,
            grads_of(1), (spot, mixed_1), pack_second if packed else None,
        )
        start_tiles(rest_pairs, 0, rest_w)
        start_out(rest_pairs, 0, rest_w)

        acc_1[...] = jnp.zeros_like(acc_1)
        q_ref, k_ref, v_ref, lse_ref = (operand.get() for operand in ins.attention_1)

        def attend_back(group, carry):
            columns = group_columns(group)
            stack = lambda values: jnp.concatenate([only_head(values, h) for h in range(HEADS_IN)], 0)
            query = stack(scaled_query(q_ref[:, columns]))
            mixed = stack(mixed_1[:, columns])
            key, value = k_ref[:, columns], v_ref[:, columns]
            scores = matmul_t(query, key) + key_bias(length, (1, SEQ), 1)
            soft = jnp.exp(scores - lse_ref[group][:, :1])
            soft_grad = matmul_t(mixed, value)
            delta = jnp.sum(soft_grad * soft, 1, keepdims=True)
            score_grad = low(soft * (soft_grad - delta))
            every = matmul(score_grad, key)
            query_grad = every[:COUNT]
            for head in range(1, HEADS_IN):
                query_grad = jnp.where(
                    head_mask(query_grad, head), every[head * COUNT : (head + 1) * COUNT], query_grad
                )
            query_grad = low(query_grad * HEAD_DIM**-0.5)
            key_grad = low(inner_rows(score_grad, query))
            value_grad = low(inner_rows(low(soft), mixed))
            for part in range(3):
                wait_qkv(qkv_pair, qkv_w, group, part)
            spot[...] += matmul_t(query_grad, qkv_w[0][group, 0])
            acc_1[...] += matmul_t(key_grad, qkv_w[0][group, 1]) + matmul_t(value_grad, qkv_w[0][group, 2])
            return carry

        lax.fori_loop(0, GROUPS, attend_back, 0)
        placed = jnp.dot(ins.chosen_t.get()[...], spot[...], precision=HIGHEST, preferred_element_type=F32)
        section_grad[...] = low(acc_1[...] + placed)

        rest_back_rows(
            ins.rest_0, SEQ, 0, norms, ins.adapter, lambda part: section_grad[part].astype(F32),
            rest_scratch, rest_pairs, rest_w, grads_of(0), (out.start.buffer, out.mixed.buffer),
            pack_both if packed else None,
        )

    scratch = [pltpu.VMEM((SEQ, D), BF16), pltpu.VMEM((SEQ, D), F32), pltpu.VMEM((SEQ, D), BF16)]
    scratch += [pltpu.VMEM((COUNT, D), F32), pltpu.VMEM((COUNT, D), BF16), pltpu.VMEM((SEQ, D), F32)]
    scratch += [pltpu.VMEM((SEQ, D), BF16)] + qkv_buffers() + rest_buffers()
    if packed:
        scratch += [pltpu.VMEM((D, BOT), F32), pltpu.VMEM((BOT, D), F32)]
        scratch += [pltpu.VMEM((COUPLING_GROUPS, PART_ROWS, LANES), BF16)]
    return moved_call(body, scalars, ins, outs, pairs, scratch, "backward")[0]


def first_backward(ins, scalars, pairs, packed):
    if packed:
        dims = (COUPLING_GROUPS, GROUP_ROWS + 8, LANES)
        outs = (shape_of(*dims), low_shape(*dims))
    else:
        outs = [shape_of(*dims) for dims in COUPLING_GRADS * 2]

    def body(ins, out, scalar_refs, pair_refs, raw_refs, scratch):
        length = scalar_refs[0][0]
        s_even, s_odd, d_even, d_odd, p_even, p_odd, ds_even, ds_odd = scratch[:8]
        qkv_w, (key_grad, value_grad, query_grad_t), refs = scratch[8:10], scratch[10:13], scratch[13:]
        start(ins.attention, ins.mixed)
        start_qkv(pair_refs[0], 0, qkv_w)
        start(ins)
        q_ref, k_ref, v_ref, lse_ref = (operand.get() for operand in ins.attention)
        mixed_ref, acc = ins.mixed.get(), ins.start.get()

        def attend_back(group, carry):
            columns = group_columns(group)
            query = scaled_query(q_ref[:, columns])
            key, value, mixed = k_ref[:, columns], v_ref[:, columns], mixed_ref[:, columns]
            lse_rows = lse_ref[group]
            key_t = jnp.transpose(key)
            buffers = ((s_even, d_even, p_even, ds_even), (s_odd, d_odd, p_odd, ds_odd)) * 2

            def product_steps(head):
                def scores():
                    buffers[head][0][...] = matmul_t(only_head(key, head), query)

                def soft_grads():
                    buffers[head][1][...] = matmul_t(only_head(value, head), mixed)

                return [scores, soft_grads] if head < HEADS_IN else []

            def soft_steps(head):
                s_buf, d_buf, p_low, ds_low = buffers[head]
                delta = [jnp.zeros((8, SEQ), F32)]

                def soft_step(rows):
                    valid = lax.broadcasted_iota(jnp.int32, (SMALL_ROWS, 1), 0) + rows.start < length
                    bias = jnp.where(valid, 0.0, -1e30)
                    soft = jnp.exp(s_buf[rows] + bias - lse_rows[head : head + 1])
                    s_buf[rows] = soft
                    p_low[rows] = low(soft)
                    product = soft * d_buf[rows]
                    for at in range(0, SMALL_ROWS, 8):
                        delta[0] = delta[0] + product[at : at + 8]

                def sum_step():
                    delta[0] = jnp.sum(delta[0], 0, keepdims=True)

                def grad_step(rows):
                    ds_low[rows] = low(s_buf[rows] * (d_buf[rows] - delta[0]))

                parts = rows_of(SEQ, SMALL_ROWS)
                steps = [functools.partial(soft_step, rows) for rows in parts] + [sum_step]
                return steps + [functools.partial(grad_step, rows) for rows in parts]

            def grad_steps(head):
                _, _, p_low, ds_low = buffers[max(head, 0)]

                def add(ref, grad):
                    ref[...] = grad if head == 0 else ref[...] + grad

                def value_step():
                    add(value_grad, matmul(p_low[...], only_head(mixed, head)))

                def key_step():
                    add(key_grad, matmul(ds_low[...], only_head(query, head)))

                def query_step():
                    rows = slice(head * HEAD_DIM, (head + 1) * HEAD_DIM)
                    query_grad_t[rows] = matmul(key_t[rows], ds_low[...])

                return [value_step, key_step, query_step] if head >= 0 else []

            alternate(product_steps(0))
            for head in range(HEADS_IN):
                alternate(soft_steps(head), product_steps(head + 1) + grad_steps(head - 1))
            alternate(grad_steps(HEADS_IN - 1))
            query_grad = jnp.transpose(query_grad_t[...]) * HEAD_DIM**-0.5
            for part, grad in enumerate((query_grad, key_grad[...], value_grad[...])):
                wait_qkv(pair_refs[0], qkv_w, group, part)
                acc[...] += matmul_t(low(grad), qkv_w[0][group, part])
            return carry

        lax.fori_loop(0, GROUPS, attend_back, 0)
        one, two = (grad_weights(ins.coupling, s) for s in range(MICRO))
        grads = refs if packed else [result.buffer for result in out]
        hidden = branch_grads(low(acc[:, HALF:]), branch_kept(ins.two), two, grads[4:])
        left = acc[:, :HALF] + matmul_t(hidden, two[0])
        branch_grads(low(left), branch_kept(ins.one), one, grads[:4])
        for ref, operand in zip(grads, (*ins.grads_one, *ins.grads_two)):
            ref[...] += operand.get()[...]
        if not packed:
            return
        here = lax.axis_index("section")
        for s in range(MICRO):
            some = grads[4 * s : 4 * s + 4]
            biases = [operand.get()[...] for operand in ins.biases[s]]
            tiles = bias_tiles(*biases, some[1][...], some[3][...])

            def store(part, chunk, s=s):
                @pl.when(here == s)
                def _():
                    out[0].buffer[part] = chunk

                @pl.when(here != s)
                def _():
                    out[1].buffer[part] = low(chunk)

            pack_coupling((some[0], some[2]), tiles, sum(BIASES) // COUPLING_GROUPS, store)

    scratch = [pltpu.VMEM((SEQ, SEQ), F32)] * 4 + [pltpu.VMEM((SEQ, SEQ), BF16)] * 4 + qkv_buffers()
    scratch += [pltpu.VMEM((SEQ, GROUP), F32)] * 2 + [pltpu.VMEM((GROUP, SEQ), F32)]
    if packed:
        scratch += [pltpu.VMEM(dims, F32) for dims in COUPLING_GRADS * 2]
    return moved_call(body, scalars, ins, outs, pairs[:1], scratch, "first_backward")[0]


VOCAB_TILE = 1280


def head_stats(top, total):
    lane = lax.broadcasted_iota(jnp.int32, (top.shape[0], LANES), 1)
    stats = jnp.zeros(lane.shape, F32)
    for j, piece in enumerate(three_low(top) + three_low(total)):
        stats = jnp.where(lane == j, piece.astype(F32), stats)
    return low(stats)


def head_kernel(rows, table):
    lines, planes, each, _ = rows.shape
    parts = lines * planes
    count, vocab = parts * each, table.shape[0]
    tiles = pl.cdiv(vocab, VOCAB_TILE)
    if vocab < VOCAB_TILE or (vocab - VOCAB_TILE) % 16 or tiles % 2:
        return blocked_head_kernel(rows.reshape(parts, each, D), table)
    starts = [min(tile * VOCAB_TILE, vocab - VOCAB_TILE) for tile in range(tiles)]

    def kernel(x_hbm, table_hbm, out_hbm, *refs):
        x_ref, out_ref, entries, acc, top, total, factor_even, factor_odd = refs[:8]
        l_even, l_odd, p_even, p_odd, sems, out_sems = refs[8:]
        fetch = pltpu.make_async_copy(x_hbm, x_ref, sems.at[tiles])
        fetch.start()
        for tile, at in enumerate(starts):
            window = table_hbm.at[pl.ds(at, VOCAB_TILE)]
            pltpu.make_async_copy(window, entries.at[tile], sems.at[tile]).start()

        def wait_tile(tile):
            window = table_hbm.at[pl.ds(0, VOCAB_TILE)]
            pltpu.make_async_copy(window, entries.at[tile], sems.at[tile]).wait()

        def logit_steps(l_ref, tile):
            def step(columns):
                l_ref[:, columns] = matmul_t(x_ref[...], entries[tile, columns])

            return [functools.partial(step, columns) for columns in rows_of(VOCAB_TILE, GROUP)]

        def soft_steps(l_ref, p_ref, factor_ref, tile):
            start = jnp.minimum(tile * VOCAB_TILE, vocab - VOCAB_TILE)
            lane = lax.broadcasted_iota(jnp.int32, (1, VOCAB_TILE), 1)
            bias = jnp.where(lane + start >= tile * VOCAB_TILE, 0.0, -1e30)

            def step(at):
                logits = l_ref[at] + bias
                earlier = top[at]
                highest = jnp.maximum(earlier, jnp.max(logits, 1, keepdims=True))
                exponent = jnp.exp(logits - highest)
                factor = jnp.exp(earlier - highest)
                top[at] = highest
                total[at] = total[at] * factor + jnp.sum(exponent, 1, keepdims=True)
                p_ref[at] = low(exponent)
                factor_ref[at] = across(factor)

            return [functools.partial(step, at) for at in rows_of(count, SMALL_ROWS)]

        def sum_steps(p_ref, factor_ref, tile):
            def step(columns):
                factor = factor_ref[...]
                factor = jnp.concatenate([factor, factor], 1)
                acc[:, columns] = acc[:, columns] * factor + matmul(p_ref[...], entries[tile, :, columns])

            return [functools.partial(step, columns) for columns in rows_of(D, GROUP)]

        acc[...] = jnp.zeros_like(acc)
        top[...] = jnp.full_like(top, -1e30)
        total[...] = jnp.zeros_like(total)
        p_odd[...] = jnp.zeros_like(p_odd)
        factor_odd[...] = jnp.ones_like(factor_odd)
        fetch.wait()
        wait_tile(0)
        alternate(logit_steps(l_even, 0))

        def turn(j, carry):
            even, odd = 2 * j, 2 * j + 1
            before, after = jnp.maximum(even - 1, 0), jnp.minimum(even + 2, tiles - 1)
            wait_tile(odd)

            @pl.when(even + 2 < tiles)
            def _():
                wait_tile(even + 2)

            alternate(
                soft_steps(l_even, p_even, factor_even, even),
                sum_steps(p_odd, factor_odd, before) + logit_steps(l_odd, odd),
            )
            alternate(
                soft_steps(l_odd, p_odd, factor_odd, odd),
                sum_steps(p_even, factor_even, even) + logit_steps(l_even, after),
            )
            return carry

        lax.fori_loop(0, tiles // 2, turn, 0)
        alternate(sum_steps(p_odd, factor_odd, tiles - 1))
        out_ref[:, :D] = low(acc[...])
        out_ref[:, D:] = head_stats(top[...], total[...])
        copies = []
        for i in range(parts):
            line, plane = divmod(i, planes)
            source = out_ref.at[i * each : (i + 1) * each]
            copies.append(pltpu.make_async_copy(source, out_hbm.at[plane * lines + line], out_sems.at[i]))
            copies[-1].start()
        for copy in copies:
            copy.wait()

    hbm = pl.BlockSpec(memory_space=pltpu.HBM)
    return pl.pallas_call(
        kernel,
        in_specs=[hbm, hbm],
        out_specs=hbm,
        out_shape=low_shape(parts, each, D + LANES),
        scratch_shapes=[
            pltpu.VMEM((count, D), BF16),
            pltpu.VMEM((count, D + LANES), BF16),
            pltpu.VMEM((tiles, VOCAB_TILE, D), BF16),
            pltpu.VMEM((count, D), F32),
            pltpu.VMEM((count, 1), F32),
            pltpu.VMEM((count, 1), F32),
        ]
        + [pltpu.VMEM((count, LANES), F32)] * 2
        + [pltpu.VMEM((count, VOCAB_TILE), F32)] * 2
        + [pltpu.VMEM((count, VOCAB_TILE), BF16)] * 2
        + [pltpu.SemaphoreType.DMA((tiles + 1,)), pltpu.SemaphoreType.DMA((parts,))],
        compiler_params=params_for(MOST_VMEM),
        name="vocabulary_head",
    )(rows.reshape(count, D), table)


def blocked_head_kernel(rows, table):
    parts_in, each, _ = rows.shape
    count, vocab = parts_in * each, table.shape[0]
    last = pl.cdiv(vocab, VOCAB_TILE) - 1
    turns = last // 2 + 1

    def kernel(x_hbm, even_ref, odd_ref, after_ref, out_hbm, *refs):
        x_ref, out_ref, acc, top, total, l_even, l_odd, p_even, p_odd, sems = refs
        turn = pl.program_id(0)

        def entries_of(ref, tile):
            row = lax.broadcasted_iota(jnp.int32, (VOCAB_TILE, 1), 0)
            return jnp.where(row < vocab - tile * VOCAB_TILE, ref[...], jnp.zeros_like(ref))

        @pl.when(turn == 0)
        def _():
            copy = pltpu.make_async_copy(x_hbm, x_ref, sems.at[0])
            copy.start()
            acc[...] = jnp.zeros_like(acc)
            top[...] = jnp.full_like(top, -1e30)
            total[...] = jnp.zeros_like(total)
            entries = entries_of(even_ref, 0)
            copy.wait()
            l_even[...] = matmul_t(x_ref[...], entries)

        even = entries_of(even_ref, 2 * turn)
        odd = entries_of(odd_ref, 2 * turn + 1)
        after = entries_of(after_ref, 2 * turn + 2)
        for tile, l_now, p_now, now, l_later, later in (
            (2 * turn, l_even, p_even, even, l_odd, odd),
            (2 * turn + 1, l_odd, p_odd, odd, l_even, after),
        ):
            bias = key_bias(vocab - tile * VOCAB_TILE, (1, VOCAB_TILE), 1)
            for at in rows_of(count, SMALL_ROWS):
                logits = l_now[at] + bias
                earlier = top[at]
                highest = jnp.maximum(earlier, jnp.max(logits, 1, keepdims=True))
                exponent = jnp.exp(logits - highest)
                factor = jnp.exp(earlier - highest)
                top[at] = highest
                total[at] = total[at] * factor + jnp.sum(exponent, 1, keepdims=True)
                p_now[at] = low(exponent)
                acc[at] = acc[at] * factor
            l_later[...] = matmul_t(x_ref[...], later)
            acc[...] += matmul(p_now[...], now)

        @pl.when(turn == turns - 1)
        def _():
            out_ref[:, :D] = low(acc[...])
            out_ref[:, D:] = head_stats(top[...], total[...])
            copy = pltpu.make_async_copy(out_ref, out_hbm, sems.at[1])
            copy.start()
            copy.wait()

    def tile_at(shift):
        return pl.BlockSpec((VOCAB_TILE, D), lambda j: (jnp.minimum(2 * j + shift, last), 0))

    hbm = pl.BlockSpec(memory_space=pltpu.HBM)
    return pl.pallas_call(
        kernel,
        grid=(turns,),
        in_specs=[hbm] + [tile_at(shift) for shift in range(3)],
        out_specs=hbm,
        out_shape=shape_of(count, D + LANES, kind=BF16),
        scratch_shapes=[
            pltpu.VMEM((count, D), BF16),
            pltpu.VMEM((count, D + LANES), BF16),
            pltpu.VMEM((count, D), F32),
            pltpu.VMEM((count, 1), F32),
            pltpu.VMEM((count, 1), F32),
            pltpu.VMEM((count, VOCAB_TILE), F32),
            pltpu.VMEM((count, VOCAB_TILE), F32),
            pltpu.VMEM((count, VOCAB_TILE), BF16),
            pltpu.VMEM((count, VOCAB_TILE), BF16),
            pltpu.SemaphoreType.DMA((2,)),
        ],
        compiler_params=params_for(MOST_VMEM),
        name="vocabulary_head",
    )(rows.reshape(count, D), table, table, table).reshape(parts_in, each, D + LANES)


def swap_add(own, other):
    came = lax.ppermute(low(other), "section", [(0, 1), (1, 0)])
    return own + came.astype(F32)


def pick(first_section, both):
    return jnp.where(first_section, both[0], both[1])


def plan_requests(ids, weights, vocab_rows, slots, parts):
    turned = jnp.transpose(ids)

    def kernel(ids_ref, turned_ref, weights_ref, asked_ref, code_ref, spot_ref):
        here = lax.axis_index("section")
        i_index = lax.broadcasted_iota(jnp.int32, (IDS, IDS), 0)
        j_index = lax.broadcasted_iota(jnp.int32, (IDS, IDS), 1)
        earlier, later = j_index < i_index, i_index < j_index

        def owner_of(values):
            return jnp.floor((values.astype(F32) + 0.5) * (1.0 / vocab_rows)).astype(jnp.int32)

        def count(hits, axis):
            return jnp.sum(hits.astype(F32), axis, keepdims=True)

        most = jnp.zeros((1, 1), F32)
        for m in range(MICRO):
            row, col = ids_ref[m : m + 1], turned_ref[:, m : m + 1]
            same_id = row == col
            first_col = count(same_id & earlier, 1) == 0
            first_row = count(same_id & later, 0) == 0
            owner_row, owner_col = owner_of(row), owner_of(col)
            same_owner = owner_row == owner_col
            rank_row = count(same_owner & later & first_col, 0)
            rank_col = count(same_owner & earlier & first_row, 1)
            most = jnp.maximum(most, jnp.max(rank_row, 1, keepdims=True))

            @pl.when(here == m)
            def _():
                slot_row = jnp.sum(jnp.where(same_id & first_col, rank_col, 0.0), 0, keepdims=True)
                slot_col = jnp.sum(jnp.where(same_id & first_row, rank_row, 0.0), 1, keepdims=True)
                slot_row, slot_col = slot_row.astype(jnp.int32), slot_col.astype(jnp.int32)
                code_ref[...] = (owner_row + parts * first_row.astype(jnp.int32)) * 1024 + slot_row
                spot = jnp.where(slot_col < slots, owner_col * slots + slot_col, -1)
                spot_ref[...] = jnp.broadcast_to(spot, (IDS, LANES))
                lane = lax.broadcasted_iota(jnp.int32, (IDS, LANES), 1)
                local = (col - owner_col * vocab_rows).astype(F32)
                wanted = first_col & (slot_col < slots) & (slot_col == lane)
                wanted = jnp.where(wanted, local, 0.0)
                for part in range(parts):
                    asked = jnp.sum(jnp.where(owner_col == part, wanted, 0.0), 0, keepdims=True)
                    asked_ref[part] = asked.astype(jnp.int32)

        rounds = jnp.floor((most + 0.5) * (1.0 / slots)).astype(jnp.int32) + 1
        total = jnp.sum(jnp.sum(weights_ref[...], 0, keepdims=True), 1, keepdims=True)
        lane = lax.broadcasted_iota(jnp.int32, (1, LANES), 1)
        for part in range(parts):
            row = asked_ref[part]
            asked_ref[part] = jnp.where(lane == slots, rounds, jnp.where(lane == slots + 1, total, row))

    return pl.pallas_call(
        kernel,
        out_shape=[
            jax.ShapeDtypeStruct((parts, 1, LANES), jnp.int32),
            jax.ShapeDtypeStruct((1, IDS), jnp.int32),
            jax.ShapeDtypeStruct((IDS, LANES), jnp.int32),
        ],
        compiler_params=params_for(24),
        name="plan_requests",
    )(ids, turned, weights)


def fetch_rows(table, ids, first_section, plan, slots):
    parts = lax.axis_size("dp")
    vocab_rows = table.shape[0]
    asked, code, spot = plan
    asked = lax.all_to_all(asked, "dp", 0, 0)[:, 0]
    total_rounds = jnp.max(asked[:, slots])
    weight_sum = jnp.sum(asked[:, slots + 1])

    def answer(asked):
        rows = table.at[asked.reshape(-1)].get(mode="promise_in_bounds").reshape(parts, slots, D)
        return lax.all_to_all(rows, "dp", 0, 0).reshape(parts * slots, D)

    came = answer(asked[:, :slots])

    def more(state):
        return state[0] < total_rounds

    def another(state):
        turn, extra = state
        place, slot = code[0] // 1024, code[0] % 1024
        owner, first = place % parts, place >= parts
        local = pick(first_section, ids) - owner * vocab_rows
        here = slot - turn * slots
        at = jnp.where((here >= 0) & (here < slots), owner * slots + here, -1)
        hits = at[:, None] == jnp.arange(parts * slots)[None, :]
        wanted = jnp.sum(jnp.where(hits & first[:, None], local[:, None], 0), 0).reshape(parts, slots)
        rows = answer(lax.all_to_all(wanted, "dp", 0, 0))
        return turn + 1, extra + matmul(hits.astype(BF16), rows)

    extra = lax.while_loop(more, another, (jnp.int32(1), jnp.zeros((IDS, D), F32)))[1]
    return came, spot, extra, total_rounds, weight_sum.astype(F32)


def three_low(values):
    high = low(values)
    rest = values - high.astype(F32)
    middle = low(rest)
    return [high, middle, low(rest - middle.astype(F32))]


def spread_rows(copies):
    parts = lax.axis_size("dp")
    if copies.shape[0] == parts:
        return lax.all_to_all(copies, "dp", 0, 0)[None]
    across_planes, in_plane = plane_groups(parts)
    some = lax.all_to_all(copies, "dp", 0, 0, axis_index_groups=across_planes)
    some = jnp.broadcast_to(some[None], (LINES, *some.shape))
    return lax.all_to_all(some, "dp", 0, 0, axis_index_groups=in_plane)


def in_groups(count):
    return lax.axis_size("dp") == COUPLING_GROUPS and count == 4 * PART_GROUPS


LINES = 4


def plane_groups(parts):
    planes = parts // LINES
    across_planes = [[plane * LINES + line for plane in range(planes)] for line in range(LINES)]
    return across_planes, [[plane * LINES + line for line in range(LINES)] for plane in range(planes)]


def gather_params(master, vector, after):
    parts = lax.axis_size("dp")
    count, width = master.shape[0], vector.shape[0]
    if in_groups(count):
        across_planes, in_plane = plane_groups(parts)
        some = pack_own(master, vector[None], len(in_plane))
        some = lax.all_to_all(some, "dp", 0, 0, axis_index_groups=across_planes)
        some, after = lax.optimization_barrier((some, after))
        own = lax.all_gather(some, "dp", axis_index_groups=in_plane)
        return *unpack_all(own, lax.ppermute(own, "section", [(0, 1), (1, 0)]), width), after
    flat = low(jnp.concatenate([master.reshape(-1), vector]))
    gathered = lax.all_gather(flat, ("section", "dp")).reshape(MICRO, parts, -1)
    size = count * BLOCK**2
    all_blocks = gathered[:, :, :size].reshape(MICRO, parts * count, BLOCK, BLOCK)
    all_vectors = gathered[:, :, size:].reshape(MICRO, parts * width)
    both = [split_params(all_blocks[s], all_vectors[s]) for s in range(MICRO)]

    def stacked(which):
        down, bias_down, up, bias_up = (jnp.stack([pair[which][i] for pair in both]) for i in range(4))
        return Params(down, bias_down.astype(F32)[:, None], up, bias_up.astype(F32)[:, None])

    return stacked(0), stacked(1), after


def sum_at_owners(grads, loss_part, count):
    parts = lax.axis_size("dp")
    width = sum(BIASES) // parts
    flat = []
    for adapter, coupling in grads:
        blocks, vector = join_params(adapter, coupling)
        flat.append(
            jnp.concatenate([blocks.reshape(parts, count * BLOCK**2), vector.reshape(parts, width)], 1)
        )
    first = lax.axis_index("section") == 0
    summed = swap_add(jnp.where(first, flat[0], flat[1]), jnp.where(first, flat[1], flat[0]))
    owned = jnp.sum(lax.all_to_all(low(summed), "dp", 0, 0).astype(F32), 0)
    blocks = owned[: count * BLOCK**2].reshape(count, BLOCK, BLOCK)
    pair = jnp.stack([jnp.sum(owned * owned), loss_part[0, 0]])
    pair = jnp.pad(pair, (0, LANES - 2))[None, None]
    return blocks, owned[count * BLOCK**2 :], jnp.broadcast_to(pair, (parts * MICRO, 8, LANES))


def to_coupling_owners(group):
    arrived = []
    for place in range(PART_GROUPS):
        route = []
        for part in range(COUPLING_GROUPS):
            owner, at = divmod(ADAPTER_GROUPS + part, PART_GROUPS)
            if at == place:
                route.append((part, owner))
        arrived.append(lax.ppermute(group, "dp", route))
    return arrived


def exact(spec, left, right):
    return jnp.einsum(spec, left, right, precision=HIGHEST)


def update(pair, products, turned_old, grad_vector, state):
    master, momentum, stat_left, stat_right, vectors, vec_first, vec_second = state
    grad, left_square, right_square, turned = products

    blocks = (1,) + grad.shape
    outs = [shape_of(*blocks)] * 5 + [low_shape(*blocks)] + [shape_of(*vectors.shape)] * 3 + [shape_of(1, 1)] * 2

    def body(ins, out, scalar_refs, pair_refs, raw_refs, scratch):
        start(ins)
        (pair_ref, grad_ref, left_ref, right_ref, turned_ref, vector_ref, old_ref), ins = (
            [operand.get() for operand in ins[:7]],
            [operand.get() for operand in ins[7:]],
        )
        master_ref, momentum_ref, stat_left_ref, stat_right_ref, vectors_ref, first_ref, second_ref = ins
        outs = [result.buffer for result in out]
        totals = jnp.sum(pair_ref[...], 0)[:1]
        norm = jnp.sqrt(totals[:, :1])
        factor = CLIP_NORM / jnp.maximum(norm, CLIP_NORM)
        outs[9][...] = norm
        outs[10][...] = totals[:, 1:2]
        square = (1.0 - STAT_DECAY) * factor * factor
        for n in range(grad_ref.shape[0]):
            clipped = grad_ref[n] * factor
            outs[0][0, n] = clipped
            outs[1][0, n] = FIRST_DECAY * momentum_ref[n] + (1.0 - FIRST_DECAY) * clipped
            outs[2][0, n] = STAT_DECAY * stat_left_ref[n] + square * left_ref[n]
            outs[3][0, n] = STAT_DECAY * stat_right_ref[n] + square * right_ref[n]
            direction = FIRST_DECAY * old_ref[n] + (1.0 - FIRST_DECAY) * factor * turned_ref[n]
            master_new = master_ref[n] - MAT_RATE * (direction + MAT_DECAY * master_ref[n])
            outs[4][0, n] = master_new
            outs[5][0, n] = low(master_new)
        clipped = vector_ref[...] * factor
        first_new = FIRST_DECAY * first_ref[...] + (1.0 - FIRST_DECAY) * clipped
        second_new = VEC_SECOND * second_ref[...] + (1.0 - VEC_SECOND) * clipped * clipped
        outs[6][...] = first_new
        outs[7][...] = second_new
        corrected_first = first_new / (1.0 - FIRST_DECAY**STEP)
        corrected_second = second_new / (1.0 - VEC_SECOND**STEP)
        outs[8][...] = vectors_ref[...] - VEC_RATE * (
            corrected_first / (jnp.sqrt(corrected_second) + VEC_EPS) + VEC_DECAY * vectors_ref[...]
        )

    ins = [pair, grad, left_square, right_square, turned, grad_vector, turned_old]
    ins += [master, momentum, stat_left, stat_right, vectors, vec_first, vec_second]
    return moved_call(body, (), ins, outs, (), [], "update")[0]


def shards(
    token_ids,
    lengths,
    positions,
    targets,
    loss_weights,
    embed_table,
    pos_table,
    norm_params,
    base_qkv,
    base_out,
    base_up,
    base_down,
    master,
    momentum,
    stat_left,
    stat_right,
    root_left,
    root_right,
    vectors,
    vec_first,
    vec_second,
):
    parts = lax.axis_size("dp")
    first_section = lax.axis_index("section") == 0
    slots = -(-IDS * 5 // (4 * parts * 16)) * 16

    ids = jnp.concatenate([token_ids[:, 0], targets[:, 0]], -1)
    asked, *plan = plan_requests(ids, loss_weights[:, 0], embed_table.shape[0], slots, parts)
    adapter, coupling, asked = gather_params(master[0], vectors[0], asked)
    swap = [(0, 1), (1, 0)]
    pairs = [(w, lax.ppermute(w, "section", swap)) for w in (base_qkv, base_out, base_up, base_down)]
    came = lax.ppermute(norm_params, "section", swap)
    norms = jnp.concatenate([pick(first_section, (norm_params, came)), pick(first_section, (came, norm_params))])

    came, spot, extra, rounds, weight_sum = fetch_rows(embed_table, ids, first_section, (asked, *plan), slots)
    turned_old = exact("nij,njk->nik", exact("nij,njk->nik", root_left[0], momentum[0]), root_right[0])
    spot, turned_old = lax.optimization_barrier((spot, turned_old))
    length = pick(first_section, lengths)
    spots = pick(first_section, positions[:, 0])
    row_weights = pick(first_section, loss_weights[:, 0]).astype(F32)
    chosen = (spots[:, None] == jnp.arange(SEQ)[None, :]).astype(BF16)
    chosen_t = (spots[None, :] == jnp.arange(SEQ)[:, None]).astype(F32)

    ins = ForwardIn(came, spot, extra, pos_table, norms, chosen, adapter, coupling)
    kept, rows = forward_kernel(ins, (length, rounds.reshape(1)), pairs, parts, slots)

    merged = lax.all_to_all(head_kernel(spread_rows(rows), embed_table), "dp", 0, 0)

    packed = in_groups(master.shape[1])
    row_weights = jnp.broadcast_to(row_weights[:, None], (COUNT, LANES))
    weight_row = jnp.broadcast_to(weight_sum, (1, LANES))
    adapter, coupling = adapter[::2], coupling[::2]
    ins = BackIn(
        merged, row_weights, weight_row, norms, chosen_t, adapter, coupling,
        kept.target_rows, kept.rest_0, kept.attention_1, kept.rest_1, kept.last,
    )
    back = backward_kernel(ins, (length,), pairs, packed)
    loss_part, mixed_grad = back.loss, back.mixed
    if packed:
        own, other = back.adapters[MICRO:]
        summed = low(swap_add(own.astype(F32), other))
        summed, mixed_grad = lax.optimization_barrier((summed, mixed_grad))
        adapter_came = lax.all_to_all(summed, "dp", 0, 0)
    ins = FirstIn(
        kept.attention_0, mixed_grad, back.start, coupling, kept.one, kept.two, back.one, back.two,
        back.adapters[:MICRO] if packed else (),
    )
    grads = first_backward(ins, (length,), pairs, packed)
    if packed:
        adapter_total, squares = sum_adapter(adapter_came)
        came = lax.all_to_all(low(swap_add(*grads)), "dp", 0, 0)
        group, bias, pair = sum_coupling(came, squares, loss_part, parts * MICRO)
        products = grad_products(adapter_total, to_coupling_owners(group), root_left[0], root_right[0])
        grad_vector = bias[:1, : vectors.shape[1]]
    else:
        both = [(back.adapters[s], grads[4 * s : 4 * s + 4]) for s in range(MICRO)]
        grad, grad_vector, pair = sum_at_owners(both, loss_part, master.shape[1])
        turned = exact("nij,njk->nik", exact("nij,njk->nik", root_left[0], grad), root_right[0])
        products = grad, exact("nij,nkj->nik", grad, grad), exact("nji,njk->nik", grad, grad), turned
        grad_vector = grad_vector[None]
    pair = lax.all_to_all(pair, ("dp", "section"), 0, 0)
    state = (master, momentum, stat_left, stat_right)
    *outs, grad_norm, loss_sum = update(
        pair, products, turned_old, grad_vector, [value[0] for value in state] + [vectors, vec_first, vec_second]
    )
    return (*outs, grad_norm[0, 0], loss_sum[0, 0], weight_sum)


def solution(mesh):
    rows = P(None, "dp", None)
    section = P("section", None, None)
    blocks = P("section", "dp", None, None)
    biases = P("section", "dp")
    return jax.shard_map(
        shards,
        mesh=mesh,
        in_specs=(rows, P(None, "dp"), rows, rows, rows, P("dp", None), P())
        + (section,) * 5
        + (blocks,) * 6
        + (biases,) * 3,
        out_specs=(blocks,) * 6 + (biases,) * 3 + (P(),) * 3,
        check_vma=False,
    )
```

```python
import functools
from typing import Any, NamedTuple

import jax
import jax.numpy as jnp
import numpy as np
from jax import lax
from jax.experimental import pallas as pl
from jax.experimental.pallas import tpu as pltpu
from jax.sharding import PartitionSpec as P

D = 768
HEADS = 12
HEAD_DIM = 64
BOT = 384
INV_H = 192
SEQ = 512
COUNT = 32
MICRO = 2
BLOCK = 48
STEP = 10
HALF = 384
IDS = SEQ + COUNT

HIGHEST = lax.Precision.HIGHEST
NORM_EPS = 1e-12
CLIP_NORM = 0.02
FIRST_DECAY = 0.9
STAT_DECAY = 0.99
MAT_RATE = 0.1
MAT_DECAY = 0.01
VEC_RATE = 0.05
VEC_SECOND = 0.999
VEC_EPS = 1e-08
VEC_DECAY = 0.01
F32 = jnp.float32
BF16 = jnp.bfloat16

CDF_SCALE = 0.42 / 2.0**0.5
CDF_POLY = (
    0.2368242366796694,
    0.239585811361218,
    0.1947261443420679,
    0.2687426685879861,
    -0.13052645834187002,
    0.4406726942003943,
    -0.32025628294963193,
    0.07023101752398136,
)


def matmul(left, right):
    return jnp.dot(left, right, preferred_element_type=F32)


def matmul_t(left, right):
    return lax.dot_general(left, right, (((1,), (1,)), ((), ())), preferred_element_type=F32)


def inner_rows(left, right):
    return lax.dot_general(left, right, (((0,), (0,)), ((), ())), preferred_element_type=F32)


def low(values):
    return values.astype(BF16)


def gelu_both(values):
    below = 1.0 + CDF_SCALE * jnp.abs(values)
    ratio = pl.reciprocal(below, approx=True)
    ratio = ratio * (2.0 - below * ratio)
    poly = jnp.full_like(ratio, 0.5 * CDF_POLY[-1])
    for factor in CDF_POLY[-2::-1]:
        poly = poly * ratio + 0.5 * factor
    bell = jnp.exp(-0.5 * values * values)
    tail = bell * (poly * ratio)
    cdf = jnp.where(values < 0, tail, 1.0 - tail)
    return values * cdf, cdf + values * (bell * (2.0 * np.pi) ** -0.5)


def layer_norm(values, gain, shift):
    centered = values - jnp.mean(values, -1, keepdims=True)
    inverse = lax.rsqrt(jnp.mean(centered * centered, -1, keepdims=True) + NORM_EPS)
    normal = centered * inverse
    return normal * gain + shift, (normal, inverse)


def norm_back(incoming, kept, gain):
    normal, inverse = kept
    scaled = incoming * gain
    return inverse * (
        scaled
        - jnp.mean(scaled, -1, keepdims=True)
        - normal * jnp.mean(scaled * normal, -1, keepdims=True)
    )


def to_blocks(matrix):
    rows_in, cols_in = matrix.shape
    return (
        matrix.reshape(rows_in // BLOCK, BLOCK, cols_in // BLOCK, BLOCK)
        .transpose(0, 2, 1, 3)
        .reshape(-1, BLOCK, BLOCK)
    )


def from_blocks(blocks, rows_in, cols_in):
    return (
        blocks.reshape(rows_in // BLOCK, cols_in // BLOCK, BLOCK, BLOCK)
        .transpose(0, 2, 1, 3)
        .reshape(rows_in, cols_in)
    )


def split_params(blocks, vector):
    adapter_count = D * BOT // BLOCK**2
    half_count = HALF * INV_H // BLOCK**2
    split_at = 2 * adapter_count
    adapter = (
        from_blocks(blocks[:adapter_count], D, BOT),
        vector[:BOT],
        from_blocks(blocks[adapter_count:split_at], BOT, D),
        vector[BOT : BOT + D],
    )
    coupling = (
        from_blocks(blocks[split_at : split_at + half_count], HALF, INV_H),
        vector[BOT + D : BOT + D + INV_H],
        from_blocks(blocks[split_at + half_count :], INV_H, HALF),
        vector[BOT + D + INV_H :],
    )
    return adapter, coupling


def join_params(adapter, coupling):
    blocks = jnp.concatenate(
        [to_blocks(adapter[0]), to_blocks(adapter[2]), to_blocks(coupling[0]), to_blocks(coupling[2])]
    )
    return blocks, jnp.concatenate([adapter[1], adapter[3], coupling[1], coupling[3]], 1)[0]


GROUP_ROWS = 72
LANES = 128


def params_for(mebibytes):
    return pltpu.CompilerParams(vmem_limit_bytes=mebibytes * 2**20)


def roll(values, shift):
    return pltpu.roll(values, shift, 1)


def lane_of(values):
    return lax.broadcasted_iota(jnp.int32, values.shape, 1)


def fold_half(values, upper):
    top, bottom = values[:24], values[24:]
    if upper:
        return jnp.where(lane_of(top) < 64, roll(top, 64), bottom)
    return jnp.where(lane_of(top) < 64, top, roll(bottom, 64))


def unfold_half(values, upper):
    turned = roll(values, 64)
    return jnp.concatenate([turned, values] if upper else [values, turned], 0)


def join_pair(main_0, rest_0, main_1, rest_1):
    left = lane_of(main_0) < 64
    turned = roll(main_1, 64)
    return (
        main_0,
        jnp.where(left, unfold_half(rest_0, False), turned),
        jnp.where(left, turned, unfold_half(rest_1, True)),
    )


def cut_pair(tile_0, tile_1, tile_2):
    left = lane_of(tile_0) < 64
    return (
        (tile_0, fold_half(tile_1, False)),
        (jnp.where(left, roll(tile_1, 64), roll(tile_2, 64)), fold_half(tile_2, True)),
    )


def chunk_rows(own_blocks):
    return own_blocks // 4 * GROUP_ROWS + 8


def bias_row(tiles, part, width):
    at, shift = divmod(part * width, LANES)
    lane = lane_of(tiles[0])
    row = tiles[at]
    if shift:
        row = jnp.where(lane < LANES - shift, roll(row, LANES - shift), roll(tiles[at + 1], LANES - shift))
    return jnp.where(lane < width, row, 0.0)


def bias_tiles(first, second, third, fourth):
    cut = lambda values: [values[:, at : at + LANES] for at in range(0, values.shape[1], LANES)]
    zero = jnp.zeros((1, LANES), F32)
    left = lane_of(zero) < 64
    third_tail = jnp.concatenate([third[:, LANES:]] * 2, 1)
    turned = [roll(tile, 64) for tile in cut(fourth)]
    joints = [jnp.where(left, one, two) for one, two in zip([third_tail] + turned, turned + [zero])]
    return cut(first) + cut(second) + [third[:, :LANES]] + joints + [zero]


def tiles_of_rows(rows, width):
    tiles = []
    for tile in range(-(-len(rows) * width // LANES)):
        value = jnp.zeros((8, LANES), F32)
        lane = lane_of(value)
        for part, row in enumerate(rows):
            shift = part * width - tile * LANES
            if shift >= LANES or shift + width <= 0:
                continue
            turned = roll(row, shift % LANES) if shift % LANES else row
            value = jnp.where((lane >= shift) & (lane < shift + width), turned, value)
        tiles.append(value)
    return tiles


def pack_own(master, vector, copies):
    count, width = master.shape[0], vector.shape[1]

    def kernel(master_ref, bias_ref, out_ref):
        row = lax.broadcasted_iota(jnp.int32, (BLOCK, 256), 0)
        col = lax.broadcasted_iota(jnp.int32, (BLOCK, 256), 1)
        pieces = []
        for group in range(count // 4):
            wide = jnp.zeros((BLOCK, 256), F32)
            for j in range(4):
                wide += matmul(low(master_ref[4 * group + j]), (col == row + BLOCK * j).astype(BF16))
            pieces += [wide[:, :LANES], fold_half(wide[:, LANES:], False)]
        bias = jnp.concatenate([bias_ref[...], jnp.zeros((1, LANES - width), F32)], 1)
        pieces.append(jnp.concatenate([bias, jnp.zeros((7, LANES), F32)], 0))
        packed = low(jnp.concatenate(pieces, 0))
        for copy in range(copies):
            out_ref[copy] = packed

    return pl.pallas_call(
        kernel,
        out_shape=jax.ShapeDtypeStruct((copies, chunk_rows(count), LANES), BF16),
        name="pack_own",
    )(master, vector)


MATRICES = ((D, BOT), (BOT, D), (HALF, INV_H), (INV_H, HALF))
BIASES = (BOT, D, INV_H, HALF)


def unpack_all(own, came, width):
    lines, planes, rows, _ = own.shape
    parts = lines * planes
    per_part = (rows - 8) // GROUP_ROWS

    def kernel(own_hbm, came_hbm, *refs):
        out_hbm, in_bufs, out_refs, in_sems, out_sems = refs[:8], refs[8], refs[9:17], refs[17], refs[18]
        here = lax.axis_index("section")
        copies = [
            pltpu.make_async_copy(ref, in_bufs.at[at], in_sems.at[i])
            for i, (ref, at) in enumerate(((own_hbm, here), (came_hbm, 1 - here)))
        ]
        for copy in copies:
            copy.start()
        for copy in copies:
            copy.wait()

        def unpack(s, carry):
            cache = {}

            def group(index):
                part = index // per_part
                if part not in cache:
                    cache.clear()
                    cache[part] = in_bufs[s, part % lines, part // lines].astype(F32)
                base = index % per_part * GROUP_ROWS
                chunk = cache[part]
                return chunk[base : base + BLOCK], chunk[base + BLOCK : base + GROUP_ROWS]

            index = 0
            for (height, columns), out_ref in zip(MATRICES, out_refs):
                for top in range(0, height, BLOCK):
                    if columns == INV_H:
                        main, rest = group(index)
                        index += 1
                        out_ref[s, top : top + BLOCK, :LANES] = low(main)
                        out_ref[s, top : top + BLOCK, LANES:] = low(unfold_half(rest, False)[:, :64])
                        continue
                    for left in range(0, columns, HALF):
                        tiles = join_pair(*group(index), *group(index + 1))
                        index += 2
                        for j, tile in enumerate(tiles):
                            at = left + j * LANES
                            out_ref[s, top : top + BLOCK, at : at + LANES] = low(tile)
            tiles = tiles_of_rows(
                [in_bufs[s, part % lines, part // lines, rows - 16 :].astype(F32)[8:] for part in range(parts)], width
            )
            first, second, third, fourth = out_refs[4:]
            first[s] = jnp.concatenate(tiles[:3], 1)[:1]
            second[s] = jnp.concatenate(tiles[3:9], 1)[:1]
            third[s] = jnp.concatenate([tiles[9], tiles[10][:, :64]], 1)[:1]
            left = lane_of(tiles[0]) < 64
            turned = [roll(tile, 64) for tile in tiles[10:14]]
            fourth[s] = jnp.concatenate(
                [jnp.where(left, one, two) for one, two in zip(turned, turned[1:])], 1
            )[:1]
            return carry

        lax.fori_loop(0, MICRO, unpack, 0)
        copies = [
            pltpu.make_async_copy(buf, ref, out_sems.at[i]) for i, (buf, ref) in enumerate(zip(out_refs, out_hbm))
        ]
        for copy in copies:
            copy.start()
        for copy in copies:
            copy.wait()

    shapes = [((MICRO,) + shape, BF16) for shape in MATRICES] + [((MICRO, 1, size), F32) for size in BIASES]
    hbm = pl.BlockSpec(memory_space=pltpu.HBM)
    arrays = pl.pallas_call(
        kernel,
        in_specs=[hbm] * 2,
        out_specs=[hbm] * 8,
        out_shape=[jax.ShapeDtypeStruct(*shape) for shape in shapes],
        scratch_shapes=[pltpu.VMEM((MICRO, lines, planes, rows, LANES), BF16)]
        + [pltpu.VMEM(*shape) for shape in shapes]
        + [pltpu.SemaphoreType.DMA((2,)), pltpu.SemaphoreType.DMA((8,))],
        compiler_params=params_for(MOST_VMEM),
        name="unpack_all",
    )(own, came)
    down, up, c_down, c_up, bias_down, bias_up, c_bias_down, c_bias_up = arrays
    return Params(down, bias_down, up, bias_up), Params(c_down, c_bias_down, c_up, c_bias_up)


ADAPTER_GROUPS = 2 * D * BOT // BLOCK**2 // 4
COUPLING_GROUPS = 2 * HALF * INV_H // BLOCK**2 // 4
PART_GROUPS = (ADAPTER_GROUPS + COUPLING_GROUPS) // COUPLING_GROUPS
PART_ROWS = PART_GROUPS * GROUP_ROWS
SUMMED_AT = (12, 13, 1, 5, 9, 0, 14, 2, 6, 10, 4, 15, 3, 7, 11, 8)


def groups_of(refs, shapes):
    groups = []
    for ref, (height, width) in zip(refs, shapes):
        for top in range(0, height, BLOCK):
            band = slice(top, top + BLOCK)
            if width == INV_H:
                tail = ref[band, LANES:]
                groups.append((ref[band, :LANES], fold_half(jnp.concatenate([tail, tail], 1), False)))
                continue
            for left in range(0, width, HALF):
                groups += cut_pair(*[ref[band, left + j * LANES : left + (j + 1) * LANES] for j in range(3)])
    return [jnp.concatenate(group, 0) for group in groups]


def pack_adapter(refs, store):
    groups = groups_of(refs, MATRICES[:2])
    empty = jnp.zeros((GROUP_ROWS, LANES), F32)
    for part in range(COUPLING_GROUPS):
        chunk = groups[part * PART_GROUPS : (part + 1) * PART_GROUPS]
        chunk += [empty] * (PART_GROUPS - len(chunk))
        store(part, low(jnp.concatenate(chunk, 0)))


def pack_coupling(refs, tiles, width, store):
    for part, group in zip(SUMMED_AT, groups_of(refs, MATRICES[2:])):
        bias = jnp.concatenate([bias_row(tiles, part, width), jnp.zeros((7, LANES), F32)], 0)
        store(part, jnp.concatenate([group, bias], 0))


def sum_parts(came_ref):
    total = came_ref[0].astype(F32)
    for part in range(1, came_ref.shape[0]):
        total += came_ref[part].astype(F32)
    return total


def square_sum(values):
    return jnp.sum(jnp.sum(values * values, 0, keepdims=True), 1, keepdims=True)


def sum_adapter(came):
    def kernel(came_ref, total_ref, square_ref):
        total = sum_parts(came_ref)
        total_ref[...] = total
        square_ref[...] = square_sum(total)

    return pl.pallas_call(
        kernel,
        out_shape=[jax.ShapeDtypeStruct((PART_ROWS, LANES), F32), jax.ShapeDtypeStruct((1, 1), F32)],
        compiler_params=params_for(32),
        name="sum_adapter",
    )(came)


def sum_coupling(came, squares, loss_part, copies):
    def kernel(came_ref, square_ref, loss_ref, group_ref, bias_ref, pair_ref):
        total = sum_parts(came_ref)
        group_ref[...] = total[:GROUP_ROWS]
        bias_ref[...] = total[GROUP_ROWS:]
        squares = square_ref[...] + square_sum(total)
        lane = lax.broadcasted_iota(jnp.int32, (8, LANES), 1)
        pair = jnp.where(lane == 0, squares, jnp.where(lane == 1, loss_ref[:, :1], 0.0))
        for copy in range(copies):
            pair_ref[copy] = pair

    return pl.pallas_call(
        kernel,
        out_shape=[
            jax.ShapeDtypeStruct((GROUP_ROWS, LANES), F32),
            jax.ShapeDtypeStruct((8, LANES), F32),
            jax.ShapeDtypeStruct((copies, 8, LANES), F32),
        ],
        name="sum_coupling",
    )(came, squares, loss_part)


def grad_products(adapter_total, coupling_groups, root_left, root_right):
    count = 4 * PART_GROUPS

    def exact_dot(left, right, dims):
        return lax.dot_general(left, right, (dims, ((), ())), precision=HIGHEST, preferred_element_type=F32)

    def body(ins, out, scalar_refs, pair_refs, raw_refs, scratch):
        start(ins)
        total_ref, left_ref, right_ref, own_ref, *group_refs = (operand.get() for operand in ins)
        part = lax.axis_index("dp")
        own_place = jnp.int32(-1)
        for i, owner in enumerate(SUMMED_AT):
            at = ADAPTER_GROUPS + i
            if at // PART_GROUPS == owner:
                own_place = jnp.where(part == owner, at % PART_GROUPS, own_place)
        grad_ref, left_square_ref, right_square_ref, turned_ref = (result.buffer for result in out)
        for group in range(PART_GROUPS):
            total = total_ref[group * GROUP_ROWS : (group + 1) * GROUP_ROWS]
            total = total + jnp.where(own_place == group, own_ref[...], 0.0)
            if group:
                total = total + group_refs[group - 1][...]
            main, rest = total[:BLOCK], unfold_half(total[BLOCK:], False)
            lane = lane_of(main)
            pieces = (
                main,
                roll(main, 80),
                jnp.where(lane < 32, roll(main, 32), roll(rest, 32)),
                roll(rest, 112),
            )
            for j, values in enumerate(pieces):
                grad_ref[4 * group + j] = values[:, :BLOCK]
        for n in range(count):
            grad = grad_ref[n]
            left_square_ref[n] = exact_dot(grad, grad, ((1,), (1,)))
            right_square_ref[n] = exact_dot(grad, grad, ((0,), (0,)))
            turned_ref[n] = exact_dot(
                exact_dot(left_ref[n], grad, ((1,), (0,))), right_ref[n], ((1,), (0,))
            )

    ins = [adapter_total, root_left, root_right, *coupling_groups]
    outs = [jax.ShapeDtypeStruct((count, BLOCK, BLOCK), F32)] * 4
    return moved_call(body, (), ins, outs, (), [], "grad_products")[0]


MOST_VMEM = 64
GROUP = 256
HEADS_IN = GROUP // HEAD_DIM
GROUPS = D // GROUP
FF = 3072
TILE = 512
TILES = FF // TILE
STEP_ROWS = 256
SMALL_ROWS = 32


def rows_of(count, size):
    return [slice(at, at + min(size, count)) for at in range(0, count, size)]


def shape_of(*dims, kind=F32):
    return jax.ShapeDtypeStruct(dims, kind)


class Params(NamedTuple):
    down: Any
    bias_down: Any
    up: Any
    bias_up: Any


class Branch(NamedTuple):
    lin: Any
    act: Any
    slope: Any


class Attention(NamedTuple):
    query: Any
    key: Any
    value: Any
    lse: Any


class Rest(NamedTuple):
    normal_1: Any
    inverse_1: Any
    slope: Any
    branch: Any
    normal_2: Any
    inverse_2: Any


class Last(NamedTuple):
    one: Any
    two: Any
    normal: Any
    inverse: Any
    normed: Any


class ForwardIn(NamedTuple):
    came: Any
    spot: Any
    extra: Any
    pos: Any
    norms: Any
    chosen: Any
    adapter: Any
    coupling: Any


class Forward(NamedTuple):
    target_rows: Any
    one: Any
    two: Any
    attention_0: Any
    rest_0: Any
    attention_1: Any
    rest_1: Any
    last: Any


class BackIn(NamedTuple):
    merged: Any
    row_weights: Any
    weight_sum: Any
    norms: Any
    chosen_t: Any
    adapter: Any
    coupling: Any
    target_rows: Any
    rest_0: Any
    attention_1: Any
    rest_1: Any
    last: Any


class Back(NamedTuple):
    loss: Any
    one: Any
    two: Any
    adapters: Any
    inner: Any


class FirstIn(NamedTuple):
    inner: Any
    norms: Any
    inner_kept: Any
    attention: Any
    coupling: Any
    one: Any
    two: Any
    grads_one: Any
    grads_two: Any
    biases: Any


class Operand:
    def __init__(self, ref, buffer, sem):
        self.buffer, self.copy = buffer, pltpu.make_async_copy(ref, buffer, sem)
        self.started = self.waited = False

    def start(self):
        if not self.started:
            self.copy.start()
        self.started = True

    def get(self):
        self.start()
        if not self.waited:
            self.copy.wait()
        self.waited = True
        return self.buffer


class Result:
    def __init__(self, ref, buffer, sem):
        self.buffer, self.copy = buffer, pltpu.make_async_copy(buffer, ref, sem)
        self.sent = False

    def send(self):
        if not self.sent:
            self.copy.start()
        self.sent = True


def start(*operands):
    for operand in jax.tree.leaves(operands):
        operand.start()


def send(*results):
    for result in jax.tree.leaves(results):
        result.send()


def moved_call(body, scalars, ins, outs, pairs, scratch, name, raw_outs=()):
    in_leaves, in_tree = jax.tree.flatten(ins)
    out_leaves, out_tree = jax.tree.flatten(outs)

    def kernel(*refs):
        refs = list(refs)

        def take(count):
            taken, refs[:] = refs[:count], refs[count:]
            return taken

        scalar_refs, in_refs = take(len(scalars)), take(len(in_leaves))
        pair_refs = [tuple(take(2)) for _ in pairs]
        out_refs, raw_refs = take(len(out_leaves)), take(len(raw_outs))
        in_buffers, out_buffers, (in_sems, out_sems) = take(len(in_leaves)), take(len(out_leaves)), take(2)
        operands = [Operand(*two, in_sems.at[i]) for i, two in enumerate(zip(in_refs, in_buffers))]
        results = [Result(*two, out_sems.at[i]) for i, two in enumerate(zip(out_refs, out_buffers))]
        body(in_tree.unflatten(operands), out_tree.unflatten(results), scalar_refs, pair_refs, raw_refs, refs)
        send(results)
        for operand in operands:
            operand.get()
        for result in results:
            result.copy.wait()

    hbm = pl.BlockSpec(memory_space=pltpu.HBM)
    buffers = [pltpu.VMEM(value.shape, value.dtype) for value in (*in_leaves, *out_leaves)]
    results = pl.pallas_call(
        kernel,
        in_specs=[pl.BlockSpec(memory_space=pltpu.SMEM)] * len(scalars) + [hbm] * (len(in_leaves) + 2 * len(pairs)),
        out_specs=[hbm] * (len(out_leaves) + len(raw_outs)),
        out_shape=[*out_leaves, *raw_outs],
        scratch_shapes=buffers
        + [pltpu.SemaphoreType.DMA((len(in_leaves),)), pltpu.SemaphoreType.DMA((len(out_leaves),))]
        + list(scratch),
        compiler_params=params_for(MOST_VMEM),
        name=name,
    )(*scalars, *in_leaves, *[w for pair in pairs for w in pair])
    return out_tree.unflatten(results[: len(out_leaves)]), results[len(out_leaves) :]


def start_copy(pair, section, window, target, sem):
    own, came = pair
    here = lax.axis_index("section") == section

    @pl.when(here)
    def _():
        pltpu.make_async_copy(own.at[window], target, sem).start()

    @pl.when(jnp.logical_not(here))
    def _():
        pltpu.make_async_copy(came.at[window], target, sem).start()


def wait_copy(pair, window, target, sem):
    pltpu.make_async_copy(pair[0].at[window], target, sem).wait()


def qkv_window(group, part):
    return 0, slice(None), pl.ds(part * D + group * GROUP, GROUP)


def qkv_buffers():
    return [pltpu.VMEM((GROUPS, 3, D, GROUP), BF16), pltpu.SemaphoreType.DMA((GROUPS, 3))]


def start_qkv(pair, section, buffers):
    for group in range(GROUPS):
        for part in range(3):
            start_copy(pair, section, qkv_window(group, part), buffers[0].at[group, part], buffers[1].at[group, part])


def wait_qkv(pair, buffers, group, part):
    wait_copy(pair, qkv_window(0, 0), buffers[0].at[group, part], buffers[1].at[group, part])


UP_WINDOWS = [(0, slice(None), slice(j * TILE, (j + 1) * TILE)) for j in range(TILES)]
DOWN_WINDOWS = [(0, slice(j * TILE, (j + 1) * TILE), slice(None)) for j in range(TILES)]
OUT_WINDOW = (0, slice(None), slice(None))


def rest_buffers():
    return [
        pltpu.VMEM((D, D), BF16),
        pltpu.VMEM((TILES, D, TILE), BF16),
        pltpu.VMEM((TILES, TILE, D), BF16),
        pltpu.SemaphoreType.DMA((2 * TILES + 1,)),
    ]


def start_out(pairs, section, buffers):
    start_copy(pairs[0], section, OUT_WINDOW, buffers[0], buffers[3].at[2 * TILES])


def start_tiles(pairs, section, buffers):
    for j in range(TILES):
        start_copy(pairs[1], section, UP_WINDOWS[j], buffers[1].at[j], buffers[3].at[j])
        start_copy(pairs[2], section, DOWN_WINDOWS[j], buffers[2].at[j], buffers[3].at[TILES + j])


def wait_out(pairs, buffers):
    wait_copy(pairs[0], OUT_WINDOW, buffers[0], buffers[3].at[2 * TILES])


def wait_up(pairs, buffers, tile):
    wait_copy(pairs[1], UP_WINDOWS[0], buffers[1].at[tile], buffers[3].at[tile])


def wait_down(pairs, buffers, tile):
    wait_copy(pairs[2], DOWN_WINDOWS[0], buffers[2].at[tile], buffers[3].at[TILES + tile])


def across(values):
    return jnp.broadcast_to(values, (values.shape[0], LANES))


def group_columns(group):
    return pl.ds(pl.multiple_of(group * GROUP, GROUP), GROUP)


def tile_columns(tile):
    return pl.ds(pl.multiple_of(tile * TILE, TILE), TILE)


def head_mask(values, head):
    lane = lax.broadcasted_iota(jnp.int32, values.shape, 1)
    return (lane >= head * HEAD_DIM) & (lane < (head + 1) * HEAD_DIM)


def only_head(values, head):
    return jnp.where(head_mask(values, head), values, jnp.zeros_like(values))


def scaled_query(query):
    return low(query.astype(F32) * HEAD_DIM**-0.5)


def key_bias(length, shape, axis):
    return jnp.where(lax.broadcasted_iota(jnp.int32, shape, axis) < length, 0.0, -1e30)


def softmax_rows(scores):
    highest = jnp.max(scores, 1, keepdims=True)
    exponent = jnp.exp(scores - highest)
    total = jnp.sum(exponent, 1, keepdims=True)
    return low(exponent * (1.0 / total)), highest + jnp.log(total)


def branch_rows(low_in, weights):
    active, slope = gelu_both(matmul(low_in, weights[0]) + weights[1])
    active = low(active)
    return matmul(active, weights[2]) + weights[3], active, low(slope)


def alternate(*lists):
    steps = [((i + 0.5) / len(steps), k, step) for k, steps in enumerate(lists) for i, step in enumerate(steps)]
    for _, _, step in sorted(steps, key=lambda entry: entry[:2]):
        step()


def section_params(params, section):
    return [operand.get()[section] for operand in params]


def rest_rows(out, rows, section, norms, adapter, hidden, mixed, finish, scratch, pairs, buffers, after_loop=None):
    att_low, acc, u_even, u_odd, g_even, g_odd = scratch
    gain = lambda i: norms[section, i : i + 1]
    parts = rows_of(rows, STEP_ROWS)
    every = slice(0, rows)
    wait_out(pairs, buffers)
    for part in parts:
        first = hidden[part] + matmul(mixed[part], buffers[0][...])
        values, (normal, inverse) = layer_norm(first, gain(2), gain(3))
        acc[part] = values
        att_low[part] = low(values)
        out.normal_1.buffer[part] = normal
        out.inverse_1.buffer[part] = across(inverse)
    send(out.normal_1, out.inverse_1)
    wait_up(pairs, buffers, 0)
    g_odd[every] = jnp.zeros_like(g_odd[every])

    def gelu_steps(u_ref, g_ref, tile):
        def step(at):
            active, slope = gelu_both(u_ref[at])
            g_ref[at] = low(active)
            out.slope.buffer[at, tile_columns(tile)] = low(slope)

        return [functools.partial(step, at) for at in rows_of(rows, SMALL_ROWS)]

    def up_steps(u_ref, tile):
        def step(columns):
            u_ref[every, columns] = matmul(att_low[every], buffers[1][tile, :, columns])

        return [functools.partial(step, columns) for columns in rows_of(TILE, GROUP)]

    def down_steps(g_ref, tile):
        def step(columns):
            acc[every, columns] += matmul(g_ref[every], buffers[2][tile, :, columns])

        return [functools.partial(step, columns) for columns in rows_of(D, GROUP)]

    alternate(up_steps(u_even, 0))

    def turn(j, carry):
        even, odd = 2 * j, 2 * j + 1
        before, after = jnp.maximum(even - 1, 0), jnp.minimum(even + 2, TILES - 1)
        wait_down(pairs, buffers, even)
        wait_up(pairs, buffers, odd)
        wait_down(pairs, buffers, odd)

        @pl.when(even + 2 < TILES)
        def _():
            wait_up(pairs, buffers, even + 2)

        alternate(gelu_steps(u_even, g_even, even), down_steps(g_odd, before) + up_steps(u_odd, odd))
        alternate(gelu_steps(u_odd, g_odd, odd), down_steps(g_even, even) + up_steps(u_even, after))
        return carry

    lax.fori_loop(0, TILES // 2, turn, 0)
    alternate(down_steps(g_odd, TILES - 1))
    if after_loop is not None:
        after_loop()
    send(out.slope)
    weights = section_params(adapter, section)
    for part in parts:
        summed = acc[part]
        low_in = low(summed)
        added, *kept = branch_rows(low_in, weights)
        for result, value in zip(out.branch, (low_in, *kept)):
            result.buffer[part] = value
        values, (normal, inverse) = layer_norm(summed + added, gain(4), gain(5))
        out.normal_2.buffer[part], out.inverse_2.buffer[part] = normal, across(inverse)
        finish(part, values)
    send(out.branch, out.normal_2, out.inverse_2)


def low_shape(*dims):
    return shape_of(*dims, kind=BF16)


def branch_shapes(rows, wide, narrow):
    return Branch(low_shape(rows, wide), low_shape(rows, narrow), low_shape(rows, narrow))


def rest_shapes(rows):
    wide, thin = shape_of(rows, D), shape_of(rows, LANES)
    return Rest(wide, thin, low_shape(rows, FF), branch_shapes(rows, D, BOT), wide, thin)


def forward_kernel(ins, scalars, pairs, parts, slots):
    coupling_shapes = lambda rows: branch_shapes(rows, HALF, INV_H)
    outs = Forward(
        target_rows=shape_of(COUNT, D),
        one=coupling_shapes(SEQ),
        two=coupling_shapes(SEQ),
        attention_0=Attention(*[low_shape(SEQ, D)] * 3, shape_of(GROUPS, 8, SEQ)),
        rest_0=rest_shapes(SEQ),
        attention_1=Attention(
            low_shape(COUNT, D), *[low_shape(SEQ, D)] * 2, shape_of(GROUPS, HEADS_IN * COUNT, LANES)
        ),
        rest_1=rest_shapes(COUNT),
        last=Last(
            coupling_shapes(COUNT), coupling_shapes(COUNT),
            shape_of(COUNT, D), shape_of(COUNT, LANES), low_shape(COUNT, D),
        ),
    )

    def body(ins, out, scalar_refs, pair_refs, raw_refs, scratch):
        length = scalar_refs[0][0]
        hidden, x_low, s_even, s_odd, p_even, p_odd, lse_buf, mixed, section_out = scratch[:9]
        at_spots, at_low, mixed_1 = scratch[9:12]
        rest_scratch, qkv_0, qkv_1, rest_w = scratch[12:18], scratch[18:20], scratch[20:22], scratch[22:26]
        row_sems, joined = scratch[26:28]
        qkv_pair, rest_pairs = pair_refs[0], pair_refs[1:]

        start(ins.came, ins.spot, ins.pos, ins.norms, ins.coupling)
        norms = ins.norms.get()
        norm = lambda s, i: norms[s, i : i + 1]

        came, spot = ins.came.get(), ins.spot.get()
        start_qkv(qkv_pair, 0, qkv_0)
        start_out(rest_pairs, 0, rest_w)

        def rows_at(part):
            lane = lax.broadcasted_iota(jnp.int32, (part.stop - part.start, parts * slots), 1)
            hits = (spot[part][:, :1] == lane).astype(BF16)
            return matmul(hits, came[...])

        targets = slice(SEQ, SEQ + COUNT)
        out.target_rows.buffer[...] = rows_at(targets)
        for part in rows_of(SEQ, STEP_ROWS):
            hidden[part] = rows_at(part)

        @pl.when(scalar_refs[1][0] > 1)
        def _():
            ins.extra.copy.start()
            ins.extra.copy.wait()
            out.target_rows.buffer[...] += ins.extra.buffer[targets]
            hidden[...] += ins.extra.buffer[:SEQ]

        ins.extra.started = ins.extra.waited = True
        send(out.target_rows)
        start(ins.adapter, ins.chosen)
        start_tiles(rest_pairs, 0, rest_w)
        one, two = section_params(ins.coupling, 0), section_params(ins.coupling, 1)

        def put(results, part, *values):
            for result, value in zip(results, values):
                result.buffer[part] = value

        for part in rows_of(SEQ, STEP_ROWS):
            started, _ = layer_norm(hidden[part] + ins.pos.get()[part].astype(F32), norm(0, 0), norm(0, 1))
            left, right = started[:, :HALF], started[:, HALF:]
            low_one = low(right)
            added, active, slope = branch_rows(low_one, one)
            put(out.one, part, low_one, active, slope)
            left = left + added
            low_two = low(left)
            added, active, slope = branch_rows(low_two, two)
            put(out.two, part, low_two, active, slope)
            right = right + added
            hidden[part, :HALF] = left
            hidden[part, HALF:] = right
            x_low[part, :HALF] = low_two
            x_low[part, HALF:] = low(right)
        send(out.one, out.two)

        start_qkv(qkv_pair, 1, qkv_1)
        lse_buf[...] = jnp.zeros((SEQ, LANES), F32)
        q_ref, k_ref, v_ref, lse_ref = (result.buffer for result in out.attention_0)

        def attend(group, carry):
            columns = group_columns(group)
            for part, ref in enumerate((q_ref, k_ref, v_ref)):
                wait_qkv(qkv_pair, qkv_0, group, part)
                ref[:, columns] = low(matmul(x_low[...], qkv_0[0][group, part]))
            query = scaled_query(q_ref[:, columns])
            key, value = k_ref[:, columns], v_ref[:, columns]
            bias = key_bias(length, (1, SEQ), 1)
            lane = lax.broadcasted_iota(jnp.int32, (SMALL_ROWS * 2, LANES), 1)
            buffers = ((s_even, p_even), (s_odd, p_odd)) * 2

            def score_steps(head):
                def step():
                    buffers[head][0][...] = matmul_t(only_head(query, head), key)

                return [step] if head < HEADS_IN else []

            def soft_steps(head):
                def step(rows):
                    soft, lse = softmax_rows(buffers[head][0][rows] + bias)
                    buffers[head][1][rows] = soft
                    lse_buf[rows] = jnp.where(lane == head, lse, lse_buf[rows])

                return [functools.partial(step, rows) for rows in rows_of(SEQ, SMALL_ROWS * 2)]

            def mix_steps(head):
                def step():
                    mixed_head = matmul(buffers[head][1][...], value)
                    if head == 0:
                        joined[...] = mixed_head
                    else:
                        joined[...] = jnp.where(head_mask(mixed_head, head), mixed_head, joined[...])

                return [step] if head >= 0 else []

            alternate(score_steps(0))
            for head in range(HEADS_IN):
                alternate(soft_steps(head), score_steps(head + 1) + mix_steps(head - 1))
            alternate(mix_steps(HEADS_IN - 1))
            mixed[:, columns] = low(joined[...])
            lse_ref[group] = jnp.transpose(lse_buf[...])[:8]
            return carry

        lax.fori_loop(0, GROUPS, attend, 0)
        send(out.attention_0)

        def to_section_out(part, values):
            section_out[part] = low(values)

        def next_weights():
            start_out(rest_pairs, 1, rest_w)
            start_tiles(rest_pairs, 1, rest_w)

        rest_rows(
            out.rest_0, SEQ, 0, norms, ins.adapter, hidden, mixed, to_section_out,
            rest_scratch, rest_pairs, rest_w, next_weights,
        )

        at_spots[...] = matmul(ins.chosen.get()[...], section_out[...])
        at_low[...] = low(at_spots[...])
        q_1, k_1, v_1, lse_1 = (result.buffer for result in out.attention_1)

        groups = rows_of(D, GROUP)
        for group, columns in enumerate(groups):
            for part, ref in enumerate((q_1, k_1, v_1)):
                wait_qkv(qkv_pair, qkv_1, group, part)
                source = at_low if part == 0 else section_out
                ref[:, columns] = low(matmul(source[...], qkv_1[0][group, part]))
        bias = key_bias(length, (1, SEQ), 1)
        for group, columns in enumerate(groups):
            query = scaled_query(q_1[:, columns])
            query = jnp.concatenate([only_head(query, head) for head in range(HEADS_IN)], 0)
            soft, lse = softmax_rows(matmul_t(query, k_1[:, columns]) + bias)
            lse_1[group] = across(lse)
            every = matmul(soft, v_1[:, columns])
            mixed_group = every[:COUNT]
            for head in range(1, HEADS_IN):
                rows = slice(head * COUNT, (head + 1) * COUNT)
                mixed_group = jnp.where(head_mask(mixed_group, head), every[rows], mixed_group)
            mixed_1[:, columns] = low(mixed_group)
        send(out.attention_1)

        def to_normed(part, values):
            left, right = values[:, :HALF], values[:, HALF:]
            low_two = low(left)
            taken, active, slope = branch_rows(low_two, two)
            put(out.last.two, part, low_two, active, slope)
            right = right - taken
            low_one = low(right)
            taken, active, slope = branch_rows(low_one, one)
            put(out.last.one, part, low_one, active, slope)
            left = left - taken
            values, (normal, inverse) = layer_norm(jnp.concatenate([left, right], 1), norm(1, 0), norm(1, 1))
            put(out.last[2:], part, normal, across(inverse), low(values))

        rest_rows(
            out.rest_1, COUNT, 1, norms, ins.adapter, at_spots, mixed_1, to_normed,
            rest_scratch, rest_pairs, rest_w,
        )
        normed = out.last.normed.buffer
        copies = [
            pltpu.make_async_copy(normed.at[half], raw_refs[i].at[part], row_sems.at[i, part])
            for i, half in enumerate(rows_of(COUNT, COUNT // 2))
            for part in range(parts)
        ]
        for copy in copies:
            copy.start()
        for copy in copies:
            copy.wait()

    buffer = lambda *dims: pltpu.VMEM(dims, F32)
    buffer_low = lambda *dims: pltpu.VMEM(dims, BF16)
    scratch = [buffer(SEQ, D), buffer_low(SEQ, D), buffer(SEQ, SEQ), buffer(SEQ, SEQ)]
    scratch += [buffer_low(SEQ, SEQ), buffer_low(SEQ, SEQ), buffer(SEQ, LANES)]
    scratch += [buffer_low(SEQ, D), buffer_low(SEQ, D)]
    scratch += [buffer(COUNT, D), buffer_low(COUNT, D), buffer_low(COUNT, D)]
    scratch += [buffer_low(SEQ, D), buffer(SEQ, D), buffer(SEQ, TILE), buffer(SEQ, TILE)]
    scratch += [buffer_low(SEQ, TILE), buffer_low(SEQ, TILE)]
    scratch += qkv_buffers() + qkv_buffers() + rest_buffers()
    scratch += [pltpu.SemaphoreType.DMA((2, parts)), buffer(SEQ, GROUP)]
    raw = [low_shape(parts, COUNT // 2, D)] * 2
    kept, rows = moved_call(body, scalars, ins, outs, pairs, scratch, "forward", raw)
    return kept, rows


def column_sum(values):
    return jnp.sum(values.astype(F32), 0, keepdims=True)


def branch_grads(grad_low, kept, weights, out_refs):
    low_in, active, slope = kept
    hidden_grad = low(matmul_t(grad_low, weights[2]) * slope.astype(F32))
    out_refs[0][...] = inner_rows(low_in, hidden_grad)
    out_refs[1][...] = column_sum(hidden_grad)
    out_refs[2][...] = inner_rows(active, grad_low)
    out_refs[3][...] = column_sum(grad_low)
    return hidden_grad


ADAPTER_GRADS = ((D, BOT), (1, BOT), (BOT, D), (1, D))
COUPLING_GRADS = ((HALF, INV_H), (1, INV_H), (INV_H, HALF), (1, HALF))


def branch_kept(branch):
    return [operand.get()[...] for operand in branch]


def grad_weights(pair, section):
    return [pair[0].get()[section], None, pair[1].get()[section]]


def back_to_inner(kept, rows, section, norms, adapter, incoming, scratch, grad_refs, packing=None):
    acc, second_low = scratch
    parts = rows_of(rows, STEP_ROWS)
    weights = grad_weights(adapter, section)
    for part in parts:
        norm_kept = kept.normal_2.get()[part], kept.inverse_2.get()[part, :1]
        second = norm_back(incoming(part), norm_kept, norms[section, 4:5])
        acc[part] = second
        second_low[part] = low(second)
    hidden_grad = branch_grads(second_low[:rows], branch_kept(kept.branch), weights, grad_refs)
    for part in parts:
        acc[part] += matmul_t(hidden_grad[part], weights[0])
    if packing is not None:
        packing()


def back_to_mixed(operands, rows, section, norms, scratch, pairs, buffers, results):
    summed_low, acc = scratch
    start_ref, mixed_ref = results
    slope, normal, inverse = (operand.get() for operand in operands)
    parts = rows_of(rows, STEP_ROWS)
    for part in parts:
        summed_low[part] = low(acc[part])

    def turn(j, carry):
        for now in (2 * j, 2 * j + 1):
            wait_up(pairs, buffers, now)
            wait_down(pairs, buffers, now)
        for now in (2 * j, 2 * j + 1):
            for part in parts:
                inner = matmul_t(summed_low[part], buffers[2][now])
                inner = low(inner * slope[part, tile_columns(now)].astype(F32))
                acc[part] += matmul_t(inner, buffers[1][now])
        return carry

    lax.fori_loop(0, TILES // 2, turn, 0)
    wait_out(pairs, buffers)
    for part in parts:
        back = norm_back(acc[part], (normal[part], inverse[part, :1]), norms[section, 2:3])
        start_ref[part] = back
        mixed_ref[part] = low(matmul_t(low(back), buffers[0][...]))


def backward_kernel(ins, scalars, pairs, packed):
    parts = ins.merged[0].shape[0]
    grads = [shape_of(*dims) for dims in COUPLING_GRADS]
    if packed:
        chunks = low_shape(COUPLING_GROUPS, PART_ROWS, LANES)
        adapters = [[shape_of(1, BOT), shape_of(1, D)] for _ in range(MICRO)] + [chunks, chunks]
    else:
        adapters = [[shape_of(*dims) for dims in ADAPTER_GRADS] for _ in range(MICRO)]
    outs = Back(shape_of(1, LANES), grads, grads, adapters, shape_of(SEQ, D))

    def body(ins, out, scalar_refs, pair_refs, raw_refs, scratch):
        length = scalar_refs[0][0]
        (summed_low, acc_0, second_low), spot, mixed_1, acc_1, section_grad = scratch[:3], *scratch[3:7]
        qkv_w, rest_w, refs = scratch[7:9], scratch[9:13], scratch[13:]
        qkv_pair, rest_pairs = pair_refs[0], pair_refs[1:]

        start(ins.merged, ins.row_weights, ins.weight_sum, ins.target_rows, ins.last, ins.norms)
        start(ins.coupling, ins.adapter, ins.rest_1)
        start_tiles(rest_pairs, 1, rest_w)
        start_out(rest_pairs, 1, rest_w)
        start_qkv(qkv_pair, 1, qkv_w)
        start(ins)
        norms = ins.norms.get()

        def merge(merged):
            stats = merged[:, :, D:].astype(F32)
            highest = jnp.sum(stats[:, :, :3], 2, keepdims=True)
            totals = jnp.sum(stats[:, :, 3:6], 2, keepdims=True)
            top = jnp.max(highest, 0)
            factor = jnp.exp(highest - top[None])
            total = jnp.sum(totals * factor, 0)
            expected = jnp.zeros((merged.shape[1], D), F32)
            for i in range(parts):
                expected += merged[i, :, :D].astype(F32) * (factor[i] / total)
            return top, total, expected

        def from_head(part):
            halves = [merge(operand.get()) for operand in ins.merged]
            top, total, expected = (jnp.concatenate(pair, 0) for pair in zip(*halves))
            target = ins.target_rows.get()[...]
            target_logit = jnp.sum(ins.last.normed.get()[...].astype(F32) * target, 1, keepdims=True)
            weight = ins.row_weights.get()[...]
            row_losses = weight[:, :1] * (top + jnp.log(total) - target_logit)
            out.loss.buffer[...] = across(jnp.sum(row_losses, 0, keepdims=True))
            normed_grad = (weight / ins.weight_sum.get()[...])[:, :1] * (expected - target)
            kept = (ins.last.normal.get()[...], ins.last.inverse.get()[:, :1])
            restored = norm_back(normed_grad, kept, norms[1, 0:1])
            left, right = restored[:, :HALF], restored[:, HALF:]
            one, two = (grad_weights(ins.coupling, s) for s in range(MICRO))
            refs_of = lambda results: [result.buffer for result in results]
            hidden = branch_grads(low(-left), branch_kept(ins.last.one), one, refs_of(out.one))
            right = right + matmul_t(hidden, one[0])
            hidden = branch_grads(low(-right), branch_kept(ins.last.two), two, refs_of(out.two))
            left = left + matmul_t(hidden, two[0])
            return jnp.concatenate([left, right], 1)

        def grads_of(section):
            buffers = [result.buffer for result in out.adapters[section]]
            return (refs[0], buffers[0], refs[1], buffers[1]) if packed else buffers

        def pack_second():
            def store(part, chunk):
                refs[2][part] = chunk

            pack_adapter((refs[0], refs[1]), store)

        def pack_both():
            here = lax.axis_index("section") == 0
            own, other = out.adapters[2:]

            def store(part, chunk):
                arrived = refs[2][part]
                own.buffer[part] = jnp.where(here, chunk, arrived)
                other.buffer[part] = jnp.where(here, arrived, chunk)

            pack_adapter((refs[0], refs[1]), store)
            send(own, other)

        back_to_inner(
            ins.rest_1, COUNT, 1, norms, ins.adapter, from_head, (acc_0, second_low), grads_of(1),
            pack_second if packed else None,
        )
        kept = ins.rest_1.slope, ins.rest_1.normal_1, ins.rest_1.inverse_1
        back_to_mixed(kept, COUNT, 1, norms, (summed_low, acc_0), rest_pairs, rest_w, (spot, mixed_1))

        acc_1[...] = jnp.zeros_like(acc_1)
        q_ref, k_ref, v_ref, lse_ref = (operand.get() for operand in ins.attention_1)

        def attend_back(group, carry):
            columns = group_columns(group)
            stack = lambda values: jnp.concatenate([only_head(values, h) for h in range(HEADS_IN)], 0)
            query = stack(scaled_query(q_ref[:, columns]))
            mixed = stack(mixed_1[:, columns])
            key, value = k_ref[:, columns], v_ref[:, columns]
            scores = matmul_t(query, key) + key_bias(length, (1, SEQ), 1)
            soft = jnp.exp(scores - lse_ref[group][:, :1])
            soft_grad = matmul_t(mixed, value)
            delta = jnp.sum(soft_grad * soft, 1, keepdims=True)
            score_grad = low(soft * (soft_grad - delta))
            every = matmul(score_grad, key)
            query_grad = every[:COUNT]
            for head in range(1, HEADS_IN):
                query_grad = jnp.where(
                    head_mask(query_grad, head), every[head * COUNT : (head + 1) * COUNT], query_grad
                )
            query_grad = low(query_grad * HEAD_DIM**-0.5)
            key_grad = low(inner_rows(score_grad, query))
            value_grad = low(inner_rows(low(soft), mixed))
            for part in range(3):
                wait_qkv(qkv_pair, qkv_w, group, part)
            spot[...] += matmul_t(query_grad, qkv_w[0][group, 0])
            acc_1[...] += matmul_t(key_grad, qkv_w[0][group, 1]) + matmul_t(value_grad, qkv_w[0][group, 2])
            return carry

        lax.fori_loop(0, GROUPS, attend_back, 0)
        placed = jnp.dot(ins.chosen_t.get()[...], spot[...], precision=HIGHEST, preferred_element_type=F32)
        section_grad[...] = low(acc_1[...] + placed)

        back_to_inner(
            ins.rest_0, SEQ, 0, norms, ins.adapter, lambda part: section_grad[part].astype(F32),
            (out.inner.buffer, second_low), grads_of(0), pack_both if packed else None,
        )

    scratch = [pltpu.VMEM((COUNT, D), BF16), pltpu.VMEM((COUNT, D), F32), pltpu.VMEM((SEQ, D), BF16)]
    scratch += [pltpu.VMEM((COUNT, D), F32), pltpu.VMEM((COUNT, D), BF16), pltpu.VMEM((SEQ, D), F32)]
    scratch += [pltpu.VMEM((SEQ, D), BF16)] + qkv_buffers() + rest_buffers()
    if packed:
        scratch += [pltpu.VMEM((D, BOT), F32), pltpu.VMEM((BOT, D), F32)]
        scratch += [pltpu.VMEM((COUPLING_GROUPS, PART_ROWS, LANES), BF16)]
    return moved_call(body, scalars, ins, outs, pairs, scratch, "backward")[0]


def first_backward(ins, scalars, pairs, packed):
    if packed:
        dims = (COUPLING_GROUPS, GROUP_ROWS + 8, LANES)
        outs = (shape_of(*dims), low_shape(*dims))
    else:
        outs = [shape_of(*dims) for dims in COUPLING_GRADS * 2]

    def body(ins, out, scalar_refs, pair_refs, raw_refs, scratch):
        length = scalar_refs[0][0]
        s_even, s_odd, d_even, d_odd, p_even, p_odd, ds_even, ds_odd = scratch[:8]
        qkv_w, (key_grad, value_grad, query_grad_t), refs = scratch[8:10], scratch[10:13], scratch[13:]
        (summed_low, mixed_ref), rest_w, refs = refs[:2], refs[2:6], refs[6:]
        start(ins.inner, ins.norms)
        start_tiles(pair_refs[1:], 0, rest_w)
        start(ins.inner_kept)
        start_out(pair_refs[1:], 0, rest_w)
        start(ins.attention)
        start_qkv(pair_refs[0], 0, qkv_w)
        start(ins)
        acc = ins.inner.get()
        back_to_mixed(
            ins.inner_kept, SEQ, 0, ins.norms.get(), (summed_low, acc), pair_refs[1:], rest_w, (acc, mixed_ref)
        )
        q_ref, k_ref, v_ref, lse_ref = (operand.get() for operand in ins.attention)

        def attend_back(group, carry):
            columns = group_columns(group)
            query = scaled_query(q_ref[:, columns])
            key, value, mixed = k_ref[:, columns], v_ref[:, columns], mixed_ref[:, columns]
            lse_rows = lse_ref[group]
            key_t = jnp.transpose(key)
            buffers = ((s_even, d_even, p_even, ds_even), (s_odd, d_odd, p_odd, ds_odd)) * 2

            def product_steps(head):
                def scores():
                    buffers[head][0][...] = matmul_t(only_head(key, head), query)

                def soft_grads():
                    buffers[head][1][...] = matmul_t(only_head(value, head), mixed)

                return [scores, soft_grads] if head < HEADS_IN else []

            def soft_steps(head):
                s_buf, d_buf, p_low, ds_low = buffers[head]
                delta = [jnp.zeros((8, SEQ), F32)]

                def soft_step(rows):
                    valid = lax.broadcasted_iota(jnp.int32, (SMALL_ROWS, 1), 0) + rows.start < length
                    bias = jnp.where(valid, 0.0, -1e30)
                    soft = jnp.exp(s_buf[rows] + bias - lse_rows[head : head + 1])
                    s_buf[rows] = soft
                    p_low[rows] = low(soft)
                    product = soft * d_buf[rows]
                    for at in range(0, SMALL_ROWS, 8):
                        delta[0] = delta[0] + product[at : at + 8]

                def sum_step():
                    delta[0] = jnp.sum(delta[0], 0, keepdims=True)

                def grad_step(rows):
                    ds_low[rows] = low(s_buf[rows] * (d_buf[rows] - delta[0]))

                parts = rows_of(SEQ, SMALL_ROWS)
                steps = [functools.partial(soft_step, rows) for rows in parts] + [sum_step]
                return steps + [functools.partial(grad_step, rows) for rows in parts]

            def grad_steps(head):
                _, _, p_low, ds_low = buffers[max(head, 0)]

                def add(ref, grad):
                    ref[...] = grad if head == 0 else ref[...] + grad

                def value_step():
                    add(value_grad, matmul(p_low[...], only_head(mixed, head)))

                def key_step():
                    add(key_grad, matmul(ds_low[...], only_head(query, head)))

                def query_step():
                    rows = slice(head * HEAD_DIM, (head + 1) * HEAD_DIM)
                    query_grad_t[rows] = matmul(key_t[rows], ds_low[...])

                return [value_step, key_step, query_step] if head >= 0 else []

            alternate(product_steps(0))
            for head in range(HEADS_IN):
                alternate(soft_steps(head), product_steps(head + 1) + grad_steps(head - 1))
            alternate(grad_steps(HEADS_IN - 1))
            query_grad = jnp.transpose(query_grad_t[...]) * HEAD_DIM**-0.5
            for part, grad in enumerate((query_grad, key_grad[...], value_grad[...])):
                wait_qkv(pair_refs[0], qkv_w, group, part)
                acc[...] += matmul_t(low(grad), qkv_w[0][group, part])
            return carry

        lax.fori_loop(0, GROUPS, attend_back, 0)
        one, two = (grad_weights(ins.coupling, s) for s in range(MICRO))
        grads = refs if packed else [result.buffer for result in out]
        hidden = branch_grads(low(acc[:, HALF:]), branch_kept(ins.two), two, grads[4:])
        left = acc[:, :HALF] + matmul_t(hidden, two[0])
        branch_grads(low(left), branch_kept(ins.one), one, grads[:4])
        for ref, operand in zip(grads, (*ins.grads_one, *ins.grads_two)):
            ref[...] += operand.get()[...]
        if not packed:
            return
        here = lax.axis_index("section")
        for s in range(MICRO):
            some = grads[4 * s : 4 * s + 4]
            biases = [operand.get()[...] for operand in ins.biases[s]]
            tiles = bias_tiles(*biases, some[1][...], some[3][...])

            def store(part, chunk, s=s):
                @pl.when(here == s)
                def _():
                    out[0].buffer[part] = chunk

                @pl.when(here != s)
                def _():
                    out[1].buffer[part] = low(chunk)

            pack_coupling((some[0], some[2]), tiles, sum(BIASES) // COUPLING_GROUPS, store)

    scratch = [pltpu.VMEM((SEQ, SEQ), F32)] * 4 + [pltpu.VMEM((SEQ, SEQ), BF16)] * 4 + qkv_buffers()
    scratch += [pltpu.VMEM((SEQ, GROUP), F32)] * 2 + [pltpu.VMEM((GROUP, SEQ), F32)]
    scratch += [pltpu.VMEM((SEQ, D), BF16)] * 2 + rest_buffers()
    if packed:
        scratch += [pltpu.VMEM(dims, F32) for dims in COUPLING_GRADS * 2]
    return moved_call(body, scalars, ins, outs, pairs, scratch, "first_backward")[0]


VOCAB_TILE = 1280


def head_stats(top, total):
    lane = lax.broadcasted_iota(jnp.int32, (top.shape[0], LANES), 1)
    stats = jnp.zeros(lane.shape, F32)
    for j, piece in enumerate(three_low(top) + three_low(total)):
        stats = jnp.where(lane == j, piece.astype(F32), stats)
    return low(stats)


def head_kernel(rows, table):
    parts, each, _ = rows.shape
    count, vocab = parts * each, table.shape[0]
    tiles = pl.cdiv(vocab, VOCAB_TILE)
    if vocab < VOCAB_TILE or (vocab - VOCAB_TILE) % 16 or tiles % 2:
        return blocked_head_kernel(rows, table)
    starts = [min(tile * VOCAB_TILE, vocab - VOCAB_TILE) for tile in range(tiles)]

    def kernel(x_hbm, table_hbm, out_hbm, *refs):
        x_ref, out_ref, entries, acc, top, total, factor_even, factor_odd = refs[:8]
        l_even, l_odd, p_even, p_odd, sems = refs[8:]
        fetch = pltpu.make_async_copy(x_hbm, x_ref, sems.at[tiles])
        fetch.start()
        for tile, at in enumerate(starts):
            window = table_hbm.at[pl.ds(at, VOCAB_TILE)]
            pltpu.make_async_copy(window, entries.at[tile], sems.at[tile]).start()

        def wait_tile(tile):
            window = table_hbm.at[pl.ds(0, VOCAB_TILE)]
            pltpu.make_async_copy(window, entries.at[tile], sems.at[tile]).wait()

        def logit_steps(l_ref, tile):
            def step(columns):
                l_ref[:, columns] = matmul_t(x_ref[...], entries[tile, columns])

            return [functools.partial(step, columns) for columns in rows_of(VOCAB_TILE, GROUP)]

        def soft_steps(l_ref, p_ref, factor_ref, tile):
            start = jnp.minimum(tile * VOCAB_TILE, vocab - VOCAB_TILE)
            lane = lax.broadcasted_iota(jnp.int32, (1, VOCAB_TILE), 1)
            bias = jnp.where(lane + start >= tile * VOCAB_TILE, 0.0, -1e30)

            def step(at):
                logits = l_ref[at] + bias
                earlier = top[at]
                highest = jnp.maximum(earlier, jnp.max(logits, 1, keepdims=True))
                exponent = jnp.exp(logits - highest)
                factor = jnp.exp(earlier - highest)
                top[at] = highest
                total[at] = total[at] * factor + jnp.sum(exponent, 1, keepdims=True)
                p_ref[at] = low(exponent)
                factor_ref[at] = across(factor)

            return [functools.partial(step, at) for at in rows_of(count, SMALL_ROWS)]

        def sum_steps(p_ref, factor_ref, tile):
            def step(columns):
                factor = factor_ref[...]
                factor = jnp.concatenate([factor, factor], 1)
                acc[:, columns] = acc[:, columns] * factor + matmul(p_ref[...], entries[tile, :, columns])

            return [functools.partial(step, columns) for columns in rows_of(D, GROUP)]

        acc[...] = jnp.zeros_like(acc)
        top[...] = jnp.full_like(top, -1e30)
        total[...] = jnp.zeros_like(total)
        p_odd[...] = jnp.zeros_like(p_odd)
        factor_odd[...] = jnp.ones_like(factor_odd)
        fetch.wait()
        wait_tile(0)
        alternate(logit_steps(l_even, 0))

        def turn(j, carry):
            even, odd = 2 * j, 2 * j + 1
            before, after = jnp.maximum(even - 1, 0), jnp.minimum(even + 2, tiles - 1)
            wait_tile(odd)

            @pl.when(even + 2 < tiles)
            def _():
                wait_tile(even + 2)

            alternate(
                soft_steps(l_even, p_even, factor_even, even),
                sum_steps(p_odd, factor_odd, before) + logit_steps(l_odd, odd),
            )
            alternate(
                soft_steps(l_odd, p_odd, factor_odd, odd),
                sum_steps(p_even, factor_even, even) + logit_steps(l_even, after),
            )
            return carry

        lax.fori_loop(0, tiles // 2, turn, 0)
        alternate(sum_steps(p_odd, factor_odd, tiles - 1))
        out_ref[:, :D] = low(acc[...])
        out_ref[:, D:] = head_stats(top[...], total[...])
        copy = pltpu.make_async_copy(out_ref, out_hbm, sems.at[tiles])
        copy.start()
        copy.wait()

    hbm = pl.BlockSpec(memory_space=pltpu.HBM)
    return pl.pallas_call(
        kernel,
        in_specs=[hbm, hbm],
        out_specs=hbm,
        out_shape=low_shape(count, D + LANES),
        scratch_shapes=[
            pltpu.VMEM((count, D), BF16),
            pltpu.VMEM((count, D + LANES), BF16),
            pltpu.VMEM((tiles, VOCAB_TILE, D), BF16),
            pltpu.VMEM((count, D), F32),
            pltpu.VMEM((count, 1), F32),
            pltpu.VMEM((count, 1), F32),
        ]
        + [pltpu.VMEM((count, LANES), F32)] * 2
        + [pltpu.VMEM((count, VOCAB_TILE), F32)] * 2
        + [pltpu.VMEM((count, VOCAB_TILE), BF16)] * 2
        + [pltpu.SemaphoreType.DMA((tiles + 1,))],
        compiler_params=params_for(MOST_VMEM),
        name="vocabulary_head",
    )(rows.reshape(count, D), table).reshape(parts, each, D + LANES)


def blocked_head_kernel(rows, table):
    parts_in, each, _ = rows.shape
    count, vocab = parts_in * each, table.shape[0]
    last = pl.cdiv(vocab, VOCAB_TILE) - 1
    turns = last // 2 + 1

    def kernel(x_hbm, even_ref, odd_ref, after_ref, out_hbm, *refs):
        x_ref, out_ref, acc, top, total, l_even, l_odd, p_even, p_odd, sems = refs
        turn = pl.program_id(0)

        def entries_of(ref, tile):
            row = lax.broadcasted_iota(jnp.int32, (VOCAB_TILE, 1), 0)
            return jnp.where(row < vocab - tile * VOCAB_TILE, ref[...], jnp.zeros_like(ref))

        @pl.when(turn == 0)
        def _():
            copy = pltpu.make_async_copy(x_hbm, x_ref, sems.at[0])
            copy.start()
            acc[...] = jnp.zeros_like(acc)
            top[...] = jnp.full_like(top, -1e30)
            total[...] = jnp.zeros_like(total)
            entries = entries_of(even_ref, 0)
            copy.wait()
            l_even[...] = matmul_t(x_ref[...], entries)

        even = entries_of(even_ref, 2 * turn)
        odd = entries_of(odd_ref, 2 * turn + 1)
        after = entries_of(after_ref, 2 * turn + 2)
        for tile, l_now, p_now, now, l_later, later in (
            (2 * turn, l_even, p_even, even, l_odd, odd),
            (2 * turn + 1, l_odd, p_odd, odd, l_even, after),
        ):
            bias = key_bias(vocab - tile * VOCAB_TILE, (1, VOCAB_TILE), 1)
            for at in rows_of(count, SMALL_ROWS):
                logits = l_now[at] + bias
                earlier = top[at]
                highest = jnp.maximum(earlier, jnp.max(logits, 1, keepdims=True))
                exponent = jnp.exp(logits - highest)
                factor = jnp.exp(earlier - highest)
                top[at] = highest
                total[at] = total[at] * factor + jnp.sum(exponent, 1, keepdims=True)
                p_now[at] = low(exponent)
                acc[at] = acc[at] * factor
            l_later[...] = matmul_t(x_ref[...], later)
            acc[...] += matmul(p_now[...], now)

        @pl.when(turn == turns - 1)
        def _():
            out_ref[:, :D] = low(acc[...])
            out_ref[:, D:] = head_stats(top[...], total[...])
            copy = pltpu.make_async_copy(out_ref, out_hbm, sems.at[1])
            copy.start()
            copy.wait()

    def tile_at(shift):
        return pl.BlockSpec((VOCAB_TILE, D), lambda j: (jnp.minimum(2 * j + shift, last), 0))

    hbm = pl.BlockSpec(memory_space=pltpu.HBM)
    return pl.pallas_call(
        kernel,
        grid=(turns,),
        in_specs=[hbm] + [tile_at(shift) for shift in range(3)],
        out_specs=hbm,
        out_shape=shape_of(count, D + LANES, kind=BF16),
        scratch_shapes=[
            pltpu.VMEM((count, D), BF16),
            pltpu.VMEM((count, D + LANES), BF16),
            pltpu.VMEM((count, D), F32),
            pltpu.VMEM((count, 1), F32),
            pltpu.VMEM((count, 1), F32),
            pltpu.VMEM((count, VOCAB_TILE), F32),
            pltpu.VMEM((count, VOCAB_TILE), F32),
            pltpu.VMEM((count, VOCAB_TILE), BF16),
            pltpu.VMEM((count, VOCAB_TILE), BF16),
            pltpu.SemaphoreType.DMA((2,)),
        ],
        compiler_params=params_for(MOST_VMEM),
        name="vocabulary_head",
    )(rows.reshape(count, D), table, table, table).reshape(parts_in, each, D + LANES)


def swap_add(own, other):
    came = lax.ppermute(low(other), "section", [(0, 1), (1, 0)])
    return own + came.astype(F32)


def pick(first_section, both):
    return jnp.where(first_section, both[0], both[1])


def plan_requests(ids, weights, vocab_rows, slots, parts):
    turned = jnp.transpose(ids)

    def kernel(ids_ref, turned_ref, weights_ref, asked_ref, code_ref, spot_ref):
        here = lax.axis_index("section")
        i_index = lax.broadcasted_iota(jnp.int32, (IDS, IDS), 0)
        j_index = lax.broadcasted_iota(jnp.int32, (IDS, IDS), 1)
        earlier, later = j_index < i_index, i_index < j_index

        def owner_of(values):
            return jnp.floor((values.astype(F32) + 0.5) * (1.0 / vocab_rows)).astype(jnp.int32)

        def count(hits, axis):
            return jnp.sum(hits.astype(F32), axis, keepdims=True)

        most = jnp.zeros((1, 1), F32)
        for m in range(MICRO):
            row, col = ids_ref[m : m + 1], turned_ref[:, m : m + 1]
            same_id = row == col
            first_col = count(same_id & earlier, 1) == 0
            first_row = count(same_id & later, 0) == 0
            owner_row, owner_col = owner_of(row), owner_of(col)
            same_owner = owner_row == owner_col
            rank_row = count(same_owner & later & first_col, 0)
            rank_col = count(same_owner & earlier & first_row, 1)
            most = jnp.maximum(most, jnp.max(rank_row, 1, keepdims=True))

            @pl.when(here == m)
            def _():
                slot_row = jnp.sum(jnp.where(same_id & first_col, rank_col, 0.0), 0, keepdims=True)
                slot_col = jnp.sum(jnp.where(same_id & first_row, rank_row, 0.0), 1, keepdims=True)
                slot_row, slot_col = slot_row.astype(jnp.int32), slot_col.astype(jnp.int32)
                code_ref[...] = (owner_row + parts * first_row.astype(jnp.int32)) * 1024 + slot_row
                spot = jnp.where(slot_col < slots, owner_col * slots + slot_col, -1)
                spot_ref[...] = jnp.broadcast_to(spot, (IDS, LANES))
                lane = lax.broadcasted_iota(jnp.int32, (IDS, LANES), 1)
                local = (col - owner_col * vocab_rows).astype(F32)
                wanted = first_col & (slot_col < slots) & (slot_col == lane)
                wanted = jnp.where(wanted, local, 0.0)
                for part in range(parts):
                    asked = jnp.sum(jnp.where(owner_col == part, wanted, 0.0), 0, keepdims=True)
                    asked_ref[part] = asked.astype(jnp.int32)

        rounds = jnp.floor((most + 0.5) * (1.0 / slots)).astype(jnp.int32) + 1
        total = jnp.sum(jnp.sum(weights_ref[...], 0, keepdims=True), 1, keepdims=True)
        lane = lax.broadcasted_iota(jnp.int32, (1, LANES), 1)
        for part in range(parts):
            row = asked_ref[part]
            asked_ref[part] = jnp.where(lane == slots, rounds, jnp.where(lane == slots + 1, total, row))

    return pl.pallas_call(
        kernel,
        out_shape=[
            jax.ShapeDtypeStruct((parts, 1, LANES), jnp.int32),
            jax.ShapeDtypeStruct((1, IDS), jnp.int32),
            jax.ShapeDtypeStruct((IDS, LANES), jnp.int32),
        ],
        compiler_params=params_for(24),
        name="plan_requests",
    )(ids, turned, weights)


def fetch_rows(table, ids, first_section, plan, slots):
    parts = lax.axis_size("dp")
    vocab_rows = table.shape[0]
    asked, code, spot = plan
    asked = lax.all_to_all(asked, "dp", 0, 0)[:, 0]
    total_rounds = jnp.max(asked[:, slots])
    weight_sum = jnp.sum(asked[:, slots + 1])

    def answer(asked):
        rows = table.at[asked.reshape(-1)].get(mode="promise_in_bounds").reshape(parts, slots, D)
        return lax.all_to_all(rows, "dp", 0, 0).reshape(parts * slots, D)

    came = answer(asked[:, :slots])

    def more(state):
        return state[0] < total_rounds

    def another(state):
        turn, extra = state
        place, slot = code[0] // 1024, code[0] % 1024
        owner, first = place % parts, place >= parts
        local = pick(first_section, ids) - owner * vocab_rows
        here = slot - turn * slots
        at = jnp.where((here >= 0) & (here < slots), owner * slots + here, -1)
        hits = at[:, None] == jnp.arange(parts * slots)[None, :]
        wanted = jnp.sum(jnp.where(hits & first[:, None], local[:, None], 0), 0).reshape(parts, slots)
        rows = answer(lax.all_to_all(wanted, "dp", 0, 0))
        return turn + 1, extra + matmul(hits.astype(BF16), rows)

    extra = lax.while_loop(more, another, (jnp.int32(1), jnp.zeros((IDS, D), F32)))[1]
    return came, spot, extra, total_rounds, weight_sum.astype(F32)


def three_low(values):
    high = low(values)
    rest = values - high.astype(F32)
    middle = low(rest)
    return [high, middle, low(rest - middle.astype(F32))]


def in_groups(count):
    return lax.axis_size("dp") == COUPLING_GROUPS and count == 4 * PART_GROUPS


LINES = 4


def plane_groups(parts):
    planes = parts // LINES
    across_planes = [[plane * LINES + line for plane in range(planes)] for line in range(LINES)]
    return across_planes, [[plane * LINES + line for line in range(LINES)] for plane in range(planes)]


def gather_params(master, vector, after):
    parts = lax.axis_size("dp")
    count, width = master.shape[0], vector.shape[0]
    if in_groups(count):
        across_planes, in_plane = plane_groups(parts)
        some = pack_own(master, vector[None], len(in_plane))
        some = lax.all_to_all(some, "dp", 0, 0, axis_index_groups=across_planes)
        some, after = lax.optimization_barrier((some, after))
        own = lax.all_gather(some, "dp", axis_index_groups=in_plane)
        return *unpack_all(own, lax.ppermute(own, "section", [(0, 1), (1, 0)]), width), after
    flat = low(jnp.concatenate([master.reshape(-1), vector]))
    gathered = lax.all_gather(flat, ("section", "dp")).reshape(MICRO, parts, -1)
    size = count * BLOCK**2
    all_blocks = gathered[:, :, :size].reshape(MICRO, parts * count, BLOCK, BLOCK)
    all_vectors = gathered[:, :, size:].reshape(MICRO, parts * width)
    both = [split_params(all_blocks[s], all_vectors[s]) for s in range(MICRO)]

    def stacked(which):
        down, bias_down, up, bias_up = (jnp.stack([pair[which][i] for pair in both]) for i in range(4))
        return Params(down, bias_down.astype(F32)[:, None], up, bias_up.astype(F32)[:, None])

    return stacked(0), stacked(1), after


def sum_at_owners(grads, loss_part, count):
    parts = lax.axis_size("dp")
    width = sum(BIASES) // parts
    flat = []
    for adapter, coupling in grads:
        blocks, vector = join_params(adapter, coupling)
        flat.append(
            jnp.concatenate([blocks.reshape(parts, count * BLOCK**2), vector.reshape(parts, width)], 1)
        )
    first = lax.axis_index("section") == 0
    summed = swap_add(jnp.where(first, flat[0], flat[1]), jnp.where(first, flat[1], flat[0]))
    owned = jnp.sum(lax.all_to_all(low(summed), "dp", 0, 0).astype(F32), 0)
    blocks = owned[: count * BLOCK**2].reshape(count, BLOCK, BLOCK)
    pair = jnp.stack([jnp.sum(owned * owned), loss_part[0, 0]])
    pair = jnp.pad(pair, (0, LANES - 2))[None, None]
    return blocks, owned[count * BLOCK**2 :], jnp.broadcast_to(pair, (parts * MICRO, 8, LANES))


def to_coupling_owners(group):
    arrived = []
    for place in range(1, PART_GROUPS):
        route = []
        for i, part in enumerate(SUMMED_AT):
            owner, at = divmod(ADAPTER_GROUPS + i, PART_GROUPS)
            if at == place and owner != part:
                route.append((part, owner))
        arrived.append(lax.ppermute(group, "dp", route))
    return [group] + arrived


def exact(spec, left, right):
    return jnp.einsum(spec, left, right, precision=HIGHEST)


def update(pair, products, turned_old, grad_vector, state):
    master, momentum, stat_left, stat_right, vectors, vec_first, vec_second = state
    grad, left_square, right_square, turned = products

    blocks = (1,) + grad.shape
    outs = [shape_of(*blocks)] * 5 + [low_shape(*blocks)] + [shape_of(*vectors.shape)] * 3 + [shape_of(1, 1)] * 2

    def body(ins, out, scalar_refs, pair_refs, raw_refs, scratch):
        start(ins)
        (pair_ref, grad_ref, left_ref, right_ref, turned_ref, vector_ref, old_ref), ins = (
            [operand.get() for operand in ins[:7]],
            [operand.get() for operand in ins[7:]],
        )
        master_ref, momentum_ref, stat_left_ref, stat_right_ref, vectors_ref, first_ref, second_ref = ins
        outs = [result.buffer for result in out]
        totals = jnp.sum(pair_ref[...], 0)[:1]
        norm = jnp.sqrt(totals[:, :1])
        factor = CLIP_NORM / jnp.maximum(norm, CLIP_NORM)
        outs[9][...] = norm
        outs[10][...] = totals[:, 1:2]
        square = (1.0 - STAT_DECAY) * factor * factor
        for n in range(grad_ref.shape[0]):
            clipped = grad_ref[n] * factor
            outs[0][0, n] = clipped
            outs[1][0, n] = FIRST_DECAY * momentum_ref[n] + (1.0 - FIRST_DECAY) * clipped
            outs[2][0, n] = STAT_DECAY * stat_left_ref[n] + square * left_ref[n]
            outs[3][0, n] = STAT_DECAY * stat_right_ref[n] + square * right_ref[n]
            direction = FIRST_DECAY * old_ref[n] + (1.0 - FIRST_DECAY) * factor * turned_ref[n]
            master_new = master_ref[n] - MAT_RATE * (direction + MAT_DECAY * master_ref[n])
            outs[4][0, n] = master_new
            outs[5][0, n] = low(master_new)
        clipped = vector_ref[...] * factor
        first_new = FIRST_DECAY * first_ref[...] + (1.0 - FIRST_DECAY) * clipped
        second_new = VEC_SECOND * second_ref[...] + (1.0 - VEC_SECOND) * clipped * clipped
        outs[6][...] = first_new
        outs[7][...] = second_new
        corrected_first = first_new / (1.0 - FIRST_DECAY**STEP)
        corrected_second = second_new / (1.0 - VEC_SECOND**STEP)
        outs[8][...] = vectors_ref[...] - VEC_RATE * (
            corrected_first / (jnp.sqrt(corrected_second) + VEC_EPS) + VEC_DECAY * vectors_ref[...]
        )

    ins = [pair, grad, left_square, right_square, turned, grad_vector, turned_old]
    ins += [master, momentum, stat_left, stat_right, vectors, vec_first, vec_second]
    return moved_call(body, (), ins, outs, (), [], "update")[0]


def shards(
    token_ids,
    lengths,
    positions,
    targets,
    loss_weights,
    embed_table,
    pos_table,
    norm_params,
    base_qkv,
    base_out,
    base_up,
    base_down,
    master,
    momentum,
    stat_left,
    stat_right,
    root_left,
    root_right,
    vectors,
    vec_first,
    vec_second,
):
    parts = lax.axis_size("dp")
    first_section = lax.axis_index("section") == 0
    slots = -(-IDS * 5 // (4 * parts * 16)) * 16

    ids = jnp.concatenate([token_ids[:, 0], targets[:, 0]], -1)
    asked, *plan = plan_requests(ids, loss_weights[:, 0], embed_table.shape[0], slots, parts)
    adapter, coupling, asked = gather_params(master[0], vectors[0], asked)
    swap = [(0, 1), (1, 0)]
    pairs = [(w, lax.ppermute(w, "section", swap)) for w in (base_qkv, base_out, base_up, base_down)]
    came = lax.ppermute(norm_params, "section", swap)
    norms = jnp.concatenate([pick(first_section, (norm_params, came)), pick(first_section, (came, norm_params))])

    came, spot, extra, rounds, weight_sum = fetch_rows(embed_table, ids, first_section, (asked, *plan), slots)
    turned_old = exact("nij,njk->nik", exact("nij,njk->nik", root_left[0], momentum[0]), root_right[0])
    spot, turned_old = lax.optimization_barrier((spot, turned_old))
    length = pick(first_section, lengths)
    spots = pick(first_section, positions[:, 0])
    row_weights = pick(first_section, loss_weights[:, 0]).astype(F32)
    chosen = (spots[:, None] == jnp.arange(SEQ)[None, :]).astype(BF16)
    chosen_t = (spots[None, :] == jnp.arange(SEQ)[:, None]).astype(F32)

    ins = ForwardIn(came, spot, extra, pos_table, norms, chosen, adapter, coupling)
    kept, rows = forward_kernel(ins, (length, rounds.reshape(1)), pairs, parts, slots)

    spread = [lax.all_to_all(half, "dp", 0, 0) for half in rows]
    first_half, spread[1] = lax.optimization_barrier((head_kernel(spread[0], embed_table), spread[1]))
    halves = [first_half, head_kernel(spread[1], embed_table)]
    merged = [lax.all_to_all(half, "dp", 0, 0) for half in halves]

    packed = in_groups(master.shape[1])
    row_weights = jnp.broadcast_to(row_weights[:, None], (COUNT, LANES))
    weight_row = jnp.broadcast_to(weight_sum, (1, LANES))
    adapter, coupling = adapter[::2], coupling[::2]
    adapter_kept = kept.rest_0._replace(slope=(), normal_1=(), inverse_1=())
    ins = BackIn(
        merged, row_weights, weight_row, norms, chosen_t, adapter, coupling,
        kept.target_rows, adapter_kept, kept.attention_1, kept.rest_1, kept.last,
    )
    back = backward_kernel(ins, (length,), pairs, packed)
    loss_part, inner = back.loss, back.inner
    if packed:
        own, other = back.adapters[MICRO:]
        summed = low(swap_add(own.astype(F32), other))
        summed, inner = lax.optimization_barrier((summed, inner))
        adapter_came = lax.all_to_all(summed, "dp", 0, 0)
    inner_kept = kept.rest_0.slope, kept.rest_0.normal_1, kept.rest_0.inverse_1
    ins = FirstIn(
        inner, norms, inner_kept, kept.attention_0, coupling, kept.one, kept.two, back.one, back.two,
        back.adapters[:MICRO] if packed else (),
    )
    grads = first_backward(ins, (length,), pairs, packed)
    if packed:
        adapter_total, squares = sum_adapter(adapter_came)
        came = lax.all_to_all(low(swap_add(*grads)), "dp", 0, 0)
        group, bias, pair = sum_coupling(came, squares, loss_part, parts * MICRO)
        products = grad_products(adapter_total, to_coupling_owners(group), root_left[0], root_right[0])
        grad_vector = bias[:1, : vectors.shape[1]]
    else:
        both = [(back.adapters[s], grads[4 * s : 4 * s + 4]) for s in range(MICRO)]
        grad, grad_vector, pair = sum_at_owners(both, loss_part, master.shape[1])
        turned = exact("nij,njk->nik", exact("nij,njk->nik", root_left[0], grad), root_right[0])
        products = grad, exact("nij,nkj->nik", grad, grad), exact("nji,njk->nik", grad, grad), turned
        grad_vector = grad_vector[None]
    pair = lax.all_to_all(pair, ("dp", "section"), 0, 0)
    state = (master, momentum, stat_left, stat_right)
    *outs, grad_norm, loss_sum = update(
        pair, products, turned_old, grad_vector, [value[0] for value in state] + [vectors, vec_first, vec_second]
    )
    return (*outs, grad_norm[0, 0], loss_sum[0, 0], weight_sum)


def solution(mesh):
    rows = P(None, "dp", None)
    section = P("section", None, None)
    blocks = P("section", "dp", None, None)
    biases = P("section", "dp")
    return jax.shard_map(
        shards,
        mesh=mesh,
        in_specs=(rows, P(None, "dp"), rows, rows, rows, P("dp", None), P())
        + (section,) * 5
        + (blocks,) * 6
        + (biases,) * 3,
        out_specs=(blocks,) * 6 + (biases,) * 3 + (P(),) * 3,
        check_vma=False,
    )
```

```python
import functools
from typing import Any, NamedTuple

import jax
import jax.numpy as jnp
import numpy as np
from jax import lax
from jax.experimental import pallas as pl
from jax.experimental.pallas import tpu as pltpu
from jax.sharding import PartitionSpec as P

D = 768
HEADS = 12
HEAD_DIM = 64
BOT = 384
INV_H = 192
SEQ = 512
COUNT = 32
MICRO = 2
BLOCK = 48
STEP = 10
HALF = 384
IDS = SEQ + COUNT

HIGHEST = lax.Precision.HIGHEST
NORM_EPS = 1e-12
CLIP_NORM = 0.02
FIRST_DECAY = 0.9
STAT_DECAY = 0.99
MAT_RATE = 0.1
MAT_DECAY = 0.01
VEC_RATE = 0.05
VEC_SECOND = 0.999
VEC_EPS = 1e-08
VEC_DECAY = 0.01
F32 = jnp.float32
BF16 = jnp.bfloat16

CDF_SCALE = 0.42 / 2.0**0.5
CDF_POLY = (
    0.2368242366796694,
    0.239585811361218,
    0.1947261443420679,
    0.2687426685879861,
    -0.13052645834187002,
    0.4406726942003943,
    -0.32025628294963193,
    0.07023101752398136,
)


def matmul(left, right):
    return jnp.dot(left, right, preferred_element_type=F32)


def matmul_t(left, right):
    return lax.dot_general(left, right, (((1,), (1,)), ((), ())), preferred_element_type=F32)


def inner_rows(left, right):
    return lax.dot_general(left, right, (((0,), (0,)), ((), ())), preferred_element_type=F32)


def low(values):
    return values.astype(BF16)


def in_strips(size, function, *arrays):
    count = arrays[0].shape[0]
    strips = [slice(at, at + size) for at in range(0, count, size)] if count % size == 0 else [slice(0, count)]
    results = [function(*[array[strip] for array in arrays]) for strip in strips]
    return tuple(jnp.concatenate(parts, 0) if len(parts) > 1 else parts[0] for parts in zip(*results))


def gelu_both(values):
    return in_strips(16, gelu_strip, values)


def gelu_strip(values):
    below = 1.0 + CDF_SCALE * jnp.abs(values)
    ratio = pl.reciprocal(below, approx=True)
    ratio = ratio * (2.0 - below * ratio)
    poly = jnp.full_like(ratio, 0.5 * CDF_POLY[-1])
    for factor in CDF_POLY[-2::-1]:
        poly = poly * ratio + 0.5 * factor
    bell = jnp.exp(-0.5 * values * values)
    tail = bell * (poly * ratio)
    cdf = jnp.where(values < 0, tail, 1.0 - tail)
    return values * cdf, cdf + values * (bell * (2.0 * np.pi) ** -0.5)


def layer_norm(values, gain, shift):
    def strip(values):
        centered = values - jnp.mean(values, -1, keepdims=True)
        inverse = lax.rsqrt(jnp.mean(centered * centered, -1, keepdims=True) + NORM_EPS)
        normal = centered * inverse
        return normal * gain + shift, normal, inverse

    values, normal, inverse = in_strips(16, strip, values)
    return values, (normal, inverse)


def norm_back(incoming, kept, gain):
    def strip(incoming, normal, inverse):
        scaled = incoming * gain
        mean = jnp.mean(scaled, -1, keepdims=True)
        return (inverse * (scaled - mean - normal * jnp.mean(scaled * normal, -1, keepdims=True)),)

    return in_strips(16, strip, incoming, *kept)[0]


def to_blocks(matrix):
    rows_in, cols_in = matrix.shape
    return (
        matrix.reshape(rows_in // BLOCK, BLOCK, cols_in // BLOCK, BLOCK)
        .transpose(0, 2, 1, 3)
        .reshape(-1, BLOCK, BLOCK)
    )


def from_blocks(blocks, rows_in, cols_in):
    return (
        blocks.reshape(rows_in // BLOCK, cols_in // BLOCK, BLOCK, BLOCK)
        .transpose(0, 2, 1, 3)
        .reshape(rows_in, cols_in)
    )


def split_params(blocks, vector):
    adapter_count = D * BOT // BLOCK**2
    half_count = HALF * INV_H // BLOCK**2
    split_at = 2 * adapter_count
    adapter = (
        from_blocks(blocks[:adapter_count], D, BOT),
        vector[:BOT],
        from_blocks(blocks[adapter_count:split_at], BOT, D),
        vector[BOT : BOT + D],
    )
    coupling = (
        from_blocks(blocks[split_at : split_at + half_count], HALF, INV_H),
        vector[BOT + D : BOT + D + INV_H],
        from_blocks(blocks[split_at + half_count :], INV_H, HALF),
        vector[BOT + D + INV_H :],
    )
    return adapter, coupling


def join_params(adapter, coupling):
    blocks = jnp.concatenate(
        [to_blocks(adapter[0]), to_blocks(adapter[2]), to_blocks(coupling[0]), to_blocks(coupling[2])]
    )
    return blocks, jnp.concatenate([adapter[1], adapter[3], coupling[1], coupling[3]], 1)[0]


GROUP_ROWS = 72
LANES = 128


def params_for(mebibytes):
    return pltpu.CompilerParams(vmem_limit_bytes=mebibytes * 2**20)


def roll(values, shift):
    return pltpu.roll(values, shift, 1)


def lane_of(values):
    return lax.broadcasted_iota(jnp.int32, values.shape, 1)


def fold_half(values, upper):
    top, bottom = values[:24], values[24:]
    if upper:
        return jnp.where(lane_of(top) < 64, roll(top, 64), bottom)
    return jnp.where(lane_of(top) < 64, top, roll(bottom, 64))


def unfold_half(values, upper):
    turned = roll(values, 64)
    return jnp.concatenate([turned, values] if upper else [values, turned], 0)


def join_pair(main_0, rest_0, main_1, rest_1):
    left = lane_of(main_0) < 64
    turned = roll(main_1, 64)
    return (
        main_0,
        jnp.where(left, unfold_half(rest_0, False), turned),
        jnp.where(left, turned, unfold_half(rest_1, True)),
    )


def cut_pair(tile_0, tile_1, tile_2):
    left = lane_of(tile_0) < 64
    return (
        (tile_0, fold_half(tile_1, False)),
        (jnp.where(left, roll(tile_1, 64), roll(tile_2, 64)), fold_half(tile_2, True)),
    )


def chunk_rows(own_blocks):
    return own_blocks // 4 * GROUP_ROWS + 8


def bias_row(tiles, part, width):
    at, shift = divmod(part * width, LANES)
    lane = lane_of(tiles[0])
    row = tiles[at]
    if shift:
        row = jnp.where(lane < LANES - shift, roll(row, LANES - shift), roll(tiles[at + 1], LANES - shift))
    return jnp.where(lane < width, row, 0.0)


def bias_tiles(first, second, third, fourth):
    cut = lambda values: [values[:, at : at + LANES] for at in range(0, values.shape[1], LANES)]
    zero = jnp.zeros((1, LANES), F32)
    left = lane_of(zero) < 64
    third_tail = jnp.concatenate([third[:, LANES:]] * 2, 1)
    turned = [roll(tile, 64) for tile in cut(fourth)]
    joints = [jnp.where(left, one, two) for one, two in zip([third_tail] + turned, turned + [zero])]
    return cut(first) + cut(second) + [third[:, :LANES]] + joints + [zero]


def tiles_of_rows(rows, width):
    tiles = []
    for tile in range(-(-len(rows) * width // LANES)):
        value = jnp.zeros((8, LANES), F32)
        lane = lane_of(value)
        for part, row in enumerate(rows):
            shift = part * width - tile * LANES
            if shift >= LANES or shift + width <= 0:
                continue
            turned = roll(row, shift % LANES) if shift % LANES else row
            value = jnp.where((lane >= shift) & (lane < shift + width), turned, value)
        tiles.append(value)
    return tiles


def pack_own(master, vector, copies):
    count, width = master.shape[0], vector.shape[1]

    def kernel(master_ref, bias_ref, out_ref):
        row = lax.broadcasted_iota(jnp.int32, (BLOCK, 256), 0)
        col = lax.broadcasted_iota(jnp.int32, (BLOCK, 256), 1)
        pieces = []
        for group in range(count // 4):
            wide = jnp.zeros((BLOCK, 256), F32)
            for j in range(4):
                wide += matmul(low(master_ref[4 * group + j]), (col == row + BLOCK * j).astype(BF16))
            pieces += [wide[:, :LANES], fold_half(wide[:, LANES:], False)]
        bias = jnp.concatenate([bias_ref[...], jnp.zeros((1, LANES - width), F32)], 1)
        pieces.append(jnp.concatenate([bias, jnp.zeros((7, LANES), F32)], 0))
        packed = low(jnp.concatenate(pieces, 0))
        for copy in range(copies):
            out_ref[copy] = packed

    return pl.pallas_call(
        kernel,
        out_shape=jax.ShapeDtypeStruct((copies, chunk_rows(count), LANES), BF16),
        name="pack_own",
    )(master, vector)


MATRICES = ((D, BOT), (BOT, D), (HALF, INV_H), (INV_H, HALF))
BIASES = (BOT, D, INV_H, HALF)


def unpack_all(own, came, width):
    lines, planes, rows, _ = own.shape
    parts = lines * planes
    per_part = (rows - 8) // GROUP_ROWS

    def kernel(own_hbm, came_hbm, *refs):
        out_hbm, in_bufs, out_refs, in_sems, out_sems = refs[:8], refs[8], refs[9:17], refs[17], refs[18]
        here = lax.axis_index("section")
        copies = [
            pltpu.make_async_copy(ref, in_bufs.at[at], in_sems.at[i])
            for i, (ref, at) in enumerate(((own_hbm, here), (came_hbm, 1 - here)))
        ]
        for copy in copies:
            copy.start()
        for copy in copies:
            copy.wait()

        def unpack(s, carry):
            cache = {}

            def group(index):
                part = index // per_part
                if part not in cache:
                    cache.clear()
                    cache[part] = in_bufs[s, part % lines, part // lines].astype(F32)
                base = index % per_part * GROUP_ROWS
                chunk = cache[part]
                return chunk[base : base + BLOCK], chunk[base + BLOCK : base + GROUP_ROWS]

            index = 0
            for (height, columns), out_ref in zip(MATRICES, out_refs):
                for top in range(0, height, BLOCK):
                    if columns == INV_H:
                        main, rest = group(index)
                        index += 1
                        out_ref[s, top : top + BLOCK, :LANES] = low(main)
                        out_ref[s, top : top + BLOCK, LANES:] = low(unfold_half(rest, False)[:, :64])
                        continue
                    for left in range(0, columns, HALF):
                        tiles = join_pair(*group(index), *group(index + 1))
                        index += 2
                        for j, tile in enumerate(tiles):
                            at = left + j * LANES
                            out_ref[s, top : top + BLOCK, at : at + LANES] = low(tile)
            tiles = tiles_of_rows(
                [in_bufs[s, part % lines, part // lines, rows - 16 :].astype(F32)[8:] for part in range(parts)], width
            )
            first, second, third, fourth = out_refs[4:]
            first[s] = jnp.concatenate(tiles[:3], 1)[:1]
            second[s] = jnp.concatenate(tiles[3:9], 1)[:1]
            third[s] = jnp.concatenate([tiles[9], tiles[10][:, :64]], 1)[:1]
            left = lane_of(tiles[0]) < 64
            turned = [roll(tile, 64) for tile in tiles[10:14]]
            fourth[s] = jnp.concatenate(
                [jnp.where(left, one, two) for one, two in zip(turned, turned[1:])], 1
            )[:1]
            return carry

        lax.fori_loop(0, MICRO, unpack, 0)
        copies = [
            pltpu.make_async_copy(buf, ref, out_sems.at[i]) for i, (buf, ref) in enumerate(zip(out_refs, out_hbm))
        ]
        for copy in copies:
            copy.start()
        for copy in copies:
            copy.wait()

    shapes = [((MICRO,) + shape, BF16) for shape in MATRICES] + [((MICRO, 1, size), F32) for size in BIASES]
    hbm = pl.BlockSpec(memory_space=pltpu.HBM)
    arrays = pl.pallas_call(
        kernel,
        in_specs=[hbm] * 2,
        out_specs=[hbm] * 8,
        out_shape=[jax.ShapeDtypeStruct(*shape) for shape in shapes],
        scratch_shapes=[pltpu.VMEM((MICRO, lines, planes, rows, LANES), BF16)]
        + [pltpu.VMEM(*shape) for shape in shapes]
        + [pltpu.SemaphoreType.DMA((2,)), pltpu.SemaphoreType.DMA((8,))],
        compiler_params=params_for(MOST_VMEM),
        name="unpack_all",
    )(own, came)
    down, up, c_down, c_up, bias_down, bias_up, c_bias_down, c_bias_up = arrays
    return Params(down, bias_down, up, bias_up), Params(c_down, c_bias_down, c_up, c_bias_up)


ADAPTER_GROUPS = 2 * D * BOT // BLOCK**2 // 4
COUPLING_GROUPS = 2 * HALF * INV_H // BLOCK**2 // 4
PART_GROUPS = (ADAPTER_GROUPS + COUPLING_GROUPS) // COUPLING_GROUPS
PART_ROWS = PART_GROUPS * GROUP_ROWS
SUMMED_AT = (12, 13, 1, 5, 9, 0, 14, 2, 6, 10, 4, 15, 3, 7, 11, 8)


def groups_of(refs, shapes):
    groups = []
    for ref, (height, width) in zip(refs, shapes):
        for top in range(0, height, BLOCK):
            band = slice(top, top + BLOCK)
            if width == INV_H:
                tail = ref[band, LANES:]
                groups.append((ref[band, :LANES], fold_half(jnp.concatenate([tail, tail], 1), False)))
                continue
            for left in range(0, width, HALF):
                groups += cut_pair(*[ref[band, left + j * LANES : left + (j + 1) * LANES] for j in range(3)])
    return [jnp.concatenate(group, 0) for group in groups]


def pack_adapter(refs, store):
    groups = groups_of(refs, MATRICES[:2])
    empty = jnp.zeros((GROUP_ROWS, LANES), F32)
    for part in range(COUPLING_GROUPS):
        chunk = groups[part * PART_GROUPS : (part + 1) * PART_GROUPS]
        chunk += [empty] * (PART_GROUPS - len(chunk))
        store(part, low(jnp.concatenate(chunk, 0)))


def pack_coupling(refs, tiles, width, store):
    for part, group in zip(SUMMED_AT, groups_of(refs, MATRICES[2:])):
        bias = jnp.concatenate([bias_row(tiles, part, width), jnp.zeros((7, LANES), F32)], 0)
        store(part, jnp.concatenate([group, bias], 0))


def sum_parts(came_ref):
    total = came_ref[0].astype(F32)
    for part in range(1, came_ref.shape[0]):
        total += came_ref[part].astype(F32)
    return total


def square_sum(values):
    return jnp.sum(jnp.sum(values * values, 0, keepdims=True), 1, keepdims=True)


def sum_adapter(came):
    def kernel(came_ref, total_ref, square_ref):
        total = sum_parts(came_ref)
        total_ref[...] = total
        square_ref[...] = square_sum(total)

    return pl.pallas_call(
        kernel,
        out_shape=[jax.ShapeDtypeStruct((PART_ROWS, LANES), F32), jax.ShapeDtypeStruct((1, 1), F32)],
        compiler_params=params_for(32),
        name="sum_adapter",
    )(came)


def sum_coupling(came, squares, loss_part, copies):
    def kernel(came_ref, square_ref, loss_ref, group_ref, bias_ref, pair_ref):
        total = sum_parts(came_ref)
        group_ref[...] = total[:GROUP_ROWS]
        bias_ref[...] = total[GROUP_ROWS:]
        squares = square_ref[...] + square_sum(total)
        lane = lax.broadcasted_iota(jnp.int32, (8, LANES), 1)
        pair = jnp.where(lane == 0, squares, jnp.where(lane == 1, loss_ref[:, :1], 0.0))
        for copy in range(copies):
            pair_ref[copy] = pair

    return pl.pallas_call(
        kernel,
        out_shape=[
            jax.ShapeDtypeStruct((GROUP_ROWS, LANES), F32),
            jax.ShapeDtypeStruct((8, LANES), F32),
            jax.ShapeDtypeStruct((copies, 8, LANES), F32),
        ],
        name="sum_coupling",
    )(came, squares, loss_part)


def exact_dot(left, right, dims):
    return lax.dot_general(left, right, (dims, ((), ())), precision=HIGHEST, preferred_element_type=F32)


def unpack_own(total_ref, own_ref, group_refs, grad_ref):
    part = lax.axis_index("dp")
    own_place = jnp.int32(-1)
    for i, owner in enumerate(SUMMED_AT):
        at = ADAPTER_GROUPS + i
        if at // PART_GROUPS == owner:
            own_place = jnp.where(part == owner, at % PART_GROUPS, own_place)
    for group in range(PART_GROUPS):
        total = total_ref[group * GROUP_ROWS : (group + 1) * GROUP_ROWS]
        total = total + jnp.where(own_place == group, own_ref[...], 0.0)
        if group:
            total = total + group_refs[group - 1][...]
        main, rest = total[:BLOCK], unfold_half(total[BLOCK:], False)
        lane = lane_of(main)
        pieces = (
            main,
            roll(main, 80),
            jnp.where(lane < 32, roll(main, 32), roll(rest, 32)),
            roll(rest, 112),
        )
        for j, values in enumerate(pieces):
            grad_ref[4 * group + j] = values[:, :BLOCK]


MOST_VMEM = 64
GROUP = 256
HEADS_IN = GROUP // HEAD_DIM
GROUPS = D // GROUP
FF = 3072
TILE = 512
TILES = FF // TILE
STEP_ROWS = 256
SMALL_ROWS = 16


def rows_of(count, size):
    return [slice(at, at + min(size, count)) for at in range(0, count, size)]


def shape_of(*dims, kind=F32):
    return jax.ShapeDtypeStruct(dims, kind)


class Params(NamedTuple):
    down: Any
    bias_down: Any
    up: Any
    bias_up: Any


class Branch(NamedTuple):
    lin: Any
    act: Any
    slope: Any


class Attention(NamedTuple):
    query: Any
    key: Any
    value: Any
    lse: Any


class Rest(NamedTuple):
    normal_1: Any
    inverse_1: Any
    slope: Any
    branch: Any
    normal_2: Any
    inverse_2: Any


class Last(NamedTuple):
    one: Any
    two: Any
    normal: Any
    inverse: Any
    normed: Any


class ForwardIn(NamedTuple):
    came: Any
    spot: Any
    extra: Any
    pos: Any
    norms: Any
    chosen: Any
    adapter: Any
    coupling: Any


class Forward(NamedTuple):
    target_rows: Any
    one: Any
    two: Any
    attention_0: Any
    rest_0: Any
    attention_1: Any
    rest_1: Any
    last: Any


class BackIn(NamedTuple):
    merged: Any
    row_weights: Any
    weight_sum: Any
    norms: Any
    chosen_t: Any
    adapter: Any
    coupling: Any
    target_rows: Any
    rest_0: Any
    attention_1: Any
    rest_1: Any
    last: Any


class Back(NamedTuple):
    loss: Any
    one: Any
    two: Any
    adapters: Any
    inner: Any


class FirstIn(NamedTuple):
    inner: Any
    norms: Any
    inner_kept: Any
    attention: Any
    coupling: Any
    one: Any
    two: Any
    grads_one: Any
    grads_two: Any
    biases: Any


class Operand:
    def __init__(self, ref, buffer, sem):
        self.buffer, self.copy = buffer, pltpu.make_async_copy(ref, buffer, sem)
        self.started = self.waited = False

    def start(self):
        if not self.started:
            self.copy.start()
        self.started = True

    def get(self):
        self.start()
        if not self.waited:
            self.copy.wait()
        self.waited = True
        return self.buffer


class Result:
    def __init__(self, ref, buffer, sem):
        self.buffer, self.copy = buffer, pltpu.make_async_copy(buffer, ref, sem)
        self.sent = False

    def send(self):
        if not self.sent:
            self.copy.start()
        self.sent = True


def start(*operands):
    for operand in jax.tree.leaves(operands):
        operand.start()


def send(*results):
    for result in jax.tree.leaves(results):
        result.send()


def moved_call(body, scalars, ins, outs, pairs, scratch, name, raw_outs=()):
    in_leaves, in_tree = jax.tree.flatten(ins)
    out_leaves, out_tree = jax.tree.flatten(outs)

    def kernel(*refs):
        refs = list(refs)

        def take(count):
            taken, refs[:] = refs[:count], refs[count:]
            return taken

        scalar_refs, in_refs = take(len(scalars)), take(len(in_leaves))
        pair_refs = [tuple(take(2)) for _ in pairs]
        out_refs, raw_refs = take(len(out_leaves)), take(len(raw_outs))
        in_buffers, out_buffers, (in_sems, out_sems) = take(len(in_leaves)), take(len(out_leaves)), take(2)
        operands = [Operand(*two, in_sems.at[i]) for i, two in enumerate(zip(in_refs, in_buffers))]
        results = [Result(*two, out_sems.at[i]) for i, two in enumerate(zip(out_refs, out_buffers))]
        body(in_tree.unflatten(operands), out_tree.unflatten(results), scalar_refs, pair_refs, raw_refs, refs)
        send(results)
        for operand in operands:
            operand.get()
        for result in results:
            result.copy.wait()

    hbm = pl.BlockSpec(memory_space=pltpu.HBM)
    buffers = [pltpu.VMEM(value.shape, value.dtype) for value in (*in_leaves, *out_leaves)]
    results = pl.pallas_call(
        kernel,
        in_specs=[pl.BlockSpec(memory_space=pltpu.SMEM)] * len(scalars) + [hbm] * (len(in_leaves) + 2 * len(pairs)),
        out_specs=[hbm] * (len(out_leaves) + len(raw_outs)),
        out_shape=[*out_leaves, *raw_outs],
        scratch_shapes=buffers
        + [pltpu.SemaphoreType.DMA((len(in_leaves),)), pltpu.SemaphoreType.DMA((len(out_leaves),))]
        + list(scratch),
        compiler_params=params_for(MOST_VMEM),
        name=name,
    )(*scalars, *in_leaves, *[w for pair in pairs for w in pair])
    return out_tree.unflatten(results[: len(out_leaves)]), results[len(out_leaves) :]


def start_copy(pair, section, window, target, sem):
    own, came = pair
    here = lax.axis_index("section") == section

    @pl.when(here)
    def _():
        pltpu.make_async_copy(own.at[window], target, sem).start()

    @pl.when(jnp.logical_not(here))
    def _():
        pltpu.make_async_copy(came.at[window], target, sem).start()


def wait_copy(pair, window, target, sem):
    pltpu.make_async_copy(pair[0].at[window], target, sem).wait()


def qkv_window(group, part):
    return 0, slice(None), pl.ds(part * D + group * GROUP, GROUP)


def qkv_buffers():
    return [pltpu.VMEM((GROUPS, 3, D, GROUP), BF16), pltpu.SemaphoreType.DMA((GROUPS, 3))]


def start_qkv(pair, section, buffers):
    for group in range(GROUPS):
        for part in range(3):
            start_copy(pair, section, qkv_window(group, part), buffers[0].at[group, part], buffers[1].at[group, part])


def wait_qkv(pair, buffers, group, part):
    wait_copy(pair, qkv_window(0, 0), buffers[0].at[group, part], buffers[1].at[group, part])


UP_WINDOWS = [(0, slice(None), slice(j * TILE, (j + 1) * TILE)) for j in range(TILES)]
DOWN_WINDOWS = [(0, slice(j * TILE, (j + 1) * TILE), slice(None)) for j in range(TILES)]
OUT_WINDOW = (0, slice(None), slice(None))


def rest_buffers():
    return [
        pltpu.VMEM((D, D), BF16),
        pltpu.VMEM((TILES, D, TILE), BF16),
        pltpu.VMEM((TILES, TILE, D), BF16),
        pltpu.SemaphoreType.DMA((2 * TILES + 1,)),
    ]


def start_out(pairs, section, buffers):
    start_copy(pairs[0], section, OUT_WINDOW, buffers[0], buffers[3].at[2 * TILES])


def start_tiles(pairs, section, buffers):
    for j in range(TILES):
        start_copy(pairs[1], section, UP_WINDOWS[j], buffers[1].at[j], buffers[3].at[j])
        start_copy(pairs[2], section, DOWN_WINDOWS[j], buffers[2].at[j], buffers[3].at[TILES + j])


def wait_out(pairs, buffers):
    wait_copy(pairs[0], OUT_WINDOW, buffers[0], buffers[3].at[2 * TILES])


def wait_up(pairs, buffers, tile):
    wait_copy(pairs[1], UP_WINDOWS[0], buffers[1].at[tile], buffers[3].at[tile])


def wait_down(pairs, buffers, tile):
    wait_copy(pairs[2], DOWN_WINDOWS[0], buffers[2].at[tile], buffers[3].at[TILES + tile])


def across(values):
    return jnp.broadcast_to(values, (values.shape[0], LANES))


def group_columns(group):
    return pl.ds(pl.multiple_of(group * GROUP, GROUP), GROUP)


def tile_columns(tile):
    return pl.ds(pl.multiple_of(tile * TILE, TILE), TILE)


def head_mask(values, head):
    lane = lax.broadcasted_iota(jnp.int32, values.shape, 1)
    return (lane >= head * HEAD_DIM) & (lane < (head + 1) * HEAD_DIM)


def only_head(values, head):
    return jnp.where(head_mask(values, head), values, jnp.zeros_like(values))


def scaled_query(query):
    return low(query.astype(F32) * HEAD_DIM**-0.5)


def key_bias(length, shape, axis):
    return jnp.where(lax.broadcasted_iota(jnp.int32, shape, axis) < length, 0.0, -1e30)


def softmax_rows(scores):
    highest = jnp.max(scores, 1, keepdims=True)
    exponent = jnp.exp(scores - highest)
    total = jnp.sum(exponent, 1, keepdims=True)
    return low(exponent * (1.0 / total)), highest + jnp.log(total)


def branch_rows(low_in, weights):
    active, slope = gelu_both(matmul(low_in, weights[0]) + weights[1])
    active = low(active)
    return matmul(active, weights[2]) + weights[3], active, low(slope)


def alternate(*lists):
    steps = [((i + 0.5) / len(steps), k, step) for k, steps in enumerate(lists) for i, step in enumerate(steps)]
    for _, _, step in sorted(steps, key=lambda entry: entry[:2]):
        step()


def section_params(params, section):
    return [operand.get()[section] for operand in params]


def rest_rows(out, rows, section, norms, adapter, hidden, mixed, finish, scratch, pairs, buffers, after_loop=None):
    att_low, acc, u_even, u_odd, g_even, g_odd = scratch
    gain = lambda i: norms[section, i : i + 1]
    parts = rows_of(rows, STEP_ROWS)
    every = slice(0, rows)
    wait_out(pairs, buffers)
    for part in parts:
        first = hidden[part] + matmul(mixed[part], buffers[0][...])
        values, (normal, inverse) = layer_norm(first, gain(2), gain(3))
        acc[part] = values
        att_low[part] = low(values)
        out.normal_1.buffer[part] = normal
        out.inverse_1.buffer[part] = across(inverse)
    send(out.normal_1, out.inverse_1)
    wait_up(pairs, buffers, 0)
    g_odd[every] = jnp.zeros_like(g_odd[every])

    def gelu_steps(u_ref, g_ref, tile):
        def step(at):
            active, slope = gelu_both(u_ref[at])
            g_ref[at] = low(active)
            out.slope.buffer[at, tile_columns(tile)] = low(slope)

        return [functools.partial(step, at) for at in rows_of(rows, SMALL_ROWS)]

    def up_steps(u_ref, tile):
        def step(columns):
            u_ref[every, columns] = matmul(att_low[every], buffers[1][tile, :, columns])

        return [functools.partial(step, columns) for columns in rows_of(TILE, GROUP)]

    def down_steps(g_ref, tile):
        def step(columns):
            acc[every, columns] += matmul(g_ref[every], buffers[2][tile, :, columns])

        return [functools.partial(step, columns) for columns in rows_of(D, GROUP)]

    alternate(up_steps(u_even, 0))

    def turn(j, carry):
        even, odd = 2 * j, 2 * j + 1
        before, after = jnp.maximum(even - 1, 0), jnp.minimum(even + 2, TILES - 1)
        wait_down(pairs, buffers, even)
        wait_up(pairs, buffers, odd)
        wait_down(pairs, buffers, odd)

        @pl.when(even + 2 < TILES)
        def _():
            wait_up(pairs, buffers, even + 2)

        alternate(gelu_steps(u_even, g_even, even), down_steps(g_odd, before) + up_steps(u_odd, odd))
        alternate(gelu_steps(u_odd, g_odd, odd), down_steps(g_even, even) + up_steps(u_even, after))
        return carry

    lax.fori_loop(0, TILES // 2, turn, 0)
    alternate(down_steps(g_odd, TILES - 1))
    if after_loop is not None:
        after_loop()
    send(out.slope)
    weights = section_params(adapter, section)
    for part in parts:
        summed = acc[part]
        low_in = low(summed)
        added, *kept = branch_rows(low_in, weights)
        for result, value in zip(out.branch, (low_in, *kept)):
            result.buffer[part] = value
        values, (normal, inverse) = layer_norm(summed + added, gain(4), gain(5))
        out.normal_2.buffer[part], out.inverse_2.buffer[part] = normal, across(inverse)
        finish(part, values)
    send(out.branch, out.normal_2, out.inverse_2)


def low_shape(*dims):
    return shape_of(*dims, kind=BF16)


def branch_shapes(rows, wide, narrow):
    return Branch(low_shape(rows, wide), low_shape(rows, narrow), low_shape(rows, narrow))


def rest_shapes(rows):
    wide, thin = shape_of(rows, D), shape_of(rows, LANES)
    return Rest(wide, thin, low_shape(rows, FF), branch_shapes(rows, D, BOT), wide, thin)


def forward_kernel(ins, scalars, pairs, parts, slots):
    coupling_shapes = lambda rows: branch_shapes(rows, HALF, INV_H)
    outs = Forward(
        target_rows=shape_of(COUNT, D),
        one=coupling_shapes(SEQ),
        two=coupling_shapes(SEQ),
        attention_0=Attention(*[low_shape(SEQ, D)] * 3, shape_of(GROUPS, 8, SEQ)),
        rest_0=rest_shapes(SEQ),
        attention_1=Attention(
            low_shape(COUNT, D), *[low_shape(SEQ, D)] * 2, shape_of(GROUPS, HEADS_IN * COUNT, LANES)
        ),
        rest_1=rest_shapes(COUNT),
        last=Last(
            coupling_shapes(COUNT), coupling_shapes(COUNT),
            shape_of(COUNT, D), shape_of(COUNT, LANES), low_shape(COUNT, D),
        ),
    )

    def body(ins, out, scalar_refs, pair_refs, raw_refs, scratch):
        length = scalar_refs[0][0]
        hidden, x_low, s_even, s_odd, p_even, p_odd, lse_buf, mixed, section_out = scratch[:9]
        at_spots, at_low, mixed_1 = scratch[9:12]
        rest_scratch, qkv_0, qkv_1, rest_w = scratch[12:18], scratch[18:20], scratch[20:22], scratch[22:26]
        row_sems, joined = scratch[26:28]
        qkv_pair, rest_pairs = pair_refs[0], pair_refs[1:]

        start(ins.came, ins.spot, ins.pos, ins.norms, ins.coupling)
        norms = ins.norms.get()
        norm = lambda s, i: norms[s, i : i + 1]

        came, spot = ins.came.get(), ins.spot.get()
        start_qkv(qkv_pair, 0, qkv_0)
        start_out(rest_pairs, 0, rest_w)

        def rows_at(part):
            lane = lax.broadcasted_iota(jnp.int32, (part.stop - part.start, parts * slots), 1)
            hits = (spot[part][:, :1] == lane).astype(BF16)
            return matmul(hits, came[...])

        targets = slice(SEQ, SEQ + COUNT)
        out.target_rows.buffer[...] = rows_at(targets)
        for part in rows_of(SEQ, STEP_ROWS):
            hidden[part] = rows_at(part)

        @pl.when(scalar_refs[1][0] > 1)
        def _():
            ins.extra.copy.start()
            ins.extra.copy.wait()
            out.target_rows.buffer[...] += ins.extra.buffer[targets]
            hidden[...] += ins.extra.buffer[:SEQ]

        ins.extra.started = ins.extra.waited = True
        send(out.target_rows)
        start(ins.adapter, ins.chosen)
        start_tiles(rest_pairs, 0, rest_w)
        one, two = section_params(ins.coupling, 0), section_params(ins.coupling, 1)

        def put(results, part, *values):
            for result, value in zip(results, values):
                result.buffer[part] = value

        for part in rows_of(SEQ, STEP_ROWS):
            started, _ = layer_norm(hidden[part] + ins.pos.get()[part].astype(F32), norm(0, 0), norm(0, 1))
            left, right = started[:, :HALF], started[:, HALF:]
            low_one = low(right)
            added, active, slope = branch_rows(low_one, one)
            put(out.one, part, low_one, active, slope)
            left = left + added
            low_two = low(left)
            added, active, slope = branch_rows(low_two, two)
            put(out.two, part, low_two, active, slope)
            right = right + added
            hidden[part, :HALF] = left
            hidden[part, HALF:] = right
            x_low[part, :HALF] = low_two
            x_low[part, HALF:] = low(right)
        send(out.one, out.two)

        start_qkv(qkv_pair, 1, qkv_1)
        lse_buf[...] = jnp.zeros((SEQ, LANES), F32)
        q_ref, k_ref, v_ref, lse_ref = (result.buffer for result in out.attention_0)

        def attend(group, carry):
            columns = group_columns(group)
            for part, ref in enumerate((q_ref, k_ref, v_ref)):
                wait_qkv(qkv_pair, qkv_0, group, part)
                ref[:, columns] = low(matmul(x_low[...], qkv_0[0][group, part]))
            query = scaled_query(q_ref[:, columns])
            key, value = k_ref[:, columns], v_ref[:, columns]
            bias = key_bias(length, (1, SEQ), 1)
            lane = lax.broadcasted_iota(jnp.int32, (SMALL_ROWS * 2, LANES), 1)
            buffers = ((s_even, p_even), (s_odd, p_odd)) * 2

            def score_steps(head):
                def step():
                    buffers[head][0][...] = matmul_t(only_head(query, head), key)

                return [step] if head < HEADS_IN else []

            def soft_steps(head):
                def step(rows):
                    soft, lse = softmax_rows(buffers[head][0][rows] + bias)
                    buffers[head][1][rows] = soft
                    lse_buf[rows] = jnp.where(lane == head, lse, lse_buf[rows])

                return [functools.partial(step, rows) for rows in rows_of(SEQ, SMALL_ROWS * 2)]

            def mix_steps(head):
                def step():
                    mixed_head = matmul(buffers[head][1][...], value)
                    if head == 0:
                        joined[...] = mixed_head
                    else:
                        joined[...] = jnp.where(head_mask(mixed_head, head), mixed_head, joined[...])

                return [step] if head >= 0 else []

            alternate(score_steps(0))
            for head in range(HEADS_IN):
                alternate(soft_steps(head), score_steps(head + 1) + mix_steps(head - 1))
            alternate(mix_steps(HEADS_IN - 1))
            mixed[:, columns] = low(joined[...])
            lse_ref[group] = jnp.transpose(lse_buf[...])[:8]
            return carry

        lax.fori_loop(0, GROUPS, attend, 0)
        send(out.attention_0)

        def to_section_out(part, values):
            section_out[part] = low(values)

        def next_weights():
            start_out(rest_pairs, 1, rest_w)
            start_tiles(rest_pairs, 1, rest_w)

        rest_rows(
            out.rest_0, SEQ, 0, norms, ins.adapter, hidden, mixed, to_section_out,
            rest_scratch, rest_pairs, rest_w, next_weights,
        )

        at_spots[...] = matmul(ins.chosen.get()[...], section_out[...])
        at_low[...] = low(at_spots[...])
        q_1, k_1, v_1, lse_1 = (result.buffer for result in out.attention_1)

        groups = rows_of(D, GROUP)
        for group, columns in enumerate(groups):
            for part, ref in enumerate((q_1, k_1, v_1)):
                wait_qkv(qkv_pair, qkv_1, group, part)
                source = at_low if part == 0 else section_out
                ref[:, columns] = low(matmul(source[...], qkv_1[0][group, part]))
        bias = key_bias(length, (1, SEQ), 1)
        for group, columns in enumerate(groups):
            query = scaled_query(q_1[:, columns])
            query = jnp.concatenate([only_head(query, head) for head in range(HEADS_IN)], 0)
            soft, lse = softmax_rows(matmul_t(query, k_1[:, columns]) + bias)
            lse_1[group] = across(lse)
            every = matmul(soft, v_1[:, columns])
            mixed_group = every[:COUNT]
            for head in range(1, HEADS_IN):
                rows = slice(head * COUNT, (head + 1) * COUNT)
                mixed_group = jnp.where(head_mask(mixed_group, head), every[rows], mixed_group)
            mixed_1[:, columns] = low(mixed_group)
        send(out.attention_1)

        def to_normed(part, values):
            left, right = values[:, :HALF], values[:, HALF:]
            low_two = low(left)
            taken, active, slope = branch_rows(low_two, two)
            put(out.last.two, part, low_two, active, slope)
            right = right - taken
            low_one = low(right)
            taken, active, slope = branch_rows(low_one, one)
            put(out.last.one, part, low_one, active, slope)
            left = left - taken
            values, (normal, inverse) = layer_norm(jnp.concatenate([left, right], 1), norm(1, 0), norm(1, 1))
            put(out.last[2:], part, normal, across(inverse), low(values))

        rest_rows(
            out.rest_1, COUNT, 1, norms, ins.adapter, at_spots, mixed_1, to_normed,
            rest_scratch, rest_pairs, rest_w,
        )
        normed = out.last.normed.buffer
        copies = [
            pltpu.make_async_copy(normed.at[half], raw_refs[i].at[part], row_sems.at[i, part])
            for i, half in enumerate(rows_of(COUNT, COUNT // 2))
            for part in range(parts)
        ]
        for copy in copies:
            copy.start()
        for copy in copies:
            copy.wait()

    buffer = lambda *dims: pltpu.VMEM(dims, F32)
    buffer_low = lambda *dims: pltpu.VMEM(dims, BF16)
    scratch = [buffer(SEQ, D), buffer_low(SEQ, D), buffer(SEQ, SEQ), buffer(SEQ, SEQ)]
    scratch += [buffer_low(SEQ, SEQ), buffer_low(SEQ, SEQ), buffer(SEQ, LANES)]
    scratch += [buffer_low(SEQ, D), buffer_low(SEQ, D)]
    scratch += [buffer(COUNT, D), buffer_low(COUNT, D), buffer_low(COUNT, D)]
    scratch += [buffer_low(SEQ, D), buffer(SEQ, D), buffer(SEQ, TILE), buffer(SEQ, TILE)]
    scratch += [buffer_low(SEQ, TILE), buffer_low(SEQ, TILE)]
    scratch += qkv_buffers() + qkv_buffers() + rest_buffers()
    scratch += [pltpu.SemaphoreType.DMA((2, parts)), buffer(SEQ, GROUP)]
    raw = [low_shape(parts, COUNT // 2, D)] * 2
    kept, rows = moved_call(body, scalars, ins, outs, pairs, scratch, "forward", raw)
    return kept, rows


def column_sum(values):
    return jnp.sum(values.astype(F32), 0, keepdims=True)


def branch_grads(grad_low, kept, weights, out_refs):
    low_in, active, slope = kept
    hidden_grad = low(matmul_t(grad_low, weights[2]) * slope.astype(F32))
    out_refs[0][...] = inner_rows(low_in, hidden_grad)
    out_refs[1][...] = column_sum(hidden_grad)
    out_refs[2][...] = inner_rows(active, grad_low)
    out_refs[3][...] = column_sum(grad_low)
    return hidden_grad


ADAPTER_GRADS = ((D, BOT), (1, BOT), (BOT, D), (1, D))
COUPLING_GRADS = ((HALF, INV_H), (1, INV_H), (INV_H, HALF), (1, HALF))


def branch_kept(branch):
    return [operand.get()[...] for operand in branch]


def grad_weights(pair, section):
    return [pair[0].get()[section], None, pair[1].get()[section]]


def back_to_inner(kept, rows, section, norms, adapter, incoming, scratch, grad_refs, packing=None):
    acc, second_low = scratch
    parts = rows_of(rows, STEP_ROWS)
    weights = grad_weights(adapter, section)
    for part in parts:
        norm_kept = kept.normal_2.get()[part], kept.inverse_2.get()[part, :1]
        second = norm_back(incoming(part), norm_kept, norms[section, 4:5])
        acc[part] = second
        second_low[part] = low(second)
    hidden_grad = branch_grads(second_low[:rows], branch_kept(kept.branch), weights, grad_refs)
    for part in parts:
        acc[part] += matmul_t(hidden_grad[part], weights[0])
    if packing is not None:
        packing()


def back_to_mixed(operands, rows, section, norms, scratch, pairs, buffers, results):
    summed_low, acc = scratch
    start_ref, mixed_ref = results
    slope, normal, inverse = (operand.get() for operand in operands)
    parts = rows_of(rows, STEP_ROWS)
    for part in parts:
        summed_low[part] = low(acc[part])

    def turn(j, carry):
        for now in (2 * j, 2 * j + 1):
            wait_up(pairs, buffers, now)
            wait_down(pairs, buffers, now)
        for now in (2 * j, 2 * j + 1):
            for part in parts:
                inner = matmul_t(summed_low[part], buffers[2][now])
                inner = low(inner * slope[part, tile_columns(now)].astype(F32))
                acc[part] += matmul_t(inner, buffers[1][now])
        return carry

    lax.fori_loop(0, TILES // 2, turn, 0)
    wait_out(pairs, buffers)
    for part in parts:
        back = norm_back(acc[part], (normal[part], inverse[part, :1]), norms[section, 2:3])
        start_ref[part] = back
        mixed_ref[part] = low(matmul_t(low(back), buffers[0][...]))


def backward_kernel(ins, scalars, pairs, packed):
    parts = ins.merged[0].shape[0]
    grads = [shape_of(*dims) for dims in COUPLING_GRADS]
    if packed:
        chunks = low_shape(COUPLING_GROUPS, PART_ROWS, LANES)
        adapters = [[shape_of(1, BOT), shape_of(1, D)] for _ in range(MICRO)] + [chunks, chunks]
    else:
        adapters = [[shape_of(*dims) for dims in ADAPTER_GRADS] for _ in range(MICRO)]
    outs = Back(shape_of(1, LANES), grads, grads, adapters, shape_of(SEQ, D))

    def body(ins, out, scalar_refs, pair_refs, raw_refs, scratch):
        length = scalar_refs[0][0]
        (summed_low, acc_0, second_low), spot, mixed_1, acc_1, section_grad = scratch[:3], *scratch[3:7]
        qkv_w, rest_w, refs = scratch[7:9], scratch[9:13], scratch[13:]
        qkv_pair, rest_pairs = pair_refs[0], pair_refs[1:]

        start(ins.merged, ins.row_weights, ins.weight_sum, ins.target_rows, ins.last, ins.norms)
        start(ins.coupling, ins.adapter, ins.rest_1)
        start_tiles(rest_pairs, 1, rest_w)
        start_out(rest_pairs, 1, rest_w)
        start_qkv(qkv_pair, 1, qkv_w)
        start(ins)
        norms = ins.norms.get()

        def merge(merged):
            stats = merged[:, :, D:].astype(F32)
            highest = jnp.sum(stats[:, :, :3], 2, keepdims=True)
            totals = jnp.sum(stats[:, :, 3:6], 2, keepdims=True)
            top = jnp.max(highest, 0)
            factor = jnp.exp(highest - top[None])
            total = jnp.sum(totals * factor, 0)
            expected = jnp.zeros((merged.shape[1], D), F32)
            for i in range(parts):
                expected += merged[i, :, :D].astype(F32) * (factor[i] / total)
            return top, total, expected

        def from_head(part):
            halves = [merge(operand.get()) for operand in ins.merged]
            top, total, expected = (jnp.concatenate(pair, 0) for pair in zip(*halves))
            target = ins.target_rows.get()[...]
            target_logit = jnp.sum(ins.last.normed.get()[...].astype(F32) * target, 1, keepdims=True)
            weight = ins.row_weights.get()[...]
            row_losses = weight[:, :1] * (top + jnp.log(total) - target_logit)
            out.loss.buffer[...] = across(jnp.sum(row_losses, 0, keepdims=True))
            normed_grad = (weight / ins.weight_sum.get()[...])[:, :1] * (expected - target)
            kept = (ins.last.normal.get()[...], ins.last.inverse.get()[:, :1])
            restored = norm_back(normed_grad, kept, norms[1, 0:1])
            left, right = restored[:, :HALF], restored[:, HALF:]
            one, two = (grad_weights(ins.coupling, s) for s in range(MICRO))
            refs_of = lambda results: [result.buffer for result in results]
            hidden = branch_grads(low(-left), branch_kept(ins.last.one), one, refs_of(out.one))
            right = right + matmul_t(hidden, one[0])
            hidden = branch_grads(low(-right), branch_kept(ins.last.two), two, refs_of(out.two))
            left = left + matmul_t(hidden, two[0])
            return jnp.concatenate([left, right], 1)

        def grads_of(section):
            buffers = [result.buffer for result in out.adapters[section]]
            return (refs[0], buffers[0], refs[1], buffers[1]) if packed else buffers

        def pack_second():
            def store(part, chunk):
                refs[2][part] = chunk

            pack_adapter((refs[0], refs[1]), store)

        def pack_both():
            here = lax.axis_index("section") == 0
            own, other = out.adapters[2:]

            def store(part, chunk):
                arrived = refs[2][part]
                own.buffer[part] = jnp.where(here, chunk, arrived)
                other.buffer[part] = jnp.where(here, arrived, chunk)

            pack_adapter((refs[0], refs[1]), store)
            send(own, other)

        back_to_inner(
            ins.rest_1, COUNT, 1, norms, ins.adapter, from_head, (acc_0, second_low), grads_of(1),
            pack_second if packed else None,
        )
        kept = ins.rest_1.slope, ins.rest_1.normal_1, ins.rest_1.inverse_1
        back_to_mixed(kept, COUNT, 1, norms, (summed_low, acc_0), rest_pairs, rest_w, (spot, mixed_1))

        acc_1[...] = jnp.zeros_like(acc_1)
        q_ref, k_ref, v_ref, lse_ref = (operand.get() for operand in ins.attention_1)

        def attend_back(group, carry):
            columns = group_columns(group)
            stack = lambda values: jnp.concatenate([only_head(values, h) for h in range(HEADS_IN)], 0)
            query = stack(scaled_query(q_ref[:, columns]))
            mixed = stack(mixed_1[:, columns])
            key, value = k_ref[:, columns], v_ref[:, columns]
            scores = matmul_t(query, key) + key_bias(length, (1, SEQ), 1)
            soft = jnp.exp(scores - lse_ref[group][:, :1])
            soft_grad = matmul_t(mixed, value)
            delta = jnp.sum(soft_grad * soft, 1, keepdims=True)
            score_grad = low(soft * (soft_grad - delta))
            every = matmul(score_grad, key)
            query_grad = every[:COUNT]
            for head in range(1, HEADS_IN):
                query_grad = jnp.where(
                    head_mask(query_grad, head), every[head * COUNT : (head + 1) * COUNT], query_grad
                )
            query_grad = low(query_grad * HEAD_DIM**-0.5)
            key_grad = low(inner_rows(score_grad, query))
            value_grad = low(inner_rows(low(soft), mixed))
            for part in range(3):
                wait_qkv(qkv_pair, qkv_w, group, part)
            spot[...] += matmul_t(query_grad, qkv_w[0][group, 0])
            acc_1[...] += matmul_t(key_grad, qkv_w[0][group, 1]) + matmul_t(value_grad, qkv_w[0][group, 2])
            return carry

        lax.fori_loop(0, GROUPS, attend_back, 0)
        placed = jnp.dot(ins.chosen_t.get()[...], spot[...], precision=HIGHEST, preferred_element_type=F32)
        section_grad[...] = low(acc_1[...] + placed)

        back_to_inner(
            ins.rest_0, SEQ, 0, norms, ins.adapter, lambda part: section_grad[part].astype(F32),
            (out.inner.buffer, second_low), grads_of(0), pack_both if packed else None,
        )

    scratch = [pltpu.VMEM((COUNT, D), BF16), pltpu.VMEM((COUNT, D), F32), pltpu.VMEM((SEQ, D), BF16)]
    scratch += [pltpu.VMEM((COUNT, D), F32), pltpu.VMEM((COUNT, D), BF16), pltpu.VMEM((SEQ, D), F32)]
    scratch += [pltpu.VMEM((SEQ, D), BF16)] + qkv_buffers() + rest_buffers()
    if packed:
        scratch += [pltpu.VMEM((D, BOT), F32), pltpu.VMEM((BOT, D), F32)]
        scratch += [pltpu.VMEM((COUPLING_GROUPS, PART_ROWS, LANES), BF16)]
    return moved_call(body, scalars, ins, outs, pairs, scratch, "backward")[0]


def first_backward(ins, scalars, pairs, packed):
    if packed:
        dims = (COUPLING_GROUPS, GROUP_ROWS + 8, LANES)
        outs = (shape_of(*dims), low_shape(*dims))
    else:
        outs = [shape_of(*dims) for dims in COUPLING_GRADS * 2]

    def body(ins, out, scalar_refs, pair_refs, raw_refs, scratch):
        length = scalar_refs[0][0]
        s_even, s_odd, d_even, d_odd, p_even, p_odd, ds_even, ds_odd = scratch[:8]
        qkv_w, (key_grad, value_grad, query_grad_t), refs = scratch[8:10], scratch[10:13], scratch[13:]
        (summed_low, mixed_ref), rest_w, refs = refs[:2], refs[2:6], refs[6:]
        start(ins.inner, ins.norms)
        start_tiles(pair_refs[1:], 0, rest_w)
        start(ins.inner_kept)
        start_out(pair_refs[1:], 0, rest_w)
        start(ins.attention)
        start_qkv(pair_refs[0], 0, qkv_w)
        start(ins)
        acc = ins.inner.get()
        back_to_mixed(
            ins.inner_kept, SEQ, 0, ins.norms.get(), (summed_low, acc), pair_refs[1:], rest_w, (acc, mixed_ref)
        )
        q_ref, k_ref, v_ref, lse_ref = (operand.get() for operand in ins.attention)

        def attend_back(group, carry):
            columns = group_columns(group)
            query = scaled_query(q_ref[:, columns])
            key, value, mixed = k_ref[:, columns], v_ref[:, columns], mixed_ref[:, columns]
            lse_rows = lse_ref[group]
            key_t = jnp.transpose(key)
            buffers = ((s_even, d_even, p_even, ds_even), (s_odd, d_odd, p_odd, ds_odd)) * 2

            def product_steps(head):
                def scores():
                    buffers[head][0][...] = matmul_t(only_head(key, head), query)

                def soft_grads():
                    buffers[head][1][...] = matmul_t(only_head(value, head), mixed)

                return [scores, soft_grads] if head < HEADS_IN else []

            def soft_steps(head):
                s_buf, d_buf, p_low, ds_low = buffers[head]
                delta = [jnp.zeros((8, SEQ), F32)]

                def soft_step(rows):
                    valid = lax.broadcasted_iota(jnp.int32, (SMALL_ROWS, 1), 0) + rows.start < length
                    bias = jnp.where(valid, 0.0, -1e30)
                    soft = jnp.exp(s_buf[rows] + bias - lse_rows[head : head + 1])
                    s_buf[rows] = soft
                    p_low[rows] = low(soft)
                    product = soft * d_buf[rows]
                    for at in range(0, SMALL_ROWS, 8):
                        delta[0] = delta[0] + product[at : at + 8]

                def sum_step():
                    delta[0] = jnp.sum(delta[0], 0, keepdims=True)

                def grad_step(rows):
                    ds_low[rows] = low(s_buf[rows] * (d_buf[rows] - delta[0]))

                parts = rows_of(SEQ, SMALL_ROWS)
                steps = [functools.partial(soft_step, rows) for rows in parts] + [sum_step]
                return steps + [functools.partial(grad_step, rows) for rows in parts]

            def grad_steps(head):
                _, _, p_low, ds_low = buffers[max(head, 0)]

                def add(ref, grad):
                    ref[...] = grad if head == 0 else ref[...] + grad

                def value_step():
                    add(value_grad, matmul(p_low[...], only_head(mixed, head)))

                def key_step():
                    add(key_grad, matmul(ds_low[...], only_head(query, head)))

                def query_step():
                    rows = slice(head * HEAD_DIM, (head + 1) * HEAD_DIM)
                    query_grad_t[rows] = matmul(key_t[rows], ds_low[...])

                return [value_step, key_step, query_step] if head >= 0 else []

            alternate(product_steps(0))
            for head in range(HEADS_IN):
                alternate(soft_steps(head), product_steps(head + 1) + grad_steps(head - 1))
            alternate(grad_steps(HEADS_IN - 1))
            query_grad = jnp.transpose(query_grad_t[...]) * HEAD_DIM**-0.5
            for part, grad in enumerate((query_grad, key_grad[...], value_grad[...])):
                wait_qkv(pair_refs[0], qkv_w, group, part)
                acc[...] += matmul_t(low(grad), qkv_w[0][group, part])
            return carry

        lax.fori_loop(0, GROUPS, attend_back, 0)
        one, two = (grad_weights(ins.coupling, s) for s in range(MICRO))
        grads = refs if packed else [result.buffer for result in out]
        hidden = branch_grads(low(acc[:, HALF:]), branch_kept(ins.two), two, grads[4:])
        left = acc[:, :HALF] + matmul_t(hidden, two[0])
        branch_grads(low(left), branch_kept(ins.one), one, grads[:4])
        for ref, operand in zip(grads, (*ins.grads_one, *ins.grads_two)):
            ref[...] += operand.get()[...]
        if not packed:
            return
        here = lax.axis_index("section")
        for s in range(MICRO):
            some = grads[4 * s : 4 * s + 4]
            biases = [operand.get()[...] for operand in ins.biases[s]]
            tiles = bias_tiles(*biases, some[1][...], some[3][...])

            def store(part, chunk, s=s):
                @pl.when(here == s)
                def _():
                    out[0].buffer[part] = chunk

                @pl.when(here != s)
                def _():
                    out[1].buffer[part] = low(chunk)

            pack_coupling((some[0], some[2]), tiles, sum(BIASES) // COUPLING_GROUPS, store)

    scratch = [pltpu.VMEM((SEQ, SEQ), F32)] * 4 + [pltpu.VMEM((SEQ, SEQ), BF16)] * 4 + qkv_buffers()
    scratch += [pltpu.VMEM((SEQ, GROUP), F32)] * 2 + [pltpu.VMEM((GROUP, SEQ), F32)]
    scratch += [pltpu.VMEM((SEQ, D), BF16)] * 2 + rest_buffers()
    if packed:
        scratch += [pltpu.VMEM(dims, F32) for dims in COUPLING_GRADS * 2]
    return moved_call(body, scalars, ins, outs, pairs, scratch, "first_backward")[0]


VOCAB_TILE = 1280


def head_stats(top, total):
    lane = lax.broadcasted_iota(jnp.int32, (top.shape[0], LANES), 1)
    stats = jnp.zeros(lane.shape, F32)
    for j, piece in enumerate(three_low(top) + three_low(total)):
        stats = jnp.where(lane == j, piece.astype(F32), stats)
    return low(stats)


def head_kernel(rows, table):
    parts, each, _ = rows.shape
    count, vocab = parts * each, table.shape[0]
    tiles = pl.cdiv(vocab, VOCAB_TILE)
    if vocab < VOCAB_TILE or (vocab - VOCAB_TILE) % 16 or tiles % 2:
        return blocked_head_kernel(rows, table)
    starts = [min(tile * VOCAB_TILE, vocab - VOCAB_TILE) for tile in range(tiles)]

    def kernel(x_hbm, table_hbm, out_hbm, *refs):
        x_ref, out_ref, entries, acc, top, total, factor_even, factor_odd = refs[:8]
        l_even, l_odd, p_even, p_odd, sems = refs[8:]
        fetch = pltpu.make_async_copy(x_hbm, x_ref, sems.at[tiles])
        fetch.start()
        for tile, at in enumerate(starts):
            window = table_hbm.at[pl.ds(at, VOCAB_TILE)]
            pltpu.make_async_copy(window, entries.at[tile], sems.at[tile]).start()

        def wait_tile(tile):
            window = table_hbm.at[pl.ds(0, VOCAB_TILE)]
            pltpu.make_async_copy(window, entries.at[tile], sems.at[tile]).wait()

        def logit_steps(l_ref, tile):
            def step(columns):
                l_ref[:, columns] = matmul_t(x_ref[...], entries[tile, columns])

            return [functools.partial(step, columns) for columns in rows_of(VOCAB_TILE, GROUP)]

        def soft_steps(l_ref, p_ref, factor_ref, tile):
            start = jnp.minimum(tile * VOCAB_TILE, vocab - VOCAB_TILE)
            lane = lax.broadcasted_iota(jnp.int32, (1, VOCAB_TILE), 1)
            bias = jnp.where(lane + start >= tile * VOCAB_TILE, 0.0, -1e30)

            def step(at):
                logits = l_ref[at] + bias
                earlier = top[at]
                highest = jnp.maximum(earlier, jnp.max(logits, 1, keepdims=True))
                exponent = jnp.exp(logits - highest)
                factor = jnp.exp(earlier - highest)
                top[at] = highest
                total[at] = total[at] * factor + jnp.sum(exponent, 1, keepdims=True)
                p_ref[at] = low(exponent)
                factor_ref[at] = across(factor)

            return [functools.partial(step, at) for at in rows_of(count, SMALL_ROWS)]

        def sum_steps(p_ref, factor_ref, tile):
            def step(columns):
                factor = factor_ref[...]
                factor = jnp.concatenate([factor, factor], 1)
                acc[:, columns] = acc[:, columns] * factor + matmul(p_ref[...], entries[tile, :, columns])

            return [functools.partial(step, columns) for columns in rows_of(D, GROUP)]

        acc[...] = jnp.zeros_like(acc)
        top[...] = jnp.full_like(top, -1e30)
        total[...] = jnp.zeros_like(total)
        p_odd[...] = jnp.zeros_like(p_odd)
        factor_odd[...] = jnp.ones_like(factor_odd)
        fetch.wait()
        wait_tile(0)
        alternate(logit_steps(l_even, 0))

        def turn(j, carry):
            even, odd = 2 * j, 2 * j + 1
            before, after = jnp.maximum(even - 1, 0), jnp.minimum(even + 2, tiles - 1)
            wait_tile(odd)

            @pl.when(even + 2 < tiles)
            def _():
                wait_tile(even + 2)

            alternate(
                soft_steps(l_even, p_even, factor_even, even),
                sum_steps(p_odd, factor_odd, before) + logit_steps(l_odd, odd),
            )
            alternate(
                soft_steps(l_odd, p_odd, factor_odd, odd),
                sum_steps(p_even, factor_even, even) + logit_steps(l_even, after),
            )
            return carry

        lax.fori_loop(0, tiles // 2, turn, 0)
        alternate(sum_steps(p_odd, factor_odd, tiles - 1))
        out_ref[:, :D] = low(acc[...])
        out_ref[:, D:] = head_stats(top[...], total[...])
        copy = pltpu.make_async_copy(out_ref, out_hbm, sems.at[tiles])
        copy.start()
        copy.wait()

    hbm = pl.BlockSpec(memory_space=pltpu.HBM)
    return pl.pallas_call(
        kernel,
        in_specs=[hbm, hbm],
        out_specs=hbm,
        out_shape=low_shape(count, D + LANES),
        scratch_shapes=[
            pltpu.VMEM((count, D), BF16),
            pltpu.VMEM((count, D + LANES), BF16),
            pltpu.VMEM((tiles, VOCAB_TILE, D), BF16),
            pltpu.VMEM((count, D), F32),
            pltpu.VMEM((count, 1), F32),
            pltpu.VMEM((count, 1), F32),
        ]
        + [pltpu.VMEM((count, LANES), F32)] * 2
        + [pltpu.VMEM((count, VOCAB_TILE), F32)] * 2
        + [pltpu.VMEM((count, VOCAB_TILE), BF16)] * 2
        + [pltpu.SemaphoreType.DMA((tiles + 1,))],
        compiler_params=params_for(MOST_VMEM),
        name="vocabulary_head",
    )(rows.reshape(count, D), table).reshape(parts, each, D + LANES)


def blocked_head_kernel(rows, table):
    parts_in, each, _ = rows.shape
    count, vocab = parts_in * each, table.shape[0]
    last = pl.cdiv(vocab, VOCAB_TILE) - 1
    turns = last // 2 + 1

    def kernel(x_hbm, even_ref, odd_ref, after_ref, out_hbm, *refs):
        x_ref, out_ref, acc, top, total, l_even, l_odd, p_even, p_odd, sems = refs
        turn = pl.program_id(0)

        def entries_of(ref, tile):
            row = lax.broadcasted_iota(jnp.int32, (VOCAB_TILE, 1), 0)
            return jnp.where(row < vocab - tile * VOCAB_TILE, ref[...], jnp.zeros_like(ref))

        @pl.when(turn == 0)
        def _():
            copy = pltpu.make_async_copy(x_hbm, x_ref, sems.at[0])
            copy.start()
            acc[...] = jnp.zeros_like(acc)
            top[...] = jnp.full_like(top, -1e30)
            total[...] = jnp.zeros_like(total)
            entries = entries_of(even_ref, 0)
            copy.wait()
            l_even[...] = matmul_t(x_ref[...], entries)

        even = entries_of(even_ref, 2 * turn)
        odd = entries_of(odd_ref, 2 * turn + 1)
        after = entries_of(after_ref, 2 * turn + 2)
        for tile, l_now, p_now, now, l_later, later in (
            (2 * turn, l_even, p_even, even, l_odd, odd),
            (2 * turn + 1, l_odd, p_odd, odd, l_even, after),
        ):
            bias = key_bias(vocab - tile * VOCAB_TILE, (1, VOCAB_TILE), 1)
            for at in rows_of(count, SMALL_ROWS):
                logits = l_now[at] + bias
                earlier = top[at]
                highest = jnp.maximum(earlier, jnp.max(logits, 1, keepdims=True))
                exponent = jnp.exp(logits - highest)
                factor = jnp.exp(earlier - highest)
                top[at] = highest
                total[at] = total[at] * factor + jnp.sum(exponent, 1, keepdims=True)
                p_now[at] = low(exponent)
                acc[at] = acc[at] * factor
            l_later[...] = matmul_t(x_ref[...], later)
            acc[...] += matmul(p_now[...], now)

        @pl.when(turn == turns - 1)
        def _():
            out_ref[:, :D] = low(acc[...])
            out_ref[:, D:] = head_stats(top[...], total[...])
            copy = pltpu.make_async_copy(out_ref, out_hbm, sems.at[1])
            copy.start()
            copy.wait()

    def tile_at(shift):
        return pl.BlockSpec((VOCAB_TILE, D), lambda j: (jnp.minimum(2 * j + shift, last), 0))

    hbm = pl.BlockSpec(memory_space=pltpu.HBM)
    return pl.pallas_call(
        kernel,
        grid=(turns,),
        in_specs=[hbm] + [tile_at(shift) for shift in range(3)],
        out_specs=hbm,
        out_shape=shape_of(count, D + LANES, kind=BF16),
        scratch_shapes=[
            pltpu.VMEM((count, D), BF16),
            pltpu.VMEM((count, D + LANES), BF16),
            pltpu.VMEM((count, D), F32),
            pltpu.VMEM((count, 1), F32),
            pltpu.VMEM((count, 1), F32),
            pltpu.VMEM((count, VOCAB_TILE), F32),
            pltpu.VMEM((count, VOCAB_TILE), F32),
            pltpu.VMEM((count, VOCAB_TILE), BF16),
            pltpu.VMEM((count, VOCAB_TILE), BF16),
            pltpu.SemaphoreType.DMA((2,)),
        ],
        compiler_params=params_for(MOST_VMEM),
        name="vocabulary_head",
    )(rows.reshape(count, D), table, table, table).reshape(parts_in, each, D + LANES)


def swap_add(own, other):
    came = lax.ppermute(low(other), "section", [(0, 1), (1, 0)])
    return own + came.astype(F32)


def pick(first_section, both):
    return jnp.where(first_section, both[0], both[1])


def plan_requests(ids, weights, vocab_rows, slots, parts):
    turned = jnp.transpose(ids)

    def kernel(ids_ref, turned_ref, weights_ref, asked_ref, code_ref, spot_ref):
        here = lax.axis_index("section")
        i_index = lax.broadcasted_iota(jnp.int32, (IDS, IDS), 0)
        j_index = lax.broadcasted_iota(jnp.int32, (IDS, IDS), 1)
        earlier, later = j_index < i_index, i_index < j_index

        def owner_of(values):
            return jnp.floor((values.astype(F32) + 0.5) * (1.0 / vocab_rows)).astype(jnp.int32)

        def count(hits, axis):
            return jnp.sum(hits.astype(F32), axis, keepdims=True)

        most = jnp.zeros((1, 1), F32)
        for m in range(MICRO):
            row, col = ids_ref[m : m + 1], turned_ref[:, m : m + 1]
            same_id = row == col
            first_col = count(same_id & earlier, 1) == 0
            first_row = count(same_id & later, 0) == 0
            owner_row, owner_col = owner_of(row), owner_of(col)
            same_owner = owner_row == owner_col
            rank_row = count(same_owner & later & first_col, 0)
            rank_col = count(same_owner & earlier & first_row, 1)
            most = jnp.maximum(most, jnp.max(rank_row, 1, keepdims=True))

            @pl.when(here == m)
            def _():
                slot_row = jnp.sum(jnp.where(same_id & first_col, rank_col, 0.0), 0, keepdims=True)
                slot_col = jnp.sum(jnp.where(same_id & first_row, rank_row, 0.0), 1, keepdims=True)
                slot_row, slot_col = slot_row.astype(jnp.int32), slot_col.astype(jnp.int32)
                code_ref[...] = (owner_row + parts * first_row.astype(jnp.int32)) * 1024 + slot_row
                spot = jnp.where(slot_col < slots, owner_col * slots + slot_col, -1)
                spot_ref[...] = jnp.broadcast_to(spot, (IDS, LANES))
                lane = lax.broadcasted_iota(jnp.int32, (IDS, LANES), 1)
                local = (col - owner_col * vocab_rows).astype(F32)
                wanted = first_col & (slot_col < slots) & (slot_col == lane)
                wanted = jnp.where(wanted, local, 0.0)
                for part in range(parts):
                    asked = jnp.sum(jnp.where(owner_col == part, wanted, 0.0), 0, keepdims=True)
                    asked_ref[part] = asked.astype(jnp.int32)

        rounds = jnp.floor((most + 0.5) * (1.0 / slots)).astype(jnp.int32) + 1
        total = jnp.sum(jnp.sum(weights_ref[...], 0, keepdims=True), 1, keepdims=True)
        lane = lax.broadcasted_iota(jnp.int32, (1, LANES), 1)
        for part in range(parts):
            row = asked_ref[part]
            asked_ref[part] = jnp.where(lane == slots, rounds, jnp.where(lane == slots + 1, total, row))

    return pl.pallas_call(
        kernel,
        out_shape=[
            jax.ShapeDtypeStruct((parts, 1, LANES), jnp.int32),
            jax.ShapeDtypeStruct((1, IDS), jnp.int32),
            jax.ShapeDtypeStruct((IDS, LANES), jnp.int32),
        ],
        compiler_params=params_for(24),
        name="plan_requests",
    )(ids, turned, weights)


def fetch_rows(table, ids, first_section, plan, slots):
    parts = lax.axis_size("dp")
    vocab_rows = table.shape[0]
    asked, code, spot = plan
    asked = lax.all_to_all(asked, "dp", 0, 0)[:, 0]
    total_rounds = jnp.max(asked[:, slots])
    weight_sum = jnp.sum(asked[:, slots + 1])

    def answer(asked):
        rows = table.at[asked.reshape(-1)].get(mode="promise_in_bounds").reshape(parts, slots, D)
        return lax.all_to_all(rows, "dp", 0, 0).reshape(parts * slots, D)

    came = answer(asked[:, :slots])

    def more(state):
        return state[0] < total_rounds

    def another(state):
        turn, extra = state
        place, slot = code[0] // 1024, code[0] % 1024
        owner, first = place % parts, place >= parts
        local = pick(first_section, ids) - owner * vocab_rows
        here = slot - turn * slots
        at = jnp.where((here >= 0) & (here < slots), owner * slots + here, -1)
        hits = at[:, None] == jnp.arange(parts * slots)[None, :]
        wanted = jnp.sum(jnp.where(hits & first[:, None], local[:, None], 0), 0).reshape(parts, slots)
        rows = answer(lax.all_to_all(wanted, "dp", 0, 0))
        return turn + 1, extra + matmul(hits.astype(BF16), rows)

    extra = lax.while_loop(more, another, (jnp.int32(1), jnp.zeros((IDS, D), F32)))[1]
    return came, spot, extra, total_rounds, weight_sum.astype(F32)


def three_low(values):
    high = low(values)
    rest = values - high.astype(F32)
    middle = low(rest)
    return [high, middle, low(rest - middle.astype(F32))]


def in_groups(count):
    return lax.axis_size("dp") == COUPLING_GROUPS and count == 4 * PART_GROUPS


LINES = 4


def plane_groups(parts):
    planes = parts // LINES
    across_planes = [[plane * LINES + line for plane in range(planes)] for line in range(LINES)]
    return across_planes, [[plane * LINES + line for line in range(LINES)] for plane in range(planes)]


def gather_params(master, vector, after, before):
    parts = lax.axis_size("dp")
    count, width = master.shape[0], vector.shape[0]
    if in_groups(count):
        across_planes, in_plane = plane_groups(parts)
        some = pack_own(master, vector[None], len(in_plane))
        some = lax.all_to_all(some, "dp", 0, 0, axis_index_groups=across_planes)
        some, after = lax.optimization_barrier((some, after))
        own = lax.all_gather(some, "dp", axis_index_groups=in_plane)
        own, before = lax.optimization_barrier((own, before))
        return *unpack_all(own, lax.ppermute(own, "section", [(0, 1), (1, 0)]), width), after, before
    flat = low(jnp.concatenate([master.reshape(-1), vector]))
    gathered = lax.all_gather(flat, ("section", "dp")).reshape(MICRO, parts, -1)
    size = count * BLOCK**2
    all_blocks = gathered[:, :, :size].reshape(MICRO, parts * count, BLOCK, BLOCK)
    all_vectors = gathered[:, :, size:].reshape(MICRO, parts * width)
    both = [split_params(all_blocks[s], all_vectors[s]) for s in range(MICRO)]

    def stacked(which):
        down, bias_down, up, bias_up = (jnp.stack([pair[which][i] for pair in both]) for i in range(4))
        return Params(down, bias_down.astype(F32)[:, None], up, bias_up.astype(F32)[:, None])

    return stacked(0), stacked(1), after, before


def sum_at_owners(grads, loss_part, count):
    parts = lax.axis_size("dp")
    width = sum(BIASES) // parts
    flat = []
    for adapter, coupling in grads:
        blocks, vector = join_params(adapter, coupling)
        flat.append(
            jnp.concatenate([blocks.reshape(parts, count * BLOCK**2), vector.reshape(parts, width)], 1)
        )
    first = lax.axis_index("section") == 0
    summed = swap_add(jnp.where(first, flat[0], flat[1]), jnp.where(first, flat[1], flat[0]))
    owned = jnp.sum(lax.all_to_all(low(summed), "dp", 0, 0).astype(F32), 0)
    blocks = owned[: count * BLOCK**2].reshape(count, BLOCK, BLOCK)
    pair = jnp.stack([jnp.sum(owned * owned), loss_part[0, 0]])
    pair = jnp.pad(pair, (0, LANES - 2))[None, None]
    return blocks, owned[count * BLOCK**2 :], jnp.broadcast_to(pair, (parts * MICRO, 8, LANES))


def to_coupling_owners(group):
    arrived = []
    for place in range(1, PART_GROUPS):
        route = []
        for i, part in enumerate(SUMMED_AT):
            owner, at = divmod(ADAPTER_GROUPS + i, PART_GROUPS)
            if at == place and owner != part:
                route.append((part, owner))
        arrived.append(lax.ppermute(group, "dp", route))
    return [group] + arrived


def exact(spec, left, right):
    return jnp.einsum(spec, left, right, precision=HIGHEST)


def update(pair, grads, grad_vector, turned_old, state):
    master, momentum, stat_left, stat_right, root_left, root_right, vectors, vec_first, vec_second = state
    count = master.shape[0]
    outs = [shape_of(1, count, BLOCK, BLOCK)] * 5 + [low_shape(1, count, BLOCK, BLOCK)]
    outs += [shape_of(*vectors.shape)] * 3 + [shape_of(1, 1)] * 2

    def body(ins, out, scalar_refs, pair_refs, raw_refs, scratch):
        start(ins)
        grads, vector_ref, old_ref, state_refs, pair_ref = jax.tree.map(lambda operand: operand.get(), ins)
        master_ref, momentum_ref, stat_left_ref, stat_right_ref, root_left_ref, root_right_ref = state_refs[:6]
        vectors_ref, first_ref, second_ref = state_refs[6:]
        outs = [result.buffer for result in out]
        grad_ref = grads[0]
        if len(grads) > 1:
            grad_ref = scratch[0]
            unpack_own(grads[0], grads[1], grads[2:], grad_ref)
        totals = jnp.sum(pair_ref[...], 0)[:1]
        norm = jnp.sqrt(totals[:, :1])
        factor = CLIP_NORM / jnp.maximum(norm, CLIP_NORM)
        outs[9][...] = norm
        outs[10][...] = totals[:, 1:2]
        square = (1.0 - STAT_DECAY) * factor * factor
        for n in range(count):
            grad = grad_ref[n]
            clipped = grad * factor
            outs[0][0, n] = clipped
            outs[1][0, n] = FIRST_DECAY * momentum_ref[n] + (1.0 - FIRST_DECAY) * clipped
            left_square = exact_dot(grad, grad, ((1,), (1,)))
            right_square = exact_dot(grad, grad, ((0,), (0,)))
            turned = exact_dot(exact_dot(root_left_ref[n], grad, ((1,), (0,))), root_right_ref[n], ((1,), (0,)))
            outs[2][0, n] = STAT_DECAY * stat_left_ref[n] + square * left_square
            outs[3][0, n] = STAT_DECAY * stat_right_ref[n] + square * right_square
            direction = FIRST_DECAY * old_ref[n] + (1.0 - FIRST_DECAY) * factor * turned
            master_new = master_ref[n] - MAT_RATE * (direction + MAT_DECAY * master_ref[n])
            outs[4][0, n] = master_new
            outs[5][0, n] = low(master_new)
        clipped = vector_ref[:1, : vectors.shape[1]] * factor
        first_new = FIRST_DECAY * first_ref[...] + (1.0 - FIRST_DECAY) * clipped
        second_new = VEC_SECOND * second_ref[...] + (1.0 - VEC_SECOND) * clipped * clipped
        outs[6][...] = first_new
        outs[7][...] = second_new
        corrected_first = first_new / (1.0 - FIRST_DECAY**STEP)
        corrected_second = second_new / (1.0 - VEC_SECOND**STEP)
        outs[8][...] = vectors_ref[...] - VEC_RATE * (
            corrected_first / (jnp.sqrt(corrected_second) + VEC_EPS) + VEC_DECAY * vectors_ref[...]
        )

    ins = (grads, grad_vector, turned_old, state, pair)
    scratch = [pltpu.VMEM((count, BLOCK, BLOCK), F32)] if len(grads) > 1 else []
    return moved_call(body, (), ins, outs, (), scratch, "update")[0]


def shards(
    token_ids,
    lengths,
    positions,
    targets,
    loss_weights,
    embed_table,
    pos_table,
    norm_params,
    base_qkv,
    base_out,
    base_up,
    base_down,
    master,
    momentum,
    stat_left,
    stat_right,
    root_left,
    root_right,
    vectors,
    vec_first,
    vec_second,
):
    parts = lax.axis_size("dp")
    first_section = lax.axis_index("section") == 0
    slots = -(-IDS * 5 // (4 * parts * 16)) * 16

    ids = jnp.concatenate([token_ids[:, 0], targets[:, 0]], -1)
    asked, *plan = plan_requests(ids, loss_weights[:, 0], embed_table.shape[0], slots, parts)
    swap = [(0, 1), (1, 0)]
    pairs = [(w, lax.ppermute(w, "section", swap)) for w in (base_qkv, base_out, base_up, base_down)]
    came = lax.ppermute(norm_params, "section", swap)
    norms = jnp.concatenate([pick(first_section, (norm_params, came)), pick(first_section, (came, norm_params))])
    length = pick(first_section, lengths)
    spots = pick(first_section, positions[:, 0])
    row_weights = pick(first_section, loss_weights[:, 0]).astype(F32)
    row_weights = jnp.broadcast_to(row_weights[:, None], (COUNT, LANES))
    chosen = (spots[:, None] == jnp.arange(SEQ)[None, :]).astype(BF16)
    chosen_t = (spots[None, :] == jnp.arange(SEQ)[:, None]).astype(F32)
    turned_old = exact("nij,njk->nik", exact("nij,njk->nik", root_left[0], momentum[0]), root_right[0])
    early = norms, length, row_weights, chosen, chosen_t, turned_old
    adapter, coupling, asked, early = gather_params(master[0], vectors[0], asked, early)
    norms, length, row_weights, chosen, chosen_t, turned_old = early
    came, spot, extra, rounds, weight_sum = fetch_rows(embed_table, ids, first_section, (asked, *plan), slots)

    ins = ForwardIn(came, spot, extra, pos_table, norms, chosen, adapter, coupling)
    kept, rows = forward_kernel(ins, (length, rounds.reshape(1)), pairs, parts, slots)

    spread = [lax.all_to_all(half, "dp", 0, 0) for half in rows]
    first_half, spread[1] = lax.optimization_barrier((head_kernel(spread[0], embed_table), spread[1]))
    halves = [first_half, head_kernel(spread[1], embed_table)]
    merged = [lax.all_to_all(half, "dp", 0, 0) for half in halves]

    packed = in_groups(master.shape[1])
    weight_row = jnp.broadcast_to(weight_sum, (1, LANES))
    adapter, coupling = adapter[::2], coupling[::2]
    adapter_kept = kept.rest_0._replace(slope=(), normal_1=(), inverse_1=())
    ins = BackIn(
        merged, row_weights, weight_row, norms, chosen_t, adapter, coupling,
        kept.target_rows, adapter_kept, kept.attention_1, kept.rest_1, kept.last,
    )
    back = backward_kernel(ins, (length,), pairs, packed)
    loss_part, inner = back.loss, back.inner
    if packed:
        own, other = back.adapters[MICRO:]
        summed = low(swap_add(own.astype(F32), other))
        summed, inner = lax.optimization_barrier((summed, inner))
        adapter_came = lax.all_to_all(summed, "dp", 0, 0)
    inner_kept = kept.rest_0.slope, kept.rest_0.normal_1, kept.rest_0.inverse_1
    ins = FirstIn(
        inner, norms, inner_kept, kept.attention_0, coupling, kept.one, kept.two, back.one, back.two,
        back.adapters[:MICRO] if packed else (),
    )
    grads = first_backward(ins, (length,), pairs, packed)
    if packed:
        adapter_total, squares = sum_adapter(adapter_came)
        came = lax.all_to_all(low(swap_add(*grads)), "dp", 0, 0)
        group, bias, pair = sum_coupling(came, squares, loss_part, parts * MICRO)
        grad, grad_vector = [adapter_total, *to_coupling_owners(group)], bias
    else:
        both = [(back.adapters[s], grads[4 * s : 4 * s + 4]) for s in range(MICRO)]
        grad, grad_vector, pair = sum_at_owners(both, loss_part, master.shape[1])
        grad, grad_vector = [grad], grad_vector[None]
    pair = lax.all_to_all(pair, ("dp", "section"), 0, 0)
    state = (master, momentum, stat_left, stat_right, root_left, root_right)
    state = [value[0] for value in state] + [vectors, vec_first, vec_second]
    *outs, grad_norm, loss_sum = update(pair, grad, grad_vector, turned_old, state)
    return (*outs, grad_norm[0, 0], loss_sum[0, 0], weight_sum)


def solution(mesh):
    rows = P(None, "dp", None)
    section = P("section", None, None)
    blocks = P("section", "dp", None, None)
    biases = P("section", "dp")
    return jax.shard_map(
        shards,
        mesh=mesh,
        in_specs=(rows, P(None, "dp"), rows, rows, rows, P("dp", None), P())
        + (section,) * 5
        + (blocks,) * 6
        + (biases,) * 3,
        out_specs=(blocks,) * 6 + (biases,) * 3 + (P(),) * 3,
        check_vma=False,
    )
```

```python
import functools
from typing import Any, NamedTuple

import jax
import jax.numpy as jnp
import numpy as np
from jax import lax
from jax.experimental import pallas as pl
from jax.experimental.pallas import tpu as pltpu
from jax.sharding import PartitionSpec as P

D = 768
HEADS = 12
HEAD_DIM = 64
BOT = 384
INV_H = 192
SEQ = 512
COUNT = 32
MICRO = 2
BLOCK = 48
STEP = 10
HALF = 384
IDS = SEQ + COUNT

HIGHEST = lax.Precision.HIGHEST
NORM_EPS = 1e-12
CLIP_NORM = 0.02
FIRST_DECAY = 0.9
STAT_DECAY = 0.99
MAT_RATE = 0.1
MAT_DECAY = 0.01
VEC_RATE = 0.05
VEC_SECOND = 0.999
VEC_EPS = 1e-08
VEC_DECAY = 0.01
F32 = jnp.float32
BF16 = jnp.bfloat16

CDF_SCALE = 0.42 / 2.0**0.5
CDF_POLY = (
    0.2368242366796694,
    0.239585811361218,
    0.1947261443420679,
    0.2687426685879861,
    -0.13052645834187002,
    0.4406726942003943,
    -0.32025628294963193,
    0.07023101752398136,
)


def matmul(left, right):
    return jnp.dot(left, right, preferred_element_type=F32)


def matmul_t(left, right):
    return lax.dot_general(left, right, (((1,), (1,)), ((), ())), preferred_element_type=F32)


def inner_rows(left, right):
    return lax.dot_general(left, right, (((0,), (0,)), ((), ())), preferred_element_type=F32)


def low(values):
    return values.astype(BF16)


def in_strips(size, function, *arrays):
    count = arrays[0].shape[0]
    strips = [slice(at, at + size) for at in range(0, count, size)] if count % size == 0 else [slice(0, count)]
    results = [function(*[array[strip] for array in arrays]) for strip in strips]
    return tuple(jnp.concatenate(parts, 0) if len(parts) > 1 else parts[0] for parts in zip(*results))


def gelu_both(values):
    return in_strips(16, gelu_strip, values)


def gelu_strip(values):
    below = 1.0 + CDF_SCALE * jnp.abs(values)
    ratio = pl.reciprocal(below, approx=True)
    ratio = ratio * (2.0 - below * ratio)
    poly = jnp.full_like(ratio, 0.5 * CDF_POLY[-1])
    for factor in CDF_POLY[-2::-1]:
        poly = poly * ratio + 0.5 * factor
    bell = jnp.exp(-0.5 * values * values)
    tail = bell * (poly * ratio)
    cdf = jnp.where(values < 0, tail, 1.0 - tail)
    return values * cdf, cdf + values * (bell * (2.0 * np.pi) ** -0.5)


def layer_norm(values, gain, shift):
    def strip(values):
        centered = values - jnp.mean(values, -1, keepdims=True)
        inverse = lax.rsqrt(jnp.mean(centered * centered, -1, keepdims=True) + NORM_EPS)
        normal = centered * inverse
        return normal * gain + shift, normal, inverse

    values, normal, inverse = in_strips(16, strip, values)
    return values, (normal, inverse)


def norm_back(incoming, kept, gain):
    def strip(incoming, normal, inverse):
        scaled = incoming * gain
        mean = jnp.mean(scaled, -1, keepdims=True)
        return (inverse * (scaled - mean - normal * jnp.mean(scaled * normal, -1, keepdims=True)),)

    return in_strips(16, strip, incoming, *kept)[0]


def to_blocks(matrix):
    rows_in, cols_in = matrix.shape
    return (
        matrix.reshape(rows_in // BLOCK, BLOCK, cols_in // BLOCK, BLOCK)
        .transpose(0, 2, 1, 3)
        .reshape(-1, BLOCK, BLOCK)
    )


def from_blocks(blocks, rows_in, cols_in):
    return (
        blocks.reshape(rows_in // BLOCK, cols_in // BLOCK, BLOCK, BLOCK)
        .transpose(0, 2, 1, 3)
        .reshape(rows_in, cols_in)
    )


def split_params(blocks, vector):
    adapter_count = D * BOT // BLOCK**2
    half_count = HALF * INV_H // BLOCK**2
    split_at = 2 * adapter_count
    adapter = (
        from_blocks(blocks[:adapter_count], D, BOT),
        vector[:BOT],
        from_blocks(blocks[adapter_count:split_at], BOT, D),
        vector[BOT : BOT + D],
    )
    coupling = (
        from_blocks(blocks[split_at : split_at + half_count], HALF, INV_H),
        vector[BOT + D : BOT + D + INV_H],
        from_blocks(blocks[split_at + half_count :], INV_H, HALF),
        vector[BOT + D + INV_H :],
    )
    return adapter, coupling


def join_params(adapter, coupling):
    blocks = jnp.concatenate(
        [to_blocks(adapter[0]), to_blocks(adapter[2]), to_blocks(coupling[0]), to_blocks(coupling[2])]
    )
    return blocks, jnp.concatenate([adapter[1], adapter[3], coupling[1], coupling[3]], 1)[0]


GROUP_ROWS = 72
LANES = 128


def params_for(mebibytes):
    return pltpu.CompilerParams(vmem_limit_bytes=mebibytes * 2**20)


def roll(values, shift):
    return pltpu.roll(values, shift, 1)


def lane_of(values):
    return lax.broadcasted_iota(jnp.int32, values.shape, 1)


def fold_half(values, upper):
    top, bottom = values[:24], values[24:]
    if upper:
        return jnp.where(lane_of(top) < 64, roll(top, 64), bottom)
    return jnp.where(lane_of(top) < 64, top, roll(bottom, 64))


def unfold_half(values, upper):
    turned = roll(values, 64)
    return jnp.concatenate([turned, values] if upper else [values, turned], 0)


def join_pair(main_0, rest_0, main_1, rest_1):
    left = lane_of(main_0) < 64
    turned = roll(main_1, 64)
    return (
        main_0,
        jnp.where(left, unfold_half(rest_0, False), turned),
        jnp.where(left, turned, unfold_half(rest_1, True)),
    )


def cut_pair(tile_0, tile_1, tile_2):
    left = lane_of(tile_0) < 64
    return (
        (tile_0, fold_half(tile_1, False)),
        (jnp.where(left, roll(tile_1, 64), roll(tile_2, 64)), fold_half(tile_2, True)),
    )


def chunk_rows(own_blocks):
    return own_blocks // 4 * GROUP_ROWS + 8


def bias_row(tiles, part, width):
    at, shift = divmod(part * width, LANES)
    lane = lane_of(tiles[0])
    row = tiles[at]
    if shift:
        row = jnp.where(lane < LANES - shift, roll(row, LANES - shift), roll(tiles[at + 1], LANES - shift))
    return jnp.where(lane < width, row, 0.0)


def bias_tiles(first, second, third, fourth):
    cut = lambda values: [values[:, at : at + LANES] for at in range(0, values.shape[1], LANES)]
    zero = jnp.zeros((1, LANES), F32)
    left = lane_of(zero) < 64
    third_tail = jnp.concatenate([third[:, LANES:]] * 2, 1)
    turned = [roll(tile, 64) for tile in cut(fourth)]
    joints = [jnp.where(left, one, two) for one, two in zip([third_tail] + turned, turned + [zero])]
    return cut(first) + cut(second) + [third[:, :LANES]] + joints + [zero]


def tiles_of_rows(rows, width):
    tiles = []
    for tile in range(-(-len(rows) * width // LANES)):
        value = jnp.zeros((8, LANES), F32)
        lane = lane_of(value)
        for part, row in enumerate(rows):
            shift = part * width - tile * LANES
            if shift >= LANES or shift + width <= 0:
                continue
            turned = roll(row, shift % LANES) if shift % LANES else row
            value = jnp.where((lane >= shift) & (lane < shift + width), turned, value)
        tiles.append(value)
    return tiles


def pack_own(master, vector, copies):
    count, width = master.shape[0], vector.shape[1]

    def kernel(master_ref, bias_ref, out_ref):
        row = lax.broadcasted_iota(jnp.int32, (BLOCK, 256), 0)
        col = lax.broadcasted_iota(jnp.int32, (BLOCK, 256), 1)
        pieces = []
        for group in range(count // 4):
            wide = jnp.zeros((BLOCK, 256), F32)
            for j in range(4):
                wide += matmul(low(master_ref[4 * group + j]), (col == row + BLOCK * j).astype(BF16))
            pieces += [wide[:, :LANES], fold_half(wide[:, LANES:], False)]
        bias = jnp.concatenate([bias_ref[...], jnp.zeros((1, LANES - width), F32)], 1)
        pieces.append(jnp.concatenate([bias, jnp.zeros((7, LANES), F32)], 0))
        packed = low(jnp.concatenate(pieces, 0))
        for copy in range(copies):
            out_ref[copy] = packed

    return pl.pallas_call(
        kernel,
        out_shape=jax.ShapeDtypeStruct((copies, chunk_rows(count), LANES), BF16),
        name="pack_own",
    )(master, vector)


MATRICES = ((D, BOT), (BOT, D), (HALF, INV_H), (INV_H, HALF))
BIASES = (BOT, D, INV_H, HALF)


def unpack_all(own, came, width):
    lines, planes, rows, _ = own.shape
    parts = lines * planes
    per_part = (rows - 8) // GROUP_ROWS

    def kernel(own_hbm, came_hbm, *refs):
        out_hbm, in_bufs, out_refs, in_sems, out_sems = refs[:8], refs[8], refs[9:17], refs[17], refs[18]
        here = lax.axis_index("section")
        copies = [
            pltpu.make_async_copy(ref, in_bufs.at[at], in_sems.at[i])
            for i, (ref, at) in enumerate(((own_hbm, here), (came_hbm, 1 - here)))
        ]
        for copy in copies:
            copy.start()
        for copy in copies:
            copy.wait()

        def unpack(s, carry):
            cache = {}

            def group(index):
                part = index // per_part
                if part not in cache:
                    cache.clear()
                    cache[part] = in_bufs[s, part % lines, part // lines].astype(F32)
                base = index % per_part * GROUP_ROWS
                chunk = cache[part]
                return chunk[base : base + BLOCK], chunk[base + BLOCK : base + GROUP_ROWS]

            index = 0
            for (height, columns), out_ref in zip(MATRICES, out_refs):
                for top in range(0, height, BLOCK):
                    if columns == INV_H:
                        main, rest = group(index)
                        index += 1
                        out_ref[s, top : top + BLOCK, :LANES] = low(main)
                        out_ref[s, top : top + BLOCK, LANES:] = low(unfold_half(rest, False)[:, :64])
                        continue
                    for left in range(0, columns, HALF):
                        tiles = join_pair(*group(index), *group(index + 1))
                        index += 2
                        for j, tile in enumerate(tiles):
                            at = left + j * LANES
                            out_ref[s, top : top + BLOCK, at : at + LANES] = low(tile)
            tiles = tiles_of_rows(
                [in_bufs[s, part % lines, part // lines, rows - 16 :].astype(F32)[8:] for part in range(parts)], width
            )
            first, second, third, fourth = out_refs[4:]
            first[s] = jnp.concatenate(tiles[:3], 1)[:1]
            second[s] = jnp.concatenate(tiles[3:9], 1)[:1]
            third[s] = jnp.concatenate([tiles[9], tiles[10][:, :64]], 1)[:1]
            left = lane_of(tiles[0]) < 64
            turned = [roll(tile, 64) for tile in tiles[10:14]]
            fourth[s] = jnp.concatenate(
                [jnp.where(left, one, two) for one, two in zip(turned, turned[1:])], 1
            )[:1]
            return carry

        lax.fori_loop(0, MICRO, unpack, 0)
        copies = [
            pltpu.make_async_copy(buf, ref, out_sems.at[i]) for i, (buf, ref) in enumerate(zip(out_refs, out_hbm))
        ]
        for copy in copies:
            copy.start()
        for copy in copies:
            copy.wait()

    shapes = [((MICRO,) + shape, BF16) for shape in MATRICES] + [((MICRO, 1, size), F32) for size in BIASES]
    hbm = pl.BlockSpec(memory_space=pltpu.HBM)
    arrays = pl.pallas_call(
        kernel,
        in_specs=[hbm] * 2,
        out_specs=[hbm] * 8,
        out_shape=[jax.ShapeDtypeStruct(*shape) for shape in shapes],
        scratch_shapes=[pltpu.VMEM((MICRO, lines, planes, rows, LANES), BF16)]
        + [pltpu.VMEM(*shape) for shape in shapes]
        + [pltpu.SemaphoreType.DMA((2,)), pltpu.SemaphoreType.DMA((8,))],
        compiler_params=params_for(MOST_VMEM),
        name="unpack_all",
    )(own, came)
    down, up, c_down, c_up, bias_down, bias_up, c_bias_down, c_bias_up = arrays
    return Params(down, bias_down, up, bias_up), Params(c_down, c_bias_down, c_up, c_bias_up)


ADAPTER_GROUPS = 2 * D * BOT // BLOCK**2 // 4
COUPLING_GROUPS = 2 * HALF * INV_H // BLOCK**2 // 4
PART_GROUPS = (ADAPTER_GROUPS + COUPLING_GROUPS) // COUPLING_GROUPS
PART_ROWS = PART_GROUPS * GROUP_ROWS
SUMMED_AT = (12, 13, 1, 5, 9, 0, 14, 2, 6, 10, 4, 15, 3, 7, 11, 8)


def groups_of(refs, shapes):
    groups = []
    for ref, (height, width) in zip(refs, shapes):
        for top in range(0, height, BLOCK):
            band = slice(top, top + BLOCK)
            if width == INV_H:
                tail = ref[band, LANES:]
                groups.append((ref[band, :LANES], fold_half(jnp.concatenate([tail, tail], 1), False)))
                continue
            for left in range(0, width, HALF):
                groups += cut_pair(*[ref[band, left + j * LANES : left + (j + 1) * LANES] for j in range(3)])
    return [jnp.concatenate(group, 0) for group in groups]


def pack_adapter(refs, store):
    groups = groups_of(refs, MATRICES[:2])
    empty = jnp.zeros((GROUP_ROWS, LANES), F32)
    for part in range(COUPLING_GROUPS):
        chunk = groups[part * PART_GROUPS : (part + 1) * PART_GROUPS]
        chunk += [empty] * (PART_GROUPS - len(chunk))
        store(part, low(jnp.concatenate(chunk, 0)))


def pack_coupling(refs, tiles, width, store):
    for part, group in zip(SUMMED_AT, groups_of(refs, MATRICES[2:])):
        bias = jnp.concatenate([bias_row(tiles, part, width), jnp.zeros((7, LANES), F32)], 0)
        store(part, jnp.concatenate([group, bias], 0))


def sum_parts(came_ref):
    total = came_ref[0].astype(F32)
    for part in range(1, came_ref.shape[0]):
        total += came_ref[part].astype(F32)
    return total


def square_sum(values):
    return jnp.sum(jnp.sum(values * values, 0, keepdims=True), 1, keepdims=True)


def sum_adapter(came):
    def kernel(came_ref, total_ref, square_ref):
        total = sum_parts(came_ref)
        total_ref[...] = total
        square_ref[...] = square_sum(total)

    return pl.pallas_call(
        kernel,
        out_shape=[jax.ShapeDtypeStruct((PART_ROWS, LANES), F32), jax.ShapeDtypeStruct((1, 1), F32)],
        compiler_params=params_for(32),
        name="sum_adapter",
    )(came)


def sum_coupling(came, squares, loss_part, copies):
    def kernel(came_ref, square_ref, loss_ref, group_ref, bias_ref, pair_ref):
        total = sum_parts(came_ref)
        group_ref[...] = total[:GROUP_ROWS]
        bias_ref[...] = total[GROUP_ROWS:]
        squares = square_ref[...] + square_sum(total)
        lane = lax.broadcasted_iota(jnp.int32, (8, LANES), 1)
        pair = jnp.where(lane == 0, squares, jnp.where(lane == 1, loss_ref[:, :1], 0.0))
        for copy in range(copies):
            pair_ref[copy] = pair

    return pl.pallas_call(
        kernel,
        out_shape=[
            jax.ShapeDtypeStruct((GROUP_ROWS, LANES), F32),
            jax.ShapeDtypeStruct((8, LANES), F32),
            jax.ShapeDtypeStruct((copies, 8, LANES), F32),
        ],
        name="sum_coupling",
    )(came, squares, loss_part)


def exact_dot(left, right, dims):
    return lax.dot_general(left, right, (dims, ((), ())), precision=HIGHEST, preferred_element_type=F32)


def unpack_own(total_ref, own_ref, group_refs, grad_ref):
    part = lax.axis_index("dp")
    own_place = jnp.int32(-1)
    for i, owner in enumerate(SUMMED_AT):
        at = ADAPTER_GROUPS + i
        if at // PART_GROUPS == owner:
            own_place = jnp.where(part == owner, at % PART_GROUPS, own_place)
    for group in range(PART_GROUPS):
        total = total_ref[group * GROUP_ROWS : (group + 1) * GROUP_ROWS]
        total = total + jnp.where(own_place == group, own_ref[...], 0.0)
        if group:
            total = total + group_refs[group - 1][...]
        main, rest = total[:BLOCK], unfold_half(total[BLOCK:], False)
        lane = lane_of(main)
        pieces = (
            main,
            roll(main, 80),
            jnp.where(lane < 32, roll(main, 32), roll(rest, 32)),
            roll(rest, 112),
        )
        for j, values in enumerate(pieces):
            grad_ref[4 * group + j] = values[:, :BLOCK]


MOST_VMEM = 64
GROUP = 256
HEADS_IN = GROUP // HEAD_DIM
GROUPS = D // GROUP
FF = 3072
TILE = 512
TILES = FF // TILE
STEP_ROWS = 256
SMALL_ROWS = 16


def rows_of(count, size):
    return [slice(at, at + min(size, count)) for at in range(0, count, size)]


def shape_of(*dims, kind=F32):
    return jax.ShapeDtypeStruct(dims, kind)


class Params(NamedTuple):
    down: Any
    bias_down: Any
    up: Any
    bias_up: Any


class Branch(NamedTuple):
    lin: Any
    act: Any
    slope: Any


class Attention(NamedTuple):
    query: Any
    key: Any
    value: Any
    lse: Any


class Rest(NamedTuple):
    normal_1: Any
    inverse_1: Any
    slope: Any
    branch: Any
    normal_2: Any
    inverse_2: Any


class Last(NamedTuple):
    one: Any
    two: Any
    normal: Any
    inverse: Any
    normed: Any


class ForwardIn(NamedTuple):
    came: Any
    spot: Any
    extra: Any
    pos: Any
    norms: Any
    chosen: Any
    adapter: Any
    coupling: Any


class Forward(NamedTuple):
    target_rows: Any
    one: Any
    two: Any
    attention_0: Any
    rest_0: Any
    attention_1: Any
    rest_1: Any
    last: Any


class BackIn(NamedTuple):
    merged: Any
    row_weights: Any
    weight_sum: Any
    norms: Any
    chosen_t: Any
    adapter: Any
    coupling: Any
    target_rows: Any
    rest_0: Any
    attention_1: Any
    rest_1: Any
    last: Any


class Back(NamedTuple):
    loss: Any
    one: Any
    two: Any
    adapters: Any
    inner: Any


class FirstIn(NamedTuple):
    inner: Any
    norms: Any
    inner_kept: Any
    attention: Any
    coupling: Any
    one: Any
    two: Any
    grads_one: Any
    grads_two: Any
    biases: Any


class Operand:
    def __init__(self, ref, buffer, sem):
        self.buffer, self.copy = buffer, pltpu.make_async_copy(ref, buffer, sem)
        self.started = self.waited = False

    def start(self):
        if not self.started:
            self.copy.start()
        self.started = True

    def get(self):
        self.start()
        if not self.waited:
            self.copy.wait()
        self.waited = True
        return self.buffer


class Result:
    def __init__(self, ref, buffer, sem):
        self.buffer, self.copy = buffer, pltpu.make_async_copy(buffer, ref, sem)
        self.sent = False

    def send(self):
        if not self.sent:
            self.copy.start()
        self.sent = True


def start(*operands):
    for operand in jax.tree.leaves(operands):
        operand.start()


def send(*results):
    for result in jax.tree.leaves(results):
        result.send()


def moved_call(body, scalars, ins, outs, pairs, scratch, name, raw_outs=()):
    in_leaves, in_tree = jax.tree.flatten(ins)
    out_leaves, out_tree = jax.tree.flatten(outs)

    def kernel(*refs):
        refs = list(refs)

        def take(count):
            taken, refs[:] = refs[:count], refs[count:]
            return taken

        scalar_refs, in_refs = take(len(scalars)), take(len(in_leaves))
        pair_refs = [tuple(take(2)) for _ in pairs]
        out_refs, raw_refs = take(len(out_leaves)), take(len(raw_outs))
        in_buffers, out_buffers, (in_sems, out_sems) = take(len(in_leaves)), take(len(out_leaves)), take(2)
        operands = [Operand(*two, in_sems.at[i]) for i, two in enumerate(zip(in_refs, in_buffers))]
        results = [Result(*two, out_sems.at[i]) for i, two in enumerate(zip(out_refs, out_buffers))]
        body(in_tree.unflatten(operands), out_tree.unflatten(results), scalar_refs, pair_refs, raw_refs, refs)
        send(results)
        for operand in operands:
            operand.get()
        for result in results:
            result.copy.wait()

    hbm = pl.BlockSpec(memory_space=pltpu.HBM)
    buffers = [pltpu.VMEM(value.shape, value.dtype) for value in (*in_leaves, *out_leaves)]
    results = pl.pallas_call(
        kernel,
        in_specs=[pl.BlockSpec(memory_space=pltpu.SMEM)] * len(scalars) + [hbm] * (len(in_leaves) + 2 * len(pairs)),
        out_specs=[hbm] * (len(out_leaves) + len(raw_outs)),
        out_shape=[*out_leaves, *raw_outs],
        scratch_shapes=buffers
        + [pltpu.SemaphoreType.DMA((len(in_leaves),)), pltpu.SemaphoreType.DMA((len(out_leaves),))]
        + list(scratch),
        compiler_params=params_for(MOST_VMEM),
        name=name,
    )(*scalars, *in_leaves, *[w for pair in pairs for w in pair])
    return out_tree.unflatten(results[: len(out_leaves)]), results[len(out_leaves) :]


def start_copy(pair, section, window, target, sem):
    own, came = pair
    here = lax.axis_index("section") == section

    @pl.when(here)
    def _():
        pltpu.make_async_copy(own.at[window], target, sem).start()

    @pl.when(jnp.logical_not(here))
    def _():
        pltpu.make_async_copy(came.at[window], target, sem).start()


def wait_copy(pair, window, target, sem):
    pltpu.make_async_copy(pair[0].at[window], target, sem).wait()


def qkv_window(group, part):
    return 0, slice(None), pl.ds(part * D + group * GROUP, GROUP)


def qkv_buffers():
    return [pltpu.VMEM((GROUPS, 3, D, GROUP), BF16), pltpu.SemaphoreType.DMA((GROUPS, 3))]


def start_qkv(pair, section, buffers):
    for group in range(GROUPS):
        for part in range(3):
            start_copy(pair, section, qkv_window(group, part), buffers[0].at[group, part], buffers[1].at[group, part])


def wait_qkv(pair, buffers, group, part):
    wait_copy(pair, qkv_window(0, 0), buffers[0].at[group, part], buffers[1].at[group, part])


UP_WINDOWS = [(0, slice(None), slice(j * TILE, (j + 1) * TILE)) for j in range(TILES)]
DOWN_WINDOWS = [(0, slice(j * TILE, (j + 1) * TILE), slice(None)) for j in range(TILES)]
OUT_WINDOW = (0, slice(None), slice(None))


def rest_buffers():
    return [
        pltpu.VMEM((D, D), BF16),
        pltpu.VMEM((TILES, D, TILE), BF16),
        pltpu.VMEM((TILES, TILE, D), BF16),
        pltpu.SemaphoreType.DMA((2 * TILES + 1,)),
    ]


def start_out(pairs, section, buffers):
    start_copy(pairs[0], section, OUT_WINDOW, buffers[0], buffers[3].at[2 * TILES])


def start_tiles(pairs, section, buffers):
    for j in range(TILES):
        start_copy(pairs[1], section, UP_WINDOWS[j], buffers[1].at[j], buffers[3].at[j])
        start_copy(pairs[2], section, DOWN_WINDOWS[j], buffers[2].at[j], buffers[3].at[TILES + j])


def wait_out(pairs, buffers):
    wait_copy(pairs[0], OUT_WINDOW, buffers[0], buffers[3].at[2 * TILES])


def wait_up(pairs, buffers, tile):
    wait_copy(pairs[1], UP_WINDOWS[0], buffers[1].at[tile], buffers[3].at[tile])


def wait_down(pairs, buffers, tile):
    wait_copy(pairs[2], DOWN_WINDOWS[0], buffers[2].at[tile], buffers[3].at[TILES + tile])


def across(values):
    return jnp.broadcast_to(values, (values.shape[0], LANES))


def group_columns(group):
    return pl.ds(pl.multiple_of(group * GROUP, GROUP), GROUP)


def tile_columns(tile):
    return pl.ds(pl.multiple_of(tile * TILE, TILE), TILE)


def head_mask(values, head):
    lane = lax.broadcasted_iota(jnp.int32, values.shape, 1)
    return (lane >= head * HEAD_DIM) & (lane < (head + 1) * HEAD_DIM)


def only_head(values, head):
    return jnp.where(head_mask(values, head), values, jnp.zeros_like(values))


def scaled_query(query):
    return low(query.astype(F32) * HEAD_DIM**-0.5)


def key_bias(length, shape, axis):
    return jnp.where(lax.broadcasted_iota(jnp.int32, shape, axis) < length, 0.0, -1e30)


def softmax_rows(scores):
    highest = jnp.max(scores, 1, keepdims=True)
    exponent = jnp.exp(scores - highest)
    total = jnp.sum(exponent, 1, keepdims=True)
    return low(exponent * (1.0 / total)), highest + jnp.log(total)


def branch_rows(low_in, weights):
    active, slope = gelu_both(matmul(low_in, weights[0]) + weights[1])
    active = low(active)
    return matmul(active, weights[2]) + weights[3], active, low(slope)


def alternate(*lists):
    steps = [((i + 0.5) / len(steps), k, step) for k, steps in enumerate(lists) for i, step in enumerate(steps)]
    for _, _, step in sorted(steps, key=lambda entry: entry[:2]):
        step()


def section_params(params, section):
    return [operand.get()[section] for operand in params]


def rest_rows(out, rows, section, norms, adapter, hidden, mixed, finish, scratch, pairs, buffers, after_loop=None):
    att_low, acc, u_even, u_odd, g_even, g_odd = scratch
    gain = lambda i: norms[section, i : i + 1]
    parts = rows_of(rows, STEP_ROWS)
    every = slice(0, rows)
    wait_out(pairs, buffers)
    for part in parts:
        first = hidden[part] + matmul(mixed[part], buffers[0][...])
        values, (normal, inverse) = layer_norm(first, gain(2), gain(3))
        acc[part] = values
        att_low[part] = low(values)
        out.normal_1.buffer[part] = normal
        out.inverse_1.buffer[part] = across(inverse)
    send(out.normal_1, out.inverse_1)
    wait_up(pairs, buffers, 0)
    g_odd[every] = jnp.zeros_like(g_odd[every])

    def gelu_steps(u_ref, g_ref, tile):
        def step(at):
            active, slope = gelu_both(u_ref[at])
            g_ref[at] = low(active)
            out.slope.buffer[at, tile_columns(tile)] = low(slope)

        return [functools.partial(step, at) for at in rows_of(rows, SMALL_ROWS)]

    def up_steps(u_ref, tile):
        def step(columns):
            u_ref[every, columns] = matmul(att_low[every], buffers[1][tile, :, columns])

        return [functools.partial(step, columns) for columns in rows_of(TILE, GROUP)]

    def down_steps(g_ref, tile):
        def step(columns):
            acc[every, columns] += matmul(g_ref[every], buffers[2][tile, :, columns])

        return [functools.partial(step, columns) for columns in rows_of(D, GROUP)]

    alternate(up_steps(u_even, 0))

    def turn(j, carry):
        even, odd = 2 * j, 2 * j + 1
        before, after = jnp.maximum(even - 1, 0), jnp.minimum(even + 2, TILES - 1)
        wait_down(pairs, buffers, even)
        wait_up(pairs, buffers, odd)
        wait_down(pairs, buffers, odd)

        @pl.when(even + 2 < TILES)
        def _():
            wait_up(pairs, buffers, even + 2)

        alternate(gelu_steps(u_even, g_even, even), down_steps(g_odd, before) + up_steps(u_odd, odd))
        alternate(gelu_steps(u_odd, g_odd, odd), down_steps(g_even, even) + up_steps(u_even, after))
        return carry

    lax.fori_loop(0, TILES // 2, turn, 0)
    alternate(down_steps(g_odd, TILES - 1))
    if after_loop is not None:
        after_loop()
    send(out.slope)
    weights = section_params(adapter, section)
    for part in parts:
        summed = acc[part]
        low_in = low(summed)
        added, *kept = branch_rows(low_in, weights)
        for result, value in zip(out.branch, (low_in, *kept)):
            result.buffer[part] = value
        values, (normal, inverse) = layer_norm(summed + added, gain(4), gain(5))
        out.normal_2.buffer[part], out.inverse_2.buffer[part] = normal, across(inverse)
        finish(part, values)
    send(out.branch, out.normal_2, out.inverse_2)


def low_shape(*dims):
    return shape_of(*dims, kind=BF16)


def branch_shapes(rows, wide, narrow):
    return Branch(low_shape(rows, wide), low_shape(rows, narrow), low_shape(rows, narrow))


def rest_shapes(rows):
    wide, thin = shape_of(rows, D), shape_of(rows, LANES)
    return Rest(wide, thin, low_shape(rows, FF), branch_shapes(rows, D, BOT), wide, thin)


def forward_kernel(ins, scalars, pairs, parts, slots):
    coupling_shapes = lambda rows: branch_shapes(rows, HALF, INV_H)
    outs = Forward(
        target_rows=shape_of(COUNT, D),
        one=coupling_shapes(SEQ),
        two=coupling_shapes(SEQ),
        attention_0=Attention(*[low_shape(SEQ, D)] * 3, shape_of(GROUPS, 8, SEQ)),
        rest_0=rest_shapes(SEQ),
        attention_1=Attention(
            low_shape(COUNT, D), *[low_shape(SEQ, D)] * 2, shape_of(GROUPS, HEADS_IN * COUNT, LANES)
        ),
        rest_1=rest_shapes(COUNT),
        last=Last(
            coupling_shapes(COUNT), coupling_shapes(COUNT),
            shape_of(COUNT, D), shape_of(COUNT, LANES), low_shape(COUNT, D),
        ),
    )

    def body(ins, out, scalar_refs, pair_refs, raw_refs, scratch):
        length = scalar_refs[0][0]
        hidden, x_low, s_even, s_odd, p_even, p_odd, lse_buf, mixed, section_out = scratch[:9]
        at_spots, at_low, mixed_1 = scratch[9:12]
        rest_scratch, qkv_0, qkv_1, rest_w = scratch[12:18], scratch[18:20], scratch[20:22], scratch[22:26]
        row_sems, joined = scratch[26:28]
        qkv_pair, rest_pairs = pair_refs[0], pair_refs[1:]

        start(ins.came, ins.spot, ins.pos, ins.norms, ins.coupling)
        norms = ins.norms.get()
        norm = lambda s, i: norms[s, i : i + 1]

        came, spot = ins.came.get(), ins.spot.get()
        start_qkv(qkv_pair, 0, qkv_0)
        start_out(rest_pairs, 0, rest_w)

        def rows_at(part):
            lane = lax.broadcasted_iota(jnp.int32, (part.stop - part.start, parts * slots), 1)
            hits = (spot[part][:, :1] == lane).astype(BF16)
            return matmul(hits, came[...])

        targets = slice(SEQ, SEQ + COUNT)
        out.target_rows.buffer[...] = rows_at(targets)
        for part in rows_of(SEQ, STEP_ROWS):
            hidden[part] = rows_at(part)

        @pl.when(scalar_refs[1][0] > 1)
        def _():
            ins.extra.copy.start()
            ins.extra.copy.wait()
            out.target_rows.buffer[...] += ins.extra.buffer[targets]
            hidden[...] += ins.extra.buffer[:SEQ]

        ins.extra.started = ins.extra.waited = True
        send(out.target_rows)
        start(ins.adapter, ins.chosen)
        start_tiles(rest_pairs, 0, rest_w)
        one, two = section_params(ins.coupling, 0), section_params(ins.coupling, 1)

        def put(results, part, *values):
            for result, value in zip(results, values):
                result.buffer[part] = value

        for part in rows_of(SEQ, STEP_ROWS):
            started, _ = layer_norm(hidden[part] + ins.pos.get()[part].astype(F32), norm(0, 0), norm(0, 1))
            left, right = started[:, :HALF], started[:, HALF:]
            low_one = low(right)
            added, active, slope = branch_rows(low_one, one)
            put(out.one, part, low_one, active, slope)
            left = left + added
            low_two = low(left)
            added, active, slope = branch_rows(low_two, two)
            put(out.two, part, low_two, active, slope)
            right = right + added
            hidden[part, :HALF] = left
            hidden[part, HALF:] = right
            x_low[part, :HALF] = low_two
            x_low[part, HALF:] = low(right)
        send(out.one, out.two)

        start_qkv(qkv_pair, 1, qkv_1)
        lse_buf[...] = jnp.zeros((SEQ, LANES), F32)
        q_ref, k_ref, v_ref, lse_ref = (result.buffer for result in out.attention_0)

        def attend(group, carry):
            columns = group_columns(group)
            for part, ref in enumerate((q_ref, k_ref, v_ref)):
                wait_qkv(qkv_pair, qkv_0, group, part)
                ref[:, columns] = low(matmul(x_low[...], qkv_0[0][group, part]))
            query = scaled_query(q_ref[:, columns])
            key, value = k_ref[:, columns], v_ref[:, columns]
            bias = key_bias(length, (1, SEQ), 1)
            lane = lax.broadcasted_iota(jnp.int32, (SMALL_ROWS * 2, LANES), 1)
            buffers = ((s_even, p_even), (s_odd, p_odd)) * 2

            def score_steps(head):
                def step():
                    buffers[head][0][...] = matmul_t(only_head(query, head), key)

                return [step] if head < HEADS_IN else []

            def soft_steps(head):
                def step(rows):
                    soft, lse = softmax_rows(buffers[head][0][rows] + bias)
                    buffers[head][1][rows] = soft
                    lse_buf[rows] = jnp.where(lane == head, lse, lse_buf[rows])

                return [functools.partial(step, rows) for rows in rows_of(SEQ, SMALL_ROWS * 2)]

            def mix_steps(head):
                def step():
                    mixed_head = matmul(buffers[head][1][...], value)
                    if head == 0:
                        joined[...] = mixed_head
                    else:
                        joined[...] = jnp.where(head_mask(mixed_head, head), mixed_head, joined[...])

                return [step] if head >= 0 else []

            alternate(score_steps(0))
            for head in range(HEADS_IN):
                alternate(soft_steps(head), score_steps(head + 1) + mix_steps(head - 1))
            alternate(mix_steps(HEADS_IN - 1))
            mixed[:, columns] = low(joined[...])
            lse_ref[group] = jnp.transpose(lse_buf[...])[:8]
            return carry

        lax.fori_loop(0, GROUPS, attend, 0)
        send(out.attention_0)

        def to_section_out(part, values):
            section_out[part] = low(values)

        def next_weights():
            start_out(rest_pairs, 1, rest_w)
            start_tiles(rest_pairs, 1, rest_w)

        rest_rows(
            out.rest_0, SEQ, 0, norms, ins.adapter, hidden, mixed, to_section_out,
            rest_scratch, rest_pairs, rest_w, next_weights,
        )

        at_spots[...] = matmul(ins.chosen.get()[...], section_out[...])
        at_low[...] = low(at_spots[...])
        q_1, k_1, v_1, lse_1 = (result.buffer for result in out.attention_1)

        groups = rows_of(D, GROUP)
        for group, columns in enumerate(groups):
            for part, ref in enumerate((q_1, k_1, v_1)):
                wait_qkv(qkv_pair, qkv_1, group, part)
                source = at_low if part == 0 else section_out
                ref[:, columns] = low(matmul(source[...], qkv_1[0][group, part]))
        bias = key_bias(length, (1, SEQ), 1)
        for group, columns in enumerate(groups):
            query = scaled_query(q_1[:, columns])
            query = jnp.concatenate([only_head(query, head) for head in range(HEADS_IN)], 0)
            soft, lse = softmax_rows(matmul_t(query, k_1[:, columns]) + bias)
            lse_1[group] = across(lse)
            every = matmul(soft, v_1[:, columns])
            mixed_group = every[:COUNT]
            for head in range(1, HEADS_IN):
                rows = slice(head * COUNT, (head + 1) * COUNT)
                mixed_group = jnp.where(head_mask(mixed_group, head), every[rows], mixed_group)
            mixed_1[:, columns] = low(mixed_group)
        send(out.attention_1)

        def to_normed(part, values):
            left, right = values[:, :HALF], values[:, HALF:]
            low_two = low(left)
            taken, active, slope = branch_rows(low_two, two)
            put(out.last.two, part, low_two, active, slope)
            right = right - taken
            low_one = low(right)
            taken, active, slope = branch_rows(low_one, one)
            put(out.last.one, part, low_one, active, slope)
            left = left - taken
            values, (normal, inverse) = layer_norm(jnp.concatenate([left, right], 1), norm(1, 0), norm(1, 1))
            put(out.last[2:], part, normal, across(inverse), low(values))

        rest_rows(
            out.rest_1, COUNT, 1, norms, ins.adapter, at_spots, mixed_1, to_normed,
            rest_scratch, rest_pairs, rest_w,
        )
        normed = out.last.normed.buffer
        copies = [
            pltpu.make_async_copy(normed.at[half], raw_refs[i].at[part], row_sems.at[i, part])
            for i, half in enumerate(rows_of(COUNT, COUNT // 2))
            for part in range(parts)
        ]
        for copy in copies:
            copy.start()
        for copy in copies:
            copy.wait()

    buffer = lambda *dims: pltpu.VMEM(dims, F32)
    buffer_low = lambda *dims: pltpu.VMEM(dims, BF16)
    scratch = [buffer(SEQ, D), buffer_low(SEQ, D), buffer(SEQ, SEQ), buffer(SEQ, SEQ)]
    scratch += [buffer_low(SEQ, SEQ), buffer_low(SEQ, SEQ), buffer(SEQ, LANES)]
    scratch += [buffer_low(SEQ, D), buffer_low(SEQ, D)]
    scratch += [buffer(COUNT, D), buffer_low(COUNT, D), buffer_low(COUNT, D)]
    scratch += [buffer_low(SEQ, D), buffer(SEQ, D), buffer(SEQ, TILE), buffer(SEQ, TILE)]
    scratch += [buffer_low(SEQ, TILE), buffer_low(SEQ, TILE)]
    scratch += qkv_buffers() + qkv_buffers() + rest_buffers()
    scratch += [pltpu.SemaphoreType.DMA((2, parts)), buffer(SEQ, GROUP)]
    raw = [low_shape(parts, COUNT // 2, D)] * 2
    kept, rows = moved_call(body, scalars, ins, outs, pairs, scratch, "forward", raw)
    return kept, rows


def column_sum(values):
    return jnp.sum(values.astype(F32), 0, keepdims=True)


def branch_grads(grad_low, kept, weights, out_refs):
    low_in, active, slope = kept
    hidden_grad = low(matmul_t(grad_low, weights[2]) * slope.astype(F32))
    out_refs[0][...] = inner_rows(low_in, hidden_grad)
    out_refs[1][...] = column_sum(hidden_grad)
    out_refs[2][...] = inner_rows(active, grad_low)
    out_refs[3][...] = column_sum(grad_low)
    return hidden_grad


ADAPTER_GRADS = ((D, BOT), (1, BOT), (BOT, D), (1, D))
COUPLING_GRADS = ((HALF, INV_H), (1, INV_H), (INV_H, HALF), (1, HALF))


def branch_kept(branch):
    return [operand.get()[...] for operand in branch]


def grad_weights(pair, section):
    return [pair[0].get()[section], None, pair[1].get()[section]]


def back_to_inner(kept, rows, section, norms, adapter, incoming, scratch, grad_refs, packing=None):
    acc, second_low = scratch
    parts = rows_of(rows, STEP_ROWS)
    weights = grad_weights(adapter, section)
    for part in parts:
        norm_kept = kept.normal_2.get()[part], kept.inverse_2.get()[part, :1]
        second = norm_back(incoming(part), norm_kept, norms[section, 4:5])
        acc[part] = second
        second_low[part] = low(second)
    hidden_grad = branch_grads(second_low[:rows], branch_kept(kept.branch), weights, grad_refs)
    for part in parts:
        acc[part] += matmul_t(hidden_grad[part], weights[0])
    if packing is not None:
        packing()


def back_to_mixed(operands, rows, section, norms, scratch, pairs, buffers, results):
    summed_low, acc = scratch
    start_ref, mixed_ref = results
    slope, normal, inverse = (operand.get() for operand in operands)
    parts = rows_of(rows, STEP_ROWS)
    for part in parts:
        summed_low[part] = low(acc[part])

    def turn(j, carry):
        for now in (2 * j, 2 * j + 1):
            wait_up(pairs, buffers, now)
            wait_down(pairs, buffers, now)
        for now in (2 * j, 2 * j + 1):
            for part in parts:
                inner = matmul_t(summed_low[part], buffers[2][now])
                inner = low(inner * slope[part, tile_columns(now)].astype(F32))
                acc[part] += matmul_t(inner, buffers[1][now])
        return carry

    lax.fori_loop(0, TILES // 2, turn, 0)
    wait_out(pairs, buffers)
    for part in parts:
        back = norm_back(acc[part], (normal[part], inverse[part, :1]), norms[section, 2:3])
        start_ref[part] = back
        mixed_ref[part] = low(matmul_t(low(back), buffers[0][...]))


def backward_kernel(ins, scalars, pairs, packed):
    parts = ins.merged[0].shape[0]
    grads = [shape_of(*dims) for dims in COUPLING_GRADS]
    if packed:
        chunks = low_shape(COUPLING_GROUPS, PART_ROWS, LANES)
        adapters = [[shape_of(1, BOT), shape_of(1, D)] for _ in range(MICRO)] + [chunks, chunks]
    else:
        adapters = [[shape_of(*dims) for dims in ADAPTER_GRADS] for _ in range(MICRO)]
    outs = Back(shape_of(1, LANES), grads, grads, adapters, shape_of(SEQ, D))

    def body(ins, out, scalar_refs, pair_refs, raw_refs, scratch):
        length = scalar_refs[0][0]
        (summed_low, acc_0, second_low), spot, mixed_1, acc_1, section_grad = scratch[:3], *scratch[3:7]
        qkv_w, rest_w, refs = scratch[7:9], scratch[9:13], scratch[13:]
        qkv_pair, rest_pairs = pair_refs[0], pair_refs[1:]

        start(ins.merged, ins.row_weights, ins.weight_sum, ins.target_rows, ins.last, ins.norms)
        start(ins.coupling, ins.adapter, ins.rest_1)
        start_tiles(rest_pairs, 1, rest_w)
        start_out(rest_pairs, 1, rest_w)
        start_qkv(qkv_pair, 1, qkv_w)
        start(ins)
        norms = ins.norms.get()

        def merge(merged):
            stats = merged[:, :, D:].astype(F32)
            highest = jnp.sum(stats[:, :, :3], 2, keepdims=True)
            totals = jnp.sum(stats[:, :, 3:6], 2, keepdims=True)
            top = jnp.max(highest, 0)
            factor = jnp.exp(highest - top[None])
            total = jnp.sum(totals * factor, 0)
            expected = jnp.zeros((merged.shape[1], D), F32)
            for i in range(parts):
                expected += merged[i, :, :D].astype(F32) * (factor[i] / total)
            return top, total, expected

        def from_head(part):
            halves = [merge(operand.get()) for operand in ins.merged]
            top, total, expected = (jnp.concatenate(pair, 0) for pair in zip(*halves))
            target = ins.target_rows.get()[...]
            target_logit = jnp.sum(ins.last.normed.get()[...].astype(F32) * target, 1, keepdims=True)
            weight = ins.row_weights.get()[...]
            row_losses = weight[:, :1] * (top + jnp.log(total) - target_logit)
            out.loss.buffer[...] = across(jnp.sum(row_losses, 0, keepdims=True))
            normed_grad = (weight / ins.weight_sum.get()[...])[:, :1] * (expected - target)
            kept = (ins.last.normal.get()[...], ins.last.inverse.get()[:, :1])
            restored = norm_back(normed_grad, kept, norms[1, 0:1])
            left, right = restored[:, :HALF], restored[:, HALF:]
            one, two = (grad_weights(ins.coupling, s) for s in range(MICRO))
            refs_of = lambda results: [result.buffer for result in results]
            hidden = branch_grads(low(-left), branch_kept(ins.last.one), one, refs_of(out.one))
            right = right + matmul_t(hidden, one[0])
            hidden = branch_grads(low(-right), branch_kept(ins.last.two), two, refs_of(out.two))
            left = left + matmul_t(hidden, two[0])
            return jnp.concatenate([left, right], 1)

        def grads_of(section):
            buffers = [result.buffer for result in out.adapters[section]]
            return (refs[0], buffers[0], refs[1], buffers[1]) if packed else buffers

        def pack_second():
            def store(part, chunk):
                refs[2][part] = chunk

            pack_adapter((refs[0], refs[1]), store)

        def pack_both():
            here = lax.axis_index("section") == 0
            own, other = out.adapters[2:]

            def store(part, chunk):
                arrived = refs[2][part]
                own.buffer[part] = jnp.where(here, chunk, arrived)
                other.buffer[part] = jnp.where(here, arrived, chunk)

            pack_adapter((refs[0], refs[1]), store)
            send(own, other)

        back_to_inner(
            ins.rest_1, COUNT, 1, norms, ins.adapter, from_head, (acc_0, second_low), grads_of(1),
            pack_second if packed else None,
        )
        kept = ins.rest_1.slope, ins.rest_1.normal_1, ins.rest_1.inverse_1
        back_to_mixed(kept, COUNT, 1, norms, (summed_low, acc_0), rest_pairs, rest_w, (spot, mixed_1))

        acc_1[...] = jnp.zeros_like(acc_1)
        q_ref, k_ref, v_ref, lse_ref = (operand.get() for operand in ins.attention_1)

        def attend_back(group, carry):
            columns = group_columns(group)
            stack = lambda values: jnp.concatenate([only_head(values, h) for h in range(HEADS_IN)], 0)
            query = stack(scaled_query(q_ref[:, columns]))
            mixed = stack(mixed_1[:, columns])
            key, value = k_ref[:, columns], v_ref[:, columns]
            scores = matmul_t(query, key) + key_bias(length, (1, SEQ), 1)
            soft = jnp.exp(scores - lse_ref[group][:, :1])
            soft_grad = matmul_t(mixed, value)
            delta = jnp.sum(soft_grad * soft, 1, keepdims=True)
            score_grad = low(soft * (soft_grad - delta))
            every = matmul(score_grad, key)
            query_grad = every[:COUNT]
            for head in range(1, HEADS_IN):
                query_grad = jnp.where(
                    head_mask(query_grad, head), every[head * COUNT : (head + 1) * COUNT], query_grad
                )
            query_grad = low(query_grad * HEAD_DIM**-0.5)
            key_grad = low(inner_rows(score_grad, query))
            value_grad = low(inner_rows(low(soft), mixed))
            for part in range(3):
                wait_qkv(qkv_pair, qkv_w, group, part)
            spot[...] += matmul_t(query_grad, qkv_w[0][group, 0])
            acc_1[...] += matmul_t(key_grad, qkv_w[0][group, 1]) + matmul_t(value_grad, qkv_w[0][group, 2])
            return carry

        lax.fori_loop(0, GROUPS, attend_back, 0)
        placed = jnp.dot(ins.chosen_t.get()[...], spot[...], precision=HIGHEST, preferred_element_type=F32)
        section_grad[...] = low(acc_1[...] + placed)

        back_to_inner(
            ins.rest_0, SEQ, 0, norms, ins.adapter, lambda part: section_grad[part].astype(F32),
            (out.inner.buffer, second_low), grads_of(0), pack_both if packed else None,
        )

    scratch = [pltpu.VMEM((COUNT, D), BF16), pltpu.VMEM((COUNT, D), F32), pltpu.VMEM((SEQ, D), BF16)]
    scratch += [pltpu.VMEM((COUNT, D), F32), pltpu.VMEM((COUNT, D), BF16), pltpu.VMEM((SEQ, D), F32)]
    scratch += [pltpu.VMEM((SEQ, D), BF16)] + qkv_buffers() + rest_buffers()
    if packed:
        scratch += [pltpu.VMEM((D, BOT), F32), pltpu.VMEM((BOT, D), F32)]
        scratch += [pltpu.VMEM((COUPLING_GROUPS, PART_ROWS, LANES), BF16)]
    return moved_call(body, scalars, ins, outs, pairs, scratch, "backward")[0]


def first_backward(ins, scalars, pairs, packed):
    if packed:
        dims = (COUPLING_GROUPS, GROUP_ROWS + 8, LANES)
        outs = (shape_of(*dims), low_shape(*dims))
    else:
        outs = [shape_of(*dims) for dims in COUPLING_GRADS * 2]

    def body(ins, out, scalar_refs, pair_refs, raw_refs, scratch):
        length = scalar_refs[0][0]
        s_even, s_odd, d_even, d_odd, p_even, p_odd, ds_even, ds_odd = scratch[:8]
        qkv_w, (key_grad, value_grad, query_grad_t), refs = scratch[8:10], scratch[10:13], scratch[13:]
        (summed_low, mixed_ref), rest_w, refs = refs[:2], refs[2:6], refs[6:]
        start(ins.inner, ins.norms)
        start_tiles(pair_refs[1:], 0, rest_w)
        start(ins.inner_kept)
        start_out(pair_refs[1:], 0, rest_w)
        start(ins.attention)
        start_qkv(pair_refs[0], 0, qkv_w)
        start(ins)
        acc = ins.inner.get()
        back_to_mixed(
            ins.inner_kept, SEQ, 0, ins.norms.get(), (summed_low, acc), pair_refs[1:], rest_w, (acc, mixed_ref)
        )
        q_ref, k_ref, v_ref, lse_ref = (operand.get() for operand in ins.attention)

        def attend_back(group, carry):
            columns = group_columns(group)
            query = scaled_query(q_ref[:, columns])
            key, value, mixed = k_ref[:, columns], v_ref[:, columns], mixed_ref[:, columns]
            lse_rows = lse_ref[group]
            key_t = jnp.transpose(key)
            buffers = ((s_even, d_even, p_even, ds_even), (s_odd, d_odd, p_odd, ds_odd)) * 2

            def product_steps(head):
                def scores():
                    buffers[head][0][...] = matmul_t(only_head(key, head), query)

                def soft_grads():
                    buffers[head][1][...] = matmul_t(only_head(value, head), mixed)

                return [scores, soft_grads] if head < HEADS_IN else []

            def soft_steps(head):
                s_buf, d_buf, p_low, ds_low = buffers[head]
                delta = [jnp.zeros((8, SEQ), F32)]

                def soft_step(rows):
                    valid = lax.broadcasted_iota(jnp.int32, (SMALL_ROWS, 1), 0) + rows.start < length
                    bias = jnp.where(valid, 0.0, -1e30)
                    soft = jnp.exp(s_buf[rows] + bias - lse_rows[head : head + 1])
                    s_buf[rows] = soft
                    p_low[rows] = low(soft)
                    product = soft * d_buf[rows]
                    for at in range(0, SMALL_ROWS, 8):
                        delta[0] = delta[0] + product[at : at + 8]

                def sum_step():
                    delta[0] = jnp.sum(delta[0], 0, keepdims=True)

                def grad_step(rows):
                    ds_low[rows] = low(s_buf[rows] * (d_buf[rows] - delta[0]))

                parts = rows_of(SEQ, SMALL_ROWS)
                steps = [functools.partial(soft_step, rows) for rows in parts] + [sum_step]
                return steps + [functools.partial(grad_step, rows) for rows in parts]

            def grad_steps(head):
                _, _, p_low, ds_low = buffers[max(head, 0)]

                def add(ref, grad):
                    ref[...] = grad if head == 0 else ref[...] + grad

                def value_step():
                    add(value_grad, matmul(p_low[...], only_head(mixed, head)))

                def key_step():
                    add(key_grad, matmul(ds_low[...], only_head(query, head)))

                def query_step():
                    rows = slice(head * HEAD_DIM, (head + 1) * HEAD_DIM)
                    query_grad_t[rows] = matmul(key_t[rows], ds_low[...])

                return [value_step, key_step, query_step] if head >= 0 else []

            alternate(product_steps(0))
            for head in range(HEADS_IN):
                alternate(soft_steps(head), product_steps(head + 1) + grad_steps(head - 1))
            alternate(grad_steps(HEADS_IN - 1))
            query_grad = jnp.transpose(query_grad_t[...]) * HEAD_DIM**-0.5
            for part, grad in enumerate((query_grad, key_grad[...], value_grad[...])):
                wait_qkv(pair_refs[0], qkv_w, group, part)
                acc[...] += matmul_t(low(grad), qkv_w[0][group, part])
            return carry

        lax.fori_loop(0, GROUPS, attend_back, 0)
        one, two = (grad_weights(ins.coupling, s) for s in range(MICRO))
        grads = refs if packed else [result.buffer for result in out]
        hidden = branch_grads(low(acc[:, HALF:]), branch_kept(ins.two), two, grads[4:])
        left = acc[:, :HALF] + matmul_t(hidden, two[0])
        branch_grads(low(left), branch_kept(ins.one), one, grads[:4])
        for ref, operand in zip(grads, (*ins.grads_one, *ins.grads_two)):
            ref[...] += operand.get()[...]
        if not packed:
            return
        here = lax.axis_index("section")
        for s in range(MICRO):
            some = grads[4 * s : 4 * s + 4]
            biases = [operand.get()[...] for operand in ins.biases[s]]
            tiles = bias_tiles(*biases, some[1][...], some[3][...])

            def store(part, chunk, s=s):
                @pl.when(here == s)
                def _():
                    out[0].buffer[part] = chunk

                @pl.when(here != s)
                def _():
                    out[1].buffer[part] = low(chunk)

            pack_coupling((some[0], some[2]), tiles, sum(BIASES) // COUPLING_GROUPS, store)

    scratch = [pltpu.VMEM((SEQ, SEQ), F32)] * 4 + [pltpu.VMEM((SEQ, SEQ), BF16)] * 4 + qkv_buffers()
    scratch += [pltpu.VMEM((SEQ, GROUP), F32)] * 2 + [pltpu.VMEM((GROUP, SEQ), F32)]
    scratch += [pltpu.VMEM((SEQ, D), BF16)] * 2 + rest_buffers()
    if packed:
        scratch += [pltpu.VMEM(dims, F32) for dims in COUPLING_GRADS * 2]
    return moved_call(body, scalars, ins, outs, pairs, scratch, "first_backward")[0]


VOCAB_TILE = 1280


def head_stats(top, total):
    lane = lax.broadcasted_iota(jnp.int32, (top.shape[0], LANES), 1)
    stats = jnp.zeros(lane.shape, F32)
    for j, piece in enumerate(three_low(top) + three_low(total)):
        stats = jnp.where(lane == j, piece.astype(F32), stats)
    return low(stats)


def head_kernel(rows, table):
    parts, each, _ = rows.shape
    count, vocab = parts * each, table.shape[0]
    tiles = pl.cdiv(vocab, VOCAB_TILE)
    if vocab < VOCAB_TILE or (vocab - VOCAB_TILE) % 16 or tiles % 2:
        return blocked_head_kernel(rows, table)
    starts = [min(tile * VOCAB_TILE, vocab - VOCAB_TILE) for tile in range(tiles)]

    def kernel(x_hbm, table_hbm, out_hbm, *refs):
        x_ref, out_ref, entries, acc, top, total, factor_even, factor_odd = refs[:8]
        l_even, l_odd, p_even, p_odd, sems = refs[8:]
        fetch = pltpu.make_async_copy(x_hbm, x_ref, sems.at[tiles])
        fetch.start()
        for tile, at in enumerate(starts):
            window = table_hbm.at[pl.ds(at, VOCAB_TILE)]
            pltpu.make_async_copy(window, entries.at[tile], sems.at[tile]).start()

        def wait_tile(tile):
            window = table_hbm.at[pl.ds(0, VOCAB_TILE)]
            pltpu.make_async_copy(window, entries.at[tile], sems.at[tile]).wait()

        def logit_steps(l_ref, tile):
            def step(columns):
                l_ref[:, columns] = matmul_t(x_ref[...], entries[tile, columns])

            return [functools.partial(step, columns) for columns in rows_of(VOCAB_TILE, GROUP)]

        def soft_steps(l_ref, p_ref, factor_ref, tile):
            start = jnp.minimum(tile * VOCAB_TILE, vocab - VOCAB_TILE)
            lane = lax.broadcasted_iota(jnp.int32, (1, VOCAB_TILE), 1)
            bias = jnp.where(lane + start >= tile * VOCAB_TILE, 0.0, -1e30)

            def step(at):
                logits = l_ref[at] + bias
                earlier = top[at]
                highest = jnp.maximum(earlier, jnp.max(logits, 1, keepdims=True))
                exponent = jnp.exp(logits - highest)
                factor = jnp.exp(earlier - highest)
                top[at] = highest
                total[at] = total[at] * factor + jnp.sum(exponent, 1, keepdims=True)
                p_ref[at] = low(exponent)
                factor_ref[at] = across(factor)

            return [functools.partial(step, at) for at in rows_of(count, SMALL_ROWS)]

        def sum_steps(p_ref, factor_ref, tile):
            def step(columns):
                factor = factor_ref[...]
                factor = jnp.concatenate([factor, factor], 1)
                acc[:, columns] = acc[:, columns] * factor + matmul(p_ref[...], entries[tile, :, columns])

            return [functools.partial(step, columns) for columns in rows_of(D, GROUP)]

        acc[...] = jnp.zeros_like(acc)
        top[...] = jnp.full_like(top, -1e30)
        total[...] = jnp.zeros_like(total)
        p_odd[...] = jnp.zeros_like(p_odd)
        factor_odd[...] = jnp.ones_like(factor_odd)
        fetch.wait()
        wait_tile(0)
        alternate(logit_steps(l_even, 0))

        def turn(j, carry):
            even, odd = 2 * j, 2 * j + 1
            before, after = jnp.maximum(even - 1, 0), jnp.minimum(even + 2, tiles - 1)
            wait_tile(odd)

            @pl.when(even + 2 < tiles)
            def _():
                wait_tile(even + 2)

            alternate(
                soft_steps(l_even, p_even, factor_even, even),
                sum_steps(p_odd, factor_odd, before) + logit_steps(l_odd, odd),
            )
            alternate(
                soft_steps(l_odd, p_odd, factor_odd, odd),
                sum_steps(p_even, factor_even, even) + logit_steps(l_even, after),
            )
            return carry

        lax.fori_loop(0, tiles // 2, turn, 0)
        alternate(sum_steps(p_odd, factor_odd, tiles - 1))
        out_ref[:, :D] = low(acc[...])
        out_ref[:, D:] = head_stats(top[...], total[...])
        copy = pltpu.make_async_copy(out_ref, out_hbm, sems.at[tiles])
        copy.start()
        copy.wait()

    hbm = pl.BlockSpec(memory_space=pltpu.HBM)
    return pl.pallas_call(
        kernel,
        in_specs=[hbm, hbm],
        out_specs=hbm,
        out_shape=low_shape(count, D + LANES),
        scratch_shapes=[
            pltpu.VMEM((count, D), BF16),
            pltpu.VMEM((count, D + LANES), BF16),
            pltpu.VMEM((tiles, VOCAB_TILE, D), BF16),
            pltpu.VMEM((count, D), F32),
            pltpu.VMEM((count, 1), F32),
            pltpu.VMEM((count, 1), F32),
        ]
        + [pltpu.VMEM((count, LANES), F32)] * 2
        + [pltpu.VMEM((count, VOCAB_TILE), F32)] * 2
        + [pltpu.VMEM((count, VOCAB_TILE), BF16)] * 2
        + [pltpu.SemaphoreType.DMA((tiles + 1,))],
        compiler_params=params_for(MOST_VMEM),
        name="vocabulary_head",
    )(rows.reshape(count, D), table).reshape(parts, each, D + LANES)


def blocked_head_kernel(rows, table):
    parts_in, each, _ = rows.shape
    count, vocab = parts_in * each, table.shape[0]
    last = pl.cdiv(vocab, VOCAB_TILE) - 1
    turns = last // 2 + 1

    def kernel(x_hbm, even_ref, odd_ref, after_ref, out_hbm, *refs):
        x_ref, out_ref, acc, top, total, l_even, l_odd, p_even, p_odd, sems = refs
        turn = pl.program_id(0)

        def entries_of(ref, tile):
            row = lax.broadcasted_iota(jnp.int32, (VOCAB_TILE, 1), 0)
            return jnp.where(row < vocab - tile * VOCAB_TILE, ref[...], jnp.zeros_like(ref))

        @pl.when(turn == 0)
        def _():
            copy = pltpu.make_async_copy(x_hbm, x_ref, sems.at[0])
            copy.start()
            acc[...] = jnp.zeros_like(acc)
            top[...] = jnp.full_like(top, -1e30)
            total[...] = jnp.zeros_like(total)
            entries = entries_of(even_ref, 0)
            copy.wait()
            l_even[...] = matmul_t(x_ref[...], entries)

        even = entries_of(even_ref, 2 * turn)
        odd = entries_of(odd_ref, 2 * turn + 1)
        after = entries_of(after_ref, 2 * turn + 2)
        for tile, l_now, p_now, now, l_later, later in (
            (2 * turn, l_even, p_even, even, l_odd, odd),
            (2 * turn + 1, l_odd, p_odd, odd, l_even, after),
        ):
            bias = key_bias(vocab - tile * VOCAB_TILE, (1, VOCAB_TILE), 1)
            for at in rows_of(count, SMALL_ROWS):
                logits = l_now[at] + bias
                earlier = top[at]
                highest = jnp.maximum(earlier, jnp.max(logits, 1, keepdims=True))
                exponent = jnp.exp(logits - highest)
                factor = jnp.exp(earlier - highest)
                top[at] = highest
                total[at] = total[at] * factor + jnp.sum(exponent, 1, keepdims=True)
                p_now[at] = low(exponent)
                acc[at] = acc[at] * factor
            l_later[...] = matmul_t(x_ref[...], later)
            acc[...] += matmul(p_now[...], now)

        @pl.when(turn == turns - 1)
        def _():
            out_ref[:, :D] = low(acc[...])
            out_ref[:, D:] = head_stats(top[...], total[...])
            copy = pltpu.make_async_copy(out_ref, out_hbm, sems.at[1])
            copy.start()
            copy.wait()

    def tile_at(shift):
        return pl.BlockSpec((VOCAB_TILE, D), lambda j: (jnp.minimum(2 * j + shift, last), 0))

    hbm = pl.BlockSpec(memory_space=pltpu.HBM)
    return pl.pallas_call(
        kernel,
        grid=(turns,),
        in_specs=[hbm] + [tile_at(shift) for shift in range(3)],
        out_specs=hbm,
        out_shape=shape_of(count, D + LANES, kind=BF16),
        scratch_shapes=[
            pltpu.VMEM((count, D), BF16),
            pltpu.VMEM((count, D + LANES), BF16),
            pltpu.VMEM((count, D), F32),
            pltpu.VMEM((count, 1), F32),
            pltpu.VMEM((count, 1), F32),
            pltpu.VMEM((count, VOCAB_TILE), F32),
            pltpu.VMEM((count, VOCAB_TILE), F32),
            pltpu.VMEM((count, VOCAB_TILE), BF16),
            pltpu.VMEM((count, VOCAB_TILE), BF16),
            pltpu.SemaphoreType.DMA((2,)),
        ],
        compiler_params=params_for(MOST_VMEM),
        name="vocabulary_head",
    )(rows.reshape(count, D), table, table, table).reshape(parts_in, each, D + LANES)


def swap_add(own, other):
    came = lax.ppermute(low(other), "section", [(0, 1), (1, 0)])
    return own + came.astype(F32)


def pick(first_section, both):
    return jnp.where(first_section, both[0], both[1])


def plan_requests(ids, weights, vocab_rows, slots, parts):
    turned = jnp.transpose(ids)

    def kernel(ids_ref, turned_ref, weights_ref, asked_ref, code_ref, spot_ref):
        here = lax.axis_index("section")
        i_index = lax.broadcasted_iota(jnp.int32, (IDS, IDS), 0)
        j_index = lax.broadcasted_iota(jnp.int32, (IDS, IDS), 1)
        earlier, later = j_index < i_index, i_index < j_index

        def owner_of(values):
            return jnp.floor((values.astype(F32) + 0.5) * (1.0 / vocab_rows)).astype(jnp.int32)

        def count(hits, axis):
            return jnp.sum(hits.astype(F32), axis, keepdims=True)

        most = jnp.zeros((1, 1), F32)
        for m in range(MICRO):
            row, col = ids_ref[m : m + 1], turned_ref[:, m : m + 1]
            same_id = row == col
            first_col = count(same_id & earlier, 1) == 0
            first_row = count(same_id & later, 0) == 0
            owner_row, owner_col = owner_of(row), owner_of(col)
            same_owner = owner_row == owner_col
            rank_row = count(same_owner & later & first_col, 0)
            rank_col = count(same_owner & earlier & first_row, 1)
            most = jnp.maximum(most, jnp.max(rank_row, 1, keepdims=True))

            @pl.when(here == m)
            def _():
                slot_row = jnp.sum(jnp.where(same_id & first_col, rank_col, 0.0), 0, keepdims=True)
                slot_col = jnp.sum(jnp.where(same_id & first_row, rank_row, 0.0), 1, keepdims=True)
                slot_row, slot_col = slot_row.astype(jnp.int32), slot_col.astype(jnp.int32)
                code_ref[...] = (owner_row + parts * first_row.astype(jnp.int32)) * 1024 + slot_row
                spot = jnp.where(slot_col < slots, owner_col * slots + slot_col, -1)
                spot_ref[...] = jnp.broadcast_to(spot, (IDS, LANES))
                lane = lax.broadcasted_iota(jnp.int32, (IDS, LANES), 1)
                local = (col - owner_col * vocab_rows).astype(F32)
                wanted = first_col & (slot_col < slots) & (slot_col == lane)
                wanted = jnp.where(wanted, local, 0.0)
                for part in range(parts):
                    asked = jnp.sum(jnp.where(owner_col == part, wanted, 0.0), 0, keepdims=True)
                    asked_ref[part] = asked.astype(jnp.int32)

        rounds = jnp.floor((most + 0.5) * (1.0 / slots)).astype(jnp.int32) + 1
        total = jnp.sum(jnp.sum(weights_ref[...], 0, keepdims=True), 1, keepdims=True)
        lane = lax.broadcasted_iota(jnp.int32, (1, LANES), 1)
        for part in range(parts):
            row = asked_ref[part]
            asked_ref[part] = jnp.where(lane == slots, rounds, jnp.where(lane == slots + 1, total, row))

    return pl.pallas_call(
        kernel,
        out_shape=[
            jax.ShapeDtypeStruct((parts, 1, LANES), jnp.int32),
            jax.ShapeDtypeStruct((1, IDS), jnp.int32),
            jax.ShapeDtypeStruct((IDS, LANES), jnp.int32),
        ],
        compiler_params=params_for(24),
        name="plan_requests",
    )(ids, turned, weights)


def fetch_rows(table, ids, first_section, plan, slots, late):
    parts = lax.axis_size("dp")
    vocab_rows = table.shape[0]
    asked, code, spot = plan
    asked = lax.all_to_all(asked, "dp", 0, 0)[:, 0]
    total_rounds = jnp.max(asked[:, slots])
    weight_sum = jnp.sum(asked[:, slots + 1])

    def look_up(asked):
        return table.at[asked.reshape(-1)].get(mode="promise_in_bounds").reshape(parts, slots, D)

    def send_rows(rows):
        return lax.all_to_all(rows, "dp", 0, 0).reshape(parts * slots, D)

    rows, late = lax.optimization_barrier((look_up(asked[:, :slots]), late))
    came = send_rows(rows)

    def more(state):
        return state[0] < total_rounds

    def another(state):
        turn, extra = state
        place, slot = code[0] // 1024, code[0] % 1024
        owner, first = place % parts, place >= parts
        local = pick(first_section, ids) - owner * vocab_rows
        here = slot - turn * slots
        at = jnp.where((here >= 0) & (here < slots), owner * slots + here, -1)
        hits = at[:, None] == jnp.arange(parts * slots)[None, :]
        wanted = jnp.sum(jnp.where(hits & first[:, None], local[:, None], 0), 0).reshape(parts, slots)
        rows = send_rows(look_up(lax.all_to_all(wanted, "dp", 0, 0)))
        return turn + 1, extra + matmul(hits.astype(BF16), rows)

    extra = lax.while_loop(more, another, (jnp.int32(1), jnp.zeros((IDS, D), F32)))[1]
    return came, spot, extra, total_rounds, weight_sum.astype(F32), late


def three_low(values):
    high = low(values)
    rest = values - high.astype(F32)
    middle = low(rest)
    return [high, middle, low(rest - middle.astype(F32))]


def in_groups(count):
    return lax.axis_size("dp") == COUPLING_GROUPS and count == 4 * PART_GROUPS


LINES = 4


def plane_groups(parts):
    planes = parts // LINES
    across_planes = [[plane * LINES + line for plane in range(planes)] for line in range(LINES)]
    return across_planes, [[plane * LINES + line for line in range(LINES)] for plane in range(planes)]


def share_params(master, vector, after):
    if not in_groups(master.shape[0]):
        return low(jnp.concatenate([master.reshape(-1), vector])), after
    across_planes, in_plane = plane_groups(lax.axis_size("dp"))
    some = pack_own(master, vector[None], len(in_plane))
    some = lax.all_to_all(some, "dp", 0, 0, axis_index_groups=across_planes)
    return lax.optimization_barrier((some, after))


def gather_params(some, count, width, before):
    parts = lax.axis_size("dp")
    if in_groups(count):
        _, in_plane = plane_groups(parts)
        own = lax.all_gather(some, "dp", axis_index_groups=in_plane)
        own, before = lax.optimization_barrier((own, before))
        return *unpack_all(own, lax.ppermute(own, "section", [(0, 1), (1, 0)]), width), before
    gathered = lax.all_gather(some, ("section", "dp")).reshape(MICRO, parts, -1)
    size = count * BLOCK**2
    all_blocks = gathered[:, :, :size].reshape(MICRO, parts * count, BLOCK, BLOCK)
    all_vectors = gathered[:, :, size:].reshape(MICRO, parts * width)
    both = [split_params(all_blocks[s], all_vectors[s]) for s in range(MICRO)]

    def stacked(which):
        down, bias_down, up, bias_up = (jnp.stack([pair[which][i] for pair in both]) for i in range(4))
        return Params(down, bias_down.astype(F32)[:, None], up, bias_up.astype(F32)[:, None])

    return stacked(0), stacked(1), before


def sum_at_owners(grads, loss_part, count):
    parts = lax.axis_size("dp")
    width = sum(BIASES) // parts
    flat = []
    for adapter, coupling in grads:
        blocks, vector = join_params(adapter, coupling)
        flat.append(
            jnp.concatenate([blocks.reshape(parts, count * BLOCK**2), vector.reshape(parts, width)], 1)
        )
    first = lax.axis_index("section") == 0
    summed = swap_add(jnp.where(first, flat[0], flat[1]), jnp.where(first, flat[1], flat[0]))
    owned = jnp.sum(lax.all_to_all(low(summed), "dp", 0, 0).astype(F32), 0)
    blocks = owned[: count * BLOCK**2].reshape(count, BLOCK, BLOCK)
    pair = jnp.stack([jnp.sum(owned * owned), loss_part[0, 0]])
    pair = jnp.pad(pair, (0, LANES - 2))[None, None]
    return blocks, owned[count * BLOCK**2 :], jnp.broadcast_to(pair, (parts * MICRO, 8, LANES))


def to_coupling_owners(group):
    arrived = []
    for place in range(1, PART_GROUPS):
        route = []
        for i, part in enumerate(SUMMED_AT):
            owner, at = divmod(ADAPTER_GROUPS + i, PART_GROUPS)
            if at == place and owner != part:
                route.append((part, owner))
        arrived.append(lax.ppermute(group, "dp", route))
    return [group] + arrived


def exact(spec, left, right):
    return jnp.einsum(spec, left, right, precision=HIGHEST)


def update(pair, grads, grad_vector, turned_old, state):
    master, momentum, stat_left, stat_right, root_left, root_right, vectors, vec_first, vec_second = state
    count = master.shape[0]
    outs = [shape_of(1, count, BLOCK, BLOCK)] * 5 + [low_shape(1, count, BLOCK, BLOCK)]
    outs += [shape_of(*vectors.shape)] * 3 + [shape_of(1, 1)] * 2

    def body(ins, out, scalar_refs, pair_refs, raw_refs, scratch):
        start(ins)
        grads, vector_ref, old_ref, state_refs, pair_ref = jax.tree.map(lambda operand: operand.get(), ins)
        master_ref, momentum_ref, stat_left_ref, stat_right_ref, root_left_ref, root_right_ref = state_refs[:6]
        vectors_ref, first_ref, second_ref = state_refs[6:]
        outs = [result.buffer for result in out]
        grad_ref = grads[0]
        if len(grads) > 1:
            grad_ref = scratch[0]
            unpack_own(grads[0], grads[1], grads[2:], grad_ref)
        totals = jnp.sum(pair_ref[...], 0)[:1]
        norm = jnp.sqrt(totals[:, :1])
        factor = CLIP_NORM / jnp.maximum(norm, CLIP_NORM)
        outs[9][...] = norm
        outs[10][...] = totals[:, 1:2]
        square = (1.0 - STAT_DECAY) * factor * factor
        for n in range(count):
            grad = grad_ref[n]
            clipped = grad * factor
            outs[0][0, n] = clipped
            outs[1][0, n] = FIRST_DECAY * momentum_ref[n] + (1.0 - FIRST_DECAY) * clipped
            left_square = exact_dot(grad, grad, ((1,), (1,)))
            right_square = exact_dot(grad, grad, ((0,), (0,)))
            turned = exact_dot(exact_dot(root_left_ref[n], grad, ((1,), (0,))), root_right_ref[n], ((1,), (0,)))
            outs[2][0, n] = STAT_DECAY * stat_left_ref[n] + square * left_square
            outs[3][0, n] = STAT_DECAY * stat_right_ref[n] + square * right_square
            direction = FIRST_DECAY * old_ref[n] + (1.0 - FIRST_DECAY) * factor * turned
            master_new = master_ref[n] - MAT_RATE * (direction + MAT_DECAY * master_ref[n])
            outs[4][0, n] = master_new
            outs[5][0, n] = low(master_new)
        clipped = vector_ref[:1, : vectors.shape[1]] * factor
        first_new = FIRST_DECAY * first_ref[...] + (1.0 - FIRST_DECAY) * clipped
        second_new = VEC_SECOND * second_ref[...] + (1.0 - VEC_SECOND) * clipped * clipped
        outs[6][...] = first_new
        outs[7][...] = second_new
        corrected_first = first_new / (1.0 - FIRST_DECAY**STEP)
        corrected_second = second_new / (1.0 - VEC_SECOND**STEP)
        outs[8][...] = vectors_ref[...] - VEC_RATE * (
            corrected_first / (jnp.sqrt(corrected_second) + VEC_EPS) + VEC_DECAY * vectors_ref[...]
        )

    ins = (grads, grad_vector, turned_old, state, pair)
    scratch = [pltpu.VMEM((count, BLOCK, BLOCK), F32)] if len(grads) > 1 else []
    return moved_call(body, (), ins, outs, (), scratch, "update")[0]


def shards(
    token_ids,
    lengths,
    positions,
    targets,
    loss_weights,
    embed_table,
    pos_table,
    norm_params,
    base_qkv,
    base_out,
    base_up,
    base_down,
    master,
    momentum,
    stat_left,
    stat_right,
    root_left,
    root_right,
    vectors,
    vec_first,
    vec_second,
):
    parts = lax.axis_size("dp")
    first_section = lax.axis_index("section") == 0
    slots = -(-IDS * 5 // (4 * parts * 16)) * 16

    ids = jnp.concatenate([token_ids[:, 0], targets[:, 0]], -1)
    asked, *plan = plan_requests(ids, loss_weights[:, 0], embed_table.shape[0], slots, parts)
    swap = [(0, 1), (1, 0)]
    pairs = [(w, lax.ppermute(w, "section", swap)) for w in (base_qkv, base_out, base_up, base_down)]
    norms_came = lax.ppermute(norm_params, "section", swap)

    some, asked = share_params(master[0], vectors[0], asked)
    late = norm_params, norms_came, lengths, positions, loss_weights, root_left, root_right, momentum
    came, spot, extra, rounds, weight_sum, late = fetch_rows(
        embed_table, ids, first_section, (asked, *plan), slots, late
    )
    norms_own, norms_came, lengths, positions, loss_weights, root_left, root_right, momentum = late
    norms = [pick(first_section, (norms_own, norms_came)), pick(first_section, (norms_came, norms_own))]
    spots = pick(first_section, positions[:, 0])
    row_weights = pick(first_section, loss_weights[:, 0]).astype(F32)
    early = (
        jnp.concatenate(norms),
        pick(first_section, lengths),
        jnp.broadcast_to(row_weights[:, None], (COUNT, LANES)),
        (spots[:, None] == jnp.arange(SEQ)[None, :]).astype(BF16),
        (spots[None, :] == jnp.arange(SEQ)[:, None]).astype(F32),
        exact("nij,njk->nik", exact("nij,njk->nik", root_left[0], momentum[0]), root_right[0]),
    )
    adapter, coupling, early = gather_params(some, master.shape[1], vectors.shape[1], early)
    norms, length, row_weights, chosen, chosen_t, turned_old = early

    ins = ForwardIn(came, spot, extra, pos_table, norms, chosen, adapter, coupling)
    kept, rows = forward_kernel(ins, (length, rounds.reshape(1)), pairs, parts, slots)

    spread = [lax.all_to_all(half, "dp", 0, 0) for half in rows]
    first_half, spread[1] = lax.optimization_barrier((head_kernel(spread[0], embed_table), spread[1]))
    halves = [first_half, head_kernel(spread[1], embed_table)]
    merged = [lax.all_to_all(half, "dp", 0, 0) for half in halves]

    packed = in_groups(master.shape[1])
    weight_row = jnp.broadcast_to(weight_sum, (1, LANES))
    adapter, coupling = adapter[::2], coupling[::2]
    adapter_kept = kept.rest_0._replace(slope=(), normal_1=(), inverse_1=())
    ins = BackIn(
        merged, row_weights, weight_row, norms, chosen_t, adapter, coupling,
        kept.target_rows, adapter_kept, kept.attention_1, kept.rest_1, kept.last,
    )
    back = backward_kernel(ins, (length,), pairs, packed)
    loss_part, inner = back.loss, back.inner
    if packed:
        own, other = back.adapters[MICRO:]
        summed = low(swap_add(own.astype(F32), other))
        summed, inner = lax.optimization_barrier((summed, inner))
        adapter_came = lax.all_to_all(summed, "dp", 0, 0)
    inner_kept = kept.rest_0.slope, kept.rest_0.normal_1, kept.rest_0.inverse_1
    ins = FirstIn(
        inner, norms, inner_kept, kept.attention_0, coupling, kept.one, kept.two, back.one, back.two,
        back.adapters[:MICRO] if packed else (),
    )
    grads = first_backward(ins, (length,), pairs, packed)
    if packed:
        adapter_total, squares = sum_adapter(adapter_came)
        came = lax.all_to_all(low(swap_add(*grads)), "dp", 0, 0)
        group, bias, pair = sum_coupling(came, squares, loss_part, parts * MICRO)
        grad, grad_vector = [adapter_total, *to_coupling_owners(group)], bias
    else:
        both = [(back.adapters[s], grads[4 * s : 4 * s + 4]) for s in range(MICRO)]
        grad, grad_vector, pair = sum_at_owners(both, loss_part, master.shape[1])
        grad, grad_vector = [grad], grad_vector[None]
    pair = lax.all_to_all(pair, ("dp", "section"), 0, 0)
    state = (master, momentum, stat_left, stat_right, root_left, root_right)
    state = [value[0] for value in state] + [vectors, vec_first, vec_second]
    *outs, grad_norm, loss_sum = update(pair, grad, grad_vector, turned_old, state)
    return (*outs, grad_norm[0, 0], loss_sum[0, 0], weight_sum)


def solution(mesh):
    rows = P(None, "dp", None)
    section = P("section", None, None)
    blocks = P("section", "dp", None, None)
    biases = P("section", "dp")
    return jax.shard_map(
        shards,
        mesh=mesh,
        in_specs=(rows, P(None, "dp"), rows, rows, rows, P("dp", None), P())
        + (section,) * 5
        + (blocks,) * 6
        + (biases,) * 3,
        out_specs=(blocks,) * 6 + (biases,) * 3 + (P(),) * 3,
        check_vma=False,
    )
```

```python
import functools
from typing import Any, NamedTuple

import jax
import jax.numpy as jnp
import numpy as np
from jax import lax
from jax.experimental import pallas as pl
from jax.experimental.pallas import tpu as pltpu
from jax.sharding import PartitionSpec as P

D = 768
HEADS = 12
HEAD_DIM = 64
BOT = 384
INV_H = 192
SEQ = 512
COUNT = 32
MICRO = 2
BLOCK = 48
STEP = 10
HALF = 384
IDS = SEQ + COUNT

HIGHEST = lax.Precision.HIGHEST
NORM_EPS = 1e-12
CLIP_NORM = 0.02
FIRST_DECAY = 0.9
STAT_DECAY = 0.99
MAT_RATE = 0.1
MAT_DECAY = 0.01
VEC_RATE = 0.05
VEC_SECOND = 0.999
VEC_EPS = 1e-08
VEC_DECAY = 0.01
F32 = jnp.float32
BF16 = jnp.bfloat16

CDF_SCALE = 0.42 / 2.0**0.5
CDF_POLY = (
    0.2368242366796694,
    0.239585811361218,
    0.1947261443420679,
    0.2687426685879861,
    -0.13052645834187002,
    0.4406726942003943,
    -0.32025628294963193,
    0.07023101752398136,
)


def matmul(left, right):
    return jnp.dot(left, right, preferred_element_type=F32)


def matmul_t(left, right):
    return lax.dot_general(left, right, (((1,), (1,)), ((), ())), preferred_element_type=F32)


def inner_rows(left, right):
    return lax.dot_general(left, right, (((0,), (0,)), ((), ())), preferred_element_type=F32)


def low(values):
    return values.astype(BF16)


def in_strips(size, function, *arrays):
    count = arrays[0].shape[0]
    strips = [slice(at, at + size) for at in range(0, count, size)] if count % size == 0 else [slice(0, count)]
    results = [function(*[array[strip] for array in arrays]) for strip in strips]
    return tuple(jnp.concatenate(parts, 0) if len(parts) > 1 else parts[0] for parts in zip(*results))


def gelu_both(values):
    return in_strips(16, gelu_strip, values)


def gelu_strip(values):
    below = 1.0 + CDF_SCALE * jnp.abs(values)
    ratio = pl.reciprocal(below, approx=True)
    ratio = ratio * (2.0 - below * ratio)
    poly = jnp.full_like(ratio, 0.5 * CDF_POLY[-1])
    for factor in CDF_POLY[-2::-1]:
        poly = poly * ratio + 0.5 * factor
    bell = jnp.exp(-0.5 * values * values)
    tail = bell * (poly * ratio)
    cdf = jnp.where(values < 0, tail, 1.0 - tail)
    return values * cdf, cdf + values * (bell * (2.0 * np.pi) ** -0.5)


def layer_norm(values, gain, shift):
    def strip(values):
        centered = values - jnp.mean(values, -1, keepdims=True)
        inverse = lax.rsqrt(jnp.mean(centered * centered, -1, keepdims=True) + NORM_EPS)
        normal = centered * inverse
        return normal * gain + shift, normal, inverse

    values, normal, inverse = in_strips(16, strip, values)
    return values, (normal, inverse)


def norm_back(incoming, kept, gain):
    def strip(incoming, normal, inverse):
        scaled = incoming * gain
        mean = jnp.mean(scaled, -1, keepdims=True)
        return (inverse * (scaled - mean - normal * jnp.mean(scaled * normal, -1, keepdims=True)),)

    return in_strips(16, strip, incoming, *kept)[0]


def to_blocks(matrix):
    rows_in, cols_in = matrix.shape
    return (
        matrix.reshape(rows_in // BLOCK, BLOCK, cols_in // BLOCK, BLOCK)
        .transpose(0, 2, 1, 3)
        .reshape(-1, BLOCK, BLOCK)
    )


def from_blocks(blocks, rows_in, cols_in):
    return (
        blocks.reshape(rows_in // BLOCK, cols_in // BLOCK, BLOCK, BLOCK)
        .transpose(0, 2, 1, 3)
        .reshape(rows_in, cols_in)
    )


def split_params(blocks, vector):
    adapter_count = D * BOT // BLOCK**2
    half_count = HALF * INV_H // BLOCK**2
    split_at = 2 * adapter_count
    adapter = (
        from_blocks(blocks[:adapter_count], D, BOT),
        vector[:BOT],
        from_blocks(blocks[adapter_count:split_at], BOT, D),
        vector[BOT : BOT + D],
    )
    coupling = (
        from_blocks(blocks[split_at : split_at + half_count], HALF, INV_H),
        vector[BOT + D : BOT + D + INV_H],
        from_blocks(blocks[split_at + half_count :], INV_H, HALF),
        vector[BOT + D + INV_H :],
    )
    return adapter, coupling


def join_params(adapter, coupling):
    blocks = jnp.concatenate(
        [to_blocks(adapter[0]), to_blocks(adapter[2]), to_blocks(coupling[0]), to_blocks(coupling[2])]
    )
    return blocks, jnp.concatenate([adapter[1], adapter[3], coupling[1], coupling[3]], 1)[0]


GROUP_ROWS = 72
LANES = 128


def params_for(mebibytes):
    return pltpu.CompilerParams(vmem_limit_bytes=mebibytes * 2**20)


def roll(values, shift):
    return pltpu.roll(values, shift, 1)


def lane_of(values):
    return lax.broadcasted_iota(jnp.int32, values.shape, 1)


def fold_half(values, upper):
    top, bottom = values[:24], values[24:]
    if upper:
        return jnp.where(lane_of(top) < 64, roll(top, 64), bottom)
    return jnp.where(lane_of(top) < 64, top, roll(bottom, 64))


def unfold_half(values, upper):
    turned = roll(values, 64)
    return jnp.concatenate([turned, values] if upper else [values, turned], 0)


def join_pair(main_0, rest_0, main_1, rest_1):
    left = lane_of(main_0) < 64
    turned = roll(main_1, 64)
    return (
        main_0,
        jnp.where(left, unfold_half(rest_0, False), turned),
        jnp.where(left, turned, unfold_half(rest_1, True)),
    )


def cut_pair(tile_0, tile_1, tile_2):
    left = lane_of(tile_0) < 64
    return (
        (tile_0, fold_half(tile_1, False)),
        (jnp.where(left, roll(tile_1, 64), roll(tile_2, 64)), fold_half(tile_2, True)),
    )


def chunk_rows(own_blocks):
    return own_blocks // 4 * GROUP_ROWS + 8


def bias_row(tiles, part, width):
    at, shift = divmod(part * width, LANES)
    lane = lane_of(tiles[0])
    row = tiles[at]
    if shift:
        row = jnp.where(lane < LANES - shift, roll(row, LANES - shift), roll(tiles[at + 1], LANES - shift))
    return jnp.where(lane < width, row, 0.0)


def bias_tiles(first, second, third, fourth):
    cut = lambda values: [values[:, at : at + LANES] for at in range(0, values.shape[1], LANES)]
    zero = jnp.zeros((1, LANES), F32)
    left = lane_of(zero) < 64
    third_tail = jnp.concatenate([third[:, LANES:]] * 2, 1)
    turned = [roll(tile, 64) for tile in cut(fourth)]
    joints = [jnp.where(left, one, two) for one, two in zip([third_tail] + turned, turned + [zero])]
    return cut(first) + cut(second) + [third[:, :LANES]] + joints + [zero]


def tiles_of_rows(rows, width):
    tiles = []
    for tile in range(-(-len(rows) * width // LANES)):
        value = jnp.zeros((8, LANES), F32)
        lane = lane_of(value)
        for part, row in enumerate(rows):
            shift = part * width - tile * LANES
            if shift >= LANES or shift + width <= 0:
                continue
            turned = roll(row, shift % LANES) if shift % LANES else row
            value = jnp.where((lane >= shift) & (lane < shift + width), turned, value)
        tiles.append(value)
    return tiles


def pack_own(master, vector, copies):
    count, width = master.shape[0], vector.shape[1]

    def kernel(master_ref, bias_ref, out_ref):
        row = lax.broadcasted_iota(jnp.int32, (BLOCK, 256), 0)
        col = lax.broadcasted_iota(jnp.int32, (BLOCK, 256), 1)
        pieces = []
        for group in range(count // 4):
            wide = jnp.zeros((BLOCK, 256), F32)
            for j in range(4):
                wide += matmul(low(master_ref[4 * group + j]), (col == row + BLOCK * j).astype(BF16))
            pieces += [wide[:, :LANES], fold_half(wide[:, LANES:], False)]
        bias = jnp.concatenate([bias_ref[...], jnp.zeros((1, LANES - width), F32)], 1)
        pieces.append(jnp.concatenate([bias, jnp.zeros((7, LANES), F32)], 0))
        packed = low(jnp.concatenate(pieces, 0))
        for copy in range(copies):
            out_ref[copy] = packed

    return pl.pallas_call(
        kernel,
        out_shape=jax.ShapeDtypeStruct((copies, chunk_rows(count), LANES), BF16),
        name="pack_own",
    )(master, vector)


MATRICES = ((D, BOT), (BOT, D), (HALF, INV_H), (INV_H, HALF))
BIASES = (BOT, D, INV_H, HALF)


def unpack_all(own, came, width):
    lines, planes, rows, _ = own.shape
    parts = lines * planes
    per_part = (rows - 8) // GROUP_ROWS

    def kernel(own_hbm, came_hbm, *refs):
        out_hbm, in_bufs, out_refs, in_sems, out_sems = refs[:8], refs[8], refs[9:17], refs[17], refs[18]
        here = lax.axis_index("section")
        copies = [
            pltpu.make_async_copy(ref, in_bufs.at[at], in_sems.at[i])
            for i, (ref, at) in enumerate(((own_hbm, here), (came_hbm, 1 - here)))
        ]
        for copy in copies:
            copy.start()
        for copy in copies:
            copy.wait()

        def unpack(s, carry):
            cache = {}

            def group(index):
                part = index // per_part
                if part not in cache:
                    cache.clear()
                    cache[part] = in_bufs[s, part % lines, part // lines].astype(F32)
                base = index % per_part * GROUP_ROWS
                chunk = cache[part]
                return chunk[base : base + BLOCK], chunk[base + BLOCK : base + GROUP_ROWS]

            index = 0
            for (height, columns), out_ref in zip(MATRICES, out_refs):
                for top in range(0, height, BLOCK):
                    if columns == INV_H:
                        main, rest = group(index)
                        index += 1
                        out_ref[s, top : top + BLOCK, :LANES] = low(main)
                        out_ref[s, top : top + BLOCK, LANES:] = low(unfold_half(rest, False)[:, :64])
                        continue
                    for left in range(0, columns, HALF):
                        tiles = join_pair(*group(index), *group(index + 1))
                        index += 2
                        for j, tile in enumerate(tiles):
                            at = left + j * LANES
                            out_ref[s, top : top + BLOCK, at : at + LANES] = low(tile)
            tiles = tiles_of_rows(
                [in_bufs[s, part % lines, part // lines, rows - 16 :].astype(F32)[8:] for part in range(parts)], width
            )
            first, second, third, fourth = out_refs[4:]
            first[s] = jnp.concatenate(tiles[:3], 1)[:1]
            second[s] = jnp.concatenate(tiles[3:9], 1)[:1]
            third[s] = jnp.concatenate([tiles[9], tiles[10][:, :64]], 1)[:1]
            left = lane_of(tiles[0]) < 64
            turned = [roll(tile, 64) for tile in tiles[10:14]]
            fourth[s] = jnp.concatenate(
                [jnp.where(left, one, two) for one, two in zip(turned, turned[1:])], 1
            )[:1]
            return carry

        lax.fori_loop(0, MICRO, unpack, 0)
        copies = [
            pltpu.make_async_copy(buf, ref, out_sems.at[i]) for i, (buf, ref) in enumerate(zip(out_refs, out_hbm))
        ]
        for copy in copies:
            copy.start()
        for copy in copies:
            copy.wait()

    shapes = [((MICRO,) + shape, BF16) for shape in MATRICES] + [((MICRO, 1, size), F32) for size in BIASES]
    hbm = pl.BlockSpec(memory_space=pltpu.HBM)
    arrays = pl.pallas_call(
        kernel,
        in_specs=[hbm] * 2,
        out_specs=[hbm] * 8,
        out_shape=[jax.ShapeDtypeStruct(*shape) for shape in shapes],
        scratch_shapes=[pltpu.VMEM((MICRO, lines, planes, rows, LANES), BF16)]
        + [pltpu.VMEM(*shape) for shape in shapes]
        + [pltpu.SemaphoreType.DMA((2,)), pltpu.SemaphoreType.DMA((8,))],
        compiler_params=params_for(MOST_VMEM),
        name="unpack_all",
    )(own, came)
    down, up, c_down, c_up, bias_down, bias_up, c_bias_down, c_bias_up = arrays
    return Params(down, bias_down, up, bias_up), Params(c_down, c_bias_down, c_up, c_bias_up)


ADAPTER_GROUPS = 2 * D * BOT // BLOCK**2 // 4
COUPLING_GROUPS = 2 * HALF * INV_H // BLOCK**2 // 4
PART_GROUPS = (ADAPTER_GROUPS + COUPLING_GROUPS) // COUPLING_GROUPS
PART_ROWS = PART_GROUPS * GROUP_ROWS
SUMMED_AT = (12, 13, 1, 5, 9, 0, 14, 2, 6, 10, 4, 15, 3, 7, 11, 8)


def groups_of(refs, shapes):
    groups = []
    for ref, (height, width) in zip(refs, shapes):
        for top in range(0, height, BLOCK):
            band = slice(top, top + BLOCK)
            if width == INV_H:
                tail = ref[band, LANES:]
                groups.append((ref[band, :LANES], fold_half(jnp.concatenate([tail, tail], 1), False)))
                continue
            for left in range(0, width, HALF):
                groups += cut_pair(*[ref[band, left + j * LANES : left + (j + 1) * LANES] for j in range(3)])
    return [jnp.concatenate(group, 0) for group in groups]


def pack_adapter(refs, store):
    groups = groups_of(refs, MATRICES[:2])
    empty = jnp.zeros((GROUP_ROWS, LANES), F32)
    for part in range(COUPLING_GROUPS):
        chunk = groups[part * PART_GROUPS : (part + 1) * PART_GROUPS]
        chunk += [empty] * (PART_GROUPS - len(chunk))
        store(part, low(jnp.concatenate(chunk, 0)))


def pack_coupling(refs, tiles, width, store):
    for part, group in zip(SUMMED_AT, groups_of(refs, MATRICES[2:])):
        bias = jnp.concatenate([bias_row(tiles, part, width), jnp.zeros((7, LANES), F32)], 0)
        store(part, jnp.concatenate([group, bias], 0))


def sum_parts(came_ref):
    total = came_ref[0].astype(F32)
    for part in range(1, came_ref.shape[0]):
        total += came_ref[part].astype(F32)
    return total


def square_sum(values):
    return jnp.sum(jnp.sum(values * values, 0, keepdims=True), 1, keepdims=True)


def sum_adapter(came):
    def kernel(came_ref, total_ref, square_ref):
        total = sum_parts(came_ref)
        total_ref[...] = total
        square_ref[...] = square_sum(total)

    return pl.pallas_call(
        kernel,
        out_shape=[jax.ShapeDtypeStruct((PART_ROWS, LANES), F32), jax.ShapeDtypeStruct((1, 1), F32)],
        compiler_params=params_for(32),
        name="sum_adapter",
    )(came)


def sum_coupling(came, squares, loss_part, copies):
    def kernel(came_ref, square_ref, loss_ref, group_ref, bias_ref, pair_ref):
        total = sum_parts(came_ref)
        group_ref[...] = total[:GROUP_ROWS]
        bias_ref[...] = total[GROUP_ROWS:]
        squares = square_ref[...] + square_sum(total)
        lane = lax.broadcasted_iota(jnp.int32, (8, LANES), 1)
        pair = jnp.where(lane == 0, squares, jnp.where(lane == 1, loss_ref[:, :1], 0.0))
        for copy in range(copies):
            pair_ref[copy] = pair

    return pl.pallas_call(
        kernel,
        out_shape=[
            jax.ShapeDtypeStruct((GROUP_ROWS, LANES), F32),
            jax.ShapeDtypeStruct((8, LANES), F32),
            jax.ShapeDtypeStruct((copies, 8, LANES), F32),
        ],
        name="sum_coupling",
    )(came, squares, loss_part)


def exact_dot(left, right, dims):
    return lax.dot_general(left, right, (dims, ((), ())), precision=HIGHEST, preferred_element_type=F32)


def unpack_own(total_ref, own_ref, group_refs, grad_ref):
    part = lax.axis_index("dp")
    own_place = jnp.int32(-1)
    for i, owner in enumerate(SUMMED_AT):
        at = ADAPTER_GROUPS + i
        if at // PART_GROUPS == owner:
            own_place = jnp.where(part == owner, at % PART_GROUPS, own_place)
    for group in range(PART_GROUPS):
        total = total_ref[group * GROUP_ROWS : (group + 1) * GROUP_ROWS]
        total = total + jnp.where(own_place == group, own_ref[...], 0.0)
        if group:
            total = total + group_refs[group - 1][...]
        main, rest = total[:BLOCK], unfold_half(total[BLOCK:], False)
        lane = lane_of(main)
        pieces = (
            main,
            roll(main, 80),
            jnp.where(lane < 32, roll(main, 32), roll(rest, 32)),
            roll(rest, 112),
        )
        for j, values in enumerate(pieces):
            grad_ref[4 * group + j] = values[:, :BLOCK]


MOST_VMEM = 64
GROUP = 256
HEADS_IN = GROUP // HEAD_DIM
GROUPS = D // GROUP
FF = 3072
TILE = 512
TILES = FF // TILE
STEP_ROWS = 256
SMALL_ROWS = 16


def rows_of(count, size):
    return [slice(at, at + min(size, count)) for at in range(0, count, size)]


def shape_of(*dims, kind=F32):
    return jax.ShapeDtypeStruct(dims, kind)


class Params(NamedTuple):
    down: Any
    bias_down: Any
    up: Any
    bias_up: Any


class Branch(NamedTuple):
    lin: Any
    act: Any
    slope: Any


class Attention(NamedTuple):
    query: Any
    key: Any
    value: Any
    lse: Any


class Rest(NamedTuple):
    normal_1: Any
    inverse_1: Any
    slope: Any
    branch: Any
    normal_2: Any
    inverse_2: Any


class Last(NamedTuple):
    one: Any
    two: Any
    normal: Any
    inverse: Any
    normed: Any


class ForwardIn(NamedTuple):
    came: Any
    spot: Any
    extra: Any
    pos: Any
    norms: Any
    chosen: Any
    adapter: Any
    coupling: Any


class Forward(NamedTuple):
    target_rows: Any
    one: Any
    two: Any
    attention_0: Any
    rest_0: Any
    attention_1: Any
    rest_1: Any
    last: Any


class BackIn(NamedTuple):
    merged: Any
    row_weights: Any
    weight_sum: Any
    norms: Any
    chosen_t: Any
    adapter: Any
    coupling: Any
    target_rows: Any
    rest_0: Any
    attention_1: Any
    rest_1: Any
    last: Any


class Back(NamedTuple):
    loss: Any
    one: Any
    two: Any
    adapters: Any
    inner: Any


class FirstIn(NamedTuple):
    inner: Any
    norms: Any
    inner_kept: Any
    attention: Any
    coupling: Any
    one: Any
    two: Any
    grads_one: Any
    grads_two: Any
    biases: Any


class Operand:
    def __init__(self, ref, buffer, sem):
        self.buffer, self.copy = buffer, pltpu.make_async_copy(ref, buffer, sem)
        self.started = self.waited = False

    def start(self):
        if not self.started:
            self.copy.start()
        self.started = True

    def get(self):
        self.start()
        if not self.waited:
            self.copy.wait()
        self.waited = True
        return self.buffer


class Result:
    def __init__(self, ref, buffer, sem):
        self.buffer, self.copy = buffer, pltpu.make_async_copy(buffer, ref, sem)
        self.sent = False

    def send(self):
        if not self.sent:
            self.copy.start()
        self.sent = True


def start(*operands):
    for operand in jax.tree.leaves(operands):
        operand.start()


def send(*results):
    for result in jax.tree.leaves(results):
        result.send()


def moved_call(body, scalars, ins, outs, pairs, scratch, name, raw_outs=()):
    in_leaves, in_tree = jax.tree.flatten(ins)
    out_leaves, out_tree = jax.tree.flatten(outs)

    def kernel(*refs):
        refs = list(refs)

        def take(count):
            taken, refs[:] = refs[:count], refs[count:]
            return taken

        scalar_refs, in_refs = take(len(scalars)), take(len(in_leaves))
        pair_refs = [tuple(take(2)) for _ in pairs]
        out_refs, raw_refs = take(len(out_leaves)), take(len(raw_outs))
        in_buffers, out_buffers, (in_sems, out_sems) = take(len(in_leaves)), take(len(out_leaves)), take(2)
        operands = [Operand(*two, in_sems.at[i]) for i, two in enumerate(zip(in_refs, in_buffers))]
        results = [Result(*two, out_sems.at[i]) for i, two in enumerate(zip(out_refs, out_buffers))]
        body(in_tree.unflatten(operands), out_tree.unflatten(results), scalar_refs, pair_refs, raw_refs, refs)
        send(results)
        for operand in operands:
            operand.get()
        for result in results:
            result.copy.wait()

    hbm = pl.BlockSpec(memory_space=pltpu.HBM)
    buffers = [pltpu.VMEM(value.shape, value.dtype) for value in (*in_leaves, *out_leaves)]
    results = pl.pallas_call(
        kernel,
        in_specs=[pl.BlockSpec(memory_space=pltpu.SMEM)] * len(scalars) + [hbm] * (len(in_leaves) + 2 * len(pairs)),
        out_specs=[hbm] * (len(out_leaves) + len(raw_outs)),
        out_shape=[*out_leaves, *raw_outs],
        scratch_shapes=buffers
        + [pltpu.SemaphoreType.DMA((len(in_leaves),)), pltpu.SemaphoreType.DMA((len(out_leaves),))]
        + list(scratch),
        compiler_params=params_for(MOST_VMEM),
        name=name,
    )(*scalars, *in_leaves, *[w for pair in pairs for w in pair])
    return out_tree.unflatten(results[: len(out_leaves)]), results[len(out_leaves) :]


def start_copy(pair, section, window, target, sem):
    own, came = pair
    here = lax.axis_index("section") == section

    @pl.when(here)
    def _():
        pltpu.make_async_copy(own.at[window], target, sem).start()

    @pl.when(jnp.logical_not(here))
    def _():
        pltpu.make_async_copy(came.at[window], target, sem).start()


def wait_copy(pair, window, target, sem):
    pltpu.make_async_copy(pair[0].at[window], target, sem).wait()


def qkv_window(group, part):
    return 0, slice(None), pl.ds(part * D + group * GROUP, GROUP)


def qkv_buffers():
    return [pltpu.VMEM((GROUPS, 3, D, GROUP), BF16), pltpu.SemaphoreType.DMA((GROUPS, 3))]


def start_qkv(pair, section, buffers):
    for group in range(GROUPS):
        for part in range(3):
            start_copy(pair, section, qkv_window(group, part), buffers[0].at[group, part], buffers[1].at[group, part])


def wait_qkv(pair, buffers, group, part):
    wait_copy(pair, qkv_window(0, 0), buffers[0].at[group, part], buffers[1].at[group, part])


UP_WINDOWS = [(0, slice(None), slice(j * TILE, (j + 1) * TILE)) for j in range(TILES)]
DOWN_WINDOWS = [(0, slice(j * TILE, (j + 1) * TILE), slice(None)) for j in range(TILES)]
OUT_WINDOW = (0, slice(None), slice(None))


def rest_buffers():
    return [
        pltpu.VMEM((D, D), BF16),
        pltpu.VMEM((TILES, D, TILE), BF16),
        pltpu.VMEM((TILES, TILE, D), BF16),
        pltpu.SemaphoreType.DMA((2 * TILES + 1,)),
    ]


def start_out(pairs, section, buffers):
    start_copy(pairs[0], section, OUT_WINDOW, buffers[0], buffers[3].at[2 * TILES])


def start_tiles(pairs, section, buffers):
    for j in range(TILES):
        start_copy(pairs[1], section, UP_WINDOWS[j], buffers[1].at[j], buffers[3].at[j])
        start_copy(pairs[2], section, DOWN_WINDOWS[j], buffers[2].at[j], buffers[3].at[TILES + j])


def wait_out(pairs, buffers):
    wait_copy(pairs[0], OUT_WINDOW, buffers[0], buffers[3].at[2 * TILES])


def wait_up(pairs, buffers, tile):
    wait_copy(pairs[1], UP_WINDOWS[0], buffers[1].at[tile], buffers[3].at[tile])


def wait_down(pairs, buffers, tile):
    wait_copy(pairs[2], DOWN_WINDOWS[0], buffers[2].at[tile], buffers[3].at[TILES + tile])


def across(values):
    return jnp.broadcast_to(values, (values.shape[0], LANES))


def group_columns(group):
    return pl.ds(pl.multiple_of(group * GROUP, GROUP), GROUP)


def tile_columns(tile):
    return pl.ds(pl.multiple_of(tile * TILE, TILE), TILE)


def head_mask(values, head):
    lane = lax.broadcasted_iota(jnp.int32, values.shape, 1)
    return (lane >= head * HEAD_DIM) & (lane < (head + 1) * HEAD_DIM)


def only_head(values, head):
    return jnp.where(head_mask(values, head), values, jnp.zeros_like(values))


def scaled_query(query):
    return low(query.astype(F32) * HEAD_DIM**-0.5)


def key_bias(length, shape, axis):
    return jnp.where(lax.broadcasted_iota(jnp.int32, shape, axis) < length, 0.0, -1e30)


def softmax_rows(scores):
    highest = jnp.max(scores, 1, keepdims=True)
    exponent = jnp.exp(scores - highest)
    total = jnp.sum(exponent, 1, keepdims=True)
    return low(exponent * (1.0 / total)), highest + jnp.log(total)


def branch_rows(low_in, weights):
    active, slope = gelu_both(matmul(low_in, weights[0]) + weights[1])
    active = low(active)
    return matmul(active, weights[2]) + weights[3], active, low(slope)


def alternate(*lists):
    steps = [((i + 0.5) / len(steps), k, step) for k, steps in enumerate(lists) for i, step in enumerate(steps)]
    for _, _, step in sorted(steps, key=lambda entry: entry[:2]):
        step()


def section_params(params, section):
    return [operand.get()[section] for operand in params]


def rest_rows(out, rows, section, norms, adapter, hidden, mixed, finish, scratch, pairs, buffers, after_loop=None):
    att_low, acc, u_even, u_odd, g_even, g_odd = scratch
    gain = lambda i: norms[section, i : i + 1]
    parts = rows_of(rows, STEP_ROWS)
    every = slice(0, rows)
    wait_out(pairs, buffers)
    for part in parts:
        first = hidden[part] + matmul(mixed[part], buffers[0][...])
        values, (normal, inverse) = layer_norm(first, gain(2), gain(3))
        acc[part] = values
        att_low[part] = low(values)
        out.normal_1.buffer[part] = normal
        out.inverse_1.buffer[part] = across(inverse)
    send(out.normal_1, out.inverse_1)
    wait_up(pairs, buffers, 0)
    g_odd[every] = jnp.zeros_like(g_odd[every])

    def gelu_steps(u_ref, g_ref, tile):
        def step(at):
            active, slope = gelu_both(u_ref[at])
            g_ref[at] = low(active)
            out.slope.buffer[at, tile_columns(tile)] = low(slope)

        return [functools.partial(step, at) for at in rows_of(rows, SMALL_ROWS)]

    def up_steps(u_ref, tile):
        def step(columns):
            u_ref[every, columns] = matmul(att_low[every], buffers[1][tile, :, columns])

        return [functools.partial(step, columns) for columns in rows_of(TILE, GROUP)]

    def down_steps(g_ref, tile):
        def step(columns):
            acc[every, columns] += matmul(g_ref[every], buffers[2][tile, :, columns])

        return [functools.partial(step, columns) for columns in rows_of(D, GROUP)]

    alternate(up_steps(u_even, 0))

    def turn(j, carry):
        even, odd = 2 * j, 2 * j + 1
        before, after = jnp.maximum(even - 1, 0), jnp.minimum(even + 2, TILES - 1)
        wait_down(pairs, buffers, even)
        wait_up(pairs, buffers, odd)
        wait_down(pairs, buffers, odd)

        @pl.when(even + 2 < TILES)
        def _():
            wait_up(pairs, buffers, even + 2)

        alternate(gelu_steps(u_even, g_even, even), down_steps(g_odd, before) + up_steps(u_odd, odd))
        alternate(gelu_steps(u_odd, g_odd, odd), down_steps(g_even, even) + up_steps(u_even, after))
        return carry

    lax.fori_loop(0, TILES // 2, turn, 0)
    alternate(down_steps(g_odd, TILES - 1))
    if after_loop is not None:
        after_loop()
    send(out.slope)
    weights = section_params(adapter, section)
    for part in parts:
        summed = acc[part]
        low_in = low(summed)
        added, *kept = branch_rows(low_in, weights)
        for result, value in zip(out.branch, (low_in, *kept)):
            result.buffer[part] = value
        values, (normal, inverse) = layer_norm(summed + added, gain(4), gain(5))
        out.normal_2.buffer[part], out.inverse_2.buffer[part] = normal, across(inverse)
        finish(part, values)
    send(out.branch, out.normal_2, out.inverse_2)


def low_shape(*dims):
    return shape_of(*dims, kind=BF16)


def branch_shapes(rows, wide, narrow):
    return Branch(low_shape(rows, wide), low_shape(rows, narrow), low_shape(rows, narrow))


def rest_shapes(rows):
    wide, thin = shape_of(rows, D), shape_of(rows, LANES)
    return Rest(wide, thin, low_shape(rows, FF), branch_shapes(rows, D, BOT), wide, thin)


def forward_kernel(ins, scalars, pairs, parts, slots):
    coupling_shapes = lambda rows: branch_shapes(rows, HALF, INV_H)
    outs = Forward(
        target_rows=shape_of(COUNT, D),
        one=coupling_shapes(SEQ),
        two=coupling_shapes(SEQ),
        attention_0=Attention(*[low_shape(SEQ, D)] * 3, shape_of(GROUPS, 8, SEQ)),
        rest_0=rest_shapes(SEQ),
        attention_1=Attention(
            low_shape(COUNT, D), *[low_shape(SEQ, D)] * 2, shape_of(GROUPS, HEADS_IN * COUNT, LANES)
        ),
        rest_1=rest_shapes(COUNT),
        last=Last(
            coupling_shapes(COUNT), coupling_shapes(COUNT),
            shape_of(COUNT, D), shape_of(COUNT, LANES), low_shape(COUNT, D),
        ),
    )

    def body(ins, out, scalar_refs, pair_refs, raw_refs, scratch):
        length = scalar_refs[0][0]
        hidden, x_low, s_even, s_odd, p_even, p_odd, lse_buf, mixed, section_out = scratch[:9]
        at_spots, at_low, mixed_1 = scratch[9:12]
        rest_scratch, qkv_0, qkv_1, rest_w = scratch[12:18], scratch[18:20], scratch[20:22], scratch[22:26]
        row_sems, joined = scratch[26:28]
        qkv_pair, rest_pairs = pair_refs[0], pair_refs[1:]

        start(ins.came, ins.spot, ins.pos, ins.norms, ins.coupling)
        norms = ins.norms.get()
        norm = lambda s, i: norms[s, i : i + 1]

        came, spot = ins.came.get(), ins.spot.get()
        start_qkv(qkv_pair, 0, qkv_0)
        start_out(rest_pairs, 0, rest_w)

        def rows_at(part):
            lane = lax.broadcasted_iota(jnp.int32, (part.stop - part.start, parts * slots), 1)
            hits = (spot[part][:, :1] == lane).astype(BF16)
            return matmul(hits, came[...])

        targets = slice(SEQ, SEQ + COUNT)
        out.target_rows.buffer[...] = rows_at(targets)
        for part in rows_of(SEQ, STEP_ROWS):
            hidden[part] = rows_at(part)

        @pl.when(scalar_refs[1][0] > 1)
        def _():
            ins.extra.copy.start()
            ins.extra.copy.wait()
            out.target_rows.buffer[...] += ins.extra.buffer[targets]
            hidden[...] += ins.extra.buffer[:SEQ]

        ins.extra.started = ins.extra.waited = True
        send(out.target_rows)
        start(ins.adapter, ins.chosen)
        start_tiles(rest_pairs, 0, rest_w)
        one, two = section_params(ins.coupling, 0), section_params(ins.coupling, 1)

        def put(results, part, *values):
            for result, value in zip(results, values):
                result.buffer[part] = value

        for part in rows_of(SEQ, STEP_ROWS):
            started, _ = layer_norm(hidden[part] + ins.pos.get()[part].astype(F32), norm(0, 0), norm(0, 1))
            left, right = started[:, :HALF], started[:, HALF:]
            low_one = low(right)
            added, active, slope = branch_rows(low_one, one)
            put(out.one, part, low_one, active, slope)
            left = left + added
            low_two = low(left)
            added, active, slope = branch_rows(low_two, two)
            put(out.two, part, low_two, active, slope)
            right = right + added
            hidden[part, :HALF] = left
            hidden[part, HALF:] = right
            x_low[part, :HALF] = low_two
            x_low[part, HALF:] = low(right)
        send(out.one, out.two)

        start_qkv(qkv_pair, 1, qkv_1)
        lse_buf[...] = jnp.zeros((SEQ, LANES), F32)
        q_ref, k_ref, v_ref, lse_ref = (result.buffer for result in out.attention_0)

        def attend(group, carry):
            columns = group_columns(group)
            for part, ref in enumerate((q_ref, k_ref, v_ref)):
                wait_qkv(qkv_pair, qkv_0, group, part)
                ref[:, columns] = low(matmul(x_low[...], qkv_0[0][group, part]))
            query = scaled_query(q_ref[:, columns])
            key, value = k_ref[:, columns], v_ref[:, columns]
            bias = key_bias(length, (1, SEQ), 1)
            lane = lax.broadcasted_iota(jnp.int32, (SMALL_ROWS * 2, LANES), 1)
            buffers = ((s_even, p_even), (s_odd, p_odd)) * 2

            def score_steps(head):
                def step():
                    buffers[head][0][...] = matmul_t(only_head(query, head), key)

                return [step] if head < HEADS_IN else []

            def soft_steps(head):
                def step(rows):
                    soft, lse = softmax_rows(buffers[head][0][rows] + bias)
                    buffers[head][1][rows] = soft
                    lse_buf[rows] = jnp.where(lane == head, lse, lse_buf[rows])

                return [functools.partial(step, rows) for rows in rows_of(SEQ, SMALL_ROWS * 2)]

            def mix_steps(head):
                def step():
                    mixed_head = matmul(buffers[head][1][...], value)
                    if head == 0:
                        joined[...] = mixed_head
                    else:
                        joined[...] = jnp.where(head_mask(mixed_head, head), mixed_head, joined[...])

                return [step] if head >= 0 else []

            alternate(score_steps(0))
            for head in range(HEADS_IN):
                alternate(soft_steps(head), score_steps(head + 1) + mix_steps(head - 1))
            alternate(mix_steps(HEADS_IN - 1))
            mixed[:, columns] = low(joined[...])
            lse_ref[group] = jnp.transpose(lse_buf[...])[:8]
            return carry

        lax.fori_loop(0, GROUPS, attend, 0)
        send(out.attention_0)

        def to_section_out(part, values):
            section_out[part] = low(values)

        def next_weights():
            start_out(rest_pairs, 1, rest_w)
            start_tiles(rest_pairs, 1, rest_w)

        rest_rows(
            out.rest_0, SEQ, 0, norms, ins.adapter, hidden, mixed, to_section_out,
            rest_scratch, rest_pairs, rest_w, next_weights,
        )

        at_spots[...] = matmul(ins.chosen.get()[...], section_out[...])
        at_low[...] = low(at_spots[...])
        q_1, k_1, v_1, lse_1 = (result.buffer for result in out.attention_1)

        groups = rows_of(D, GROUP)
        for group, columns in enumerate(groups):
            for part, ref in enumerate((q_1, k_1, v_1)):
                wait_qkv(qkv_pair, qkv_1, group, part)
                source = at_low if part == 0 else section_out
                ref[:, columns] = low(matmul(source[...], qkv_1[0][group, part]))
        bias = key_bias(length, (1, SEQ), 1)
        for group, columns in enumerate(groups):
            query = scaled_query(q_1[:, columns])
            query = jnp.concatenate([only_head(query, head) for head in range(HEADS_IN)], 0)
            soft, lse = softmax_rows(matmul_t(query, k_1[:, columns]) + bias)
            lse_1[group] = across(lse)
            every = matmul(soft, v_1[:, columns])
            mixed_group = every[:COUNT]
            for head in range(1, HEADS_IN):
                rows = slice(head * COUNT, (head + 1) * COUNT)
                mixed_group = jnp.where(head_mask(mixed_group, head), every[rows], mixed_group)
            mixed_1[:, columns] = low(mixed_group)
        send(out.attention_1)

        def to_normed(part, values):
            left, right = values[:, :HALF], values[:, HALF:]
            low_two = low(left)
            taken, active, slope = branch_rows(low_two, two)
            put(out.last.two, part, low_two, active, slope)
            right = right - taken
            low_one = low(right)
            taken, active, slope = branch_rows(low_one, one)
            put(out.last.one, part, low_one, active, slope)
            left = left - taken
            values, (normal, inverse) = layer_norm(jnp.concatenate([left, right], 1), norm(1, 0), norm(1, 1))
            put(out.last[2:], part, normal, across(inverse), low(values))

        rest_rows(
            out.rest_1, COUNT, 1, norms, ins.adapter, at_spots, mixed_1, to_normed,
            rest_scratch, rest_pairs, rest_w,
        )
        normed = out.last.normed.buffer
        copies = [
            pltpu.make_async_copy(normed.at[half], raw_refs[i].at[part], row_sems.at[i, part])
            for i, half in enumerate(rows_of(COUNT, COUNT // 2))
            for part in range(parts)
        ]
        for copy in copies:
            copy.start()
        for copy in copies:
            copy.wait()

    buffer = lambda *dims: pltpu.VMEM(dims, F32)
    buffer_low = lambda *dims: pltpu.VMEM(dims, BF16)
    scratch = [buffer(SEQ, D), buffer_low(SEQ, D), buffer(SEQ, SEQ), buffer(SEQ, SEQ)]
    scratch += [buffer_low(SEQ, SEQ), buffer_low(SEQ, SEQ), buffer(SEQ, LANES)]
    scratch += [buffer_low(SEQ, D), buffer_low(SEQ, D)]
    scratch += [buffer(COUNT, D), buffer_low(COUNT, D), buffer_low(COUNT, D)]
    scratch += [buffer_low(SEQ, D), buffer(SEQ, D), buffer(SEQ, TILE), buffer(SEQ, TILE)]
    scratch += [buffer_low(SEQ, TILE), buffer_low(SEQ, TILE)]
    scratch += qkv_buffers() + qkv_buffers() + rest_buffers()
    scratch += [pltpu.SemaphoreType.DMA((2, parts)), buffer(SEQ, GROUP)]
    raw = [low_shape(parts, COUNT // 2, D)] * 2
    kept, rows = moved_call(body, scalars, ins, outs, pairs, scratch, "forward", raw)
    return kept, rows


def column_sum(values):
    return jnp.sum(values.astype(F32), 0, keepdims=True)


def branch_grads(grad_low, kept, weights, out_refs):
    low_in, active, slope = kept
    hidden_grad = low(matmul_t(grad_low, weights[2]) * slope.astype(F32))
    out_refs[0][...] = inner_rows(low_in, hidden_grad)
    out_refs[1][...] = column_sum(hidden_grad)
    out_refs[2][...] = inner_rows(active, grad_low)
    out_refs[3][...] = column_sum(grad_low)
    return hidden_grad


ADAPTER_GRADS = ((D, BOT), (1, BOT), (BOT, D), (1, D))
COUPLING_GRADS = ((HALF, INV_H), (1, INV_H), (INV_H, HALF), (1, HALF))


def branch_kept(branch):
    return [operand.get()[...] for operand in branch]


def grad_weights(pair, section):
    return [pair[0].get()[section], None, pair[1].get()[section]]


def back_to_inner(kept, rows, section, norms, adapter, incoming, scratch, grad_refs, packing=None):
    acc, second_low = scratch
    parts = rows_of(rows, STEP_ROWS)
    weights = grad_weights(adapter, section)
    for part in parts:
        norm_kept = kept.normal_2.get()[part], kept.inverse_2.get()[part, :1]
        second = norm_back(incoming(part), norm_kept, norms[section, 4:5])
        acc[part] = second
        second_low[part] = low(second)
    hidden_grad = branch_grads(second_low[:rows], branch_kept(kept.branch), weights, grad_refs)
    for part in parts:
        acc[part] += matmul_t(hidden_grad[part], weights[0])
    if packing is not None:
        packing()


def back_to_mixed(operands, rows, section, norms, scratch, pairs, buffers, results):
    summed_low, acc = scratch
    start_ref, mixed_ref = results
    slope, normal, inverse = (operand.get() for operand in operands)
    parts = rows_of(rows, STEP_ROWS)
    for part in parts:
        summed_low[part] = low(acc[part])

    def turn(j, carry):
        for now in (2 * j, 2 * j + 1):
            wait_up(pairs, buffers, now)
            wait_down(pairs, buffers, now)
        for now in (2 * j, 2 * j + 1):
            for part in parts:
                inner = matmul_t(summed_low[part], buffers[2][now])
                inner = low(inner * slope[part, tile_columns(now)].astype(F32))
                acc[part] += matmul_t(inner, buffers[1][now])
        return carry

    lax.fori_loop(0, TILES // 2, turn, 0)
    wait_out(pairs, buffers)
    for part in parts:
        back = norm_back(acc[part], (normal[part], inverse[part, :1]), norms[section, 2:3])
        start_ref[part] = back
        mixed_ref[part] = low(matmul_t(low(back), buffers[0][...]))


def backward_kernel(ins, scalars, pairs, packed):
    parts = ins.merged[0].shape[0]
    grads = [shape_of(*dims) for dims in COUPLING_GRADS]
    if packed:
        chunks = low_shape(COUPLING_GROUPS, PART_ROWS, LANES)
        adapters = [[shape_of(1, BOT), shape_of(1, D)] for _ in range(MICRO)] + [chunks, chunks]
    else:
        adapters = [[shape_of(*dims) for dims in ADAPTER_GRADS] for _ in range(MICRO)]
    outs = Back(shape_of(1, LANES), grads, grads, adapters, shape_of(SEQ, D))

    def body(ins, out, scalar_refs, pair_refs, raw_refs, scratch):
        length = scalar_refs[0][0]
        (summed_low, acc_0, second_low), spot, mixed_1, acc_1, section_grad = scratch[:3], *scratch[3:7]
        qkv_w, rest_w, refs = scratch[7:9], scratch[9:13], scratch[13:]
        qkv_pair, rest_pairs = pair_refs[0], pair_refs[1:]

        start(ins.merged, ins.row_weights, ins.weight_sum, ins.target_rows, ins.last, ins.norms)
        start(ins.coupling, ins.adapter, ins.rest_1)
        start_tiles(rest_pairs, 1, rest_w)
        start_out(rest_pairs, 1, rest_w)
        start_qkv(qkv_pair, 1, qkv_w)
        start(ins)
        norms = ins.norms.get()

        def merge(merged):
            stats = merged[:, :, D:].astype(F32)
            highest = jnp.sum(stats[:, :, :3], 2, keepdims=True)
            totals = jnp.sum(stats[:, :, 3:6], 2, keepdims=True)
            top = jnp.max(highest, 0)
            factor = jnp.exp(highest - top[None])
            total = jnp.sum(totals * factor, 0)
            expected = jnp.zeros((merged.shape[1], D), F32)
            for i in range(parts):
                expected += merged[i, :, :D].astype(F32) * (factor[i] / total)
            return top, total, expected

        def from_head(part):
            halves = [merge(operand.get()) for operand in ins.merged]
            top, total, expected = (jnp.concatenate(pair, 0) for pair in zip(*halves))
            target = ins.target_rows.get()[...]
            target_logit = jnp.sum(ins.last.normed.get()[...].astype(F32) * target, 1, keepdims=True)
            weight = ins.row_weights.get()[...]
            row_losses = weight[:, :1] * (top + jnp.log(total) - target_logit)
            out.loss.buffer[...] = across(jnp.sum(row_losses, 0, keepdims=True))
            normed_grad = (weight / ins.weight_sum.get()[...])[:, :1] * (expected - target)
            kept = (ins.last.normal.get()[...], ins.last.inverse.get()[:, :1])
            restored = norm_back(normed_grad, kept, norms[1, 0:1])
            left, right = restored[:, :HALF], restored[:, HALF:]
            one, two = (grad_weights(ins.coupling, s) for s in range(MICRO))
            refs_of = lambda results: [result.buffer for result in results]
            hidden = branch_grads(low(-left), branch_kept(ins.last.one), one, refs_of(out.one))
            right = right + matmul_t(hidden, one[0])
            hidden = branch_grads(low(-right), branch_kept(ins.last.two), two, refs_of(out.two))
            left = left + matmul_t(hidden, two[0])
            return jnp.concatenate([left, right], 1)

        def grads_of(section):
            buffers = [result.buffer for result in out.adapters[section]]
            return (refs[0], buffers[0], refs[1], buffers[1]) if packed else buffers

        def pack_second():
            def store(part, chunk):
                refs[2][part] = chunk

            pack_adapter((refs[0], refs[1]), store)

        def pack_both():
            here = lax.axis_index("section") == 0
            own, other = out.adapters[2:]

            def store(part, chunk):
                arrived = refs[2][part]
                own.buffer[part] = jnp.where(here, chunk, arrived)
                other.buffer[part] = jnp.where(here, arrived, chunk)

            pack_adapter((refs[0], refs[1]), store)
            send(own, other)

        back_to_inner(
            ins.rest_1, COUNT, 1, norms, ins.adapter, from_head, (acc_0, second_low), grads_of(1),
            pack_second if packed else None,
        )
        kept = ins.rest_1.slope, ins.rest_1.normal_1, ins.rest_1.inverse_1
        back_to_mixed(kept, COUNT, 1, norms, (summed_low, acc_0), rest_pairs, rest_w, (spot, mixed_1))

        acc_1[...] = jnp.zeros_like(acc_1)
        q_ref, k_ref, v_ref, lse_ref = (operand.get() for operand in ins.attention_1)

        def attend_back(group, carry):
            columns = group_columns(group)
            stack = lambda values: jnp.concatenate([only_head(values, h) for h in range(HEADS_IN)], 0)
            query = stack(scaled_query(q_ref[:, columns]))
            mixed = stack(mixed_1[:, columns])
            key, value = k_ref[:, columns], v_ref[:, columns]
            scores = matmul_t(query, key) + key_bias(length, (1, SEQ), 1)
            soft = jnp.exp(scores - lse_ref[group][:, :1])
            soft_grad = matmul_t(mixed, value)
            delta = jnp.sum(soft_grad * soft, 1, keepdims=True)
            score_grad = low(soft * (soft_grad - delta))
            every = matmul(score_grad, key)
            query_grad = every[:COUNT]
            for head in range(1, HEADS_IN):
                query_grad = jnp.where(
                    head_mask(query_grad, head), every[head * COUNT : (head + 1) * COUNT], query_grad
                )
            query_grad = low(query_grad * HEAD_DIM**-0.5)
            key_grad = low(inner_rows(score_grad, query))
            value_grad = low(inner_rows(low(soft), mixed))
            for part in range(3):
                wait_qkv(qkv_pair, qkv_w, group, part)
            spot[...] += matmul_t(query_grad, qkv_w[0][group, 0])
            acc_1[...] += matmul_t(key_grad, qkv_w[0][group, 1]) + matmul_t(value_grad, qkv_w[0][group, 2])
            return carry

        lax.fori_loop(0, GROUPS, attend_back, 0)
        placed = jnp.dot(ins.chosen_t.get()[...], spot[...], precision=HIGHEST, preferred_element_type=F32)
        section_grad[...] = low(acc_1[...] + placed)

        back_to_inner(
            ins.rest_0, SEQ, 0, norms, ins.adapter, lambda part: section_grad[part].astype(F32),
            (out.inner.buffer, second_low), grads_of(0), pack_both if packed else None,
        )

    scratch = [pltpu.VMEM((COUNT, D), BF16), pltpu.VMEM((COUNT, D), F32), pltpu.VMEM((SEQ, D), BF16)]
    scratch += [pltpu.VMEM((COUNT, D), F32), pltpu.VMEM((COUNT, D), BF16), pltpu.VMEM((SEQ, D), F32)]
    scratch += [pltpu.VMEM((SEQ, D), BF16)] + qkv_buffers() + rest_buffers()
    if packed:
        scratch += [pltpu.VMEM((D, BOT), F32), pltpu.VMEM((BOT, D), F32)]
        scratch += [pltpu.VMEM((COUPLING_GROUPS, PART_ROWS, LANES), BF16)]
    return moved_call(body, scalars, ins, outs, pairs, scratch, "backward")[0]


def first_backward(ins, scalars, pairs, packed):
    if packed:
        dims = (COUPLING_GROUPS, GROUP_ROWS + 8, LANES)
        outs = (shape_of(*dims), low_shape(*dims))
    else:
        outs = [shape_of(*dims) for dims in COUPLING_GRADS * 2]

    def body(ins, out, scalar_refs, pair_refs, raw_refs, scratch):
        length = scalar_refs[0][0]
        s_even, s_odd, d_even, d_odd, p_even, p_odd, ds_even, ds_odd = scratch[:8]
        qkv_w, (key_grad, value_grad, query_grad_t), refs = scratch[8:10], scratch[10:13], scratch[13:]
        (summed_low, mixed_ref), rest_w, refs = refs[:2], refs[2:6], refs[6:]
        start(ins.inner, ins.norms)
        start_tiles(pair_refs[1:], 0, rest_w)
        start(ins.inner_kept)
        start_out(pair_refs[1:], 0, rest_w)
        start(ins.attention)
        start_qkv(pair_refs[0], 0, qkv_w)
        start(ins)
        acc = ins.inner.get()
        back_to_mixed(
            ins.inner_kept, SEQ, 0, ins.norms.get(), (summed_low, acc), pair_refs[1:], rest_w, (acc, mixed_ref)
        )
        q_ref, k_ref, v_ref, lse_ref = (operand.get() for operand in ins.attention)

        def attend_back(group, carry):
            columns = group_columns(group)
            query = scaled_query(q_ref[:, columns])
            key, value, mixed = k_ref[:, columns], v_ref[:, columns], mixed_ref[:, columns]
            lse_rows = lse_ref[group]
            key_t = jnp.transpose(key)
            buffers = ((s_even, d_even, p_even, ds_even), (s_odd, d_odd, p_odd, ds_odd)) * 2

            def product_steps(head):
                def scores():
                    buffers[head][0][...] = matmul_t(only_head(key, head), query)

                def soft_grads():
                    buffers[head][1][...] = matmul_t(only_head(value, head), mixed)

                return [scores, soft_grads] if head < HEADS_IN else []

            def soft_steps(head):
                s_buf, d_buf, p_low, ds_low = buffers[head]
                delta = [jnp.zeros((8, SEQ), F32)]

                def soft_step(rows):
                    valid = lax.broadcasted_iota(jnp.int32, (SMALL_ROWS, 1), 0) + rows.start < length
                    bias = jnp.where(valid, 0.0, -1e30)
                    soft = jnp.exp(s_buf[rows] + bias - lse_rows[head : head + 1])
                    s_buf[rows] = soft
                    p_low[rows] = low(soft)
                    product = soft * d_buf[rows]
                    for at in range(0, SMALL_ROWS, 8):
                        delta[0] = delta[0] + product[at : at + 8]

                def sum_step():
                    delta[0] = jnp.sum(delta[0], 0, keepdims=True)

                def grad_step(rows):
                    ds_low[rows] = low(s_buf[rows] * (d_buf[rows] - delta[0]))

                parts = rows_of(SEQ, SMALL_ROWS)
                steps = [functools.partial(soft_step, rows) for rows in parts] + [sum_step]
                return steps + [functools.partial(grad_step, rows) for rows in parts]

            def grad_steps(head):
                _, _, p_low, ds_low = buffers[max(head, 0)]

                def add(ref, grad):
                    ref[...] = grad if head == 0 else ref[...] + grad

                def value_step():
                    add(value_grad, matmul(p_low[...], only_head(mixed, head)))

                def key_step():
                    add(key_grad, matmul(ds_low[...], only_head(query, head)))

                def query_step():
                    rows = slice(head * HEAD_DIM, (head + 1) * HEAD_DIM)
                    query_grad_t[rows] = matmul(key_t[rows], ds_low[...])

                return [value_step, key_step, query_step] if head >= 0 else []

            alternate(product_steps(0))
            for head in range(HEADS_IN):
                alternate(soft_steps(head), product_steps(head + 1) + grad_steps(head - 1))
            alternate(grad_steps(HEADS_IN - 1))
            query_grad = jnp.transpose(query_grad_t[...]) * HEAD_DIM**-0.5
            for part, grad in enumerate((query_grad, key_grad[...], value_grad[...])):
                wait_qkv(pair_refs[0], qkv_w, group, part)
                acc[...] += matmul_t(low(grad), qkv_w[0][group, part])
            return carry

        lax.fori_loop(0, GROUPS, attend_back, 0)
        one, two = (grad_weights(ins.coupling, s) for s in range(MICRO))
        grads = refs if packed else [result.buffer for result in out]
        hidden = branch_grads(low(acc[:, HALF:]), branch_kept(ins.two), two, grads[4:])
        left = acc[:, :HALF] + matmul_t(hidden, two[0])
        branch_grads(low(left), branch_kept(ins.one), one, grads[:4])
        for ref, operand in zip(grads, (*ins.grads_one, *ins.grads_two)):
            ref[...] += operand.get()[...]
        if not packed:
            return
        here = lax.axis_index("section")
        for s in range(MICRO):
            some = grads[4 * s : 4 * s + 4]
            biases = [operand.get()[...] for operand in ins.biases[s]]
            tiles = bias_tiles(*biases, some[1][...], some[3][...])

            def store(part, chunk, s=s):
                @pl.when(here == s)
                def _():
                    out[0].buffer[part] = chunk

                @pl.when(here != s)
                def _():
                    out[1].buffer[part] = low(chunk)

            pack_coupling((some[0], some[2]), tiles, sum(BIASES) // COUPLING_GROUPS, store)

    scratch = [pltpu.VMEM((SEQ, SEQ), F32)] * 4 + [pltpu.VMEM((SEQ, SEQ), BF16)] * 4 + qkv_buffers()
    scratch += [pltpu.VMEM((SEQ, GROUP), F32)] * 2 + [pltpu.VMEM((GROUP, SEQ), F32)]
    scratch += [pltpu.VMEM((SEQ, D), BF16)] * 2 + rest_buffers()
    if packed:
        scratch += [pltpu.VMEM(dims, F32) for dims in COUPLING_GRADS * 2]
    return moved_call(body, scalars, ins, outs, pairs, scratch, "first_backward")[0]


VOCAB_TILE = 1280


def head_stats(top, total):
    lane = lax.broadcasted_iota(jnp.int32, (top.shape[0], LANES), 1)
    stats = jnp.zeros(lane.shape, F32)
    for j, piece in enumerate(three_low(top) + three_low(total)):
        stats = jnp.where(lane == j, piece.astype(F32), stats)
    return low(stats)


def head_kernel(rows, table):
    parts, each, _ = rows.shape
    count, vocab = parts * each, table.shape[0]
    tiles = pl.cdiv(vocab, VOCAB_TILE)
    if vocab < VOCAB_TILE or (vocab - VOCAB_TILE) % 16 or tiles % 2:
        return blocked_head_kernel(rows, table)
    starts = [min(tile * VOCAB_TILE, vocab - VOCAB_TILE) for tile in range(tiles)]

    def kernel(x_hbm, table_hbm, out_hbm, *refs):
        x_ref, out_ref, entries, acc, top, total, factor_even, factor_odd = refs[:8]
        l_even, l_odd, p_even, p_odd, sems = refs[8:]
        fetch = pltpu.make_async_copy(x_hbm, x_ref, sems.at[tiles])
        fetch.start()
        for tile, at in enumerate(starts):
            window = table_hbm.at[pl.ds(at, VOCAB_TILE)]
            pltpu.make_async_copy(window, entries.at[tile], sems.at[tile]).start()

        def wait_tile(tile):
            window = table_hbm.at[pl.ds(0, VOCAB_TILE)]
            pltpu.make_async_copy(window, entries.at[tile], sems.at[tile]).wait()

        def logit_steps(l_ref, tile):
            def step(columns):
                l_ref[:, columns] = matmul_t(x_ref[...], entries[tile, columns])

            return [functools.partial(step, columns) for columns in rows_of(VOCAB_TILE, GROUP)]

        def soft_steps(l_ref, p_ref, factor_ref, tile):
            start = jnp.minimum(tile * VOCAB_TILE, vocab - VOCAB_TILE)
            lane = lax.broadcasted_iota(jnp.int32, (1, VOCAB_TILE), 1)
            bias = jnp.where(lane + start >= tile * VOCAB_TILE, 0.0, -1e30)

            def step(at):
                logits = l_ref[at] + bias
                earlier = top[at]
                highest = jnp.maximum(earlier, jnp.max(logits, 1, keepdims=True))
                exponent = jnp.exp(logits - highest)
                factor = jnp.exp(earlier - highest)
                top[at] = highest
                total[at] = total[at] * factor + jnp.sum(exponent, 1, keepdims=True)
                p_ref[at] = low(exponent)
                factor_ref[at] = across(factor)

            return [functools.partial(step, at) for at in rows_of(count, SMALL_ROWS)]

        def sum_steps(p_ref, factor_ref, tile):
            def step(columns):
                factor = factor_ref[...]
                factor = jnp.concatenate([factor, factor], 1)
                acc[:, columns] = acc[:, columns] * factor + matmul(p_ref[...], entries[tile, :, columns])

            return [functools.partial(step, columns) for columns in rows_of(D, GROUP)]

        acc[...] = jnp.zeros_like(acc)
        top[...] = jnp.full_like(top, -1e30)
        total[...] = jnp.zeros_like(total)
        p_odd[...] = jnp.zeros_like(p_odd)
        factor_odd[...] = jnp.ones_like(factor_odd)
        fetch.wait()
        wait_tile(0)
        alternate(logit_steps(l_even, 0))

        def turn(j, carry):
            even, odd = 2 * j, 2 * j + 1
            before, after = jnp.maximum(even - 1, 0), jnp.minimum(even + 2, tiles - 1)
            wait_tile(odd)

            @pl.when(even + 2 < tiles)
            def _():
                wait_tile(even + 2)

            alternate(
                soft_steps(l_even, p_even, factor_even, even),
                sum_steps(p_odd, factor_odd, before) + logit_steps(l_odd, odd),
            )
            alternate(
                soft_steps(l_odd, p_odd, factor_odd, odd),
                sum_steps(p_even, factor_even, even) + logit_steps(l_even, after),
            )
            return carry

        lax.fori_loop(0, tiles // 2, turn, 0)
        alternate(sum_steps(p_odd, factor_odd, tiles - 1))
        out_ref[:, :D] = low(acc[...])
        out_ref[:, D:] = head_stats(top[...], total[...])
        copy = pltpu.make_async_copy(out_ref, out_hbm, sems.at[tiles])
        copy.start()
        copy.wait()

    hbm = pl.BlockSpec(memory_space=pltpu.HBM)
    return pl.pallas_call(
        kernel,
        in_specs=[hbm, hbm],
        out_specs=hbm,
        out_shape=low_shape(count, D + LANES),
        scratch_shapes=[
            pltpu.VMEM((count, D), BF16),
            pltpu.VMEM((count, D + LANES), BF16),
            pltpu.VMEM((tiles, VOCAB_TILE, D), BF16),
            pltpu.VMEM((count, D), F32),
            pltpu.VMEM((count, 1), F32),
            pltpu.VMEM((count, 1), F32),
        ]
        + [pltpu.VMEM((count, LANES), F32)] * 2
        + [pltpu.VMEM((count, VOCAB_TILE), F32)] * 2
        + [pltpu.VMEM((count, VOCAB_TILE), BF16)] * 2
        + [pltpu.SemaphoreType.DMA((tiles + 1,))],
        compiler_params=params_for(MOST_VMEM),
        name="vocabulary_head",
    )(rows.reshape(count, D), table).reshape(parts, each, D + LANES)


def blocked_head_kernel(rows, table):
    parts_in, each, _ = rows.shape
    count, vocab = parts_in * each, table.shape[0]
    last = pl.cdiv(vocab, VOCAB_TILE) - 1
    turns = last // 2 + 1

    def kernel(x_hbm, even_ref, odd_ref, after_ref, out_hbm, *refs):
        x_ref, out_ref, acc, top, total, l_even, l_odd, p_even, p_odd, sems = refs
        turn = pl.program_id(0)

        def entries_of(ref, tile):
            row = lax.broadcasted_iota(jnp.int32, (VOCAB_TILE, 1), 0)
            return jnp.where(row < vocab - tile * VOCAB_TILE, ref[...], jnp.zeros_like(ref))

        @pl.when(turn == 0)
        def _():
            copy = pltpu.make_async_copy(x_hbm, x_ref, sems.at[0])
            copy.start()
            acc[...] = jnp.zeros_like(acc)
            top[...] = jnp.full_like(top, -1e30)
            total[...] = jnp.zeros_like(total)
            entries = entries_of(even_ref, 0)
            copy.wait()
            l_even[...] = matmul_t(x_ref[...], entries)

        even = entries_of(even_ref, 2 * turn)
        odd = entries_of(odd_ref, 2 * turn + 1)
        after = entries_of(after_ref, 2 * turn + 2)
        for tile, l_now, p_now, now, l_later, later in (
            (2 * turn, l_even, p_even, even, l_odd, odd),
            (2 * turn + 1, l_odd, p_odd, odd, l_even, after),
        ):
            bias = key_bias(vocab - tile * VOCAB_TILE, (1, VOCAB_TILE), 1)
            for at in rows_of(count, SMALL_ROWS):
                logits = l_now[at] + bias
                earlier = top[at]
                highest = jnp.maximum(earlier, jnp.max(logits, 1, keepdims=True))
                exponent = jnp.exp(logits - highest)
                factor = jnp.exp(earlier - highest)
                top[at] = highest
                total[at] = total[at] * factor + jnp.sum(exponent, 1, keepdims=True)
                p_now[at] = low(exponent)
                acc[at] = acc[at] * factor
            l_later[...] = matmul_t(x_ref[...], later)
            acc[...] += matmul(p_now[...], now)

        @pl.when(turn == turns - 1)
        def _():
            out_ref[:, :D] = low(acc[...])
            out_ref[:, D:] = head_stats(top[...], total[...])
            copy = pltpu.make_async_copy(out_ref, out_hbm, sems.at[1])
            copy.start()
            copy.wait()

    def tile_at(shift):
        return pl.BlockSpec((VOCAB_TILE, D), lambda j: (jnp.minimum(2 * j + shift, last), 0))

    hbm = pl.BlockSpec(memory_space=pltpu.HBM)
    return pl.pallas_call(
        kernel,
        grid=(turns,),
        in_specs=[hbm] + [tile_at(shift) for shift in range(3)],
        out_specs=hbm,
        out_shape=shape_of(count, D + LANES, kind=BF16),
        scratch_shapes=[
            pltpu.VMEM((count, D), BF16),
            pltpu.VMEM((count, D + LANES), BF16),
            pltpu.VMEM((count, D), F32),
            pltpu.VMEM((count, 1), F32),
            pltpu.VMEM((count, 1), F32),
            pltpu.VMEM((count, VOCAB_TILE), F32),
            pltpu.VMEM((count, VOCAB_TILE), F32),
            pltpu.VMEM((count, VOCAB_TILE), BF16),
            pltpu.VMEM((count, VOCAB_TILE), BF16),
            pltpu.SemaphoreType.DMA((2,)),
        ],
        compiler_params=params_for(MOST_VMEM),
        name="vocabulary_head",
    )(rows.reshape(count, D), table, table, table).reshape(parts_in, each, D + LANES)


def swap_add(own, other):
    came = lax.ppermute(low(other), "section", [(0, 1), (1, 0)])
    return own + came.astype(F32)


def pick(first_section, both):
    return jnp.where(first_section, both[0], both[1])


def plan_requests(ids, weights, vocab_rows, slots, parts):
    turned = jnp.transpose(ids)

    def kernel(ids_ref, turned_ref, weights_ref, asked_ref, code_ref, spot_ref):
        here = lax.axis_index("section")
        i_index = lax.broadcasted_iota(jnp.int32, (IDS, IDS), 0)
        j_index = lax.broadcasted_iota(jnp.int32, (IDS, IDS), 1)
        earlier, later = j_index < i_index, i_index < j_index

        def owner_of(values):
            return jnp.floor((values.astype(F32) + 0.5) * (1.0 / vocab_rows)).astype(jnp.int32)

        def count(hits, axis):
            return jnp.sum(hits.astype(F32), axis, keepdims=True)

        most = jnp.zeros((1, 1), F32)
        for m in range(MICRO):
            row, col = ids_ref[m : m + 1], turned_ref[:, m : m + 1]
            same_id = row == col
            first_col = count(same_id & earlier, 1) == 0
            first_row = count(same_id & later, 0) == 0
            owner_row, owner_col = owner_of(row), owner_of(col)
            same_owner = owner_row == owner_col
            rank_row = count(same_owner & later & first_col, 0)
            rank_col = count(same_owner & earlier & first_row, 1)
            most = jnp.maximum(most, jnp.max(rank_row, 1, keepdims=True))

            @pl.when(here == m)
            def _():
                slot_row = jnp.sum(jnp.where(same_id & first_col, rank_col, 0.0), 0, keepdims=True)
                slot_col = jnp.sum(jnp.where(same_id & first_row, rank_row, 0.0), 1, keepdims=True)
                slot_row, slot_col = slot_row.astype(jnp.int32), slot_col.astype(jnp.int32)
                code_ref[...] = (owner_row + parts * first_row.astype(jnp.int32)) * 1024 + slot_row
                spot = jnp.where(slot_col < slots, owner_col * slots + slot_col, -1)
                spot_ref[...] = jnp.broadcast_to(spot, (IDS, LANES))
                lane = lax.broadcasted_iota(jnp.int32, (IDS, LANES), 1)
                local = (col - owner_col * vocab_rows).astype(F32)
                wanted = first_col & (slot_col < slots) & (slot_col == lane)
                wanted = jnp.where(wanted, local, 0.0)
                for part in range(parts):
                    asked = jnp.sum(jnp.where(owner_col == part, wanted, 0.0), 0, keepdims=True)
                    asked_ref[part] = asked.astype(jnp.int32)

        rounds = jnp.floor((most + 0.5) * (1.0 / slots)).astype(jnp.int32) + 1
        total = jnp.sum(jnp.sum(weights_ref[...], 0, keepdims=True), 1, keepdims=True)
        lane = lax.broadcasted_iota(jnp.int32, (1, LANES), 1)
        for part in range(parts):
            row = asked_ref[part]
            asked_ref[part] = jnp.where(lane == slots, rounds, jnp.where(lane == slots + 1, total, row))

    return pl.pallas_call(
        kernel,
        out_shape=[
            jax.ShapeDtypeStruct((parts, 1, LANES), jnp.int32),
            jax.ShapeDtypeStruct((1, IDS), jnp.int32),
            jax.ShapeDtypeStruct((IDS, LANES), jnp.int32),
        ],
        compiler_params=params_for(24),
        name="plan_requests",
    )(ids, turned, weights)


def fetch_rows(table, ids, first_section, plan, slots, late):
    parts = lax.axis_size("dp")
    vocab_rows = table.shape[0]
    asked, code, spot = plan
    asked = lax.all_to_all(asked, "dp", 0, 0)[:, 0]
    total_rounds = jnp.max(asked[:, slots])
    weight_sum = jnp.sum(asked[:, slots + 1])

    def look_up(asked):
        return table.at[asked.reshape(-1)].get(mode="promise_in_bounds").reshape(parts, slots, D)

    def send_rows(rows):
        return lax.all_to_all(rows, "dp", 0, 0).reshape(parts * slots, D)

    rows, late = lax.optimization_barrier((look_up(asked[:, :slots]), late))
    came = send_rows(rows)

    def more(state):
        return state[0] < total_rounds

    def another(state):
        turn, extra = state
        place, slot = code[0] // 1024, code[0] % 1024
        owner, first = place % parts, place >= parts
        local = pick(first_section, ids) - owner * vocab_rows
        here = slot - turn * slots
        at = jnp.where((here >= 0) & (here < slots), owner * slots + here, -1)
        hits = at[:, None] == jnp.arange(parts * slots)[None, :]
        wanted = jnp.sum(jnp.where(hits & first[:, None], local[:, None], 0), 0).reshape(parts, slots)
        rows = send_rows(look_up(lax.all_to_all(wanted, "dp", 0, 0)))
        return turn + 1, extra + matmul(hits.astype(BF16), rows)

    extra = lax.while_loop(more, another, (jnp.int32(1), jnp.zeros((IDS, D), F32)))[1]
    return came, spot, extra, total_rounds, weight_sum.astype(F32), late


def three_low(values):
    high = low(values)
    rest = values - high.astype(F32)
    middle = low(rest)
    return [high, middle, low(rest - middle.astype(F32))]


def in_groups(count):
    return lax.axis_size("dp") == COUPLING_GROUPS and count == 4 * PART_GROUPS


LINES = 4


def plane_groups(parts):
    planes = parts // LINES
    across_planes = [[plane * LINES + line for plane in range(planes)] for line in range(LINES)]
    return across_planes, [[plane * LINES + line for line in range(LINES)] for plane in range(planes)]


def share_params(master, vector, after):
    if not in_groups(master.shape[0]):
        return low(jnp.concatenate([master.reshape(-1), vector])), after
    across_planes, in_plane = plane_groups(lax.axis_size("dp"))
    some = pack_own(master, vector[None], len(in_plane))
    some = lax.all_to_all(some, "dp", 0, 0, axis_index_groups=across_planes)
    return lax.optimization_barrier((some, after))


def gather_params(some, count, width, before):
    parts = lax.axis_size("dp")
    if in_groups(count):
        _, in_plane = plane_groups(parts)
        own = lax.all_gather(some, "dp", axis_index_groups=in_plane)
        own, before = lax.optimization_barrier((own, before))
        return *unpack_all(own, lax.ppermute(own, "section", [(0, 1), (1, 0)]), width), before
    gathered = lax.all_gather(some, ("section", "dp")).reshape(MICRO, parts, -1)
    size = count * BLOCK**2
    all_blocks = gathered[:, :, :size].reshape(MICRO, parts * count, BLOCK, BLOCK)
    all_vectors = gathered[:, :, size:].reshape(MICRO, parts * width)
    both = [split_params(all_blocks[s], all_vectors[s]) for s in range(MICRO)]

    def stacked(which):
        down, bias_down, up, bias_up = (jnp.stack([pair[which][i] for pair in both]) for i in range(4))
        return Params(down, bias_down.astype(F32)[:, None], up, bias_up.astype(F32)[:, None])

    return stacked(0), stacked(1), before


def sum_at_owners(grads, loss_part, count):
    parts = lax.axis_size("dp")
    width = sum(BIASES) // parts
    flat = []
    for adapter, coupling in grads:
        blocks, vector = join_params(adapter, coupling)
        flat.append(
            jnp.concatenate([blocks.reshape(parts, count * BLOCK**2), vector.reshape(parts, width)], 1)
        )
    first = lax.axis_index("section") == 0
    summed = swap_add(jnp.where(first, flat[0], flat[1]), jnp.where(first, flat[1], flat[0]))
    owned = jnp.sum(lax.all_to_all(low(summed), "dp", 0, 0).astype(F32), 0)
    blocks = owned[: count * BLOCK**2].reshape(count, BLOCK, BLOCK)
    pair = jnp.stack([jnp.sum(owned * owned), loss_part[0, 0]])
    pair = jnp.pad(pair, (0, LANES - 2))[None, None]
    return blocks, owned[count * BLOCK**2 :], jnp.broadcast_to(pair, (parts * MICRO, 8, LANES))


def to_coupling_owners(group):
    arrived = []
    for place in range(1, PART_GROUPS):
        route = []
        for i, part in enumerate(SUMMED_AT):
            owner, at = divmod(ADAPTER_GROUPS + i, PART_GROUPS)
            if at == place and owner != part:
                route.append((part, owner))
        arrived.append(lax.ppermute(group, "dp", route))
    return [group] + arrived


def exact(spec, left, right):
    return jnp.einsum(spec, left, right, precision=HIGHEST)


def update(pair, grads, grad_vector, turned_old, state):
    master, momentum, stat_left, stat_right, root_left, root_right, vectors, vec_first, vec_second = state
    count = master.shape[0]
    outs = [shape_of(1, count, BLOCK, BLOCK)] * 5 + [low_shape(1, count, BLOCK, BLOCK)]
    outs += [shape_of(*vectors.shape)] * 3 + [shape_of(1, 1)] * 2

    def body(ins, out, scalar_refs, pair_refs, raw_refs, scratch):
        start(ins)
        grads, vector_ref, old_ref, state_refs, pair_ref = jax.tree.map(lambda operand: operand.get(), ins)
        master_ref, momentum_ref, stat_left_ref, stat_right_ref, root_left_ref, root_right_ref = state_refs[:6]
        vectors_ref, first_ref, second_ref = state_refs[6:]
        outs = [result.buffer for result in out]
        grad_ref = grads[0]
        if len(grads) > 1:
            grad_ref = scratch[0]
            unpack_own(grads[0], grads[1], grads[2:], grad_ref)
        totals = jnp.sum(pair_ref[...], 0)[:1]
        norm = jnp.sqrt(totals[:, :1])
        factor = CLIP_NORM / jnp.maximum(norm, CLIP_NORM)
        outs[9][...] = norm
        outs[10][...] = totals[:, 1:2]
        square = (1.0 - STAT_DECAY) * factor * factor
        for n in range(count):
            grad = grad_ref[n]
            clipped = grad * factor
            outs[0][0, n] = clipped
            outs[1][0, n] = FIRST_DECAY * momentum_ref[n] + (1.0 - FIRST_DECAY) * clipped
            left_square = exact_dot(grad, grad, ((1,), (1,)))
            right_square = exact_dot(grad, grad, ((0,), (0,)))
            turned = exact_dot(exact_dot(root_left_ref[n], grad, ((1,), (0,))), root_right_ref[n], ((1,), (0,)))
            outs[2][0, n] = STAT_DECAY * stat_left_ref[n] + square * left_square
            outs[3][0, n] = STAT_DECAY * stat_right_ref[n] + square * right_square
            direction = FIRST_DECAY * old_ref[n] + (1.0 - FIRST_DECAY) * factor * turned
            master_new = master_ref[n] - MAT_RATE * (direction + MAT_DECAY * master_ref[n])
            outs[4][0, n] = master_new
            outs[5][0, n] = low(master_new)
        clipped = vector_ref[:1, : vectors.shape[1]] * factor
        first_new = FIRST_DECAY * first_ref[...] + (1.0 - FIRST_DECAY) * clipped
        second_new = VEC_SECOND * second_ref[...] + (1.0 - VEC_SECOND) * clipped * clipped
        outs[6][...] = first_new
        outs[7][...] = second_new
        corrected_first = first_new / (1.0 - FIRST_DECAY**STEP)
        corrected_second = second_new / (1.0 - VEC_SECOND**STEP)
        outs[8][...] = vectors_ref[...] - VEC_RATE * (
            corrected_first / (jnp.sqrt(corrected_second) + VEC_EPS) + VEC_DECAY * vectors_ref[...]
        )

    ins = (grads, grad_vector, turned_old, state, pair)
    scratch = [pltpu.VMEM((count, BLOCK, BLOCK), F32)] if len(grads) > 1 else []
    return moved_call(body, (), ins, outs, (), scratch, "update")[0]


def shards(
    token_ids,
    lengths,
    positions,
    targets,
    loss_weights,
    embed_table,
    pos_table,
    norm_params,
    base_qkv,
    base_out,
    base_up,
    base_down,
    master,
    momentum,
    stat_left,
    stat_right,
    root_left,
    root_right,
    vectors,
    vec_first,
    vec_second,
):
    parts = lax.axis_size("dp")
    first_section = lax.axis_index("section") == 0
    slots = -(-IDS * 5 // (4 * parts * 16)) * 16

    ids = jnp.concatenate([token_ids[:, 0], targets[:, 0]], -1)
    some, ids = share_params(master[0], vectors[0], ids)
    plan = plan_requests(ids, loss_weights[:, 0], embed_table.shape[0], slots, parts)
    swap = [(0, 1), (1, 0)]
    pairs = [(w, lax.ppermute(w, "section", swap)) for w in (base_qkv, base_out, base_up, base_down)]
    norms_came = lax.ppermute(norm_params, "section", swap)

    late = norm_params, norms_came, lengths, positions, loss_weights, root_left, root_right, momentum
    came, spot, extra, rounds, weight_sum, late = fetch_rows(
        embed_table, ids, first_section, plan, slots, late
    )
    norms_own, norms_came, lengths, positions, loss_weights, root_left, root_right, momentum = late
    norms = [pick(first_section, (norms_own, norms_came)), pick(first_section, (norms_came, norms_own))]
    spots = pick(first_section, positions[:, 0])
    row_weights = pick(first_section, loss_weights[:, 0]).astype(F32)
    early = (
        jnp.concatenate(norms),
        pick(first_section, lengths),
        jnp.broadcast_to(row_weights[:, None], (COUNT, LANES)),
        (spots[:, None] == jnp.arange(SEQ)[None, :]).astype(BF16),
        (spots[None, :] == jnp.arange(SEQ)[:, None]).astype(F32),
        exact("nij,njk->nik", exact("nij,njk->nik", root_left[0], momentum[0]), root_right[0]),
    )
    adapter, coupling, early = gather_params(some, master.shape[1], vectors.shape[1], early)
    norms, length, row_weights, chosen, chosen_t, turned_old = early

    ins = ForwardIn(came, spot, extra, pos_table, norms, chosen, adapter, coupling)
    kept, rows = forward_kernel(ins, (length, rounds.reshape(1)), pairs, parts, slots)

    spread = [lax.all_to_all(half, "dp", 0, 0) for half in rows]
    first_half, spread[1] = lax.optimization_barrier((head_kernel(spread[0], embed_table), spread[1]))
    halves = [first_half, head_kernel(spread[1], embed_table)]
    merged = [lax.all_to_all(half, "dp", 0, 0) for half in halves]

    packed = in_groups(master.shape[1])
    weight_row = jnp.broadcast_to(weight_sum, (1, LANES))
    adapter, coupling = adapter[::2], coupling[::2]
    adapter_kept = kept.rest_0._replace(slope=(), normal_1=(), inverse_1=())
    ins = BackIn(
        merged, row_weights, weight_row, norms, chosen_t, adapter, coupling,
        kept.target_rows, adapter_kept, kept.attention_1, kept.rest_1, kept.last,
    )
    back = backward_kernel(ins, (length,), pairs, packed)
    loss_part, inner = back.loss, back.inner
    if packed:
        own, other = back.adapters[MICRO:]
        summed = low(swap_add(own.astype(F32), other))
        summed, inner = lax.optimization_barrier((summed, inner))
        adapter_came = lax.all_to_all(summed, "dp", 0, 0)
    inner_kept = kept.rest_0.slope, kept.rest_0.normal_1, kept.rest_0.inverse_1
    ins = FirstIn(
        inner, norms, inner_kept, kept.attention_0, coupling, kept.one, kept.two, back.one, back.two,
        back.adapters[:MICRO] if packed else (),
    )
    grads = first_backward(ins, (length,), pairs, packed)
    if packed:
        adapter_total, squares = sum_adapter(adapter_came)
        came = lax.all_to_all(low(swap_add(*grads)), "dp", 0, 0)
        group, bias, pair = sum_coupling(came, squares, loss_part, parts * MICRO)
        grad, grad_vector = [adapter_total, *to_coupling_owners(group)], bias
    else:
        both = [(back.adapters[s], grads[4 * s : 4 * s + 4]) for s in range(MICRO)]
        grad, grad_vector, pair = sum_at_owners(both, loss_part, master.shape[1])
        grad, grad_vector = [grad], grad_vector[None]
    pair = lax.all_to_all(pair, ("dp", "section"), 0, 0)
    state = (master, momentum, stat_left, stat_right, root_left, root_right)
    state = [value[0] for value in state] + [vectors, vec_first, vec_second]
    *outs, grad_norm, loss_sum = update(pair, grad, grad_vector, turned_old, state)
    return (*outs, grad_norm[0, 0], loss_sum[0, 0], weight_sum)


def solution(mesh):
    rows = P(None, "dp", None)
    section = P("section", None, None)
    blocks = P("section", "dp", None, None)
    biases = P("section", "dp")
    return jax.shard_map(
        shards,
        mesh=mesh,
        in_specs=(rows, P(None, "dp"), rows, rows, rows, P("dp", None), P())
        + (section,) * 5
        + (blocks,) * 6
        + (biases,) * 3,
        out_specs=(blocks,) * 6 + (biases,) * 3 + (P(),) * 3,
        check_vma=False,
    )
```
